32 devices in a mesh: dp: 8 (over z, x), mp: 4 (over y, core).
Axes of the slice: x: 2, y: 2, z: 4, core: 2. Of those that a mesh axis runs over, the one named last changes fastest.
Arguments:
- tokens: bfloat16 [32768, 768], P(('dp', 'mp')), may hold values from -6 to 6
- cotangent: bfloat16 [32768, 768], P(('dp', 'mp'))
- lengths: int32 [32], P('dp'), may hold values from 64 to 1024, as said below
- input_weight: float32 [768, 3, 768], P('dp', None, 'mp'), may hold values from -0.21875 to 0.21875
- output_weight: float32 [768, 768], P('mp', 'dp')
- expand_weight: float32 [768, 3072], P('dp', 'mp'), may hold values from -0.21875 to 0.21875
- shrink_weight: float32 [3072, 768], P('mp', 'dp')
- layer_vectors: float32 [6, 768], replicated
- head_bias: float32 [2, 768], P(None, 'mp'), may hold values from -1 to 1
- expand_bias: float32 [3072], P('mp'), may hold values from -1 to 1
- first_input: float32 [768, 3, 768], P('dp', None, 'mp')
- first_output: float32 [768, 768], P('mp', 'dp')
- first_expand: float32 [768, 3072], P('dp', 'mp')
- first_shrink: float32 [3072, 768], P('mp', 'dp')
- first_vectors: float32 [6, 768], replicated
- first_head: float32 [2, 768], P(None, 'mp')
- first_bias: float32 [3072], P('mp')
- second_input: float32 [768, 3, 768], P('dp', None, 'mp'), as said below
- second_output: float32 [768, 768], P('mp', 'dp'), as said below
- second_expand: float32 [768, 3072], P('dp', 'mp'), as said below
- second_shrink: float32 [3072, 768], P('mp', 'dp'), as said below
- second_vectors: float32 [6, 768], replicated, as said below
- second_head: float32 [2, 768], P(None, 'mp'), as said below
- second_bias: float32 [3072], P('mp'), as said below
Outputs:
- block_out: bfloat16 [32768, 768], P(('dp', 'mp'))
- token_grad: bfloat16 [32768, 768], P(('dp', 'mp'))
- grad_norm: float32 [], replicated
- moment_input: float32 [768, 3, 768], P('dp', None, 'mp')
- square_input: float32 [768, 3, 768], P('dp', None, 'mp')
- updated_input: float32 [768, 3, 768], P('dp', None, 'mp')
- moment_output: float32 [768, 768], P('mp', 'dp')
- square_output: float32 [768, 768], P('mp', 'dp')
- updated_output: float32 [768, 768], P('mp', 'dp')
- moment_expand: float32 [768, 3072], P('dp', 'mp')
- square_expand: float32 [768, 3072], P('dp', 'mp')
- updated_expand: float32 [768, 3072], P('dp', 'mp')
- moment_shrink: float32 [3072, 768], P('mp', 'dp')
- square_shrink: float32 [3072, 768], P('mp', 'dp')
- updated_shrink: float32 [3072, 768], P('mp', 'dp')
- moment_vectors: float32 [6, 768], replicated
- square_vectors: float32 [6, 768], replicated
- updated_vectors: float32 [6, 768], replicated
- moment_head: float32 [2, 768], P(None, 'mp')
- square_head: float32 [2, 768], P(None, 'mp')
- updated_head: float32 [2, 768], P(None, 'mp')
- moment_bias: float32 [3072], P('mp')
- square_bias: float32 [3072], P('mp')
- updated_bias: float32 [3072], P('mp')
The draws below stay inside these ranges and needn't reach their ends.
Inputs may be any that keep to these rules, and one draw needn't show every extreme that they name: lengths of the sequences; some sequence has all 1024 positions valid. `second_input`: positive. `second_output`: positive. `second_expand`: positive. `second_shrink`: positive. `second_vectors`: positive. `second_head`: positive. `second_bias`: positive.
All inputs are finite; a program needn't handle non-finite values.
Results may differ from the reference program's by a relative error of at most 0.012.
Values may be sent and summed in bfloat16 or wider, within the bound.
No kernel may reach another device: no remote copies, remote signals or barrier semaphores. Data moves between devices by JAX's collectives and lax.ppermute only.
A program may use at most 192 MiB of HBM per device.

```python
import math
import jax
import jax.numpy as jnp
from jax import lax

D = 768
HEADS = 12
HEAD_DIM = 64
FF = 3072
SEQ_LEN = 1024
MIN_LEN = 64
STEP = 10
NSEQ = 32
TOKENS = 32768


clip_norm = 1.0


def rising(count):
    return 0.6 + 1.2 * jnp.arange(count, dtype=jnp.float32) / count


def entry_size(scale):
    total_params = 4 * D * D + 2 * D * FF + 8 * D + FF
    return scale * clip_norm / math.sqrt(total_params)


def first_state(key, shape, scale):
    size = entry_size(scale)
    noise = jnp.clip(jax.random.normal(key, shape, jnp.float32), -5.0, 5.0)
    return 0.1 / 0.9 * size * noise


def second_state(key, shape, scale):
    size = entry_size(scale)
    spread = jax.random.uniform(key, shape, jnp.float32, math.log(0.5), math.log(8.0))
    return 0.001 / 0.999 * size * size * jnp.exp(spread)


def draw_cotangent(key, part):
    key = jax.random.fold_in(key, 1)
    noise = jnp.clip(jax.random.normal(key, (TOKENS, D), jnp.float32), -5.0, 5.0)
    return (noise * rising(D)[None, :]).astype(jnp.bfloat16)


def draw_lengths(key, part):
    key = jax.random.fold_in(key, 2)
    first_key, second_key = jax.random.split(key)
    picks = jax.random.randint(first_key, (3, NSEQ), 0, SEQ_LEN - MIN_LEN + 1)
    result = MIN_LEN + jnp.min(picks, axis=0)
    longest = jax.random.randint(second_key, (), 0, NSEQ)
    return jnp.where(jnp.arange(NSEQ) == longest, SEQ_LEN, result).astype(jnp.int32)


def draw_output_weight(key, part):
    key = jax.random.fold_in(key, 3)
    noise = jnp.clip(jax.random.normal(key, (D, D), jnp.float32), -5.0, 5.0)
    return noise * (4.0 / math.sqrt(D)) * rising(D)[:, None]


def draw_shrink_weight(key, part):
    key = jax.random.fold_in(key, 4)
    noise = jnp.clip(jax.random.normal(key, (FF, D), jnp.float32), -5.0, 5.0)
    return noise * (1.0 / math.sqrt(FF)) * rising(FF)[:, None]


def draw_layer_vectors(key, part):
    key = jax.random.fold_in(key, 5)
    noise = jnp.clip(jax.random.normal(key, (6, D), jnp.float32), -4.0, 4.0)
    gain_one = rising(D) * (1.0 + 0.1 * noise[0])
    gain_two = rising(D) * (1.0 + 0.1 * noise[2])
    return jnp.stack([gain_one, 0.2 * noise[1], gain_two, 0.2 * noise[3], 0.2 * noise[4], 0.2 * noise[5]])


def draw_first_input(key, part):
    key = jax.random.fold_in(key, 11)
    return first_state(key, (D, 3, D), 1.0)


def draw_first_output(key, part):
    key = jax.random.fold_in(key, 12)
    return first_state(key, (D, D), 1.0)


def draw_first_expand(key, part):
    key = jax.random.fold_in(key, 13)
    return first_state(key, (D, FF), 1.0)


def draw_first_shrink(key, part):
    key = jax.random.fold_in(key, 14)
    return first_state(key, (FF, D), 1.0)


def draw_first_vectors(key, part):
    key = jax.random.fold_in(key, 15)
    return first_state(key, (6, D), 4.0)


def draw_first_head(key, part):
    key = jax.random.fold_in(key, 16)
    return first_state(key, (2, D), 2.0)


def draw_first_bias(key, part):
    key = jax.random.fold_in(key, 17)
    return first_state(key, (FF,), 0.6)


def draw_second_input(key, part):
    key = jax.random.fold_in(key, 21)
    return second_state(key, (D, 3, D), 1.0)


def draw_second_output(key, part):
    key = jax.random.fold_in(key, 22)
    return second_state(key, (D, D), 1.0)


def draw_second_expand(key, part):
    key = jax.random.fold_in(key, 23)
    return second_state(key, (D, FF), 1.0)


def draw_second_shrink(key, part):
    key = jax.random.fold_in(key, 24)
    return second_state(key, (FF, D), 1.0)


def draw_second_vectors(key, part):
    key = jax.random.fold_in(key, 25)
    return second_state(key, (6, D), 4.0)


def draw_second_head(key, part):
    key = jax.random.fold_in(key, 26)
    return second_state(key, (2, D), 2.0)


def draw_second_bias(key, part):
    key = jax.random.fold_in(key, 27)
    return second_state(key, (FF,), 0.6)


def shard_levels(stream_key, extent, cuts, smallest, top_value):
    factor_of, own = 1.0, jax.random.fold_in(stream_key, 6)
    for dim, parts in cuts:
        heights = jnp.exp(jax.random.uniform(jax.random.fold_in(own, dim), (parts,), jnp.float32, smallest / len(cuts), top_value / len(cuts)))
        factor_of = factor_of * jnp.repeat(heights, extent[dim] // parts).reshape([-1 if axis == dim else 1 for axis in range(len(extent))])
    return factor_of


def bell_draw(rng, shape, scale, limit, shards=(), held_as=jnp.bfloat16):
    factor_of = shard_levels(rng, shape, shards, -0.22, 0.18) if shards else 1.0
    array = jax.random.normal(rng, shape, jnp.float32) * scale * factor_of
    return jnp.minimum(jnp.maximum(array, -limit), limit).astype(held_as)


def setup_inputs(seed: int = 0) -> dict:
    splits = jax.random.split(jax.random.key(seed), 25)
    tokens = bell_draw(splits[0], (TOKENS, D), 1.0, 6.0, ((0, 32),))
    cotangent = draw_cotangent(jax.random.fold_in(splits[24], 71), 0)
    lengths = draw_lengths(jax.random.fold_in(splits[24], 71), 0)
    input_weight = bell_draw(splits[3], (D, 3, D), D ** -0.5, 0.21875, ((0, 8), (2, 4)), jnp.float32)
    output_weight = draw_output_weight(jax.random.fold_in(splits[24], 71), 0)
    expand_weight = bell_draw(splits[5], (D, FF), D ** -0.5, 0.21875, ((0, 8), (1, 4)), jnp.float32)
    shrink_weight = draw_shrink_weight(jax.random.fold_in(splits[24], 71), 0)
    layer_vectors = draw_layer_vectors(jax.random.fold_in(splits[24], 71), 0)
    head_bias = bell_draw(splits[8], (2, D), 0.2, 1.0, ((1, 4),), jnp.float32)
    expand_bias = bell_draw(splits[9], (FF,), 0.2, 1.0, ((0, 4),), jnp.float32)
    first_input = draw_first_input(jax.random.fold_in(splits[24], 71), 0)
    first_output = draw_first_output(jax.random.fold_in(splits[24], 71), 0)
    first_expand = draw_first_expand(jax.random.fold_in(splits[24], 71), 0)
    first_shrink = draw_first_shrink(jax.random.fold_in(splits[24], 71), 0)
    first_vectors = draw_first_vectors(jax.random.fold_in(splits[24], 71), 0)
    first_head = draw_first_head(jax.random.fold_in(splits[24], 71), 0)
    first_bias = draw_first_bias(jax.random.fold_in(splits[24], 71), 0)
    second_input = draw_second_input(jax.random.fold_in(splits[24], 71), 0)
    second_output = draw_second_output(jax.random.fold_in(splits[24], 71), 0)
    second_expand = draw_second_expand(jax.random.fold_in(splits[24], 71), 0)
    second_shrink = draw_second_shrink(jax.random.fold_in(splits[24], 71), 0)
    second_vectors = draw_second_vectors(jax.random.fold_in(splits[24], 71), 0)
    second_head = draw_second_head(jax.random.fold_in(splits[24], 71), 0)
    second_bias = draw_second_bias(jax.random.fold_in(splits[24], 71), 0)
    return dict(tokens=tokens, cotangent=cotangent, lengths=lengths, input_weight=input_weight, output_weight=output_weight, expand_weight=expand_weight, shrink_weight=shrink_weight, layer_vectors=layer_vectors, head_bias=head_bias, expand_bias=expand_bias, first_input=first_input, first_output=first_output, first_expand=first_expand, first_shrink=first_shrink, first_vectors=first_vectors, first_head=first_head, first_bias=first_bias, second_input=second_input, second_output=second_output, second_expand=second_expand, second_shrink=second_shrink, second_vectors=second_vectors, second_head=second_head, second_bias=second_bias)


@jax.custom_vjp
def low(v):
    return lax.optimization_barrier(v.astype(jnp.bfloat16)).astype(jnp.float32)

@jax.custom_vjp
def low_back(v):
    return v

def low_keep(v):
    return (low(v), None)

def low_pass(kept, grad):
    return (grad,)

def back_keep(v):
    return (v, None)

def back_low(kept, grad):
    return (low(grad),)
low.defvjp(low_keep, low_pass)
low_back.defvjp(back_keep, back_low)
eps_norm = 1e-05
clip_norm = 1.0
beta_one = 0.9
beta_two = 0.999
adam_eps = 1e-08
rate = 0.05
vector_rate = 0.5
decay = 0.01
highest = lax.Precision.HIGHEST

def layer_norm(values, norm_gain, norm_shift):
    average = lax.optimization_barrier(jnp.mean(values, axis=-1, keepdims=True))
    centred = values - average
    inverse = lax.rsqrt(lax.optimization_barrier(jnp.mean(centred * centred, axis=-1, keepdims=True)) + eps_norm)
    return centred * inverse * norm_gain + norm_shift

def attention_layer(params, inputs, length):
    input_weight, output_weight, expand_weight, shrink_weight, layer_vectors, head_bias, expand_bias = params
    seq_length = inputs.shape[0]
    normed = low(layer_norm(inputs, layer_vectors[0], layer_vectors[1]))
    projected = jnp.einsum('td,dce->tce', normed, low(input_weight), precision=highest)
    bias_rows = jnp.stack([head_bias[0], jnp.zeros_like(head_bias[0]), head_bias[1]])
    packed = low_back(low(projected + bias_rows[None])).reshape(seq_length, 3, HEADS, HEAD_DIM)
    scores = jnp.einsum('qhd,khd->hqk', packed[:, 0], packed[:, 1], precision=highest) * HEAD_DIM ** (-0.5)
    scores = low_back(scores)
    row_ids = jnp.arange(seq_length)[:, None]
    col_ids = jnp.arange(seq_length)[None, :]
    visible = (col_ids <= row_ids) & (col_ids < length)
    scores = jnp.where(visible[None], scores, -1e+30)
    probabilities = jax.nn.softmax(scores, axis=-1)
    mixture = jnp.einsum('hqk,khd->qhd', low(probabilities), packed[:, 2], precision=highest)
    row_live = (jnp.arange(seq_length) < length)[:, None, None]
    mixture = low_back(low(jnp.where(row_live, mixture, 0.0))).reshape(seq_length, D)
    attended = low_back(jnp.dot(mixture, low(output_weight), precision=highest)) + layer_vectors[4]
    middle = inputs + attended
    hidden_in = low(layer_norm(middle, layer_vectors[2], layer_vectors[3]))
    pre_act = low_back(jnp.dot(hidden_in, low(expand_weight), precision=highest) + expand_bias)
    activation = low(jax.nn.gelu(pre_act, approximate=True))
    shrunk = low_back(jnp.dot(activation, low(shrink_weight), precision=highest)) + layer_vectors[5]
    return middle + shrunk

def adam_step(weight, gradient, first_old, second_old, factor, step_rate):
    scaled = gradient * factor
    moment = beta_one * first_old + (1.0 - beta_one) * scaled
    square = beta_two * second_old + (1.0 - beta_two) * scaled * scaled
    corrected = moment / (1.0 - beta_one ** STEP)
    spread = jnp.sqrt(square / (1.0 - beta_two ** STEP))
    updated = weight - step_rate * (corrected / (spread + adam_eps) + decay * weight)
    return (moment, square, updated)

def reference(tokens, cotangent, lengths, input_weight, output_weight, expand_weight, shrink_weight, layer_vectors, head_bias, expand_bias, first_input, first_output, first_expand, first_shrink, first_vectors, first_head, first_bias, second_input, second_output, second_expand, second_shrink, second_vectors, second_head, second_bias):
    params = (input_weight, output_weight, expand_weight, shrink_weight, layer_vectors, head_bias, expand_bias)
    seq_tokens = tokens.astype(jnp.float32).reshape(NSEQ, SEQ_LEN, D)
    seq_backs = cotangent.astype(jnp.float32).reshape(NSEQ, SEQ_LEN, D)

    def visit(running, bundle):
        seq_inputs, seq_back, length = bundle

        def apply_layer(weights_now, inputs_now):
            return attention_layer(weights_now, inputs_now, length)
        outputs, pullback = jax.vjp(apply_layer, params, seq_inputs)
        weight_grads, input_grads = pullback(seq_back)
        running = jax.tree.map(jnp.add, running, weight_grads)
        return (running, (outputs, input_grads))
    initial = jax.tree.map(jnp.zeros_like, params)
    totals, (outputs, input_grads) = lax.scan(visit, initial, (seq_tokens, seq_backs, lengths))
    squared = sum((jnp.sum(leaf_grad * leaf_grad) for leaf_grad in totals))
    grad_norm = jnp.sqrt(squared)
    factor = clip_norm / jnp.maximum(grad_norm, clip_norm)
    moment_input, square_input, updated_input = adam_step(input_weight, totals[0], first_input, second_input, factor, rate)
    moment_output, square_output, updated_output = adam_step(output_weight, totals[1], first_output, second_output, factor, rate)
    moment_expand, square_expand, updated_expand = adam_step(expand_weight, totals[2], first_expand, second_expand, factor, rate)
    moment_shrink, square_shrink, updated_shrink = adam_step(shrink_weight, totals[3], first_shrink, second_shrink, factor, rate)
    moment_vectors, square_vectors, updated_vectors = adam_step(layer_vectors, totals[4], first_vectors, second_vectors, factor, vector_rate)
    moment_head, square_head, updated_head = adam_step(head_bias, totals[5], first_head, second_head, factor, vector_rate)
    moment_bias, square_bias, updated_bias = adam_step(expand_bias, totals[6], first_bias, second_bias, factor, vector_rate)
    block_out = outputs.reshape(TOKENS, D).astype(jnp.bfloat16)
    token_grad = input_grads.reshape(TOKENS, D).astype(jnp.bfloat16)
    return (block_out, token_grad, grad_norm, moment_input, square_input, updated_input, moment_output, square_output, updated_output, moment_expand, square_expand, updated_expand, moment_shrink, square_shrink, updated_shrink, moment_vectors, square_vectors, updated_vectors, moment_head, square_head, updated_head, moment_bias, square_bias, updated_bias)
```

```python
import jax
import jax.numpy as jnp
from jax import lax
from jax.sharding import PartitionSpec as P

HEAD_DIM = 64
BLOCK = 512
STEP = 10


eps_norm = 1e-05
clip_norm = 1.0
beta_one = 0.9
beta_two = 0.999
adam_eps = 1e-08
rate = 0.05
vector_rate = 0.5
decay = 0.01
excluded = -1e30


def layer_norm(values, norm_gain, norm_shift):
    average = jnp.mean(values, axis=-1, keepdims=True)
    centred = values - average
    inverse = lax.rsqrt(jnp.mean(centred * centred, axis=-1, keepdims=True) + eps_norm)
    return centred * inverse * norm_gain + norm_shift


def gelu_tanh(values):
    return jax.nn.gelu(values, approximate=True)


def block_scores(queries, key_rows, first_row, length):
    scores = jnp.einsum(
        "qhd,khd->hqk", queries, key_rows, preferred_element_type=jnp.float32
    ) * HEAD_DIM ** (-0.5)
    row_ids = first_row + jnp.arange(queries.shape[0])[:, None]
    col_ids = jnp.arange(key_rows.shape[0])[None, :]
    visible = (col_ids <= row_ids) & (col_ids < length)
    return (jnp.where(visible[None], scores, excluded), visible)


def forward_block(queries, key_rows, value_rows, first_row, length):
    scores, visible = block_scores(queries, key_rows, first_row, length)
    row_max = jnp.max(scores, axis=-1, keepdims=True)
    weights = jnp.exp(scores - row_max)
    totals = jnp.sum(weights, axis=-1, keepdims=True)
    probabilities = (weights / totals).astype(jnp.bfloat16)
    mixture = jnp.einsum(
        "hqk,khd->qhd", probabilities, value_rows, preferred_element_type=jnp.float32
    )
    row_live = (first_row + jnp.arange(queries.shape[0]) < length)[:, None, None]
    mixture = jnp.where(row_live, mixture, 0.0).astype(jnp.bfloat16)
    return (mixture, (row_max + jnp.log(totals))[..., 0])


def attend_forward(packed, length):
    mixtures = []
    log_parts = []
    for block_index in range(packed.shape[0] // BLOCK):
        first_row = block_index * BLOCK
        last_row = first_row + BLOCK
        queries = packed[first_row:last_row, 0]
        key_rows = packed[:last_row, 1]
        value_rows = packed[:last_row, 2]
        mixture, log_total = forward_block(queries, key_rows, value_rows, first_row, length)
        mixtures.append(mixture)
        log_parts.append(log_total)
    return (jnp.concatenate(mixtures, axis=0), jnp.concatenate(log_parts, axis=1))


def backward_block(queries, key_rows, value_rows, upstream, log_total, first_row, length):
    scores, visible = block_scores(queries, key_rows, first_row, length)
    probabilities = jnp.exp(scores - log_total[..., None])
    prob_grad = jnp.einsum("qhd,khd->hqk", upstream, value_rows, preferred_element_type=jnp.float32)
    inner = jnp.sum(probabilities * prob_grad, axis=-1, keepdims=True)
    score_grad = jnp.where(visible[None], probabilities * (prob_grad - inner), 0.0).astype(
        jnp.bfloat16
    )
    scale_factor = HEAD_DIM ** (-0.5)
    query_grad = (
        jnp.einsum("hqk,khd->qhd", score_grad, key_rows, preferred_element_type=jnp.float32)
        * scale_factor
    )
    key_grad = (
        jnp.einsum("hqk,qhd->khd", score_grad, queries, preferred_element_type=jnp.float32)
        * scale_factor
    )
    value_grad = jnp.einsum(
        "hqk,qhd->khd",
        probabilities.astype(jnp.bfloat16),
        upstream,
        preferred_element_type=jnp.float32,
    )
    return (query_grad, key_grad, value_grad)


def attend_backward(packed, mixture_grad, log_totals, length):
    seq_length = packed.shape[0]
    key_sum = jnp.zeros(packed[:, 1].shape, jnp.float32)
    value_sum = jnp.zeros(packed[:, 2].shape, jnp.float32)
    query_parts = []
    for block_index in range(seq_length // BLOCK):
        first_row = block_index * BLOCK
        last_row = first_row + BLOCK
        queries = packed[first_row:last_row, 0]
        key_rows = packed[:last_row, 1]
        value_rows = packed[:last_row, 2]
        upstream = mixture_grad[first_row:last_row]
        log_total = log_totals[:, first_row:last_row]
        query_grad, key_grad, value_grad = backward_block(
            queries, key_rows, value_rows, upstream, log_total, first_row, length
        )
        query_parts.append(query_grad)
        key_sum = key_sum.at[:last_row].add(key_grad)
        value_sum = value_sum.at[:last_row].add(value_grad)
    query_all = jnp.concatenate(query_parts, axis=0)
    return jnp.stack([query_all, key_sum, value_sum], axis=1).astype(jnp.bfloat16)


CORE_ORDERS = ((4, 3, 2, 1), (1, 4, 3, 2))


def flat_index():
    return lax.axis_index("dp") * lax.axis_size("mp") + lax.axis_index("mp")


def cube_permute(values, stage):
    pairs = []
    for device in range(32):
        pairs.append((device, device ^ (1 << CORE_ORDERS[device & 1][stage])))
    return lax.ppermute(values, ("dp", "mp"), pairs)


def twin_permute(values):
    return lax.ppermute(values, ("dp", "mp"), [(device, device ^ 1) for device in range(32)])


def place(relative, core):
    spots = []
    for order in CORE_ORDERS:
        spots.append(sum(((relative >> bit) & 1) << step for step, bit in enumerate(order)))
    return jnp.where(core == 0, spots[0], spots[1])


def gather_blocks(shard):
    count = lax.axis_size("dp") * lax.axis_size("mp")
    if count != 32:
        first = lax.all_gather(shard, ("dp", "mp"), axis=0, tiled=False)
        return first
    held = shard[None]
    for stage in range(4):
        held = jnp.concatenate([held, cube_permute(held, stage)], axis=0)
    both = jnp.concatenate([held, twin_permute(held)], axis=0)
    me = flat_index()
    core = me & 1
    distance = jnp.arange(32) ^ me
    other = distance & 1
    index = place(distance, core ^ other) + 16 * other
    return jnp.take(both, index, axis=0)


def scatter_blocks(blocks):
    count = lax.axis_size("dp") * lax.axis_size("mp")
    if count != 32:
        return lax.psum_scatter(blocks, ("dp", "mp"), scatter_dimension=0, tiled=False)
    me = flat_index()
    core = me & 1
    devices = jnp.arange(32)
    distance = devices ^ me
    spots = place(distance, core ^ (distance & 1)) + 16 * (distance & 1)
    index = jnp.zeros((32,), jnp.int32).at[spots].set(devices)
    sorted_blocks = jnp.take(blocks, index, axis=0)
    held = sorted_blocks[:16] + twin_permute(sorted_blocks[16:])
    for stage in reversed(range(4)):
        half = 1 << stage
        held = held[:half] + cube_permute(held[half:], stage)
    return held[0]


def adam_step(weight, gradient, first_old, second_old, factor, step_rate):
    scaled = gradient * factor
    moment = beta_one * first_old + (1.0 - beta_one) * scaled
    square = beta_two * second_old + (1.0 - beta_two) * scaled * scaled
    corrected = moment / (1.0 - beta_one**STEP)
    spread = jnp.sqrt(square / (1.0 - beta_two**STEP))
    updated = weight - step_rate * (corrected / (spread + adam_eps) + decay * weight)
    return (moment, square, updated)


def squares(values):
    return jnp.sum(values * values)


def shards(
    tokens,
    cotangent,
    lengths,
    input_weight,
    output_weight,
    expand_weight,
    shrink_weight,
    layer_vectors,
    head_bias,
    expand_bias,
    first_input,
    first_output,
    first_expand,
    first_shrink,
    first_vectors,
    first_head,
    first_bias,
    second_input,
    second_output,
    second_expand,
    second_shrink,
    second_vectors,
    second_head,
    second_bias,
):
    dp_count = lax.axis_size("dp")
    mp_count = lax.axis_size("mp")
    count = dp_count * mp_count
    rows = input_weight.shape[0]
    width = input_weight.shape[2]
    hidden = expand_weight.shape[1]
    depth = tokens.shape[1]
    seq_length = tokens.shape[0]
    model_index = lax.axis_index("mp")
    low = jnp.bfloat16
    packed_shard = jnp.concatenate(
        [
            input_weight.astype(low).reshape(rows, 3 * width),
            output_weight.astype(low).T,
            expand_weight.astype(low),
            shrink_weight.astype(low).T,
        ],
        axis=1,
    )
    columns = packed_shard.shape[1]
    gathered = gather_blocks(packed_shard).reshape(dp_count, mp_count, rows, columns)
    wide_input = (
        gathered[..., : 3 * width]
        .reshape(dp_count, mp_count, rows, 3, width)
        .transpose(0, 2, 3, 1, 4)
        .reshape(depth, 3, mp_count * width)
    )

    def wide(first, last):
        piece = gathered[..., first:last]
        return piece.transpose(0, 2, 1, 3).reshape(depth, mp_count * (last - first))

    output_t = wide(3 * width, 4 * width)
    wide_expand = wide(4 * width, 4 * width + hidden)
    shrink_t = wide(4 * width + hidden, columns)

    local_length = lax.dynamic_index_in_dim(lengths, model_index, 0, keepdims=False)
    residual = tokens.astype(jnp.float32)
    back_rows = cotangent.astype(jnp.float32)
    norm_one, pull_one = jax.vjp(layer_norm, residual, layer_vectors[0], layer_vectors[1])
    normed = norm_one.astype(low)
    projected = jnp.einsum("td,dce->tce", normed, wide_input, preferred_element_type=jnp.float32)
    full_head = lax.all_gather(head_bias, "mp", axis=1, tiled=True)
    full_bias = lax.all_gather(expand_bias, "mp", axis=0, tiled=True)
    bias_rows = jnp.stack([full_head[0], jnp.zeros_like(full_head[0]), full_head[1]])
    head_count = depth // HEAD_DIM
    packed = (projected + bias_rows[None]).astype(low).reshape(seq_length, 3, head_count, HEAD_DIM)
    mixture, log_totals = attend_forward(packed, local_length)
    mixture_flat = mixture.reshape(seq_length, depth)
    attended = jnp.einsum("tc,dc->td", mixture_flat, output_t, preferred_element_type=jnp.float32)
    middle = residual + attended + layer_vectors[4]
    norm_two, pull_two = jax.vjp(layer_norm, middle, layer_vectors[2], layer_vectors[3])
    hidden_in = norm_two.astype(low)
    pre_act = jnp.dot(hidden_in, wide_expand, preferred_element_type=jnp.float32) + full_bias
    activation, pull_gelu = jax.vjp(gelu_tanh, pre_act)
    activation = activation.astype(low)
    shrunk = jnp.einsum("tf,df->td", activation, shrink_t, preferred_element_type=jnp.float32)
    block_out = (middle + shrunk + layer_vectors[5]).astype(low)
    grad_shrink_t = jnp.einsum("td,tf->df", cotangent, activation, preferred_element_type=jnp.float32)
    act_grad = jnp.dot(cotangent, shrink_t, preferred_element_type=jnp.float32)
    pre_grad = pull_gelu(act_grad)[0].astype(low)
    grad_expand = jnp.einsum("td,tf->df", hidden_in, pre_grad, preferred_element_type=jnp.float32)
    bias_grad = jnp.sum(pre_grad.astype(jnp.float32), axis=0)
    norm_two_grad = jnp.einsum("tf,df->td", pre_grad, wide_expand, preferred_element_type=jnp.float32)
    middle_part, gain_two_grad, shift_two_grad = pull_two(norm_two_grad)
    middle_grad = back_rows + middle_part
    attend_grad = middle_grad.astype(low)
    grad_output_t = jnp.einsum("td,tc->dc", attend_grad, mixture_flat, preferred_element_type=jnp.float32)
    mixture_grad = jnp.dot(attend_grad, output_t, preferred_element_type=jnp.float32).astype(low)
    alive = (jnp.arange(seq_length) < local_length)[:, None]
    mixture_grad = jnp.where(alive, mixture_grad, jnp.zeros_like(mixture_grad))
    packed_grad = attend_backward(
        packed, mixture_grad.reshape(seq_length, head_count, HEAD_DIM), log_totals, local_length
    ).reshape(seq_length, 3, depth)
    grad_input = jnp.einsum("td,tce->dce", normed, packed_grad, preferred_element_type=jnp.float32)
    part_sums = jnp.sum(packed_grad.astype(jnp.float32), axis=0)
    head_grad = jnp.stack([part_sums[0], part_sums[2]])
    norm_one_grad = jnp.einsum("tce,dce->td", packed_grad, wide_input, preferred_element_type=jnp.float32)
    input_part, gain_one_grad, shift_one_grad = pull_one(norm_one_grad)
    token_grad = (middle_grad + input_part).astype(low)

    def blocks(values):
        return (
            values.astype(low)
            .reshape(dp_count, rows, mp_count, values.shape[1] // mp_count)
            .transpose(0, 2, 1, 3)
        )

    grad_blocks = jnp.concatenate(
        [
            grad_input.astype(low)
            .reshape(dp_count, rows, 3, mp_count, width)
            .transpose(0, 3, 1, 2, 4)
            .reshape(dp_count, mp_count, rows, 3 * width),
            blocks(grad_output_t),
            blocks(grad_expand),
            blocks(grad_shrink_t),
        ],
        axis=3,
    ).reshape(count, rows, columns)
    own = scatter_blocks(grad_blocks).astype(jnp.float32)
    input_total = own[:, : 3 * width].reshape(rows, 3, width)
    output_total = own[:, 3 * width : 4 * width].T
    expand_total = own[:, 4 * width : 4 * width + hidden]
    shrink_total = own[:, 4 * width + hidden :].T

    vector_local = jnp.stack(
        [
            gain_one_grad,
            shift_one_grad,
            gain_two_grad,
            shift_two_grad,
            jnp.sum(middle_grad, axis=0),
            jnp.sum(back_rows, axis=0),
        ]
    )
    vector_grad, head_summed, bias_summed = lax.psum(
        (vector_local, head_grad, bias_grad), ("dp", "mp")
    )
    head_total = lax.dynamic_slice_in_dim(head_summed, model_index * width, width, 1)
    bias_total = lax.dynamic_slice_in_dim(bias_summed, model_index * hidden, hidden, 0)
    owned = (
        squares(input_total) + squares(output_total) + squares(expand_total) + squares(shrink_total)
    )
    squared = (
        lax.psum(owned, ("dp", "mp"))
        + squares(vector_grad)
        + squares(head_summed)
        + squares(bias_summed)
    )
    grad_norm = jnp.sqrt(squared)
    factor = clip_norm / jnp.maximum(grad_norm, clip_norm)
    moment_input, square_input, updated_input = adam_step(
        input_weight, input_total, first_input, second_input, factor, rate
    )
    moment_output, square_output, updated_output = adam_step(
        output_weight, output_total, first_output, second_output, factor, rate
    )
    moment_expand, square_expand, updated_expand = adam_step(
        expand_weight, expand_total, first_expand, second_expand, factor, rate
    )
    moment_shrink, square_shrink, updated_shrink = adam_step(
        shrink_weight, shrink_total, first_shrink, second_shrink, factor, rate
    )
    moment_vectors, square_vectors, updated_vectors = adam_step(
        layer_vectors, vector_grad, first_vectors, second_vectors, factor, vector_rate
    )
    moment_head, square_head, updated_head = adam_step(
        head_bias, head_total, first_head, second_head, factor, vector_rate
    )
    moment_bias, square_bias, updated_bias = adam_step(
        expand_bias, bias_total, first_bias, second_bias, factor, vector_rate
    )
    return (
        block_out,
        token_grad,
        grad_norm,
        moment_input,
        square_input,
        updated_input,
        moment_output,
        square_output,
        updated_output,
        moment_expand,
        square_expand,
        updated_expand,
        moment_shrink,
        square_shrink,
        updated_shrink,
        moment_vectors,
        square_vectors,
        updated_vectors,
        moment_head,
        square_head,
        updated_head,
        moment_bias,
        square_bias,
        updated_bias,
    )


def solution(mesh):
    in_specs = (
        P(("dp", "mp"), None),
        P(("dp", "mp"), None),
        P("dp"),
        P("dp", None, "mp"),
        P("mp", "dp"),
        P("dp", "mp"),
        P("mp", "dp"),
        P(),
        P(None, "mp"),
        P("mp"),
        P("dp", None, "mp"),
        P("mp", "dp"),
        P("dp", "mp"),
        P("mp", "dp"),
        P(),
        P(None, "mp"),
        P("mp"),
        P("dp", None, "mp"),
        P("mp", "dp"),
        P("dp", "mp"),
        P("mp", "dp"),
        P(),
        P(None, "mp"),
        P("mp"),
    )
    out_specs = (
        P(("dp", "mp"), None),
        P(("dp", "mp"), None),
        P(),
        P("dp", None, "mp"),
        P("dp", None, "mp"),
        P("dp", None, "mp"),
        P("mp", "dp"),
        P("mp", "dp"),
        P("mp", "dp"),
        P("dp", "mp"),
        P("dp", "mp"),
        P("dp", "mp"),
        P("mp", "dp"),
        P("mp", "dp"),
        P("mp", "dp"),
        P(),
        P(),
        P(),
        P(None, "mp"),
        P(None, "mp"),
        P(None, "mp"),
        P("mp"),
        P("mp"),
        P("mp"),
    )
    return jax.shard_map(shards, mesh=mesh, in_specs=in_specs, out_specs=out_specs, check_vma=False)
```

```python
import functools
import jax
import jax.numpy as jnp
from jax import lax
from jax.experimental import pallas as pl
from jax.experimental.pallas import tpu as pltpu
from jax.sharding import PartitionSpec as P

HEAD_DIM = 64
TILE = 256
STEP = 10

eps_norm = 1e-05
clip_norm = 1.0
beta_one = 0.9
beta_two = 0.999
adam_eps = 1e-08
rate = 0.05
vector_rate = 0.5
decay = 0.01
excluded = -1e30
low = jnp.bfloat16
f32 = jnp.float32
GELU_A = 0.7978845608028654
GELU_B = GELU_A * 0.044715


def params(limit_mib, **kw):
    return pltpu.CompilerParams(vmem_limit_bytes=limit_mib * 1024 * 1024, **kw)


def cost(flops, moved, special=0):
    return pl.CostEstimate(flops=int(flops), bytes_accessed=int(moved), transcendentals=int(special))


def mm(a, b):
    return jnp.dot(a, b, preferred_element_type=f32)


def mm_nt(a, b):
    return lax.dot_general(a, b, (((1,), (1,)), ((), ())), preferred_element_type=f32)


def whole(shape):
    zeros = (0,) * len(shape)
    return pl.BlockSpec(shape, lambda *_: zeros)


def sds(shape, dtype):
    return jax.ShapeDtypeStruct(shape, dtype)


def live_blocks(length_ref, count, body):
    length = length_ref[0]
    for blocks in range(1, count + 1):
        low_end = (blocks - 1) * TILE
        high_end = blocks * TILE
        @pl.when((length > low_end) & (length <= high_end))
        def _(blocks=blocks):
            body(length, blocks)


def forward_body(length_ref, q_ref, k_ref, v_ref, o_ref, lse_ref, vt_ref):
    seq = q_ref.shape[0]
    vt_ref[...] = v_ref[...].T
    lane = lax.broadcasted_iota(jnp.int32, (TILE, 2 * HEAD_DIM), 1)
    causal = lax.broadcasted_iota(jnp.int32, (TILE, TILE), 0) <= lax.broadcasted_iota(jnp.int32, (TILE, TILE), 1)

    def run(length, blocks):
        tasks = [(b, h) for b in range(blocks) for h in range(2)]

        def scores(i):
            b, h = tasks[i]
            q = q_ref[b * TILE : (b + 1) * TILE, :] * jnp.asarray(HEAD_DIM**-0.5, low)
            qh = jnp.where((lane < HEAD_DIM) if h == 0 else (lane >= HEAD_DIM), q, jnp.zeros_like(q))
            return mm_nt(k_ref[: (b + 1) * TILE, :], qh)

        now = scores(0)
        outs = []
        for i, (b, h) in enumerate(tasks):
            start, stop = b * TILE, (b + 1) * TILE
            later = scores(i + 1) if i + 1 < len(tasks) else None
            last = jnp.where(causal, now[start:, :], excluded)
            top = jnp.max(last, axis=0, keepdims=True)
            if b:
                top = jnp.maximum(top, jnp.max(now[:start], axis=0, keepdims=True))
            p = jnp.exp(last - top)
            total = jnp.sum(p, axis=0, keepdims=True)
            pb = p.astype(low)
            if b:
                pf = jnp.exp(now[:start] - top)
                total = total + jnp.sum(pf, axis=0, keepdims=True)
                pb = jnp.concatenate([pf.astype(low), pb], axis=0)
            out = mm(vt_ref[h * HEAD_DIM : (h + 1) * HEAD_DIM, :stop], pb)
            outs.append(out / total)
            lse_ref[0, h : h + 1, start:stop] = top + jnp.log(total)
            if h:
                both = jnp.concatenate(outs, axis=0).T
                outs = []
                row = start + lax.broadcasted_iota(jnp.int32, both.shape, 0)
                o_ref[start:stop, :] = jnp.where(row < length, both, 0.0).astype(low)
            now = later
        if blocks * TILE < seq:
            o_ref[blocks * TILE :, :] = jnp.zeros((seq - blocks * TILE, 2 * HEAD_DIM), low)
            lse_ref[0, :, blocks * TILE :] = jnp.zeros((2, seq - blocks * TILE), f32)

    live_blocks(length_ref, seq // TILE, run)


def attend_forward(length, qkv):
    seq, width = qkv.shape[0], qkv.shape[1] // 3
    pair = 2 * HEAD_DIM
    pairs = width // pair
    half = seq * seq * 5 // 8
    spec = lambda part: pl.BlockSpec((seq, pair), lambda i, s: (0, part * pairs + i))
    return pl.pallas_call(
        forward_body,
        grid_spec=pltpu.PrefetchScalarGridSpec(
            num_scalar_prefetch=1,
            grid=(pairs,),
            in_specs=[spec(0), spec(1), spec(2)],
            out_specs=[
                pl.BlockSpec((seq, pair), lambda i, s: (0, i)),
                pl.BlockSpec((1, 2, seq), lambda i, s: (i, 0, 0)),
            ],
            scratch_shapes=[pltpu.VMEM((pair, seq), low)],
        ),
        out_shape=[sds((seq, width), low), sds((pairs, 2, seq), f32)],
        compiler_params=params(40),
        cost_estimate=cost(pairs * 2 * half * 2 * 2 * 256, seq * width * 8, pairs * 2 * half),
        name="attend_forward",
    )(length, qkv, qkv, qkv)


def backward_body(length_ref, q_ref, k_ref, v_ref, do_ref, lse_ref, out_ref, kt_ref, ksum, vsum):
    seq = q_ref.shape[0]
    scale = HEAD_DIM**-0.5
    kt_ref[...] = k_ref[...].T
    lane = lax.broadcasted_iota(jnp.int32, (TILE, 2 * HEAD_DIM), 1)
    causal = lax.broadcasted_iota(jnp.int32, (TILE, TILE), 0) <= lax.broadcasted_iota(jnp.int32, (TILE, TILE), 1)

    def run(length, blocks):
        tasks = [(b, h) for b in reversed(range(blocks)) for h in range(2)]

        def scores(i):
            b, h = tasks[i]
            mine = (lane < HEAD_DIM) if h == 0 else (lane >= HEAD_DIM)
            q = q_ref[b * TILE : (b + 1) * TILE, :] * jnp.asarray(scale, low)
            up = do_ref[b * TILE : (b + 1) * TILE, :]
            qh = jnp.where(mine, q, jnp.zeros_like(q))
            uh = jnp.where(mine, up, jnp.zeros_like(up))
            stop = (b + 1) * TILE
            return qh, uh, mm_nt(k_ref[:stop, :], qh), mm_nt(v_ref[:stop, :], uh)

        now = scores(0)
        dqs, dss, pbs, qs, us = [], [], [], [], []
        for i, (b, h) in enumerate(tasks):
            start, stop = b * TILE, (b + 1) * TILE
            later = scores(i + 1) if i + 1 < len(tasks) else None
            qh, uh, s, dp = now
            lse = lse_ref[0, h : h + 1, start:stop]
            p = jnp.exp(jnp.where(causal, s[start:], excluded) - lse)
            inner = jnp.sum(p * dp[start:], axis=0, keepdims=True)
            if b:
                pf = jnp.exp(s[:start] - lse)
                inner = inner + jnp.sum(pf * dp[:start], axis=0, keepdims=True)
            ds = (p * (dp[start:] - inner)).astype(low)
            pb = p.astype(low)
            if b:
                ds = jnp.concatenate([(pf * (dp[:start] - inner)).astype(low), ds], axis=0)
                pb = jnp.concatenate([pf.astype(low), pb], axis=0)
            dqs.append(mm(kt_ref[h * HEAD_DIM : (h + 1) * HEAD_DIM, :stop], ds))
            dss.append(ds)
            pbs.append(pb)
            qs.append(qh)
            us.append(uh)
            if h:
                dk = mm(jnp.concatenate(dss, axis=1), jnp.concatenate(qs, axis=0))
                dv = mm(jnp.concatenate(pbs, axis=1), jnp.concatenate(us, axis=0))
                if b == blocks - 1:
                    ksum[:stop, :] = dk
                    vsum[:stop, :] = dv
                else:
                    ksum[:stop, :] += dk
                    vsum[:stop, :] += dv
                out_ref[1, start:stop, :] = ksum[start:stop, :].astype(low)
                out_ref[2, start:stop, :] = vsum[start:stop, :].astype(low)
                out_ref[0, start:stop, :] = (jnp.concatenate(dqs, axis=0).T * scale).astype(low)
                dqs, dss, pbs, qs, us = [], [], [], [], []
            now = later
        if blocks * TILE < seq:
            rest = jnp.zeros((seq - blocks * TILE, 2 * HEAD_DIM), low)
            for part in range(3):
                out_ref[part, blocks * TILE :, :] = rest

    live_blocks(length_ref, seq // TILE, run)


def attend_backward(length, qkv, upstream, lse):
    seq, width = upstream.shape
    pair = 2 * HEAD_DIM
    pairs = width // pair
    half = seq * seq * 5 // 8
    spec = lambda part: pl.BlockSpec((seq, pair), lambda i, s: (0, part * pairs + i))
    own = pl.BlockSpec((seq, pair), lambda i, s: (0, i))
    return pl.pallas_call(
        backward_body,
        grid_spec=pltpu.PrefetchScalarGridSpec(
            num_scalar_prefetch=1,
            grid=(pairs,),
            in_specs=[spec(0), spec(1), spec(2), own, pl.BlockSpec((1, 2, seq), lambda i, s: (i, 0, 0))],
            out_specs=pl.BlockSpec((3, seq, pair), lambda i, s: (0, 0, i)),
            scratch_shapes=[
                pltpu.VMEM((pair, seq), low),
                pltpu.VMEM((seq, pair), f32),
                pltpu.VMEM((seq, pair), f32),
            ],
        ),
        out_shape=sds((3, seq, width), low),
        compiler_params=params(48),
        cost_estimate=cost(pairs * 2 * half * 5 * 2 * 256, seq * width * 14, pairs * 2 * half),
        name="attend_backward",
    )(length, qkv, qkv, qkv, upstream, lse)


def normalize(values):
    average = jnp.mean(values, axis=-1, keepdims=True)
    centred = values - average
    inverse = lax.rsqrt(jnp.mean(centred * centred, axis=-1, keepdims=True) + eps_norm)
    return centred * inverse, inverse


def pull_norm(scaled, unit, inverse):
    first = jnp.mean(scaled, axis=-1, keepdims=True)
    second = jnp.mean(scaled * unit, axis=-1, keepdims=True)
    return inverse * (scaled - first - unit * second)


def columns_of(values):
    return jnp.sum(values, axis=0, keepdims=True)


def prepare_body(x_ref, up_ref, vec_ref, h_ref, ht_ref, upt_ref):
    unit, _ = normalize(x_ref[...].astype(f32))
    h = (unit * vec_ref[0:1, :] + vec_ref[1:2, :]).astype(low)
    h_ref[...] = h
    ht_ref[...] = h.T
    upt_ref[...] = up_ref[...].T


def prepare(x, up, vectors):
    seq, depth = x.shape
    rows = pl.BlockSpec((TILE, depth), lambda i: (i, 0))
    turned = pl.BlockSpec((depth, TILE), lambda i: (0, i))
    return pl.pallas_call(
        prepare_body,
        grid=(seq // TILE,),
        in_specs=[rows, rows, whole(vectors.shape)],
        out_specs=[rows, turned, turned],
        out_shape=[sds((seq, depth), low), sds((depth, seq), low), sds((depth, seq), low)],
        compiler_params=params(24),
        cost_estimate=cost(seq * depth * 10, seq * depth * 10),
        name="prepare",
    )(x, up, vectors)


def project_body(core_ref, spots_ref, h_ref, mine_ref, twin_ref, bias_ref, qkv_ref, wide_ref):
    part = pl.program_id(0)
    rows = mine_ref.shape[1]
    width = mine_ref.shape[2] // 4
    groups = wide_ref.shape[1] // rows

    def collect(sources, index):
        at = slice(index * width, (index + 1) * width)
        for group in range(groups):
            pieces = [sources[model % 2][spots_ref[model, group], :, at] for model in range(4)]
            wide_ref[0, group * rows : (group + 1) * rows, :] = jnp.concatenate(pieces, axis=1)

    for index in range(4):
        for core in range(2):

            @pl.when((part == index) & (core_ref[0] == core))
            def _(index=index, core=core):
                collect((mine_ref, twin_ref) if core == 0 else (twin_ref, mine_ref), index)

    @pl.when(part < 3)
    def _():
        qkv_ref[...] = (mm(h_ref[...], wide_ref[0]) + bias_ref[0]).astype(low)


def project(core, spots, h, mine, twin, bias):
    seq, depth = h.shape
    return pl.pallas_call(
        project_body,
        grid_spec=pltpu.PrefetchScalarGridSpec(
            num_scalar_prefetch=2,
            grid=(4,),
            in_specs=[
                whole((seq, depth)),
                whole(mine.shape),
                whole(twin.shape),
                pl.BlockSpec((1, 1, depth), lambda i, *_: (jnp.minimum(i, 2), 0, 0)),
            ],
            out_specs=[
                pl.BlockSpec((seq, depth), lambda i, *_: (0, jnp.minimum(i, 2))),
                pl.BlockSpec((1, depth, depth), lambda i, *_: (i, 0, 0)),
            ],
        ),
        out_shape=[sds((seq, 3 * depth), low), sds((4, depth, depth), low)],
        compiler_params=params(40),
        cost_estimate=cost(2 * seq * depth * depth * 3, seq * depth * 16),
        name="project",
    )(core, spots, h, mine, twin, bias)


def attend_out_body(o_ref, w_ref, x_ref, vec_ref, middle_ref, h_ref, ht_ref):
    middle = x_ref[...].astype(f32) + mm_nt(o_ref[...], w_ref[0]) + vec_ref[4:5, :]
    middle_ref[...] = middle
    unit, _ = normalize(middle)
    h = (unit * vec_ref[2:3, :] + vec_ref[3:4, :]).astype(low)
    h_ref[...] = h
    ht_ref[...] = h.T


def attend_out(o, wide, x, vectors):
    seq, depth = x.shape
    rows = pl.BlockSpec((TILE, depth), lambda i: (i, 0))
    turned = pl.BlockSpec((depth, TILE), lambda i: (0, i))
    return pl.pallas_call(
        attend_out_body,
        grid=(seq // TILE,),
        in_specs=[
            rows,
            pl.BlockSpec((1, depth, depth), lambda i: (3, 0, 0)),
            rows,
            whole(vectors.shape),
        ],
        out_specs=[rows, rows, turned],
        out_shape=[sds((seq, depth), f32), sds((seq, depth), low), sds((depth, seq), low)],
        compiler_params=params(24),
        cost_estimate=cost(2 * seq * depth * depth, seq * depth * 14),
        name="attend_out",
    )(o, wide, x, vectors)


def feed_body(
    spots_ref,
    h2_ref,
    h2t_ref,
    up_ref,
    upt_ref,
    mine_a,
    mine_b,
    twin_a,
    twin_b,
    bias_ref,
    out_ref,
    back_ref,
    keep_a,
    keep_b,
    send_a,
    send_b,
    bias_grad_ref,
    wide_ref,
    act_ref,
    pre_ref,
):
    step = pl.program_id(0)
    side = lax.rem(step, 2)
    half = mine_a.shape[1]
    part = mine_a.shape[2] // 2
    groups = wide_ref.shape[0] // (2 * half)

    @pl.when(step == 0)
    def _():
        out_ref[...] = jnp.zeros_like(out_ref)
        back_ref[...] = jnp.zeros_like(back_ref)

    for group in range(groups):
        for which, (mine, twin) in enumerate(((mine_a, twin_a), (mine_b, twin_b))):
            first = (2 * group + which) * half
            own = mine[spots_ref[0, side, group]]
            other = twin[spots_ref[1, side, group]]
            wide_ref[first : first + half, :part] = own[:, :part]
            wide_ref[first : first + half, part : 2 * part] = other[:, :part]
            wide_ref[first : first + half, 2 * part : 3 * part] = own[:, part:]
            wide_ref[first : first + half, 3 * part :] = other[:, part:]

    expand = wide_ref[:, : 2 * part]
    shrink = wide_ref[:, 2 * part :]
    bias = bias_ref[0]
    sums = jnp.zeros((1, 2 * part), f32)
    for tile in range(h2_ref.shape[0] // TILE):
        at = slice(tile * TILE, (tile + 1) * TILE)
        u = mm(h2_ref[at, :], expand) + bias
        square = u * u
        th = jnp.tanh(u * (GELU_A + GELU_B * square))
        gate = 0.5 * th + 0.5
        slope = gate + (gate * (1.0 - gate)) * (u * (2.0 * GELU_A + (6.0 * GELU_B) * square))
        pre = (mm(up_ref[at, :], shrink) * slope).astype(low)
        act_ref[at, :] = (u * gate).astype(low)
        pre_ref[at, :] = pre
        sums = sums + columns_of(pre.astype(f32))
    bias_grad_ref[0] = sums
    out_ref[...] += mm_nt(act_ref[...], shrink)
    back_ref[...] += mm_nt(pre_ref[...], expand)
    grad_expand = mm(h2t_ref[...], pre_ref[...]).astype(low)
    grad_shrink = mm(upt_ref[...], act_ref[...]).astype(low)
    for group in range(groups):
        for which, (keep, send) in enumerate(((keep_a, send_a), (keep_b, send_b))):
            first = (2 * group + which) * half
            at = slice(first, first + half)
            own, other = spots_ref[0, side, group], spots_ref[1, side, group]
            keep[own, :, :part] = grad_expand[at, :part]
            keep[own, :, part:] = grad_shrink[at, :part]
            send[other, :, :part] = grad_expand[at, part:]
            send[other, :, part:] = grad_shrink[at, part:]


def feed(spots, h2, h2t, up, upt, pieces, bias):
    seq, depth = h2.shape
    slots, half, columns = pieces[0].shape
    steps = bias.shape[0]
    part = bias.shape[2] // 2
    piece = pl.BlockSpec((slots, half, 2 * part), lambda i, s: (0, 0, i // 2))
    bias_spec = pl.BlockSpec((1, 1, 2 * part), lambda i, s: (i, 0, 0))
    return pl.pallas_call(
        feed_body,
        grid_spec=pltpu.PrefetchScalarGridSpec(
            num_scalar_prefetch=1,
            grid=(steps,),
            in_specs=[
                whole((seq, depth)),
                whole((depth, seq)),
                whole((seq, depth)),
                whole((depth, seq)),
                piece,
                piece,
                piece,
                piece,
                bias_spec,
            ],
            out_specs=[whole((seq, depth)), whole((seq, depth)), piece, piece, piece, piece, bias_spec],
            scratch_shapes=[
                pltpu.VMEM((depth, 4 * part), low),
                pltpu.VMEM((seq, 2 * part), low),
                pltpu.VMEM((seq, 2 * part), low),
            ],
        ),
        out_shape=[sds((seq, depth), f32), sds((seq, depth), f32)]
        + [sds(pieces[0].shape, low)] * 4
        + [sds(bias.shape, f32)],
        compiler_params=params(60),
        cost_estimate=cost(12 * seq * depth * steps * 2 * part, seq * depth * 40, seq * steps * part),
        name="feed",
    )(spots, h2, h2t, up, upt, *pieces, bias)


def middle_back_body(
    length_ref,
    back_ref,
    out_ref,
    middle_ref,
    up_ref,
    o_ref,
    w_ref,
    vec_ref,
    block_ref,
    grad_ref,
    mixture_ref,
    weight_ref,
    sums_ref,
):
    step = pl.program_id(0)
    middle = middle_ref[...]
    block_ref[...] = (middle + out_ref[...] + vec_ref[5:6, :]).astype(low)
    unit, inverse = normalize(middle)
    back = back_ref[...]
    up = up_ref[...].astype(f32)
    grad = up + pull_norm(back * vec_ref[2:3, :], unit, inverse)
    grad_ref[...] = grad
    rounded = grad.astype(low)
    first = step * TILE
    row = first + lax.broadcasted_iota(jnp.int32, (TILE, grad.shape[1]), 0)
    mixture_ref[...] = jnp.where(row < length_ref[0], mm(rounded, w_ref[0]), 0.0).astype(low)
    share = mm(rounded.T, o_ref[...])
    sums = jnp.concatenate(
        [columns_of(back * unit), columns_of(back), columns_of(grad), columns_of(up)], axis=0
    )

    @pl.when(step == 0)
    def _():
        weight_ref[...] = share
        sums_ref[...] = sums

    @pl.when(step > 0)
    def _():
        weight_ref[...] += share
        sums_ref[...] += sums


def middle_back(length, back, out, middle, up, o, wide, vectors):
    seq, depth = middle.shape
    rows = pl.BlockSpec((TILE, depth), lambda i, s: (i, 0))
    return pl.pallas_call(
        middle_back_body,
        grid_spec=pltpu.PrefetchScalarGridSpec(
            num_scalar_prefetch=1,
            grid=(seq // TILE,),
            in_specs=[
                rows,
                rows,
                rows,
                rows,
                rows,
                pl.BlockSpec((1, depth, depth), lambda i, s: (3, 0, 0)),
                whole(vectors.shape),
            ],
            out_specs=[rows, rows, rows, whole((depth, depth)), whole((4, depth))],
        ),
        out_shape=[
            sds((seq, depth), low),
            sds((seq, depth), f32),
            sds((seq, depth), low),
            sds((depth, depth), f32),
            sds((4, depth), f32),
        ],
        compiler_params=params(32),
        cost_estimate=cost(4 * seq * depth * depth, seq * depth * 28),
        name="middle_back",
    )(length, back, out, middle, up, o, wide, vectors)


def input_grad_body(core_ref, spots_ref, ht_ref, back_ref, out_grad_ref, keep_ref, send_ref, sums_ref):
    part = pl.program_id(0)
    rows = keep_ref.shape[1]
    width = keep_ref.shape[2] // 4
    groups = ht_ref.shape[0] // rows

    def spread(targets, index, grad):
        at = slice(index * width, (index + 1) * width)
        for group in range(groups):
            for model in range(4):
                targets[model % 2][spots_ref[model, group], :, at] = grad[
                    group * rows : (group + 1) * rows, model * width : (model + 1) * width
                ]

    for index in range(4):

        @pl.when(part == index)
        def _(index=index):
            if index < 3:
                sums_ref[0] = columns_of(back_ref[0].astype(f32))
                grad = mm(ht_ref[...], back_ref[0]).astype(low)
            else:
                grad = out_grad_ref[...].astype(low)
            for core in range(2):

                @pl.when(core_ref[0] == core)
                def _(core=core):
                    spread((keep_ref, send_ref) if core == 0 else (send_ref, keep_ref), index, grad)


def input_grad(core, spots, ht, back, out_grad, slots, rows):
    depth, seq = ht.shape
    shape = (slots, rows, 4 * (depth // 4))
    return pl.pallas_call(
        input_grad_body,
        grid_spec=pltpu.PrefetchScalarGridSpec(
            num_scalar_prefetch=2,
            grid=(4,),
            in_specs=[
                whole((depth, seq)),
                pl.BlockSpec((1, seq, depth), lambda i, *_: (jnp.minimum(i, 2), 0, 0)),
                whole((depth, depth)),
            ],
            out_specs=[
                whole(shape),
                whole(shape),
                pl.BlockSpec((1, 1, depth), lambda i, *_: (jnp.minimum(i, 2), 0, 0)),
            ],
        ),
        out_shape=[sds(shape, low), sds(shape, low), sds((3, 1, depth), f32)],
        compiler_params=params(40),
        cost_estimate=cost(6 * seq * depth * depth, seq * depth * 14),
        name="input_grad",
    )(core, spots, ht, back, out_grad)


def token_back_body(back_ref, w_ref, x_ref, grad_ref, vec_ref, token_ref, sums_ref):
    step = pl.program_id(0)
    back = mm_nt(back_ref[0], w_ref[0]) + mm_nt(back_ref[1], w_ref[1]) + mm_nt(back_ref[2], w_ref[2])
    unit, inverse = normalize(x_ref[...].astype(f32))
    token_ref[...] = (grad_ref[...] + pull_norm(back * vec_ref[0:1, :], unit, inverse)).astype(low)
    sums = jnp.concatenate([columns_of(back * unit), columns_of(back)], axis=0)

    @pl.when(step == 0)
    def _():
        sums_ref[...] = sums

    @pl.when(step > 0)
    def _():
        sums_ref[...] += sums


def token_back(back, wide, x, grad, vectors):
    seq, depth = x.shape
    rows = pl.BlockSpec((TILE, depth), lambda i: (i, 0))
    return pl.pallas_call(
        token_back_body,
        grid=(seq // TILE,),
        in_specs=[
            pl.BlockSpec((3, TILE, depth), lambda i: (0, i, 0)),
            pl.BlockSpec((3, depth, depth), lambda i: (0, 0, 0)),
            rows,
            rows,
            whole(vectors.shape),
        ],
        out_specs=[rows, whole((2, depth))],
        out_shape=[sds((seq, depth), low), sds((2, depth), f32)],
        compiler_params=params(32),
        cost_estimate=cost(6 * seq * depth * depth, seq * depth * 16),
        name="token_back",
    )(back, wide, x, grad, vectors)


CORE_ORDERS = ((4, 3, 2, 1), (1, 4, 3, 2))
STAGES = 4


def cube_permute(values, stage):
    pairs = [(device, device ^ (1 << CORE_ORDERS[device & 1][stage])) for device in range(32)]
    return lax.ppermute(values, ("dp", "mp"), pairs)


def bit_permute(values, bit):
    return lax.ppermute(values, ("dp", "mp"), [(device, device ^ (1 << bit)) for device in range(32)])


def place(distance, core):
    spots = [
        sum(((distance >> bit) & 1) << step for step, bit in enumerate(order)) for order in CORE_ORDERS
    ]
    return jnp.where(core == 0, spots[0], spots[1])


def cube_gather(shard):
    held = shard[None]
    for stage in range(STAGES):
        held = jnp.concatenate([held, cube_permute(held, stage)], axis=0)
    return held, bit_permute(held, 0)


def cube_scatter(keep, send):
    other = bit_permute(send, 0)
    for stage in reversed(range(STAGES)):
        half = 1 << stage
        away = keep[half:] + other[half:]
        arrived = cube_permute(away, stage)
        keep, other = keep[:half] + other[:half], arrived
    return keep[0].astype(f32) + other[0].astype(f32)


def cube_sum(values):
    for bit in range(5):
        values = values + bit_permute(values, bit)
    return values


def adam_step(weight, gradient, first_old, second_old, factor, step_rate):
    scaled = gradient * factor
    moment = beta_one * first_old + (1.0 - beta_one) * scaled
    square = beta_two * second_old + (1.0 - beta_two) * scaled * scaled
    corrected = moment / (1.0 - beta_one**STEP)
    spread = jnp.sqrt(square / (1.0 - beta_two**STEP))
    updated = weight - step_rate * (corrected / (spread + adam_eps) + decay * weight)
    return (moment, square, updated)


def squares(values):
    return jnp.sum(values * values)


def shards(
    tokens,
    cotangent,
    lengths,
    input_weight,
    output_weight,
    expand_weight,
    shrink_weight,
    layer_vectors,
    head_bias,
    expand_bias,
    first_input,
    first_output,
    first_expand,
    first_shrink,
    first_vectors,
    first_head,
    first_bias,
    second_input,
    second_output,
    second_expand,
    second_shrink,
    second_vectors,
    second_head,
    second_bias,
):
    dp_count = lax.axis_size("dp")
    mp_count = lax.axis_size("mp")
    cube = dp_count == 8 and mp_count == 4
    rows = input_weight.shape[0]
    width = input_weight.shape[2]
    hidden = expand_weight.shape[1]
    seq, depth = tokens.shape
    part = hidden // 3
    model_index = lax.axis_index("mp")
    me = lax.axis_index("dp") * mp_count + model_index

    attend_shard = jnp.concatenate(
        [input_weight.astype(low).reshape(rows, 3 * width), output_weight.astype(low).T], axis=1
    )
    expand_low = expand_weight.astype(low)
    shrink_low = shrink_weight.astype(low).T
    feed_shard = jnp.concatenate(
        [
            piece[:, index * part : (index + 1) * part]
            for index in range(3)
            for piece in (expand_low, shrink_low)
        ],
        axis=1,
    )
    bias_shard = jnp.concatenate([head_bias.reshape(1, 2 * width), expand_bias[None]], axis=1)

    if cube:
        core = me & 1
        mine_attend, twin_attend = cube_gather(attend_shard)
        mine_a, twin_a = cube_gather(feed_shard[: rows // 2])
        mine_b, twin_b = cube_gather(feed_shard[rows // 2 :])
        bias_full = jnp.where(jnp.arange(4)[:, None] == model_index, bias_shard, 0.0)
        bias_full = bias_full + bit_permute(bias_full, 0)
        bias_full = bias_full + bit_permute(bias_full, 1)
        devices = jnp.arange(32).reshape(8, 4).T
        spots = place(devices ^ me, devices & 1).astype(jnp.int32)
        near = model_index
    else:
        core = jnp.zeros((), jnp.int32)

        def planes(shard):
            full = lax.all_gather(lax.all_gather(shard, "dp", axis=0, tiled=True), "mp", axis=0)
            full = full.reshape(2, 2, 8, depth // 8, shard.shape[1]).transpose(1, 0, 2, 3, 4)
            return full.reshape(2, 16, depth // 8, shard.shape[1])

        mine_attend, twin_attend = planes(attend_shard)
        feed_planes = planes(feed_shard)
        middle_row = depth // 16
        mine_a, twin_a = feed_planes[:, :, :middle_row]
        mine_b, twin_b = feed_planes[:, :, middle_row:]
        bias_full = lax.all_gather(bias_shard, "mp", axis=0, tiled=True)
        spots = (jnp.arange(4)[:, None] // 2 * 8 + jnp.arange(8)[None]).astype(jnp.int32)
        near = jnp.zeros((), jnp.int32)
    near_models = near ^ jnp.arange(4)
    near_spots = jnp.take(spots, near_models, axis=0).reshape(2, 2, 8).transpose(1, 0, 2)
    core = core.astype(jnp.int32).reshape(1)

    length = lax.dynamic_slice_in_dim(lengths, model_index, 1, 0)
    head_full = bias_full[:, : 2 * width].reshape(4, 2, width).transpose(1, 0, 2).reshape(2, depth)
    qkv_bias = jnp.stack([head_full[0], jnp.zeros_like(head_full[0]), head_full[1]])[:, None]
    feed_bias = (
        jnp.take(bias_full[:, 2 * width :], near_models, axis=0)
        .reshape(2, 2, 3, part)
        .transpose(2, 0, 1, 3)
        .reshape(6, 1, 2 * part)
    )

    normed, normed_t, upstream_t = prepare(tokens, cotangent, layer_vectors)
    qkv, wide = project(core, spots, normed, mine_attend, twin_attend, qkv_bias)
    mixture, log_totals = attend_forward(length, qkv)
    middle, hidden_in, hidden_t = attend_out(mixture, wide, tokens, layer_vectors)
    out, back, keep_a, keep_b, send_a, send_b, feed_bias_grad = feed(
        near_spots, hidden_in, hidden_t, cotangent, upstream_t, (mine_a, mine_b, twin_a, twin_b), feed_bias
    )
    block_out, middle_grad, mixture_grad, output_grad, middle_sums = middle_back(
        length, back, out, middle, cotangent, mixture, wide, layer_vectors
    )
    packed_grad = attend_backward(length, qkv, mixture_grad, log_totals)
    keep_attend, send_attend, head_sums = input_grad(
        core, spots, normed_t, packed_grad, output_grad, 16, depth // 8
    )
    token_grad, token_sums = token_back(packed_grad, wide, tokens, middle_grad, layer_vectors)

    bias_near = feed_bias_grad.reshape(3, 2, 2, part).transpose(1, 2, 0, 3).reshape(4, hidden)
    bias_grad = jnp.take(bias_near, near_models, axis=0)
    vector_local = jnp.concatenate(
        [token_sums, middle_sums, head_sums[0], head_sums[2], bias_grad.reshape(4, depth)], axis=0
    )
    if cube:
        feed_a = cube_scatter(keep_a, send_a)
        feed_b = cube_scatter(keep_b, send_b)
        attend_total = cube_scatter(keep_attend, send_attend)
        vector_total = cube_sum(vector_local)
        feed_total = jnp.concatenate([feed_a, feed_b], axis=0)
    else:

        def own_block(keep, send):
            full = jnp.stack([keep, send]).reshape(2, 2, 8, depth // 8, keep.shape[2])
            full = full.transpose(1, 0, 2, 3, 4).reshape(4, depth, keep.shape[2])
            full = lax.psum_scatter(full, "mp", scatter_dimension=0, tiled=False)
            return lax.psum_scatter(full, "dp", scatter_dimension=0, tiled=True).astype(f32)

        attend_total = own_block(keep_attend, send_attend)
        feed_total = own_block(
            jnp.concatenate([keep_a, keep_b], axis=1), jnp.concatenate([send_a, send_b], axis=1)
        )
        vector_total = lax.psum(vector_local, ("dp", "mp"))
    input_total = attend_total[:, : 3 * width].reshape(rows, 3, width)
    output_total = attend_total[:, 3 * width :].T
    pieces = feed_total.reshape(rows, 3, 2, part)
    expand_total = pieces[:, :, 0].reshape(rows, hidden)
    shrink_total = pieces[:, :, 1].reshape(rows, hidden).T
    vector_grad = vector_total[:6]
    head_total = lax.dynamic_slice_in_dim(vector_total[6:8], model_index * width, width, 1)
    bias_total = lax.dynamic_slice_in_dim(vector_total[8:].reshape(-1), model_index * hidden, hidden, 0)
    owned = jnp.sum(attend_total * attend_total) + jnp.sum(feed_total * feed_total)
    if cube:
        owned = cube_sum(jnp.full((8, 128), owned, f32))[0, 0]
    else:
        owned = lax.psum(owned, ("dp", "mp"))
    grad_norm = jnp.sqrt(owned + jnp.sum(vector_total * vector_total))
    factor = clip_norm / jnp.maximum(grad_norm, clip_norm)
    moment_input, square_input, updated_input = adam_step(
        input_weight, input_total, first_input, second_input, factor, rate
    )
    moment_output, square_output, updated_output = adam_step(
        output_weight, output_total, first_output, second_output, factor, rate
    )
    moment_expand, square_expand, updated_expand = adam_step(
        expand_weight, expand_total, first_expand, second_expand, factor, rate
    )
    moment_shrink, square_shrink, updated_shrink = adam_step(
        shrink_weight, shrink_total, first_shrink, second_shrink, factor, rate
    )
    moment_vectors, square_vectors, updated_vectors = adam_step(
        layer_vectors, vector_grad, first_vectors, second_vectors, factor, vector_rate
    )
    moment_head, square_head, updated_head = adam_step(
        head_bias, head_total, first_head, second_head, factor, vector_rate
    )
    moment_bias, square_bias, updated_bias = adam_step(
        expand_bias, bias_total, first_bias, second_bias, factor, vector_rate
    )
    return (
        block_out,
        token_grad,
        grad_norm,
        moment_input,
        square_input,
        updated_input,
        moment_output,
        square_output,
        updated_output,
        moment_expand,
        square_expand,
        updated_expand,
        moment_shrink,
        square_shrink,
        updated_shrink,
        moment_vectors,
        square_vectors,
        updated_vectors,
        moment_head,
        square_head,
        updated_head,
        moment_bias,
        square_bias,
        updated_bias,
    )


def solution(mesh):
    in_specs = (
        P(("dp", "mp"), None),
        P(("dp", "mp"), None),
        P("dp"),
        P("dp", None, "mp"),
        P("mp", "dp"),
        P("dp", "mp"),
        P("mp", "dp"),
        P(),
        P(None, "mp"),
        P("mp"),
        P("dp", None, "mp"),
        P("mp", "dp"),
        P("dp", "mp"),
        P("mp", "dp"),
        P(),
        P(None, "mp"),
        P("mp"),
        P("dp", None, "mp"),
        P("mp", "dp"),
        P("dp", "mp"),
        P("mp", "dp"),
        P(),
        P(None, "mp"),
        P("mp"),
    )
    out_specs = (
        P(("dp", "mp"), None),
        P(("dp", "mp"), None),
        P(),
        P("dp", None, "mp"),
        P("dp", None, "mp"),
        P("dp", None, "mp"),
        P("mp", "dp"),
        P("mp", "dp"),
        P("mp", "dp"),
        P("dp", "mp"),
        P("dp", "mp"),
        P("dp", "mp"),
        P("mp", "dp"),
        P("mp", "dp"),
        P("mp", "dp"),
        P(),
        P(),
        P(),
        P(None, "mp"),
        P(None, "mp"),
        P(None, "mp"),
        P("mp"),
        P("mp"),
        P("mp"),
    )
    return jax.shard_map(shards, mesh=mesh, in_specs=in_specs, out_specs=out_specs, check_vma=False)
```

```python
import functools
import jax
import jax.numpy as jnp
from jax import lax
from jax.experimental import pallas as pl
from jax.experimental.pallas import tpu as pltpu
from jax.sharding import PartitionSpec as P

HEAD_DIM = 64
TILE = 256
STEP = 10

eps_norm = 1e-05
clip_norm = 1.0
beta_one = 0.9
beta_two = 0.999
adam_eps = 1e-08
rate = 0.05
vector_rate = 0.5
decay = 0.01
excluded = -1e30
low = jnp.bfloat16
f32 = jnp.float32
GELU_A = 0.7978845608028654
GELU_B = GELU_A * 0.044715


def params(limit_mib, **kw):
    return pltpu.CompilerParams(vmem_limit_bytes=limit_mib * 1024 * 1024, **kw)


def cost(flops, moved, special=0):
    return pl.CostEstimate(flops=int(flops), bytes_accessed=int(moved), transcendentals=int(special))


def mm(a, b):
    return jnp.dot(a, b, preferred_element_type=f32)


def mm_nt(a, b):
    return lax.dot_general(a, b, (((1,), (1,)), ((), ())), preferred_element_type=f32)


def whole(shape):
    zeros = (0,) * len(shape)
    return pl.BlockSpec(shape, lambda *_: zeros)


def held_back(body, first, count):
    def run(*refs):
        return body(*refs[:first], *refs[first + count :])

    return run


LATER = pl.BlockSpec(memory_space=pl.ANY)


def sds(shape, dtype):
    return jax.ShapeDtypeStruct(shape, dtype)


def live_blocks(length_ref, count, body):
    length = length_ref[0]
    for blocks in range(1, count + 1):
        low_end = (blocks - 1) * TILE
        high_end = blocks * TILE
        @pl.when((length > low_end) & (length <= high_end))
        def _(blocks=blocks):
            body(length, blocks)


def forward_body(length_ref, q_ref, k_ref, v_ref, o_ref, lse_ref, vt_ref):
    seq = q_ref.shape[0]
    vt_ref[...] = v_ref[...].T
    lane = lax.broadcasted_iota(jnp.int32, (TILE, 2 * HEAD_DIM), 1)
    causal = lax.broadcasted_iota(jnp.int32, (TILE, TILE), 0) <= lax.broadcasted_iota(jnp.int32, (TILE, TILE), 1)

    def run(length, blocks):
        tasks = [(b, h) for b in range(blocks) for h in range(2)]

        def scores(i):
            b, h = tasks[i]
            q = q_ref[b * TILE : (b + 1) * TILE, :] * jnp.asarray(HEAD_DIM**-0.5, low)
            qh = jnp.where((lane < HEAD_DIM) if h == 0 else (lane >= HEAD_DIM), q, jnp.zeros_like(q))
            return mm_nt(k_ref[: (b + 1) * TILE, :], qh)

        now = scores(0)
        outs = []
        for i, (b, h) in enumerate(tasks):
            start, stop = b * TILE, (b + 1) * TILE
            later = scores(i + 1) if i + 1 < len(tasks) else None
            last = jnp.where(causal, now[start:, :], excluded)
            top = jnp.max(last, axis=0, keepdims=True)
            if b:
                top = jnp.maximum(top, jnp.max(now[:start], axis=0, keepdims=True))
            p = jnp.exp(last - top)
            total = jnp.sum(p, axis=0, keepdims=True)
            pb = p.astype(low)
            if b:
                pf = jnp.exp(now[:start] - top)
                total = total + jnp.sum(pf, axis=0, keepdims=True)
                pb = jnp.concatenate([pf.astype(low), pb], axis=0)
            out = mm(vt_ref[h * HEAD_DIM : (h + 1) * HEAD_DIM, :stop], pb)
            outs.append(out / total)
            lse_ref[0, h : h + 1, start:stop] = top + jnp.log(total)
            if h:
                both = jnp.concatenate(outs, axis=0).T
                outs = []
                row = start + lax.broadcasted_iota(jnp.int32, both.shape, 0)
                o_ref[start:stop, :] = jnp.where(row < length, both, 0.0).astype(low)
            now = later
        if blocks * TILE < seq:
            o_ref[blocks * TILE :, :] = jnp.zeros((seq - blocks * TILE, 2 * HEAD_DIM), low)
            lse_ref[0, :, blocks * TILE :] = jnp.zeros((2, seq - blocks * TILE), f32)

    live_blocks(length_ref, seq // TILE, run)


def attend_forward(length, qkv, after):
    seq, width = qkv.shape[0], qkv.shape[1] // 3
    pair = 2 * HEAD_DIM
    pairs = width // pair
    half = seq * seq * 5 // 8
    spec = lambda part: pl.BlockSpec((seq, pair), lambda i, s: (0, part * pairs + i))
    return pl.pallas_call(
        held_back(forward_body, 4, len(after)),
        grid_spec=pltpu.PrefetchScalarGridSpec(
            num_scalar_prefetch=1,
            grid=(pairs,),
            in_specs=[spec(0), spec(1), spec(2)] + [LATER] * len(after),
            out_specs=[
                pl.BlockSpec((seq, pair), lambda i, s: (0, i)),
                pl.BlockSpec((1, 2, seq), lambda i, s: (i, 0, 0)),
            ],
            scratch_shapes=[pltpu.VMEM((pair, seq), low)],
        ),
        out_shape=[sds((seq, width), low), sds((pairs, 2, seq), f32)],
        compiler_params=params(60),
        cost_estimate=cost(pairs * 2 * half * 2 * 2 * 256, seq * width * 8, pairs * 2 * half),
        name="attend_forward",
    )(length, qkv, qkv, qkv, *after)


def backward_body(length_ref, q_ref, k_ref, v_ref, do_ref, lse_ref, out_ref, kt_ref, ksum, vsum):
    seq = q_ref.shape[0]
    scale = HEAD_DIM**-0.5
    kt_ref[...] = k_ref[...].T
    lane = lax.broadcasted_iota(jnp.int32, (TILE, 2 * HEAD_DIM), 1)
    causal = lax.broadcasted_iota(jnp.int32, (TILE, TILE), 0) <= lax.broadcasted_iota(jnp.int32, (TILE, TILE), 1)

    def run(length, blocks):
        tasks = [(b, h) for b in reversed(range(blocks)) for h in range(2)]

        def scores(i):
            b, h = tasks[i]
            mine = (lane < HEAD_DIM) if h == 0 else (lane >= HEAD_DIM)
            q = q_ref[b * TILE : (b + 1) * TILE, :] * jnp.asarray(scale, low)
            up = do_ref[b * TILE : (b + 1) * TILE, :]
            qh = jnp.where(mine, q, jnp.zeros_like(q))
            uh = jnp.where(mine, up, jnp.zeros_like(up))
            stop = (b + 1) * TILE
            return qh, uh, mm_nt(k_ref[:stop, :], qh), mm_nt(v_ref[:stop, :], uh)

        now = scores(0)
        dqs, dss, pbs, qs, us = [], [], [], [], []
        for i, (b, h) in enumerate(tasks):
            start, stop = b * TILE, (b + 1) * TILE
            later = scores(i + 1) if i + 1 < len(tasks) else None
            qh, uh, s, dp = now
            lse = lse_ref[0, h : h + 1, start:stop]
            p = jnp.exp(jnp.where(causal, s[start:], excluded) - lse)
            inner = jnp.sum(p * dp[start:], axis=0, keepdims=True)
            if b:
                pf = jnp.exp(s[:start] - lse)
                inner = inner + jnp.sum(pf * dp[:start], axis=0, keepdims=True)
            ds = (p * (dp[start:] - inner)).astype(low)
            pb = p.astype(low)
            if b:
                ds = jnp.concatenate([(pf * (dp[:start] - inner)).astype(low), ds], axis=0)
                pb = jnp.concatenate([pf.astype(low), pb], axis=0)
            dqs.append(mm(kt_ref[h * HEAD_DIM : (h + 1) * HEAD_DIM, :stop], ds))
            dss.append(ds)
            pbs.append(pb)
            qs.append(qh)
            us.append(uh)
            if h:
                dk = mm(jnp.concatenate(dss, axis=1), jnp.concatenate(qs, axis=0))
                dv = mm(jnp.concatenate(pbs, axis=1), jnp.concatenate(us, axis=0))
                if b == blocks - 1:
                    ksum[:stop, :] = dk
                    vsum[:stop, :] = dv
                else:
                    ksum[:stop, :] += dk
                    vsum[:stop, :] += dv
                out_ref[1, start:stop, :] = ksum[start:stop, :].astype(low)
                out_ref[2, start:stop, :] = vsum[start:stop, :].astype(low)
                out_ref[0, start:stop, :] = (jnp.concatenate(dqs, axis=0).T * scale).astype(low)
                dqs, dss, pbs, qs, us = [], [], [], [], []
            now = later
        if blocks * TILE < seq:
            rest = jnp.zeros((seq - blocks * TILE, 2 * HEAD_DIM), low)
            for part in range(3):
                out_ref[part, blocks * TILE :, :] = rest

    live_blocks(length_ref, seq // TILE, run)


def attend_backward(length, qkv, upstream, lse, after):
    seq, width = upstream.shape
    pair = 2 * HEAD_DIM
    pairs = width // pair
    half = seq * seq * 5 // 8
    spec = lambda part: pl.BlockSpec((seq, pair), lambda i, s: (0, part * pairs + i))
    own = pl.BlockSpec((seq, pair), lambda i, s: (0, i))
    return pl.pallas_call(
        held_back(backward_body, 6, len(after)),
        grid_spec=pltpu.PrefetchScalarGridSpec(
            num_scalar_prefetch=1,
            grid=(pairs,),
            in_specs=[spec(0), spec(1), spec(2), own, pl.BlockSpec((1, 2, seq), lambda i, s: (i, 0, 0))]
            + [LATER] * len(after),
            out_specs=pl.BlockSpec((3, seq, pair), lambda i, s: (0, 0, i)),
            scratch_shapes=[
                pltpu.VMEM((pair, seq), low),
                pltpu.VMEM((seq, pair), f32),
                pltpu.VMEM((seq, pair), f32),
            ],
        ),
        out_shape=sds((3, seq, width), low),
        compiler_params=params(60),
        cost_estimate=cost(pairs * 2 * half * 5 * 2 * 256, seq * width * 14, pairs * 2 * half),
        name="attend_backward",
    )(length, qkv, qkv, qkv, upstream, lse, *after)


def normalize(values):
    average = jnp.mean(values, axis=-1, keepdims=True)
    centred = values - average
    inverse = lax.rsqrt(jnp.mean(centred * centred, axis=-1, keepdims=True) + eps_norm)
    return centred * inverse, inverse


def pull_norm(scaled, unit, inverse):
    first = jnp.mean(scaled, axis=-1, keepdims=True)
    second = jnp.mean(scaled * unit, axis=-1, keepdims=True)
    return inverse * (scaled - first - unit * second)


def columns_of(values):
    return jnp.sum(values, axis=0, keepdims=True)


def prepare_body(x_ref, up_ref, vec_ref, expand_ref, shrink_ref, h_ref, ht_ref, upt_ref, shard_ref):
    part = expand_ref.shape[1] // 3
    for index in range(3):
        at = slice(index * part, (index + 1) * part)
        shard_ref[:, 2 * index * part : (2 * index + 1) * part] = expand_ref[:, at].astype(low)
        shard_ref[:, (2 * index + 1) * part : (2 * index + 2) * part] = shrink_ref[:, at].astype(low)
    unit, _ = normalize(x_ref[...].astype(f32))
    h = (unit * vec_ref[0:1, :] + vec_ref[1:2, :]).astype(low)
    h_ref[...] = h
    ht_ref[...] = h.T
    upt_ref[...] = up_ref[...].T


def prepare(x, up, vectors, expand, shrink_t, after):
    seq, depth = x.shape
    shard = (expand.shape[0], 2 * expand.shape[1])
    rows = pl.BlockSpec((TILE, depth), lambda i: (i, 0))
    turned = pl.BlockSpec((depth, TILE), lambda i: (0, i))
    return pl.pallas_call(
        held_back(prepare_body, 5, len(after)),
        grid=(seq // TILE,),
        in_specs=[rows, rows, whole(vectors.shape), whole(expand.shape), whole(expand.shape)]
        + [LATER] * len(after),
        out_specs=[rows, turned, turned, whole(shard)],
        out_shape=[
            sds((seq, depth), low),
            sds((depth, seq), low),
            sds((depth, seq), low),
            sds(shard, low),
        ],
        compiler_params=params(60),
        cost_estimate=cost(seq * depth * 10, seq * depth * 10),
        name="prepare",
    )(x, up, vectors, expand, shrink_t, *after)


def project_body(core_ref, spots_ref, h_ref, mine_ref, twin_ref, bias_ref, qkv_ref, wide_ref):
    part = pl.program_id(0)
    rows = mine_ref.shape[1]
    width = mine_ref.shape[2] // 4
    groups = wide_ref.shape[1] // rows

    def collect(sources, index):
        at = slice(index * width, (index + 1) * width)
        for group in range(groups):
            pieces = [sources[model % 2][spots_ref[model, group], :, at] for model in range(4)]
            wide_ref[0, group * rows : (group + 1) * rows, :] = jnp.concatenate(pieces, axis=1)

    for index in range(4):
        for core in range(2):

            @pl.when((part == index) & (core_ref[0] == core))
            def _(index=index, core=core):
                collect((mine_ref, twin_ref) if core == 0 else (twin_ref, mine_ref), index)

    @pl.when(part < 3)
    def _():
        qkv_ref[...] = (mm(h_ref[...], wide_ref[0]) + bias_ref[0]).astype(low)


def project(core, spots, h, mine, twin, bias, after):
    seq, depth = h.shape
    return pl.pallas_call(
        held_back(project_body, 6, len(after)),
        grid_spec=pltpu.PrefetchScalarGridSpec(
            num_scalar_prefetch=2,
            grid=(4,),
            in_specs=[
                whole((seq, depth)),
                whole(mine.shape),
                whole(twin.shape),
                pl.BlockSpec((1, 1, depth), lambda i, *_: (jnp.minimum(i, 2), 0, 0)),
            ]
            + [LATER] * len(after),
            out_specs=[
                pl.BlockSpec((seq, depth), lambda i, *_: (0, jnp.minimum(i, 2))),
                pl.BlockSpec((1, depth, depth), lambda i, *_: (i, 0, 0)),
            ],
        ),
        out_shape=[sds((seq, 3 * depth), low), sds((4, depth, depth), low)],
        compiler_params=params(60),
        cost_estimate=cost(2 * seq * depth * depth * 3, seq * depth * 16),
        name="project",
    )(core, spots, h, mine, twin, bias, *after)


def attend_out_body(o_ref, w_ref, x_ref, vec_ref, middle_ref, h_ref, ht_ref):
    middle = x_ref[...].astype(f32) + mm_nt(o_ref[...], w_ref[0]) + vec_ref[4:5, :]
    middle_ref[...] = middle
    unit, _ = normalize(middle)
    h = (unit * vec_ref[2:3, :] + vec_ref[3:4, :]).astype(low)
    h_ref[...] = h
    ht_ref[...] = h.T


def attend_out(o, wide, x, vectors):
    seq, depth = x.shape
    rows = pl.BlockSpec((TILE, depth), lambda i: (i, 0))
    turned = pl.BlockSpec((depth, TILE), lambda i: (0, i))
    return pl.pallas_call(
        attend_out_body,
        grid=(seq // TILE,),
        in_specs=[
            rows,
            pl.BlockSpec((1, depth, depth), lambda i: (3, 0, 0)),
            rows,
            whole(vectors.shape),
        ],
        out_specs=[rows, rows, turned],
        out_shape=[sds((seq, depth), f32), sds((seq, depth), low), sds((depth, seq), low)],
        compiler_params=params(60),
        cost_estimate=cost(2 * seq * depth * depth, seq * depth * 14),
        name="attend_out",
    )(o, wide, x, vectors)


def feed_body(
    spots_ref,
    h2_ref,
    h2t_ref,
    up_ref,
    upt_ref,
    mine_ref,
    twin_ref,
    bias_ref,
    middle_ref,
    vec_ref,
    block_ref,
    back_ref,
    keep_ref,
    send_ref,
    bias_grad_ref,
    out_ref,
    wide_ref,
    act_ref,
    pre_ref,
):
    step = pl.program_id(0)
    side = lax.rem(step, 2)
    rows = mine_ref.shape[1]
    part = mine_ref.shape[2] // 2
    groups = wide_ref.shape[0] // rows

    @pl.when(step == 0)
    def _():
        out_ref[...] = middle_ref[...] + vec_ref[5:6, :]
        back_ref[...] = jnp.zeros_like(back_ref)

    for group in range(groups):
        at = slice(group * rows, (group + 1) * rows)
        own = mine_ref[spots_ref[0, side, group]]
        other = twin_ref[spots_ref[1, side, group]]
        wide_ref[at, :part] = own[:, :part]
        wide_ref[at, part : 2 * part] = other[:, :part]
        wide_ref[at, 2 * part : 3 * part] = own[:, part:]
        wide_ref[at, 3 * part :] = other[:, part:]

    expand = wide_ref[:, : 2 * part]
    shrink = wide_ref[:, 2 * part :]
    bias = bias_ref[0]
    sums = jnp.zeros((1, 2 * part), f32)
    for tile in range(h2_ref.shape[0] // TILE):
        at = slice(tile * TILE, (tile + 1) * TILE)
        u = mm(h2_ref[at, :], expand) + bias
        square = u * u
        th = jnp.tanh(u * (GELU_A + GELU_B * square))
        gate = 0.5 * th + 0.5
        slope = gate + (gate * (1.0 - gate)) * (u * (2.0 * GELU_A + (6.0 * GELU_B) * square))
        pre = (mm(up_ref[at, :], shrink) * slope).astype(low)
        act_ref[at, :] = (u * gate).astype(low)
        pre_ref[at, :] = pre
        sums = sums + columns_of(pre.astype(f32))
    bias_grad_ref[0] = sums
    out_ref[...] += mm_nt(act_ref[...], shrink)
    back_ref[...] += mm_nt(pre_ref[...], expand)
    grad_expand = mm(h2t_ref[...], pre_ref[...]).astype(low)
    grad_shrink = mm(upt_ref[...], act_ref[...]).astype(low)
    for group in range(groups):
        at = slice(group * rows, (group + 1) * rows)
        own, other = spots_ref[0, side, group], spots_ref[1, side, group]
        keep_ref[own, :, :part] = grad_expand[at, :part]
        keep_ref[own, :, part:] = grad_shrink[at, :part]
        send_ref[other, :, :part] = grad_expand[at, part:]
        send_ref[other, :, part:] = grad_shrink[at, part:]

    @pl.when(step == pl.num_programs(0) - 1)
    def _():
        block_ref[...] = out_ref[...].astype(low)


def feed(spots, h2, h2t, up, upt, mine, twin, bias, middle, vectors):
    seq, depth = h2.shape
    slots, rows, columns = mine.shape
    steps = bias.shape[0]
    part = bias.shape[2] // 2
    piece = pl.BlockSpec((slots, rows, 2 * part), lambda i, s: (0, 0, i // 2))
    bias_spec = pl.BlockSpec((1, 1, 2 * part), lambda i, s: (i, 0, 0))
    return pl.pallas_call(
        feed_body,
        grid_spec=pltpu.PrefetchScalarGridSpec(
            num_scalar_prefetch=1,
            grid=(steps,),
            in_specs=[
                whole((seq, depth)),
                whole((depth, seq)),
                whole((seq, depth)),
                whole((depth, seq)),
                piece,
                piece,
                bias_spec,
                whole((seq, depth)),
                whole(vectors.shape),
            ],
            out_specs=[whole((seq, depth)), whole((seq, depth)), piece, piece, bias_spec],
            scratch_shapes=[
                pltpu.VMEM((seq, depth), f32),
                pltpu.VMEM((depth, 4 * part), low),
                pltpu.VMEM((seq, 2 * part), low),
                pltpu.VMEM((seq, 2 * part), low),
            ],
        ),
        out_shape=[sds((seq, depth), low), sds((seq, depth), f32)]
        + [sds(mine.shape, low)] * 2
        + [sds(bias.shape, f32)],
        compiler_params=params(60),
        cost_estimate=cost(12 * seq * depth * steps * 2 * part, seq * depth * 40, seq * steps * part),
        name="feed",
    )(spots, h2, h2t, up, upt, mine, twin, bias, middle, vectors)


def middle_back_body(
    length_ref,
    back_ref,
    middle_ref,
    up_ref,
    o_ref,
    w_ref,
    vec_ref,
    grad_ref,
    mixture_ref,
    weight_ref,
    sums_ref,
):
    step = pl.program_id(0)
    middle = middle_ref[...]
    unit, inverse = normalize(middle)
    back = back_ref[...]
    up = up_ref[...].astype(f32)
    grad = up + pull_norm(back * vec_ref[2:3, :], unit, inverse)
    grad_ref[...] = grad
    rounded = grad.astype(low)
    first = step * TILE
    row = first + lax.broadcasted_iota(jnp.int32, (TILE, grad.shape[1]), 0)
    mixture_ref[...] = jnp.where(row < length_ref[0], mm(rounded, w_ref[0]), 0.0).astype(low)
    share = mm(rounded.T, o_ref[...])
    sums = jnp.concatenate(
        [columns_of(back * unit), columns_of(back), columns_of(grad), columns_of(up)], axis=0
    )

    @pl.when(step == 0)
    def _():
        weight_ref[...] = share
        sums_ref[...] = sums

    @pl.when(step > 0)
    def _():
        weight_ref[...] += share
        sums_ref[...] += sums


def middle_back(length, back, middle, up, o, wide, vectors):
    seq, depth = middle.shape
    rows = pl.BlockSpec((TILE, depth), lambda i, s: (i, 0))
    return pl.pallas_call(
        middle_back_body,
        grid_spec=pltpu.PrefetchScalarGridSpec(
            num_scalar_prefetch=1,
            grid=(seq // TILE,),
            in_specs=[
                rows,
                rows,
                rows,
                rows,
                pl.BlockSpec((1, depth, depth), lambda i, s: (3, 0, 0)),
                whole(vectors.shape),
            ],
            out_specs=[rows, rows, whole((depth, depth)), whole((4, depth))],
        ),
        out_shape=[
            sds((seq, depth), f32),
            sds((seq, depth), low),
            sds((depth, depth), f32),
            sds((4, depth), f32),
        ],
        compiler_params=params(60),
        cost_estimate=cost(4 * seq * depth * depth, seq * depth * 28),
        name="middle_back",
    )(length, back, middle, up, o, wide, vectors)


def input_grad_body(core_ref, spots_ref, ht_ref, back_ref, out_grad_ref, keep_ref, send_ref, sums_ref):
    part = pl.program_id(0)
    rows = keep_ref.shape[1]
    width = keep_ref.shape[2] // 4
    groups = ht_ref.shape[0] // rows

    def spread(targets, index, grad):
        at = slice(index * width, (index + 1) * width)
        for group in range(groups):
            for model in range(4):
                targets[model % 2][spots_ref[model, group], :, at] = grad[
                    group * rows : (group + 1) * rows, model * width : (model + 1) * width
                ]

    for index in range(4):

        @pl.when(part == index)
        def _(index=index):
            if index < 3:
                sums_ref[0] = columns_of(back_ref[0].astype(f32))
                grad = mm(ht_ref[...], back_ref[0]).astype(low)
            else:
                grad = out_grad_ref[...].astype(low)
            for core in range(2):

                @pl.when(core_ref[0] == core)
                def _(core=core):
                    spread((keep_ref, send_ref) if core == 0 else (send_ref, keep_ref), index, grad)


def input_grad(core, spots, ht, back, out_grad, slots, rows, after):
    depth, seq = ht.shape
    shape = (slots, rows, 4 * (depth // 4))
    return pl.pallas_call(
        held_back(input_grad_body, 5, len(after)),
        grid_spec=pltpu.PrefetchScalarGridSpec(
            num_scalar_prefetch=2,
            grid=(4,),
            in_specs=[
                whole((depth, seq)),
                pl.BlockSpec((1, seq, depth), lambda i, *_: (jnp.minimum(i, 2), 0, 0)),
                whole((depth, depth)),
            ]
            + [LATER] * len(after),
            out_specs=[
                whole(shape),
                whole(shape),
                pl.BlockSpec((1, 1, depth), lambda i, *_: (jnp.minimum(i, 2), 0, 0)),
            ],
        ),
        out_shape=[sds(shape, low), sds(shape, low), sds((3, 1, depth), f32)],
        compiler_params=params(60),
        cost_estimate=cost(6 * seq * depth * depth, seq * depth * 14),
        name="input_grad",
    )(core, spots, ht, back, out_grad, *after)


def token_back_body(back_ref, w_ref, x_ref, grad_ref, vec_ref, token_ref, sums_ref):
    step = pl.program_id(0)
    back = mm_nt(back_ref[0], w_ref[0]) + mm_nt(back_ref[1], w_ref[1]) + mm_nt(back_ref[2], w_ref[2])
    unit, inverse = normalize(x_ref[...].astype(f32))
    token_ref[...] = (grad_ref[...] + pull_norm(back * vec_ref[0:1, :], unit, inverse)).astype(low)
    sums = jnp.concatenate([columns_of(back * unit), columns_of(back)], axis=0)

    @pl.when(step == 0)
    def _():
        sums_ref[...] = sums

    @pl.when(step > 0)
    def _():
        sums_ref[...] += sums


def token_back(back, wide, x, grad, vectors):
    seq, depth = x.shape
    rows = pl.BlockSpec((TILE, depth), lambda i: (i, 0))
    return pl.pallas_call(
        token_back_body,
        grid=(seq // TILE,),
        in_specs=[
            pl.BlockSpec((3, TILE, depth), lambda i: (0, i, 0)),
            pl.BlockSpec((3, depth, depth), lambda i: (0, 0, 0)),
            rows,
            rows,
            whole(vectors.shape),
        ],
        out_specs=[rows, whole((2, depth))],
        out_shape=[sds((seq, depth), low), sds((2, depth), f32)],
        compiler_params=params(60),
        cost_estimate=cost(6 * seq * depth * depth, seq * depth * 16),
        name="token_back",
    )(back, wide, x, grad, vectors)


CORE_ORDERS = ((4, 3, 2, 1), (3, 4, 1, 2))
STAGES = 4


def cube_permute(values, stage):
    pairs = [(device, device ^ (1 << CORE_ORDERS[device & 1][stage])) for device in range(32)]
    return lax.ppermute(values, ("dp", "mp"), pairs)


def bit_permute(values, bit):
    return lax.ppermute(values, ("dp", "mp"), [(device, device ^ (1 << bit)) for device in range(32)])


def place(distance, core):
    spots = [
        sum(((distance >> bit) & 1) << step for step, bit in enumerate(order)) for order in CORE_ORDERS
    ]
    return jnp.where(core == 0, spots[0], spots[1])


def gather_stage(held, stage):
    return jnp.concatenate([held, cube_permute(held, stage)], axis=0)


def scatter_stage(keep, other, stage):
    half = 1 << stage
    away = keep[half:] + other[half:]
    return away, keep[:half] + other[:half]


def cube_sum(values):
    for bit in range(5):
        values = values + bit_permute(values, bit)
    return values


def adam_step(weight, gradient, first_old, second_old, factor, step_rate):
    scaled = gradient * factor
    moment = beta_one * first_old + (1.0 - beta_one) * scaled
    square = beta_two * second_old + (1.0 - beta_two) * scaled * scaled
    corrected = moment / (1.0 - beta_one**STEP)
    spread = jnp.sqrt(square / (1.0 - beta_two**STEP))
    updated = weight - step_rate * (corrected / (spread + adam_eps) + decay * weight)
    return (moment, square, updated)


def squares(values):
    return jnp.sum(values * values)


def shards(
    tokens,
    cotangent,
    lengths,
    input_weight,
    output_weight,
    expand_weight,
    shrink_weight,
    layer_vectors,
    head_bias,
    expand_bias,
    first_input,
    first_output,
    first_expand,
    first_shrink,
    first_vectors,
    first_head,
    first_bias,
    second_input,
    second_output,
    second_expand,
    second_shrink,
    second_vectors,
    second_head,
    second_bias,
):
    dp_count = lax.axis_size("dp")
    mp_count = lax.axis_size("mp")
    cube = dp_count == 8 and mp_count == 4
    rows = input_weight.shape[0]
    width = input_weight.shape[2]
    hidden = expand_weight.shape[1]
    seq, depth = tokens.shape
    part = hidden // 3
    model_index = lax.axis_index("mp")
    me = lax.axis_index("dp") * mp_count + model_index

    attend_shard = jnp.concatenate(
        [input_weight.astype(low).reshape(rows, 3 * width), output_weight.astype(low).T], axis=1
    )
    bias_shard = jnp.concatenate([head_bias.reshape(1, 2 * width), expand_bias[None]], axis=1)

    bias_full = jnp.where(jnp.arange(4)[:, None] == model_index, bias_shard, 0.0)
    if cube:
        core = me & 1
        bias_full = bias_full + bit_permute(bias_full, 0)
        bias_full = bias_full + bit_permute(bias_full, 1)
        devices = jnp.arange(32).reshape(8, 4).T
        spots = place(devices ^ me, devices & 1).astype(jnp.int32)
        near = model_index
    else:
        core = jnp.zeros((), jnp.int32)
        bias_full = lax.psum(bias_full, "mp")
        spots = (jnp.arange(4)[:, None] // 2 * 8 + jnp.arange(8)[None]).astype(jnp.int32)
        near = jnp.zeros((), jnp.int32)
    near_models = near ^ jnp.arange(4)
    near_spots = jnp.take(spots, near_models, axis=0).reshape(2, 2, 8).transpose(1, 0, 2)
    core = core.astype(jnp.int32).reshape(1)

    length = lax.dynamic_slice_in_dim(lengths, model_index, 1, 0)
    head_full = bias_full[:, : 2 * width].reshape(4, 2, width).transpose(1, 0, 2).reshape(2, depth)
    qkv_bias = jnp.stack([head_full[0], jnp.zeros_like(head_full[0]), head_full[1]])[:, None]
    feed_bias = (
        jnp.take(bias_full[:, 2 * width :], near_models, axis=0)
        .reshape(2, 2, 3, part)
        .transpose(2, 0, 1, 3)
        .reshape(6, 1, 2 * part)
    )

    def prepared(after):
        return prepare(tokens, cotangent, layer_vectors, expand_weight, shrink_weight.T, after)

    if cube:
        held = gather_stage(gather_stage(attend_shard[None], 0), 1)
        normed, normed_t, upstream_t, feed_shard = prepared((held,))
        held = gather_stage(held, 2)
        feed_held = gather_stage(feed_shard[None], 0)
        held, feed_held = lax.optimization_barrier((held, feed_held))
        mine_attend = gather_stage(held, 3)
        feed_held = gather_stage(feed_held, 1)
        twin_attend = bit_permute(mine_attend, 0)
        twin_attend, feed_held = lax.optimization_barrier((twin_attend, feed_held))
        qkv, wide = project(core, spots, normed, mine_attend, twin_attend, qkv_bias, ())
        feed_held = gather_stage(feed_held, 2)
        mixture, log_totals = attend_forward(length, qkv, (feed_held,))
        middle, hidden_in, hidden_t = attend_out(mixture, wide, tokens, layer_vectors)
        arrived = cube_permute(feed_held, 3)
        feed_held, hidden_in = lax.optimization_barrier((feed_held, hidden_in))
        mine_feed = jnp.concatenate([feed_held, arrived], axis=0)
        twin_feed = bit_permute(mine_feed, 0)
    else:

        def planes(shard):
            full = lax.all_gather(lax.all_gather(shard, "dp", axis=0, tiled=True), "mp", axis=0)
            full = full.reshape(2, 2, 8, depth // 8, shard.shape[1]).transpose(1, 0, 2, 3, 4)
            return full.reshape(2, 16, depth // 8, shard.shape[1])

        normed, normed_t, upstream_t, feed_shard = prepared(())
        mine_attend, twin_attend = planes(attend_shard)
        mine_feed, twin_feed = planes(feed_shard)
        qkv, wide = project(core, spots, normed, mine_attend, twin_attend, qkv_bias, ())
        mixture, log_totals = attend_forward(length, qkv, ())
        middle, hidden_in, hidden_t = attend_out(mixture, wide, tokens, layer_vectors)
    block_out, back, keep_feed, send_feed, feed_bias_grad = feed(
        near_spots,
        hidden_in,
        hidden_t,
        cotangent,
        upstream_t,
        mine_feed,
        twin_feed,
        feed_bias,
        middle,
        layer_vectors,
    )
    middle_grad, mixture_grad, output_grad, middle_sums = middle_back(
        length, back, middle, cotangent, mixture, wide, layer_vectors
    )
    if cube:
        other = bit_permute(send_feed, 0)
        keep_feed, mixture_grad = lax.optimization_barrier((keep_feed, mixture_grad))
        away, keep_feed = scatter_stage(keep_feed, other, 3)
        packed_grad = attend_backward(length, qkv, mixture_grad, log_totals, (away,))
        away, keep_feed = scatter_stage(keep_feed, cube_permute(away, 3), 2)
        keep_attend, send_attend, head_sums = input_grad(
            core, spots, normed_t, packed_grad, output_grad, 16, depth // 8, (away,)
        )
        other = bit_permute(send_attend, 0)
    else:
        packed_grad = attend_backward(length, qkv, mixture_grad, log_totals, ())
        keep_attend, send_attend, head_sums = input_grad(
            core, spots, normed_t, packed_grad, output_grad, 16, depth // 8, ()
        )
    token_grad, token_sums = token_back(packed_grad, wide, tokens, middle_grad, layer_vectors)

    bias_near = feed_bias_grad.reshape(3, 2, 2, part).transpose(1, 2, 0, 3).reshape(4, hidden)
    bias_grad = jnp.take(bias_near, near_models, axis=0)
    vector_local = jnp.concatenate(
        [token_sums, middle_sums, head_sums[0], head_sums[2], bias_grad.reshape(4, depth)], axis=0
    )
    if cube:
        feed_other = cube_permute(away, 2)
        for stage in (3, 2, 1, 0):
            away, keep_attend = scatter_stage(keep_attend, other, stage)
            other = cube_permute(away, stage)
            if stage == 3:
                keep_attend, vector_local = lax.optimization_barrier((keep_attend, vector_local))
            if stage >= 2:
                away, keep_feed = scatter_stage(keep_feed, feed_other, stage - 2)
                feed_other = cube_permute(away, stage - 2)
        feed_total = keep_feed[0].astype(f32) + feed_other[0].astype(f32)
        attend_total = keep_attend[0].astype(f32) + other[0].astype(f32)
        vector_total = cube_sum(vector_local)
    else:

        def own_block(keep, send):
            full = jnp.stack([keep, send]).reshape(2, 2, 8, depth // 8, keep.shape[2])
            full = full.transpose(1, 0, 2, 3, 4).reshape(4, depth, keep.shape[2])
            full = lax.psum_scatter(full, "mp", scatter_dimension=0, tiled=False)
            return lax.psum_scatter(full, "dp", scatter_dimension=0, tiled=True).astype(f32)

        attend_total = own_block(keep_attend, send_attend)
        feed_total = own_block(keep_feed, send_feed)
        vector_total = lax.psum(vector_local, ("dp", "mp"))
    input_total = attend_total[:, : 3 * width].reshape(rows, 3, width)
    output_total = attend_total[:, 3 * width :].T
    pieces = feed_total.reshape(rows, 3, 2, part)
    expand_total = pieces[:, :, 0].reshape(rows, hidden)
    shrink_total = pieces[:, :, 1].reshape(rows, hidden).T
    vector_grad = vector_total[:6]
    head_total = lax.dynamic_slice_in_dim(vector_total[6:8], model_index * width, width, 1)
    bias_total = lax.dynamic_slice_in_dim(vector_total[8:].reshape(-1), model_index * hidden, hidden, 0)
    owned = jnp.sum(attend_total * attend_total) + jnp.sum(feed_total * feed_total)
    if cube:
        owned = cube_sum(jnp.full((8, 128), owned, f32))[0, 0]
    else:
        owned = lax.psum(owned, ("dp", "mp"))
    grad_norm = jnp.sqrt(owned + jnp.sum(vector_total * vector_total))
    factor = clip_norm / jnp.maximum(grad_norm, clip_norm)
    moment_input, square_input, updated_input = adam_step(
        input_weight, input_total, first_input, second_input, factor, rate
    )
    moment_output, square_output, updated_output = adam_step(
        output_weight, output_total, first_output, second_output, factor, rate
    )
    moment_expand, square_expand, updated_expand = adam_step(
        expand_weight, expand_total, first_expand, second_expand, factor, rate
    )
    moment_shrink, square_shrink, updated_shrink = adam_step(
        shrink_weight, shrink_total, first_shrink, second_shrink, factor, rate
    )
    moment_vectors, square_vectors, updated_vectors = adam_step(
        layer_vectors, vector_grad, first_vectors, second_vectors, factor, vector_rate
    )
    moment_head, square_head, updated_head = adam_step(
        head_bias, head_total, first_head, second_head, factor, vector_rate
    )
    moment_bias, square_bias, updated_bias = adam_step(
        expand_bias, bias_total, first_bias, second_bias, factor, vector_rate
    )
    return (
        block_out,
        token_grad,
        grad_norm,
        moment_input,
        square_input,
        updated_input,
        moment_output,
        square_output,
        updated_output,
        moment_expand,
        square_expand,
        updated_expand,
        moment_shrink,
        square_shrink,
        updated_shrink,
        moment_vectors,
        square_vectors,
        updated_vectors,
        moment_head,
        square_head,
        updated_head,
        moment_bias,
        square_bias,
        updated_bias,
    )


def solution(mesh):
    in_specs = (
        P(("dp", "mp"), None),
        P(("dp", "mp"), None),
        P("dp"),
        P("dp", None, "mp"),
        P("mp", "dp"),
        P("dp", "mp"),
        P("mp", "dp"),
        P(),
        P(None, "mp"),
        P("mp"),
        P("dp", None, "mp"),
        P("mp", "dp"),
        P("dp", "mp"),
        P("mp", "dp"),
        P(),
        P(None, "mp"),
        P("mp"),
        P("dp", None, "mp"),
        P("mp", "dp"),
        P("dp", "mp"),
        P("mp", "dp"),
        P(),
        P(None, "mp"),
        P("mp"),
    )
    out_specs = (
        P(("dp", "mp"), None),
        P(("dp", "mp"), None),
        P(),
        P("dp", None, "mp"),
        P("dp", None, "mp"),
        P("dp", None, "mp"),
        P("mp", "dp"),
        P("mp", "dp"),
        P("mp", "dp"),
        P("dp", "mp"),
        P("dp", "mp"),
        P("dp", "mp"),
        P("mp", "dp"),
        P("mp", "dp"),
        P("mp", "dp"),
        P(),
        P(),
        P(),
        P(None, "mp"),
        P(None, "mp"),
        P(None, "mp"),
        P("mp"),
        P("mp"),
        P("mp"),
    )
    return jax.shard_map(shards, mesh=mesh, in_specs=in_specs, out_specs=out_specs, check_vma=False)
```

```python
import functools
import jax
import jax.numpy as jnp
from jax import lax
from jax.experimental import pallas as pl
from jax.experimental.pallas import tpu as pltpu
from jax.sharding import PartitionSpec as P

HEAD_DIM = 64
TILE = 256
STEP = 10

eps_norm = 1e-05
clip_norm = 1.0
beta_one = 0.9
beta_two = 0.999
adam_eps = 1e-08
rate = 0.05
vector_rate = 0.5
decay = 0.01
excluded = -1e30
low = jnp.bfloat16
f32 = jnp.float32
GELU_A = 0.7978845608028654
GELU_B = GELU_A * 0.044715


def params(limit_mib, **kw):
    return pltpu.CompilerParams(vmem_limit_bytes=limit_mib * 1024 * 1024, **kw)


def cost(flops, moved, special=0):
    return pl.CostEstimate(flops=int(flops), bytes_accessed=int(moved), transcendentals=int(special))


def mm(a, b):
    return jnp.dot(a, b, preferred_element_type=f32)


def mm_nt(a, b):
    return lax.dot_general(a, b, (((1,), (1,)), ((), ())), preferred_element_type=f32)


def whole(shape):
    zeros = (0,) * len(shape)
    return pl.BlockSpec(shape, lambda *_: zeros)


def held_back(body, first, count):
    def run(*refs):
        return body(*refs[:first], *refs[first + count :])

    return run


LATER = pl.BlockSpec(memory_space=pl.ANY)


def sds(shape, dtype):
    return jax.ShapeDtypeStruct(shape, dtype)


def live_blocks(length_ref, count, body):
    length = length_ref[0]
    for blocks in range(1, count + 1):
        low_end = (blocks - 1) * TILE
        high_end = blocks * TILE
        @pl.when((length > low_end) & (length <= high_end))
        def _(blocks=blocks):
            body(length, blocks)


def forward_body(length_ref, q_ref, k_ref, v_ref, o_ref, lse_ref, vt_ref):
    seq = q_ref.shape[0]
    vt_ref[...] = v_ref[...].T
    lane = lax.broadcasted_iota(jnp.int32, (TILE, 2 * HEAD_DIM), 1)
    causal = lax.broadcasted_iota(jnp.int32, (TILE, TILE), 0) <= lax.broadcasted_iota(jnp.int32, (TILE, TILE), 1)

    def run(length, blocks):
        tasks = [(b, h) for b in range(blocks) for h in range(2)]

        def scores(i):
            b, h = tasks[i]
            q = q_ref[b * TILE : (b + 1) * TILE, :] * jnp.asarray(HEAD_DIM**-0.5, low)
            qh = jnp.where((lane < HEAD_DIM) if h == 0 else (lane >= HEAD_DIM), q, jnp.zeros_like(q))
            return mm_nt(k_ref[: (b + 1) * TILE, :], qh)

        now = scores(0)
        outs = []
        for i, (b, h) in enumerate(tasks):
            start, stop = b * TILE, (b + 1) * TILE
            later = scores(i + 1) if i + 1 < len(tasks) else None
            last = jnp.where(causal, now[start:, :], excluded)
            top = jnp.max(last, axis=0, keepdims=True)
            if b:
                top = jnp.maximum(top, jnp.max(now[:start], axis=0, keepdims=True))
            p = jnp.exp(last - top)
            total = jnp.sum(p, axis=0, keepdims=True)
            pb = p.astype(low)
            if b:
                pf = jnp.exp(now[:start] - top)
                total = total + jnp.sum(pf, axis=0, keepdims=True)
                pb = jnp.concatenate([pf.astype(low), pb], axis=0)
            out = mm(vt_ref[h * HEAD_DIM : (h + 1) * HEAD_DIM, :stop], pb)
            outs.append(out / total)
            lse_ref[0, h : h + 1, start:stop] = top + jnp.log(total)
            if h:
                both = jnp.concatenate(outs, axis=0).T
                outs = []
                row = start + lax.broadcasted_iota(jnp.int32, both.shape, 0)
                o_ref[start:stop, :] = jnp.where(row < length, both, 0.0).astype(low)
            now = later
        if blocks * TILE < seq:
            o_ref[blocks * TILE :, :] = jnp.zeros((seq - blocks * TILE, 2 * HEAD_DIM), low)
            lse_ref[0, :, blocks * TILE :] = jnp.zeros((2, seq - blocks * TILE), f32)

    live_blocks(length_ref, seq // TILE, run)


def attend_forward(length, qkv, after):
    seq, width = qkv.shape[0], qkv.shape[1] // 3
    pair = 2 * HEAD_DIM
    pairs = width // pair
    half = seq * seq * 5 // 8
    spec = lambda part: pl.BlockSpec((seq, pair), lambda i, s: (0, part * pairs + i))
    return pl.pallas_call(
        held_back(forward_body, 4, len(after)),
        grid_spec=pltpu.PrefetchScalarGridSpec(
            num_scalar_prefetch=1,
            grid=(pairs,),
            in_specs=[spec(0), spec(1), spec(2)] + [LATER] * len(after),
            out_specs=[
                pl.BlockSpec((seq, pair), lambda i, s: (0, i)),
                pl.BlockSpec((1, 2, seq), lambda i, s: (i, 0, 0)),
            ],
            scratch_shapes=[pltpu.VMEM((pair, seq), low)],
        ),
        out_shape=[sds((seq, width), low), sds((pairs, 2, seq), f32)],
        compiler_params=params(60),
        cost_estimate=cost(pairs * 2 * half * 2 * 2 * 256, seq * width * 8, pairs * 2 * half),
        name="attend_forward",
    )(length, qkv, qkv, qkv, *after)


def backward_body(length_ref, q_ref, k_ref, v_ref, do_ref, lse_ref, out_ref, kt_ref, ksum, vsum):
    seq = q_ref.shape[0]
    scale = HEAD_DIM**-0.5
    kt_ref[...] = k_ref[...].T
    lane = lax.broadcasted_iota(jnp.int32, (TILE, 2 * HEAD_DIM), 1)
    causal = lax.broadcasted_iota(jnp.int32, (TILE, TILE), 0) <= lax.broadcasted_iota(jnp.int32, (TILE, TILE), 1)

    def run(length, blocks):
        tasks = [(b, h) for b in reversed(range(blocks)) for h in range(2)]

        def scores(i):
            b, h = tasks[i]
            mine = (lane < HEAD_DIM) if h == 0 else (lane >= HEAD_DIM)
            q = q_ref[b * TILE : (b + 1) * TILE, :] * jnp.asarray(scale, low)
            up = do_ref[b * TILE : (b + 1) * TILE, :]
            qh = jnp.where(mine, q, jnp.zeros_like(q))
            uh = jnp.where(mine, up, jnp.zeros_like(up))
            stop = (b + 1) * TILE
            return qh, uh, mm_nt(k_ref[:stop, :], qh), mm_nt(v_ref[:stop, :], uh)

        now = scores(0)
        dqs, dss, pbs, qs, us = [], [], [], [], []
        for i, (b, h) in enumerate(tasks):
            start, stop = b * TILE, (b + 1) * TILE
            later = scores(i + 1) if i + 1 < len(tasks) else None
            qh, uh, s, dp = now
            lse = lse_ref[0, h : h + 1, start:stop]
            p = jnp.exp(jnp.where(causal, s[start:], excluded) - lse)
            inner = jnp.sum(p * dp[start:], axis=0, keepdims=True)
            if b:
                pf = jnp.exp(s[:start] - lse)
                inner = inner + jnp.sum(pf * dp[:start], axis=0, keepdims=True)
            ds = (p * (dp[start:] - inner)).astype(low)
            pb = p.astype(low)
            if b:
                ds = jnp.concatenate([(pf * (dp[:start] - inner)).astype(low), ds], axis=0)
                pb = jnp.concatenate([pf.astype(low), pb], axis=0)
            dqs.append(mm(kt_ref[h * HEAD_DIM : (h + 1) * HEAD_DIM, :stop], ds))
            dss.append(ds)
            pbs.append(pb)
            qs.append(qh)
            us.append(uh)
            if h:
                dk = mm(jnp.concatenate(dss, axis=1), jnp.concatenate(qs, axis=0))
                dv = mm(jnp.concatenate(pbs, axis=1), jnp.concatenate(us, axis=0))
                if b == blocks - 1:
                    ksum[:stop, :] = dk
                    vsum[:stop, :] = dv
                else:
                    ksum[:stop, :] += dk
                    vsum[:stop, :] += dv
                out_ref[1, start:stop, :] = ksum[start:stop, :].astype(low)
                out_ref[2, start:stop, :] = vsum[start:stop, :].astype(low)
                out_ref[0, start:stop, :] = (jnp.concatenate(dqs, axis=0).T * scale).astype(low)
                dqs, dss, pbs, qs, us = [], [], [], [], []
            now = later
        if blocks * TILE < seq:
            rest = jnp.zeros((seq - blocks * TILE, 2 * HEAD_DIM), low)
            for part in range(3):
                out_ref[part, blocks * TILE :, :] = rest

    live_blocks(length_ref, seq // TILE, run)


def attend_backward(length, qkv, upstream, lse, after):
    seq, width = upstream.shape
    pair = 2 * HEAD_DIM
    pairs = width // pair
    half = seq * seq * 5 // 8
    spec = lambda part: pl.BlockSpec((seq, pair), lambda i, s: (0, part * pairs + i))
    own = pl.BlockSpec((seq, pair), lambda i, s: (0, i))
    return pl.pallas_call(
        held_back(backward_body, 6, len(after)),
        grid_spec=pltpu.PrefetchScalarGridSpec(
            num_scalar_prefetch=1,
            grid=(pairs,),
            in_specs=[spec(0), spec(1), spec(2), own, pl.BlockSpec((1, 2, seq), lambda i, s: (i, 0, 0))]
            + [LATER] * len(after),
            out_specs=pl.BlockSpec((3, seq, pair), lambda i, s: (0, 0, i)),
            scratch_shapes=[
                pltpu.VMEM((pair, seq), low),
                pltpu.VMEM((seq, pair), f32),
                pltpu.VMEM((seq, pair), f32),
            ],
        ),
        out_shape=sds((3, seq, width), low),
        compiler_params=params(60),
        cost_estimate=cost(pairs * 2 * half * 5 * 2 * 256, seq * width * 14, pairs * 2 * half),
        name="attend_backward",
    )(length, qkv, qkv, qkv, upstream, lse, *after)


def normalize(values):
    average = jnp.mean(values, axis=-1, keepdims=True)
    centred = values - average
    inverse = lax.rsqrt(jnp.mean(centred * centred, axis=-1, keepdims=True) + eps_norm)
    return centred * inverse, inverse


def pull_norm(scaled, unit, inverse):
    first = jnp.mean(scaled, axis=-1, keepdims=True)
    second = jnp.mean(scaled * unit, axis=-1, keepdims=True)
    return inverse * (scaled - first - unit * second)


def columns_of(values):
    return jnp.sum(values, axis=0, keepdims=True)


def pack_body(input_ref, output_ref, expand_ref, shrink_ref, attend_ref, feed_ref):
    width = input_ref.shape[2]
    part = expand_ref.shape[1] // 3
    for index in range(3):
        attend_ref[:, index * width : (index + 1) * width] = input_ref[index].astype(low)
        at = slice(index * part, (index + 1) * part)
        feed_ref[:, 2 * index * part : (2 * index + 1) * part] = expand_ref[:, at].astype(low)
        feed_ref[:, (2 * index + 1) * part : (2 * index + 2) * part] = shrink_ref[:, at].astype(low)
    attend_ref[:, 3 * width :] = output_ref[...].T.astype(low)


def pack(input_weight, output_weight, expand, shrink):
    rows, width = input_weight.shape[1:]
    hidden = expand.shape[1]
    return pl.pallas_call(
        pack_body,
        out_shape=[sds((rows, 4 * width), low), sds((rows, 2 * hidden), low)],
        compiler_params=params(60),
        cost_estimate=cost(rows * hidden, rows * hidden * 18),
        name="pack",
    )(input_weight, output_weight, expand, shrink)


def prepare_body(x_ref, up_ref, vec_ref, h_ref, ht_ref, upt_ref):
    unit, _ = normalize(x_ref[...].astype(f32))
    h = (unit * vec_ref[0:1, :] + vec_ref[1:2, :]).astype(low)
    h_ref[...] = h
    ht_ref[...] = h.T
    upt_ref[...] = up_ref[...].T


def prepare(x, up, vectors, after):
    seq, depth = x.shape
    rows = pl.BlockSpec((TILE, depth), lambda i: (i, 0))
    turned = pl.BlockSpec((depth, TILE), lambda i: (0, i))
    return pl.pallas_call(
        held_back(prepare_body, 3, len(after)),
        grid=(seq // TILE,),
        in_specs=[rows, rows, whole(vectors.shape)] + [LATER] * len(after),
        out_specs=[rows, turned, turned],
        out_shape=[sds((seq, depth), low), sds((depth, seq), low), sds((depth, seq), low)],
        compiler_params=params(60),
        cost_estimate=cost(seq * depth * 10, seq * depth * 10),
        name="prepare",
    )(x, up, vectors, *after)


def slot(halves, spot, at):
    first, second = halves
    inner = spot & 7
    return jnp.where(spot < 8, first[inner, :, at], second[inner, :, at])


def project_body(
    core_ref, spots_ref, h_ref, mine_a, mine_b, twin_a, twin_b, bias_ref, qkv_ref, wide_ref
):
    part = pl.program_id(0)
    rows = mine_a.shape[1]
    width = mine_a.shape[2] // 4
    groups = wide_ref.shape[1] // rows

    def collect(sources, index):
        at = slice(index * width, (index + 1) * width)
        for group in range(groups):
            pieces = [slot(sources[model % 2], spots_ref[model, group], at) for model in range(4)]
            wide_ref[0, group * rows : (group + 1) * rows, :] = jnp.concatenate(pieces, axis=1)

    for index in range(4):
        for core in range(2):

            @pl.when((part == index) & (core_ref[0] == core))
            def _(index=index, core=core):
                mine, twin = (mine_a, mine_b), (twin_a, twin_b)
                collect((mine, twin) if core == 0 else (twin, mine), index)

    @pl.when(part < 3)
    def _():
        qkv_ref[...] = (mm(h_ref[...], wide_ref[0]) + bias_ref[0]).astype(low)


def project(core, spots, h, halves, bias, after):
    seq, depth = h.shape
    return pl.pallas_call(
        held_back(project_body, 8, len(after)),
        grid_spec=pltpu.PrefetchScalarGridSpec(
            num_scalar_prefetch=2,
            grid=(4,),
            in_specs=[
                whole((seq, depth)),
                *[whole(halves[0].shape)] * 4,
                pl.BlockSpec((1, 1, depth), lambda i, *_: (jnp.minimum(i, 2), 0, 0)),
            ]
            + [LATER] * len(after),
            out_specs=[
                pl.BlockSpec((seq, depth), lambda i, *_: (0, jnp.minimum(i, 2))),
                pl.BlockSpec((1, depth, depth), lambda i, *_: (i, 0, 0)),
            ],
        ),
        out_shape=[sds((seq, 3 * depth), low), sds((4, depth, depth), low)],
        compiler_params=params(60),
        cost_estimate=cost(2 * seq * depth * depth * 3, seq * depth * 16),
        name="project",
    )(core, spots, h, *halves, bias, *after)


def attend_out_body(o_ref, w_ref, x_ref, vec_ref, middle_ref, h_ref, ht_ref):
    middle = x_ref[...].astype(f32) + mm_nt(o_ref[...], w_ref[0]) + vec_ref[4:5, :]
    middle_ref[...] = middle
    unit, _ = normalize(middle)
    h = (unit * vec_ref[2:3, :] + vec_ref[3:4, :]).astype(low)
    h_ref[...] = h
    ht_ref[...] = h.T


def attend_out(o, wide, x, vectors):
    seq, depth = x.shape
    rows = pl.BlockSpec((TILE, depth), lambda i: (i, 0))
    turned = pl.BlockSpec((depth, TILE), lambda i: (0, i))
    return pl.pallas_call(
        attend_out_body,
        grid=(seq // TILE,),
        in_specs=[
            rows,
            pl.BlockSpec((1, depth, depth), lambda i: (3, 0, 0)),
            rows,
            whole(vectors.shape),
        ],
        out_specs=[rows, rows, turned],
        out_shape=[sds((seq, depth), f32), sds((seq, depth), low), sds((depth, seq), low)],
        compiler_params=params(60),
        cost_estimate=cost(2 * seq * depth * depth, seq * depth * 14),
        name="attend_out",
    )(o, wide, x, vectors)


def feed_body(
    spots_ref,
    h2_ref,
    h2t_ref,
    up_ref,
    upt_ref,
    mine_a,
    mine_b,
    twin_a,
    twin_b,
    bias_ref,
    middle_ref,
    vec_ref,
    block_ref,
    back_ref,
    keep_ref,
    send_ref,
    bias_grad_ref,
    out_ref,
    wide_ref,
    act_ref,
    pre_ref,
):
    step = pl.program_id(0)
    side = lax.rem(step, 2)
    rows = mine_a.shape[1]
    part = mine_a.shape[2] // 2
    groups = wide_ref.shape[0] // rows

    @pl.when(step == 0)
    def _():
        out_ref[...] = middle_ref[...] + vec_ref[5:6, :]
        back_ref[...] = jnp.zeros_like(back_ref)

    for group in range(groups):
        at = slice(group * rows, (group + 1) * rows)
        own = slot((mine_a, mine_b), spots_ref[0, side, group], slice(None))
        other = slot((twin_a, twin_b), spots_ref[1, side, group], slice(None))
        wide_ref[at, :part] = own[:, :part]
        wide_ref[at, part : 2 * part] = other[:, :part]
        wide_ref[at, 2 * part : 3 * part] = own[:, part:]
        wide_ref[at, 3 * part :] = other[:, part:]

    expand = wide_ref[:, : 2 * part]
    shrink = wide_ref[:, 2 * part :]
    bias = bias_ref[0]
    sums = jnp.zeros((1, 2 * part), f32)
    for tile in range(h2_ref.shape[0] // TILE):
        at = slice(tile * TILE, (tile + 1) * TILE)
        u = mm(h2_ref[at, :], expand) + bias
        square = u * u
        th = jnp.tanh(u * (GELU_A + GELU_B * square))
        gate = 0.5 * th + 0.5
        slope = gate + (gate * (1.0 - gate)) * (u * (2.0 * GELU_A + (6.0 * GELU_B) * square))
        pre = (mm(up_ref[at, :], shrink) * slope).astype(low)
        act_ref[at, :] = (u * gate).astype(low)
        pre_ref[at, :] = pre
        sums = sums + columns_of(pre.astype(f32))
    bias_grad_ref[0] = sums
    out_ref[...] += mm_nt(act_ref[...], shrink)
    back_ref[...] += mm_nt(pre_ref[...], expand)
    grad_expand = mm(h2t_ref[...], pre_ref[...]).astype(low)
    grad_shrink = mm(upt_ref[...], act_ref[...]).astype(low)
    for group in range(groups):
        at = slice(group * rows, (group + 1) * rows)
        own, other = spots_ref[0, side, group], spots_ref[1, side, group]
        keep_ref[own, :, :part] = grad_expand[at, :part]
        keep_ref[own, :, part:] = grad_shrink[at, :part]
        send_ref[other, :, :part] = grad_expand[at, part:]
        send_ref[other, :, part:] = grad_shrink[at, part:]

    @pl.when(step == pl.num_programs(0) - 1)
    def _():
        block_ref[...] = out_ref[...].astype(low)


def feed(spots, h2, h2t, up, upt, halves, bias, middle, vectors):
    seq, depth = h2.shape
    half, rows, columns = halves[0].shape
    steps = bias.shape[0]
    part = bias.shape[2] // 2
    half_piece = pl.BlockSpec((half, rows, 2 * part), lambda i, s: (0, 0, i // 2))
    piece = pl.BlockSpec((2 * half, rows, 2 * part), lambda i, s: (0, 0, i // 2))
    bias_spec = pl.BlockSpec((1, 1, 2 * part), lambda i, s: (i, 0, 0))
    return pl.pallas_call(
        feed_body,
        grid_spec=pltpu.PrefetchScalarGridSpec(
            num_scalar_prefetch=1,
            grid=(steps,),
            in_specs=[
                whole((seq, depth)),
                whole((depth, seq)),
                whole((seq, depth)),
                whole((depth, seq)),
                *[half_piece] * 4,
                bias_spec,
                whole((seq, depth)),
                whole(vectors.shape),
            ],
            out_specs=[whole((seq, depth)), whole((seq, depth)), piece, piece, bias_spec],
            scratch_shapes=[
                pltpu.VMEM((seq, depth), f32),
                pltpu.VMEM((depth, 4 * part), low),
                pltpu.VMEM((seq, 2 * part), low),
                pltpu.VMEM((seq, 2 * part), low),
            ],
        ),
        out_shape=[sds((seq, depth), low), sds((seq, depth), f32)]
        + [sds((2 * half, rows, columns), low)] * 2
        + [sds(bias.shape, f32)],
        compiler_params=params(60),
        cost_estimate=cost(12 * seq * depth * steps * 2 * part, seq * depth * 40, seq * steps * part),
        name="feed",
    )(spots, h2, h2t, up, upt, *halves, bias, middle, vectors)


def middle_back_body(
    length_ref,
    back_ref,
    middle_ref,
    up_ref,
    o_ref,
    w_ref,
    vec_ref,
    grad_ref,
    mixture_ref,
    weight_ref,
    sums_ref,
):
    step = pl.program_id(0)
    middle = middle_ref[...]
    unit, inverse = normalize(middle)
    back = back_ref[...]
    up = up_ref[...].astype(f32)
    grad = up + pull_norm(back * vec_ref[2:3, :], unit, inverse)
    grad_ref[...] = grad
    rounded = grad.astype(low)
    first = step * TILE
    row = first + lax.broadcasted_iota(jnp.int32, (TILE, grad.shape[1]), 0)
    mixture_ref[...] = jnp.where(row < length_ref[0], mm(rounded, w_ref[0]), 0.0).astype(low)
    share = mm(rounded.T, o_ref[...])
    sums = jnp.concatenate(
        [columns_of(back * unit), columns_of(back), columns_of(grad), columns_of(up)], axis=0
    )

    @pl.when(step == 0)
    def _():
        weight_ref[...] = share
        sums_ref[...] = sums

    @pl.when(step > 0)
    def _():
        weight_ref[...] += share
        sums_ref[...] += sums


def middle_back(length, back, middle, up, o, wide, vectors):
    seq, depth = middle.shape
    rows = pl.BlockSpec((TILE, depth), lambda i, s: (i, 0))
    return pl.pallas_call(
        middle_back_body,
        grid_spec=pltpu.PrefetchScalarGridSpec(
            num_scalar_prefetch=1,
            grid=(seq // TILE,),
            in_specs=[
                rows,
                rows,
                rows,
                rows,
                pl.BlockSpec((1, depth, depth), lambda i, s: (3, 0, 0)),
                whole(vectors.shape),
            ],
            out_specs=[rows, rows, whole((depth, depth)), whole((4, depth))],
        ),
        out_shape=[
            sds((seq, depth), f32),
            sds((seq, depth), low),
            sds((depth, depth), f32),
            sds((4, depth), f32),
        ],
        compiler_params=params(60),
        cost_estimate=cost(4 * seq * depth * depth, seq * depth * 28),
        name="middle_back",
    )(length, back, middle, up, o, wide, vectors)


def input_grad_body(core_ref, spots_ref, ht_ref, back_ref, out_grad_ref, keep_ref, send_ref, sums_ref):
    part = pl.program_id(0)
    rows = keep_ref.shape[1]
    width = keep_ref.shape[2] // 4
    groups = ht_ref.shape[0] // rows

    def spread(targets, index, grad):
        at = slice(index * width, (index + 1) * width)
        for group in range(groups):
            for model in range(4):
                targets[model % 2][spots_ref[model, group], :, at] = grad[
                    group * rows : (group + 1) * rows, model * width : (model + 1) * width
                ]

    for index in range(4):

        @pl.when(part == index)
        def _(index=index):
            if index < 3:
                sums_ref[0] = columns_of(back_ref[0].astype(f32))
                grad = mm(ht_ref[...], back_ref[0]).astype(low)
            else:
                grad = out_grad_ref[...].astype(low)
            for core in range(2):

                @pl.when(core_ref[0] == core)
                def _(core=core):
                    spread((keep_ref, send_ref) if core == 0 else (send_ref, keep_ref), index, grad)


def input_grad(core, spots, ht, back, out_grad, slots, rows, after):
    depth, seq = ht.shape
    shape = (slots, rows, 4 * (depth // 4))
    return pl.pallas_call(
        held_back(input_grad_body, 5, len(after)),
        grid_spec=pltpu.PrefetchScalarGridSpec(
            num_scalar_prefetch=2,
            grid=(4,),
            in_specs=[
                whole((depth, seq)),
                pl.BlockSpec((1, seq, depth), lambda i, *_: (jnp.minimum(i, 2), 0, 0)),
                whole((depth, depth)),
            ]
            + [LATER] * len(after),
            out_specs=[
                whole(shape),
                whole(shape),
                pl.BlockSpec((1, 1, depth), lambda i, *_: (jnp.minimum(i, 2), 0, 0)),
            ],
        ),
        out_shape=[sds(shape, low), sds(shape, low), sds((3, 1, depth), f32)],
        compiler_params=params(60),
        cost_estimate=cost(6 * seq * depth * depth, seq * depth * 14),
        name="input_grad",
    )(core, spots, ht, back, out_grad, *after)


def token_back_body(back_ref, w_ref, x_ref, grad_ref, vec_ref, token_ref, sums_ref):
    step = pl.program_id(0)
    back = mm_nt(back_ref[0], w_ref[0]) + mm_nt(back_ref[1], w_ref[1]) + mm_nt(back_ref[2], w_ref[2])
    unit, inverse = normalize(x_ref[...].astype(f32))
    token_ref[...] = (grad_ref[...] + pull_norm(back * vec_ref[0:1, :], unit, inverse)).astype(low)
    sums = jnp.concatenate([columns_of(back * unit), columns_of(back)], axis=0)

    @pl.when(step == 0)
    def _():
        sums_ref[...] = sums

    @pl.when(step > 0)
    def _():
        sums_ref[...] += sums


def token_back(back, wide, x, grad, vectors, after):
    seq, depth = x.shape
    rows = pl.BlockSpec((TILE, depth), lambda i: (i, 0))
    return pl.pallas_call(
        held_back(token_back_body, 5, len(after)),
        grid=(seq // TILE,),
        in_specs=[
            pl.BlockSpec((3, TILE, depth), lambda i: (0, i, 0)),
            pl.BlockSpec((3, depth, depth), lambda i: (0, 0, 0)),
            rows,
            rows,
            whole(vectors.shape),
        ]
        + [LATER] * len(after),
        out_specs=[rows, whole((2, depth))],
        out_shape=[sds((seq, depth), low), sds((2, depth), f32)],
        compiler_params=params(60),
        cost_estimate=cost(6 * seq * depth * depth, seq * depth * 16),
        name="token_back",
    )(back, wide, x, grad, vectors, *after)


CORE_ORDERS = ((4, 3, 2, 1), (3, 4, 1, 2))
STAGES = 4


def cube_permute(values, stage):
    pairs = [(device, device ^ (1 << CORE_ORDERS[device & 1][stage])) for device in range(32)]
    return lax.ppermute(values, ("dp", "mp"), pairs)


def bit_permute(values, bit):
    return lax.ppermute(values, ("dp", "mp"), [(device, device ^ (1 << bit)) for device in range(32)])


def place(distance, core):
    spots = [
        sum(((distance >> bit) & 1) << step for step, bit in enumerate(order)) for order in CORE_ORDERS
    ]
    return jnp.where(core == 0, spots[0], spots[1])


def joined(held, arrived):
    return jnp.concatenate([held, arrived], axis=0)


def leaving(parts, stage):
    half = 1 << stage
    return sum(part[half:].astype(f32) for part in parts).astype(low)


def staying(parts, stage):
    return [part[: 1 << stage] for part in parts]


def summed(parts):
    return sum(part[0].astype(f32) for part in parts)


def cube_sum(values, bits=range(5)):
    for bit in bits:
        values = values + bit_permute(values, bit)
    return values


def adam_parts(weight, gradient, first_old, second_old, factor, step_rate):
    scaled = gradient * factor
    moment = beta_one * first_old + (1.0 - beta_one) * scaled
    square = beta_two * second_old + (1.0 - beta_two) * scaled * scaled
    spread = jnp.sqrt(square * (1.0 / (1.0 - beta_two**STEP)))
    ratio = moment * (1.0 / (1.0 - beta_one**STEP)) / (spread + adam_eps)
    return moment, square, weight - step_rate * (ratio + decay * weight)


def optimize_body(owned_ref, vector_ref, attend_ref, feed_ref, *refs):
    state, outs = refs[:15], refs[15:]
    vectors = vector_ref[...]
    total = owned_ref[0:1, 0:1] + jnp.sum(vectors * vectors)
    norm = jnp.sqrt(total)
    factor = clip_norm / jnp.maximum(norm, clip_norm)
    outs[0][...] = norm
    outs[1][...] = factor
    width = state[0].shape[2]
    part = state[6].shape[1] // 3

    def update(param, at, gradient, step_rate):
        weight, first, second = (ref[at] for ref in state[3 * param : 3 * param + 3])
        results = adam_parts(weight, gradient, first, second, factor, step_rate)
        for ref, result in zip(outs[2 + 3 * param : 5 + 3 * param], results):
            ref[at] = result

    for index in range(3):
        update(0, (index,), attend_ref[:, index * width : (index + 1) * width], rate)
    update(1, (...,), attend_ref[:, 3 * width :].T, rate)
    for index in range(3):
        at = (slice(None), slice(index * part, (index + 1) * part))
        first = 2 * index * part
        update(2, at, feed_ref[:, first : first + part], rate)
        update(3, at, feed_ref[:, first + part : first + 2 * part], rate)
    update(4, (...,), vectors[:6], vector_rate)


def optimize(owned, vector_total, attend_total, feed_total, state):
    shapes = [sds(group[0].shape, f32) for group in state for _ in range(3)]
    return pl.pallas_call(
        optimize_body,
        out_shape=[sds((1, 1), f32), sds((1, 1), f32)] + shapes,
        compiler_params=params(60),
        cost_estimate=cost(4e6, 8e6),
        name="optimize",
    )(owned, vector_total, attend_total, feed_total, *[array for group in state for array in group])


def shards(
    tokens,
    cotangent,
    lengths,
    input_weight,
    output_weight,
    expand_weight,
    shrink_weight,
    layer_vectors,
    head_bias,
    expand_bias,
    first_input,
    first_output,
    first_expand,
    first_shrink,
    first_vectors,
    first_head,
    first_bias,
    second_input,
    second_output,
    second_expand,
    second_shrink,
    second_vectors,
    second_head,
    second_bias,
):
    dp_count = lax.axis_size("dp")
    mp_count = lax.axis_size("mp")
    cube = dp_count == 8 and mp_count == 4
    rows = input_weight.shape[0]
    width = input_weight.shape[2]
    hidden = expand_weight.shape[1]
    seq, depth = tokens.shape
    part = hidden // 3
    model_index = lax.axis_index("mp")
    me = lax.axis_index("dp") * mp_count + model_index

    attend_shard, feed_shard = pack(
        input_weight.transpose(1, 0, 2), output_weight, expand_weight, shrink_weight.T
    )
    bias_shard = jnp.concatenate([head_bias.reshape(1, 2 * width), expand_bias[None]], axis=1)

    bias_full = jnp.where(jnp.arange(4)[:, None] == model_index, bias_shard, 0.0)
    if cube:
        core = me & 1
        bias_full = bias_full + bit_permute(bias_full, 0)
        bias_full = bias_full + bit_permute(bias_full, 1)
        devices = jnp.arange(32).reshape(8, 4).T
        spots = place(devices ^ me, devices & 1).astype(jnp.int32)
        near = model_index
    else:
        core = jnp.zeros((), jnp.int32)
        bias_full = lax.psum(bias_full, "mp")
        spots = (jnp.arange(4)[:, None] // 2 * 8 + jnp.arange(8)[None]).astype(jnp.int32)
        near = jnp.zeros((), jnp.int32)
    near_models = near ^ jnp.arange(4)
    near_spots = jnp.take(spots, near_models, axis=0).reshape(2, 2, 8).transpose(1, 0, 2)
    core = core.astype(jnp.int32).reshape(1)

    length = lax.dynamic_slice_in_dim(lengths, model_index, 1, 0)
    head_full = bias_full[:, : 2 * width].reshape(4, 2, width).transpose(1, 0, 2).reshape(2, depth)
    qkv_bias = jnp.stack([head_full[0], jnp.zeros_like(head_full[0]), head_full[1]])[:, None]
    feed_bias = (
        jnp.take(bias_full[:, 2 * width :], near_models, axis=0)
        .reshape(2, 2, 3, part)
        .transpose(2, 0, 1, 3)
        .reshape(6, 1, 2 * part)
    )

    if cube:
        held = attend_shard[None]
        held = joined(held, cube_permute(held, 0))
        feed_held = feed_shard[None]
        feed_held = joined(feed_held, cube_permute(feed_held, 0))
        arrived = cube_permute(held, 1)
        normed, normed_t, upstream_t = prepare(tokens, cotangent, layer_vectors, (held,))
        held, normed = lax.optimization_barrier((held, normed))
        held = joined(held, arrived)
        held, feed_held = lax.optimization_barrier((held, feed_held))
        held = joined(held, cube_permute(held, 2))
        far, far_feed = cube_permute(held, 3), cube_permute(feed_held, 1)
        twin = bit_permute(held, 0)
        feed_held = joined(feed_held, far_feed)
        far, feed_held = lax.optimization_barrier((far, feed_held))
        attend_halves = (held, far, twin, bit_permute(far, 0))
        arrived = cube_permute(feed_held, 2)
        qkv, wide = project(core, spots, normed, attend_halves, qkv_bias, ())
        feed_held, qkv = lax.optimization_barrier((feed_held, qkv))
        feed_held = joined(feed_held, arrived)
        far, twin = cube_permute(feed_held, 3), bit_permute(feed_held, 0)
        mixture, log_totals = attend_forward(length, qkv, (feed_held,))
        middle, hidden_in, hidden_t = attend_out(mixture, wide, tokens, layer_vectors)
        far, hidden_in = lax.optimization_barrier((far, hidden_in))
        feed_halves = (feed_held, far, twin, bit_permute(far, 0))
    else:

        def planes(shard):
            full = lax.all_gather(lax.all_gather(shard, "dp", axis=0, tiled=True), "mp", axis=0)
            full = full.reshape(2, 2, 8, depth // 8, shard.shape[1]).transpose(1, 0, 2, 3, 4)
            return tuple(full.reshape(4, 8, depth // 8, shard.shape[1]))

        normed, normed_t, upstream_t = prepare(tokens, cotangent, layer_vectors, ())
        qkv, wide = project(core, spots, normed, planes(attend_shard), qkv_bias, ())
        mixture, log_totals = attend_forward(length, qkv, ())
        middle, hidden_in, hidden_t = attend_out(mixture, wide, tokens, layer_vectors)
        feed_halves = planes(feed_shard)
    block_out, back, keep_feed, send_feed, feed_bias_grad = feed(
        near_spots,
        hidden_in,
        hidden_t,
        cotangent,
        upstream_t,
        feed_halves,
        feed_bias,
        middle,
        layer_vectors,
    )
    middle_grad, mixture_grad, output_grad, middle_sums = middle_back(
        length, back, middle, cotangent, mixture, wide, layer_vectors
    )
    if cube:
        feed_parts = [keep_feed, bit_permute(send_feed, 0)]
        keep_feed, mixture_grad = lax.optimization_barrier((keep_feed, mixture_grad))
        feed_parts[0] = keep_feed
        away = leaving(feed_parts, 3)
        packed_grad = attend_backward(length, qkv, mixture_grad, log_totals, (away,))
        feed_parts = staying(feed_parts, 3) + [cube_permute(away, 3)]
        feed_parts[0], packed_grad = lax.optimization_barrier((feed_parts[0], packed_grad))
        away = leaving(feed_parts, 2)
        keep_attend, send_attend, head_sums = input_grad(
            core, spots, normed_t, packed_grad, output_grad, 16, depth // 8, (away,)
        )
        feed_parts = staying(feed_parts, 2) + [cube_permute(away, 2)]
        feed_parts[-1], send_attend = lax.optimization_barrier((feed_parts[-1], send_attend))
        attend_parts = [keep_attend, bit_permute(send_attend, 0)]
        away, feed_away = leaving(attend_parts, 3), leaving(feed_parts, 1)
        token_grad, token_sums = token_back(
            packed_grad, wide, tokens, middle_grad, layer_vectors, (away, feed_away)
        )
    else:
        packed_grad = attend_backward(length, qkv, mixture_grad, log_totals, ())
        keep_attend, send_attend, head_sums = input_grad(
            core, spots, normed_t, packed_grad, output_grad, 16, depth // 8, ()
        )
        token_grad, token_sums = token_back(packed_grad, wide, tokens, middle_grad, layer_vectors, ())

    bias_near = feed_bias_grad.reshape(3, 2, 2, part).transpose(1, 2, 0, 3).reshape(4, hidden)
    bias_grad = jnp.take(bias_near, near_models, axis=0)
    vector_local = jnp.concatenate(
        [token_sums, middle_sums, head_sums[0], head_sums[2], bias_grad.reshape(4, depth)], axis=0
    )
    if cube:
        attend_parts = staying(attend_parts, 3) + [cube_permute(away, 3)]
        feed_parts = staying(feed_parts, 1) + [cube_permute(feed_away, 1)]
        vector_total = cube_sum(vector_local, (0, 1))
        attend_parts[0], vector_total = lax.optimization_barrier((attend_parts[0], vector_total))
        away = leaving(attend_parts, 2)
        attend_parts = staying(attend_parts, 2) + [cube_permute(away, 2)]
        feed_away = leaving(feed_parts, 0)
        feed_parts = staying(feed_parts, 0) + [cube_permute(feed_away, 0)]
        vector_total = cube_sum(vector_total, (2, 3))
        attend_parts[0], vector_total = lax.optimization_barrier((attend_parts[0], vector_total))
        away = leaving(attend_parts, 1)
        attend_parts = staying(attend_parts, 1) + [cube_permute(away, 1)]
        vector_total = cube_sum(vector_total, (4,))
        feed_total = summed(feed_parts)
        feed_squares = jnp.sum(feed_total * feed_total)
        attend_parts[0], vector_total, feed_squares = lax.optimization_barrier(
            (attend_parts[0], vector_total, feed_squares)
        )
        away = leaving(attend_parts, 0)
        attend_parts = staying(attend_parts, 0) + [cube_permute(away, 0)]
        attend_total = summed(attend_parts)
    else:

        def own_block(keep, send):
            full = jnp.stack([keep, send]).reshape(2, 2, 8, depth // 8, keep.shape[2])
            full = full.transpose(1, 0, 2, 3, 4).reshape(4, depth, keep.shape[2])
            full = lax.psum_scatter(full, "mp", scatter_dimension=0, tiled=False)
            return lax.psum_scatter(full, "dp", scatter_dimension=0, tiled=True).astype(f32)

        attend_total = own_block(keep_attend, send_attend)
        feed_total = own_block(keep_feed, send_feed)
        vector_total = lax.psum(vector_local, ("dp", "mp"))
        feed_squares = jnp.sum(feed_total * feed_total)
    owned = jnp.full((8, 128), jnp.sum(attend_total * attend_total) + feed_squares, f32)
    owned = cube_sum(owned) if cube else lax.psum(owned, ("dp", "mp"))
    head_total = lax.dynamic_slice_in_dim(vector_total[6:8], model_index * width, width, 1)
    bias_total = lax.dynamic_slice_in_dim(vector_total[8:].reshape(-1), model_index * hidden, hidden, 0)

    def turned(array):
        return array.transpose(1, 0, 2)

    state = (
        (turned(input_weight), turned(first_input), turned(second_input)),
        (output_weight, first_output, second_output),
        (expand_weight, first_expand, second_expand),
        (shrink_weight.T, first_shrink.T, second_shrink.T),
        (layer_vectors, first_vectors, second_vectors),
    )
    grad_norm, factor, *updates = optimize(owned, vector_total, attend_total, feed_total, state)
    grad_norm, factor = grad_norm[0, 0], factor[0, 0]
    moment_input, square_input, updated_input = (turned(array) for array in updates[:3])
    moment_output, square_output, updated_output = updates[3:6]
    moment_expand, square_expand, updated_expand = updates[6:9]
    moment_shrink, square_shrink, updated_shrink = (array.T for array in updates[9:12])
    moment_vectors, square_vectors, updated_vectors = updates[12:]
    moment_head, square_head, updated_head = adam_parts(
        head_bias, head_total, first_head, second_head, factor, vector_rate
    )
    moment_bias, square_bias, updated_bias = adam_parts(
        expand_bias, bias_total, first_bias, second_bias, factor, vector_rate
    )
    return (
        block_out,
        token_grad,
        grad_norm,
        moment_input,
        square_input,
        updated_input,
        moment_output,
        square_output,
        updated_output,
        moment_expand,
        square_expand,
        updated_expand,
        moment_shrink,
        square_shrink,
        updated_shrink,
        moment_vectors,
        square_vectors,
        updated_vectors,
        moment_head,
        square_head,
        updated_head,
        moment_bias,
        square_bias,
        updated_bias,
    )


def solution(mesh):
    in_specs = (
        P(("dp", "mp"), None),
        P(("dp", "mp"), None),
        P("dp"),
        P("dp", None, "mp"),
        P("mp", "dp"),
        P("dp", "mp"),
        P("mp", "dp"),
        P(),
        P(None, "mp"),
        P("mp"),
        P("dp", None, "mp"),
        P("mp", "dp"),
        P("dp", "mp"),
        P("mp", "dp"),
        P(),
        P(None, "mp"),
        P("mp"),
        P("dp", None, "mp"),
        P("mp", "dp"),
        P("dp", "mp"),
        P("mp", "dp"),
        P(),
        P(None, "mp"),
        P("mp"),
    )
    out_specs = (
        P(("dp", "mp"), None),
        P(("dp", "mp"), None),
        P(),
        P("dp", None, "mp"),
        P("dp", None, "mp"),
        P("dp", None, "mp"),
        P("mp", "dp"),
        P("mp", "dp"),
        P("mp", "dp"),
        P("dp", "mp"),
        P("dp", "mp"),
        P("dp", "mp"),
        P("mp", "dp"),
        P("mp", "dp"),
        P("mp", "dp"),
        P(),
        P(),
        P(),
        P(None, "mp"),
        P(None, "mp"),
        P(None, "mp"),
        P("mp"),
        P("mp"),
        P("mp"),
    )
    return jax.shard_map(shards, mesh=mesh, in_specs=in_specs, out_specs=out_specs, check_vma=False)
```

```python
import functools
import jax
import jax.numpy as jnp
from jax import lax
from jax.experimental import pallas as pl
from jax.experimental.pallas import tpu as pltpu
from jax.sharding import PartitionSpec as P

HEAD_DIM = 64
TILE = 256
STEP = 10

eps_norm = 1e-05
clip_norm = 1.0
beta_one = 0.9
beta_two = 0.999
adam_eps = 1e-08
rate = 0.05
vector_rate = 0.5
decay = 0.01
excluded = -1e30
low = jnp.bfloat16
f32 = jnp.float32
GELU_A = 0.7978845608028654
GELU_B = GELU_A * 0.044715


def params(limit_mib, **kw):
    return pltpu.CompilerParams(vmem_limit_bytes=limit_mib * 1024 * 1024, **kw)


def cost(flops, moved, special=0):
    return pl.CostEstimate(flops=int(flops), bytes_accessed=int(moved), transcendentals=int(special))


def mm(a, b):
    return jnp.dot(a, b, preferred_element_type=f32)


def mm_nt(a, b):
    return lax.dot_general(a, b, (((1,), (1,)), ((), ())), preferred_element_type=f32)


def whole(shape):
    zeros = (0,) * len(shape)
    return pl.BlockSpec(shape, lambda *_: zeros)


def held_back(body, first, count):
    def run(*refs):
        return body(*refs[:first], *refs[first + count :])

    return run


LATER = pl.BlockSpec(memory_space=pl.ANY)


def sds(shape, dtype):
    return jax.ShapeDtypeStruct(shape, dtype)


def live_blocks(length, count, body):
    for blocks in range(1, count + 1):
        low_end = (blocks - 1) * TILE
        high_end = blocks * TILE
        @pl.when((length > low_end) & (length <= high_end))
        def _(blocks=blocks):
            body(length, blocks)


PAIR = 2 * HEAD_DIM


def span(block):
    return slice(block * TILE, (block + 1) * TILE)


def both_heads(values):
    lane = lax.broadcasted_iota(jnp.int32, values.shape, 1)
    none = jnp.zeros_like(values)
    return jnp.concatenate(
        [jnp.where(lane < HEAD_DIM, values, none), jnp.where(lane >= HEAD_DIM, values, none)], axis=0
    )


def causal_mask():
    key_id = lax.broadcasted_iota(jnp.int32, (TILE, 2 * TILE), 0)
    query_id = lax.broadcasted_iota(jnp.int32, (TILE, 2 * TILE), 1) & (TILE - 1)
    return key_id <= query_id


def forward_body(where_ref, lengths_ref, q_ref, k_ref, v_ref, o_ref, lse_ref, vt_ref):
    seq = q_ref.shape[0]
    vt_ref[...] = v_ref[...].T
    causal = causal_mask()

    def run(length, blocks):
        def scores(b):
            q = q_ref[span(b), :] * jnp.asarray(HEAD_DIM**-0.5, low)
            return mm_nt(k_ref[: (b + 1) * TILE, :], both_heads(q))

        now = scores(0)
        for b in range(blocks):
            start, stop = b * TILE, (b + 1) * TILE
            later = scores(b + 1) if b + 1 < blocks else None
            last = jnp.where(causal, now[start:, :], excluded)
            top = jnp.max(last, axis=0, keepdims=True)
            if b:
                top = jnp.maximum(top, jnp.max(now[:start], axis=0, keepdims=True))
            p = jnp.exp(last - top)
            total = jnp.sum(p, axis=0, keepdims=True)
            pb = p.astype(low)
            if b:
                pf = jnp.exp(now[:start] - top)
                total = total + jnp.sum(pf, axis=0, keepdims=True)
                pb = jnp.concatenate([pf.astype(low), pb], axis=0)
            inverse = 1.0 / total
            lse = top + jnp.log(total)
            outs = []
            for h in range(2):
                at = slice(h * TILE, (h + 1) * TILE)
                out = mm(vt_ref[h * HEAD_DIM : (h + 1) * HEAD_DIM, :stop], pb[:, at])
                outs.append(out * inverse[:, at])
                lse_ref[0, h : h + 1, start:stop] = lse[:, at]
            both = jnp.concatenate(outs, axis=0).T
            row = start + lax.broadcasted_iota(jnp.int32, both.shape, 0)
            o_ref[start:stop, :] = jnp.where(row < length, both, 0.0).astype(low)
            now = later
        if blocks * TILE < seq:
            o_ref[blocks * TILE :, :] = jnp.zeros((seq - blocks * TILE, PAIR), low)
            lse_ref[0, :, blocks * TILE :] = jnp.zeros((2, seq - blocks * TILE), f32)

    live_blocks(lengths_ref[where_ref[2]], seq // TILE, run)


def attend_forward(where, lengths, qkv, after):
    seq, width = qkv.shape[0], qkv.shape[1] // 3
    pair = 2 * HEAD_DIM
    pairs = width // pair
    half = seq * seq * 5 // 8
    spec = lambda part: pl.BlockSpec((seq, pair), lambda i, *_: (0, part * pairs + i))
    return pl.pallas_call(
        held_back(forward_body, 5, len(after)),
        grid_spec=pltpu.PrefetchScalarGridSpec(
            num_scalar_prefetch=2,
            grid=(pairs,),
            in_specs=[spec(0), spec(1), spec(2)] + [LATER] * len(after),
            out_specs=[
                pl.BlockSpec((seq, pair), lambda i, *_: (0, i)),
                pl.BlockSpec((1, 2, seq), lambda i, *_: (i, 0, 0)),
            ],
            scratch_shapes=[pltpu.VMEM((pair, seq), low)],
        ),
        out_shape=[sds((seq, width), low), sds((pairs, 2, seq), f32)],
        compiler_params=params(60),
        cost_estimate=cost(pairs * 2 * half * 2 * 2 * 256, seq * width * 8, pairs * 2 * half),
        name="attend_forward",
    )(where, lengths, qkv, qkv, qkv, *after)


def backward_body(where_ref, lengths_ref, q_ref, k_ref, v_ref, do_ref, lse_ref, out_ref, kt_ref, ksum, vsum):
    seq = q_ref.shape[0]
    scale = HEAD_DIM**-0.5
    kt_ref[...] = k_ref[...].T
    causal = causal_mask()

    def run(length, blocks):
        def scores(b):
            qq = both_heads(q_ref[span(b), :] * jnp.asarray(scale, low))
            uu = both_heads(do_ref[span(b), :])
            stop = (b + 1) * TILE
            return qq, uu, mm_nt(k_ref[:stop, :], qq), mm_nt(v_ref[:stop, :], uu)

        now = scores(blocks - 1)
        for b in reversed(range(blocks)):
            start, stop = b * TILE, (b + 1) * TILE
            later = scores(b - 1) if b else None
            qq, uu, s, dp = now
            lse = jnp.concatenate([lse_ref[0, 0:1, start:stop], lse_ref[0, 1:2, start:stop]], axis=1)
            p = jnp.exp(jnp.where(causal, s[start:], excluded) - lse)
            inner = jnp.sum(p * dp[start:], axis=0, keepdims=True)
            if b:
                pf = jnp.exp(s[:start] - lse)
                inner = inner + jnp.sum(pf * dp[:start], axis=0, keepdims=True)
            ds = (p * (dp[start:] - inner)).astype(low)
            pb = p.astype(low)
            if b:
                ds = jnp.concatenate([(pf * (dp[:start] - inner)).astype(low), ds], axis=0)
                pb = jnp.concatenate([pf.astype(low), pb], axis=0)
            dk, dv = mm(ds, qq), mm(pb, uu)
            if b == blocks - 1:
                ksum[:stop, :] = dk
                vsum[:stop, :] = dv
            else:
                ksum[:stop, :] += dk
                vsum[:stop, :] += dv
            dq = jnp.concatenate(
                [
                    mm(
                        kt_ref[h * HEAD_DIM : (h + 1) * HEAD_DIM, :stop],
                        ds[:, h * TILE : (h + 1) * TILE],
                    )
                    for h in range(2)
                ],
                axis=0,
            )
            out_ref[1, start:stop, :] = ksum[start:stop, :].astype(low)
            out_ref[2, start:stop, :] = vsum[start:stop, :].astype(low)
            out_ref[0, start:stop, :] = (dq.T * scale).astype(low)
            now = later
        if blocks * TILE < seq:
            rest = jnp.zeros((seq - blocks * TILE, PAIR), low)
            for part in range(3):
                out_ref[part, blocks * TILE :, :] = rest

    live_blocks(lengths_ref[where_ref[2]], seq // TILE, run)


def attend_backward(where, lengths, qkv, upstream, lse, after):
    seq, width = upstream.shape
    pair = 2 * HEAD_DIM
    pairs = width // pair
    half = seq * seq * 5 // 8
    spec = lambda part: pl.BlockSpec((seq, pair), lambda i, *_: (0, part * pairs + i))
    own = pl.BlockSpec((seq, pair), lambda i, *_: (0, i))
    return pl.pallas_call(
        held_back(backward_body, 7, len(after)),
        grid_spec=pltpu.PrefetchScalarGridSpec(
            num_scalar_prefetch=2,
            grid=(pairs,),
            in_specs=[spec(0), spec(1), spec(2), own, pl.BlockSpec((1, 2, seq), lambda i, *_: (i, 0, 0))]
            + [LATER] * len(after),
            out_specs=pl.BlockSpec((3, seq, pair), lambda i, *_: (0, 0, i)),
            scratch_shapes=[
                pltpu.VMEM((pair, seq), low),
                pltpu.VMEM((seq, pair), f32),
                pltpu.VMEM((seq, pair), f32),
            ],
        ),
        out_shape=sds((3, seq, width), low),
        compiler_params=params(60),
        cost_estimate=cost(pairs * 2 * half * 5 * 2 * 256, seq * width * 14, pairs * 2 * half),
        name="attend_backward",
    )(where, lengths, qkv, qkv, qkv, upstream, lse, *after)


def normalize(values):
    average = jnp.mean(values, axis=-1, keepdims=True)
    centred = values - average
    inverse = lax.rsqrt(jnp.mean(centred * centred, axis=-1, keepdims=True) + eps_norm)
    return centred * inverse, inverse


def pull_norm(scaled, unit, inverse):
    first = jnp.mean(scaled, axis=-1, keepdims=True)
    second = jnp.mean(scaled * unit, axis=-1, keepdims=True)
    return inverse * (scaled - first - unit * second)


def columns_of(values):
    return jnp.sum(values, axis=0, keepdims=True)


def pack_body(input_ref, output_ref, expand_ref, shrink_ref, attend_ref, feed_ref):
    width = input_ref.shape[2]
    part = expand_ref.shape[1] // 3
    for index in range(3):
        attend_ref[:, index * width : (index + 1) * width] = input_ref[index].astype(low)
        at = slice(index * part, (index + 1) * part)
        feed_ref[:, 2 * index * part : (2 * index + 1) * part] = expand_ref[:, at].astype(low)
        feed_ref[:, (2 * index + 1) * part : (2 * index + 2) * part] = shrink_ref[:, at].astype(low)
    attend_ref[:, 3 * width :] = output_ref[...].T.astype(low)


def pack(input_weight, output_weight, expand, shrink):
    rows, width = input_weight.shape[1:]
    hidden = expand.shape[1]
    return pl.pallas_call(
        pack_body,
        out_shape=[sds((rows, 4 * width), low), sds((rows, 2 * hidden), low)],
        compiler_params=params(60),
        cost_estimate=cost(rows * hidden, rows * hidden * 18),
        name="pack",
    )(input_weight, output_weight, expand, shrink)


def prepare_body(x_ref, up_ref, vec_ref, h_ref, ht_ref, upt_ref):
    unit, _ = normalize(x_ref[...].astype(f32))
    h = (unit * vec_ref[0:1, :] + vec_ref[1:2, :]).astype(low)
    h_ref[...] = h
    ht_ref[...] = h.T
    upt_ref[...] = up_ref[...].T


def prepare(x, up, vectors, after):
    seq, depth = x.shape
    rows = pl.BlockSpec((2 * TILE, depth), lambda i: (i, 0))
    turned = pl.BlockSpec((depth, 2 * TILE), lambda i: (0, i))
    return pl.pallas_call(
        held_back(prepare_body, 3, len(after)),
        grid=(seq // (2 * TILE),),
        in_specs=[rows, rows, whole(vectors.shape)] + [LATER] * len(after),
        out_specs=[rows, turned, turned],
        out_shape=[sds((seq, depth), low), sds((depth, seq), low), sds((depth, seq), low)],
        compiler_params=params(60),
        cost_estimate=cost(seq * depth * 10, seq * depth * 10),
        name="prepare",
    )(x, up, vectors, *after)


def slot(halves, spot, at):
    first, second = halves
    inner = spot & 7
    return jnp.where(spot < 8, first[inner, :, at], second[inner, :, at])


def project_body(
    where_ref, spots_ref, h_ref, mine_a, mine_b, twin_a, twin_b, bias_ref, qkv_ref, wide_ref
):
    part = pl.program_id(0)
    rows = mine_a.shape[1]
    width = mine_a.shape[2] // 4
    groups = wide_ref.shape[1] // rows

    def collect(sources, index):
        at = slice(index * width, (index + 1) * width)
        for group in range(groups):
            pieces = [slot(sources[model % 2], spots_ref[model, group], at) for model in range(4)]
            wide_ref[0, group * rows : (group + 1) * rows, :] = jnp.concatenate(pieces, axis=1)

    for index in range(4):
        for core in range(2):

            @pl.when((part == index) & (where_ref[0] == core))
            def _(index=index, core=core):
                mine, twin = (mine_a, mine_b), (twin_a, twin_b)
                collect((mine, twin) if core == 0 else (twin, mine), index)

    for index in range(3):

        @pl.when(part == index)
        def _(index=index):
            out = mm(h_ref[...], wide_ref[0])
            if index != 1:
                at = slice(index // 2 * width, (index // 2 + 1) * width)
                bias = jnp.concatenate([bias_ref[model : model + 1, at] for model in range(4)], axis=1)
                out = out + bias
            qkv_ref[...] = out.astype(low)


def project(where, spots, h, halves, bias, after):
    seq, depth = h.shape
    return pl.pallas_call(
        held_back(project_body, 8, len(after)),
        grid_spec=pltpu.PrefetchScalarGridSpec(
            num_scalar_prefetch=2,
            grid=(4,),
            in_specs=[
                whole((seq, depth)),
                *[whole(halves[0].shape)] * 4,
                whole(bias.shape),
            ]
            + [LATER] * len(after),
            out_specs=[
                pl.BlockSpec((seq, depth), lambda i, *_: (0, jnp.minimum(i, 2))),
                pl.BlockSpec((1, depth, depth), lambda i, *_: (i, 0, 0)),
            ],
        ),
        out_shape=[sds((seq, 3 * depth), low), sds((4, depth, depth), low)],
        compiler_params=params(60),
        cost_estimate=cost(2 * seq * depth * depth * 3, seq * depth * 16),
        name="project",
    )(where, spots, h, *halves, bias, *after)


def attend_out_body(o_ref, w_ref, x_ref, vec_ref, middle_ref, h_ref, ht_ref):
    middle = x_ref[...].astype(f32) + mm_nt(o_ref[...], w_ref[0]) + vec_ref[4:5, :]
    middle_ref[...] = middle.astype(low)
    unit, _ = normalize(middle)
    h = (unit * vec_ref[2:3, :] + vec_ref[3:4, :]).astype(low)
    h_ref[...] = h
    ht_ref[...] = h.T


def attend_out(o, wide, x, vectors):
    seq, depth = x.shape
    rows = pl.BlockSpec((TILE, depth), lambda i: (i, 0))
    turned = pl.BlockSpec((depth, TILE), lambda i: (0, i))
    return pl.pallas_call(
        attend_out_body,
        grid=(seq // TILE,),
        in_specs=[
            rows,
            pl.BlockSpec((1, depth, depth), lambda i: (3, 0, 0)),
            rows,
            whole(vectors.shape),
        ],
        out_specs=[rows, rows, turned],
        out_shape=[sds((seq, depth), low), sds((seq, depth), low), sds((depth, seq), low)],
        compiler_params=params(60),
        cost_estimate=cost(2 * seq * depth * depth, seq * depth * 14),
        name="attend_out",
    )(o, wide, x, vectors)


def feed_body(
    where_ref,
    spots_ref,
    h2_ref,
    h2t_ref,
    up_ref,
    upt_ref,
    mine_a,
    mine_b,
    twin_a,
    twin_b,
    bias_ref,
    middle_ref,
    vec_ref,
    block_ref,
    back_ref,
    keep_ref,
    send_ref,
    bias_grad_ref,
    out_ref,
    sum_ref,
    wide_ref,
    act_ref,
    pre_ref,
):
    step = pl.program_id(0)
    side = lax.rem(step, 2)
    models = [where_ref[1] ^ (2 * side + core) for core in range(2)]
    rows = mine_a.shape[1]
    part = mine_a.shape[2] // 2
    groups = wide_ref.shape[0] // rows

    @pl.when(step == 0)
    def _():
        out_ref[...] = middle_ref[...].astype(f32) + vec_ref[5:6, :]
        sum_ref[...] = jnp.zeros_like(sum_ref)

    for group in range(groups):
        at = slice(group * rows, (group + 1) * rows)
        own = slot((mine_a, mine_b), spots_ref[models[0], group], slice(None))
        other = slot((twin_a, twin_b), spots_ref[models[1], group], slice(None))
        wide_ref[at, :part] = own[:, :part]
        wide_ref[at, part : 2 * part] = other[:, :part]
        wide_ref[at, 2 * part : 3 * part] = own[:, part:]
        wide_ref[at, 3 * part :] = other[:, part:]

    expand = wide_ref[:, : 2 * part]
    shrink = wide_ref[:, 2 * part :]
    first = step // 2 * part
    skip = bias_ref.shape[1] - bias_grad_ref.shape[1]
    bias = jnp.concatenate(
        [bias_ref[pl.ds(model, 1), pl.ds(pl.multiple_of(skip + first, 128), part)] for model in models],
        axis=1,
    )
    sums = jnp.zeros((1, 2 * part), f32)
    for tile in range(h2_ref.shape[0] // TILE):
        at = slice(tile * TILE, (tile + 1) * TILE)
        u = mm(h2_ref[at, :], expand) + bias
        square = u * u
        th = jnp.tanh(u * (GELU_A + GELU_B * square))
        gate = 0.5 * th + 0.5
        slope = gate + (gate * (1.0 - gate)) * (u * (2.0 * GELU_A + (6.0 * GELU_B) * square))
        pre = (mm(up_ref[at, :], shrink) * slope).astype(low)
        act_ref[at, :] = (u * gate).astype(low)
        pre_ref[at, :] = pre
        sums = sums + columns_of(pre.astype(f32))
    for core, model in enumerate(models):
        bias_grad_ref[pl.ds(model, 1), pl.ds(pl.multiple_of(first, 128), part)] = sums[
            :, core * part : (core + 1) * part
        ]
    out_ref[...] += mm_nt(act_ref[...], shrink)
    sum_ref[...] += mm_nt(pre_ref[...], expand)
    grad_expand = mm(h2t_ref[...], pre_ref[...]).astype(low)
    grad_shrink = mm(upt_ref[...], act_ref[...]).astype(low)
    for group in range(groups):
        at = slice(group * rows, (group + 1) * rows)
        own, other = spots_ref[models[0], group], spots_ref[models[1], group]
        keep_ref[own, :, :part] = grad_expand[at, :part]
        keep_ref[own, :, part:] = grad_shrink[at, :part]
        send_ref[other, :, :part] = grad_expand[at, part:]
        send_ref[other, :, part:] = grad_shrink[at, part:]

    @pl.when(step == pl.num_programs(0) - 1)
    def _():
        block_ref[...] = out_ref[...].astype(low)
        back_ref[...] = sum_ref[...].astype(low)


def feed(where, spots, h2, h2t, up, upt, halves, bias, middle, vectors):
    seq, depth = h2.shape
    half, rows, columns = halves[0].shape
    steps, part = 6, columns // 6
    half_piece = pl.BlockSpec((half, rows, 2 * part), lambda i, *_: (0, 0, i // 2))
    piece = pl.BlockSpec((2 * half, rows, 2 * part), lambda i, *_: (0, 0, i // 2))
    return pl.pallas_call(
        feed_body,
        grid_spec=pltpu.PrefetchScalarGridSpec(
            num_scalar_prefetch=2,
            grid=(steps,),
            in_specs=[
                whole((seq, depth)),
                whole((depth, seq)),
                whole((seq, depth)),
                whole((depth, seq)),
                *[half_piece] * 4,
                whole(bias.shape),
                whole((seq, depth)),
                whole(vectors.shape),
            ],
            out_specs=[whole((seq, depth)), whole((seq, depth)), piece, piece, whole((4, 3 * part))],
            scratch_shapes=[
                pltpu.VMEM((seq, depth), f32),
                pltpu.VMEM((seq, depth), f32),
                pltpu.VMEM((depth, 4 * part), low),
                pltpu.VMEM((seq, 2 * part), low),
                pltpu.VMEM((seq, 2 * part), low),
            ],
        ),
        out_shape=[sds((seq, depth), low)] * 2
        + [sds((2 * half, rows, columns), low)] * 2
        + [sds((4, 3 * part), f32)],
        compiler_params=params(60),
        cost_estimate=cost(12 * seq * depth * steps * 2 * part, seq * depth * 40, seq * steps * part),
        name="feed",
    )(where, spots, h2, h2t, up, upt, *halves, bias, middle, vectors)


def middle_back_body(
    where_ref,
    lengths_ref,
    back_ref,
    middle_ref,
    up_ref,
    o_ref,
    w_ref,
    vec_ref,
    grad_ref,
    mixture_ref,
    weight_ref,
    sums_ref,
    total_ref,
):
    step = pl.program_id(0)
    unit, inverse = normalize(middle_ref[...].astype(f32))
    back = back_ref[...].astype(f32)
    up = up_ref[...].astype(f32)
    grad = up + pull_norm(back * vec_ref[2:3, :], unit, inverse)
    rounded = grad.astype(low)
    grad_ref[...] = rounded
    row = step * grad.shape[0] + lax.broadcasted_iota(jnp.int32, grad.shape, 0)
    length = lengths_ref[where_ref[2]]
    mixture_ref[...] = jnp.where(row < length, mm(rounded, w_ref[0]), 0.0).astype(low)
    share = mm(rounded.T, o_ref[...])
    sums = jnp.concatenate(
        [columns_of(back * unit), columns_of(back), columns_of(grad), columns_of(up)], axis=0
    )

    @pl.when(step == 0)
    def _():
        total_ref[...] = share
        sums_ref[...] = sums

    @pl.when(step > 0)
    def _():
        total_ref[...] += share
        sums_ref[...] += sums

    @pl.when(step == pl.num_programs(0) - 1)
    def _():
        weight_ref[...] = total_ref[...].astype(low)


def middle_back(where, lengths, back, middle, up, o, wide, vectors):
    seq, depth = middle.shape
    rows = pl.BlockSpec((2 * TILE, depth), lambda i, *_: (i, 0))
    return pl.pallas_call(
        middle_back_body,
        grid_spec=pltpu.PrefetchScalarGridSpec(
            num_scalar_prefetch=2,
            grid=(seq // (2 * TILE),),
            in_specs=[
                rows,
                rows,
                rows,
                rows,
                pl.BlockSpec((1, depth, depth), lambda i, *_: (3, 0, 0)),
                whole(vectors.shape),
            ],
            out_specs=[rows, rows, whole((depth, depth)), whole((4, depth))],
            scratch_shapes=[pltpu.VMEM((depth, depth), f32)],
        ),
        out_shape=[
            sds((seq, depth), low),
            sds((seq, depth), low),
            sds((depth, depth), low),
            sds((4, depth), f32),
        ],
        compiler_params=params(60),
        cost_estimate=cost(4 * seq * depth * depth, seq * depth * 28),
        name="middle_back",
    )(where, lengths, back, middle, up, o, wide, vectors)


def input_grad_body(where_ref, spots_ref, ht_ref, back_ref, out_grad_ref, keep_ref, send_ref, sums_ref):
    part = pl.program_id(0)
    rows = keep_ref.shape[1]
    width = keep_ref.shape[2] // 4
    groups = ht_ref.shape[0] // rows

    def spread(targets, index, grad):
        at = slice(index * width, (index + 1) * width)
        for group in range(groups):
            for model in range(4):
                targets[model % 2][spots_ref[model, group], :, at] = grad[
                    group * rows : (group + 1) * rows, model * width : (model + 1) * width
                ]

    for index in range(4):

        @pl.when(part == index)
        def _(index=index):
            if index < 3:
                sums_ref[0] = columns_of(back_ref[0].astype(f32))
                grad = mm(ht_ref[...], back_ref[0]).astype(low)
            else:
                grad = out_grad_ref[...]
            for core in range(2):

                @pl.when(where_ref[0] == core)
                def _(core=core):
                    spread((keep_ref, send_ref) if core == 0 else (send_ref, keep_ref), index, grad)


def input_grad(where, spots, ht, back, out_grad, slots, rows, after):
    depth, seq = ht.shape
    shape = (slots, rows, 4 * (depth // 4))
    return pl.pallas_call(
        held_back(input_grad_body, 5, len(after)),
        grid_spec=pltpu.PrefetchScalarGridSpec(
            num_scalar_prefetch=2,
            grid=(4,),
            in_specs=[
                whole((depth, seq)),
                pl.BlockSpec((1, seq, depth), lambda i, *_: (jnp.minimum(i, 2), 0, 0)),
                whole((depth, depth)),
            ]
            + [LATER] * len(after),
            out_specs=[
                whole(shape),
                whole(shape),
                pl.BlockSpec((1, 1, depth), lambda i, *_: (jnp.minimum(i, 2), 0, 0)),
            ],
        ),
        out_shape=[sds(shape, low), sds(shape, low), sds((3, 1, depth), f32)],
        compiler_params=params(60),
        cost_estimate=cost(6 * seq * depth * depth, seq * depth * 14),
        name="input_grad",
    )(where, spots, ht, back, out_grad, *after)


def token_back_body(
    back_ref, w_ref, x_ref, grad_ref, vec_ref, middle_ref, head_ref, bias_ref, token_ref, sums_ref
):
    step = pl.program_id(0)
    back = mm_nt(back_ref[0], w_ref[0]) + mm_nt(back_ref[1], w_ref[1]) + mm_nt(back_ref[2], w_ref[2])
    unit, inverse = normalize(x_ref[...].astype(f32))
    grad = grad_ref[...].astype(f32)
    token_ref[...] = (grad + pull_norm(back * vec_ref[0:1, :], unit, inverse)).astype(low)
    sums = jnp.concatenate([columns_of(back * unit), columns_of(back)], axis=0)

    @pl.when(step == 0)
    def _():
        sums_ref[:2] = sums
        sums_ref[2:6] = middle_ref[...]
        sums_ref[6:7] = head_ref[0]
        sums_ref[7:8] = head_ref[2]
        sums_ref[8:] = bias_ref[...]

    @pl.when(step > 0)
    def _():
        sums_ref[:2] += sums


def token_back(back, wide, x, grad, vectors, sums, after):
    seq, depth = x.shape
    rows = pl.BlockSpec((TILE, depth), lambda i: (i, 0))
    return pl.pallas_call(
        held_back(token_back_body, 8, len(after)),
        grid=(seq // TILE,),
        in_specs=[
            pl.BlockSpec((3, TILE, depth), lambda i: (0, i, 0)),
            pl.BlockSpec((3, depth, depth), lambda i: (0, 0, 0)),
            rows,
            rows,
            whole(vectors.shape),
            *[whole(array.shape) for array in sums],
        ]
        + [LATER] * len(after),
        out_specs=[rows, whole((12, depth))],
        out_shape=[sds((seq, depth), low), sds((12, depth), f32)],
        compiler_params=params(60),
        cost_estimate=cost(6 * seq * depth * depth, seq * depth * 16),
        name="token_back",
    )(back, wide, x, grad, vectors, *sums, *after)


CORE_ORDERS = ((4, 3, 2, 1), (3, 4, 1, 2))
STAGES = 4


def cube_permute(values, stage):
    pairs = [(device, device ^ (1 << CORE_ORDERS[device & 1][stage])) for device in range(32)]
    return lax.ppermute(values, ("dp", "mp"), pairs)


def bit_permute(values, bit):
    return lax.ppermute(values, ("dp", "mp"), [(device, device ^ (1 << bit)) for device in range(32)])


def place(distance, core):
    spots = [
        sum(((distance >> bit) & 1) << step for step, bit in enumerate(order)) for order in CORE_ORDERS
    ]
    return jnp.where(core == 0, spots[0], spots[1])


def joined(held, arrived):
    return jnp.concatenate([held, arrived], axis=0)


def leaving(parts, stage):
    half = 1 << stage
    return sum(part[half:].astype(f32) for part in parts).astype(low)


def staying(parts, stage):
    return [part[: 1 << stage] for part in parts]


def summed(parts):
    return sum(part[0].astype(f32) for part in parts)


def cube_sum(values, bits=range(5)):
    for bit in bits:
        values = values + bit_permute(values, bit)
    return values


def adam_parts(weight, gradient, first_old, second_old, factor, step_rate):
    scaled = gradient * factor
    moment = beta_one * first_old + (1.0 - beta_one) * scaled
    square = beta_two * second_old + (1.0 - beta_two) * scaled * scaled
    spread = jnp.sqrt(square * (1.0 / (1.0 - beta_two**STEP)))
    ratio = moment * (1.0 / (1.0 - beta_one**STEP)) / (spread + adam_eps)
    return moment, square, weight - step_rate * (ratio + decay * weight)


def optimize_body(owned_ref, vector_ref, attend_ref, feed_ref, *refs):
    state, outs = refs[:15], refs[15:]
    vectors = vector_ref[...]
    total = owned_ref[0:1, 0:1] + jnp.sum(vectors * vectors)
    norm = jnp.sqrt(total)
    factor = clip_norm / jnp.maximum(norm, clip_norm)
    outs[0][...] = norm
    outs[1][...] = factor
    width = state[0].shape[2]
    part = state[6].shape[1] // 3

    def update(param, at, gradient, step_rate):
        weight, first, second = (ref[at] for ref in state[3 * param : 3 * param + 3])
        results = adam_parts(weight, gradient, first, second, factor, step_rate)
        for ref, result in zip(outs[2 + 3 * param : 5 + 3 * param], results):
            ref[at] = result

    for index in range(3):
        update(0, (index,), attend_ref[:, index * width : (index + 1) * width], rate)
    update(1, (...,), attend_ref[:, 3 * width :].T, rate)
    for index in range(3):
        at = (slice(None), slice(index * part, (index + 1) * part))
        first = 2 * index * part
        update(2, at, feed_ref[:, first : first + part], rate)
        update(3, at, feed_ref[:, first + part : first + 2 * part], rate)
    update(4, (...,), vectors[:6], vector_rate)


def optimize(owned, vector_total, attend_total, feed_total, state):
    shapes = [sds(group[0].shape, f32) for group in state for _ in range(3)]
    return pl.pallas_call(
        optimize_body,
        out_shape=[sds((1, 1), f32), sds((1, 1), f32)] + shapes,
        compiler_params=params(60),
        cost_estimate=cost(4e6, 8e6),
        name="optimize",
    )(owned, vector_total, attend_total, feed_total, *[array for group in state for array in group])


def shards(
    tokens,
    cotangent,
    lengths,
    input_weight,
    output_weight,
    expand_weight,
    shrink_weight,
    layer_vectors,
    head_bias,
    expand_bias,
    first_input,
    first_output,
    first_expand,
    first_shrink,
    first_vectors,
    first_head,
    first_bias,
    second_input,
    second_output,
    second_expand,
    second_shrink,
    second_vectors,
    second_head,
    second_bias,
):
    dp_count = lax.axis_size("dp")
    mp_count = lax.axis_size("mp")
    cube = dp_count == 8 and mp_count == 4
    rows = input_weight.shape[0]
    width = input_weight.shape[2]
    hidden = expand_weight.shape[1]
    seq, depth = tokens.shape
    part = hidden // 3
    model_index = lax.axis_index("mp")
    me = lax.axis_index("dp") * mp_count + model_index

    attend_shard, feed_shard = pack(
        input_weight.transpose(1, 0, 2), output_weight, expand_weight, shrink_weight.T
    )
    bias_shard = jnp.concatenate([head_bias.reshape(1, 2 * width), expand_bias[None]], axis=1)

    bias_full = jnp.where(jnp.arange(4)[:, None] == model_index, bias_shard, 0.0)
    if cube:
        core, near = me & 1, model_index
        devices = jnp.arange(32).reshape(8, 4).T
        spots = place(devices ^ me, devices & 1).astype(jnp.int32)
    else:
        core = near = jnp.zeros((), jnp.int32)
        spots = (jnp.arange(4)[:, None] // 2 * 8 + jnp.arange(8)[None]).astype(jnp.int32)
    where = jnp.stack([core, near, model_index]).astype(jnp.int32)

    if cube:
        held = attend_shard[None]
        arrived = cube_permute(held, 0)
        bias_full = bias_full + bit_permute(bias_full, 0)
        held = joined(held, arrived)
        arrived = cube_permute(held, 1)
        normed, normed_t, upstream_t = prepare(tokens, cotangent, layer_vectors, (held,))
        bias_full = bias_full + bit_permute(bias_full, 1)
        held, feed_shard, normed, bias_full, spots, where = lax.optimization_barrier(
            (held, feed_shard, normed, bias_full, spots, where)
        )
        held = joined(held, arrived)
        feed_held = feed_shard[None]
        arrived, far_feed = cube_permute(held, 2), cube_permute(feed_held, 0)
        held = joined(held, arrived)
        feed_held = joined(feed_held, far_feed)
        held, feed_held = lax.optimization_barrier((held, feed_held))
        far, far_feed = cube_permute(held, 3), cube_permute(feed_held, 1)
        twin = bit_permute(held, 0)
        feed_held = joined(feed_held, far_feed)
        far, feed_held = lax.optimization_barrier((far, feed_held))
        attend_halves = (held, far, twin, bit_permute(far, 0))
        arrived = cube_permute(feed_held, 2)
        qkv, wide = project(where, spots, normed, attend_halves, bias_full, ())
        feed_held, qkv = lax.optimization_barrier((feed_held, qkv))
        feed_held = joined(feed_held, arrived)
        far, twin = cube_permute(feed_held, 3), bit_permute(feed_held, 0)
        mixture, log_totals = attend_forward(where, lengths, qkv, (feed_held,))
        middle, hidden_in, hidden_t = attend_out(mixture, wide, tokens, layer_vectors)
        far, hidden_in = lax.optimization_barrier((far, hidden_in))
        feed_halves = (feed_held, far, twin, bit_permute(far, 0))
    else:

        def planes(shard):
            full = lax.all_gather(lax.all_gather(shard, "dp", axis=0, tiled=True), "mp", axis=0)
            full = full.reshape(2, 2, 8, depth // 8, shard.shape[1]).transpose(1, 0, 2, 3, 4)
            return tuple(full.reshape(4, 8, depth // 8, shard.shape[1]))

        normed, normed_t, upstream_t = prepare(tokens, cotangent, layer_vectors, ())
        bias_full = lax.psum(bias_full, "mp")
        qkv, wide = project(where, spots, normed, planes(attend_shard), bias_full, ())
        mixture, log_totals = attend_forward(where, lengths, qkv, ())
        middle, hidden_in, hidden_t = attend_out(mixture, wide, tokens, layer_vectors)
        feed_halves = planes(feed_shard)
    block_out, back, keep_feed, send_feed, bias_grad = feed(
        where,
        spots,
        hidden_in,
        hidden_t,
        cotangent,
        upstream_t,
        feed_halves,
        bias_full,
        middle,
        layer_vectors,
    )
    middle_grad, mixture_grad, output_grad, middle_sums = middle_back(
        where, lengths, back, middle, cotangent, mixture, wide, layer_vectors
    )
    if cube:
        feed_parts = [keep_feed, bit_permute(send_feed, 0)]
        keep_feed, mixture_grad = lax.optimization_barrier((keep_feed, mixture_grad))
        feed_parts[0] = keep_feed
        away = leaving(feed_parts, 3)
        packed_grad = attend_backward(where, lengths, qkv, mixture_grad, log_totals, (away,))
        feed_parts = staying(feed_parts, 3) + [cube_permute(away, 3)]
        feed_parts[0], packed_grad = lax.optimization_barrier((feed_parts[0], packed_grad))
        away = leaving(feed_parts, 2)
        keep_attend, send_attend, head_sums = input_grad(
            where, spots, normed_t, packed_grad, output_grad, 16, depth // 8, (away,)
        )
        feed_parts = staying(feed_parts, 2) + [cube_permute(away, 2)]
        feed_parts[-1], send_attend = lax.optimization_barrier((feed_parts[-1], send_attend))
        attend_parts = [keep_attend, bit_permute(send_attend, 0)]
        away, feed_away = leaving(attend_parts, 3), leaving(feed_parts, 1)
        token_grad, vector_total = token_back(
            packed_grad,
            wide,
            tokens,
            middle_grad,
            layer_vectors,
            (middle_sums, head_sums, bias_grad),
            (away, feed_away),
        )
    else:
        packed_grad = attend_backward(where, lengths, qkv, mixture_grad, log_totals, ())
        keep_attend, send_attend, head_sums = input_grad(
            where, spots, normed_t, packed_grad, output_grad, 16, depth // 8, ()
        )
        token_grad, vector_total = token_back(
            packed_grad,
            wide,
            tokens,
            middle_grad,
            layer_vectors,
            (middle_sums, head_sums, bias_grad),
            (),
        )

    if cube:
        attend_parts = staying(attend_parts, 3) + [cube_permute(away, 3)]
        feed_parts = staying(feed_parts, 1) + [cube_permute(feed_away, 1)]
        attend_parts[0], vector_total = lax.optimization_barrier((attend_parts[0], vector_total))
        away, feed_away = leaving(attend_parts, 2), leaving(feed_parts, 0)
        attend_parts = staying(attend_parts, 2) + [cube_permute(away, 2)]
        feed_parts = staying(feed_parts, 0) + [cube_permute(feed_away, 0)]
        away, vector_total = lax.optimization_barrier((away, vector_total))
        vector_total = cube_sum(vector_total, (0, 1))
        attend_parts[0], vector_total = lax.optimization_barrier((attend_parts[0], vector_total))
        away = leaving(attend_parts, 1)
        attend_parts = staying(attend_parts, 1) + [cube_permute(away, 1)]
        away, vector_total = lax.optimization_barrier((away, vector_total))
        vector_total = cube_sum(vector_total, (2, 3))
        feed_total = summed(feed_parts)
        feed_squares = jnp.sum(feed_total * feed_total)
        attend_parts[0], vector_total, feed_squares = lax.optimization_barrier(
            (attend_parts[0], vector_total, feed_squares)
        )
        away = leaving(attend_parts, 0)
        attend_parts = staying(attend_parts, 0) + [cube_permute(away, 0)]
        away, vector_total = lax.optimization_barrier((away, vector_total))
        vector_total = cube_sum(vector_total, (4,))
        attend_total = summed(attend_parts)
    else:

        def own_block(keep, send):
            full = jnp.stack([keep, send]).reshape(2, 2, 8, depth // 8, keep.shape[2])
            full = full.transpose(1, 0, 2, 3, 4).reshape(4, depth, keep.shape[2])
            full = lax.psum_scatter(full, "mp", scatter_dimension=0, tiled=False)
            return lax.psum_scatter(full, "dp", scatter_dimension=0, tiled=True).astype(f32)

        attend_total = own_block(keep_attend, send_attend)
        feed_total = own_block(keep_feed, send_feed)
        vector_total = lax.psum(vector_total, ("dp", "mp"))
        feed_squares = jnp.sum(feed_total * feed_total)
    owned = jnp.full((8, 128), jnp.sum(attend_total * attend_total) + feed_squares, f32)
    owned = cube_sum(owned) if cube else lax.psum(owned, ("dp", "mp"))
    head_total = lax.dynamic_slice_in_dim(vector_total[6:8], model_index * width, width, 1)
    bias_total = lax.dynamic_slice_in_dim(vector_total[8:].reshape(-1), model_index * hidden, hidden, 0)

    def turned(array):
        return array.transpose(1, 0, 2)

    state = (
        (turned(input_weight), turned(first_input), turned(second_input)),
        (output_weight, first_output, second_output),
        (expand_weight, first_expand, second_expand),
        (shrink_weight.T, first_shrink.T, second_shrink.T),
        (layer_vectors, first_vectors, second_vectors),
    )
    grad_norm, factor, *updates = optimize(owned, vector_total, attend_total, feed_total, state)
    grad_norm, factor = grad_norm[0, 0], factor[0, 0]
    moment_input, square_input, updated_input = (turned(array) for array in updates[:3])
    moment_output, square_output, updated_output = updates[3:6]
    moment_expand, square_expand, updated_expand = updates[6:9]
    moment_shrink, square_shrink, updated_shrink = (array.T for array in updates[9:12])
    moment_vectors, square_vectors, updated_vectors = updates[12:]
    moment_head, square_head, updated_head = adam_parts(
        head_bias, head_total, first_head, second_head, factor, vector_rate
    )
    moment_bias, square_bias, updated_bias = adam_parts(
        expand_bias, bias_total, first_bias, second_bias, factor, vector_rate
    )
    return (
        block_out,
        token_grad,
        grad_norm,
        moment_input,
        square_input,
        updated_input,
        moment_output,
        square_output,
        updated_output,
        moment_expand,
        square_expand,
        updated_expand,
        moment_shrink,
        square_shrink,
        updated_shrink,
        moment_vectors,
        square_vectors,
        updated_vectors,
        moment_head,
        square_head,
        updated_head,
        moment_bias,
        square_bias,
        updated_bias,
    )


def solution(mesh):
    in_specs = (
        P(("dp", "mp"), None),
        P(("dp", "mp"), None),
        P("dp"),
        P("dp", None, "mp"),
        P("mp", "dp"),
        P("dp", "mp"),
        P("mp", "dp"),
        P(),
        P(None, "mp"),
        P("mp"),
        P("dp", None, "mp"),
        P("mp", "dp"),
        P("dp", "mp"),
        P("mp", "dp"),
        P(),
        P(None, "mp"),
        P("mp"),
        P("dp", None, "mp"),
        P("mp", "dp"),
        P("dp", "mp"),
        P("mp", "dp"),
        P(),
        P(None, "mp"),
        P("mp"),
    )
    out_specs = (
        P(("dp", "mp"), None),
        P(("dp", "mp"), None),
        P(),
        P("dp", None, "mp"),
        P("dp", None, "mp"),
        P("dp", None, "mp"),
        P("mp", "dp"),
        P("mp", "dp"),
        P("mp", "dp"),
        P("dp", "mp"),
        P("dp", "mp"),
        P("dp", "mp"),
        P("mp", "dp"),
        P("mp", "dp"),
        P("mp", "dp"),
        P(),
        P(),
        P(),
        P(None, "mp"),
        P(None, "mp"),
        P(None, "mp"),
        P("mp"),
        P("mp"),
        P("mp"),
    )
    return jax.shard_map(shards, mesh=mesh, in_specs=in_specs, out_specs=out_specs, check_vma=False)
```

```python
import functools
import jax
import jax.numpy as jnp
from jax import lax
from jax.experimental import pallas as pl
from jax.experimental.pallas import tpu as pltpu
from jax.sharding import PartitionSpec as P

HEAD_DIM = 64
TILE = 256
STEP = 10

eps_norm = 1e-05
clip_norm = 1.0
beta_one = 0.9
beta_two = 0.999
adam_eps = 1e-08
rate = 0.05
vector_rate = 0.5
decay = 0.01
excluded = -1e30
low = jnp.bfloat16
f32 = jnp.float32
GELU_A = 0.7978845608028654
GELU_B = GELU_A * 0.044715


def params(limit_mib, **kw):
    return pltpu.CompilerParams(vmem_limit_bytes=limit_mib * 1024 * 1024, **kw)


def cost(flops, moved, special=0):
    return pl.CostEstimate(flops=int(flops), bytes_accessed=int(moved), transcendentals=int(special))


def mm(a, b):
    return jnp.dot(a, b, preferred_element_type=f32)


def mm_nt(a, b):
    return lax.dot_general(a, b, (((1,), (1,)), ((), ())), preferred_element_type=f32)


def whole(shape):
    zeros = (0,) * len(shape)
    return pl.BlockSpec(shape, lambda *_: zeros)


def once(shape):
    zeros = (0,) * len(shape)
    return pl.BlockSpec(shape, lambda *_: zeros, pipeline_mode=pl.Buffered(1))


def held_back(body, first, count):
    def run(*refs):
        return body(*refs[:first], *refs[first + count :])

    return run


LATER = pl.BlockSpec(memory_space=pl.ANY)


def far_away(shape, dtype):
    return pltpu.HBM(shape, dtype)


def from_far(*arrays):
    return [pltpu.with_memory_space_constraint(array, pltpu.HBM) for array in arrays]


def sds(shape, dtype):
    return jax.ShapeDtypeStruct(shape, dtype)


def live_blocks(length, count, body):
    for blocks in range(1, count + 1):
        low_end = (blocks - 1) * TILE
        high_end = blocks * TILE
        @pl.when((length > low_end) & (length <= high_end))
        def _(blocks=blocks):
            body(length, blocks)


PAIR = 2 * HEAD_DIM


def span(block):
    return slice(block * TILE, (block + 1) * TILE)


def both_heads(values):
    lane = lax.broadcasted_iota(jnp.int32, values.shape, 1)
    none = jnp.zeros_like(values)
    return jnp.concatenate(
        [jnp.where(lane < HEAD_DIM, values, none), jnp.where(lane >= HEAD_DIM, values, none)], axis=0
    )


def causal_mask():
    key_id = lax.broadcasted_iota(jnp.int32, (TILE, 2 * TILE), 0)
    query_id = lax.broadcasted_iota(jnp.int32, (TILE, 2 * TILE), 1) & (TILE - 1)
    return key_id <= query_id


def forward_body(where_ref, lengths_ref, q_ref, k_ref, v_ref, o_ref, lse_ref, vt_ref):
    seq = q_ref.shape[0]
    vt_ref[...] = v_ref[...].T
    causal = causal_mask()

    def run(length, blocks):
        def scores(b):
            q = q_ref[span(b), :] * jnp.asarray(HEAD_DIM**-0.5, low)
            return mm_nt(k_ref[: (b + 1) * TILE, :], both_heads(q))

        now = scores(0)
        for b in range(blocks):
            start, stop = b * TILE, (b + 1) * TILE
            later = scores(b + 1) if b + 1 < blocks else None
            last = jnp.where(causal, now[start:, :], excluded)
            top = jnp.max(last, axis=0, keepdims=True)
            if b:
                top = jnp.maximum(top, jnp.max(now[:start], axis=0, keepdims=True))
            p = jnp.exp(last - top)
            total = jnp.sum(p, axis=0, keepdims=True)
            pb = p.astype(low)
            if b:
                pf = jnp.exp(now[:start] - top)
                total = total + jnp.sum(pf, axis=0, keepdims=True)
                pb = jnp.concatenate([pf.astype(low), pb], axis=0)
            inverse = 1.0 / total
            lse = top + jnp.log(total)
            outs = []
            for h in range(2):
                at = slice(h * TILE, (h + 1) * TILE)
                out = mm(vt_ref[h * HEAD_DIM : (h + 1) * HEAD_DIM, :stop], pb[:, at])
                outs.append(out * inverse[:, at])
                lse_ref[0, h : h + 1, start:stop] = lse[:, at]
            both = jnp.concatenate(outs, axis=0).T
            row = start + lax.broadcasted_iota(jnp.int32, both.shape, 0)
            o_ref[start:stop, :] = jnp.where(row < length, both, 0.0).astype(low)
            now = later
        if blocks * TILE < seq:
            o_ref[blocks * TILE :, :] = jnp.zeros((seq - blocks * TILE, PAIR), low)
            lse_ref[0, :, blocks * TILE :] = jnp.zeros((2, seq - blocks * TILE), f32)

    live_blocks(lengths_ref[where_ref[2]], seq // TILE, run)


def attend_forward(where, lengths, qkv, after):
    seq, width = qkv.shape[0], qkv.shape[1] // 3
    pair = 2 * HEAD_DIM
    pairs = width // pair
    half = seq * seq * 5 // 8
    spec = lambda part: pl.BlockSpec((seq, pair), lambda i, *_: (0, part * pairs + i))
    return pl.pallas_call(
        held_back(forward_body, 5, len(after)),
        grid_spec=pltpu.PrefetchScalarGridSpec(
            num_scalar_prefetch=2,
            grid=(pairs,),
            in_specs=[spec(0), spec(1), spec(2)] + [LATER] * len(after),
            out_specs=[
                pl.BlockSpec((seq, pair), lambda i, *_: (0, i)),
                pl.BlockSpec((1, 2, seq), lambda i, *_: (i, 0, 0)),
            ],
            scratch_shapes=[pltpu.VMEM((pair, seq), low)],
        ),
        out_shape=[sds((seq, width), low), far_away((pairs, 2, seq), f32)],
        compiler_params=params(20),
        cost_estimate=cost(pairs * 2 * half * 2 * 2 * 256, seq * width * 8, pairs * 2 * half),
        name="attend_forward",
    )(where, lengths, *from_far(qkv, qkv, qkv), *after)


def backward_body(where_ref, lengths_ref, q_ref, k_ref, v_ref, do_ref, lse_ref, out_ref, kt_ref, ksum, vsum):
    seq = q_ref.shape[0]
    scale = HEAD_DIM**-0.5
    kt_ref[...] = k_ref[...].T
    causal = causal_mask()

    def run(length, blocks):
        def scores(b):
            qq = both_heads(q_ref[span(b), :] * jnp.asarray(scale, low))
            uu = both_heads(do_ref[span(b), :])
            stop = (b + 1) * TILE
            return qq, uu, mm_nt(k_ref[:stop, :], qq), mm_nt(v_ref[:stop, :], uu)

        now = scores(blocks - 1)
        for b in reversed(range(blocks)):
            start, stop = b * TILE, (b + 1) * TILE
            later = scores(b - 1) if b else None
            qq, uu, s, dp = now
            lse = jnp.concatenate([lse_ref[0, 0:1, start:stop], lse_ref[0, 1:2, start:stop]], axis=1)
            p = jnp.exp(jnp.where(causal, s[start:], excluded) - lse)
            inner = jnp.sum(p * dp[start:], axis=0, keepdims=True)
            if b:
                pf = jnp.exp(s[:start] - lse)
                inner = inner + jnp.sum(pf * dp[:start], axis=0, keepdims=True)
            ds = (p * (dp[start:] - inner)).astype(low)
            pb = p.astype(low)
            if b:
                ds = jnp.concatenate([(pf * (dp[:start] - inner)).astype(low), ds], axis=0)
                pb = jnp.concatenate([pf.astype(low), pb], axis=0)
            dk, dv = mm(ds, qq), mm(pb, uu)
            if b == blocks - 1:
                ksum[:stop, :] = dk
                vsum[:stop, :] = dv
            else:
                ksum[:stop, :] += dk
                vsum[:stop, :] += dv
            dq = jnp.concatenate(
                [
                    mm(
                        kt_ref[h * HEAD_DIM : (h + 1) * HEAD_DIM, :stop],
                        ds[:, h * TILE : (h + 1) * TILE],
                    )
                    for h in range(2)
                ],
                axis=0,
            )
            out_ref[1, start:stop, :] = ksum[start:stop, :].astype(low)
            out_ref[2, start:stop, :] = vsum[start:stop, :].astype(low)
            out_ref[0, start:stop, :] = (dq.T * scale).astype(low)
            now = later
        if blocks * TILE < seq:
            rest = jnp.zeros((seq - blocks * TILE, PAIR), low)
            for part in range(3):
                out_ref[part, blocks * TILE :, :] = rest

    live_blocks(lengths_ref[where_ref[2]], seq // TILE, run)


def attend_backward(where, lengths, qkv, upstream, lse, after):
    seq, width = upstream.shape
    pair = 2 * HEAD_DIM
    pairs = width // pair
    half = seq * seq * 5 // 8
    spec = lambda part: pl.BlockSpec((seq, pair), lambda i, *_: (0, part * pairs + i))
    own = pl.BlockSpec((seq, pair), lambda i, *_: (0, i))
    return pl.pallas_call(
        held_back(backward_body, 7, len(after)),
        grid_spec=pltpu.PrefetchScalarGridSpec(
            num_scalar_prefetch=2,
            grid=(pairs,),
            in_specs=[spec(0), spec(1), spec(2), own, pl.BlockSpec((1, 2, seq), lambda i, *_: (i, 0, 0))]
            + [LATER] * len(after),
            out_specs=pl.BlockSpec((3, seq, pair), lambda i, *_: (0, 0, i)),
            scratch_shapes=[
                pltpu.VMEM((pair, seq), low),
                pltpu.VMEM((seq, pair), f32),
                pltpu.VMEM((seq, pair), f32),
            ],
        ),
        out_shape=sds((3, seq, width), low),
        compiler_params=params(28),
        cost_estimate=cost(pairs * 2 * half * 5 * 2 * 256, seq * width * 14, pairs * 2 * half),
        name="attend_backward",
    )(where, lengths, *from_far(qkv, qkv, qkv), upstream, *from_far(lse), *after)


def normalize(values):
    average = jnp.mean(values, axis=-1, keepdims=True)
    centred = values - average
    inverse = lax.rsqrt(jnp.mean(centred * centred, axis=-1, keepdims=True) + eps_norm)
    return centred * inverse, inverse


def pull_norm(scaled, unit, inverse):
    first = jnp.mean(scaled, axis=-1, keepdims=True)
    second = jnp.mean(scaled * unit, axis=-1, keepdims=True)
    return inverse * (scaled - first - unit * second)


def columns_of(values):
    return jnp.sum(values, axis=0, keepdims=True)


def pack_body(input_ref, output_ref, expand_ref, shrink_ref, attend_ref, feed_ref):
    width = input_ref.shape[2]
    part = expand_ref.shape[1] // 3
    for index in range(3):
        attend_ref[:, index * width : (index + 1) * width] = input_ref[index].astype(low)
        at = slice(index * part, (index + 1) * part)
        feed_ref[:, 2 * index * part : (2 * index + 1) * part] = expand_ref[:, at].astype(low)
        feed_ref[:, (2 * index + 1) * part : (2 * index + 2) * part] = shrink_ref[:, at].astype(low)
    attend_ref[:, 3 * width :] = output_ref[...].T.astype(low)


def pack(input_weight, output_weight, expand, shrink):
    rows, width = input_weight.shape[1:]
    hidden = expand.shape[1]
    return pl.pallas_call(
        pack_body,
        out_shape=[sds((rows, 4 * width), low), sds((rows, 2 * hidden), low)],
        compiler_params=params(6),
        cost_estimate=cost(rows * hidden, rows * hidden * 18),
        name="pack",
    )(*from_far(input_weight, output_weight, expand, shrink))


def prepare_body(x_ref, up_ref, vec_ref, h_ref, ht_ref, upt_ref):
    unit, _ = normalize(x_ref[...].astype(f32))
    h = (unit * vec_ref[0:1, :] + vec_ref[1:2, :]).astype(low)
    h_ref[...] = h
    ht_ref[...] = h.T
    upt_ref[...] = up_ref[...].T


def prepare(x, up, vectors, after):
    seq, depth = x.shape
    rows = pl.BlockSpec((2 * TILE, depth), lambda i: (i, 0))
    turned = pl.BlockSpec((depth, 2 * TILE), lambda i: (0, i))
    return pl.pallas_call(
        held_back(prepare_body, 3, len(after)),
        grid=(seq // (2 * TILE),),
        in_specs=[rows, rows, once(vectors.shape)] + [LATER] * len(after),
        out_specs=[rows, turned, turned],
        out_shape=[sds((seq, depth), low), far_away((depth, seq), low), far_away((depth, seq), low)],
        compiler_params=params(16),
        cost_estimate=cost(seq * depth * 10, seq * depth * 10),
        name="prepare",
    )(*from_far(x, up), vectors, *after)


def slot(halves, spot, at):
    first, second = halves
    inner = spot & 7
    return jnp.where(spot < 8, first[inner, :, at], second[inner, :, at])


def project_body(
    where_ref, spots_ref, h_ref, mine_a, mine_b, twin_a, twin_b, bias_ref, qkv_ref, wide_ref
):
    part = pl.program_id(0)
    rows = mine_a.shape[1]
    width = mine_a.shape[2] // 4
    groups = wide_ref.shape[1] // rows

    def collect(sources, index):
        at = slice(index * width, (index + 1) * width)
        for group in range(groups):
            pieces = [slot(sources[model % 2], spots_ref[model, group], at) for model in range(4)]
            wide_ref[0, group * rows : (group + 1) * rows, :] = jnp.concatenate(pieces, axis=1)

    for index in range(4):
        for core in range(2):

            @pl.when((part == index) & (where_ref[0] == core))
            def _(index=index, core=core):
                mine, twin = (mine_a, mine_b), (twin_a, twin_b)
                collect((mine, twin) if core == 0 else (twin, mine), index)

    for index in range(3):

        @pl.when(part == index)
        def _(index=index):
            out = mm(h_ref[...], wide_ref[0])
            if index != 1:
                at = slice(index // 2 * width, (index // 2 + 1) * width)
                bias = jnp.concatenate([bias_ref[model : model + 1, at] for model in range(4)], axis=1)
                out = out + bias
            qkv_ref[...] = out.astype(low)


def project(where, spots, h, halves, bias, after):
    seq, depth = h.shape
    return pl.pallas_call(
        held_back(project_body, 8, len(after)),
        grid_spec=pltpu.PrefetchScalarGridSpec(
            num_scalar_prefetch=2,
            grid=(4,),
            in_specs=[
                once((seq, depth)),
                *[once(halves[0].shape)] * 4,
                once(bias.shape),
            ]
            + [LATER] * len(after),
            out_specs=[
                pl.BlockSpec((seq, depth), lambda i, *_: (0, jnp.minimum(i, 2))),
                pl.BlockSpec((1, depth, depth), lambda i, *_: (i, 0, 0)),
            ],
        ),
        out_shape=[far_away((seq, 3 * depth), low), far_away((4, depth, depth), low)],
        compiler_params=params(24),
        cost_estimate=cost(2 * seq * depth * depth * 3, seq * depth * 16),
        name="project",
    )(where, spots, h, *halves, bias, *after)


def attend_out_body(o_ref, w_ref, x_ref, vec_ref, middle_ref, h_ref, ht_ref):
    middle = x_ref[...].astype(f32) + mm_nt(o_ref[...], w_ref[0]) + vec_ref[4:5, :]
    middle_ref[...] = middle.astype(low)
    unit, _ = normalize(middle)
    h = (unit * vec_ref[2:3, :] + vec_ref[3:4, :]).astype(low)
    h_ref[...] = h
    ht_ref[...] = h.T


def attend_out(o, wide, x, vectors):
    seq, depth = x.shape
    rows = pl.BlockSpec((TILE, depth), lambda i: (i, 0))
    turned = pl.BlockSpec((depth, TILE), lambda i: (0, i))
    return pl.pallas_call(
        attend_out_body,
        grid=(seq // TILE,),
        in_specs=[
            rows,
            pl.BlockSpec((1, depth, depth), lambda i: (3, 0, 0)),
            rows,
            once(vectors.shape),
        ],
        out_specs=[rows, rows, turned],
        out_shape=[sds((seq, depth), low), sds((seq, depth), low), sds((depth, seq), low)],
        compiler_params=params(14),
        cost_estimate=cost(2 * seq * depth * depth, seq * depth * 14),
        name="attend_out",
    )(o, *from_far(wide, x), vectors)


def feed_body(
    where_ref,
    spots_ref,
    h2_ref,
    h2t_ref,
    up_ref,
    upt_ref,
    mine_a,
    mine_b,
    twin_a,
    twin_b,
    bias_ref,
    middle_ref,
    vec_ref,
    block_ref,
    back_ref,
    keep_ref,
    send_ref,
    bias_grad_ref,
    out_ref,
    sum_ref,
    wide_ref,
    act_ref,
    pre_ref,
):
    step = pl.program_id(0)
    side = lax.rem(step, 2)
    models = [where_ref[1] ^ (2 * side + core) for core in range(2)]
    rows = mine_a.shape[1]
    part = mine_a.shape[2] // 2
    groups = wide_ref.shape[0] // rows

    @pl.when(step == 0)
    def _():
        out_ref[...] = middle_ref[...].astype(f32) + vec_ref[5:6, :]
        sum_ref[...] = jnp.zeros_like(sum_ref)

    for group in range(groups):
        at = slice(group * rows, (group + 1) * rows)
        own = slot((mine_a, mine_b), spots_ref[models[0], group], slice(None))
        other = slot((twin_a, twin_b), spots_ref[models[1], group], slice(None))
        wide_ref[at, :part] = own[:, :part]
        wide_ref[at, part : 2 * part] = other[:, :part]
        wide_ref[at, 2 * part : 3 * part] = own[:, part:]
        wide_ref[at, 3 * part :] = other[:, part:]

    expand = wide_ref[:, : 2 * part]
    shrink = wide_ref[:, 2 * part :]
    first = step // 2 * part
    skip = bias_ref.shape[1] - bias_grad_ref.shape[1]
    bias = jnp.concatenate(
        [bias_ref[pl.ds(model, 1), pl.ds(pl.multiple_of(skip + first, 128), part)] for model in models],
        axis=1,
    )
    sums = jnp.zeros((1, 2 * part), f32)
    for tile in range(h2_ref.shape[0] // TILE):
        at = slice(tile * TILE, (tile + 1) * TILE)
        u = mm(h2_ref[at, :], expand) + bias
        square = u * u
        th = jnp.tanh(u * (GELU_A + GELU_B * square))
        gate = 0.5 * th + 0.5
        slope = gate + (gate * (1.0 - gate)) * (u * (2.0 * GELU_A + (6.0 * GELU_B) * square))
        pre = (mm(up_ref[at, :], shrink) * slope).astype(low)
        act_ref[at, :] = (u * gate).astype(low)
        pre_ref[at, :] = pre
        sums = sums + columns_of(pre.astype(f32))
    for core, model in enumerate(models):
        bias_grad_ref[pl.ds(model, 1), pl.ds(pl.multiple_of(first, 128), part)] = sums[
            :, core * part : (core + 1) * part
        ]
    out_ref[...] += mm_nt(act_ref[...], shrink)
    sum_ref[...] += mm_nt(pre_ref[...], expand)
    grad_expand = mm(h2t_ref[...], pre_ref[...]).astype(low)
    grad_shrink = mm(upt_ref[...], act_ref[...]).astype(low)
    for group in range(groups):
        at = slice(group * rows, (group + 1) * rows)
        own, other = spots_ref[models[0], group], spots_ref[models[1], group]
        keep_ref[own, :, :part] = grad_expand[at, :part]
        keep_ref[own, :, part:] = grad_shrink[at, :part]
        send_ref[other, :, :part] = grad_expand[at, part:]
        send_ref[other, :, part:] = grad_shrink[at, part:]

    @pl.when(step == pl.num_programs(0) - 1)
    def _():
        block_ref[...] = out_ref[...].astype(low)
        back_ref[...] = sum_ref[...].astype(low)


def feed(where, spots, h2, h2t, up, upt, halves, bias, middle, vectors):
    seq, depth = h2.shape
    half, rows, columns = halves[0].shape
    steps, part = 6, columns // 6
    half_piece = pl.BlockSpec((half, rows, 2 * part), lambda i, *_: (0, 0, i // 2))
    piece = pl.BlockSpec((2 * half, rows, 2 * part), lambda i, *_: (0, 0, i // 2))
    return pl.pallas_call(
        feed_body,
        grid_spec=pltpu.PrefetchScalarGridSpec(
            num_scalar_prefetch=2,
            grid=(steps,),
            in_specs=[
                once((seq, depth)),
                once((depth, seq)),
                once((seq, depth)),
                once((depth, seq)),
                *[half_piece] * 4,
                once(bias.shape),
                once((seq, depth)),
                once(vectors.shape),
            ],
            out_specs=[whole((seq, depth)), whole((seq, depth)), piece, piece, whole((4, 3 * part))],
            scratch_shapes=[
                pltpu.VMEM((seq, depth), f32),
                pltpu.VMEM((seq, depth), f32),
                pltpu.VMEM((depth, 4 * part), low),
                pltpu.VMEM((seq, 2 * part), low),
                pltpu.VMEM((seq, 2 * part), low),
            ],
        ),
        out_shape=[sds((seq, depth), low)] * 2
        + [sds((2 * half, rows, columns), low)] * 2
        + [sds((4, 3 * part), f32)],
        compiler_params=params(31),
        cost_estimate=cost(12 * seq * depth * steps * 2 * part, seq * depth * 40, seq * steps * part),
        name="feed",
    )(where, spots, h2, h2t, *from_far(up, upt), *halves, bias, middle, vectors)


def middle_back_body(
    where_ref,
    lengths_ref,
    back_ref,
    middle_ref,
    up_ref,
    o_ref,
    w_ref,
    vec_ref,
    grad_ref,
    mixture_ref,
    weight_ref,
    sums_ref,
    total_ref,
):
    step = pl.program_id(0)
    unit, inverse = normalize(middle_ref[...].astype(f32))
    back = back_ref[...].astype(f32)
    up = up_ref[...].astype(f32)
    grad = up + pull_norm(back * vec_ref[2:3, :], unit, inverse)
    rounded = grad.astype(low)
    grad_ref[...] = rounded
    row = step * grad.shape[0] + lax.broadcasted_iota(jnp.int32, grad.shape, 0)
    length = lengths_ref[where_ref[2]]
    mixture_ref[...] = jnp.where(row < length, mm(rounded, w_ref[0]), 0.0).astype(low)
    share = mm(rounded.T, o_ref[...])
    sums = jnp.concatenate(
        [columns_of(back * unit), columns_of(back), columns_of(grad), columns_of(up)], axis=0
    )

    @pl.when(step == 0)
    def _():
        total_ref[...] = share
        sums_ref[...] = sums

    @pl.when(step > 0)
    def _():
        total_ref[...] += share
        sums_ref[...] += sums

    @pl.when(step == pl.num_programs(0) - 1)
    def _():
        weight_ref[...] = total_ref[...].astype(low)


def middle_back(where, lengths, back, middle, up, o, wide, vectors):
    seq, depth = middle.shape
    rows = pl.BlockSpec((2 * TILE, depth), lambda i, *_: (i, 0))
    return pl.pallas_call(
        middle_back_body,
        grid_spec=pltpu.PrefetchScalarGridSpec(
            num_scalar_prefetch=2,
            grid=(seq // (2 * TILE),),
            in_specs=[
                rows,
                rows,
                rows,
                rows,
                pl.BlockSpec((1, depth, depth), lambda i, *_: (3, 0, 0)),
                once(vectors.shape),
            ],
            out_specs=[rows, rows, whole((depth, depth)), whole((4, depth))],
            scratch_shapes=[pltpu.VMEM((depth, depth), f32)],
        ),
        out_shape=[
            sds((seq, depth), low),
            sds((seq, depth), low),
            sds((depth, depth), low),
            sds((4, depth), f32),
        ],
        compiler_params=params(24),
        cost_estimate=cost(4 * seq * depth * depth, seq * depth * 28),
        name="middle_back",
    )(where, lengths, back, middle, *from_far(up), o, *from_far(wide), vectors)


def input_grad_body(where_ref, spots_ref, ht_ref, back_ref, out_grad_ref, keep_ref, send_ref, sums_ref):
    part = pl.program_id(0)
    rows = keep_ref.shape[1]
    width = keep_ref.shape[2] // 4
    groups = ht_ref.shape[0] // rows

    def spread(targets, index, grad):
        at = slice(index * width, (index + 1) * width)
        for group in range(groups):
            for model in range(4):
                targets[model % 2][spots_ref[model, group], :, at] = grad[
                    group * rows : (group + 1) * rows, model * width : (model + 1) * width
                ]

    for index in range(4):

        @pl.when(part == index)
        def _(index=index):
            if index < 3:
                sums_ref[0] = columns_of(back_ref[0].astype(f32))
                grad = mm(ht_ref[...], back_ref[0]).astype(low)
            else:
                grad = out_grad_ref[...]
            for core in range(2):

                @pl.when(where_ref[0] == core)
                def _(core=core):
                    spread((keep_ref, send_ref) if core == 0 else (send_ref, keep_ref), index, grad)


def input_grad(where, spots, ht, back, out_grad, slots, rows, after):
    depth, seq = ht.shape
    shape = (slots, rows, 4 * (depth // 4))
    return pl.pallas_call(
        held_back(input_grad_body, 5, len(after)),
        grid_spec=pltpu.PrefetchScalarGridSpec(
            num_scalar_prefetch=2,
            grid=(4,),
            in_specs=[
                once((depth, seq)),
                pl.BlockSpec((1, seq, depth), lambda i, *_: (jnp.minimum(i, 2), 0, 0)),
                once((depth, depth)),
            ]
            + [LATER] * len(after),
            out_specs=[
                whole(shape),
                whole(shape),
                pl.BlockSpec((1, 1, depth), lambda i, *_: (jnp.minimum(i, 2), 0, 0)),
            ],
        ),
        out_shape=[sds(shape, low), sds(shape, low), sds((3, 1, depth), f32)],
        compiler_params=params(24),
        cost_estimate=cost(6 * seq * depth * depth, seq * depth * 14),
        name="input_grad",
    )(where, spots, *from_far(ht), back, out_grad, *after)


def token_back_body(
    back_ref, w_ref, x_ref, grad_ref, vec_ref, middle_ref, head_ref, bias_ref, token_ref, sums_ref
):
    step = pl.program_id(0)
    back = mm_nt(back_ref[0], w_ref[0]) + mm_nt(back_ref[1], w_ref[1]) + mm_nt(back_ref[2], w_ref[2])
    unit, inverse = normalize(x_ref[...].astype(f32))
    grad = grad_ref[...].astype(f32)
    token_ref[...] = (grad + pull_norm(back * vec_ref[0:1, :], unit, inverse)).astype(low)
    sums = jnp.concatenate([columns_of(back * unit), columns_of(back)], axis=0)

    @pl.when(step == 0)
    def _():
        sums_ref[:2] = sums
        sums_ref[2:6] = middle_ref[...]
        sums_ref[6:7] = head_ref[0]
        sums_ref[7:8] = head_ref[2]
        sums_ref[8:] = bias_ref[...]

    @pl.when(step > 0)
    def _():
        sums_ref[:2] += sums


def token_back(back, wide, x, grad, vectors, sums, after):
    seq, depth = x.shape
    rows = pl.BlockSpec((TILE, depth), lambda i: (i, 0))
    return pl.pallas_call(
        held_back(token_back_body, 8, len(after)),
        grid=(seq // TILE,),
        in_specs=[
            pl.BlockSpec((3, TILE, depth), lambda i: (0, i, 0)),
            pl.BlockSpec((3, depth, depth), lambda i: (0, 0, 0)),
            rows,
            rows,
            once(vectors.shape),
            *[once(array.shape) for array in sums],
        ]
        + [LATER] * len(after),
        out_specs=[rows, whole((12, depth))],
        out_shape=[sds((seq, depth), low), sds((12, depth), f32)],
        compiler_params=params(24),
        cost_estimate=cost(6 * seq * depth * depth, seq * depth * 16),
        name="token_back",
    )(back, *from_far(wide, x), grad, vectors, *sums, *after)


CORE_ORDERS = ((4, 3, 2, 1), (3, 4, 1, 2))
STAGES = 4


def cube_permute(values, stage):
    pairs = [(device, device ^ (1 << CORE_ORDERS[device & 1][stage])) for device in range(32)]
    return lax.ppermute(values, ("dp", "mp"), pairs)


def bit_permute(values, bit):
    return lax.ppermute(values, ("dp", "mp"), [(device, device ^ (1 << bit)) for device in range(32)])


def place(distance, core):
    spots = [
        sum(((distance >> bit) & 1) << step for step, bit in enumerate(order)) for order in CORE_ORDERS
    ]
    return jnp.where(core == 0, spots[0], spots[1])


def joined(held, arrived):
    return jnp.concatenate([held, arrived], axis=0)


def leaving(parts, stage):
    half = 1 << stage
    return sum(part[half:].astype(f32) for part in parts).astype(low)


def staying(parts, stage):
    return [part[: 1 << stage] for part in parts]


def summed(parts):
    return sum(part[0].astype(f32) for part in parts)


def cube_sum(values, bits=range(5)):
    for bit in bits:
        values = values + bit_permute(values, bit)
    return values


def adam_parts(weight, gradient, first_old, second_old, factor, step_rate):
    scaled = gradient * factor
    moment = beta_one * first_old + (1.0 - beta_one) * scaled
    square = beta_two * second_old + (1.0 - beta_two) * scaled * scaled
    spread = jnp.sqrt(square * (1.0 / (1.0 - beta_two**STEP)))
    ratio = moment * (1.0 / (1.0 - beta_one**STEP)) / (spread + adam_eps)
    return moment, square, weight - step_rate * (ratio + decay * weight)


def optimize_body(owned_ref, vector_ref, attend_ref, feed_ref, *refs):
    state, outs = refs[:15], refs[15:]
    vectors = vector_ref[...]
    total = owned_ref[0:1, 0:1] + jnp.sum(vectors * vectors)
    norm = jnp.sqrt(total)
    factor = clip_norm / jnp.maximum(norm, clip_norm)
    outs[0][...] = norm
    outs[1][...] = factor
    width = state[0].shape[2]
    part = state[6].shape[1] // 3

    def update(param, at, gradient, step_rate):
        weight, first, second = (ref[at] for ref in state[3 * param : 3 * param + 3])
        results = adam_parts(weight, gradient, first, second, factor, step_rate)
        for ref, result in zip(outs[2 + 3 * param : 5 + 3 * param], results):
            ref[at] = result

    for index in range(3):
        update(0, (index,), attend_ref[:, index * width : (index + 1) * width], rate)
    update(1, (...,), attend_ref[:, 3 * width :].T, rate)
    for index in range(3):
        at = (slice(None), slice(index * part, (index + 1) * part))
        first = 2 * index * part
        update(2, at, feed_ref[:, first : first + part], rate)
        update(3, at, feed_ref[:, first + part : first + 2 * part], rate)
    update(4, (...,), vectors[:6], vector_rate)


def optimize(owned, vector_total, attend_total, feed_total, state):
    shapes = [sds(group[0].shape, f32) for group in state for _ in range(3)]
    return pl.pallas_call(
        optimize_body,
        out_shape=[sds((1, 1), f32), sds((1, 1), f32)] + shapes,
        compiler_params=params(20),
        cost_estimate=cost(4e6, 8e6),
        name="optimize",
    )(owned, vector_total, attend_total, feed_total, *[array for group in state for array in group])


def shards(
    tokens,
    cotangent,
    lengths,
    input_weight,
    output_weight,
    expand_weight,
    shrink_weight,
    layer_vectors,
    head_bias,
    expand_bias,
    first_input,
    first_output,
    first_expand,
    first_shrink,
    first_vectors,
    first_head,
    first_bias,
    second_input,
    second_output,
    second_expand,
    second_shrink,
    second_vectors,
    second_head,
    second_bias,
):
    dp_count = lax.axis_size("dp")
    mp_count = lax.axis_size("mp")
    cube = dp_count == 8 and mp_count == 4
    rows = input_weight.shape[0]
    width = input_weight.shape[2]
    hidden = expand_weight.shape[1]
    seq, depth = tokens.shape
    part = hidden // 3
    model_index = lax.axis_index("mp")
    me = lax.axis_index("dp") * mp_count + model_index

    attend_shard, feed_shard = pack(
        input_weight.transpose(1, 0, 2), output_weight, expand_weight, shrink_weight.T
    )
    bias_shard = jnp.concatenate([head_bias.reshape(1, 2 * width), expand_bias[None]], axis=1)

    bias_full = jnp.where(jnp.arange(4)[:, None] == model_index, bias_shard, 0.0)
    if cube:
        core, near = me & 1, model_index
        devices = jnp.arange(32).reshape(8, 4).T
        spots = place(devices ^ me, devices & 1).astype(jnp.int32)
    else:
        core = near = jnp.zeros((), jnp.int32)
        spots = (jnp.arange(4)[:, None] // 2 * 8 + jnp.arange(8)[None]).astype(jnp.int32)
    where = jnp.stack([core, near, model_index]).astype(jnp.int32)

    if cube:
        held = attend_shard[None]
        arrived = cube_permute(held, 0)
        bias_full = bias_full + bit_permute(bias_full, 0)
        held = joined(held, arrived)
        arrived = cube_permute(held, 1)
        normed, normed_t, upstream_t = prepare(tokens, cotangent, layer_vectors, (held,))
        bias_full = bias_full + bit_permute(bias_full, 1)
        held, feed_shard, normed, bias_full, spots, where = lax.optimization_barrier(
            (held, feed_shard, normed, bias_full, spots, where)
        )
        held = joined(held, arrived)
        feed_held = feed_shard[None]
        arrived, far_feed = cube_permute(held, 2), cube_permute(feed_held, 0)
        held = joined(held, arrived)
        feed_held = joined(feed_held, far_feed)
        held, feed_held = lax.optimization_barrier((held, feed_held))
        far, far_feed = cube_permute(held, 3), cube_permute(feed_held, 1)
        twin = bit_permute(held, 0)
        feed_held = joined(feed_held, far_feed)
        far, feed_held = lax.optimization_barrier((far, feed_held))
        attend_halves = (held, far, twin, bit_permute(far, 0))
        arrived = cube_permute(feed_held, 2)
        qkv, wide = project(where, spots, normed, attend_halves, bias_full, ())
        feed_held, qkv = lax.optimization_barrier((feed_held, qkv))
        feed_held = joined(feed_held, arrived)
        far, twin = cube_permute(feed_held, 3), bit_permute(feed_held, 0)
        mixture, log_totals = attend_forward(where, lengths, qkv, (feed_held,))
        middle, hidden_in, hidden_t = attend_out(mixture, wide, tokens, layer_vectors)
        far, hidden_in = lax.optimization_barrier((far, hidden_in))
        feed_halves = (feed_held, far, twin, bit_permute(far, 0))
    else:

        def planes(shard):
            full = lax.all_gather(lax.all_gather(shard, "dp", axis=0, tiled=True), "mp", axis=0)
            full = full.reshape(2, 2, 8, depth // 8, shard.shape[1]).transpose(1, 0, 2, 3, 4)
            return tuple(full.reshape(4, 8, depth // 8, shard.shape[1]))

        normed, normed_t, upstream_t = prepare(tokens, cotangent, layer_vectors, ())
        bias_full = lax.psum(bias_full, "mp")
        qkv, wide = project(where, spots, normed, planes(attend_shard), bias_full, ())
        mixture, log_totals = attend_forward(where, lengths, qkv, ())
        middle, hidden_in, hidden_t = attend_out(mixture, wide, tokens, layer_vectors)
        feed_halves = planes(feed_shard)
    block_out, back, keep_feed, send_feed, bias_grad = feed(
        where,
        spots,
        hidden_in,
        hidden_t,
        cotangent,
        upstream_t,
        feed_halves,
        bias_full,
        middle,
        layer_vectors,
    )
    middle_grad, mixture_grad, output_grad, middle_sums = middle_back(
        where, lengths, back, middle, cotangent, mixture, wide, layer_vectors
    )
    if cube:
        feed_parts = [keep_feed, bit_permute(send_feed, 0)]
        keep_feed, mixture_grad = lax.optimization_barrier((keep_feed, mixture_grad))
        feed_parts[0] = keep_feed
        away = leaving(feed_parts, 3)
        packed_grad = attend_backward(where, lengths, qkv, mixture_grad, log_totals, (away,))
        feed_parts = staying(feed_parts, 3) + [cube_permute(away, 3)]
        feed_parts[0], packed_grad = lax.optimization_barrier((feed_parts[0], packed_grad))
        away = leaving(feed_parts, 2)
        keep_attend, send_attend, head_sums = input_grad(
            where, spots, normed_t, packed_grad, output_grad, 16, depth // 8, (away,)
        )
        feed_parts = staying(feed_parts, 2) + [cube_permute(away, 2)]
        feed_parts[-1], send_attend = lax.optimization_barrier((feed_parts[-1], send_attend))
        attend_parts = [keep_attend, bit_permute(send_attend, 0)]
        away, feed_away = leaving(attend_parts, 3), leaving(feed_parts, 1)
        token_grad, vector_total = token_back(
            packed_grad,
            wide,
            tokens,
            middle_grad,
            layer_vectors,
            (middle_sums, head_sums, bias_grad),
            (away, feed_away),
        )
    else:
        packed_grad = attend_backward(where, lengths, qkv, mixture_grad, log_totals, ())
        keep_attend, send_attend, head_sums = input_grad(
            where, spots, normed_t, packed_grad, output_grad, 16, depth // 8, ()
        )
        token_grad, vector_total = token_back(
            packed_grad,
            wide,
            tokens,
            middle_grad,
            layer_vectors,
            (middle_sums, head_sums, bias_grad),
            (),
        )

    if cube:
        attend_parts = staying(attend_parts, 3) + [cube_permute(away, 3)]
        feed_parts = staying(feed_parts, 1) + [cube_permute(feed_away, 1)]
        attend_parts[0], vector_total = lax.optimization_barrier((attend_parts[0], vector_total))
        away, feed_away = leaving(attend_parts, 2), leaving(feed_parts, 0)
        attend_parts = staying(attend_parts, 2) + [cube_permute(away, 2)]
        feed_parts = staying(feed_parts, 0) + [cube_permute(feed_away, 0)]
        away, vector_total = lax.optimization_barrier((away, vector_total))
        vector_total = cube_sum(vector_total, (0, 1))
        attend_parts[0], vector_total = lax.optimization_barrier((attend_parts[0], vector_total))
        away = leaving(attend_parts, 1)
        attend_parts = staying(attend_parts, 1) + [cube_permute(away, 1)]
        away, vector_total = lax.optimization_barrier((away, vector_total))
        vector_total = cube_sum(vector_total, (2, 3))
        feed_total = summed(feed_parts)
        feed_squares = jnp.sum(feed_total * feed_total)
        attend_parts[0], vector_total, feed_squares = lax.optimization_barrier(
            (attend_parts[0], vector_total, feed_squares)
        )
        away = leaving(attend_parts, 0)
        attend_parts = staying(attend_parts, 0) + [cube_permute(away, 0)]
        away, vector_total = lax.optimization_barrier((away, vector_total))
        vector_total = cube_sum(vector_total, (4,))
        attend_total = summed(attend_parts)
    else:

        def own_block(keep, send):
            full = jnp.stack([keep, send]).reshape(2, 2, 8, depth // 8, keep.shape[2])
            full = full.transpose(1, 0, 2, 3, 4).reshape(4, depth, keep.shape[2])
            full = lax.psum_scatter(full, "mp", scatter_dimension=0, tiled=False)
            return lax.psum_scatter(full, "dp", scatter_dimension=0, tiled=True).astype(f32)

        attend_total = own_block(keep_attend, send_attend)
        feed_total = own_block(keep_feed, send_feed)
        vector_total = lax.psum(vector_total, ("dp", "mp"))
        feed_squares = jnp.sum(feed_total * feed_total)
    owned = jnp.full((8, 128), jnp.sum(attend_total * attend_total) + feed_squares, f32)
    owned = cube_sum(owned) if cube else lax.psum(owned, ("dp", "mp"))
    head_total = lax.dynamic_slice_in_dim(vector_total[6:8], model_index * width, width, 1)
    bias_total = lax.dynamic_slice_in_dim(vector_total[8:].reshape(-1), model_index * hidden, hidden, 0)

    def turned(array):
        return array.transpose(1, 0, 2)

    state = (
        (turned(input_weight), turned(first_input), turned(second_input)),
        (output_weight, first_output, second_output),
        (expand_weight, first_expand, second_expand),
        (shrink_weight.T, first_shrink.T, second_shrink.T),
        (layer_vectors, first_vectors, second_vectors),
    )
    grad_norm, factor, *updates = optimize(owned, vector_total, attend_total, feed_total, state)
    grad_norm, factor = grad_norm[0, 0], factor[0, 0]
    moment_input, square_input, updated_input = (turned(array) for array in updates[:3])
    moment_output, square_output, updated_output = updates[3:6]
    moment_expand, square_expand, updated_expand = updates[6:9]
    moment_shrink, square_shrink, updated_shrink = (array.T for array in updates[9:12])
    moment_vectors, square_vectors, updated_vectors = updates[12:]
    moment_head, square_head, updated_head = adam_parts(
        head_bias, head_total, first_head, second_head, factor, vector_rate
    )
    moment_bias, square_bias, updated_bias = adam_parts(
        expand_bias, bias_total, first_bias, second_bias, factor, vector_rate
    )
    return (
        block_out,
        token_grad,
        grad_norm,
        moment_input,
        square_input,
        updated_input,
        moment_output,
        square_output,
        updated_output,
        moment_expand,
        square_expand,
        updated_expand,
        moment_shrink,
        square_shrink,
        updated_shrink,
        moment_vectors,
        square_vectors,
        updated_vectors,
        moment_head,
        square_head,
        updated_head,
        moment_bias,
        square_bias,
        updated_bias,
    )


def solution(mesh):
    in_specs = (
        P(("dp", "mp"), None),
        P(("dp", "mp"), None),
        P("dp"),
        P("dp", None, "mp"),
        P("mp", "dp"),
        P("dp", "mp"),
        P("mp", "dp"),
        P(),
        P(None, "mp"),
        P("mp"),
        P("dp", None, "mp"),
        P("mp", "dp"),
        P("dp", "mp"),
        P("mp", "dp"),
        P(),
        P(None, "mp"),
        P("mp"),
        P("dp", None, "mp"),
        P("mp", "dp"),
        P("dp", "mp"),
        P("mp", "dp"),
        P(),
        P(None, "mp"),
        P("mp"),
    )
    out_specs = (
        P(("dp", "mp"), None),
        P(("dp", "mp"), None),
        P(),
        P("dp", None, "mp"),
        P("dp", None, "mp"),
        P("dp", None, "mp"),
        P("mp", "dp"),
        P("mp", "dp"),
        P("mp", "dp"),
        P("dp", "mp"),
        P("dp", "mp"),
        P("dp", "mp"),
        P("mp", "dp"),
        P("mp", "dp"),
        P("mp", "dp"),
        P(),
        P(),
        P(),
        P(None, "mp"),
        P(None, "mp"),
        P(None, "mp"),
        P("mp"),
        P("mp"),
        P("mp"),
    )
    return jax.shard_map(shards, mesh=mesh, in_specs=in_specs, out_specs=out_specs, check_vma=False)
```

```python
import functools
import jax
import jax.numpy as jnp
from jax import lax
from jax.experimental import pallas as pl
from jax.experimental.pallas import tpu as pltpu
from jax.sharding import PartitionSpec as P

HEAD_DIM = 64
TILE = 256
STEP = 10

eps_norm = 1e-05
clip_norm = 1.0
beta_one = 0.9
beta_two = 0.999
adam_eps = 1e-08
rate = 0.05
vector_rate = 0.5
decay = 0.01
excluded = -1e30
low = jnp.bfloat16
f32 = jnp.float32
GELU_A = 0.7978845608028654
GELU_B = GELU_A * 0.044715


def params(limit_mib, **kw):
    return pltpu.CompilerParams(vmem_limit_bytes=limit_mib * 1024 * 1024, **kw)


def cost(flops, moved, special=0):
    return pl.CostEstimate(flops=int(flops), bytes_accessed=int(moved), transcendentals=int(special))


def mm(a, b):
    return jnp.dot(a, b, preferred_element_type=f32)


def mm_nt(a, b):
    return lax.dot_general(a, b, (((1,), (1,)), ((), ())), preferred_element_type=f32)


def whole(shape):
    zeros = (0,) * len(shape)
    return pl.BlockSpec(shape, lambda *_: zeros)


def once(shape):
    zeros = (0,) * len(shape)
    return pl.BlockSpec(shape, lambda *_: zeros, pipeline_mode=pl.Buffered(1))


def held_back(body, first, count):
    def run(*refs):
        return body(*refs[:first], *refs[first + count :])

    return run


LATER = pl.BlockSpec(memory_space=pl.ANY)


def far_away(shape, dtype):
    return pltpu.HBM(shape, dtype)


def from_far(*arrays):
    return [pltpu.with_memory_space_constraint(array, pltpu.HBM) for array in arrays]


def sds(shape, dtype):
    return jax.ShapeDtypeStruct(shape, dtype)


def live_blocks(length, count, body):
    for blocks in range(1, count + 1):
        low_end = (blocks - 1) * TILE
        high_end = blocks * TILE
        @pl.when((length > low_end) & (length <= high_end))
        def _(blocks=blocks):
            body(length, blocks)


PAIR = 2 * HEAD_DIM


def span(block):
    return slice(block * TILE, (block + 1) * TILE)


def both_heads(values):
    lane = lax.broadcasted_iota(jnp.int32, values.shape, 1)
    none = jnp.zeros_like(values)
    return jnp.concatenate(
        [jnp.where(lane < HEAD_DIM, values, none), jnp.where(lane >= HEAD_DIM, values, none)], axis=0
    )


def causal_mask():
    key_id = lax.broadcasted_iota(jnp.int32, (TILE, 2 * TILE), 0)
    query_id = lax.broadcasted_iota(jnp.int32, (TILE, 2 * TILE), 1) & (TILE - 1)
    return key_id <= query_id


def forward_body(where_ref, lengths_ref, q_ref, k_ref, v_ref, o_ref, lse_ref, vt_ref):
    seq = q_ref.shape[0]
    vt_ref[...] = v_ref[...].T
    causal = causal_mask()

    def run(length, blocks):
        def scores(b):
            q = q_ref[span(b), :] * jnp.asarray(HEAD_DIM**-0.5, low)
            return mm_nt(k_ref[: (b + 1) * TILE, :], both_heads(q))

        now = scores(0)
        for b in range(blocks):
            start, stop = b * TILE, (b + 1) * TILE
            later = scores(b + 1) if b + 1 < blocks else None
            last = jnp.where(causal, now[start:, :], excluded)
            top = jnp.max(last, axis=0, keepdims=True)
            if b:
                top = jnp.maximum(top, jnp.max(now[:start], axis=0, keepdims=True))
            p = jnp.exp(last - top)
            total = jnp.sum(p, axis=0, keepdims=True)
            pb = p.astype(low)
            if b:
                pf = jnp.exp(now[:start] - top)
                total = total + jnp.sum(pf, axis=0, keepdims=True)
                pb = jnp.concatenate([pf.astype(low), pb], axis=0)
            inverse = 1.0 / total
            lse = top + jnp.log(total)
            outs = []
            for h in range(2):
                at = slice(h * TILE, (h + 1) * TILE)
                out = mm(vt_ref[h * HEAD_DIM : (h + 1) * HEAD_DIM, :stop], pb[:, at])
                outs.append(out * inverse[:, at])
                lse_ref[0, h : h + 1, start:stop] = lse[:, at]
            both = jnp.concatenate(outs, axis=0).T
            row = start + lax.broadcasted_iota(jnp.int32, both.shape, 0)
            o_ref[start:stop, :] = jnp.where(row < length, both, 0.0).astype(low)
            now = later
        if blocks * TILE < seq:
            o_ref[blocks * TILE :, :] = jnp.zeros((seq - blocks * TILE, PAIR), low)
            lse_ref[0, :, blocks * TILE :] = jnp.zeros((2, seq - blocks * TILE), f32)

    live_blocks(lengths_ref[where_ref[2]], seq // TILE, run)


def attend_forward(where, lengths, qkv, after):
    seq, width = qkv.shape[0], qkv.shape[1] // 3
    pair = 2 * HEAD_DIM
    pairs = width // pair
    half = seq * seq * 5 // 8
    spec = lambda part: pl.BlockSpec((seq, pair), lambda i, *_: (0, part * pairs + i))
    return pl.pallas_call(
        held_back(forward_body, 5, len(after)),
        grid_spec=pltpu.PrefetchScalarGridSpec(
            num_scalar_prefetch=2,
            grid=(pairs,),
            in_specs=[spec(0), spec(1), spec(2)] + [LATER] * len(after),
            out_specs=[
                pl.BlockSpec((seq, pair), lambda i, *_: (0, i)),
                pl.BlockSpec((1, 2, seq), lambda i, *_: (i, 0, 0)),
            ],
            scratch_shapes=[pltpu.VMEM((pair, seq), low)],
        ),
        out_shape=[sds((seq, width), low), far_away((pairs, 2, seq), f32)],
        compiler_params=params(20),
        cost_estimate=cost(pairs * 2 * half * 2 * 2 * 256, seq * width * 8, pairs * 2 * half),
        name="attend_forward",
    )(where, lengths, *from_far(qkv, qkv, qkv), *after)


def backward_body(where_ref, lengths_ref, q_ref, k_ref, v_ref, do_ref, lse_ref, out_ref, kt_ref, ksum, vsum):
    seq = q_ref.shape[0]
    scale = HEAD_DIM**-0.5
    kt_ref[...] = k_ref[...].T
    causal = causal_mask()

    def run(length, blocks):
        def scores(b):
            qq = both_heads(q_ref[span(b), :] * jnp.asarray(scale, low))
            uu = both_heads(do_ref[span(b), :])
            stop = (b + 1) * TILE
            return qq, uu, mm_nt(k_ref[:stop, :], qq), mm_nt(v_ref[:stop, :], uu)

        now = scores(blocks - 1)
        for b in reversed(range(blocks)):
            start, stop = b * TILE, (b + 1) * TILE
            later = scores(b - 1) if b else None
            qq, uu, s, dp = now
            lse = jnp.concatenate([lse_ref[0, 0:1, start:stop], lse_ref[0, 1:2, start:stop]], axis=1)
            p = jnp.exp(jnp.where(causal, s[start:], excluded) - lse)
            inner = jnp.sum(p * dp[start:], axis=0, keepdims=True)
            if b:
                pf = jnp.exp(s[:start] - lse)
                inner = inner + jnp.sum(pf * dp[:start], axis=0, keepdims=True)
            ds = (p * (dp[start:] - inner)).astype(low)
            pb = p.astype(low)
            if b:
                ds = jnp.concatenate([(pf * (dp[:start] - inner)).astype(low), ds], axis=0)
                pb = jnp.concatenate([pf.astype(low), pb], axis=0)
            dk, dv = mm(ds, qq), mm(pb, uu)
            if b == blocks - 1:
                ksum[:stop, :] = dk
                vsum[:stop, :] = dv
            else:
                ksum[:stop, :] += dk
                vsum[:stop, :] += dv
            dq = jnp.concatenate(
                [
                    mm(
                        kt_ref[h * HEAD_DIM : (h + 1) * HEAD_DIM, :stop],
                        ds[:, h * TILE : (h + 1) * TILE],
                    )
                    for h in range(2)
                ],
                axis=0,
            )
            out_ref[1, start:stop, :] = ksum[start:stop, :].astype(low)
            out_ref[2, start:stop, :] = vsum[start:stop, :].astype(low)
            out_ref[0, start:stop, :] = (dq.T * scale).astype(low)
            now = later
        if blocks * TILE < seq:
            rest = jnp.zeros((seq - blocks * TILE, PAIR), low)
            for part in range(3):
                out_ref[part, blocks * TILE :, :] = rest

    live_blocks(lengths_ref[where_ref[2]], seq // TILE, run)


def attend_backward(where, lengths, qkv, upstream, lse, after):
    seq, width = upstream.shape
    pair = 2 * HEAD_DIM
    pairs = width // pair
    half = seq * seq * 5 // 8
    spec = lambda part: pl.BlockSpec((seq, pair), lambda i, *_: (0, part * pairs + i))
    own = pl.BlockSpec((seq, pair), lambda i, *_: (0, i))
    return pl.pallas_call(
        held_back(backward_body, 7, len(after)),
        grid_spec=pltpu.PrefetchScalarGridSpec(
            num_scalar_prefetch=2,
            grid=(pairs,),
            in_specs=[spec(0), spec(1), spec(2), own, pl.BlockSpec((1, 2, seq), lambda i, *_: (i, 0, 0))]
            + [LATER] * len(after),
            out_specs=pl.BlockSpec((3, seq, pair), lambda i, *_: (0, 0, i)),
            scratch_shapes=[
                pltpu.VMEM((pair, seq), low),
                pltpu.VMEM((seq, pair), f32),
                pltpu.VMEM((seq, pair), f32),
            ],
        ),
        out_shape=sds((3, seq, width), low),
        compiler_params=params(28),
        cost_estimate=cost(pairs * 2 * half * 5 * 2 * 256, seq * width * 14, pairs * 2 * half),
        name="attend_backward",
    )(where, lengths, *from_far(qkv, qkv, qkv), upstream, *from_far(lse), *after)


def normalize(values):
    average = jnp.mean(values, axis=-1, keepdims=True)
    centred = values - average
    inverse = lax.rsqrt(jnp.mean(centred * centred, axis=-1, keepdims=True) + eps_norm)
    return centred * inverse, inverse


def pull_norm(scaled, unit, inverse):
    first = jnp.mean(scaled, axis=-1, keepdims=True)
    second = jnp.mean(scaled * unit, axis=-1, keepdims=True)
    return inverse * (scaled - first - unit * second)


def columns_of(values):
    return jnp.sum(values, axis=0, keepdims=True)


def pack_body(input_ref, output_ref, expand_ref, shrink_ref, attend_ref, feed_ref):
    width = input_ref.shape[2]
    part = expand_ref.shape[1] // 3
    for index in range(3):
        attend_ref[:, index * width : (index + 1) * width] = input_ref[index].astype(low)
        at = slice(index * part, (index + 1) * part)
        feed_ref[:, 2 * index * part : (2 * index + 1) * part] = expand_ref[:, at].astype(low)
        feed_ref[:, (2 * index + 1) * part : (2 * index + 2) * part] = shrink_ref[:, at].astype(low)
    attend_ref[:, 3 * width :] = output_ref[...].T.astype(low)


def pack(input_weight, output_weight, expand, shrink):
    rows, width = input_weight.shape[1:]
    hidden = expand.shape[1]
    return pl.pallas_call(
        pack_body,
        out_shape=[sds((rows, 4 * width), low), sds((rows, 2 * hidden), low)],
        compiler_params=params(6),
        cost_estimate=cost(rows * hidden, rows * hidden * 18),
        name="pack",
    )(*from_far(input_weight, output_weight, expand, shrink))


def prepare_body(x_ref, up_ref, vec_ref, h_ref, ht_ref, upt_ref):
    unit, _ = normalize(x_ref[...].astype(f32))
    h = (unit * vec_ref[0:1, :] + vec_ref[1:2, :]).astype(low)
    h_ref[...] = h
    ht_ref[...] = h.T
    upt_ref[...] = up_ref[...].T


def prepare(x, up, vectors, after):
    seq, depth = x.shape
    rows = pl.BlockSpec((2 * TILE, depth), lambda i: (i, 0))
    turned = pl.BlockSpec((depth, 2 * TILE), lambda i: (0, i))
    return pl.pallas_call(
        held_back(prepare_body, 3, len(after)),
        grid=(seq // (2 * TILE),),
        in_specs=[rows, rows, once(vectors.shape)] + [LATER] * len(after),
        out_specs=[rows, turned, turned],
        out_shape=[sds((seq, depth), low), far_away((depth, seq), low), far_away((depth, seq), low)],
        compiler_params=params(16),
        cost_estimate=cost(seq * depth * 10, seq * depth * 10),
        name="prepare",
    )(*from_far(x, up), vectors, *after)


def slot(halves, spot, at):
    first, second = halves
    inner = spot & 7
    return jnp.where(spot < 8, first[inner, :, at], second[inner, :, at])


def project_body(
    where_ref, spots_ref, h_ref, mine_a, mine_b, twin_a, twin_b, bias_ref, qkv_ref, wide_ref
):
    part = pl.program_id(0)
    rows = mine_a.shape[1]
    width = mine_a.shape[2] // 4
    groups = wide_ref.shape[1] // rows

    def collect(sources, index):
        at = slice(index * width, (index + 1) * width)
        for group in range(groups):
            pieces = [slot(sources[model % 2], spots_ref[model, group], at) for model in range(4)]
            wide_ref[0, group * rows : (group + 1) * rows, :] = jnp.concatenate(pieces, axis=1)

    for index in range(4):
        for core in range(2):

            @pl.when((part == index) & (where_ref[0] == core))
            def _(index=index, core=core):
                mine, twin = (mine_a, mine_b), (twin_a, twin_b)
                collect((mine, twin) if core == 0 else (twin, mine), index)

    for index in range(3):

        @pl.when(part == index)
        def _(index=index):
            out = mm(h_ref[...], wide_ref[0])
            if index != 1:
                at = slice(index // 2 * width, (index // 2 + 1) * width)
                bias = jnp.concatenate([bias_ref[model : model + 1, at] for model in range(4)], axis=1)
                out = out + bias
            qkv_ref[...] = out.astype(low)


def project(where, spots, h, halves, bias, after):
    seq, depth = h.shape
    return pl.pallas_call(
        held_back(project_body, 8, len(after)),
        grid_spec=pltpu.PrefetchScalarGridSpec(
            num_scalar_prefetch=2,
            grid=(4,),
            in_specs=[
                once((seq, depth)),
                *[once(halves[0].shape)] * 4,
                once(bias.shape),
            ]
            + [LATER] * len(after),
            out_specs=[
                pl.BlockSpec((seq, depth), lambda i, *_: (0, jnp.minimum(i, 2))),
                pl.BlockSpec((1, depth, depth), lambda i, *_: (i, 0, 0)),
            ],
        ),
        out_shape=[far_away((seq, 3 * depth), low), far_away((4, depth, depth), low)],
        compiler_params=params(24),
        cost_estimate=cost(2 * seq * depth * depth * 3, seq * depth * 16),
        name="project",
    )(where, spots, h, *halves, bias, *after)


def attend_out_body(o_ref, w_ref, x_ref, vec_ref, middle_ref, h_ref, ht_ref):
    middle = x_ref[...].astype(f32) + mm_nt(o_ref[...], w_ref[0]) + vec_ref[4:5, :]
    middle_ref[...] = middle.astype(low)
    unit, _ = normalize(middle)
    h = (unit * vec_ref[2:3, :] + vec_ref[3:4, :]).astype(low)
    h_ref[...] = h
    ht_ref[...] = h.T


def attend_out(o, wide, x, vectors):
    seq, depth = x.shape
    rows = pl.BlockSpec((TILE, depth), lambda i: (i, 0))
    turned = pl.BlockSpec((depth, TILE), lambda i: (0, i))
    return pl.pallas_call(
        attend_out_body,
        grid=(seq // TILE,),
        in_specs=[
            rows,
            pl.BlockSpec((1, depth, depth), lambda i: (3, 0, 0)),
            rows,
            once(vectors.shape),
        ],
        out_specs=[rows, rows, turned],
        out_shape=[sds((seq, depth), low), sds((seq, depth), low), sds((depth, seq), low)],
        compiler_params=params(14),
        cost_estimate=cost(2 * seq * depth * depth, seq * depth * 14),
        name="attend_out",
    )(o, *from_far(wide, x), vectors)


def feed_body(
    where_ref,
    spots_ref,
    h2_ref,
    h2t_ref,
    up_ref,
    upt_ref,
    mine_a,
    mine_b,
    twin_a,
    twin_b,
    bias_ref,
    middle_ref,
    vec_ref,
    block_ref,
    back_ref,
    keep_ref,
    send_ref,
    bias_grad_ref,
    out_ref,
    sum_ref,
    wide_ref,
    act_ref,
    pre_ref,
):
    step = pl.program_id(0)
    side = lax.rem(step, 2)
    models = [where_ref[1] ^ (2 * side + core) for core in range(2)]
    rows = mine_a.shape[1]
    part = mine_a.shape[2] // 2
    groups = wide_ref.shape[0] // rows

    @pl.when(step == 0)
    def _():
        out_ref[...] = middle_ref[...].astype(f32) + vec_ref[5:6, :]
        sum_ref[...] = jnp.zeros_like(sum_ref)

    for group in range(groups):
        at = slice(group * rows, (group + 1) * rows)
        own = slot((mine_a, mine_b), spots_ref[models[0], group], slice(None))
        other = slot((twin_a, twin_b), spots_ref[models[1], group], slice(None))
        wide_ref[at, :part] = own[:, :part]
        wide_ref[at, part : 2 * part] = other[:, :part]
        wide_ref[at, 2 * part : 3 * part] = own[:, part:]
        wide_ref[at, 3 * part :] = other[:, part:]

    expand = wide_ref[:, : 2 * part]
    shrink = wide_ref[:, 2 * part :]
    first = step // 2 * part
    skip = bias_ref.shape[1] - bias_grad_ref.shape[1]
    bias = jnp.concatenate(
        [bias_ref[pl.ds(model, 1), pl.ds(pl.multiple_of(skip + first, 128), part)] for model in models],
        axis=1,
    )
    sums = jnp.zeros((1, 2 * part), f32)
    for tile in range(h2_ref.shape[0] // TILE):
        at = slice(tile * TILE, (tile + 1) * TILE)
        u = mm(h2_ref[at, :], expand) + bias
        square = u * u
        th = jnp.tanh(u * (GELU_A + GELU_B * square))
        gate = 0.5 * th + 0.5
        slope = gate + (gate * (1.0 - gate)) * (u * (2.0 * GELU_A + (6.0 * GELU_B) * square))
        pre = (mm(up_ref[at, :], shrink) * slope).astype(low)
        act_ref[at, :] = (u * gate).astype(low)
        pre_ref[at, :] = pre
        sums = sums + columns_of(pre.astype(f32))
    for core, model in enumerate(models):
        bias_grad_ref[pl.ds(model, 1), pl.ds(pl.multiple_of(first, 128), part)] = sums[
            :, core * part : (core + 1) * part
        ]
    out_ref[...] += mm_nt(act_ref[...], shrink)
    sum_ref[...] += mm_nt(pre_ref[...], expand)
    grad_expand = mm(h2t_ref[...], pre_ref[...]).astype(low)
    grad_shrink = mm(upt_ref[...], act_ref[...]).astype(low)
    for group in range(groups):
        at = slice(group * rows, (group + 1) * rows)
        own, other = spots_ref[models[0], group], spots_ref[models[1], group]
        keep_ref[own, :, :part] = grad_expand[at, :part]
        keep_ref[own, :, part:] = grad_shrink[at, :part]
        send_ref[other, :, :part] = grad_expand[at, part:]
        send_ref[other, :, part:] = grad_shrink[at, part:]

    @pl.when(step == pl.num_programs(0) - 1)
    def _():
        block_ref[...] = out_ref[...].astype(low)
        back_ref[...] = sum_ref[...].astype(low)


def feed(where, spots, h2, h2t, up, upt, halves, bias, middle, vectors):
    seq, depth = h2.shape
    half, rows, columns = halves[0].shape
    steps, part = 6, columns // 6
    half_piece = pl.BlockSpec((half, rows, 2 * part), lambda i, *_: (0, 0, i // 2))
    piece = pl.BlockSpec((2 * half, rows, 2 * part), lambda i, *_: (0, 0, i // 2))
    return pl.pallas_call(
        feed_body,
        grid_spec=pltpu.PrefetchScalarGridSpec(
            num_scalar_prefetch=2,
            grid=(steps,),
            in_specs=[
                once((seq, depth)),
                once((depth, seq)),
                once((seq, depth)),
                once((depth, seq)),
                *[half_piece] * 4,
                once(bias.shape),
                once((seq, depth)),
                once(vectors.shape),
            ],
            out_specs=[whole((seq, depth)), whole((seq, depth)), piece, piece, whole((4, 3 * part))],
            scratch_shapes=[
                pltpu.VMEM((seq, depth), f32),
                pltpu.VMEM((seq, depth), f32),
                pltpu.VMEM((depth, 4 * part), low),
                pltpu.VMEM((seq, 2 * part), low),
                pltpu.VMEM((seq, 2 * part), low),
            ],
        ),
        out_shape=[sds((seq, depth), low)] * 2
        + [sds((2 * half, rows, columns), low)] * 2
        + [sds((4, 3 * part), f32)],
        compiler_params=params(31),
        cost_estimate=cost(12 * seq * depth * steps * 2 * part, seq * depth * 40, seq * steps * part),
        name="feed",
    )(where, spots, h2, h2t, *from_far(up, upt), *halves, bias, middle, vectors)


def middle_back_body(
    where_ref,
    lengths_ref,
    back_ref,
    middle_ref,
    up_ref,
    o_ref,
    w_ref,
    vec_ref,
    grad_ref,
    mixture_ref,
    weight_ref,
    sums_ref,
    total_ref,
):
    step = pl.program_id(0)
    unit, inverse = normalize(middle_ref[...].astype(f32))
    back = back_ref[...].astype(f32)
    up = up_ref[...].astype(f32)
    grad = up + pull_norm(back * vec_ref[2:3, :], unit, inverse)
    rounded = grad.astype(low)
    grad_ref[...] = rounded
    row = step * grad.shape[0] + lax.broadcasted_iota(jnp.int32, grad.shape, 0)
    length = lengths_ref[where_ref[2]]
    mixture_ref[...] = jnp.where(row < length, mm(rounded, w_ref[0]), 0.0).astype(low)
    share = mm(rounded.T, o_ref[...])
    sums = jnp.concatenate(
        [columns_of(back * unit), columns_of(back), columns_of(grad), columns_of(up)], axis=0
    )

    @pl.when(step == 0)
    def _():
        total_ref[...] = share
        sums_ref[...] = sums

    @pl.when(step > 0)
    def _():
        total_ref[...] += share
        sums_ref[...] += sums

    @pl.when(step == pl.num_programs(0) - 1)
    def _():
        weight_ref[...] = total_ref[...].astype(low)


def middle_back(where, lengths, back, middle, up, o, wide, vectors):
    seq, depth = middle.shape
    rows = pl.BlockSpec((2 * TILE, depth), lambda i, *_: (i, 0))
    return pl.pallas_call(
        middle_back_body,
        grid_spec=pltpu.PrefetchScalarGridSpec(
            num_scalar_prefetch=2,
            grid=(seq // (2 * TILE),),
            in_specs=[
                rows,
                rows,
                rows,
                rows,
                pl.BlockSpec((1, depth, depth), lambda i, *_: (3, 0, 0)),
                once(vectors.shape),
            ],
            out_specs=[rows, rows, whole((depth, depth)), whole((4, depth))],
            scratch_shapes=[pltpu.VMEM((depth, depth), f32)],
        ),
        out_shape=[
            sds((seq, depth), low),
            sds((seq, depth), low),
            sds((depth, depth), low),
            sds((4, depth), f32),
        ],
        compiler_params=params(24),
        cost_estimate=cost(4 * seq * depth * depth, seq * depth * 28),
        name="middle_back",
    )(where, lengths, back, middle, *from_far(up), o, *from_far(wide), vectors)


def input_grad_body(where_ref, spots_ref, ht_ref, back_ref, out_grad_ref, keep_ref, send_ref, sums_ref):
    part = pl.program_id(0)
    rows = keep_ref.shape[1]
    width = keep_ref.shape[2] // 4
    groups = ht_ref.shape[0] // rows

    def spread(targets, index, grad):
        at = slice(index * width, (index + 1) * width)
        for group in range(groups):
            for model in range(4):
                targets[model % 2][spots_ref[model, group], :, at] = grad[
                    group * rows : (group + 1) * rows, model * width : (model + 1) * width
                ]

    for index in range(4):

        @pl.when(part == index)
        def _(index=index):
            if index < 3:
                sums_ref[0] = columns_of(back_ref[0].astype(f32))
                grad = mm(ht_ref[...], back_ref[0]).astype(low)
            else:
                grad = out_grad_ref[...]
            for core in range(2):

                @pl.when(where_ref[0] == core)
                def _(core=core):
                    spread((keep_ref, send_ref) if core == 0 else (send_ref, keep_ref), index, grad)


def input_grad(where, spots, ht, back, out_grad, slots, rows, after):
    depth, seq = ht.shape
    shape = (slots, rows, 4 * (depth // 4))
    return pl.pallas_call(
        held_back(input_grad_body, 5, len(after)),
        grid_spec=pltpu.PrefetchScalarGridSpec(
            num_scalar_prefetch=2,
            grid=(4,),
            in_specs=[
                once((depth, seq)),
                pl.BlockSpec((1, seq, depth), lambda i, *_: (jnp.minimum(i, 2), 0, 0)),
                once((depth, depth)),
            ]
            + [LATER] * len(after),
            out_specs=[
                whole(shape),
                whole(shape),
                pl.BlockSpec((1, 1, depth), lambda i, *_: (jnp.minimum(i, 2), 0, 0)),
            ],
        ),
        out_shape=[sds(shape, low), sds(shape, low), sds((3, 1, depth), f32)],
        compiler_params=params(24),
        cost_estimate=cost(6 * seq * depth * depth, seq * depth * 14),
        name="input_grad",
    )(where, spots, *from_far(ht), back, out_grad, *after)


def token_back_body(
    back_ref, w_ref, x_ref, grad_ref, vec_ref, middle_ref, head_ref, bias_ref, token_ref, sums_ref
):
    step = pl.program_id(0)
    back = mm_nt(back_ref[0], w_ref[0]) + mm_nt(back_ref[1], w_ref[1]) + mm_nt(back_ref[2], w_ref[2])
    unit, inverse = normalize(x_ref[...].astype(f32))
    grad = grad_ref[...].astype(f32)
    token_ref[...] = (grad + pull_norm(back * vec_ref[0:1, :], unit, inverse)).astype(low)
    sums = jnp.concatenate([columns_of(back * unit), columns_of(back)], axis=0)

    @pl.when(step == 0)
    def _():
        sums_ref[:2] = sums
        sums_ref[2:6] = middle_ref[...]
        sums_ref[6:7] = head_ref[0]
        sums_ref[7:8] = head_ref[2]
        sums_ref[8:] = bias_ref[...]

    @pl.when(step > 0)
    def _():
        sums_ref[:2] += sums


def token_back(back, wide, x, grad, vectors, sums, after):
    seq, depth = x.shape
    rows = pl.BlockSpec((TILE, depth), lambda i: (i, 0))
    return pl.pallas_call(
        held_back(token_back_body, 8, len(after)),
        grid=(seq // TILE,),
        in_specs=[
            pl.BlockSpec((3, TILE, depth), lambda i: (0, i, 0)),
            pl.BlockSpec((3, depth, depth), lambda i: (0, 0, 0)),
            rows,
            rows,
            once(vectors.shape),
            *[once(array.shape) for array in sums],
        ]
        + [LATER] * len(after),
        out_specs=[rows, whole((12, depth))],
        out_shape=[sds((seq, depth), low), sds((12, depth), f32)],
        compiler_params=params(24),
        cost_estimate=cost(6 * seq * depth * depth, seq * depth * 16),
        name="token_back",
    )(back, *from_far(wide, x), grad, vectors, *sums, *after)


CORE_ORDERS = ((4, 3, 2, 1), (3, 4, 1, 2))
STAGES = 4


def cube_permute(values, stage):
    pairs = [(device, device ^ (1 << CORE_ORDERS[device & 1][stage])) for device in range(32)]
    return lax.ppermute(values, ("dp", "mp"), pairs)


def bit_permute(values, bit):
    return lax.ppermute(values, ("dp", "mp"), [(device, device ^ (1 << bit)) for device in range(32)])


def place(distance, core):
    spots = [
        sum(((distance >> bit) & 1) << step for step, bit in enumerate(order)) for order in CORE_ORDERS
    ]
    return jnp.where(core == 0, spots[0], spots[1])


def joined(held, arrived):
    return jnp.concatenate([held, arrived], axis=0)


def leaving(parts, stage):
    half = 1 << stage
    return sum(part[half:].astype(f32) for part in parts).astype(low)


def staying(parts, stage):
    return [part[: 1 << stage] for part in parts]


def summed(parts):
    return sum(part[0].astype(f32) for part in parts)


def cube_sum(values, bits=range(5)):
    for bit in bits:
        values = values + bit_permute(values, bit)
    return values


def adam_parts(weight, gradient, first_old, second_old, factor, step_rate):
    scaled = gradient * factor
    moment = beta_one * first_old + (1.0 - beta_one) * scaled
    square = beta_two * second_old + (1.0 - beta_two) * scaled * scaled
    spread = jnp.sqrt(square * (1.0 / (1.0 - beta_two**STEP)))
    ratio = moment * (1.0 / (1.0 - beta_one**STEP)) / (spread + adam_eps)
    return moment, square, weight - step_rate * (ratio + decay * weight)


def optimize_body(where_ref, owned_ref, vector_ref, attend_ref, feed_ref, *refs):
    state, outs = refs[:21], refs[21:]
    vectors = vector_ref[...]
    total = owned_ref[0:1, 0:1] + jnp.sum(vectors * vectors)
    norm = jnp.sqrt(total)
    factor = clip_norm / jnp.maximum(norm, clip_norm)
    outs[0][...] = norm
    width = state[0].shape[2]
    part = state[6].shape[1] // 3

    def update(param, at, gradient, step_rate):
        weight, first, second = (ref[at] for ref in state[3 * param : 3 * param + 3])
        results = adam_parts(weight, gradient, first, second, factor, step_rate)
        for ref, result in zip(outs[1 + 3 * param : 4 + 3 * param], results):
            ref[at] = result

    for index in range(3):
        update(0, (index,), attend_ref[:, index * width : (index + 1) * width], rate)
    update(1, (...,), attend_ref[:, 3 * width :].T, rate)
    for index in range(3):
        at = (slice(None), slice(index * part, (index + 1) * part))
        first = 2 * index * part
        update(2, at, feed_ref[:, first : first + part], rate)
        update(3, at, feed_ref[:, first + part : first + 2 * part], rate)
    update(4, (...,), vectors[:6], vector_rate)
    model = where_ref[2]
    head = jnp.zeros((2, width), f32)
    for index in range(4):
        head = head + jnp.where(model == index, vectors[6:8, index * width : (index + 1) * width], 0.0)
    update(5, (...,), head, vector_rate)
    update(6, (...,), vector_ref[pl.ds(8 + model, 1), :], vector_rate)


def optimize(where, owned, vector_total, attend_total, feed_total, state):
    shapes = [sds(group[0].shape, f32) for group in state for _ in range(3)]
    arrays = [array for group in state for array in group]
    return pl.pallas_call(
        optimize_body,
        in_specs=[pl.BlockSpec(memory_space=pltpu.SMEM)]
        + [pl.BlockSpec(memory_space=pltpu.VMEM)] * (4 + len(arrays)),
        out_shape=[sds((1, 1), f32)] + shapes,
        compiler_params=params(20),
        cost_estimate=cost(4e6, 8e6),
        name="optimize",
    )(where, owned, vector_total, attend_total, feed_total, *arrays)


def shards(
    tokens,
    cotangent,
    lengths,
    input_weight,
    output_weight,
    expand_weight,
    shrink_weight,
    layer_vectors,
    head_bias,
    expand_bias,
    first_input,
    first_output,
    first_expand,
    first_shrink,
    first_vectors,
    first_head,
    first_bias,
    second_input,
    second_output,
    second_expand,
    second_shrink,
    second_vectors,
    second_head,
    second_bias,
):
    dp_count = lax.axis_size("dp")
    mp_count = lax.axis_size("mp")
    cube = dp_count == 8 and mp_count == 4
    rows = input_weight.shape[0]
    width = input_weight.shape[2]
    hidden = expand_weight.shape[1]
    seq, depth = tokens.shape
    part = hidden // 3
    model_index = lax.axis_index("mp")
    me = lax.axis_index("dp") * mp_count + model_index

    attend_shard, feed_shard = pack(
        input_weight.transpose(1, 0, 2), output_weight, expand_weight, shrink_weight.T
    )
    bias_shard = jnp.concatenate([head_bias.reshape(1, 2 * width), expand_bias[None]], axis=1)

    bias_full = jnp.where(jnp.arange(4)[:, None] == model_index, bias_shard, 0.0)
    if cube:
        core, near = me & 1, model_index
        devices = jnp.arange(32).reshape(8, 4).T
        spots = place(devices ^ me, devices & 1).astype(jnp.int32)
    else:
        core = near = jnp.zeros((), jnp.int32)
        spots = (jnp.arange(4)[:, None] // 2 * 8 + jnp.arange(8)[None]).astype(jnp.int32)
    where = jnp.stack([core, near, model_index]).astype(jnp.int32)

    if cube:
        held = attend_shard[None]
        arrived = cube_permute(held, 0)
        bias_full = bias_full + bit_permute(bias_full, 0)
        held = joined(held, arrived)
        arrived = cube_permute(held, 1)
        normed, normed_t, upstream_t = prepare(tokens, cotangent, layer_vectors, (held,))
        bias_full = bias_full + bit_permute(bias_full, 1)
        held, feed_shard, normed, bias_full, spots, where = lax.optimization_barrier(
            (held, feed_shard, normed, bias_full, spots, where)
        )
        held = joined(held, arrived)
        feed_held = feed_shard[None]
        arrived, far_feed = cube_permute(held, 2), cube_permute(feed_held, 0)
        held = joined(held, arrived)
        feed_held = joined(feed_held, far_feed)
        held, feed_held = lax.optimization_barrier((held, feed_held))
        far, far_feed = cube_permute(held, 3), cube_permute(feed_held, 1)
        twin = bit_permute(held, 0)
        feed_held = joined(feed_held, far_feed)
        far, feed_held = lax.optimization_barrier((far, feed_held))
        attend_halves = (held, far, twin, bit_permute(far, 0))
        arrived = cube_permute(feed_held, 2)
        qkv, wide = project(where, spots, normed, attend_halves, bias_full, ())
        feed_held, qkv = lax.optimization_barrier((feed_held, qkv))
        feed_held = joined(feed_held, arrived)
        far, twin = cube_permute(feed_held, 3), bit_permute(feed_held, 0)
        mixture, log_totals = attend_forward(where, lengths, qkv, (feed_held,))
        middle, hidden_in, hidden_t = attend_out(mixture, wide, tokens, layer_vectors)
        far, hidden_in = lax.optimization_barrier((far, hidden_in))
        feed_halves = (feed_held, far, twin, bit_permute(far, 0))
    else:

        def planes(shard):
            full = lax.all_gather(lax.all_gather(shard, "dp", axis=0, tiled=True), "mp", axis=0)
            full = full.reshape(2, 2, 8, depth // 8, shard.shape[1]).transpose(1, 0, 2, 3, 4)
            return tuple(full.reshape(4, 8, depth // 8, shard.shape[1]))

        normed, normed_t, upstream_t = prepare(tokens, cotangent, layer_vectors, ())
        bias_full = lax.psum(bias_full, "mp")
        qkv, wide = project(where, spots, normed, planes(attend_shard), bias_full, ())
        mixture, log_totals = attend_forward(where, lengths, qkv, ())
        middle, hidden_in, hidden_t = attend_out(mixture, wide, tokens, layer_vectors)
        feed_halves = planes(feed_shard)
    block_out, back, keep_feed, send_feed, bias_grad = feed(
        where,
        spots,
        hidden_in,
        hidden_t,
        cotangent,
        upstream_t,
        feed_halves,
        bias_full,
        middle,
        layer_vectors,
    )
    middle_grad, mixture_grad, output_grad, middle_sums = middle_back(
        where, lengths, back, middle, cotangent, mixture, wide, layer_vectors
    )
    if cube:
        feed_parts = [keep_feed, bit_permute(send_feed, 0)]
        keep_feed, mixture_grad = lax.optimization_barrier((keep_feed, mixture_grad))
        feed_parts[0] = keep_feed
        away = leaving(feed_parts, 3)
        packed_grad = attend_backward(where, lengths, qkv, mixture_grad, log_totals, (away,))
        feed_parts = staying(feed_parts, 3) + [cube_permute(away, 3)]
        feed_parts[0], packed_grad = lax.optimization_barrier((feed_parts[0], packed_grad))
        away = leaving(feed_parts, 2)
        keep_attend, send_attend, head_sums = input_grad(
            where, spots, normed_t, packed_grad, output_grad, 16, depth // 8, (away,)
        )
        feed_parts = staying(feed_parts, 2) + [cube_permute(away, 2)]
        feed_parts[-1], send_attend = lax.optimization_barrier((feed_parts[-1], send_attend))
        twin_b, twin_a = bit_permute(send_attend[8:], 0), bit_permute(send_attend[:8], 0)
        away = (keep_attend[8:].astype(f32) + twin_b.astype(f32)).astype(low)
        attend_parts = [keep_attend[:8], twin_a, cube_permute(away, 3)]
        feed_away = leaving(feed_parts, 1)
        token_grad, vector_total = token_back(
            packed_grad,
            wide,
            tokens,
            middle_grad,
            layer_vectors,
            (middle_sums, head_sums, bias_grad),
            (away, feed_away),
        )
    else:
        packed_grad = attend_backward(where, lengths, qkv, mixture_grad, log_totals, ())
        keep_attend, send_attend, head_sums = input_grad(
            where, spots, normed_t, packed_grad, output_grad, 16, depth // 8, ()
        )
        token_grad, vector_total = token_back(
            packed_grad,
            wide,
            tokens,
            middle_grad,
            layer_vectors,
            (middle_sums, head_sums, bias_grad),
            (),
        )

    if cube:

        def behind(value, parts):
            first, value = lax.optimization_barrier((parts[0], value))
            return value, [first] + parts[1:]

        feed_parts = staying(feed_parts, 1) + [cube_permute(feed_away, 1)]
        vector_total = cube_sum(vector_total, (0, 1))
        vector_total, attend_parts = behind(vector_total, attend_parts)
        away = leaving(attend_parts, 2)
        attend_parts = staying(attend_parts, 2) + [cube_permute(away, 2)]
        away, vector_total = lax.optimization_barrier((away, vector_total))
        away, feed_parts = behind(away, feed_parts)
        away = leaving(feed_parts, 0)
        feed_parts = staying(feed_parts, 0) + [cube_permute(away, 0)]
        vector_total = cube_sum(vector_total, (2,))
        vector_total, attend_parts = behind(vector_total, attend_parts)
        away = leaving(attend_parts, 1)
        attend_parts = staying(attend_parts, 1) + [cube_permute(away, 1)]
        away, vector_total = lax.optimization_barrier((away, vector_total))
        vector_total = cube_sum(vector_total, (3,))
        feed_total = summed(feed_parts)
        feed_squares = jnp.sum(feed_total * feed_total)
        vector_total, feed_squares = lax.optimization_barrier((vector_total, feed_squares))
        vector_total, attend_parts = behind(vector_total, attend_parts)
        away = leaving(attend_parts, 0)
        attend_parts = staying(attend_parts, 0) + [cube_permute(away, 0)]
        away, vector_total = lax.optimization_barrier((away, vector_total))
        vector_total = cube_sum(vector_total, (4,))
        vector_total, attend_parts = behind(vector_total, attend_parts)
        attend_total = summed(attend_parts)
    else:

        def own_block(keep, send):
            full = jnp.stack([keep, send]).reshape(2, 2, 8, depth // 8, keep.shape[2])
            full = full.transpose(1, 0, 2, 3, 4).reshape(4, depth, keep.shape[2])
            full = lax.psum_scatter(full, "mp", scatter_dimension=0, tiled=False)
            return lax.psum_scatter(full, "dp", scatter_dimension=0, tiled=True).astype(f32)

        attend_total = own_block(keep_attend, send_attend)
        feed_total = own_block(keep_feed, send_feed)
        vector_total = lax.psum(vector_total, ("dp", "mp"))
        feed_squares = jnp.sum(feed_total * feed_total)
    owned = jnp.full((8, 128), jnp.sum(attend_total * attend_total) + feed_squares, f32)
    owned = cube_sum(owned) if cube else lax.psum(owned, ("dp", "mp"))
    def turned(array):
        return array.transpose(1, 0, 2)

    state = (
        (turned(input_weight), turned(first_input), turned(second_input)),
        (output_weight, first_output, second_output),
        (expand_weight, first_expand, second_expand),
        (shrink_weight.T, first_shrink.T, second_shrink.T),
        (layer_vectors, first_vectors, second_vectors),
        (head_bias, first_head, second_head),
        (expand_bias[None], first_bias[None], second_bias[None]),
    )
    grad_norm, *updates = optimize(where, owned, vector_total, attend_total, feed_total, state)
    grad_norm = grad_norm[0, 0]
    moment_input, square_input, updated_input = (turned(array) for array in updates[:3])
    moment_output, square_output, updated_output = updates[3:6]
    moment_expand, square_expand, updated_expand = updates[6:9]
    moment_shrink, square_shrink, updated_shrink = (array.T for array in updates[9:12])
    moment_vectors, square_vectors, updated_vectors = updates[12:15]
    moment_head, square_head, updated_head = updates[15:18]
    moment_bias, square_bias, updated_bias = (array[0] for array in updates[18:])
    return (
        block_out,
        token_grad,
        grad_norm,
        moment_input,
        square_input,
        updated_input,
        moment_output,
        square_output,
        updated_output,
        moment_expand,
        square_expand,
        updated_expand,
        moment_shrink,
        square_shrink,
        updated_shrink,
        moment_vectors,
        square_vectors,
        updated_vectors,
        moment_head,
        square_head,
        updated_head,
        moment_bias,
        square_bias,
        updated_bias,
    )


def solution(mesh):
    in_specs = (
        P(("dp", "mp"), None),
        P(("dp", "mp"), None),
        P("dp"),
        P("dp", None, "mp"),
        P("mp", "dp"),
        P("dp", "mp"),
        P("mp", "dp"),
        P(),
        P(None, "mp"),
        P("mp"),
        P("dp", None, "mp"),
        P("mp", "dp"),
        P("dp", "mp"),
        P("mp", "dp"),
        P(),
        P(None, "mp"),
        P("mp"),
        P("dp", None, "mp"),
        P("mp", "dp"),
        P("dp", "mp"),
        P("mp", "dp"),
        P(),
        P(None, "mp"),
        P("mp"),
    )
    out_specs = (
        P(("dp", "mp"), None),
        P(("dp", "mp"), None),
        P(),
        P("dp", None, "mp"),
        P("dp", None, "mp"),
        P("dp", None, "mp"),
        P("mp", "dp"),
        P("mp", "dp"),
        P("mp", "dp"),
        P("dp", "mp"),
        P("dp", "mp"),
        P("dp", "mp"),
        P("mp", "dp"),
        P("mp", "dp"),
        P("mp", "dp"),
        P(),
        P(),
        P(),
        P(None, "mp"),
        P(None, "mp"),
        P(None, "mp"),
        P("mp"),
        P("mp"),
        P("mp"),
    )
    return jax.shard_map(shards, mesh=mesh, in_specs=in_specs, out_specs=out_specs, check_vma=False)
```

```python
import functools
import jax
import jax.numpy as jnp
from jax import lax
from jax.experimental import pallas as pl
from jax.experimental.pallas import tpu as pltpu
from jax.sharding import PartitionSpec as P

HEAD_DIM = 64
TILE = 256
STEP = 10

eps_norm = 1e-05
clip_norm = 1.0
beta_one = 0.9
beta_two = 0.999
adam_eps = 1e-08
rate = 0.05
vector_rate = 0.5
decay = 0.01
excluded = -1e30
low = jnp.bfloat16
f32 = jnp.float32
GELU_A = 0.7978845608028654
GELU_B = GELU_A * 0.044715


def params(limit_mib, **kw):
    return pltpu.CompilerParams(vmem_limit_bytes=limit_mib * 1024 * 1024, **kw)


def cost(flops, moved, special=0):
    return pl.CostEstimate(flops=int(flops), bytes_accessed=int(moved), transcendentals=int(special))


def mm(a, b):
    return jnp.dot(a, b, preferred_element_type=f32)


def mm_nt(a, b):
    return lax.dot_general(a, b, (((1,), (1,)), ((), ())), preferred_element_type=f32)


def whole(shape):
    zeros = (0,) * len(shape)
    return pl.BlockSpec(shape, lambda *_: zeros)


def once(shape):
    zeros = (0,) * len(shape)
    return pl.BlockSpec(shape, lambda *_: zeros, pipeline_mode=pl.Buffered(1))


def held_back(body, first, count):
    def run(*refs):
        return body(*refs[:first], *refs[first + count :])

    return run


LATER = pl.BlockSpec(memory_space=pl.ANY)


def far_away(shape, dtype):
    return pltpu.HBM(shape, dtype)


def from_far(*arrays):
    return [pltpu.with_memory_space_constraint(array, pltpu.HBM) for array in arrays]


def sds(shape, dtype):
    return jax.ShapeDtypeStruct(shape, dtype)


def live_blocks(length, count, body):
    for blocks in range(1, count + 1):
        low_end = (blocks - 1) * TILE
        high_end = blocks * TILE
        @pl.when((length > low_end) & (length <= high_end))
        def _(blocks=blocks):
            body(length, blocks)


PAIR = 2 * HEAD_DIM


def span(block):
    return slice(block * TILE, (block + 1) * TILE)


def both_heads(values):
    lane = lax.broadcasted_iota(jnp.int32, values.shape, 1)
    none = jnp.zeros_like(values)
    return jnp.concatenate(
        [jnp.where(lane < HEAD_DIM, values, none), jnp.where(lane >= HEAD_DIM, values, none)], axis=0
    )


def causal_mask():
    key_id = lax.broadcasted_iota(jnp.int32, (TILE, 2 * TILE), 0)
    query_id = lax.broadcasted_iota(jnp.int32, (TILE, 2 * TILE), 1) & (TILE - 1)
    return key_id <= query_id


def forward_body(where_ref, lengths_ref, q_ref, k_ref, v_ref, o_ref, lse_ref, vt_ref):
    seq = q_ref.shape[0]
    vt_ref[...] = v_ref[...].T
    causal = causal_mask()

    def run(length, blocks):
        def scores(b):
            q = q_ref[span(b), :] * jnp.asarray(HEAD_DIM**-0.5, low)
            return mm_nt(k_ref[: (b + 1) * TILE, :], both_heads(q))

        now = scores(0)
        for b in range(blocks):
            start, stop = b * TILE, (b + 1) * TILE
            later = scores(b + 1) if b + 1 < blocks else None
            last = jnp.where(causal, now[start:, :], excluded)
            top = jnp.max(last, axis=0, keepdims=True)
            if b:
                top = jnp.maximum(top, jnp.max(now[:start], axis=0, keepdims=True))
            p = jnp.exp(last - top)
            total = jnp.sum(p, axis=0, keepdims=True)
            pb = p.astype(low)
            if b:
                pf = jnp.exp(now[:start] - top)
                total = total + jnp.sum(pf, axis=0, keepdims=True)
                pb = jnp.concatenate([pf.astype(low), pb], axis=0)
            inverse = 1.0 / total
            lse = top + jnp.log(total)
            outs = []
            for h in range(2):
                at = slice(h * TILE, (h + 1) * TILE)
                out = mm(vt_ref[h * HEAD_DIM : (h + 1) * HEAD_DIM, :stop], pb[:, at])
                outs.append(out * inverse[:, at])
                lse_ref[0, h : h + 1, start:stop] = lse[:, at]
            both = jnp.concatenate(outs, axis=0).T
            row = start + lax.broadcasted_iota(jnp.int32, both.shape, 0)
            o_ref[start:stop, :] = jnp.where(row < length, both, 0.0).astype(low)
            now = later
        if blocks * TILE < seq:
            o_ref[blocks * TILE :, :] = jnp.zeros((seq - blocks * TILE, PAIR), low)
            lse_ref[0, :, blocks * TILE :] = jnp.zeros((2, seq - blocks * TILE), f32)

    live_blocks(lengths_ref[where_ref[2]], seq // TILE, run)


def attend_forward(where, lengths, qkv, after):
    seq, width = qkv.shape[0], qkv.shape[1] // 3
    pair = 2 * HEAD_DIM
    pairs = width // pair
    half = seq * seq * 5 // 8
    spec = lambda part: pl.BlockSpec((seq, pair), lambda i, *_: (0, part * pairs + i))
    return pl.pallas_call(
        held_back(forward_body, 5, len(after)),
        grid_spec=pltpu.PrefetchScalarGridSpec(
            num_scalar_prefetch=2,
            grid=(pairs,),
            in_specs=[spec(0), spec(1), spec(2)] + [LATER] * len(after),
            out_specs=[
                pl.BlockSpec((seq, pair), lambda i, *_: (0, i)),
                pl.BlockSpec((1, 2, seq), lambda i, *_: (i, 0, 0)),
            ],
            scratch_shapes=[pltpu.VMEM((pair, seq), low)],
        ),
        out_shape=[sds((seq, width), low), far_away((pairs, 2, seq), f32)],
        compiler_params=params(20),
        cost_estimate=cost(pairs * 2 * half * 2 * 2 * 256, seq * width * 8, pairs * 2 * half),
        name="attend_forward",
    )(where, lengths, *from_far(qkv, qkv, qkv), *after)


def backward_body(where_ref, lengths_ref, q_ref, k_ref, v_ref, do_ref, lse_ref, out_ref, kt_ref, ksum, vsum):
    seq = q_ref.shape[0]
    scale = HEAD_DIM**-0.5
    kt_ref[...] = k_ref[...].T
    causal = causal_mask()

    def run(length, blocks):
        def scores(b):
            qq = both_heads(q_ref[span(b), :] * jnp.asarray(scale, low))
            uu = both_heads(do_ref[span(b), :])
            stop = (b + 1) * TILE
            return qq, uu, mm_nt(k_ref[:stop, :], qq), mm_nt(v_ref[:stop, :], uu)

        now = scores(blocks - 1)
        for b in reversed(range(blocks)):
            start, stop = b * TILE, (b + 1) * TILE
            later = scores(b - 1) if b else None
            qq, uu, s, dp = now
            lse = jnp.concatenate([lse_ref[0, 0:1, start:stop], lse_ref[0, 1:2, start:stop]], axis=1)
            p = jnp.exp(jnp.where(causal, s[start:], excluded) - lse)
            inner = jnp.sum(p * dp[start:], axis=0, keepdims=True)
            if b:
                pf = jnp.exp(s[:start] - lse)
                inner = inner + jnp.sum(pf * dp[:start], axis=0, keepdims=True)
            ds = (p * (dp[start:] - inner)).astype(low)
            pb = p.astype(low)
            if b:
                ds = jnp.concatenate([(pf * (dp[:start] - inner)).astype(low), ds], axis=0)
                pb = jnp.concatenate([pf.astype(low), pb], axis=0)
            dk, dv = mm(ds, qq), mm(pb, uu)
            if b == blocks - 1:
                ksum[:stop, :] = dk
                vsum[:stop, :] = dv
            else:
                ksum[:stop, :] += dk
                vsum[:stop, :] += dv
            dq = jnp.concatenate(
                [
                    mm(
                        kt_ref[h * HEAD_DIM : (h + 1) * HEAD_DIM, :stop],
                        ds[:, h * TILE : (h + 1) * TILE],
                    )
                    for h in range(2)
                ],
                axis=0,
            )
            out_ref[1, start:stop, :] = ksum[start:stop, :].astype(low)
            out_ref[2, start:stop, :] = vsum[start:stop, :].astype(low)
            out_ref[0, start:stop, :] = (dq.T * scale).astype(low)
            now = later
        if blocks * TILE < seq:
            rest = jnp.zeros((seq - blocks * TILE, PAIR), low)
            for part in range(3):
                out_ref[part, blocks * TILE :, :] = rest

    live_blocks(lengths_ref[where_ref[2]], seq // TILE, run)


def attend_backward(where, lengths, qkv, upstream, lse, after):
    seq, width = upstream.shape
    pair = 2 * HEAD_DIM
    pairs = width // pair
    half = seq * seq * 5 // 8
    spec = lambda part: pl.BlockSpec((seq, pair), lambda i, *_: (0, part * pairs + i))
    own = pl.BlockSpec((seq, pair), lambda i, *_: (0, i))
    return pl.pallas_call(
        held_back(backward_body, 7, len(after)),
        grid_spec=pltpu.PrefetchScalarGridSpec(
            num_scalar_prefetch=2,
            grid=(pairs,),
            in_specs=[spec(0), spec(1), spec(2), own, pl.BlockSpec((1, 2, seq), lambda i, *_: (i, 0, 0))]
            + [LATER] * len(after),
            out_specs=pl.BlockSpec((3, seq, pair), lambda i, *_: (0, 0, i)),
            scratch_shapes=[
                pltpu.VMEM((pair, seq), low),
                pltpu.VMEM((seq, pair), f32),
                pltpu.VMEM((seq, pair), f32),
            ],
        ),
        out_shape=sds((3, seq, width), low),
        compiler_params=params(28),
        cost_estimate=cost(pairs * 2 * half * 5 * 2 * 256, seq * width * 14, pairs * 2 * half),
        name="attend_backward",
    )(where, lengths, *from_far(qkv, qkv, qkv), upstream, *from_far(lse), *after)


def normalize(values):
    average = jnp.mean(values, axis=-1, keepdims=True)
    centred = values - average
    inverse = lax.rsqrt(jnp.mean(centred * centred, axis=-1, keepdims=True) + eps_norm)
    return centred * inverse, inverse


def pull_norm(scaled, unit, inverse):
    first = jnp.mean(scaled, axis=-1, keepdims=True)
    second = jnp.mean(scaled * unit, axis=-1, keepdims=True)
    return inverse * (scaled - first - unit * second)


def columns_of(values):
    return jnp.sum(values, axis=0, keepdims=True)


def pack_body(input_ref, output_ref, expand_ref, shrink_ref, attend_ref, feed_ref):
    width = input_ref.shape[2]
    part = expand_ref.shape[1] // 3
    for index in range(3):
        attend_ref[:, index * width : (index + 1) * width] = input_ref[index].astype(low)
        at = slice(index * part, (index + 1) * part)
        feed_ref[:, 2 * index * part : (2 * index + 1) * part] = expand_ref[:, at].astype(low)
        feed_ref[:, (2 * index + 1) * part : (2 * index + 2) * part] = shrink_ref[:, at].astype(low)
    attend_ref[:, 3 * width :] = output_ref[...].T.astype(low)


def pack(input_weight, output_weight, expand, shrink):
    rows, width = input_weight.shape[1:]
    hidden = expand.shape[1]
    return pl.pallas_call(
        pack_body,
        out_shape=[sds((rows, 4 * width), low), sds((rows, 2 * hidden), low)],
        compiler_params=params(6),
        cost_estimate=cost(rows * hidden, rows * hidden * 18),
        name="pack",
    )(*from_far(input_weight, output_weight, expand, shrink))


def prepare_body(x_ref, up_ref, vec_ref, h_ref, ht_ref, upt_ref):
    unit, _ = normalize(x_ref[...].astype(f32))
    h = (unit * vec_ref[0:1, :] + vec_ref[1:2, :]).astype(low)
    h_ref[...] = h
    ht_ref[...] = h.T
    upt_ref[...] = up_ref[...].T


def prepare(x, up, vectors, after):
    seq, depth = x.shape
    rows = pl.BlockSpec((2 * TILE, depth), lambda i: (i, 0))
    turned = pl.BlockSpec((depth, 2 * TILE), lambda i: (0, i))
    return pl.pallas_call(
        held_back(prepare_body, 3, len(after)),
        grid=(seq // (2 * TILE),),
        in_specs=[rows, rows, once(vectors.shape)] + [LATER] * len(after),
        out_specs=[rows, turned, turned],
        out_shape=[sds((seq, depth), low), far_away((depth, seq), low), far_away((depth, seq), low)],
        compiler_params=params(16),
        cost_estimate=cost(seq * depth * 10, seq * depth * 10),
        name="prepare",
    )(*from_far(x, up), vectors, *after)


def slot(halves, spot, at):
    first, second = halves
    inner = spot & 7
    return jnp.where(spot < 8, first[inner, :, at], second[inner, :, at])


def project_body(
    where_ref, spots_ref, h_ref, mine_a, mine_b, twin_a, twin_b, bias_ref, qkv_ref, wide_ref
):
    part = pl.program_id(0)
    rows = mine_a.shape[1]
    width = mine_a.shape[2] // 4
    groups = wide_ref.shape[1] // rows

    def collect(sources, index):
        at = slice(index * width, (index + 1) * width)
        for group in range(groups):
            pieces = [slot(sources[model % 2], spots_ref[model, group], at) for model in range(4)]
            wide_ref[0, group * rows : (group + 1) * rows, :] = jnp.concatenate(pieces, axis=1)

    for index in range(4):
        for core in range(2):

            @pl.when((part == index) & (where_ref[0] == core))
            def _(index=index, core=core):
                mine, twin = (mine_a, mine_b), (twin_a, twin_b)
                collect((mine, twin) if core == 0 else (twin, mine), index)

    for index in range(3):

        @pl.when(part == index)
        def _(index=index):
            out = mm(h_ref[...], wide_ref[0])
            if index != 1:
                at = slice(index // 2 * width, (index // 2 + 1) * width)
                bias = jnp.concatenate([bias_ref[model : model + 1, at] for model in range(4)], axis=1)
                out = out + bias
            qkv_ref[...] = out.astype(low)


def project(where, spots, h, halves, bias, after):
    seq, depth = h.shape
    return pl.pallas_call(
        held_back(project_body, 8, len(after)),
        grid_spec=pltpu.PrefetchScalarGridSpec(
            num_scalar_prefetch=2,
            grid=(4,),
            in_specs=[
                once((seq, depth)),
                *[once(halves[0].shape)] * 4,
                once(bias.shape),
            ]
            + [LATER] * len(after),
            out_specs=[
                pl.BlockSpec((seq, depth), lambda i, *_: (0, jnp.minimum(i, 2))),
                pl.BlockSpec((1, depth, depth), lambda i, *_: (i, 0, 0)),
            ],
        ),
        out_shape=[far_away((seq, 3 * depth), low), far_away((4, depth, depth), low)],
        compiler_params=params(24),
        cost_estimate=cost(2 * seq * depth * depth * 3, seq * depth * 16),
        name="project",
    )(where, spots, h, *halves, bias, *after)


def attend_out_body(o_ref, w_ref, x_ref, vec_ref, middle_ref, h_ref, ht_ref):
    middle = x_ref[...].astype(f32) + mm_nt(o_ref[...], w_ref[0]) + vec_ref[4:5, :]
    middle_ref[...] = middle.astype(low)
    unit, _ = normalize(middle)
    h = (unit * vec_ref[2:3, :] + vec_ref[3:4, :]).astype(low)
    h_ref[...] = h
    ht_ref[...] = h.T


def attend_out(o, wide, x, vectors):
    seq, depth = x.shape
    rows = pl.BlockSpec((TILE, depth), lambda i: (i, 0))
    turned = pl.BlockSpec((depth, TILE), lambda i: (0, i))
    return pl.pallas_call(
        attend_out_body,
        grid=(seq // TILE,),
        in_specs=[
            rows,
            pl.BlockSpec((1, depth, depth), lambda i: (3, 0, 0)),
            rows,
            once(vectors.shape),
        ],
        out_specs=[rows, rows, turned],
        out_shape=[sds((seq, depth), low), sds((seq, depth), low), sds((depth, seq), low)],
        compiler_params=params(14),
        cost_estimate=cost(2 * seq * depth * depth, seq * depth * 14),
        name="attend_out",
    )(o, *from_far(wide, x), vectors)


def feed_body(
    where_ref,
    spots_ref,
    h2_ref,
    h2t_ref,
    up_ref,
    upt_ref,
    mine_a,
    mine_b,
    twin_a,
    twin_b,
    bias_ref,
    middle_ref,
    vec_ref,
    block_ref,
    back_ref,
    keep_ref,
    send_ref,
    bias_grad_ref,
    out_ref,
    sum_ref,
    wide_ref,
    act_ref,
    pre_ref,
):
    step = pl.program_id(0)
    side = lax.rem(step, 2)
    models = [where_ref[1] ^ (2 * side + core) for core in range(2)]
    rows = mine_a.shape[1]
    part = mine_a.shape[2] // 2
    groups = wide_ref.shape[0] // rows

    @pl.when(step == 0)
    def _():
        out_ref[...] = middle_ref[...].astype(f32) + vec_ref[5:6, :]
        sum_ref[...] = jnp.zeros_like(sum_ref)

    for group in range(groups):
        at = slice(group * rows, (group + 1) * rows)
        own = slot((mine_a, mine_b), spots_ref[models[0], group], slice(None))
        other = slot((twin_a, twin_b), spots_ref[models[1], group], slice(None))
        wide_ref[at, :part] = own[:, :part]
        wide_ref[at, part : 2 * part] = other[:, :part]
        wide_ref[at, 2 * part : 3 * part] = own[:, part:]
        wide_ref[at, 3 * part :] = other[:, part:]

    expand = wide_ref[:, : 2 * part]
    shrink = wide_ref[:, 2 * part :]
    first = step // 2 * part
    skip = bias_ref.shape[1] - bias_grad_ref.shape[1]
    bias = jnp.concatenate(
        [bias_ref[pl.ds(model, 1), pl.ds(pl.multiple_of(skip + first, 128), part)] for model in models],
        axis=1,
    )
    sums = jnp.zeros((1, 2 * part), f32)
    for tile in range(h2_ref.shape[0] // TILE):
        at = slice(tile * TILE, (tile + 1) * TILE)
        u = mm(h2_ref[at, :], expand) + bias
        square = u * u
        th = jnp.tanh(u * (GELU_A + GELU_B * square))
        gate = 0.5 * th + 0.5
        slope = gate + (gate * (1.0 - gate)) * (u * (2.0 * GELU_A + (6.0 * GELU_B) * square))
        pre = (mm(up_ref[at, :], shrink) * slope).astype(low)
        act_ref[at, :] = (u * gate).astype(low)
        pre_ref[at, :] = pre
        sums = sums + columns_of(pre.astype(f32))
    for core, model in enumerate(models):
        bias_grad_ref[pl.ds(model, 1), pl.ds(pl.multiple_of(first, 128), part)] = sums[
            :, core * part : (core + 1) * part
        ]
    out_ref[...] += mm_nt(act_ref[...], shrink)
    sum_ref[...] += mm_nt(pre_ref[...], expand)
    grad_expand = mm(h2t_ref[...], pre_ref[...]).astype(low)
    grad_shrink = mm(upt_ref[...], act_ref[...]).astype(low)
    for group in range(groups):
        at = slice(group * rows, (group + 1) * rows)
        own, other = spots_ref[models[0], group], spots_ref[models[1], group]
        keep_ref[own, :, :part] = grad_expand[at, :part]
        keep_ref[own, :, part:] = grad_shrink[at, :part]
        send_ref[other, :, :part] = grad_expand[at, part:]
        send_ref[other, :, part:] = grad_shrink[at, part:]

    @pl.when(step == pl.num_programs(0) - 1)
    def _():
        block_ref[...] = out_ref[...].astype(low)
        back_ref[...] = sum_ref[...].astype(low)


def feed(where, spots, h2, h2t, up, upt, halves, bias, middle, vectors):
    seq, depth = h2.shape
    half, rows, columns = halves[0].shape
    steps, part = 6, columns // 6
    half_piece = pl.BlockSpec((half, rows, 2 * part), lambda i, *_: (0, 0, i // 2))
    piece = pl.BlockSpec((2 * half, rows, 2 * part), lambda i, *_: (0, 0, i // 2))
    return pl.pallas_call(
        feed_body,
        grid_spec=pltpu.PrefetchScalarGridSpec(
            num_scalar_prefetch=2,
            grid=(steps,),
            in_specs=[
                once((seq, depth)),
                once((depth, seq)),
                once((seq, depth)),
                once((depth, seq)),
                *[half_piece] * 4,
                once(bias.shape),
                once((seq, depth)),
                once(vectors.shape),
            ],
            out_specs=[whole((seq, depth)), whole((seq, depth)), piece, piece, whole((4, 3 * part))],
            scratch_shapes=[
                pltpu.VMEM((seq, depth), f32),
                pltpu.VMEM((seq, depth), f32),
                pltpu.VMEM((depth, 4 * part), low),
                pltpu.VMEM((seq, 2 * part), low),
                pltpu.VMEM((seq, 2 * part), low),
            ],
        ),
        out_shape=[sds((seq, depth), low)] * 2
        + [sds((2 * half, rows, columns), low)] * 2
        + [sds((4, 3 * part), f32)],
        compiler_params=params(31),
        cost_estimate=cost(12 * seq * depth * steps * 2 * part, seq * depth * 40, seq * steps * part),
        name="feed",
    )(where, spots, h2, h2t, *from_far(up, upt), *halves, bias, middle, vectors)


def middle_back_body(
    where_ref,
    lengths_ref,
    back_ref,
    middle_ref,
    up_ref,
    o_ref,
    w_ref,
    vec_ref,
    grad_ref,
    mixture_ref,
    weight_ref,
    sums_ref,
    total_ref,
):
    step = pl.program_id(0)
    unit, inverse = normalize(middle_ref[...].astype(f32))
    back = back_ref[...].astype(f32)
    up = up_ref[...].astype(f32)
    grad = up + pull_norm(back * vec_ref[2:3, :], unit, inverse)
    rounded = grad.astype(low)
    grad_ref[...] = rounded
    row = step * grad.shape[0] + lax.broadcasted_iota(jnp.int32, grad.shape, 0)
    length = lengths_ref[where_ref[2]]
    mixture_ref[...] = jnp.where(row < length, mm(rounded, w_ref[0]), 0.0).astype(low)
    share = mm(rounded.T, o_ref[...])
    sums = jnp.concatenate(
        [columns_of(back * unit), columns_of(back), columns_of(grad), columns_of(up)], axis=0
    )

    @pl.when(step == 0)
    def _():
        total_ref[...] = share
        sums_ref[...] = sums

    @pl.when(step > 0)
    def _():
        total_ref[...] += share
        sums_ref[...] += sums

    @pl.when(step == pl.num_programs(0) - 1)
    def _():
        weight_ref[...] = total_ref[...].astype(low)


def middle_back(where, lengths, back, middle, up, o, wide, vectors):
    seq, depth = middle.shape
    rows = pl.BlockSpec((2 * TILE, depth), lambda i, *_: (i, 0))
    return pl.pallas_call(
        middle_back_body,
        grid_spec=pltpu.PrefetchScalarGridSpec(
            num_scalar_prefetch=2,
            grid=(seq // (2 * TILE),),
            in_specs=[
                rows,
                rows,
                rows,
                rows,
                pl.BlockSpec((1, depth, depth), lambda i, *_: (3, 0, 0)),
                once(vectors.shape),
            ],
            out_specs=[rows, rows, whole((depth, depth)), whole((4, depth))],
            scratch_shapes=[pltpu.VMEM((depth, depth), f32)],
        ),
        out_shape=[
            sds((seq, depth), low),
            sds((seq, depth), low),
            sds((depth, depth), low),
            sds((4, depth), f32),
        ],
        compiler_params=params(24),
        cost_estimate=cost(4 * seq * depth * depth, seq * depth * 28),
        name="middle_back",
    )(where, lengths, back, middle, *from_far(up), o, *from_far(wide), vectors)


def input_grad_body(where_ref, spots_ref, ht_ref, back_ref, out_grad_ref, keep_ref, send_ref, sums_ref):
    part = pl.program_id(0)
    rows = keep_ref.shape[1]
    width = keep_ref.shape[2] // 4
    groups = ht_ref.shape[0] // rows

    def spread(targets, index, grad):
        at = slice(index * width, (index + 1) * width)
        for group in range(groups):
            for model in range(4):
                targets[model % 2][spots_ref[model, group], :, at] = grad[
                    group * rows : (group + 1) * rows, model * width : (model + 1) * width
                ]

    for index in range(4):

        @pl.when(part == index)
        def _(index=index):
            if index < 3:
                sums_ref[0] = columns_of(back_ref[0].astype(f32))
                grad = mm(ht_ref[...], back_ref[0]).astype(low)
            else:
                grad = out_grad_ref[...]
            for core in range(2):

                @pl.when(where_ref[0] == core)
                def _(core=core):
                    spread((keep_ref, send_ref) if core == 0 else (send_ref, keep_ref), index, grad)


def input_grad(where, spots, ht, back, out_grad, slots, rows, after):
    depth, seq = ht.shape
    shape = (slots, rows, 4 * (depth // 4))
    return pl.pallas_call(
        held_back(input_grad_body, 5, len(after)),
        grid_spec=pltpu.PrefetchScalarGridSpec(
            num_scalar_prefetch=2,
            grid=(4,),
            in_specs=[
                once((depth, seq)),
                pl.BlockSpec((1, seq, depth), lambda i, *_: (jnp.minimum(i, 2), 0, 0)),
                once((depth, depth)),
            ]
            + [LATER] * len(after),
            out_specs=[
                whole(shape),
                whole(shape),
                pl.BlockSpec((1, 1, depth), lambda i, *_: (jnp.minimum(i, 2), 0, 0)),
            ],
        ),
        out_shape=[sds(shape, low), sds(shape, low), sds((3, 1, depth), f32)],
        compiler_params=params(24),
        cost_estimate=cost(6 * seq * depth * depth, seq * depth * 14),
        name="input_grad",
    )(where, spots, *from_far(ht), back, out_grad, *after)


def token_back_body(
    back_ref, w_ref, x_ref, grad_ref, vec_ref, middle_ref, bias_ref, token_ref, sums_ref
):
    step = pl.program_id(0)
    back = mm_nt(back_ref[0], w_ref[0]) + mm_nt(back_ref[1], w_ref[1]) + mm_nt(back_ref[2], w_ref[2])
    unit, inverse = normalize(x_ref[...].astype(f32))
    grad = grad_ref[...].astype(f32)
    token_ref[...] = (grad + pull_norm(back * vec_ref[0:1, :], unit, inverse)).astype(low)
    sums = jnp.concatenate([columns_of(back * unit), columns_of(back)], axis=0)

    @pl.when(step == 0)
    def _():
        sums_ref[:2] = sums
        sums_ref[2:6] = middle_ref[...]
        sums_ref[6:8] = jnp.zeros((2, sums_ref.shape[1]), f32)
        sums_ref[8:] = bias_ref[...]

    @pl.when(step > 0)
    def _():
        sums_ref[:2] += sums


def token_back(back, wide, x, grad, vectors, sums, after):
    seq, depth = x.shape
    rows = pl.BlockSpec((TILE, depth), lambda i: (i, 0))
    return pl.pallas_call(
        held_back(token_back_body, 7, len(after)),
        grid=(seq // TILE,),
        in_specs=[
            pl.BlockSpec((3, TILE, depth), lambda i: (0, i, 0)),
            pl.BlockSpec((3, depth, depth), lambda i: (0, 0, 0)),
            rows,
            rows,
            once(vectors.shape),
            *[once(array.shape) for array in sums],
        ]
        + [LATER] * len(after),
        out_specs=[rows, whole((12, depth))],
        out_shape=[sds((seq, depth), low), sds((12, depth), f32)],
        compiler_params=params(24),
        cost_estimate=cost(6 * seq * depth * depth, seq * depth * 16),
        name="token_back",
    )(back, *from_far(wide, x), grad, vectors, *sums, *after)


CORE_ORDERS = ((4, 3, 2, 1), (3, 4, 1, 2))
STAGES = 4


def cube_permute(values, stage):
    pairs = [(device, device ^ (1 << CORE_ORDERS[device & 1][stage])) for device in range(32)]
    return lax.ppermute(values, ("dp", "mp"), pairs)


def bit_permute(values, bit):
    return lax.ppermute(values, ("dp", "mp"), [(device, device ^ (1 << bit)) for device in range(32)])


def place(distance, core):
    spots = [
        sum(((distance >> bit) & 1) << step for step, bit in enumerate(order)) for order in CORE_ORDERS
    ]
    return jnp.where(core == 0, spots[0], spots[1])


def joined(held, arrived):
    return jnp.concatenate([held, arrived], axis=0)


def leaving(parts, stage):
    half = 1 << stage
    return sum(part[half:].astype(f32) for part in parts).astype(low)


def staying(parts, stage):
    return [part[: 1 << stage] for part in parts]


def summed(parts):
    return sum(part[0].astype(f32) for part in parts)


def join_vectors(sums, head_sums):
    row = lax.broadcasted_iota(jnp.int32, sums.shape, 0)
    return jnp.where(row == 6, head_sums[0], jnp.where(row == 7, head_sums[2], sums))


def two_parts(values):
    high = lax.reduce_precision(values, 8, 7)
    rest = lax.reduce_precision(values - high, 8, 7)
    return jnp.concatenate([high, rest], axis=0).astype(low)


def one_part(parts):
    half = parts.shape[0] // 2
    return parts[:half].astype(f32) + parts[half:].astype(f32)


def with_rider(blocks, rider, send):
    count, rows, columns = blocks.shape
    parts = two_parts(rider)
    arrived = send(jnp.concatenate([blocks.reshape(count * rows, columns), parts], axis=0))
    total = one_part(parts) + one_part(arrived[count * rows :])
    return arrived[: count * rows].reshape(count, rows, columns), total


def cube_sum(values, bits=range(5)):
    for bit in bits:
        values = values + bit_permute(values, bit)
    return values


def adam_parts(weight, gradient, first_old, second_old, factor, step_rate):
    scaled = gradient * factor
    moment = beta_one * first_old + (1.0 - beta_one) * scaled
    square = beta_two * second_old + (1.0 - beta_two) * scaled * scaled
    spread = jnp.sqrt(square * (1.0 / (1.0 - beta_two**STEP)))
    ratio = moment * (1.0 / (1.0 - beta_one**STEP)) / (spread + adam_eps)
    return moment, square, weight - step_rate * (ratio + decay * weight)


def optimize_body(where_ref, owned_ref, vector_ref, attend_ref, feed_ref, *refs):
    state, outs = refs[:21], refs[21:]
    vectors = vector_ref[...]
    total = owned_ref[0:1, 0:1] + jnp.sum(vectors * vectors)
    norm = jnp.sqrt(total)
    factor = clip_norm / jnp.maximum(norm, clip_norm)
    outs[0][...] = norm
    width = state[0].shape[2]
    part = state[6].shape[1] // 3

    def update(param, at, gradient, step_rate):
        weight, first, second = (ref[at] for ref in state[3 * param : 3 * param + 3])
        results = adam_parts(weight, gradient, first, second, factor, step_rate)
        for ref, result in zip(outs[1 + 3 * param : 4 + 3 * param], results):
            ref[at] = result

    for index in range(3):
        update(0, (index,), attend_ref[:, index * width : (index + 1) * width], rate)
    update(1, (...,), attend_ref[:, 3 * width :].T, rate)
    for index in range(3):
        at = (slice(None), slice(index * part, (index + 1) * part))
        first = 2 * index * part
        update(2, at, feed_ref[:, first : first + part], rate)
        update(3, at, feed_ref[:, first + part : first + 2 * part], rate)
    update(4, (...,), vectors[:6], vector_rate)
    model = where_ref[2]
    head = jnp.zeros((2, width), f32)
    for index in range(4):
        head = head + jnp.where(model == index, vectors[6:8, index * width : (index + 1) * width], 0.0)
    update(5, (...,), head, vector_rate)
    bias = vector_ref[pl.ds(8 + model, 1), :]
    bias = jnp.concatenate([bias[:, at : at + 128] for at in range(0, bias.shape[1], 128)], axis=0)
    update(6, (...,), bias, vector_rate)


def optimize(where, owned, vector_total, attend_total, feed_total, state):
    shapes = [sds(group[0].shape, f32) for group in state for _ in range(3)]
    arrays = [array for group in state for array in group]
    return pl.pallas_call(
        optimize_body,
        in_specs=[pl.BlockSpec(memory_space=pltpu.SMEM)]
        + [pl.BlockSpec(memory_space=pltpu.VMEM)] * (4 + len(arrays)),
        out_shape=[sds((1, 1), f32)] + shapes,
        compiler_params=params(20),
        cost_estimate=cost(4e6, 8e6),
        name="optimize",
    )(where, owned, vector_total, attend_total, feed_total, *from_far(*arrays))


def shards(
    tokens,
    cotangent,
    lengths,
    input_weight,
    output_weight,
    expand_weight,
    shrink_weight,
    layer_vectors,
    head_bias,
    expand_bias,
    first_input,
    first_output,
    first_expand,
    first_shrink,
    first_vectors,
    first_head,
    first_bias,
    second_input,
    second_output,
    second_expand,
    second_shrink,
    second_vectors,
    second_head,
    second_bias,
):
    dp_count = lax.axis_size("dp")
    mp_count = lax.axis_size("mp")
    cube = dp_count == 8 and mp_count == 4
    rows = input_weight.shape[0]
    width = input_weight.shape[2]
    hidden = expand_weight.shape[1]
    seq, depth = tokens.shape
    part = hidden // 3
    model_index = lax.axis_index("mp")
    me = lax.axis_index("dp") * mp_count + model_index

    attend_shard, feed_shard = pack(
        input_weight.transpose(1, 0, 2), output_weight, expand_weight, shrink_weight.T
    )
    bias_shard = jnp.concatenate([head_bias.reshape(1, 2 * width), expand_bias[None]], axis=1)

    bias_full = jnp.where(jnp.arange(4)[:, None] == model_index, bias_shard, 0.0)
    if cube:
        core, near = me & 1, model_index
        devices = jnp.arange(32).reshape(8, 4).T
        spots = place(devices ^ me, devices & 1).astype(jnp.int32)
    else:
        core = near = jnp.zeros((), jnp.int32)
        spots = (jnp.arange(4)[:, None] // 2 * 8 + jnp.arange(8)[None]).astype(jnp.int32)
    where = jnp.stack([core, near, model_index]).astype(jnp.int32)

    if cube:
        held = attend_shard[None]
        arrived = cube_permute(held, 0)
        bias_full = bias_full + bit_permute(bias_full, 0)
        held = joined(held, arrived)
        arrived = cube_permute(held, 1)
        normed, normed_t, upstream_t = prepare(tokens, cotangent, layer_vectors, (held,))
        bias_full = bias_full + bit_permute(bias_full, 1)
        held, feed_shard, normed, bias_full, spots, where = lax.optimization_barrier(
            (held, feed_shard, normed, bias_full, spots, where)
        )
        held = joined(held, arrived)
        feed_held = feed_shard[None]
        arrived, far_feed = cube_permute(held, 2), cube_permute(feed_held, 0)
        held = joined(held, arrived)
        feed_held = joined(feed_held, far_feed)
        held, feed_held = lax.optimization_barrier((held, feed_held))
        far, far_feed = cube_permute(held, 3), cube_permute(feed_held, 1)
        twin = bit_permute(held, 0)
        feed_held = joined(feed_held, far_feed)
        far, feed_held = lax.optimization_barrier((far, feed_held))
        attend_halves = (held, far, twin, bit_permute(far, 0))
        arrived = cube_permute(feed_held, 2)
        qkv, wide = project(where, spots, normed, attend_halves, bias_full, ())
        feed_held, qkv = lax.optimization_barrier((feed_held, qkv))
        feed_held = joined(feed_held, arrived)
        far, twin = cube_permute(feed_held, 3), bit_permute(feed_held, 0)
        mixture, log_totals = attend_forward(where, lengths, qkv, (feed_held,))
        middle, hidden_in, hidden_t = attend_out(mixture, wide, tokens, layer_vectors)
        far, hidden_in = lax.optimization_barrier((far, hidden_in))
        feed_halves = (feed_held, far, twin, bit_permute(far, 0))
    else:

        def planes(shard):
            full = lax.all_gather(lax.all_gather(shard, "dp", axis=0, tiled=True), "mp", axis=0)
            full = full.reshape(2, 2, 8, depth // 8, shard.shape[1]).transpose(1, 0, 2, 3, 4)
            return tuple(full.reshape(4, 8, depth // 8, shard.shape[1]))

        normed, normed_t, upstream_t = prepare(tokens, cotangent, layer_vectors, ())
        bias_full = lax.psum(bias_full, "mp")
        qkv, wide = project(where, spots, normed, planes(attend_shard), bias_full, ())
        mixture, log_totals = attend_forward(where, lengths, qkv, ())
        middle, hidden_in, hidden_t = attend_out(mixture, wide, tokens, layer_vectors)
        feed_halves = planes(feed_shard)
    block_out, back, keep_feed, send_feed, bias_grad = feed(
        where,
        spots,
        hidden_in,
        hidden_t,
        cotangent,
        upstream_t,
        feed_halves,
        bias_full,
        middle,
        layer_vectors,
    )
    middle_grad, mixture_grad, output_grad, middle_sums = middle_back(
        where, lengths, back, middle, cotangent, mixture, wide, layer_vectors
    )
    if cube:
        feed_parts = [keep_feed, bit_permute(send_feed, 0)]
        keep_feed, mixture_grad = lax.optimization_barrier((keep_feed, mixture_grad))
        feed_parts[0] = keep_feed
        away = leaving(feed_parts, 3)
        packed_grad = attend_backward(where, lengths, qkv, mixture_grad, log_totals, (away,))
        feed_parts = staying(feed_parts, 3) + [cube_permute(away, 3)]
        feed_parts[0], packed_grad = lax.optimization_barrier((feed_parts[0], packed_grad))
        away = leaving(feed_parts, 2)
        feed_parts = staying(feed_parts, 2) + [cube_permute(away, 2)]
        token_grad, token_sums = token_back(
            packed_grad, wide, tokens, middle_grad, layer_vectors, (middle_sums, bias_grad), (away,)
        )
        keep_attend, send_attend, head_sums = input_grad(
            where, spots, normed_t, packed_grad, output_grad, 16, depth // 8, (token_sums,)
        )
        rider = join_vectors(token_sums, head_sums)
        feed_parts[-1], send_attend = lax.optimization_barrier((feed_parts[-1], send_attend))
        twin_b, rider = with_rider(send_attend[8:], rider, lambda values: bit_permute(values, 0))
        twin_a = bit_permute(send_attend[:8], 0)
        away = (keep_attend[8:].astype(f32) + twin_b.astype(f32)).astype(low)
        arrived, rider = with_rider(away, rider, lambda values: cube_permute(values, 3))
        attend_parts = [keep_attend[:8], twin_a, arrived]
        away = leaving(feed_parts, 1)
        feed_parts = staying(feed_parts, 1) + [cube_permute(away, 1)]
        away = leaving(attend_parts, 2)
        arrived, rider = with_rider(away, rider, lambda values: cube_permute(values, 2))
        attend_parts = staying(attend_parts, 2) + [arrived]
        away, feed_parts[0] = lax.optimization_barrier((away, feed_parts[0]))
        away = leaving(feed_parts, 0)
        feed_parts = staying(feed_parts, 0) + [cube_permute(away, 0)]
        away = leaving(attend_parts, 1)
        arrived, rider = with_rider(away, rider, lambda values: cube_permute(values, 1))
        attend_parts = staying(attend_parts, 1) + [arrived]
        away, feed_parts[0] = lax.optimization_barrier((away, feed_parts[0]))
        feed_total = summed(feed_parts)
        feed_squares = jnp.sum(feed_total * feed_total)
        away = leaving(attend_parts, 0)
        away, feed_squares = lax.optimization_barrier((away, feed_squares))
        arrived, vector_total = with_rider(away, rider, lambda values: cube_permute(values, 0))
        attend_parts = staying(attend_parts, 0) + [arrived]
        attend_total = summed(attend_parts)
    else:
        packed_grad = attend_backward(where, lengths, qkv, mixture_grad, log_totals, ())
        token_grad, token_sums = token_back(
            packed_grad, wide, tokens, middle_grad, layer_vectors, (middle_sums, bias_grad), ()
        )
        keep_attend, send_attend, head_sums = input_grad(
            where, spots, normed_t, packed_grad, output_grad, 16, depth // 8, ()
        )
        vector_total = lax.psum(join_vectors(token_sums, head_sums), ("dp", "mp"))

    if not cube:

        def own_block(keep, send):
            full = jnp.stack([keep, send]).reshape(2, 2, 8, depth // 8, keep.shape[2])
            full = full.transpose(1, 0, 2, 3, 4).reshape(4, depth, keep.shape[2])
            full = lax.psum_scatter(full, "mp", scatter_dimension=0, tiled=False)
            return lax.psum_scatter(full, "dp", scatter_dimension=0, tiled=True).astype(f32)

        attend_total = own_block(keep_attend, send_attend)
        feed_total = own_block(keep_feed, send_feed)
        feed_squares = jnp.sum(feed_total * feed_total)
    owned = jnp.full((8, 128), jnp.sum(attend_total * attend_total) + feed_squares, f32)
    owned = cube_sum(owned) if cube else lax.psum(owned, ("dp", "mp"))
    def turned(array):
        return array.transpose(1, 0, 2)

    state = (
        (turned(input_weight), turned(first_input), turned(second_input)),
        (output_weight, first_output, second_output),
        (expand_weight, first_expand, second_expand),
        (shrink_weight.T, first_shrink.T, second_shrink.T),
        (layer_vectors, first_vectors, second_vectors),
        (head_bias, first_head, second_head),
        tuple(array.reshape(hidden // 128, 128) for array in (expand_bias, first_bias, second_bias)),
    )
    grad_norm, *updates = optimize(where, owned, vector_total, attend_total, feed_total, state)
    grad_norm = grad_norm[0, 0]
    moment_input, square_input, updated_input = (turned(array) for array in updates[:3])
    moment_output, square_output, updated_output = updates[3:6]
    moment_expand, square_expand, updated_expand = updates[6:9]
    moment_shrink, square_shrink, updated_shrink = (array.T for array in updates[9:12])
    moment_vectors, square_vectors, updated_vectors = updates[12:15]
    moment_head, square_head, updated_head = updates[15:18]
    moment_bias, square_bias, updated_bias = (array.reshape(hidden) for array in updates[18:])
    return (
        block_out,
        token_grad,
        grad_norm,
        moment_input,
        square_input,
        updated_input,
        moment_output,
        square_output,
        updated_output,
        moment_expand,
        square_expand,
        updated_expand,
        moment_shrink,
        square_shrink,
        updated_shrink,
        moment_vectors,
        square_vectors,
        updated_vectors,
        moment_head,
        square_head,
        updated_head,
        moment_bias,
        square_bias,
        updated_bias,
    )


def solution(mesh):
    in_specs = (
        P(("dp", "mp"), None),
        P(("dp", "mp"), None),
        P("dp"),
        P("dp", None, "mp"),
        P("mp", "dp"),
        P("dp", "mp"),
        P("mp", "dp"),
        P(),
        P(None, "mp"),
        P("mp"),
        P("dp", None, "mp"),
        P("mp", "dp"),
        P("dp", "mp"),
        P("mp", "dp"),
        P(),
        P(None, "mp"),
        P("mp"),
        P("dp", None, "mp"),
        P("mp", "dp"),
        P("dp", "mp"),
        P("mp", "dp"),
        P(),
        P(None, "mp"),
        P("mp"),
    )
    out_specs = (
        P(("dp", "mp"), None),
        P(("dp", "mp"), None),
        P(),
        P("dp", None, "mp"),
        P("dp", None, "mp"),
        P("dp", None, "mp"),
        P("mp", "dp"),
        P("mp", "dp"),
        P("mp", "dp"),
        P("dp", "mp"),
        P("dp", "mp"),
        P("dp", "mp"),
        P("mp", "dp"),
        P("mp", "dp"),
        P("mp", "dp"),
        P(),
        P(),
        P(),
        P(None, "mp"),
        P(None, "mp"),
        P(None, "mp"),
        P("mp"),
        P("mp"),
        P("mp"),
    )
    return jax.shard_map(shards, mesh=mesh, in_specs=in_specs, out_specs=out_specs, check_vma=False)
```

```python
import functools
import jax
import jax.numpy as jnp
from jax import lax
from jax.experimental import pallas as pl
from jax.experimental.pallas import tpu as pltpu
from jax.sharding import PartitionSpec as P

HEAD_DIM = 64
TILE = 256
STEP = 10

eps_norm = 1e-05
clip_norm = 1.0
beta_one = 0.9
beta_two = 0.999
adam_eps = 1e-08
rate = 0.05
vector_rate = 0.5
decay = 0.01
excluded = -1e30
low = jnp.bfloat16
f32 = jnp.float32
GELU_A = 0.7978845608028654
GELU_B = GELU_A * 0.044715


def params(limit_mib, **kw):
    return pltpu.CompilerParams(vmem_limit_bytes=limit_mib * 1024 * 1024, **kw)


def cost(flops, moved, special=0):
    return pl.CostEstimate(flops=int(flops), bytes_accessed=int(moved), transcendentals=int(special))


def mm(a, b):
    return jnp.dot(a, b, preferred_element_type=f32)


def mm_nt(a, b):
    return lax.dot_general(a, b, (((1,), (1,)), ((), ())), preferred_element_type=f32)


def whole(shape):
    zeros = (0,) * len(shape)
    return pl.BlockSpec(shape, lambda *_: zeros)


def once(shape):
    zeros = (0,) * len(shape)
    return pl.BlockSpec(shape, lambda *_: zeros, pipeline_mode=pl.Buffered(1))


def held_back(body, first, count):
    def run(*refs):
        return body(*refs[:first], *refs[first + count :])

    return run


LATER = pl.BlockSpec(memory_space=pl.ANY)


def far_away(shape, dtype):
    return pltpu.HBM(shape, dtype)


def from_far(*arrays):
    return [pltpu.with_memory_space_constraint(array, pltpu.HBM) for array in arrays]


def sds(shape, dtype):
    return jax.ShapeDtypeStruct(shape, dtype)


def live_blocks(length, count, body):
    for blocks in range(1, count + 1):
        low_end = (blocks - 1) * TILE
        high_end = blocks * TILE
        @pl.when((length > low_end) & (length <= high_end))
        def _(blocks=blocks):
            body(length, blocks)


PAIR = 2 * HEAD_DIM


def span(block):
    return slice(block * TILE, (block + 1) * TILE)


def both_heads(values):
    lane = lax.broadcasted_iota(jnp.int32, values.shape, 1)
    none = jnp.zeros_like(values)
    return jnp.concatenate(
        [jnp.where(lane < HEAD_DIM, values, none), jnp.where(lane >= HEAD_DIM, values, none)], axis=0
    )


def causal_mask():
    key_id = lax.broadcasted_iota(jnp.int32, (TILE, 2 * TILE), 0)
    query_id = lax.broadcasted_iota(jnp.int32, (TILE, 2 * TILE), 1) & (TILE - 1)
    return key_id <= query_id


def forward_body(where_ref, lengths_ref, q_ref, k_ref, v_ref, o_ref, lse_ref, vt_ref):
    seq = q_ref.shape[0]
    vt_ref[...] = v_ref[...].T
    causal = causal_mask()

    def run(length, blocks):
        def scores(b):
            q = q_ref[span(b), :] * jnp.asarray(HEAD_DIM**-0.5, low)
            return mm_nt(k_ref[: (b + 1) * TILE, :], both_heads(q))

        now = scores(0)
        for b in range(blocks):
            start, stop = b * TILE, (b + 1) * TILE
            later = scores(b + 1) if b + 1 < blocks else None
            last = jnp.where(causal, now[start:, :], excluded)
            top = jnp.max(last, axis=0, keepdims=True)
            if b:
                top = jnp.maximum(top, jnp.max(now[:start], axis=0, keepdims=True))
            p = jnp.exp(last - top)
            total = jnp.sum(p, axis=0, keepdims=True)
            pb = p.astype(low)
            if b:
                pf = jnp.exp(now[:start] - top)
                total = total + jnp.sum(pf, axis=0, keepdims=True)
                pb = jnp.concatenate([pf.astype(low), pb], axis=0)
            inverse = 1.0 / total
            lse = top + jnp.log(total)
            outs = []
            for h in range(2):
                at = slice(h * TILE, (h + 1) * TILE)
                out = mm(vt_ref[h * HEAD_DIM : (h + 1) * HEAD_DIM, :stop], pb[:, at])
                outs.append(out * inverse[:, at])
                lse_ref[0, h : h + 1, start:stop] = lse[:, at]
            both = jnp.concatenate(outs, axis=0).T
            row = start + lax.broadcasted_iota(jnp.int32, both.shape, 0)
            o_ref[start:stop, :] = jnp.where(row < length, both, 0.0).astype(low)
            now = later
        if blocks * TILE < seq:
            o_ref[blocks * TILE :, :] = jnp.zeros((seq - blocks * TILE, PAIR), low)
            lse_ref[0, :, blocks * TILE :] = jnp.zeros((2, seq - blocks * TILE), f32)

    live_blocks(lengths_ref[where_ref[2]], seq // TILE, run)


def attend_forward(where, lengths, qkv, after):
    seq, width = qkv.shape[0], qkv.shape[1] // 3
    pair = 2 * HEAD_DIM
    pairs = width // pair
    half = seq * seq * 5 // 8
    spec = lambda part: pl.BlockSpec((seq, pair), lambda i, *_: (0, part * pairs + i))
    return pl.pallas_call(
        held_back(forward_body, 5, len(after)),
        grid_spec=pltpu.PrefetchScalarGridSpec(
            num_scalar_prefetch=2,
            grid=(pairs,),
            in_specs=[spec(0), spec(1), spec(2)] + [LATER] * len(after),
            out_specs=[
                pl.BlockSpec((seq, pair), lambda i, *_: (0, i)),
                pl.BlockSpec((1, 2, seq), lambda i, *_: (i, 0, 0)),
            ],
            scratch_shapes=[pltpu.VMEM((pair, seq), low)],
        ),
        out_shape=[sds((seq, width), low), far_away((pairs, 2, seq), f32)],
        compiler_params=params(20),
        cost_estimate=cost(pairs * 2 * half * 2 * 2 * 256, seq * width * 8, pairs * 2 * half),
        name="attend_forward",
    )(where, lengths, *from_far(qkv, qkv, qkv), *after)


def backward_body(where_ref, lengths_ref, q_ref, k_ref, v_ref, do_ref, lse_ref, out_ref, kt_ref, ksum, vsum):
    seq = q_ref.shape[0]
    scale = HEAD_DIM**-0.5
    kt_ref[...] = k_ref[...].T
    causal = causal_mask()

    def run(length, blocks):
        def scores(b):
            qq = both_heads(q_ref[span(b), :] * jnp.asarray(scale, low))
            uu = both_heads(do_ref[span(b), :])
            stop = (b + 1) * TILE
            return qq, uu, mm_nt(k_ref[:stop, :], qq), mm_nt(v_ref[:stop, :], uu)

        now = scores(blocks - 1)
        for b in reversed(range(blocks)):
            start, stop = b * TILE, (b + 1) * TILE
            later = scores(b - 1) if b else None
            qq, uu, s, dp = now
            lse = jnp.concatenate([lse_ref[0, 0:1, start:stop], lse_ref[0, 1:2, start:stop]], axis=1)
            p = jnp.exp(jnp.where(causal, s[start:], excluded) - lse)
            inner = jnp.sum(p * dp[start:], axis=0, keepdims=True)
            if b:
                pf = jnp.exp(s[:start] - lse)
                inner = inner + jnp.sum(pf * dp[:start], axis=0, keepdims=True)
            ds = (p * (dp[start:] - inner)).astype(low)
            pb = p.astype(low)
            if b:
                ds = jnp.concatenate([(pf * (dp[:start] - inner)).astype(low), ds], axis=0)
                pb = jnp.concatenate([pf.astype(low), pb], axis=0)
            dk, dv = mm(ds, qq), mm(pb, uu)
            if b == blocks - 1:
                ksum[:stop, :] = dk
                vsum[:stop, :] = dv
            else:
                ksum[:stop, :] += dk
                vsum[:stop, :] += dv
            dq = jnp.concatenate(
                [
                    mm(
                        kt_ref[h * HEAD_DIM : (h + 1) * HEAD_DIM, :stop],
                        ds[:, h * TILE : (h + 1) * TILE],
                    )
                    for h in range(2)
                ],
                axis=0,
            )
            out_ref[1, start:stop, :] = ksum[start:stop, :].astype(low)
            out_ref[2, start:stop, :] = vsum[start:stop, :].astype(low)
            out_ref[0, start:stop, :] = (dq.T * scale).astype(low)
            now = later
        if blocks * TILE < seq:
            rest = jnp.zeros((seq - blocks * TILE, PAIR), low)
            for part in range(3):
                out_ref[part, blocks * TILE :, :] = rest

    live_blocks(lengths_ref[where_ref[2]], seq // TILE, run)


def attend_backward(where, lengths, qkv, upstream, lse, after):
    seq, width = upstream.shape
    pair = 2 * HEAD_DIM
    pairs = width // pair
    half = seq * seq * 5 // 8
    spec = lambda part: pl.BlockSpec((seq, pair), lambda i, *_: (0, part * pairs + i))
    own = pl.BlockSpec((seq, pair), lambda i, *_: (0, i))
    return pl.pallas_call(
        held_back(backward_body, 7, len(after)),
        grid_spec=pltpu.PrefetchScalarGridSpec(
            num_scalar_prefetch=2,
            grid=(pairs,),
            in_specs=[spec(0), spec(1), spec(2), own, pl.BlockSpec((1, 2, seq), lambda i, *_: (i, 0, 0))]
            + [LATER] * len(after),
            out_specs=pl.BlockSpec((3, seq, pair), lambda i, *_: (0, 0, i)),
            scratch_shapes=[
                pltpu.VMEM((pair, seq), low),
                pltpu.VMEM((seq, pair), f32),
                pltpu.VMEM((seq, pair), f32),
            ],
        ),
        out_shape=sds((3, seq, width), low),
        compiler_params=params(28),
        cost_estimate=cost(pairs * 2 * half * 5 * 2 * 256, seq * width * 14, pairs * 2 * half),
        name="attend_backward",
    )(where, lengths, *from_far(qkv, qkv, qkv), upstream, *from_far(lse), *after)


def normalize(values):
    average = jnp.mean(values, axis=-1, keepdims=True)
    centred = values - average
    inverse = lax.rsqrt(jnp.mean(centred * centred, axis=-1, keepdims=True) + eps_norm)
    return centred * inverse, inverse


def pull_norm(scaled, unit, inverse):
    first = jnp.mean(scaled, axis=-1, keepdims=True)
    second = jnp.mean(scaled * unit, axis=-1, keepdims=True)
    return inverse * (scaled - first - unit * second)


def columns_of(values):
    return jnp.sum(values, axis=0, keepdims=True)


def pack_body(input_ref, output_ref, expand_ref, shrink_ref, attend_ref, feed_ref):
    width = input_ref.shape[2]
    part = expand_ref.shape[1] // 3
    for index in range(3):
        attend_ref[:, index * width : (index + 1) * width] = input_ref[index].astype(low)
        at = slice(index * part, (index + 1) * part)
        feed_ref[:, 2 * index * part : (2 * index + 1) * part] = expand_ref[:, at].astype(low)
        feed_ref[:, (2 * index + 1) * part : (2 * index + 2) * part] = shrink_ref[:, at].astype(low)
    attend_ref[:, 3 * width :] = output_ref[...].T.astype(low)


def pack(input_weight, output_weight, expand, shrink):
    rows, width = input_weight.shape[1:]
    hidden = expand.shape[1]
    return pl.pallas_call(
        pack_body,
        out_shape=[sds((rows, 4 * width), low), sds((rows, 2 * hidden), low)],
        compiler_params=params(6),
        cost_estimate=cost(rows * hidden, rows * hidden * 18),
        name="pack",
    )(*from_far(input_weight, output_weight, expand, shrink))


def prepare_body(x_ref, up_ref, vec_ref, h_ref, ht_ref, upt_ref):
    unit, _ = normalize(x_ref[...].astype(f32))
    h = (unit * vec_ref[0:1, :] + vec_ref[1:2, :]).astype(low)
    h_ref[...] = h
    ht_ref[...] = h.T
    upt_ref[...] = up_ref[...].T


def prepare(x, up, vectors, after):
    seq, depth = x.shape
    rows = pl.BlockSpec((2 * TILE, depth), lambda i: (i, 0))
    turned = pl.BlockSpec((depth, 2 * TILE), lambda i: (0, i))
    return pl.pallas_call(
        held_back(prepare_body, 3, len(after)),
        grid=(seq // (2 * TILE),),
        in_specs=[rows, rows, once(vectors.shape)] + [LATER] * len(after),
        out_specs=[rows, turned, turned],
        out_shape=[sds((seq, depth), low), far_away((depth, seq), low), far_away((depth, seq), low)],
        compiler_params=params(16),
        cost_estimate=cost(seq * depth * 10, seq * depth * 10),
        name="prepare",
    )(*from_far(x, up), vectors, *after)


def slot(halves, spot, at):
    first, second = halves
    inner = spot & 7
    return jnp.where(spot < 8, first[inner, :, at], second[inner, :, at])


def project_body(
    where_ref, spots_ref, h_ref, mine_a, mine_b, twin_a, twin_b, bias_ref, qkv_ref, wide_ref
):
    part = pl.program_id(0)
    rows = mine_a.shape[1]
    width = mine_a.shape[2] // 4
    groups = wide_ref.shape[1] // rows

    def collect(sources, index):
        at = slice(index * width, (index + 1) * width)
        for group in range(groups):
            pieces = [slot(sources[model % 2], spots_ref[model, group], at) for model in range(4)]
            wide_ref[0, group * rows : (group + 1) * rows, :] = jnp.concatenate(pieces, axis=1)

    for index in range(4):
        for core in range(2):

            @pl.when((part == index) & (where_ref[0] == core))
            def _(index=index, core=core):
                mine, twin = (mine_a, mine_b), (twin_a, twin_b)
                collect((mine, twin) if core == 0 else (twin, mine), index)

    for index in range(3):

        @pl.when(part == index)
        def _(index=index):
            out = mm(h_ref[...], wide_ref[0])
            if index != 1:
                at = slice(index // 2 * width, (index // 2 + 1) * width)
                bias = jnp.concatenate([bias_ref[model : model + 1, at] for model in range(4)], axis=1)
                out = out + bias
            qkv_ref[...] = out.astype(low)


def project(where, spots, h, halves, bias, after):
    seq, depth = h.shape
    return pl.pallas_call(
        held_back(project_body, 8, len(after)),
        grid_spec=pltpu.PrefetchScalarGridSpec(
            num_scalar_prefetch=2,
            grid=(4,),
            in_specs=[
                once((seq, depth)),
                *[once(halves[0].shape)] * 4,
                once(bias.shape),
            ]
            + [LATER] * len(after),
            out_specs=[
                pl.BlockSpec((seq, depth), lambda i, *_: (0, jnp.minimum(i, 2))),
                pl.BlockSpec((1, depth, depth), lambda i, *_: (i, 0, 0)),
            ],
        ),
        out_shape=[far_away((seq, 3 * depth), low), far_away((4, depth, depth), low)],
        compiler_params=params(24),
        cost_estimate=cost(2 * seq * depth * depth * 3, seq * depth * 16),
        name="project",
    )(where, spots, h, *halves, bias, *after)


def attend_out_body(o_ref, w_ref, x_ref, vec_ref, middle_ref, h_ref, ht_ref, unit_ref, inverse_ref):
    middle = x_ref[...].astype(f32) + mm_nt(o_ref[...], w_ref[0]) + vec_ref[4:5, :]
    middle_ref[...] = middle.astype(low)
    unit, inverse = normalize(middle)
    unit_ref[...] = unit.astype(low)
    inverse_ref[...] = jnp.broadcast_to(inverse, inverse_ref.shape)
    h = (unit * vec_ref[2:3, :] + vec_ref[3:4, :]).astype(low)
    h_ref[...] = h
    ht_ref[...] = h.T


def attend_out(o, wide, x, vectors):
    seq, depth = x.shape
    rows = pl.BlockSpec((TILE, depth), lambda i: (i, 0))
    turned = pl.BlockSpec((depth, TILE), lambda i: (0, i))
    return pl.pallas_call(
        attend_out_body,
        grid=(seq // TILE,),
        in_specs=[
            rows,
            pl.BlockSpec((1, depth, depth), lambda i: (3, 0, 0)),
            rows,
            once(vectors.shape),
        ],
        out_specs=[rows, rows, turned, rows, pl.BlockSpec((TILE, 128), lambda i: (i, 0))],
        out_shape=[
            sds((seq, depth), low),
            sds((seq, depth), low),
            sds((depth, seq), low),
            sds((seq, depth), low),
            sds((seq, 128), f32),
        ],
        compiler_params=params(14),
        cost_estimate=cost(2 * seq * depth * depth, seq * depth * 14),
        name="attend_out",
    )(o, *from_far(wide, x), vectors)


def feed_body(
    where_ref,
    spots_ref,
    h2_ref,
    h2t_ref,
    up_ref,
    upt_ref,
    mine_a,
    mine_b,
    twin_a,
    twin_b,
    bias_ref,
    middle_ref,
    vec_ref,
    block_ref,
    back_ref,
    keep_ref,
    send_ref,
    bias_grad_ref,
    out_ref,
    sum_ref,
    wide_ref,
    act_ref,
    pre_ref,
):
    step = pl.program_id(0)
    side = lax.rem(step, 2)
    models = [where_ref[1] ^ (2 * side + core) for core in range(2)]
    rows = mine_a.shape[1]
    part = mine_a.shape[2] // 2
    groups = wide_ref.shape[0] // rows

    for group in range(groups):
        at = slice(group * rows, (group + 1) * rows)
        own = slot((mine_a, mine_b), spots_ref[models[0], group], slice(None))
        other = slot((twin_a, twin_b), spots_ref[models[1], group], slice(None))
        wide_ref[at, :part] = own[:, :part]
        wide_ref[at, part : 2 * part] = other[:, :part]
        wide_ref[at, 2 * part : 3 * part] = own[:, part:]
        wide_ref[at, 3 * part :] = other[:, part:]

    expand = wide_ref[:, : 2 * part]
    shrink = wide_ref[:, 2 * part :]
    first = step // 2 * part
    skip = bias_ref.shape[1] - bias_grad_ref.shape[1]
    bias = jnp.concatenate(
        [bias_ref[pl.ds(model, 1), pl.ds(pl.multiple_of(skip + first, 128), part)] for model in models],
        axis=1,
    )
    sums = jnp.zeros((1, 2 * part), f32)
    for tile in range(h2_ref.shape[0] // TILE):
        at = slice(tile * TILE, (tile + 1) * TILE)
        u = mm(h2_ref[at, :], expand) + bias
        square = u * u
        th = jnp.tanh(u * (GELU_A + GELU_B * square))
        gate = 0.5 * th + 0.5
        slope = gate + (gate * (1.0 - gate)) * (u * (2.0 * GELU_A + (6.0 * GELU_B) * square))
        pre = (mm(up_ref[at, :], shrink) * slope).astype(low)
        act_ref[at, :] = (u * gate).astype(low)
        pre_ref[at, :] = pre
        sums = sums + columns_of(pre.astype(f32))
    for core, model in enumerate(models):
        bias_grad_ref[pl.ds(model, 1), pl.ds(pl.multiple_of(first, 128), part)] = sums[
            :, core * part : (core + 1) * part
        ]
    out = mm_nt(act_ref[...], shrink)
    back = mm_nt(pre_ref[...], expand)

    @pl.when(step == 0)
    def _():
        out_ref[...] = middle_ref[...].astype(f32) + vec_ref[5:6, :] + out
        sum_ref[...] = back

    @pl.when((step > 0) & (step < pl.num_programs(0) - 1))
    def _():
        out_ref[...] += out
        sum_ref[...] += back

    @pl.when(step == pl.num_programs(0) - 1)
    def _():
        block_ref[...] = (out_ref[...] + out).astype(low)
        back_ref[...] = (sum_ref[...] + back).astype(low)

    grad_expand = mm(h2t_ref[...], pre_ref[...]).astype(low)
    grad_shrink = mm(upt_ref[...], act_ref[...]).astype(low)
    for group in range(groups):
        at = slice(group * rows, (group + 1) * rows)
        own, other = spots_ref[models[0], group], spots_ref[models[1], group]
        keep_ref[own, :, :part] = grad_expand[at, :part]
        keep_ref[own, :, part:] = grad_shrink[at, :part]
        send_ref[other, :, :part] = grad_expand[at, part:]
        send_ref[other, :, part:] = grad_shrink[at, part:]


def feed(where, spots, h2, h2t, up, upt, halves, bias, middle, vectors):
    seq, depth = h2.shape
    half, rows, columns = halves[0].shape
    steps, part = 6, columns // 6
    half_piece = pl.BlockSpec((half, rows, 2 * part), lambda i, *_: (0, 0, i // 2))
    piece = pl.BlockSpec((2 * half, rows, 2 * part), lambda i, *_: (0, 0, i // 2))
    return pl.pallas_call(
        feed_body,
        grid_spec=pltpu.PrefetchScalarGridSpec(
            num_scalar_prefetch=2,
            grid=(steps,),
            in_specs=[
                once((seq, depth)),
                once((depth, seq)),
                once((seq, depth)),
                once((depth, seq)),
                *[half_piece] * 4,
                once(bias.shape),
                once((seq, depth)),
                once(vectors.shape),
            ],
            out_specs=[whole((seq, depth)), whole((seq, depth)), piece, piece, whole((4, 3 * part))],
            scratch_shapes=[
                pltpu.VMEM((seq, depth), f32),
                pltpu.VMEM((seq, depth), f32),
                pltpu.VMEM((depth, 4 * part), low),
                pltpu.VMEM((seq, 2 * part), low),
                pltpu.VMEM((seq, 2 * part), low),
            ],
        ),
        out_shape=[sds((seq, depth), low)] * 2
        + [sds((2 * half, rows, columns), low)] * 2
        + [sds((4, 3 * part), f32)],
        compiler_params=params(31),
        cost_estimate=cost(12 * seq * depth * steps * 2 * part, seq * depth * 40, seq * steps * part),
        name="feed",
    )(where, spots, h2, h2t, *from_far(up, upt), *halves, bias, middle, vectors)


def middle_back_body(
    where_ref,
    lengths_ref,
    back_ref,
    unit_ref,
    inverse_ref,
    up_ref,
    o_ref,
    w_ref,
    vec_ref,
    grad_ref,
    mixture_ref,
    weight_ref,
    sums_ref,
    total_ref,
):
    step = pl.program_id(0)
    unit, inverse = unit_ref[...].astype(f32), inverse_ref[:, 0:1]
    back = back_ref[...].astype(f32)
    up = up_ref[...].astype(f32)
    grad = up + pull_norm(back * vec_ref[2:3, :], unit, inverse)
    rounded = grad.astype(low)
    grad_ref[...] = rounded
    row = step * grad.shape[0] + lax.broadcasted_iota(jnp.int32, grad.shape, 0)
    length = lengths_ref[where_ref[2]]
    mixture_ref[...] = jnp.where(row < length, mm(rounded, w_ref[0]), 0.0).astype(low)
    share = mm(rounded.T, o_ref[...])
    sums = jnp.concatenate(
        [columns_of(back * unit), columns_of(back), columns_of(grad), columns_of(up)], axis=0
    )

    @pl.when(step == 0)
    def _():
        total_ref[...] = share
        sums_ref[...] = sums

    @pl.when(step > 0)
    def _():
        total_ref[...] += share
        sums_ref[...] += sums

    @pl.when(step == pl.num_programs(0) - 1)
    def _():
        weight_ref[...] = total_ref[...].astype(low)


def middle_back(where, lengths, back, unit, inverse, up, o, wide, vectors):
    seq, depth = unit.shape
    rows = pl.BlockSpec((2 * TILE, depth), lambda i, *_: (i, 0))
    return pl.pallas_call(
        middle_back_body,
        grid_spec=pltpu.PrefetchScalarGridSpec(
            num_scalar_prefetch=2,
            grid=(seq // (2 * TILE),),
            in_specs=[
                rows,
                rows,
                pl.BlockSpec((2 * TILE, 128), lambda i, *_: (i, 0)),
                rows,
                rows,
                pl.BlockSpec((1, depth, depth), lambda i, *_: (3, 0, 0)),
                once(vectors.shape),
            ],
            out_specs=[rows, rows, whole((depth, depth)), whole((4, depth))],
            scratch_shapes=[pltpu.VMEM((depth, depth), f32)],
        ),
        out_shape=[
            sds((seq, depth), low),
            sds((seq, depth), low),
            sds((depth, depth), low),
            sds((4, depth), f32),
        ],
        compiler_params=params(24),
        cost_estimate=cost(4 * seq * depth * depth, seq * depth * 28),
        name="middle_back",
    )(where, lengths, back, unit, inverse, *from_far(up), o, *from_far(wide), vectors)


def input_grad_body(
    where_ref,
    spots_ref,
    ht_ref,
    back_ref,
    out_grad_ref,
    middle_ref,
    bias_ref,
    keep_ref,
    send_ref,
    sums_ref,
):
    part = pl.program_id(0)
    rows = keep_ref.shape[1]
    width = keep_ref.shape[2] // 4
    groups = ht_ref.shape[0] // rows

    def spread(targets, index, grad):
        at = slice(index * width, (index + 1) * width)
        for group in range(groups):
            for model in range(4):
                targets[model % 2][spots_ref[model, group], :, at] = grad[
                    group * rows : (group + 1) * rows, model * width : (model + 1) * width
                ]

    for index in range(4):

        @pl.when(part == index)
        def _(index=index):
            if index < 3:
                if index == 0:
                    sums_ref[:2] = jnp.zeros((2, sums_ref.shape[1]), f32)
                    sums_ref[2:6] = middle_ref[...]
                    sums_ref[8:] = bias_ref[...]
                if index != 1:
                    row = 6 + index // 2
                    sums_ref[row : row + 1, :] = columns_of(back_ref[0].astype(f32))
                grad = mm(ht_ref[...], back_ref[0]).astype(low)
            else:
                grad = out_grad_ref[...]
            for core in range(2):

                @pl.when(where_ref[0] == core)
                def _(core=core):
                    spread((keep_ref, send_ref) if core == 0 else (send_ref, keep_ref), index, grad)


def input_grad(where, spots, ht, back, out_grad, sums, slots, rows, after):
    depth, seq = ht.shape
    shape = (slots, rows, 4 * (depth // 4))
    return pl.pallas_call(
        held_back(input_grad_body, 7, len(after)),
        grid_spec=pltpu.PrefetchScalarGridSpec(
            num_scalar_prefetch=2,
            grid=(4,),
            in_specs=[
                once((depth, seq)),
                pl.BlockSpec((1, seq, depth), lambda i, *_: (jnp.minimum(i, 2), 0, 0)),
                once((depth, depth)),
                *[once(array.shape) for array in sums],
            ]
            + [LATER] * len(after),
            out_specs=[
                whole(shape),
                whole(shape),
                whole((12, depth)),
            ],
        ),
        out_shape=[sds(shape, low), sds(shape, low), sds((12, depth), f32)],
        compiler_params=params(24),
        cost_estimate=cost(6 * seq * depth * depth, seq * depth * 14),
        name="input_grad",
    )(where, spots, *from_far(ht), back, out_grad, *sums, *after)


def token_back_body(
    back_ref, w_ref, x_ref, grad_ref, vec_ref, token_ref, sums_ref
):
    step = pl.program_id(0)
    back = mm_nt(back_ref[0], w_ref[0]) + mm_nt(back_ref[1], w_ref[1]) + mm_nt(back_ref[2], w_ref[2])
    unit, inverse = normalize(x_ref[...].astype(f32))
    grad = grad_ref[...].astype(f32)
    token_ref[...] = (grad + pull_norm(back * vec_ref[0:1, :], unit, inverse)).astype(low)
    sums = jnp.concatenate([columns_of(back * unit), columns_of(back)], axis=0)

    @pl.when(step == 0)
    def _():
        sums_ref[...] = sums

    @pl.when(step > 0)
    def _():
        sums_ref[...] += sums


def token_back(back, wide, x, grad, vectors, after):
    seq, depth = x.shape
    rows = pl.BlockSpec((TILE, depth), lambda i: (i, 0))
    return pl.pallas_call(
        held_back(token_back_body, 5, len(after)),
        grid=(seq // TILE,),
        in_specs=[
            pl.BlockSpec((3, TILE, depth), lambda i: (0, i, 0)),
            pl.BlockSpec((3, depth, depth), lambda i: (0, 0, 0)),
            rows,
            rows,
            once(vectors.shape),
        ]
        + [LATER] * len(after),
        out_specs=[rows, whole((2, depth))],
        out_shape=[sds((seq, depth), low), sds((2, depth), f32)],
        compiler_params=params(24),
        cost_estimate=cost(0, 0),
        name="token_back",
    )(back, *from_far(wide, x), grad, vectors, *after)


CORE_ORDERS = ((4, 3, 2, 1), (3, 4, 1, 2))
STAGES = 4


def cube_permute(values, stage):
    pairs = [(device, device ^ (1 << CORE_ORDERS[device & 1][stage])) for device in range(32)]
    return lax.ppermute(values, ("dp", "mp"), pairs)


def bit_permute(values, bit):
    return lax.ppermute(values, ("dp", "mp"), [(device, device ^ (1 << bit)) for device in range(32)])


def place(distance, core):
    spots = [
        sum(((distance >> bit) & 1) << step for step, bit in enumerate(order)) for order in CORE_ORDERS
    ]
    return jnp.where(core == 0, spots[0], spots[1])


def joined(held, arrived):
    return jnp.concatenate([held, arrived], axis=0)


def leaving(parts, stage):
    half = 1 << stage
    return sum(part[half:].astype(f32) for part in parts).astype(low)


def staying(parts, stage):
    return [part[: 1 << stage] for part in parts]


def summed(parts):
    return sum(part[0].astype(f32) for part in parts)


def two_parts(values):
    high = lax.reduce_precision(values, 8, 7)
    rest = lax.reduce_precision(values - high, 8, 7)
    return jnp.concatenate([high, rest], axis=0).astype(low)


def one_part(parts):
    half = parts.shape[0] // 2
    return parts[:half].astype(f32) + parts[half:].astype(f32)


def with_rider(blocks, rider, send):
    count, rows, columns = blocks.shape
    parts = two_parts(rider)
    arrived = send(jnp.concatenate([blocks.reshape(count * rows, columns), parts], axis=0))
    total = one_part(parts) + one_part(arrived[count * rows :])
    return arrived[: count * rows].reshape(count, rows, columns), total


def cube_sum(values, bits=range(5)):
    for bit in bits:
        values = values + bit_permute(values, bit)
    return values


def adam_parts(weight, gradient, first_old, second_old, factor, step_rate):
    scaled = gradient * factor
    moment = beta_one * first_old + (1.0 - beta_one) * scaled
    square = beta_two * second_old + (1.0 - beta_two) * scaled * scaled
    spread = jnp.sqrt(square * (1.0 / (1.0 - beta_two**STEP)))
    ratio = moment * (1.0 / (1.0 - beta_one**STEP)) / (spread + adam_eps)
    return moment, square, weight - step_rate * (ratio + decay * weight)


def optimize_body(where_ref, owned_ref, vector_ref, attend_ref, feed_ref, *refs):
    state, outs = refs[:21], refs[21:]
    vectors = vector_ref[...]
    total = owned_ref[0:1, 0:1] + jnp.sum(vectors * vectors)
    norm = jnp.sqrt(total)
    factor = clip_norm / jnp.maximum(norm, clip_norm)
    outs[0][...] = norm
    width = state[0].shape[2]
    part = state[6].shape[1] // 3

    def update(param, at, gradient, step_rate):
        weight, first, second = (ref[at] for ref in state[3 * param : 3 * param + 3])
        results = adam_parts(weight, gradient, first, second, factor, step_rate)
        for ref, result in zip(outs[1 + 3 * param : 4 + 3 * param], results):
            ref[at] = result

    for index in range(3):
        update(0, (index,), attend_ref[:, index * width : (index + 1) * width], rate)
    update(1, (...,), attend_ref[:, 3 * width :].T, rate)
    for index in range(3):
        at = (slice(None), slice(index * part, (index + 1) * part))
        first = 2 * index * part
        update(2, at, feed_ref[:, first : first + part], rate)
        update(3, at, feed_ref[:, first + part : first + 2 * part], rate)
    update(4, (...,), vectors[:6], vector_rate)
    model = where_ref[2]
    head = jnp.zeros((2, width), f32)
    for index in range(4):
        head = head + jnp.where(model == index, vectors[6:8, index * width : (index + 1) * width], 0.0)
    update(5, (...,), head, vector_rate)
    bias = vector_ref[pl.ds(8 + model, 1), :]
    bias = jnp.concatenate([bias[:, at : at + 128] for at in range(0, bias.shape[1], 128)], axis=0)
    update(6, (...,), bias, vector_rate)


def optimize(where, owned, vector_total, attend_total, feed_total, state):
    shapes = [sds(group[0].shape, f32) for group in state for _ in range(3)]
    arrays = [array for group in state for array in group]
    return pl.pallas_call(
        optimize_body,
        in_specs=[pl.BlockSpec(memory_space=pltpu.SMEM)]
        + [pl.BlockSpec(memory_space=pltpu.VMEM)] * (4 + len(arrays)),
        out_shape=[sds((1, 1), f32)] + shapes,
        compiler_params=params(20),
        cost_estimate=cost(4e6, 8e6),
        name="optimize",
    )(where, owned, vector_total, attend_total, feed_total, *from_far(*arrays))


def shards(
    tokens,
    cotangent,
    lengths,
    input_weight,
    output_weight,
    expand_weight,
    shrink_weight,
    layer_vectors,
    head_bias,
    expand_bias,
    first_input,
    first_output,
    first_expand,
    first_shrink,
    first_vectors,
    first_head,
    first_bias,
    second_input,
    second_output,
    second_expand,
    second_shrink,
    second_vectors,
    second_head,
    second_bias,
):
    dp_count = lax.axis_size("dp")
    mp_count = lax.axis_size("mp")
    cube = dp_count == 8 and mp_count == 4
    rows = input_weight.shape[0]
    width = input_weight.shape[2]
    hidden = expand_weight.shape[1]
    seq, depth = tokens.shape
    part = hidden // 3
    model_index = lax.axis_index("mp")
    me = lax.axis_index("dp") * mp_count + model_index

    attend_shard, feed_shard = pack(
        input_weight.transpose(1, 0, 2), output_weight, expand_weight, shrink_weight.T
    )
    bias_shard = jnp.concatenate([head_bias.reshape(1, 2 * width), expand_bias[None]], axis=1)

    bias_full = jnp.where(jnp.arange(4)[:, None] == model_index, bias_shard, 0.0)
    if cube:
        core, near = me & 1, model_index
        devices = jnp.arange(32).reshape(8, 4).T
        spots = place(devices ^ me, devices & 1).astype(jnp.int32)
    else:
        core = near = jnp.zeros((), jnp.int32)
        spots = (jnp.arange(4)[:, None] // 2 * 8 + jnp.arange(8)[None]).astype(jnp.int32)
    where = jnp.stack([core, near, model_index]).astype(jnp.int32)

    if cube:
        held = attend_shard[None]
        arrived = cube_permute(held, 0)
        bias_full = bias_full + bit_permute(bias_full, 0)
        held = joined(held, arrived)
        arrived = cube_permute(held, 1)
        normed, normed_t, upstream_t = prepare(tokens, cotangent, layer_vectors, (held,))
        bias_full = bias_full + bit_permute(bias_full, 1)
        held, feed_shard, normed, bias_full, spots, where = lax.optimization_barrier(
            (held, feed_shard, normed, bias_full, spots, where)
        )
        held = joined(held, arrived)
        feed_held = feed_shard[None]
        arrived, far_feed = cube_permute(held, 2), cube_permute(feed_held, 0)
        held = joined(held, arrived)
        feed_held = joined(feed_held, far_feed)
        held, feed_held = lax.optimization_barrier((held, feed_held))
        far, far_feed = cube_permute(held, 3), cube_permute(feed_held, 1)
        twin = bit_permute(held, 0)
        feed_held = joined(feed_held, far_feed)
        far, feed_held = lax.optimization_barrier((far, feed_held))
        attend_halves = (held, far, twin, bit_permute(far, 0))
        arrived = cube_permute(feed_held, 2)
        qkv, wide = project(where, spots, normed, attend_halves, bias_full, ())
        feed_held, qkv = lax.optimization_barrier((feed_held, qkv))
        feed_held = joined(feed_held, arrived)
        far, twin = cube_permute(feed_held, 3), bit_permute(feed_held, 0)
        mixture, log_totals = attend_forward(where, lengths, qkv, (feed_held,))
        middle, hidden_in, hidden_t, unit, inverse = attend_out(mixture, wide, tokens, layer_vectors)
        far, hidden_in = lax.optimization_barrier((far, hidden_in))
        feed_halves = (feed_held, far, twin, bit_permute(far, 0))
    else:

        def planes(shard):
            full = lax.all_gather(lax.all_gather(shard, "dp", axis=0, tiled=True), "mp", axis=0)
            full = full.reshape(2, 2, 8, depth // 8, shard.shape[1]).transpose(1, 0, 2, 3, 4)
            return tuple(full.reshape(4, 8, depth // 8, shard.shape[1]))

        normed, normed_t, upstream_t = prepare(tokens, cotangent, layer_vectors, ())
        bias_full = lax.psum(bias_full, "mp")
        qkv, wide = project(where, spots, normed, planes(attend_shard), bias_full, ())
        mixture, log_totals = attend_forward(where, lengths, qkv, ())
        middle, hidden_in, hidden_t, unit, inverse = attend_out(mixture, wide, tokens, layer_vectors)
        feed_halves = planes(feed_shard)
    block_out, back, keep_feed, send_feed, bias_grad = feed(
        where,
        spots,
        hidden_in,
        hidden_t,
        cotangent,
        upstream_t,
        feed_halves,
        bias_full,
        middle,
        layer_vectors,
    )
    middle_grad, mixture_grad, output_grad, middle_sums = middle_back(
        where, lengths, back, unit, inverse, cotangent, mixture, wide, layer_vectors
    )
    if cube:
        feed_parts = [keep_feed, bit_permute(send_feed, 0)]
        keep_feed, mixture_grad = lax.optimization_barrier((keep_feed, mixture_grad))
        feed_parts[0] = keep_feed
        away = leaving(feed_parts, 3)
        packed_grad = attend_backward(where, lengths, qkv, mixture_grad, log_totals, (away,))
        feed_parts = staying(feed_parts, 3) + [cube_permute(away, 3)]
        feed_parts[0], packed_grad = lax.optimization_barrier((feed_parts[0], packed_grad))
        away = leaving(feed_parts, 2)
        onward, rest = cube_permute(away[2:], 2), cube_permute(away[:2], 2)
        feed_parts = staying(feed_parts, 2)
        sums = (middle_sums, bias_grad)
        keep_attend, send_attend, rider = input_grad(
            where, spots, normed_t, packed_grad, output_grad, sums, 16, depth // 8, (away,)
        )
        onward, send_attend = lax.optimization_barrier((onward, send_attend))
        twin_b, rider = with_rider(send_attend[8:], rider, lambda values: bit_permute(values, 0))
        twin_a = bit_permute(send_attend[:8], 0)
        away = (keep_attend[8:].astype(f32) + twin_b.astype(f32)).astype(low)
        arrived, rider = with_rider(away, rider, lambda values: cube_permute(values, 3))
        attend_parts = [keep_attend[:8], twin_a, arrived]
        feed_away = (sum(part[2:].astype(f32) for part in feed_parts) + onward.astype(f32)).astype(low)
        token_grad, token_sums = token_back(
            packed_grad, wide, tokens, middle_grad, layer_vectors, (away, feed_away)
        )
        feed_parts = staying(feed_parts, 1) + [rest, cube_permute(feed_away, 1)]
        token_sums = token_sums + bit_permute(token_sums, 0)
        token_sums = token_sums + cube_permute(token_sums, 3)
        rider = jnp.concatenate([token_sums, rider[2:]], axis=0)
        away = leaving(attend_parts, 2)
        arrived, rider = with_rider(away, rider, lambda values: cube_permute(values, 2))
        attend_parts = staying(attend_parts, 2) + [arrived]
        away, feed_parts[0] = lax.optimization_barrier((away, feed_parts[0]))
        away = leaving(feed_parts, 0)
        feed_parts = staying(feed_parts, 0) + [cube_permute(away, 0)]
        away = leaving(attend_parts, 1)
        arrived, rider = with_rider(away, rider, lambda values: cube_permute(values, 1))
        attend_parts = staying(attend_parts, 1) + [arrived]
        away, feed_parts[0] = lax.optimization_barrier((away, feed_parts[0]))
        feed_total = summed(feed_parts)
        feed_squares = jnp.sum(feed_total * feed_total)
        away = leaving(attend_parts, 0)
        away, feed_squares = lax.optimization_barrier((away, feed_squares))
        arrived, vector_total = with_rider(away, rider, lambda values: cube_permute(values, 0))
        attend_parts = staying(attend_parts, 0) + [arrived]
        attend_total = summed(attend_parts)
    else:
        packed_grad = attend_backward(where, lengths, qkv, mixture_grad, log_totals, ())
        sums = (middle_sums, bias_grad)
        keep_attend, send_attend, vector_total = input_grad(
            where, spots, normed_t, packed_grad, output_grad, sums, 16, depth // 8, ()
        )
        token_grad, token_sums = token_back(packed_grad, wide, tokens, middle_grad, layer_vectors, ())
        vector_total = jnp.concatenate([token_sums, vector_total[2:]], axis=0)
        vector_total = lax.psum(vector_total, ("dp", "mp"))

    if not cube:

        def own_block(keep, send):
            full = jnp.stack([keep, send]).reshape(2, 2, 8, depth // 8, keep.shape[2])
            full = full.transpose(1, 0, 2, 3, 4).reshape(4, depth, keep.shape[2])
            full = lax.psum_scatter(full, "mp", scatter_dimension=0, tiled=False)
            return lax.psum_scatter(full, "dp", scatter_dimension=0, tiled=True).astype(f32)

        attend_total = own_block(keep_attend, send_attend)
        feed_total = own_block(keep_feed, send_feed)
        feed_squares = jnp.sum(feed_total * feed_total)
    owned = jnp.full((8, 128), jnp.sum(attend_total * attend_total) + feed_squares, f32)
    owned = cube_sum(owned) if cube else lax.psum(owned, ("dp", "mp"))
    def turned(array):
        return array.transpose(1, 0, 2)

    state = (
        (turned(input_weight), turned(first_input), turned(second_input)),
        (output_weight, first_output, second_output),
        (expand_weight, first_expand, second_expand),
        (shrink_weight.T, first_shrink.T, second_shrink.T),
        (layer_vectors, first_vectors, second_vectors),
        (head_bias, first_head, second_head),
        tuple(array.reshape(hidden // 128, 128) for array in (expand_bias, first_bias, second_bias)),
    )
    grad_norm, *updates = optimize(where, owned, vector_total, attend_total, feed_total, state)
    grad_norm = grad_norm[0, 0]
    moment_input, square_input, updated_input = (turned(array) for array in updates[:3])
    moment_output, square_output, updated_output = updates[3:6]
    moment_expand, square_expand, updated_expand = updates[6:9]
    moment_shrink, square_shrink, updated_shrink = (array.T for array in updates[9:12])
    moment_vectors, square_vectors, updated_vectors = updates[12:15]
    moment_head, square_head, updated_head = updates[15:18]
    moment_bias, square_bias, updated_bias = (array.reshape(hidden) for array in updates[18:])
    return (
        block_out,
        token_grad,
        grad_norm,
        moment_input,
        square_input,
        updated_input,
        moment_output,
        square_output,
        updated_output,
        moment_expand,
        square_expand,
        updated_expand,
        moment_shrink,
        square_shrink,
        updated_shrink,
        moment_vectors,
        square_vectors,
        updated_vectors,
        moment_head,
        square_head,
        updated_head,
        moment_bias,
        square_bias,
        updated_bias,
    )


def solution(mesh):
    in_specs = (
        P(("dp", "mp"), None),
        P(("dp", "mp"), None),
        P("dp"),
        P("dp", None, "mp"),
        P("mp", "dp"),
        P("dp", "mp"),
        P("mp", "dp"),
        P(),
        P(None, "mp"),
        P("mp"),
        P("dp", None, "mp"),
        P("mp", "dp"),
        P("dp", "mp"),
        P("mp", "dp"),
        P(),
        P(None, "mp"),
        P("mp"),
        P("dp", None, "mp"),
        P("mp", "dp"),
        P("dp", "mp"),
        P("mp", "dp"),
        P(),
        P(None, "mp"),
        P("mp"),
    )
    out_specs = (
        P(("dp", "mp"), None),
        P(("dp", "mp"), None),
        P(),
        P("dp", None, "mp"),
        P("dp", None, "mp"),
        P("dp", None, "mp"),
        P("mp", "dp"),
        P("mp", "dp"),
        P("mp", "dp"),
        P("dp", "mp"),
        P("dp", "mp"),
        P("dp", "mp"),
        P("mp", "dp"),
        P("mp", "dp"),
        P("mp", "dp"),
        P(),
        P(),
        P(),
        P(None, "mp"),
        P(None, "mp"),
        P(None, "mp"),
        P("mp"),
        P("mp"),
        P("mp"),
    )
    return jax.shard_map(shards, mesh=mesh, in_specs=in_specs, out_specs=out_specs, check_vma=False)
```

```python
import functools
import jax
import jax.numpy as jnp
from jax import lax
from jax.experimental import pallas as pl
from jax.experimental.pallas import tpu as pltpu
from jax.sharding import PartitionSpec as P

HEAD_DIM = 64
TILE = 256
STEP = 10

eps_norm = 1e-05
clip_norm = 1.0
beta_one = 0.9
beta_two = 0.999
adam_eps = 1e-08
rate = 0.05
vector_rate = 0.5
decay = 0.01
excluded = -1e30
low = jnp.bfloat16
f32 = jnp.float32
GELU_A = 0.7978845608028654
GELU_B = GELU_A * 0.044715


def params(limit_mib, **kw):
    return pltpu.CompilerParams(vmem_limit_bytes=limit_mib * 1024 * 1024, **kw)


def cost(flops, moved, special=0):
    return pl.CostEstimate(flops=int(flops), bytes_accessed=int(moved), transcendentals=int(special))


def mm(a, b):
    return jnp.dot(a, b, preferred_element_type=f32)


def mm_nt(a, b):
    return lax.dot_general(a, b, (((1,), (1,)), ((), ())), preferred_element_type=f32)


def whole(shape):
    zeros = (0,) * len(shape)
    return pl.BlockSpec(shape, lambda *_: zeros)


def once(shape):
    zeros = (0,) * len(shape)
    return pl.BlockSpec(shape, lambda *_: zeros, pipeline_mode=pl.Buffered(1))


def held_back(body, first, count):
    def run(*refs):
        return body(*refs[:first], *refs[first + count :])

    return run


LATER = pl.BlockSpec(memory_space=pl.ANY)


def far_away(shape, dtype):
    return pltpu.HBM(shape, dtype)


def from_far(*arrays):
    return [pltpu.with_memory_space_constraint(array, pltpu.HBM) for array in arrays]


def sds(shape, dtype):
    return jax.ShapeDtypeStruct(shape, dtype)


def live_blocks(length, count, body):
    for blocks in range(1, count + 1):
        low_end = (blocks - 1) * TILE
        high_end = blocks * TILE
        @pl.when((length > low_end) & (length <= high_end))
        def _(blocks=blocks):
            body(length, blocks)


PAIR = 2 * HEAD_DIM


def span(block):
    return slice(block * TILE, (block + 1) * TILE)


def both_heads(values):
    lane = lax.broadcasted_iota(jnp.int32, values.shape, 1)
    none = jnp.zeros_like(values)
    return jnp.concatenate(
        [jnp.where(lane < HEAD_DIM, values, none), jnp.where(lane >= HEAD_DIM, values, none)], axis=0
    )


def causal_mask():
    key_id = lax.broadcasted_iota(jnp.int32, (TILE, 2 * TILE), 0)
    query_id = lax.broadcasted_iota(jnp.int32, (TILE, 2 * TILE), 1) & (TILE - 1)
    return key_id <= query_id


def forward_body(where_ref, lengths_ref, q_ref, k_ref, v_ref, o_ref, lse_ref, vt_ref):
    seq = q_ref.shape[0]
    vt_ref[...] = v_ref[...].T
    causal = causal_mask()

    def run(length, blocks):
        def scores(b):
            q = q_ref[span(b), :] * jnp.asarray(HEAD_DIM**-0.5, low)
            return mm_nt(k_ref[: (b + 1) * TILE, :], both_heads(q))

        now = scores(0)
        for b in range(blocks):
            start, stop = b * TILE, (b + 1) * TILE
            later = scores(b + 1) if b + 1 < blocks else None
            last = jnp.where(causal, now[start:, :], excluded)
            top = jnp.max(last, axis=0, keepdims=True)
            if b:
                top = jnp.maximum(top, jnp.max(now[:start], axis=0, keepdims=True))
            p = jnp.exp(last - top)
            total = jnp.sum(p, axis=0, keepdims=True)
            pb = p.astype(low)
            if b:
                pf = jnp.exp(now[:start] - top)
                total = total + jnp.sum(pf, axis=0, keepdims=True)
                pb = jnp.concatenate([pf.astype(low), pb], axis=0)
            inverse = 1.0 / total
            lse = top + jnp.log(total)
            outs = []
            for h in range(2):
                at = slice(h * TILE, (h + 1) * TILE)
                out = mm(vt_ref[h * HEAD_DIM : (h + 1) * HEAD_DIM, :stop], pb[:, at])
                outs.append(out * inverse[:, at])
                lse_ref[0, h : h + 1, start:stop] = lse[:, at]
            both = jnp.concatenate(outs, axis=0).T
            row = start + lax.broadcasted_iota(jnp.int32, both.shape, 0)
            o_ref[start:stop, :] = jnp.where(row < length, both, 0.0).astype(low)
            now = later
        if blocks * TILE < seq:
            o_ref[blocks * TILE :, :] = jnp.zeros((seq - blocks * TILE, PAIR), low)
            lse_ref[0, :, blocks * TILE :] = jnp.zeros((2, seq - blocks * TILE), f32)

    live_blocks(lengths_ref[where_ref[2]], seq // TILE, run)


def attend_forward(where, lengths, qkv, after):
    seq, width = qkv.shape[0], qkv.shape[1] // 3
    pair = 2 * HEAD_DIM
    pairs = width // pair
    half = seq * seq * 5 // 8
    spec = lambda part: pl.BlockSpec((seq, pair), lambda i, *_: (0, part * pairs + i))
    return pl.pallas_call(
        held_back(forward_body, 5, len(after)),
        grid_spec=pltpu.PrefetchScalarGridSpec(
            num_scalar_prefetch=2,
            grid=(pairs,),
            in_specs=[spec(0), spec(1), spec(2)] + [LATER] * len(after),
            out_specs=[
                pl.BlockSpec((seq, pair), lambda i, *_: (0, i)),
                pl.BlockSpec((1, 2, seq), lambda i, *_: (i, 0, 0)),
            ],
            scratch_shapes=[pltpu.VMEM((pair, seq), low)],
        ),
        out_shape=[sds((seq, width), low), far_away((pairs, 2, seq), f32)],
        compiler_params=params(20),
        cost_estimate=cost(pairs * 2 * half * 2 * 2 * 256, seq * width * 8, pairs * 2 * half),
        name="attend_forward",
    )(where, lengths, *from_far(qkv, qkv, qkv), *after)


def backward_body(where_ref, lengths_ref, q_ref, k_ref, v_ref, do_ref, lse_ref, out_ref, kt_ref, ksum, vsum):
    seq = q_ref.shape[0]
    scale = HEAD_DIM**-0.5
    kt_ref[...] = k_ref[...].T
    causal = causal_mask()

    def run(length, blocks):
        def scores(b):
            qq = both_heads(q_ref[span(b), :] * jnp.asarray(scale, low))
            uu = both_heads(do_ref[span(b), :])
            stop = (b + 1) * TILE
            return qq, uu, mm_nt(k_ref[:stop, :], qq), mm_nt(v_ref[:stop, :], uu)

        now = scores(blocks - 1)
        for b in reversed(range(blocks)):
            start, stop = b * TILE, (b + 1) * TILE
            later = scores(b - 1) if b else None
            qq, uu, s, dp = now
            lse = jnp.concatenate([lse_ref[0, 0:1, start:stop], lse_ref[0, 1:2, start:stop]], axis=1)
            p = jnp.exp(jnp.where(causal, s[start:], excluded) - lse)
            inner = jnp.sum(p * dp[start:], axis=0, keepdims=True)
            if b:
                pf = jnp.exp(s[:start] - lse)
                inner = inner + jnp.sum(pf * dp[:start], axis=0, keepdims=True)
            ds = (p * (dp[start:] - inner)).astype(low)
            pb = p.astype(low)
            if b:
                ds = jnp.concatenate([(pf * (dp[:start] - inner)).astype(low), ds], axis=0)
                pb = jnp.concatenate([pf.astype(low), pb], axis=0)
            dk, dv = mm(ds, qq), mm(pb, uu)
            if b == blocks - 1:
                ksum[:stop, :] = dk
                vsum[:stop, :] = dv
            else:
                ksum[:stop, :] += dk
                vsum[:stop, :] += dv
            dq = jnp.concatenate(
                [
                    mm(
                        kt_ref[h * HEAD_DIM : (h + 1) * HEAD_DIM, :stop],
                        ds[:, h * TILE : (h + 1) * TILE],
                    )
                    for h in range(2)
                ],
                axis=0,
            )
            out_ref[1, start:stop, :] = ksum[start:stop, :].astype(low)
            out_ref[2, start:stop, :] = vsum[start:stop, :].astype(low)
            out_ref[0, start:stop, :] = (dq.T * scale).astype(low)
            now = later
        if blocks * TILE < seq:
            rest = jnp.zeros((seq - blocks * TILE, PAIR), low)
            for part in range(3):
                out_ref[part, blocks * TILE :, :] = rest

    live_blocks(lengths_ref[where_ref[2]], seq // TILE, run)


def attend_backward(where, lengths, qkv, upstream, lse, after):
    seq, width = upstream.shape
    pair = 2 * HEAD_DIM
    pairs = width // pair
    half = seq * seq * 5 // 8
    spec = lambda part: pl.BlockSpec((seq, pair), lambda i, *_: (0, part * pairs + i))
    own = pl.BlockSpec((seq, pair), lambda i, *_: (0, i))
    return pl.pallas_call(
        held_back(backward_body, 7, len(after)),
        grid_spec=pltpu.PrefetchScalarGridSpec(
            num_scalar_prefetch=2,
            grid=(pairs,),
            in_specs=[spec(0), spec(1), spec(2), own, pl.BlockSpec((1, 2, seq), lambda i, *_: (i, 0, 0))]
            + [LATER] * len(after),
            out_specs=pl.BlockSpec((3, seq, pair), lambda i, *_: (0, 0, i)),
            scratch_shapes=[
                pltpu.VMEM((pair, seq), low),
                pltpu.VMEM((seq, pair), f32),
                pltpu.VMEM((seq, pair), f32),
            ],
        ),
        out_shape=sds((3, seq, width), low),
        compiler_params=params(28),
        cost_estimate=cost(pairs * 2 * half * 5 * 2 * 256, seq * width * 14, pairs * 2 * half),
        name="attend_backward",
    )(where, lengths, *from_far(qkv, qkv, qkv), upstream, *from_far(lse), *after)


def normalize(values):
    average = jnp.mean(values, axis=-1, keepdims=True)
    centred = values - average
    inverse = lax.rsqrt(jnp.mean(centred * centred, axis=-1, keepdims=True) + eps_norm)
    return centred * inverse, inverse


def pull_norm(scaled, unit, inverse):
    first = jnp.mean(scaled, axis=-1, keepdims=True)
    second = jnp.mean(scaled * unit, axis=-1, keepdims=True)
    return inverse * (scaled - first - unit * second)


def columns_of(values):
    return jnp.sum(values, axis=0, keepdims=True)


def pack_body(input_ref, output_ref, expand_ref, shrink_ref, attend_ref, feed_ref):
    width = input_ref.shape[2]
    part = expand_ref.shape[1] // 3
    for index in range(3):
        attend_ref[:, index * width : (index + 1) * width] = input_ref[index].astype(low)
        at = slice(index * part, (index + 1) * part)
        feed_ref[:, 2 * index * part : (2 * index + 1) * part] = expand_ref[:, at].astype(low)
        feed_ref[:, (2 * index + 1) * part : (2 * index + 2) * part] = shrink_ref[:, at].astype(low)
    attend_ref[:, 3 * width :] = output_ref[...].T.astype(low)


def pack(input_weight, output_weight, expand, shrink):
    rows, width = input_weight.shape[1:]
    hidden = expand.shape[1]
    return pl.pallas_call(
        pack_body,
        out_shape=[sds((rows, 4 * width), low), sds((rows, 2 * hidden), low)],
        compiler_params=params(6),
        cost_estimate=cost(rows * hidden, rows * hidden * 18),
        name="pack",
    )(*from_far(input_weight, output_weight, expand, shrink))


def prepare_body(x_ref, up_ref, vec_ref, h_ref, ht_ref, upt_ref):
    unit, _ = normalize(x_ref[...].astype(f32))
    h = (unit * vec_ref[0:1, :] + vec_ref[1:2, :]).astype(low)
    h_ref[...] = h
    ht_ref[...] = h.T
    upt_ref[...] = up_ref[...].T


def prepare(x, up, vectors, after):
    seq, depth = x.shape
    rows = pl.BlockSpec((2 * TILE, depth), lambda i: (i, 0))
    turned = pl.BlockSpec((depth, 2 * TILE), lambda i: (0, i))
    return pl.pallas_call(
        held_back(prepare_body, 3, len(after)),
        grid=(seq // (2 * TILE),),
        in_specs=[rows, rows, once(vectors.shape)] + [LATER] * len(after),
        out_specs=[rows, turned, turned],
        out_shape=[sds((seq, depth), low), far_away((depth, seq), low), far_away((depth, seq), low)],
        compiler_params=params(16),
        cost_estimate=cost(seq * depth * 10, seq * depth * 10),
        name="prepare",
    )(*from_far(x, up), vectors, *after)


def slot(halves, spot, at):
    first, second = halves
    inner = spot & 7
    return jnp.where(spot < 8, first[inner, :, at], second[inner, :, at])


def project_body(
    where_ref, spots_ref, h_ref, mine_a, mine_b, twin_a, twin_b, bias_ref, qkv_ref, wide_ref
):
    part = pl.program_id(0)
    rows = mine_a.shape[1]
    width = mine_a.shape[2] // 4
    groups = wide_ref.shape[1] // rows

    def collect(sources, index):
        at = slice(index * width, (index + 1) * width)
        for group in range(groups):
            pieces = [slot(sources[model % 2], spots_ref[model, group], at) for model in range(4)]
            wide_ref[0, group * rows : (group + 1) * rows, :] = jnp.concatenate(pieces, axis=1)

    for index in range(4):
        for core in range(2):

            @pl.when((part == index) & (where_ref[0] == core))
            def _(index=index, core=core):
                mine, twin = (mine_a, mine_b), (twin_a, twin_b)
                collect((mine, twin) if core == 0 else (twin, mine), index)

    for index in range(3):

        @pl.when(part == index)
        def _(index=index):
            out = mm(h_ref[...], wide_ref[0])
            if index != 1:
                at = slice(index // 2 * width, (index // 2 + 1) * width)
                bias = jnp.concatenate([bias_ref[model : model + 1, at] for model in range(4)], axis=1)
                out = out + bias
            qkv_ref[...] = out.astype(low)


def project(where, spots, h, halves, bias, after):
    seq, depth = h.shape
    return pl.pallas_call(
        held_back(project_body, 8, len(after)),
        grid_spec=pltpu.PrefetchScalarGridSpec(
            num_scalar_prefetch=2,
            grid=(4,),
            in_specs=[
                once((seq, depth)),
                *[once(halves[0].shape)] * 4,
                once(bias.shape),
            ]
            + [LATER] * len(after),
            out_specs=[
                pl.BlockSpec((seq, depth), lambda i, *_: (0, jnp.minimum(i, 2))),
                pl.BlockSpec((1, depth, depth), lambda i, *_: (i, 0, 0)),
            ],
        ),
        out_shape=[far_away((seq, 3 * depth), low), far_away((4, depth, depth), low)],
        compiler_params=params(24),
        cost_estimate=cost(2 * seq * depth * depth * 3, seq * depth * 16),
        name="project",
    )(where, spots, h, *halves, bias, *after)


def attend_out_body(o_ref, w_ref, x_ref, vec_ref, middle_ref, h_ref, ht_ref, unit_ref, inverse_ref):
    middle = x_ref[...].astype(f32) + mm_nt(o_ref[...], w_ref[0]) + vec_ref[4:5, :]
    middle_ref[...] = middle.astype(low)
    unit, inverse = normalize(middle)
    unit_ref[...] = unit.astype(low)
    inverse_ref[...] = jnp.broadcast_to(inverse, inverse_ref.shape)
    h = (unit * vec_ref[2:3, :] + vec_ref[3:4, :]).astype(low)
    h_ref[...] = h
    ht_ref[...] = h.T


def attend_out(o, wide, x, vectors):
    seq, depth = x.shape
    rows = pl.BlockSpec((TILE, depth), lambda i: (i, 0))
    turned = pl.BlockSpec((depth, TILE), lambda i: (0, i))
    return pl.pallas_call(
        attend_out_body,
        grid=(seq // TILE,),
        in_specs=[
            rows,
            pl.BlockSpec((1, depth, depth), lambda i: (3, 0, 0)),
            rows,
            once(vectors.shape),
        ],
        out_specs=[rows, rows, turned, rows, pl.BlockSpec((TILE, 128), lambda i: (i, 0))],
        out_shape=[
            sds((seq, depth), low),
            sds((seq, depth), low),
            sds((depth, seq), low),
            sds((seq, depth), low),
            sds((seq, 128), f32),
        ],
        compiler_params=params(14),
        cost_estimate=cost(2 * seq * depth * depth, seq * depth * 14),
        name="attend_out",
    )(o, *from_far(wide, x), vectors)


def feed_body(
    where_ref,
    spots_ref,
    h2_ref,
    h2t_ref,
    up_ref,
    upt_ref,
    mine_a,
    mine_b,
    twin_a,
    twin_b,
    bias_ref,
    middle_ref,
    vec_ref,
    block_ref,
    back_ref,
    keep_ref,
    send_ref,
    bias_grad_ref,
    out_ref,
    sum_ref,
    wide_ref,
    act_ref,
    pre_ref,
):
    step = pl.program_id(0)
    side = lax.rem(step, 2)
    models = [where_ref[1] ^ (2 * side + core) for core in range(2)]
    rows = mine_a.shape[1]
    part = mine_a.shape[2] // 2
    groups = wide_ref.shape[0] // rows

    @pl.when(step == 0)
    def _():
        out_ref[...] = middle_ref[...].astype(f32) + vec_ref[5:6, :]
        sum_ref[...] = jnp.zeros_like(sum_ref)

    for group in range(groups):
        at = slice(group * rows, (group + 1) * rows)
        own = slot((mine_a, mine_b), spots_ref[models[0], group], slice(None))
        other = slot((twin_a, twin_b), spots_ref[models[1], group], slice(None))
        wide_ref[at, :part] = own[:, :part]
        wide_ref[at, part : 2 * part] = other[:, :part]
        wide_ref[at, 2 * part : 3 * part] = own[:, part:]
        wide_ref[at, 3 * part :] = other[:, part:]

    expand = wide_ref[:, : 2 * part]
    shrink = wide_ref[:, 2 * part :]
    first = step // 2 * part
    skip = bias_ref.shape[1] - bias_grad_ref.shape[1]
    bias = jnp.concatenate(
        [bias_ref[pl.ds(model, 1), pl.ds(pl.multiple_of(skip + first, 128), part)] for model in models],
        axis=1,
    )
    sums = jnp.zeros((1, 2 * part), f32)
    for tile in range(h2_ref.shape[0] // TILE):
        at = slice(tile * TILE, (tile + 1) * TILE)
        u = mm(h2_ref[at, :], expand) + bias
        square = u * u
        th = jnp.tanh(u * (GELU_A + GELU_B * square))
        gate = 0.5 * th + 0.5
        slope = gate + (gate * (1.0 - gate)) * (u * (2.0 * GELU_A + (6.0 * GELU_B) * square))
        pre = (mm(up_ref[at, :], shrink) * slope).astype(low)
        act_ref[at, :] = (u * gate).astype(low)
        pre_ref[at, :] = pre
        sums = sums + columns_of(pre.astype(f32))
    for core, model in enumerate(models):
        bias_grad_ref[pl.ds(model, 1), pl.ds(pl.multiple_of(first, 128), part)] = sums[
            :, core * part : (core + 1) * part
        ]
    out_ref[...] += mm_nt(act_ref[...], shrink)
    sum_ref[...] += mm_nt(pre_ref[...], expand)
    grad_expand = mm(h2t_ref[...], pre_ref[...]).astype(low)
    grad_shrink = mm(upt_ref[...], act_ref[...]).astype(low)
    for group in range(groups):
        at = slice(group * rows, (group + 1) * rows)
        own, other = spots_ref[models[0], group], spots_ref[models[1], group]
        keep_ref[own, :, :part] = grad_expand[at, :part]
        keep_ref[own, :, part:] = grad_shrink[at, :part]
        send_ref[other, :, :part] = grad_expand[at, part:]
        send_ref[other, :, part:] = grad_shrink[at, part:]

    @pl.when(step == pl.num_programs(0) - 1)
    def _():
        block_ref[...] = out_ref[...].astype(low)
        back_ref[...] = sum_ref[...].astype(low)


def feed(where, spots, h2, h2t, up, upt, halves, bias, middle, vectors):
    seq, depth = h2.shape
    half, rows, columns = halves[0].shape
    steps, part = 6, columns // 6
    half_piece = pl.BlockSpec((half, rows, 2 * part), lambda i, *_: (0, 0, i // 2))
    piece = pl.BlockSpec((2 * half, rows, 2 * part), lambda i, *_: (0, 0, i // 2))
    return pl.pallas_call(
        feed_body,
        grid_spec=pltpu.PrefetchScalarGridSpec(
            num_scalar_prefetch=2,
            grid=(steps,),
            in_specs=[
                once((seq, depth)),
                once((depth, seq)),
                once((seq, depth)),
                once((depth, seq)),
                *[half_piece] * 4,
                once(bias.shape),
                once((seq, depth)),
                once(vectors.shape),
            ],
            out_specs=[whole((seq, depth)), whole((seq, depth)), piece, piece, whole((4, 3 * part))],
            scratch_shapes=[
                pltpu.VMEM((seq, depth), f32),
                pltpu.VMEM((seq, depth), f32),
                pltpu.VMEM((depth, 4 * part), low),
                pltpu.VMEM((seq, 2 * part), low),
                pltpu.VMEM((seq, 2 * part), low),
            ],
        ),
        out_shape=[sds((seq, depth), low)] * 2
        + [sds((2 * half, rows, columns), low)] * 2
        + [sds((4, 3 * part), f32)],
        compiler_params=params(31),
        cost_estimate=cost(12 * seq * depth * steps * 2 * part, seq * depth * 40, seq * steps * part),
        name="feed",
    )(where, spots, h2, h2t, *from_far(up, upt), *halves, bias, middle, vectors)


def middle_back_body(
    where_ref,
    lengths_ref,
    back_ref,
    unit_ref,
    inverse_ref,
    up_ref,
    o_ref,
    w_ref,
    vec_ref,
    grad_ref,
    mixture_ref,
    weight_ref,
    sums_ref,
    total_ref,
):
    step = pl.program_id(0)
    unit, inverse = unit_ref[...].astype(f32), inverse_ref[:, 0:1]
    back = back_ref[...].astype(f32)
    up = up_ref[...].astype(f32)
    grad = up + pull_norm(back * vec_ref[2:3, :], unit, inverse)
    rounded = grad.astype(low)
    grad_ref[...] = rounded
    row = step * grad.shape[0] + lax.broadcasted_iota(jnp.int32, grad.shape, 0)
    length = lengths_ref[where_ref[2]]
    mixture_ref[...] = jnp.where(row < length, mm(rounded, w_ref[0]), 0.0).astype(low)
    share = mm(rounded.T, o_ref[...])
    sums = jnp.concatenate(
        [columns_of(back * unit), columns_of(back), columns_of(grad), columns_of(up)], axis=0
    )

    @pl.when(step == 0)
    def _():
        total_ref[...] = share
        sums_ref[...] = sums

    @pl.when(step > 0)
    def _():
        total_ref[...] += share
        sums_ref[...] += sums

    @pl.when(step == pl.num_programs(0) - 1)
    def _():
        weight_ref[...] = total_ref[...].astype(low)


def middle_back(where, lengths, back, unit, inverse, up, o, wide, vectors):
    seq, depth = unit.shape
    rows = pl.BlockSpec((2 * TILE, depth), lambda i, *_: (i, 0))
    return pl.pallas_call(
        middle_back_body,
        grid_spec=pltpu.PrefetchScalarGridSpec(
            num_scalar_prefetch=2,
            grid=(seq // (2 * TILE),),
            in_specs=[
                rows,
                rows,
                pl.BlockSpec((2 * TILE, 128), lambda i, *_: (i, 0)),
                rows,
                rows,
                pl.BlockSpec((1, depth, depth), lambda i, *_: (3, 0, 0)),
                once(vectors.shape),
            ],
            out_specs=[rows, rows, whole((depth, depth)), whole((4, depth))],
            scratch_shapes=[pltpu.VMEM((depth, depth), f32)],
        ),
        out_shape=[
            sds((seq, depth), low),
            sds((seq, depth), low),
            sds((depth, depth), low),
            sds((4, depth), f32),
        ],
        compiler_params=params(24),
        cost_estimate=cost(4 * seq * depth * depth, seq * depth * 28),
        name="middle_back",
    )(where, lengths, back, unit, inverse, *from_far(up), o, *from_far(wide), vectors)


def input_grad_body(
    where_ref,
    spots_ref,
    ht_ref,
    back_ref,
    out_grad_ref,
    middle_ref,
    bias_ref,
    keep_ref,
    send_ref,
    sums_ref,
):
    part = pl.program_id(0)
    rows = keep_ref.shape[1]
    width = keep_ref.shape[2] // 4
    groups = ht_ref.shape[0] // rows

    def spread(targets, index, grad):
        at = slice(index * width, (index + 1) * width)
        for group in range(groups):
            for model in range(4):
                targets[model % 2][spots_ref[model, group], :, at] = grad[
                    group * rows : (group + 1) * rows, model * width : (model + 1) * width
                ]

    for index in range(4):

        @pl.when(part == index)
        def _(index=index):
            if index < 3:
                if index == 0:
                    sums_ref[:2] = jnp.zeros((2, sums_ref.shape[1]), f32)
                    sums_ref[2:6] = middle_ref[...]
                    sums_ref[8:] = bias_ref[...]
                if index != 1:
                    row = 6 + index // 2
                    sums_ref[row : row + 1, :] = columns_of(back_ref[0].astype(f32))
                grad = mm(ht_ref[...], back_ref[0]).astype(low)
            else:
                grad = out_grad_ref[...]
            for core in range(2):

                @pl.when(where_ref[0] == core)
                def _(core=core):
                    spread((keep_ref, send_ref) if core == 0 else (send_ref, keep_ref), index, grad)


def input_grad(where, spots, ht, back, out_grad, sums, slots, rows, after):
    depth, seq = ht.shape
    shape = (slots, rows, 4 * (depth // 4))
    return pl.pallas_call(
        held_back(input_grad_body, 7, len(after)),
        grid_spec=pltpu.PrefetchScalarGridSpec(
            num_scalar_prefetch=2,
            grid=(4,),
            in_specs=[
                once((depth, seq)),
                pl.BlockSpec((1, seq, depth), lambda i, *_: (jnp.minimum(i, 2), 0, 0)),
                once((depth, depth)),
                *[once(array.shape) for array in sums],
            ]
            + [LATER] * len(after),
            out_specs=[
                whole(shape),
                whole(shape),
                whole((12, depth)),
            ],
        ),
        out_shape=[sds(shape, low), sds(shape, low), sds((12, depth), f32)],
        compiler_params=params(24),
        cost_estimate=cost(6 * seq * depth * depth, seq * depth * 14),
        name="input_grad",
    )(where, spots, *from_far(ht), back, out_grad, *sums, *after)


def token_back_body(
    back_ref, w_ref, x_ref, grad_ref, vec_ref, token_ref, sums_ref
):
    step = pl.program_id(0)
    back = mm_nt(back_ref[0], w_ref[0]) + mm_nt(back_ref[1], w_ref[1]) + mm_nt(back_ref[2], w_ref[2])
    unit, inverse = normalize(x_ref[...].astype(f32))
    grad = grad_ref[...].astype(f32)
    token_ref[...] = (grad + pull_norm(back * vec_ref[0:1, :], unit, inverse)).astype(low)
    sums = jnp.concatenate([columns_of(back * unit), columns_of(back)], axis=0)

    @pl.when(step == 0)
    def _():
        sums_ref[...] = sums

    @pl.when(step > 0)
    def _():
        sums_ref[...] += sums


def token_back(back, wide, x, grad, vectors, after):
    seq, depth = x.shape
    rows = pl.BlockSpec((TILE, depth), lambda i: (i, 0))
    return pl.pallas_call(
        held_back(token_back_body, 5, len(after)),
        grid=(seq // TILE,),
        in_specs=[
            pl.BlockSpec((3, TILE, depth), lambda i: (0, i, 0)),
            pl.BlockSpec((3, depth, depth), lambda i: (0, 0, 0)),
            rows,
            rows,
            once(vectors.shape),
        ]
        + [LATER] * len(after),
        out_specs=[rows, whole((2, depth))],
        out_shape=[sds((seq, depth), low), sds((2, depth), f32)],
        compiler_params=params(24),
        cost_estimate=cost(0, 0),
        name="token_back",
    )(back, *from_far(wide, x), grad, vectors, *after)


CORE_ORDERS = ((4, 3, 2, 1), (3, 4, 1, 2))
STAGES = 4


def cube_permute(values, stage):
    pairs = [(device, device ^ (1 << CORE_ORDERS[device & 1][stage])) for device in range(32)]
    return lax.ppermute(values, ("dp", "mp"), pairs)


def bit_permute(values, bit):
    return lax.ppermute(values, ("dp", "mp"), [(device, device ^ (1 << bit)) for device in range(32)])


def place(distance, core):
    spots = [
        sum(((distance >> bit) & 1) << step for step, bit in enumerate(order)) for order in CORE_ORDERS
    ]
    return jnp.where(core == 0, spots[0], spots[1])


def joined(held, arrived):
    return jnp.concatenate([held, arrived], axis=0)


def leaving(parts, stage):
    half = 1 << stage
    return sum(part[half:].astype(f32) for part in parts).astype(low)


def staying(parts, stage):
    return [part[: 1 << stage] for part in parts]


def summed(parts):
    return sum(part[0].astype(f32) for part in parts)


def two_parts(values):
    high = lax.reduce_precision(values, 8, 7)
    rest = lax.reduce_precision(values - high, 8, 7)
    return jnp.concatenate([high, rest], axis=0).astype(low)


def one_part(parts):
    half = parts.shape[0] // 2
    return parts[:half].astype(f32) + parts[half:].astype(f32)


def with_rider(blocks, rider, send):
    count, rows, columns = blocks.shape
    parts = two_parts(rider)
    arrived = send(jnp.concatenate([blocks.reshape(count * rows, columns), parts], axis=0))
    total = one_part(parts) + one_part(arrived[count * rows :])
    return arrived[: count * rows].reshape(count, rows, columns), total


def cube_sum(values, bits=range(5)):
    for bit in bits:
        values = values + bit_permute(values, bit)
    return values


def adam_parts(weight, gradient, first_old, second_old, factor, step_rate):
    scaled = gradient * factor
    moment = beta_one * first_old + (1.0 - beta_one) * scaled
    square = beta_two * second_old + (1.0 - beta_two) * scaled * scaled
    spread = jnp.sqrt(square * (1.0 / (1.0 - beta_two**STEP)))
    ratio = moment * (1.0 / (1.0 - beta_one**STEP)) / (spread + adam_eps)
    return moment, square, weight - step_rate * (ratio + decay * weight)


def optimize_body(where_ref, owned_ref, vector_ref, attend_ref, feed_ref, *refs):
    state, outs = refs[:21], refs[21:]
    vectors = jnp.concatenate([owned_ref[:2], vector_ref[2:]], axis=0)
    total = owned_ref[2:3, 0:1] + jnp.sum(vectors * vectors)
    norm = jnp.sqrt(total)
    factor = clip_norm / jnp.maximum(norm, clip_norm)
    outs[0][...] = norm
    width = state[0].shape[2]
    part = state[6].shape[1] // 3

    def update(param, at, gradient, step_rate):
        weight, first, second = (ref[at] for ref in state[3 * param : 3 * param + 3])
        results = adam_parts(weight, gradient, first, second, factor, step_rate)
        for ref, result in zip(outs[1 + 3 * param : 4 + 3 * param], results):
            ref[at] = result

    for index in range(3):
        update(0, (index,), attend_ref[:, index * width : (index + 1) * width], rate)
    update(1, (...,), attend_ref[:, 3 * width :].T, rate)
    for index in range(3):
        at = (slice(None), slice(index * part, (index + 1) * part))
        first = 2 * index * part
        update(2, at, feed_ref[:, first : first + part], rate)
        update(3, at, feed_ref[:, first + part : first + 2 * part], rate)
    update(4, (...,), vectors[:6], vector_rate)
    model = where_ref[2]
    head = jnp.zeros((2, width), f32)
    for index in range(4):
        head = head + jnp.where(model == index, vectors[6:8, index * width : (index + 1) * width], 0.0)
    update(5, (...,), head, vector_rate)
    bias = vector_ref[pl.ds(8 + model, 1), :]
    bias = jnp.concatenate([bias[:, at : at + 128] for at in range(0, bias.shape[1], 128)], axis=0)
    update(6, (...,), bias, vector_rate)


def optimize(where, owned, vector_total, attend_total, feed_total, state):
    shapes = [sds(group[0].shape, f32) for group in state for _ in range(3)]
    arrays = [array for group in state for array in group]
    return pl.pallas_call(
        optimize_body,
        in_specs=[pl.BlockSpec(memory_space=pltpu.SMEM)]
        + [pl.BlockSpec(memory_space=pltpu.VMEM)] * (4 + len(arrays)),
        out_shape=[sds((1, 1), f32)] + shapes,
        compiler_params=params(20),
        cost_estimate=cost(4e6, 8e6),
        name="optimize",
    )(where, owned, vector_total, attend_total, feed_total, *from_far(*arrays))


def shards(
    tokens,
    cotangent,
    lengths,
    input_weight,
    output_weight,
    expand_weight,
    shrink_weight,
    layer_vectors,
    head_bias,
    expand_bias,
    first_input,
    first_output,
    first_expand,
    first_shrink,
    first_vectors,
    first_head,
    first_bias,
    second_input,
    second_output,
    second_expand,
    second_shrink,
    second_vectors,
    second_head,
    second_bias,
):
    dp_count = lax.axis_size("dp")
    mp_count = lax.axis_size("mp")
    cube = dp_count == 8 and mp_count == 4
    rows = input_weight.shape[0]
    width = input_weight.shape[2]
    hidden = expand_weight.shape[1]
    seq, depth = tokens.shape
    part = hidden // 3
    model_index = lax.axis_index("mp")
    me = lax.axis_index("dp") * mp_count + model_index

    attend_shard, feed_shard = pack(
        input_weight.transpose(1, 0, 2), output_weight, expand_weight, shrink_weight.T
    )
    bias_shard = jnp.concatenate([head_bias.reshape(1, 2 * width), expand_bias[None]], axis=1)

    bias_full = jnp.where(jnp.arange(4)[:, None] == model_index, bias_shard, 0.0)
    if cube:
        core, near = me & 1, model_index
        devices = jnp.arange(32).reshape(8, 4).T
        spots = place(devices ^ me, devices & 1).astype(jnp.int32)
    else:
        core = near = jnp.zeros((), jnp.int32)
        spots = (jnp.arange(4)[:, None] // 2 * 8 + jnp.arange(8)[None]).astype(jnp.int32)
    where = jnp.stack([core, near, model_index]).astype(jnp.int32)

    if cube:
        held = attend_shard[None]
        arrived = cube_permute(held, 0)
        bias_full = bias_full + bit_permute(bias_full, 0)
        held = joined(held, arrived)
        arrived = cube_permute(held, 1)
        normed, normed_t, upstream_t = prepare(tokens, cotangent, layer_vectors, (held,))
        bias_full = bias_full + bit_permute(bias_full, 1)
        held, feed_shard, normed, bias_full, spots, where = lax.optimization_barrier(
            (held, feed_shard, normed, bias_full, spots, where)
        )
        held = joined(held, arrived)
        feed_held = feed_shard[None]
        arrived, far_feed = cube_permute(held, 2), cube_permute(feed_held, 0)
        held = joined(held, arrived)
        feed_held = joined(feed_held, far_feed)
        held, feed_held = lax.optimization_barrier((held, feed_held))
        far, far_feed = cube_permute(held, 3), cube_permute(feed_held, 1)
        twin = bit_permute(held, 0)
        feed_held = joined(feed_held, far_feed)
        far, feed_held = lax.optimization_barrier((far, feed_held))
        attend_halves = (held, far, twin, bit_permute(far, 0))
        arrived = cube_permute(feed_held, 2)
        qkv, wide = project(where, spots, normed, attend_halves, bias_full, ())
        feed_held, qkv = lax.optimization_barrier((feed_held, qkv))
        feed_held = joined(feed_held, arrived)
        far, twin = cube_permute(feed_held, 3), bit_permute(feed_held, 0)
        mixture, log_totals = attend_forward(where, lengths, qkv, (feed_held,))
        middle, hidden_in, hidden_t, unit, inverse = attend_out(mixture, wide, tokens, layer_vectors)
        far, hidden_in = lax.optimization_barrier((far, hidden_in))
        feed_halves = (feed_held, far, twin, bit_permute(far, 0))
    else:

        def planes(shard):
            full = lax.all_gather(lax.all_gather(shard, "dp", axis=0, tiled=True), "mp", axis=0)
            full = full.reshape(2, 2, 8, depth // 8, shard.shape[1]).transpose(1, 0, 2, 3, 4)
            return tuple(full.reshape(4, 8, depth // 8, shard.shape[1]))

        normed, normed_t, upstream_t = prepare(tokens, cotangent, layer_vectors, ())
        bias_full = lax.psum(bias_full, "mp")
        qkv, wide = project(where, spots, normed, planes(attend_shard), bias_full, ())
        mixture, log_totals = attend_forward(where, lengths, qkv, ())
        middle, hidden_in, hidden_t, unit, inverse = attend_out(mixture, wide, tokens, layer_vectors)
        feed_halves = planes(feed_shard)
    block_out, back, keep_feed, send_feed, bias_grad = feed(
        where,
        spots,
        hidden_in,
        hidden_t,
        cotangent,
        upstream_t,
        feed_halves,
        bias_full,
        middle,
        layer_vectors,
    )
    middle_grad, mixture_grad, output_grad, middle_sums = middle_back(
        where, lengths, back, unit, inverse, cotangent, mixture, wide, layer_vectors
    )
    if cube:
        feed_parts = [keep_feed, bit_permute(send_feed, 0)]
        keep_feed, mixture_grad = lax.optimization_barrier((keep_feed, mixture_grad))
        feed_parts[0] = keep_feed
        away = leaving(feed_parts, 3)
        packed_grad = attend_backward(where, lengths, qkv, mixture_grad, log_totals, (away,))
        feed_parts = staying(feed_parts, 3) + [cube_permute(away, 3)]
        feed_parts[0], packed_grad = lax.optimization_barrier((feed_parts[0], packed_grad))
        away = leaving(feed_parts, 2)
        feed_parts = staying(feed_parts, 2) + [cube_permute(away, 2)]
        sums = (middle_sums, bias_grad)
        keep_attend, send_attend, rider = input_grad(
            where, spots, normed_t, packed_grad, output_grad, sums, 16, depth // 8, (away,)
        )
        feed_parts[-1], send_attend = lax.optimization_barrier((feed_parts[-1], send_attend))
        twin_b, rider = with_rider(send_attend[8:], rider, lambda values: bit_permute(values, 0))
        twin_a = bit_permute(send_attend[:8], 0)
        away = (keep_attend[8:].astype(f32) + twin_b.astype(f32)).astype(low)
        arrived, rider = with_rider(away, rider, lambda values: cube_permute(values, 3))
        attend_parts = [keep_attend[:8], twin_a, arrived]
        feed_away = leaving(feed_parts, 1)
        token_grad, token_sums = token_back(
            packed_grad, wide, tokens, middle_grad, layer_vectors, (away, feed_away)
        )
        feed_parts = staying(feed_parts, 1) + [cube_permute(feed_away, 1)]
        attend_parts[0], token_sums = lax.optimization_barrier((attend_parts[0], token_sums))
        away = leaving(attend_parts, 2)
        arrived, rider = with_rider(away, rider, lambda values: cube_permute(values, 2))
        attend_parts = staying(attend_parts, 2) + [arrived]
        away, feed_parts[0] = lax.optimization_barrier((away, feed_parts[0]))
        away = leaving(feed_parts, 0)
        feed_parts = staying(feed_parts, 0) + [cube_permute(away, 0)]
        away = leaving(attend_parts, 1)
        arrived, rider = with_rider(away, rider, lambda values: cube_permute(values, 1))
        attend_parts = staying(attend_parts, 1) + [arrived]
        away, feed_parts[0] = lax.optimization_barrier((away, feed_parts[0]))
        feed_total = summed(feed_parts)
        feed_squares = jnp.sum(feed_total * feed_total)
        away = leaving(attend_parts, 0)
        away, feed_squares = lax.optimization_barrier((away, feed_squares))
        arrived, vector_total = with_rider(away, rider, lambda values: cube_permute(values, 0))
        attend_parts = staying(attend_parts, 0) + [arrived]
        attend_total = summed(attend_parts)
    else:
        packed_grad = attend_backward(where, lengths, qkv, mixture_grad, log_totals, ())
        sums = (middle_sums, bias_grad)
        keep_attend, send_attend, vector_total = input_grad(
            where, spots, normed_t, packed_grad, output_grad, sums, 16, depth // 8, ()
        )
        token_grad, token_sums = token_back(packed_grad, wide, tokens, middle_grad, layer_vectors, ())
        vector_total = lax.psum(vector_total, ("dp", "mp"))

    if not cube:

        def own_block(keep, send):
            full = jnp.stack([keep, send]).reshape(2, 2, 8, depth // 8, keep.shape[2])
            full = full.transpose(1, 0, 2, 3, 4).reshape(4, depth, keep.shape[2])
            full = lax.psum_scatter(full, "mp", scatter_dimension=0, tiled=False)
            return lax.psum_scatter(full, "dp", scatter_dimension=0, tiled=True).astype(f32)

        attend_total = own_block(keep_attend, send_attend)
        feed_total = own_block(keep_feed, send_feed)
        feed_squares = jnp.sum(feed_total * feed_total)
    owned = jnp.sum(attend_total * attend_total) + feed_squares
    row = lax.broadcasted_iota(jnp.int32, (3, depth), 0)
    owned = jnp.where(row == 2, owned, jnp.pad(token_sums, ((0, 1), (0, 0))))
    owned = cube_sum(owned) if cube else lax.psum(owned, ("dp", "mp"))
    def turned(array):
        return array.transpose(1, 0, 2)

    state = (
        (turned(input_weight), turned(first_input), turned(second_input)),
        (output_weight, first_output, second_output),
        (expand_weight, first_expand, second_expand),
        (shrink_weight.T, first_shrink.T, second_shrink.T),
        (layer_vectors, first_vectors, second_vectors),
        (head_bias, first_head, second_head),
        tuple(array.reshape(hidden // 128, 128) for array in (expand_bias, first_bias, second_bias)),
    )
    grad_norm, *updates = optimize(where, owned, vector_total, attend_total, feed_total, state)
    grad_norm = grad_norm[0, 0]
    moment_input, square_input, updated_input = (turned(array) for array in updates[:3])
    moment_output, square_output, updated_output = updates[3:6]
    moment_expand, square_expand, updated_expand = updates[6:9]
    moment_shrink, square_shrink, updated_shrink = (array.T for array in updates[9:12])
    moment_vectors, square_vectors, updated_vectors = updates[12:15]
    moment_head, square_head, updated_head = updates[15:18]
    moment_bias, square_bias, updated_bias = (array.reshape(hidden) for array in updates[18:])
    return (
        block_out,
        token_grad,
        grad_norm,
        moment_input,
        square_input,
        updated_input,
        moment_output,
        square_output,
        updated_output,
        moment_expand,
        square_expand,
        updated_expand,
        moment_shrink,
        square_shrink,
        updated_shrink,
        moment_vectors,
        square_vectors,
        updated_vectors,
        moment_head,
        square_head,
        updated_head,
        moment_bias,
        square_bias,
        updated_bias,
    )


def solution(mesh):
    in_specs = (
        P(("dp", "mp"), None),
        P(("dp", "mp"), None),
        P("dp"),
        P("dp", None, "mp"),
        P("mp", "dp"),
        P("dp", "mp"),
        P("mp", "dp"),
        P(),
        P(None, "mp"),
        P("mp"),
        P("dp", None, "mp"),
        P("mp", "dp"),
        P("dp", "mp"),
        P("mp", "dp"),
        P(),
        P(None, "mp"),
        P("mp"),
        P("dp", None, "mp"),
        P("mp", "dp"),
        P("dp", "mp"),
        P("mp", "dp"),
        P(),
        P(None, "mp"),
        P("mp"),
    )
    out_specs = (
        P(("dp", "mp"), None),
        P(("dp", "mp"), None),
        P(),
        P("dp", None, "mp"),
        P("dp", None, "mp"),
        P("dp", None, "mp"),
        P("mp", "dp"),
        P("mp", "dp"),
        P("mp", "dp"),
        P("dp", "mp"),
        P("dp", "mp"),
        P("dp", "mp"),
        P("mp", "dp"),
        P("mp", "dp"),
        P("mp", "dp"),
        P(),
        P(),
        P(),
        P(None, "mp"),
        P(None, "mp"),
        P(None, "mp"),
        P("mp"),
        P("mp"),
        P("mp"),
    )
    return jax.shard_map(shards, mesh=mesh, in_specs=in_specs, out_specs=out_specs, check_vma=False)
```

```python
import functools
import jax
import jax.numpy as jnp
from jax import lax
from jax.experimental import pallas as pl
from jax.experimental.pallas import tpu as pltpu
from jax.sharding import PartitionSpec as P

HEAD_DIM = 64
TILE = 256
STEP = 10

eps_norm = 1e-05
clip_norm = 1.0
beta_one = 0.9
beta_two = 0.999
adam_eps = 1e-08
rate = 0.05
vector_rate = 0.5
decay = 0.01
excluded = -1e30
low = jnp.bfloat16
f32 = jnp.float32
GELU_A = 0.7978845608028654
GELU_B = GELU_A * 0.044715


def params(limit_mib, **kw):
    return pltpu.CompilerParams(vmem_limit_bytes=limit_mib * 1024 * 1024, **kw)


def cost(flops, moved, special=0):
    return pl.CostEstimate(flops=int(flops), bytes_accessed=int(moved), transcendentals=int(special))


def mm(a, b):
    return jnp.dot(a, b, preferred_element_type=f32)


def mm_nt(a, b):
    return lax.dot_general(a, b, (((1,), (1,)), ((), ())), preferred_element_type=f32)


def whole(shape):
    zeros = (0,) * len(shape)
    return pl.BlockSpec(shape, lambda *_: zeros)


def once(shape):
    zeros = (0,) * len(shape)
    return pl.BlockSpec(shape, lambda *_: zeros, pipeline_mode=pl.Buffered(1))


def held_back(body, first, count):
    def run(*refs):
        return body(*refs[:first], *refs[first + count :])

    return run


LATER = pl.BlockSpec(memory_space=pl.ANY)


def far_away(shape, dtype):
    return pltpu.HBM(shape, dtype)


def from_far(*arrays):
    return [pltpu.with_memory_space_constraint(array, pltpu.HBM) for array in arrays]


def sds(shape, dtype):
    return jax.ShapeDtypeStruct(shape, dtype)


def live_blocks(length, count, body):
    for blocks in range(1, count + 1):
        low_end = (blocks - 1) * TILE
        high_end = blocks * TILE
        @pl.when((length > low_end) & (length <= high_end))
        def _(blocks=blocks):
            body(length, blocks)


PAIR = 2 * HEAD_DIM


def span(block):
    return slice(block * TILE, (block + 1) * TILE)


def both_heads(values):
    lane = lax.broadcasted_iota(jnp.int32, values.shape, 1)
    none = jnp.zeros_like(values)
    return jnp.concatenate(
        [jnp.where(lane < HEAD_DIM, values, none), jnp.where(lane >= HEAD_DIM, values, none)], axis=0
    )


def causal_mask():
    key_id = lax.broadcasted_iota(jnp.int32, (TILE, 2 * TILE), 0)
    query_id = lax.broadcasted_iota(jnp.int32, (TILE, 2 * TILE), 1) & (TILE - 1)
    return key_id <= query_id


def forward_body(where_ref, lengths_ref, q_ref, k_ref, v_ref, o_ref, lse_ref, vt_ref):
    seq = q_ref.shape[0]
    vt_ref[...] = v_ref[...].T
    causal = causal_mask()

    def run(length, blocks):
        def scores(b):
            q = q_ref[span(b), :] * jnp.asarray(HEAD_DIM**-0.5, low)
            return mm_nt(k_ref[: (b + 1) * TILE, :], both_heads(q))

        now = scores(0)
        for b in range(blocks):
            start, stop = b * TILE, (b + 1) * TILE
            later = scores(b + 1) if b + 1 < blocks else None
            last = jnp.where(causal, now[start:, :], excluded)
            top = jnp.max(last, axis=0, keepdims=True)
            if b:
                top = jnp.maximum(top, jnp.max(now[:start], axis=0, keepdims=True))
            p = jnp.exp(last - top)
            total = jnp.sum(p, axis=0, keepdims=True)
            pb = p.astype(low)
            if b:
                pf = jnp.exp(now[:start] - top)
                total = total + jnp.sum(pf, axis=0, keepdims=True)
                pb = jnp.concatenate([pf.astype(low), pb], axis=0)
            inverse = 1.0 / total
            lse = top + jnp.log(total)
            outs = []
            for h in range(2):
                at = slice(h * TILE, (h + 1) * TILE)
                out = mm(vt_ref[h * HEAD_DIM : (h + 1) * HEAD_DIM, :stop], pb[:, at])
                outs.append(out * inverse[:, at])
                lse_ref[0, h : h + 1, start:stop] = lse[:, at]
            both = jnp.concatenate(outs, axis=0).T
            row = start + lax.broadcasted_iota(jnp.int32, both.shape, 0)
            o_ref[start:stop, :] = jnp.where(row < length, both, 0.0).astype(low)
            now = later
        if blocks * TILE < seq:
            o_ref[blocks * TILE :, :] = jnp.zeros((seq - blocks * TILE, PAIR), low)
            lse_ref[0, :, blocks * TILE :] = jnp.zeros((2, seq - blocks * TILE), f32)

    live_blocks(lengths_ref[where_ref[2]], seq // TILE, run)


def attend_forward(where, lengths, qkv, after):
    seq, width = qkv.shape[0], qkv.shape[1] // 3
    pair = 2 * HEAD_DIM
    pairs = width // pair
    half = seq * seq * 5 // 8
    spec = lambda part: pl.BlockSpec((seq, pair), lambda i, *_: (0, part * pairs + i))
    return pl.pallas_call(
        held_back(forward_body, 5, len(after)),
        grid_spec=pltpu.PrefetchScalarGridSpec(
            num_scalar_prefetch=2,
            grid=(pairs,),
            in_specs=[spec(0), spec(1), spec(2)] + [LATER] * len(after),
            out_specs=[
                pl.BlockSpec((seq, pair), lambda i, *_: (0, i)),
                pl.BlockSpec((1, 2, seq), lambda i, *_: (i, 0, 0)),
            ],
            scratch_shapes=[pltpu.VMEM((pair, seq), low)],
        ),
        out_shape=[sds((seq, width), low), far_away((pairs, 2, seq), f32)],
        compiler_params=params(20),
        cost_estimate=cost(pairs * 2 * half * 2 * 2 * 256, seq * width * 8, pairs * 2 * half),
        name="attend_forward",
    )(where, lengths, *from_far(qkv, qkv, qkv), *after)


def backward_body(where_ref, lengths_ref, q_ref, k_ref, v_ref, do_ref, lse_ref, out_ref, kt_ref, ksum, vsum):
    seq = q_ref.shape[0]
    scale = HEAD_DIM**-0.5
    kt_ref[...] = k_ref[...].T
    causal = causal_mask()

    def run(length, blocks):
        def scores(b):
            qq = both_heads(q_ref[span(b), :] * jnp.asarray(scale, low))
            uu = both_heads(do_ref[span(b), :])
            stop = (b + 1) * TILE
            return qq, uu, mm_nt(k_ref[:stop, :], qq), mm_nt(v_ref[:stop, :], uu)

        now = scores(blocks - 1)
        for b in reversed(range(blocks)):
            start, stop = b * TILE, (b + 1) * TILE
            later = scores(b - 1) if b else None
            qq, uu, s, dp = now
            lse = jnp.concatenate([lse_ref[0, 0:1, start:stop], lse_ref[0, 1:2, start:stop]], axis=1)
            p = jnp.exp(jnp.where(causal, s[start:], excluded) - lse)
            inner = jnp.sum(p * dp[start:], axis=0, keepdims=True)
            if b:
                pf = jnp.exp(s[:start] - lse)
                inner = inner + jnp.sum(pf * dp[:start], axis=0, keepdims=True)
            ds = (p * (dp[start:] - inner)).astype(low)
            pb = p.astype(low)
            if b:
                ds = jnp.concatenate([(pf * (dp[:start] - inner)).astype(low), ds], axis=0)
                pb = jnp.concatenate([pf.astype(low), pb], axis=0)
            dk, dv = mm(ds, qq), mm(pb, uu)
            if b == blocks - 1:
                ksum[:stop, :] = dk
                vsum[:stop, :] = dv
            else:
                ksum[:stop, :] += dk
                vsum[:stop, :] += dv
            dq = jnp.concatenate(
                [
                    mm(
                        kt_ref[h * HEAD_DIM : (h + 1) * HEAD_DIM, :stop],
                        ds[:, h * TILE : (h + 1) * TILE],
                    )
                    for h in range(2)
                ],
                axis=0,
            )
            out_ref[1, start:stop, :] = ksum[start:stop, :].astype(low)
            out_ref[2, start:stop, :] = vsum[start:stop, :].astype(low)
            out_ref[0, start:stop, :] = (dq.T * scale).astype(low)
            now = later
        if blocks * TILE < seq:
            rest = jnp.zeros((seq - blocks * TILE, PAIR), low)
            for part in range(3):
                out_ref[part, blocks * TILE :, :] = rest

    live_blocks(lengths_ref[where_ref[2]], seq // TILE, run)


def attend_backward(where, lengths, qkv, upstream, lse, after):
    seq, width = upstream.shape
    pair = 2 * HEAD_DIM
    pairs = width // pair
    half = seq * seq * 5 // 8
    spec = lambda part: pl.BlockSpec((seq, pair), lambda i, *_: (0, part * pairs + i))
    own = pl.BlockSpec((seq, pair), lambda i, *_: (0, i))
    return pl.pallas_call(
        held_back(backward_body, 7, len(after)),
        grid_spec=pltpu.PrefetchScalarGridSpec(
            num_scalar_prefetch=2,
            grid=(pairs,),
            in_specs=[spec(0), spec(1), spec(2), own, pl.BlockSpec((1, 2, seq), lambda i, *_: (i, 0, 0))]
            + [LATER] * len(after),
            out_specs=pl.BlockSpec((3, seq, pair), lambda i, *_: (0, 0, i)),
            scratch_shapes=[
                pltpu.VMEM((pair, seq), low),
                pltpu.VMEM((seq, pair), f32),
                pltpu.VMEM((seq, pair), f32),
            ],
        ),
        out_shape=sds((3, seq, width), low),
        compiler_params=params(28),
        cost_estimate=cost(pairs * 2 * half * 5 * 2 * 256, seq * width * 14, pairs * 2 * half),
        name="attend_backward",
    )(where, lengths, *from_far(qkv, qkv, qkv), upstream, *from_far(lse), *after)


def normalize(values):
    average = jnp.mean(values, axis=-1, keepdims=True)
    centred = values - average
    inverse = lax.rsqrt(jnp.mean(centred * centred, axis=-1, keepdims=True) + eps_norm)
    return centred * inverse, inverse


def pull_norm(scaled, unit, inverse):
    first = jnp.mean(scaled, axis=-1, keepdims=True)
    second = jnp.mean(scaled * unit, axis=-1, keepdims=True)
    return inverse * (scaled - first - unit * second)


def columns_of(values):
    return jnp.sum(values, axis=0, keepdims=True)


def pack_body(input_ref, output_ref, expand_ref, shrink_ref, attend_ref, feed_ref):
    width = input_ref.shape[2]
    part = expand_ref.shape[1] // 3
    for index in range(3):
        attend_ref[:, index * width : (index + 1) * width] = input_ref[index].astype(low)
        at = slice(index * part, (index + 1) * part)
        feed_ref[:, 2 * index * part : (2 * index + 1) * part] = expand_ref[:, at].astype(low)
        feed_ref[:, (2 * index + 1) * part : (2 * index + 2) * part] = shrink_ref[:, at].astype(low)
    attend_ref[:, 3 * width :] = output_ref[...].T.astype(low)


def pack(input_weight, output_weight, expand, shrink):
    rows, width = input_weight.shape[1:]
    hidden = expand.shape[1]
    return pl.pallas_call(
        pack_body,
        out_shape=[sds((rows, 4 * width), low), sds((rows, 2 * hidden), low)],
        compiler_params=params(6),
        cost_estimate=cost(rows * hidden, rows * hidden * 18),
        name="pack",
    )(*from_far(input_weight, output_weight, expand, shrink))


def prepare_body(x_ref, up_ref, vec_ref, h_ref, ht_ref, upt_ref):
    unit, _ = normalize(x_ref[...].astype(f32))
    h = (unit * vec_ref[0:1, :] + vec_ref[1:2, :]).astype(low)
    h_ref[...] = h
    ht_ref[...] = h.T
    upt_ref[...] = up_ref[...].T


def prepare(x, up, vectors, after):
    seq, depth = x.shape
    rows = pl.BlockSpec((2 * TILE, depth), lambda i: (i, 0))
    turned = pl.BlockSpec((depth, 2 * TILE), lambda i: (0, i))
    return pl.pallas_call(
        held_back(prepare_body, 3, len(after)),
        grid=(seq // (2 * TILE),),
        in_specs=[rows, rows, once(vectors.shape)] + [LATER] * len(after),
        out_specs=[rows, turned, turned],
        out_shape=[sds((seq, depth), low), far_away((depth, seq), low), far_away((depth, seq), low)],
        compiler_params=params(16),
        cost_estimate=cost(seq * depth * 10, seq * depth * 10),
        name="prepare",
    )(*from_far(x, up), vectors, *after)


def slot(halves, spot, at):
    first, second = halves
    inner = spot & 7
    return jnp.where(spot < 8, first[inner, :, at], second[inner, :, at])


def project_body(
    where_ref, spots_ref, h_ref, mine_a, mine_b, twin_a, twin_b, bias_ref, qkv_ref, wide_ref
):
    part = pl.program_id(0)
    rows = mine_a.shape[1]
    width = mine_a.shape[2] // 4
    groups = wide_ref.shape[1] // rows

    def collect(sources, index):
        at = slice(index * width, (index + 1) * width)
        for group in range(groups):
            pieces = [slot(sources[model % 2], spots_ref[model, group], at) for model in range(4)]
            wide_ref[0, group * rows : (group + 1) * rows, :] = jnp.concatenate(pieces, axis=1)

    for index in range(4):
        for core in range(2):

            @pl.when((part == index) & (where_ref[0] == core))
            def _(index=index, core=core):
                mine, twin = (mine_a, mine_b), (twin_a, twin_b)
                collect((mine, twin) if core == 0 else (twin, mine), index)

    for index in range(3):

        @pl.when(part == index)
        def _(index=index):
            out = mm(h_ref[...], wide_ref[0])
            if index != 1:
                at = slice(index // 2 * width, (index // 2 + 1) * width)
                bias = jnp.concatenate([bias_ref[model : model + 1, at] for model in range(4)], axis=1)
                out = out + bias
            qkv_ref[...] = out.astype(low)


def project(where, spots, h, halves, bias, after):
    seq, depth = h.shape
    return pl.pallas_call(
        held_back(project_body, 8, len(after)),
        grid_spec=pltpu.PrefetchScalarGridSpec(
            num_scalar_prefetch=2,
            grid=(4,),
            in_specs=[
                once((seq, depth)),
                *[once(halves[0].shape)] * 4,
                once(bias.shape),
            ]
            + [LATER] * len(after),
            out_specs=[
                pl.BlockSpec((seq, depth), lambda i, *_: (0, jnp.minimum(i, 2))),
                pl.BlockSpec((1, depth, depth), lambda i, *_: (i, 0, 0)),
            ],
        ),
        out_shape=[far_away((seq, 3 * depth), low), far_away((4, depth, depth), low)],
        compiler_params=params(24),
        cost_estimate=cost(2 * seq * depth * depth * 3, seq * depth * 16),
        name="project",
    )(where, spots, h, *halves, bias, *after)


def attend_out_body(o_ref, w_ref, x_ref, vec_ref, middle_ref, h_ref, ht_ref, unit_ref, inverse_ref):
    middle = x_ref[...].astype(f32) + mm_nt(o_ref[...], w_ref[0]) + vec_ref[4:5, :]
    middle_ref[...] = middle.astype(low)
    unit, inverse = normalize(middle)
    unit_ref[...] = unit.astype(low)
    inverse_ref[...] = jnp.broadcast_to(inverse, inverse_ref.shape)
    h = (unit * vec_ref[2:3, :] + vec_ref[3:4, :]).astype(low)
    h_ref[...] = h
    ht_ref[...] = h.T


def attend_out(o, wide, x, vectors):
    seq, depth = x.shape
    rows = pl.BlockSpec((TILE, depth), lambda i: (i, 0))
    turned = pl.BlockSpec((depth, TILE), lambda i: (0, i))
    return pl.pallas_call(
        attend_out_body,
        grid=(seq // TILE,),
        in_specs=[
            rows,
            pl.BlockSpec((1, depth, depth), lambda i: (3, 0, 0)),
            rows,
            once(vectors.shape),
        ],
        out_specs=[rows, rows, turned, rows, pl.BlockSpec((TILE, 128), lambda i: (i, 0))],
        out_shape=[
            sds((seq, depth), low),
            sds((seq, depth), low),
            sds((depth, seq), low),
            sds((seq, depth), low),
            sds((seq, 128), f32),
        ],
        compiler_params=params(14),
        cost_estimate=cost(2 * seq * depth * depth, seq * depth * 14),
        name="attend_out",
    )(o, *from_far(wide, x), vectors)


def feed_body(
    where_ref,
    spots_ref,
    h2_ref,
    h2t_ref,
    up_ref,
    upt_ref,
    mine_a,
    mine_b,
    twin_a,
    twin_b,
    mine_c,
    mine_d,
    twin_c,
    twin_d,
    bias_ref,
    middle_ref,
    vec_ref,
    block_ref,
    back_ref,
    keep_a,
    send_a,
    keep_b,
    send_b,
    bias_grad_ref,
    out_ref,
    sum_ref,
    wide_ref,
    act_ref,
    pre_ref,
):
    step = pl.program_id(0)
    side = lax.rem(step, 2)
    models = [where_ref[1] ^ (2 * side + core) for core in range(2)]
    part = mine_a.shape[2] // 2
    groups = spots_ref.shape[1]
    rows = wide_ref.shape[0] // groups
    split = mine_a.shape[1]
    pieces = (
        ((mine_a, mine_b), (twin_a, twin_b), keep_a, send_a, 0, slice(0, split)),
        ((mine_c, mine_d), (twin_c, twin_d), keep_b, send_b, 4, slice(split, rows)),
    )

    @pl.when(step == 0)
    def _():
        out_ref[...] = middle_ref[...].astype(f32) + vec_ref[5:6, :]
        sum_ref[...] = jnp.zeros_like(sum_ref)

    for group in range(groups):
        for mine, twin, _, _, table, within in pieces:
            at = slice(group * rows + within.start, group * rows + within.stop)
            own = slot(mine, spots_ref[table + models[0], group], slice(None))
            other = slot(twin, spots_ref[table + models[1], group], slice(None))
            wide_ref[at, :part] = own[:, :part]
            wide_ref[at, part : 2 * part] = other[:, :part]
            wide_ref[at, 2 * part : 3 * part] = own[:, part:]
            wide_ref[at, 3 * part :] = other[:, part:]

    expand = wide_ref[:, : 2 * part]
    shrink = wide_ref[:, 2 * part :]
    first = step // 2 * part
    skip = bias_ref.shape[1] - bias_grad_ref.shape[1]
    bias = jnp.concatenate(
        [bias_ref[pl.ds(model, 1), pl.ds(pl.multiple_of(skip + first, 128), part)] for model in models],
        axis=1,
    )
    sums = jnp.zeros((1, 2 * part), f32)
    for tile in range(h2_ref.shape[0] // TILE):
        at = slice(tile * TILE, (tile + 1) * TILE)
        u = mm(h2_ref[at, :], expand) + bias
        square = u * u
        th = jnp.tanh(u * (GELU_A + GELU_B * square))
        gate = 0.5 * th + 0.5
        slope = gate + (gate * (1.0 - gate)) * (u * (2.0 * GELU_A + (6.0 * GELU_B) * square))
        pre = (mm(up_ref[at, :], shrink) * slope).astype(low)
        act_ref[at, :] = (u * gate).astype(low)
        pre_ref[at, :] = pre
        sums = sums + columns_of(pre.astype(f32))
    for core, model in enumerate(models):
        bias_grad_ref[pl.ds(model, 1), pl.ds(pl.multiple_of(first, 128), part)] = sums[
            :, core * part : (core + 1) * part
        ]
    out_ref[...] += mm_nt(act_ref[...], shrink)
    sum_ref[...] += mm_nt(pre_ref[...], expand)
    grad_expand = mm(h2t_ref[...], pre_ref[...]).astype(low)
    grad_shrink = mm(upt_ref[...], act_ref[...]).astype(low)
    for group in range(groups):
        for _, _, keep, send, table, within in pieces:
            at = slice(group * rows + within.start, group * rows + within.stop)
            own, other = spots_ref[table + models[0], group], spots_ref[table + models[1], group]
            keep[own, :, :part] = grad_expand[at, :part]
            keep[own, :, part:] = grad_shrink[at, :part]
            send[other, :, :part] = grad_expand[at, part:]
            send[other, :, part:] = grad_shrink[at, part:]

    @pl.when(step == pl.num_programs(0) - 1)
    def _():
        block_ref[...] = out_ref[...].astype(low)
        back_ref[...] = sum_ref[...].astype(low)


def feed(where, spots, h2, h2t, up, upt, halves, bias, middle, vectors):
    seq, depth = h2.shape
    half, _, columns = halves[0].shape
    steps, part = 6, columns // 6
    splits = [halves[0].shape[1], halves[4].shape[1]]

    def piece(count, rows):
        return pl.BlockSpec((count, rows, 2 * part), lambda i, *_: (0, 0, i // 2))

    return pl.pallas_call(
        feed_body,
        grid_spec=pltpu.PrefetchScalarGridSpec(
            num_scalar_prefetch=2,
            grid=(steps,),
            in_specs=[
                once((seq, depth)),
                once((depth, seq)),
                once((seq, depth)),
                once((depth, seq)),
                *[piece(half, rows) for rows in splits for _ in range(4)],
                once(bias.shape),
                once((seq, depth)),
                once(vectors.shape),
            ],
            out_specs=[whole((seq, depth)), whole((seq, depth))]
            + [piece(2 * half, rows) for rows in splits for _ in range(2)]
            + [whole((4, 3 * part))],
            scratch_shapes=[
                pltpu.VMEM((seq, depth), f32),
                pltpu.VMEM((seq, depth), f32),
                pltpu.VMEM((depth, 4 * part), low),
                pltpu.VMEM((seq, 2 * part), low),
                pltpu.VMEM((seq, 2 * part), low),
            ],
        ),
        out_shape=[sds((seq, depth), low)] * 2
        + [sds((2 * half, rows, columns), low) for rows in splits for _ in range(2)]
        + [sds((4, 3 * part), f32)],
        compiler_params=params(31),
        cost_estimate=cost(12 * seq * depth * steps * 2 * part, seq * depth * 40, seq * steps * part),
        name="feed",
    )(where, spots, h2, h2t, *from_far(up, upt), *halves, bias, middle, vectors)


def middle_back_body(
    where_ref,
    lengths_ref,
    back_ref,
    unit_ref,
    inverse_ref,
    up_ref,
    o_ref,
    w_ref,
    vec_ref,
    grad_ref,
    mixture_ref,
    weight_ref,
    sums_ref,
    total_ref,
):
    step = pl.program_id(0)
    unit, inverse = unit_ref[...].astype(f32), inverse_ref[:, 0:1]
    back = back_ref[...].astype(f32)
    up = up_ref[...].astype(f32)
    grad = up + pull_norm(back * vec_ref[2:3, :], unit, inverse)
    rounded = grad.astype(low)
    grad_ref[...] = rounded
    row = step * grad.shape[0] + lax.broadcasted_iota(jnp.int32, grad.shape, 0)
    length = lengths_ref[where_ref[2]]
    mixture_ref[...] = jnp.where(row < length, mm(rounded, w_ref[0]), 0.0).astype(low)
    share = mm(rounded.T, o_ref[...])
    sums = jnp.concatenate(
        [columns_of(back * unit), columns_of(back), columns_of(grad), columns_of(up)], axis=0
    )

    @pl.when(step == 0)
    def _():
        total_ref[...] = share
        sums_ref[...] = sums

    @pl.when(step > 0)
    def _():
        total_ref[...] += share
        sums_ref[...] += sums

    @pl.when(step == pl.num_programs(0) - 1)
    def _():
        weight_ref[...] = total_ref[...].astype(low)


def middle_back(where, lengths, back, unit, inverse, up, o, wide, vectors):
    seq, depth = unit.shape
    rows = pl.BlockSpec((2 * TILE, depth), lambda i, *_: (i, 0))
    return pl.pallas_call(
        middle_back_body,
        grid_spec=pltpu.PrefetchScalarGridSpec(
            num_scalar_prefetch=2,
            grid=(seq // (2 * TILE),),
            in_specs=[
                rows,
                rows,
                pl.BlockSpec((2 * TILE, 128), lambda i, *_: (i, 0)),
                rows,
                rows,
                pl.BlockSpec((1, depth, depth), lambda i, *_: (3, 0, 0)),
                once(vectors.shape),
            ],
            out_specs=[rows, rows, whole((depth, depth)), whole((4, depth))],
            scratch_shapes=[pltpu.VMEM((depth, depth), f32)],
        ),
        out_shape=[
            sds((seq, depth), low),
            sds((seq, depth), low),
            sds((depth, depth), low),
            sds((4, depth), f32),
        ],
        compiler_params=params(24),
        cost_estimate=cost(4 * seq * depth * depth, seq * depth * 28),
        name="middle_back",
    )(where, lengths, back, unit, inverse, *from_far(up), o, *from_far(wide), vectors)


def input_grad_body(
    where_ref,
    spots_ref,
    ht_ref,
    back_ref,
    out_grad_ref,
    middle_ref,
    bias_ref,
    keep_ref,
    send_ref,
    sums_ref,
):
    part = pl.program_id(0)
    rows = keep_ref.shape[1]
    width = keep_ref.shape[2] // 4
    groups = ht_ref.shape[0] // rows

    def spread(targets, index, grad):
        at = slice(index * width, (index + 1) * width)
        for group in range(groups):
            for model in range(4):
                targets[model % 2][spots_ref[model, group], :, at] = grad[
                    group * rows : (group + 1) * rows, model * width : (model + 1) * width
                ]

    for index in range(4):

        @pl.when(part == index)
        def _(index=index):
            if index < 3:
                if index == 0:
                    sums_ref[:2] = jnp.zeros((2, sums_ref.shape[1]), f32)
                    sums_ref[2:6] = middle_ref[...]
                    sums_ref[8:] = bias_ref[...]
                if index != 1:
                    row = 6 + index // 2
                    sums_ref[row : row + 1, :] = columns_of(back_ref[0].astype(f32))
                grad = mm(ht_ref[...], back_ref[0]).astype(low)
            else:
                grad = out_grad_ref[...]
            for core in range(2):

                @pl.when(where_ref[0] == core)
                def _(core=core):
                    spread((keep_ref, send_ref) if core == 0 else (send_ref, keep_ref), index, grad)


def input_grad(where, spots, ht, back, out_grad, sums, slots, rows, after):
    depth, seq = ht.shape
    shape = (slots, rows, 4 * (depth // 4))
    return pl.pallas_call(
        held_back(input_grad_body, 7, len(after)),
        grid_spec=pltpu.PrefetchScalarGridSpec(
            num_scalar_prefetch=2,
            grid=(4,),
            in_specs=[
                once((depth, seq)),
                pl.BlockSpec((1, seq, depth), lambda i, *_: (jnp.minimum(i, 2), 0, 0)),
                once((depth, depth)),
                *[once(array.shape) for array in sums],
            ]
            + [LATER] * len(after),
            out_specs=[
                whole(shape),
                whole(shape),
                whole((12, depth)),
            ],
        ),
        out_shape=[sds(shape, low), sds(shape, low), sds((12, depth), f32)],
        compiler_params=params(24),
        cost_estimate=cost(6 * seq * depth * depth, seq * depth * 14),
        name="input_grad",
    )(where, spots, *from_far(ht), back, out_grad, *sums, *after)


def token_back_body(
    back_ref, w_ref, x_ref, grad_ref, vec_ref, token_ref, sums_ref
):
    step = pl.program_id(0)
    back = mm_nt(back_ref[0], w_ref[0]) + mm_nt(back_ref[1], w_ref[1]) + mm_nt(back_ref[2], w_ref[2])
    unit, inverse = normalize(x_ref[...].astype(f32))
    grad = grad_ref[...].astype(f32)
    token_ref[...] = (grad + pull_norm(back * vec_ref[0:1, :], unit, inverse)).astype(low)
    sums = jnp.concatenate([columns_of(back * unit), columns_of(back)], axis=0)

    @pl.when(step == 0)
    def _():
        sums_ref[...] = sums

    @pl.when(step > 0)
    def _():
        sums_ref[...] += sums


def token_back(back, wide, x, grad, vectors, after):
    seq, depth = x.shape
    rows = pl.BlockSpec((TILE, depth), lambda i: (i, 0))
    return pl.pallas_call(
        held_back(token_back_body, 5, len(after)),
        grid=(seq // TILE,),
        in_specs=[
            pl.BlockSpec((3, TILE, depth), lambda i: (0, i, 0)),
            pl.BlockSpec((3, depth, depth), lambda i: (0, 0, 0)),
            rows,
            rows,
            once(vectors.shape),
        ]
        + [LATER] * len(after),
        out_specs=[rows, whole((2, depth))],
        out_shape=[sds((seq, depth), low), sds((2, depth), f32)],
        compiler_params=params(24),
        cost_estimate=cost(0, 0),
        name="token_back",
    )(back, *from_far(wide, x), grad, vectors, *after)


CORE_ORDERS = ((4, 3, 2, 1), (3, 4, 1, 2))
LATE_ORDERS = ((2, 1, 4, 3), (1, 2, 3, 4))
STAGES = 4


def cube_permute(values, stage, orders=CORE_ORDERS):
    pairs = [(device, device ^ (1 << orders[device & 1][stage])) for device in range(32)]
    return lax.ppermute(values, ("dp", "mp"), pairs)


def bit_permute(values, bit):
    return lax.ppermute(values, ("dp", "mp"), [(device, device ^ (1 << bit)) for device in range(32)])


def place(distance, core, orders):
    spots = [
        sum(((distance >> bit) & 1) << step for step, bit in enumerate(order)) for order in orders
    ]
    return jnp.where(core == 0, spots[0], spots[1])


def joined(held, arrived):
    return jnp.concatenate([held, arrived], axis=0)


def leaving(parts, stage):
    half = 1 << stage
    return sum(part[half:].astype(f32) for part in parts).astype(low)


def staying(parts, stage):
    return [part[: 1 << stage] for part in parts]


def summed(parts):
    return sum(part[0].astype(f32) for part in parts)


def two_parts(values):
    high = lax.reduce_precision(values, 8, 7)
    rest = lax.reduce_precision(values - high, 8, 7)
    return jnp.concatenate([high, rest], axis=0).astype(low)


def one_part(parts):
    half = parts.shape[0] // 2
    return parts[:half].astype(f32) + parts[half:].astype(f32)


def with_rider(blocks, rider, send):
    count, rows, columns = blocks.shape
    parts = two_parts(rider)
    arrived = send(jnp.concatenate([blocks.reshape(count * rows, columns), parts], axis=0))
    total = one_part(parts) + one_part(arrived[count * rows :])
    return arrived[: count * rows].reshape(count, rows, columns), total


def cube_sum(values, bits=range(5)):
    for bit in bits:
        values = values + bit_permute(values, bit)
    return values


def adam_parts(weight, gradient, first_old, second_old, factor, step_rate):
    scaled = gradient * factor
    moment = beta_one * first_old + (1.0 - beta_one) * scaled
    square = beta_two * second_old + (1.0 - beta_two) * scaled * scaled
    spread = jnp.sqrt(square * (1.0 / (1.0 - beta_two**STEP)))
    ratio = moment * (1.0 / (1.0 - beta_one**STEP)) / (spread + adam_eps)
    return moment, square, weight - step_rate * (ratio + decay * weight)


def optimize_body(where_ref, owned_ref, vector_ref, attend_ref, feed_a, feed_b, *refs):
    state, outs = refs[:21], refs[21:]
    vectors = jnp.concatenate([owned_ref[:2], vector_ref[2:]], axis=0)
    total = owned_ref[2:3, 0:1] + jnp.sum(vectors * vectors)
    norm = jnp.sqrt(total)
    factor = clip_norm / jnp.maximum(norm, clip_norm)
    outs[0][...] = norm
    width = state[0].shape[2]
    part = state[6].shape[1] // 3

    def update(param, at, gradient, step_rate):
        weight, first, second = (ref[at] for ref in state[3 * param : 3 * param + 3])
        results = adam_parts(weight, gradient, first, second, factor, step_rate)
        for ref, result in zip(outs[1 + 3 * param : 4 + 3 * param], results):
            ref[at] = result

    for index in range(3):
        update(0, (index,), attend_ref[:, index * width : (index + 1) * width], rate)
    update(1, (...,), attend_ref[:, 3 * width :].T, rate)
    split, rows = feed_a.shape[0], state[6].shape[0]
    for feed_ref, within in ((feed_a, slice(0, split)), (feed_b, slice(split, rows))):
        for index in range(3):
            at = (within, slice(index * part, (index + 1) * part))
            first = 2 * index * part
            update(2, at, feed_ref[:, first : first + part], rate)
            update(3, at, feed_ref[:, first + part : first + 2 * part], rate)
    update(4, (...,), vectors[:6], vector_rate)
    model = where_ref[2]
    head = jnp.zeros((2, width), f32)
    for index in range(4):
        head = head + jnp.where(model == index, vectors[6:8, index * width : (index + 1) * width], 0.0)
    update(5, (...,), head, vector_rate)
    bias = vector_ref[pl.ds(8 + model, 1), :]
    bias = jnp.concatenate([bias[:, at : at + 128] for at in range(0, bias.shape[1], 128)], axis=0)
    update(6, (...,), bias, vector_rate)


def optimize(where, owned, vector_total, attend_total, feed_totals, state):
    shapes = [sds(group[0].shape, f32) for group in state for _ in range(3)]
    arrays = [array for group in state for array in group]
    return pl.pallas_call(
        optimize_body,
        in_specs=[pl.BlockSpec(memory_space=pltpu.SMEM)]
        + [pl.BlockSpec(memory_space=pltpu.VMEM)] * (5 + len(arrays)),
        out_shape=[sds((1, 1), f32)] + shapes,
        compiler_params=params(20),
        cost_estimate=cost(4e6, 8e6),
        name="optimize",
    )(where, owned, vector_total, attend_total, *feed_totals, *from_far(*arrays))


def shards(
    tokens,
    cotangent,
    lengths,
    input_weight,
    output_weight,
    expand_weight,
    shrink_weight,
    layer_vectors,
    head_bias,
    expand_bias,
    first_input,
    first_output,
    first_expand,
    first_shrink,
    first_vectors,
    first_head,
    first_bias,
    second_input,
    second_output,
    second_expand,
    second_shrink,
    second_vectors,
    second_head,
    second_bias,
):
    dp_count = lax.axis_size("dp")
    mp_count = lax.axis_size("mp")
    cube = dp_count == 8 and mp_count == 4
    rows = input_weight.shape[0]
    width = input_weight.shape[2]
    hidden = expand_weight.shape[1]
    seq, depth = tokens.shape
    part = hidden // 3
    model_index = lax.axis_index("mp")
    me = lax.axis_index("dp") * mp_count + model_index

    attend_shard, feed_shard = pack(
        input_weight.transpose(1, 0, 2), output_weight, expand_weight, shrink_weight.T
    )
    bias_shard = jnp.concatenate([head_bias.reshape(1, 2 * width), expand_bias[None]], axis=1)

    bias_full = jnp.where(jnp.arange(4)[:, None] == model_index, bias_shard, 0.0)
    if cube:
        core, near = me & 1, model_index
        devices = jnp.arange(32).reshape(8, 4).T
        spots = jnp.concatenate(
            [place(devices ^ me, devices & 1, orders) for orders in (CORE_ORDERS, LATE_ORDERS)]
        ).astype(jnp.int32)
    else:
        core = near = jnp.zeros((), jnp.int32)
        spots = (jnp.arange(8)[:, None] % 4 // 2 * 8 + jnp.arange(8)[None]).astype(jnp.int32)
    where = jnp.stack([core, near, model_index]).astype(jnp.int32)

    if cube:
        split = rows * 2 // 3
        held, early, late = attend_shard[None], feed_shard[None, :split], feed_shard[None, split:]
        arrived, far_late = cube_permute(held, 0), cube_permute(late, 0, LATE_ORDERS)
        bias_full = bias_full + bit_permute(bias_full, 0)
        held = joined(held, arrived)
        arrived = cube_permute(held, 1)
        normed, normed_t, upstream_t = prepare(tokens, cotangent, layer_vectors, (held,))
        bias_full = bias_full + bit_permute(bias_full, 1)
        late = joined(late, far_late)
        held, early, late, normed, bias_full, spots, where = lax.optimization_barrier(
            (held, early, late, normed, bias_full, spots, where)
        )
        held = joined(held, arrived)
        arrived, far_early = cube_permute(held, 2), cube_permute(early, 0)
        far_late = cube_permute(late, 1, LATE_ORDERS)
        held, early, late = joined(held, arrived), joined(early, far_early), joined(late, far_late)
        held, early, late = lax.optimization_barrier((held, early, late))
        far, far_early = cube_permute(held, 3), cube_permute(early, 1)
        twin = bit_permute(held, 0)
        early = joined(early, far_early)
        far, early, late = lax.optimization_barrier((far, early, late))
        attend_halves = (held, far, twin, bit_permute(far, 0))
        far_early, far_late = cube_permute(early, 2), cube_permute(late, 2, LATE_ORDERS)
        qkv, wide = project(where, spots, normed, attend_halves, bias_full, ())
        far_early, far_late, qkv = lax.optimization_barrier((far_early, far_late, qkv))
        early, late = joined(early, far_early), joined(late, far_late)
        far_early, far_late = cube_permute(early, 3), cube_permute(late, 3, LATE_ORDERS)
        twin_early, twin_late = bit_permute(early, 0), bit_permute(late, 0)
        mixture, log_totals = attend_forward(where, lengths, qkv, (early, late))
        middle, hidden_in, hidden_t, unit, inverse = attend_out(mixture, wide, tokens, layer_vectors)
        far_early, far_late, twin_late, hidden_in = lax.optimization_barrier(
            (far_early, far_late, twin_late, hidden_in)
        )
        feed_halves = (early, far_early, twin_early, bit_permute(far_early, 0)) + (
            late,
            far_late,
            twin_late,
            bit_permute(far_late, 0),
        )
    else:

        def planes(shard):
            full = lax.all_gather(lax.all_gather(shard, "dp", axis=0, tiled=True), "mp", axis=0)
            full = full.reshape(2, 2, 8, depth // 8, shard.shape[1]).transpose(1, 0, 2, 3, 4)
            return tuple(full.reshape(4, 8, depth // 8, shard.shape[1]))

        normed, normed_t, upstream_t = prepare(tokens, cotangent, layer_vectors, ())
        bias_full = lax.psum(bias_full, "mp")
        qkv, wide = project(where, spots, normed, planes(attend_shard), bias_full, ())
        mixture, log_totals = attend_forward(where, lengths, qkv, ())
        middle, hidden_in, hidden_t, unit, inverse = attend_out(mixture, wide, tokens, layer_vectors)
        split = depth // 8 * 2 // 3
        feed_planes = planes(feed_shard)
        feed_halves = tuple(array[:, :split] for array in feed_planes) + tuple(
            array[:, split:] for array in feed_planes
        )
    block_out, back, keep_early, send_early, keep_late, send_late, bias_grad = feed(
        where,
        spots,
        hidden_in,
        hidden_t,
        cotangent,
        upstream_t,
        feed_halves,
        bias_full,
        middle,
        layer_vectors,
    )
    middle_grad, mixture_grad, output_grad, middle_sums = middle_back(
        where, lengths, back, unit, inverse, cotangent, mixture, wide, layer_vectors
    )
    if cube:
        early = [keep_early, bit_permute(send_early, 0)]
        late = [keep_late, bit_permute(send_late, 0)]
        early[0], late[0], mixture_grad = lax.optimization_barrier((early[0], late[0], mixture_grad))
        away, far_away_late = leaving(early, 3), leaving(late, 3)
        packed_grad = attend_backward(
            where, lengths, qkv, mixture_grad, log_totals, (away, far_away_late)
        )
        early = staying(early, 3) + [cube_permute(away, 3)]
        late = staying(late, 3) + [cube_permute(far_away_late, 3, LATE_ORDERS)]
        early[0], late[0], packed_grad = lax.optimization_barrier((early[0], late[0], packed_grad))
        away, far_away_late = leaving(early, 2), leaving(late, 2)
        sums = (middle_sums, bias_grad)
        keep_attend, send_attend, rider = input_grad(
            where, spots, normed_t, packed_grad, output_grad, sums, 16, depth // 8, (away, far_away_late)
        )
        early = staying(early, 2) + [cube_permute(away, 2)]
        late = staying(late, 2) + [cube_permute(far_away_late, 2, LATE_ORDERS)]
        early[-1], late[-1], send_attend = lax.optimization_barrier((early[-1], late[-1], send_attend))
        twin_b, rider = with_rider(send_attend[8:], rider, lambda values: bit_permute(values, 0))
        twin_a = bit_permute(send_attend[:8], 0)
        away = (keep_attend[8:].astype(f32) + twin_b.astype(f32)).astype(low)
        arrived, rider = with_rider(away, rider, lambda values: cube_permute(values, 3))
        attend_parts = [keep_attend[:8], twin_a, arrived]
        feed_away = leaving(early, 1)
        token_grad, token_sums = token_back(
            packed_grad, wide, tokens, middle_grad, layer_vectors, (away, feed_away)
        )
        early = staying(early, 1) + [cube_permute(feed_away, 1)]
        attend_parts[0], late[0], token_sums = lax.optimization_barrier(
            (attend_parts[0], late[0], token_sums)
        )
        away = leaving(attend_parts, 2)
        arrived, rider = with_rider(away, rider, lambda values: cube_permute(values, 2))
        attend_parts = staying(attend_parts, 2) + [arrived]
        away, early[0] = lax.optimization_barrier((away, early[0]))
        feed_away = leaving(early, 0)
        early = staying(early, 0) + [cube_permute(feed_away, 0)]
        feed_away = leaving(late, 1)
        away = leaving(attend_parts, 1)
        arrived, rider = with_rider(away, rider, lambda values: cube_permute(values, 1))
        late = staying(late, 1) + [cube_permute(feed_away, 1, LATE_ORDERS)]
        attend_parts = staying(attend_parts, 1) + [arrived]
        away, early[0] = lax.optimization_barrier((away, early[0]))
        early_total = summed(early)
        feed_away = leaving(late, 0)
        away = leaving(attend_parts, 0)
        away, early_total = lax.optimization_barrier((away, early_total))
        arrived, vector_total = with_rider(away, rider, lambda values: cube_permute(values, 0))
        late = staying(late, 0) + [cube_permute(feed_away, 0, LATE_ORDERS)]
        attend_parts = staying(attend_parts, 0) + [arrived]
        late_total, attend_total = summed(late), summed(attend_parts)
        feed_totals = (early_total, late_total)
    else:
        packed_grad = attend_backward(where, lengths, qkv, mixture_grad, log_totals, ())
        sums = (middle_sums, bias_grad)
        keep_attend, send_attend, vector_total = input_grad(
            where, spots, normed_t, packed_grad, output_grad, sums, 16, depth // 8, ()
        )
        token_grad, token_sums = token_back(packed_grad, wide, tokens, middle_grad, layer_vectors, ())
        vector_total = lax.psum(vector_total, ("dp", "mp"))

    if not cube:

        def own_block(keep, send):
            full = jnp.stack([keep, send]).reshape(2, 2, 8, keep.shape[1], keep.shape[2])
            full = full.transpose(1, 0, 2, 3, 4).reshape(4, 8 * keep.shape[1], keep.shape[2])
            full = lax.psum_scatter(full, "mp", scatter_dimension=0, tiled=False)
            return lax.psum(full, "dp")

        def own_rows(*blocks):
            full = jnp.concatenate([block.reshape(8, -1, block.shape[1]) for block in blocks], axis=1)
            full = full.reshape(depth, full.shape[2]).astype(f32)
            return lax.dynamic_slice_in_dim(full, lax.axis_index("dp") * rows, rows, 0)

        attend_total = own_rows(own_block(keep_attend, send_attend))
        feed_total = own_rows(own_block(keep_early, send_early), own_block(keep_late, send_late))
        feed_totals = feed_total[: rows * 2 // 3], feed_total[rows * 2 // 3 :]
    owned = sum(jnp.sum(total * total) for total in (attend_total, *feed_totals))
    row = lax.broadcasted_iota(jnp.int32, (3, depth), 0)
    owned = jnp.where(row == 2, owned, jnp.pad(token_sums, ((0, 1), (0, 0))))
    owned = cube_sum(owned) if cube else lax.psum(owned, ("dp", "mp"))
    def turned(array):
        return array.transpose(1, 0, 2)

    state = (
        (turned(input_weight), turned(first_input), turned(second_input)),
        (output_weight, first_output, second_output),
        (expand_weight, first_expand, second_expand),
        (shrink_weight.T, first_shrink.T, second_shrink.T),
        (layer_vectors, first_vectors, second_vectors),
        (head_bias, first_head, second_head),
        tuple(array.reshape(hidden // 128, 128) for array in (expand_bias, first_bias, second_bias)),
    )
    grad_norm, *updates = optimize(where, owned, vector_total, attend_total, feed_totals, state)
    grad_norm = grad_norm[0, 0]
    moment_input, square_input, updated_input = (turned(array) for array in updates[:3])
    moment_output, square_output, updated_output = updates[3:6]
    moment_expand, square_expand, updated_expand = updates[6:9]
    moment_shrink, square_shrink, updated_shrink = (array.T for array in updates[9:12])
    moment_vectors, square_vectors, updated_vectors = updates[12:15]
    moment_head, square_head, updated_head = updates[15:18]
    moment_bias, square_bias, updated_bias = (array.reshape(hidden) for array in updates[18:])
    return (
        block_out,
        token_grad,
        grad_norm,
        moment_input,
        square_input,
        updated_input,
        moment_output,
        square_output,
        updated_output,
        moment_expand,
        square_expand,
        updated_expand,
        moment_shrink,
        square_shrink,
        updated_shrink,
        moment_vectors,
        square_vectors,
        updated_vectors,
        moment_head,
        square_head,
        updated_head,
        moment_bias,
        square_bias,
        updated_bias,
    )


def solution(mesh):
    in_specs = (
        P(("dp", "mp"), None),
        P(("dp", "mp"), None),
        P("dp"),
        P("dp", None, "mp"),
        P("mp", "dp"),
        P("dp", "mp"),
        P("mp", "dp"),
        P(),
        P(None, "mp"),
        P("mp"),
        P("dp", None, "mp"),
        P("mp", "dp"),
        P("dp", "mp"),
        P("mp", "dp"),
        P(),
        P(None, "mp"),
        P("mp"),
        P("dp", None, "mp"),
        P("mp", "dp"),
        P("dp", "mp"),
        P("mp", "dp"),
        P(),
        P(None, "mp"),
        P("mp"),
    )
    out_specs = (
        P(("dp", "mp"), None),
        P(("dp", "mp"), None),
        P(),
        P("dp", None, "mp"),
        P("dp", None, "mp"),
        P("dp", None, "mp"),
        P("mp", "dp"),
        P("mp", "dp"),
        P("mp", "dp"),
        P("dp", "mp"),
        P("dp", "mp"),
        P("dp", "mp"),
        P("mp", "dp"),
        P("mp", "dp"),
        P("mp", "dp"),
        P(),
        P(),
        P(),
        P(None, "mp"),
        P(None, "mp"),
        P(None, "mp"),
        P("mp"),
        P("mp"),
        P("mp"),
    )
    return jax.shard_map(shards, mesh=mesh, in_specs=in_specs, out_specs=out_specs, check_vma=False)
```

```python
import functools
import jax
import jax.numpy as jnp
from jax import lax
from jax.experimental import pallas as pl
from jax.experimental.pallas import tpu as pltpu
from jax.sharding import PartitionSpec as P

HEAD_DIM = 64
TILE = 256
STEP = 10

eps_norm = 1e-05
clip_norm = 1.0
beta_one = 0.9
beta_two = 0.999
adam_eps = 1e-08
rate = 0.05
vector_rate = 0.5
decay = 0.01
excluded = -1e30
low = jnp.bfloat16
f32 = jnp.float32
GELU_A = 0.7978845608028654
GELU_B = GELU_A * 0.044715


def params(limit_mib, **kw):
    return pltpu.CompilerParams(vmem_limit_bytes=limit_mib * 1024 * 1024, **kw)


def cost(flops, moved, special=0):
    return pl.CostEstimate(flops=int(flops), bytes_accessed=int(moved), transcendentals=int(special))


def mm(a, b):
    return jnp.dot(a, b, preferred_element_type=f32)


def mm_nt(a, b):
    return lax.dot_general(a, b, (((1,), (1,)), ((), ())), preferred_element_type=f32)


def whole(shape):
    zeros = (0,) * len(shape)
    return pl.BlockSpec(shape, lambda *_: zeros)


def once(shape):
    zeros = (0,) * len(shape)
    return pl.BlockSpec(shape, lambda *_: zeros, pipeline_mode=pl.Buffered(1))


def held_back(body, first, count):
    def run(*refs):
        return body(*refs[:first], *refs[first + count :])

    return run


LATER = pl.BlockSpec(memory_space=pl.ANY)


def far_away(shape, dtype):
    return pltpu.HBM(shape, dtype)


def from_far(*arrays):
    return [pltpu.with_memory_space_constraint(array, pltpu.HBM) for array in arrays]


def sds(shape, dtype):
    return jax.ShapeDtypeStruct(shape, dtype)


def live_blocks(length, count, body):
    for blocks in range(1, count + 1):
        low_end = (blocks - 1) * TILE
        high_end = blocks * TILE
        @pl.when((length > low_end) & (length <= high_end))
        def _(blocks=blocks):
            body(length, blocks)


PAIR = 2 * HEAD_DIM


def span(block):
    return slice(block * TILE, (block + 1) * TILE)


def both_heads(values):
    lane = lax.broadcasted_iota(jnp.int32, values.shape, 1)
    none = jnp.zeros_like(values)
    return jnp.concatenate(
        [jnp.where(lane < HEAD_DIM, values, none), jnp.where(lane >= HEAD_DIM, values, none)], axis=0
    )


def causal_mask():
    key_id = lax.broadcasted_iota(jnp.int32, (TILE, 2 * TILE), 0)
    query_id = lax.broadcasted_iota(jnp.int32, (TILE, 2 * TILE), 1) & (TILE - 1)
    return key_id <= query_id


def forward_body(where_ref, lengths_ref, q_ref, k_ref, v_ref, o_ref, lse_ref, vt_ref):
    seq = q_ref.shape[0]
    vt_ref[...] = v_ref[...].T
    causal = causal_mask()

    def run(length, blocks):
        def scores(b):
            q = q_ref[span(b), :] * jnp.asarray(HEAD_DIM**-0.5, low)
            return mm_nt(k_ref[: (b + 1) * TILE, :], both_heads(q))

        now = scores(0)
        for b in range(blocks):
            start, stop = b * TILE, (b + 1) * TILE
            later = scores(b + 1) if b + 1 < blocks else None
            last = jnp.where(causal, now[start:, :], excluded)
            top = jnp.max(last, axis=0, keepdims=True)
            if b:
                top = jnp.maximum(top, jnp.max(now[:start], axis=0, keepdims=True))
            p = jnp.exp(last - top)
            total = jnp.sum(p, axis=0, keepdims=True)
            pb = p.astype(low)
            if b:
                pf = jnp.exp(now[:start] - top)
                total = total + jnp.sum(pf, axis=0, keepdims=True)
                pb = jnp.concatenate([pf.astype(low), pb], axis=0)
            inverse = 1.0 / total
            lse = top + jnp.log(total)
            outs = []
            for h in range(2):
                at = slice(h * TILE, (h + 1) * TILE)
                out = mm(vt_ref[h * HEAD_DIM : (h + 1) * HEAD_DIM, :stop], pb[:, at])
                outs.append(out * inverse[:, at])
                lse_ref[0, h : h + 1, start:stop] = lse[:, at]
            both = jnp.concatenate(outs, axis=0).T
            row = start + lax.broadcasted_iota(jnp.int32, both.shape, 0)
            o_ref[start:stop, :] = jnp.where(row < length, both, 0.0).astype(low)
            now = later
        if blocks * TILE < seq:
            o_ref[blocks * TILE :, :] = jnp.zeros((seq - blocks * TILE, PAIR), low)
            lse_ref[0, :, blocks * TILE :] = jnp.zeros((2, seq - blocks * TILE), f32)

    live_blocks(lengths_ref[where_ref[2]], seq // TILE, run)


def attend_forward(where, lengths, qkv, after):
    seq, width = qkv.shape[0], qkv.shape[1] // 3
    pair = 2 * HEAD_DIM
    pairs = width // pair
    half = seq * seq * 5 // 8
    spec = lambda part: pl.BlockSpec((seq, pair), lambda i, *_: (0, part * pairs + i))
    return pl.pallas_call(
        held_back(forward_body, 5, len(after)),
        grid_spec=pltpu.PrefetchScalarGridSpec(
            num_scalar_prefetch=2,
            grid=(pairs,),
            in_specs=[spec(0), spec(1), spec(2)] + [LATER] * len(after),
            out_specs=[
                pl.BlockSpec((seq, pair), lambda i, *_: (0, i)),
                pl.BlockSpec((1, 2, seq), lambda i, *_: (i, 0, 0)),
            ],
            scratch_shapes=[pltpu.VMEM((pair, seq), low)],
        ),
        out_shape=[sds((seq, width), low), far_away((pairs, 2, seq), f32)],
        compiler_params=params(20),
        cost_estimate=cost(pairs * 2 * half * 2 * 2 * 256, seq * width * 8, pairs * 2 * half),
        name="attend_forward",
    )(where, lengths, *from_far(qkv, qkv, qkv), *after)


def backward_body(where_ref, lengths_ref, q_ref, k_ref, v_ref, do_ref, lse_ref, out_ref, kt_ref, ksum, vsum):
    seq = q_ref.shape[0]
    scale = HEAD_DIM**-0.5
    kt_ref[...] = k_ref[...].T
    causal = causal_mask()

    def run(length, blocks):
        def scores(b):
            qq = both_heads(q_ref[span(b), :] * jnp.asarray(scale, low))
            uu = both_heads(do_ref[span(b), :])
            stop = (b + 1) * TILE
            return qq, uu, mm_nt(k_ref[:stop, :], qq), mm_nt(v_ref[:stop, :], uu)

        now = scores(blocks - 1)
        for b in reversed(range(blocks)):
            start, stop = b * TILE, (b + 1) * TILE
            later = scores(b - 1) if b else None
            qq, uu, s, dp = now
            lse = jnp.concatenate([lse_ref[0, 0:1, start:stop], lse_ref[0, 1:2, start:stop]], axis=1)
            p = jnp.exp(jnp.where(causal, s[start:], excluded) - lse)
            inner = jnp.sum(p * dp[start:], axis=0, keepdims=True)
            if b:
                pf = jnp.exp(s[:start] - lse)
                inner = inner + jnp.sum(pf * dp[:start], axis=0, keepdims=True)
            ds = (p * (dp[start:] - inner)).astype(low)
            pb = p.astype(low)
            if b:
                ds = jnp.concatenate([(pf * (dp[:start] - inner)).astype(low), ds], axis=0)
                pb = jnp.concatenate([pf.astype(low), pb], axis=0)
            dk, dv = mm(ds, qq), mm(pb, uu)
            if b == blocks - 1:
                ksum[:stop, :] = dk
                vsum[:stop, :] = dv
            else:
                ksum[:stop, :] += dk
                vsum[:stop, :] += dv
            dq = jnp.concatenate(
                [
                    mm(
                        kt_ref[h * HEAD_DIM : (h + 1) * HEAD_DIM, :stop],
                        ds[:, h * TILE : (h + 1) * TILE],
                    )
                    for h in range(2)
                ],
                axis=0,
            )
            out_ref[1, start:stop, :] = ksum[start:stop, :].astype(low)
            out_ref[2, start:stop, :] = vsum[start:stop, :].astype(low)
            out_ref[0, start:stop, :] = (dq.T * scale).astype(low)
            now = later
        if blocks * TILE < seq:
            rest = jnp.zeros((seq - blocks * TILE, PAIR), low)
            for part in range(3):
                out_ref[part, blocks * TILE :, :] = rest

    live_blocks(lengths_ref[where_ref[2]], seq // TILE, run)


def attend_backward(where, lengths, qkv, upstream, lse, after):
    seq, width = upstream.shape
    pair = 2 * HEAD_DIM
    pairs = width // pair
    half = seq * seq * 5 // 8
    spec = lambda part: pl.BlockSpec((seq, pair), lambda i, *_: (0, part * pairs + i))
    own = pl.BlockSpec((seq, pair), lambda i, *_: (0, i))
    return pl.pallas_call(
        held_back(backward_body, 7, len(after)),
        grid_spec=pltpu.PrefetchScalarGridSpec(
            num_scalar_prefetch=2,
            grid=(pairs,),
            in_specs=[spec(0), spec(1), spec(2), own, pl.BlockSpec((1, 2, seq), lambda i, *_: (i, 0, 0))]
            + [LATER] * len(after),
            out_specs=pl.BlockSpec((3, seq, pair), lambda i, *_: (0, 0, i)),
            scratch_shapes=[
                pltpu.VMEM((pair, seq), low),
                pltpu.VMEM((seq, pair), f32),
                pltpu.VMEM((seq, pair), f32),
            ],
        ),
        out_shape=sds((3, seq, width), low),
        compiler_params=params(28),
        cost_estimate=cost(pairs * 2 * half * 5 * 2 * 256, seq * width * 14, pairs * 2 * half),
        name="attend_backward",
    )(where, lengths, *from_far(qkv, qkv, qkv), upstream, *from_far(lse), *after)


def normalize(values):
    average = jnp.mean(values, axis=-1, keepdims=True)
    centred = values - average
    inverse = lax.rsqrt(jnp.mean(centred * centred, axis=-1, keepdims=True) + eps_norm)
    return centred * inverse, inverse


def pull_norm(scaled, unit, inverse):
    first = jnp.mean(scaled, axis=-1, keepdims=True)
    second = jnp.mean(scaled * unit, axis=-1, keepdims=True)
    return inverse * (scaled - first - unit * second)


def columns_of(values):
    return jnp.sum(values, axis=0, keepdims=True)


def pack_body(
    input_ref, output_ref, expand_ref, shrink_ref, head_ref, hidden_ref, attend_ref, feed_ref, bias_ref
):
    width = input_ref.shape[2]
    part = expand_ref.shape[1] // 3
    for index in range(3):
        attend_ref[:, index * width : (index + 1) * width] = input_ref[index].astype(low)
        at = slice(index * part, (index + 1) * part)
        feed_ref[:, 2 * index * part : (2 * index + 1) * part] = expand_ref[:, at].astype(low)
        feed_ref[:, (2 * index + 1) * part : (2 * index + 2) * part] = shrink_ref[:, at].astype(low)
    attend_ref[:, 3 * width :] = output_ref[...].T.astype(low)
    pieces = [head_ref[0:1, :], head_ref[1:2, :]]
    pieces += [hidden_ref[row : row + 1, :] for row in range(hidden_ref.shape[0])]
    bias_ref[...] = jnp.zeros_like(bias_ref)
    bias_ref[pl.ds(lax.axis_index("mp"), 1), :] = jnp.concatenate(pieces, axis=1)


def pack(input_weight, output_weight, expand, shrink, head_bias, hidden_bias):
    rows, width = input_weight.shape[1:]
    hidden = expand.shape[1]
    return pl.pallas_call(
        pack_body,
        out_shape=[
            sds((rows, 4 * width), low),
            sds((rows, 2 * hidden), low),
            sds((4, 2 * width + hidden), f32),
        ],
        compiler_params=params(6),
        cost_estimate=cost(rows * hidden, rows * hidden * 18),
        name="pack",
    )(*from_far(input_weight, output_weight, expand, shrink, head_bias, hidden_bias))


def prepare_body(x_ref, up_ref, vec_ref, h_ref, ht_ref, upt_ref):
    unit, _ = normalize(x_ref[...].astype(f32))
    h = (unit * vec_ref[0:1, :] + vec_ref[1:2, :]).astype(low)
    h_ref[...] = h
    ht_ref[...] = h.T
    upt_ref[...] = up_ref[...].T


def prepare(x, up, vectors, after):
    seq, depth = x.shape
    rows = pl.BlockSpec((2 * TILE, depth), lambda i: (i, 0))
    turned = pl.BlockSpec((depth, 2 * TILE), lambda i: (0, i))
    return pl.pallas_call(
        held_back(prepare_body, 3, len(after)),
        grid=(seq // (2 * TILE),),
        in_specs=[rows, rows, once(vectors.shape)] + [LATER] * len(after),
        out_specs=[rows, turned, turned],
        out_shape=[sds((seq, depth), low), far_away((depth, seq), low), far_away((depth, seq), low)],
        compiler_params=params(16),
        cost_estimate=cost(seq * depth * 10, seq * depth * 10),
        name="prepare",
    )(*from_far(x, up), vectors, *after)


def slot(halves, spot, at):
    first, second = halves
    inner = spot & 7
    return jnp.where(spot < 8, first[inner, :, at], second[inner, :, at])


def project_body(
    where_ref, spots_ref, h_ref, mine_a, mine_b, twin_a, twin_b, bias_ref, qkv_ref, wide_ref
):
    part = pl.program_id(0)
    rows = mine_a.shape[1]
    width = mine_a.shape[2] // 4
    groups = wide_ref.shape[1] // rows

    def collect(sources, index):
        at = slice(index * width, (index + 1) * width)
        for group in range(groups):
            pieces = [slot(sources[model % 2], spots_ref[model, group], at) for model in range(4)]
            wide_ref[0, group * rows : (group + 1) * rows, :] = jnp.concatenate(pieces, axis=1)

    for index in range(4):
        for core in range(2):

            @pl.when((part == index) & (where_ref[0] == core))
            def _(index=index, core=core):
                mine, twin = (mine_a, mine_b), (twin_a, twin_b)
                collect((mine, twin) if core == 0 else (twin, mine), index)

    for index in range(3):

        @pl.when(part == index)
        def _(index=index):
            out = mm(h_ref[...], wide_ref[0])
            if index != 1:
                at = slice(index // 2 * width, (index // 2 + 1) * width)
                bias = jnp.concatenate([bias_ref[model : model + 1, at] for model in range(4)], axis=1)
                out = out + bias
            qkv_ref[...] = out.astype(low)


def project(where, spots, h, halves, bias, after):
    seq, depth = h.shape
    return pl.pallas_call(
        held_back(project_body, 8, len(after)),
        grid_spec=pltpu.PrefetchScalarGridSpec(
            num_scalar_prefetch=2,
            grid=(4,),
            in_specs=[
                once((seq, depth)),
                *[once(halves[0].shape)] * 4,
                once(bias.shape),
            ]
            + [LATER] * len(after),
            out_specs=[
                pl.BlockSpec((seq, depth), lambda i, *_: (0, jnp.minimum(i, 2))),
                pl.BlockSpec((1, depth, depth), lambda i, *_: (i, 0, 0)),
            ],
        ),
        out_shape=[far_away((seq, 3 * depth), low), far_away((4, depth, depth), low)],
        compiler_params=params(24),
        cost_estimate=cost(2 * seq * depth * depth * 3, seq * depth * 16),
        name="project",
    )(where, spots, h, *halves, bias, *after)


def attend_out_body(o_ref, w_ref, x_ref, vec_ref, middle_ref, h_ref, ht_ref, unit_ref, inverse_ref):
    middle = x_ref[...].astype(f32) + mm_nt(o_ref[...], w_ref[0]) + vec_ref[4:5, :]
    middle_ref[...] = middle.astype(low)
    unit, inverse = normalize(middle)
    unit_ref[...] = unit.astype(low)
    inverse_ref[...] = jnp.broadcast_to(inverse, inverse_ref.shape)
    h = (unit * vec_ref[2:3, :] + vec_ref[3:4, :]).astype(low)
    h_ref[...] = h
    ht_ref[...] = h.T


def attend_out(o, wide, x, vectors):
    seq, depth = x.shape
    rows = pl.BlockSpec((TILE, depth), lambda i: (i, 0))
    turned = pl.BlockSpec((depth, TILE), lambda i: (0, i))
    return pl.pallas_call(
        attend_out_body,
        grid=(seq // TILE,),
        in_specs=[
            rows,
            pl.BlockSpec((1, depth, depth), lambda i: (3, 0, 0)),
            rows,
            once(vectors.shape),
        ],
        out_specs=[rows, rows, turned, rows, pl.BlockSpec((TILE, 128), lambda i: (i, 0))],
        out_shape=[
            sds((seq, depth), low),
            sds((seq, depth), low),
            sds((depth, seq), low),
            sds((seq, depth), low),
            sds((seq, 128), f32),
        ],
        compiler_params=params(14),
        cost_estimate=cost(2 * seq * depth * depth, seq * depth * 14),
        name="attend_out",
    )(o, *from_far(wide, x), vectors)


def feed_body(
    where_ref,
    spots_ref,
    h2_ref,
    h2t_ref,
    up_ref,
    upt_ref,
    mine_a,
    mine_b,
    twin_a,
    twin_b,
    mine_c,
    mine_d,
    twin_c,
    twin_d,
    bias_ref,
    middle_ref,
    vec_ref,
    block_ref,
    back_ref,
    keep_a,
    send_a,
    keep_b,
    send_b,
    bias_grad_ref,
    out_ref,
    sum_ref,
    wide_ref,
    act_ref,
    pre_ref,
):
    step = pl.program_id(0)
    side = lax.rem(step, 2)
    models = [where_ref[1] ^ (2 * side + core) for core in range(2)]
    part = mine_a.shape[2] // 2
    groups = spots_ref.shape[1]
    rows = wide_ref.shape[0] // groups
    split = mine_a.shape[1]
    pieces = (
        ((mine_a, mine_b), (twin_a, twin_b), keep_a, send_a, 0, slice(0, split)),
        ((mine_c, mine_d), (twin_c, twin_d), keep_b, send_b, 4, slice(split, rows)),
    )

    @pl.when(step == 0)
    def _():
        out_ref[...] = middle_ref[...].astype(f32) + vec_ref[5:6, :]
        sum_ref[...] = jnp.zeros_like(sum_ref)

    for group in range(groups):
        for mine, twin, _, _, table, within in pieces:
            at = slice(group * rows + within.start, group * rows + within.stop)
            own = slot(mine, spots_ref[table + models[0], group], slice(None))
            other = slot(twin, spots_ref[table + models[1], group], slice(None))
            wide_ref[at, :part] = own[:, :part]
            wide_ref[at, part : 2 * part] = other[:, :part]
            wide_ref[at, 2 * part : 3 * part] = own[:, part:]
            wide_ref[at, 3 * part :] = other[:, part:]

    expand = wide_ref[:, : 2 * part]
    shrink = wide_ref[:, 2 * part :]
    first = step // 2 * part
    skip = bias_ref.shape[1] - bias_grad_ref.shape[1]
    bias = jnp.concatenate(
        [bias_ref[pl.ds(model, 1), pl.ds(pl.multiple_of(skip + first, 128), part)] for model in models],
        axis=1,
    )
    sums = jnp.zeros((1, 2 * part), f32)
    for tile in range(h2_ref.shape[0] // TILE):
        at = slice(tile * TILE, (tile + 1) * TILE)
        u = mm(h2_ref[at, :], expand) + bias
        square = u * u
        th = jnp.tanh(u * (GELU_A + GELU_B * square))
        gate = 0.5 * th + 0.5
        slope = gate + (gate * (1.0 - gate)) * (u * (2.0 * GELU_A + (6.0 * GELU_B) * square))
        pre = (mm(up_ref[at, :], shrink) * slope).astype(low)
        act_ref[at, :] = (u * gate).astype(low)
        pre_ref[at, :] = pre
        sums = sums + columns_of(pre.astype(f32))
    for core, model in enumerate(models):
        bias_grad_ref[pl.ds(model, 1), pl.ds(pl.multiple_of(first, 128), part)] = sums[
            :, core * part : (core + 1) * part
        ]
    out_ref[...] += mm_nt(act_ref[...], shrink)
    sum_ref[...] += mm_nt(pre_ref[...], expand)
    grad_expand = mm(h2t_ref[...], pre_ref[...]).astype(low)
    grad_shrink = mm(upt_ref[...], act_ref[...]).astype(low)
    for group in range(groups):
        for _, _, keep, send, table, within in pieces:
            at = slice(group * rows + within.start, group * rows + within.stop)
            own, other = spots_ref[table + models[0], group], spots_ref[table + models[1], group]
            keep[own, :, :part] = grad_expand[at, :part]
            keep[own, :, part:] = grad_shrink[at, :part]
            send[other, :, :part] = grad_expand[at, part:]
            send[other, :, part:] = grad_shrink[at, part:]

    @pl.when(step == pl.num_programs(0) - 1)
    def _():
        block_ref[...] = out_ref[...].astype(low)
        back_ref[...] = sum_ref[...].astype(low)


def feed(where, spots, h2, h2t, up, upt, halves, bias, middle, vectors):
    seq, depth = h2.shape
    half, _, columns = halves[0].shape
    steps, part = 6, columns // 6
    splits = [halves[0].shape[1], halves[4].shape[1]]

    def piece(count, rows):
        return pl.BlockSpec((count, rows, 2 * part), lambda i, *_: (0, 0, i // 2))

    return pl.pallas_call(
        feed_body,
        grid_spec=pltpu.PrefetchScalarGridSpec(
            num_scalar_prefetch=2,
            grid=(steps,),
            in_specs=[
                once((seq, depth)),
                once((depth, seq)),
                once((seq, depth)),
                once((depth, seq)),
                *[piece(half, rows) for rows in splits for _ in range(4)],
                once(bias.shape),
                once((seq, depth)),
                once(vectors.shape),
            ],
            out_specs=[whole((seq, depth)), whole((seq, depth))]
            + [piece(2 * half, rows) for rows in splits for _ in range(2)]
            + [whole((4, 3 * part))],
            scratch_shapes=[
                pltpu.VMEM((seq, depth), f32),
                pltpu.VMEM((seq, depth), f32),
                pltpu.VMEM((depth, 4 * part), low),
                pltpu.VMEM((seq, 2 * part), low),
                pltpu.VMEM((seq, 2 * part), low),
            ],
        ),
        out_shape=[sds((seq, depth), low)] * 2
        + [sds((2 * half, rows, columns), low) for rows in splits for _ in range(2)]
        + [sds((4, 3 * part), f32)],
        compiler_params=params(31),
        cost_estimate=cost(12 * seq * depth * steps * 2 * part, seq * depth * 40, seq * steps * part),
        name="feed",
    )(where, spots, h2, h2t, *from_far(up, upt), *halves, bias, middle, vectors)


def middle_back_body(
    where_ref,
    lengths_ref,
    back_ref,
    unit_ref,
    inverse_ref,
    up_ref,
    o_ref,
    w_ref,
    vec_ref,
    grad_ref,
    mixture_ref,
    weight_ref,
    sums_ref,
    total_ref,
):
    step = pl.program_id(0)
    unit, inverse = unit_ref[...].astype(f32), inverse_ref[:, 0:1]
    back = back_ref[...].astype(f32)
    up = up_ref[...].astype(f32)
    grad = up + pull_norm(back * vec_ref[2:3, :], unit, inverse)
    rounded = grad.astype(low)
    grad_ref[...] = rounded
    row = step * grad.shape[0] + lax.broadcasted_iota(jnp.int32, grad.shape, 0)
    length = lengths_ref[where_ref[2]]
    mixture_ref[...] = jnp.where(row < length, mm(rounded, w_ref[0]), 0.0).astype(low)
    share = mm(rounded.T, o_ref[...])
    sums = jnp.concatenate(
        [columns_of(back * unit), columns_of(back), columns_of(grad), columns_of(up)], axis=0
    )

    @pl.when(step == 0)
    def _():
        total_ref[...] = share
        sums_ref[...] = sums

    @pl.when(step > 0)
    def _():
        total_ref[...] += share
        sums_ref[...] += sums

    @pl.when(step == pl.num_programs(0) - 1)
    def _():
        weight_ref[...] = total_ref[...].astype(low)


def middle_back(where, lengths, back, unit, inverse, up, o, wide, vectors):
    seq, depth = unit.shape
    rows = pl.BlockSpec((2 * TILE, depth), lambda i, *_: (i, 0))
    return pl.pallas_call(
        middle_back_body,
        grid_spec=pltpu.PrefetchScalarGridSpec(
            num_scalar_prefetch=2,
            grid=(seq // (2 * TILE),),
            in_specs=[
                rows,
                rows,
                pl.BlockSpec((2 * TILE, 128), lambda i, *_: (i, 0)),
                rows,
                rows,
                pl.BlockSpec((1, depth, depth), lambda i, *_: (3, 0, 0)),
                once(vectors.shape),
            ],
            out_specs=[rows, rows, whole((depth, depth)), whole((4, depth))],
            scratch_shapes=[pltpu.VMEM((depth, depth), f32)],
        ),
        out_shape=[
            sds((seq, depth), low),
            sds((seq, depth), low),
            sds((depth, depth), low),
            sds((4, depth), f32),
        ],
        compiler_params=params(24),
        cost_estimate=cost(4 * seq * depth * depth, seq * depth * 28),
        name="middle_back",
    )(where, lengths, back, unit, inverse, *from_far(up), o, *from_far(wide), vectors)


def input_grad_body(
    where_ref,
    spots_ref,
    ht_ref,
    back_ref,
    out_grad_ref,
    middle_ref,
    bias_ref,
    keep_ref,
    send_ref,
    sums_ref,
):
    part = pl.program_id(0)
    rows = keep_ref.shape[1]
    width = keep_ref.shape[2] // 4
    groups = ht_ref.shape[0] // rows

    def spread(targets, index, grad):
        at = slice(index * width, (index + 1) * width)
        for group in range(groups):
            for model in range(4):
                targets[model % 2][spots_ref[model, group], :, at] = grad[
                    group * rows : (group + 1) * rows, model * width : (model + 1) * width
                ]

    for index in range(4):

        @pl.when(part == index)
        def _(index=index):
            if index < 3:
                if index == 0:
                    sums_ref[:2] = jnp.zeros((2, sums_ref.shape[1]), f32)
                    sums_ref[2:6] = middle_ref[...]
                    sums_ref[8:] = bias_ref[...]
                if index != 1:
                    row = 6 + index // 2
                    sums_ref[row : row + 1, :] = columns_of(back_ref[0].astype(f32))
                grad = mm(ht_ref[...], back_ref[0]).astype(low)
            else:
                grad = out_grad_ref[...]
            for core in range(2):

                @pl.when(where_ref[0] == core)
                def _(core=core):
                    spread((keep_ref, send_ref) if core == 0 else (send_ref, keep_ref), index, grad)


def input_grad(where, spots, ht, back, out_grad, sums, slots, rows, after):
    depth, seq = ht.shape
    shape = (slots, rows, 4 * (depth // 4))
    return pl.pallas_call(
        held_back(input_grad_body, 7, len(after)),
        grid_spec=pltpu.PrefetchScalarGridSpec(
            num_scalar_prefetch=2,
            grid=(4,),
            in_specs=[
                once((depth, seq)),
                pl.BlockSpec((1, seq, depth), lambda i, *_: (jnp.minimum(i, 2), 0, 0)),
                once((depth, depth)),
                *[once(array.shape) for array in sums],
            ]
            + [LATER] * len(after),
            out_specs=[
                whole(shape),
                whole(shape),
                whole((12, depth)),
            ],
        ),
        out_shape=[sds(shape, low), sds(shape, low), sds((12, depth), f32)],
        compiler_params=params(24),
        cost_estimate=cost(6 * seq * depth * depth, seq * depth * 14),
        name="input_grad",
    )(where, spots, *from_far(ht), back, out_grad, *sums, *after)


def token_back_body(
    back_ref, w_ref, x_ref, grad_ref, vec_ref, token_ref, sums_ref
):
    step = pl.program_id(0)
    back = mm_nt(back_ref[0], w_ref[0]) + mm_nt(back_ref[1], w_ref[1]) + mm_nt(back_ref[2], w_ref[2])
    unit, inverse = normalize(x_ref[...].astype(f32))
    grad = grad_ref[...].astype(f32)
    token_ref[...] = (grad + pull_norm(back * vec_ref[0:1, :], unit, inverse)).astype(low)
    sums = jnp.concatenate([columns_of(back * unit), columns_of(back)], axis=0)

    @pl.when(step == 0)
    def _():
        sums_ref[...] = sums

    @pl.when(step > 0)
    def _():
        sums_ref[...] += sums


def token_back(back, wide, x, grad, vectors, after):
    seq, depth = x.shape
    rows = pl.BlockSpec((TILE, depth), lambda i: (i, 0))
    return pl.pallas_call(
        held_back(token_back_body, 5, len(after)),
        grid=(seq // TILE,),
        in_specs=[
            pl.BlockSpec((3, TILE, depth), lambda i: (0, i, 0)),
            pl.BlockSpec((3, depth, depth), lambda i: (0, 0, 0)),
            rows,
            rows,
            once(vectors.shape),
        ]
        + [LATER] * len(after),
        out_specs=[rows, whole((2, depth))],
        out_shape=[sds((seq, depth), low), sds((2, depth), f32)],
        compiler_params=params(24),
        cost_estimate=cost(0, 0),
        name="token_back",
    )(back, *from_far(wide, x), grad, vectors, *after)


CORE_ORDERS = ((4, 3, 2, 1), (3, 4, 1, 2))
LATE_ORDERS = ((2, 1, 4, 3), (1, 2, 3, 4))
STAGES = 4


def cube_permute(values, stage, orders=CORE_ORDERS):
    pairs = [(device, device ^ (1 << orders[device & 1][stage])) for device in range(32)]
    return lax.ppermute(values, ("dp", "mp"), pairs)


def bit_permute(values, bit):
    return lax.ppermute(values, ("dp", "mp"), [(device, device ^ (1 << bit)) for device in range(32)])


def place(distance, core, orders):
    spots = [
        sum(((distance >> bit) & 1) << step for step, bit in enumerate(order)) for order in orders
    ]
    return jnp.where(core == 0, spots[0], spots[1])


def joined(held, arrived):
    return jnp.concatenate([held, arrived], axis=0)


def leaving(parts, stage):
    half = 1 << stage
    return sum(part[half:].astype(f32) for part in parts).astype(low)


def staying(parts, stage):
    return [part[: 1 << stage] for part in parts]


def summed(parts):
    return sum(part[0].astype(f32) for part in parts)


def two_parts(values):
    high = lax.reduce_precision(values, 8, 7)
    rest = lax.reduce_precision(values - high, 8, 7)
    return jnp.concatenate([high, rest], axis=0).astype(low)


def one_part(parts):
    half = parts.shape[0] // 2
    return parts[:half].astype(f32) + parts[half:].astype(f32)


def with_rider(blocks, rider, send):
    count, rows, columns = blocks.shape
    parts = two_parts(rider)
    arrived = send(jnp.concatenate([blocks.reshape(count * rows, columns), parts], axis=0))
    total = one_part(parts) + one_part(arrived[count * rows :])
    return arrived[: count * rows].reshape(count, rows, columns), total


def cube_sum(values, bits=range(5)):
    for bit in bits:
        values = values + bit_permute(values, bit)
    return values


def adam_parts(weight, gradient, first_old, second_old, factor, step_rate):
    scaled = gradient * factor
    moment = beta_one * first_old + (1.0 - beta_one) * scaled
    square = beta_two * second_old + (1.0 - beta_two) * scaled * scaled
    spread = jnp.sqrt(square * (1.0 / (1.0 - beta_two**STEP)))
    ratio = moment * (1.0 / (1.0 - beta_one**STEP)) / (spread + adam_eps)
    return moment, square, weight - step_rate * (ratio + decay * weight)


def optimize_body(where_ref, owned_ref, vector_ref, attend_ref, feed_a, feed_b, *refs):
    state, outs = refs[:21], refs[21:]
    vectors = jnp.concatenate([owned_ref[:2], vector_ref[2:]], axis=0)
    total = owned_ref[2:3, 0:1] + jnp.sum(vectors * vectors)
    norm = jnp.sqrt(total)
    factor = clip_norm / jnp.maximum(norm, clip_norm)
    outs[0][...] = norm
    width = state[0].shape[2]
    part = state[6].shape[1] // 3

    def update(param, at, gradient, step_rate):
        weight, first, second = (ref[at] for ref in state[3 * param : 3 * param + 3])
        results = adam_parts(weight, gradient, first, second, factor, step_rate)
        for ref, result in zip(outs[1 + 3 * param : 4 + 3 * param], results):
            ref[at] = result

    for index in range(3):
        update(0, (index,), attend_ref[:, index * width : (index + 1) * width], rate)
    update(1, (...,), attend_ref[:, 3 * width :].T, rate)
    split, rows = feed_a.shape[0], state[6].shape[0]
    for feed_ref, within in ((feed_a, slice(0, split)), (feed_b, slice(split, rows))):
        for index in range(3):
            at = (within, slice(index * part, (index + 1) * part))
            first = 2 * index * part
            update(2, at, feed_ref[:, first : first + part], rate)
            update(3, at, feed_ref[:, first + part : first + 2 * part], rate)
    update(4, (...,), vectors[:6], vector_rate)
    model = where_ref[2]
    head = jnp.zeros((2, width), f32)
    for index in range(4):
        head = head + jnp.where(model == index, vectors[6:8, index * width : (index + 1) * width], 0.0)
    update(5, (...,), head, vector_rate)
    bias = vector_ref[pl.ds(8 + model, 1), :]
    bias = jnp.concatenate([bias[:, at : at + 128] for at in range(0, bias.shape[1], 128)], axis=0)
    update(6, (...,), bias, vector_rate)


def optimize(where, owned, vector_total, attend_total, feed_totals, state):
    shapes = [sds(group[0].shape, f32) for group in state for _ in range(3)]
    arrays = [array for group in state for array in group]
    return pl.pallas_call(
        optimize_body,
        in_specs=[pl.BlockSpec(memory_space=pltpu.SMEM)]
        + [pl.BlockSpec(memory_space=pltpu.VMEM)] * (5 + len(arrays)),
        out_shape=[sds((1, 1), f32)] + shapes,
        compiler_params=params(20),
        cost_estimate=cost(4e6, 8e6),
        name="optimize",
    )(where, owned, vector_total, attend_total, *feed_totals, *from_far(*arrays))


def shards(
    tokens,
    cotangent,
    lengths,
    input_weight,
    output_weight,
    expand_weight,
    shrink_weight,
    layer_vectors,
    head_bias,
    expand_bias,
    first_input,
    first_output,
    first_expand,
    first_shrink,
    first_vectors,
    first_head,
    first_bias,
    second_input,
    second_output,
    second_expand,
    second_shrink,
    second_vectors,
    second_head,
    second_bias,
):
    dp_count = lax.axis_size("dp")
    mp_count = lax.axis_size("mp")
    cube = dp_count == 8 and mp_count == 4
    rows = input_weight.shape[0]
    width = input_weight.shape[2]
    hidden = expand_weight.shape[1]
    seq, depth = tokens.shape
    part = hidden // 3
    model_index = lax.axis_index("mp")
    me = lax.axis_index("dp") * mp_count + model_index

    attend_shard, feed_shard, bias_full = pack(
        input_weight.transpose(1, 0, 2),
        output_weight,
        expand_weight,
        shrink_weight.T,
        head_bias,
        expand_bias.reshape(hidden // 128, 128),
    )
    if cube:
        core, near = me & 1, model_index
        devices = jnp.arange(32).reshape(8, 4).T
        spots = jnp.concatenate(
            [place(devices ^ me, devices & 1, orders) for orders in (CORE_ORDERS, LATE_ORDERS)]
        ).astype(jnp.int32)
    else:
        core = near = jnp.zeros((), jnp.int32)
        spots = (jnp.arange(8)[:, None] % 4 // 2 * 8 + jnp.arange(8)[None]).astype(jnp.int32)
    where = jnp.stack([core, near, model_index]).astype(jnp.int32)

    if cube:
        split = rows * 2 // 3
        held, early, late = attend_shard[None], feed_shard[None, :split], feed_shard[None, split:]
        arrived, far_late = cube_permute(held, 0), cube_permute(late, 0, LATE_ORDERS)
        held, bias_full = lax.optimization_barrier((joined(held, arrived), bias_full))
        arrived = cube_permute(held, 1)
        bias_full = bias_full + bit_permute(bias_full, 0)
        normed, normed_t, upstream_t = prepare(tokens, cotangent, layer_vectors, (held,))
        late = joined(late, far_late)
        held, early, late, normed, bias_full, spots, where = lax.optimization_barrier(
            (held, early, late, normed, bias_full, spots, where)
        )
        held = joined(held, arrived)
        arrived, far_early = cube_permute(held, 2), cube_permute(early, 0)
        far_late = cube_permute(late, 1, LATE_ORDERS)
        bias_full = bias_full + bit_permute(bias_full, 1)
        held, early, late = joined(held, arrived), joined(early, far_early), joined(late, far_late)
        held, early, late, bias_full = lax.optimization_barrier((held, early, late, bias_full))
        far, far_early = cube_permute(held, 3), cube_permute(early, 1)
        twin = bit_permute(held, 0)
        early = joined(early, far_early)
        far, early, late = lax.optimization_barrier((far, early, late))
        attend_halves = (held, far, twin, bit_permute(far, 0))
        far_early, far_late = cube_permute(early, 2), cube_permute(late, 2, LATE_ORDERS)
        qkv, wide = project(where, spots, normed, attend_halves, bias_full, ())
        far_early, far_late, qkv = lax.optimization_barrier((far_early, far_late, qkv))
        early, late = joined(early, far_early), joined(late, far_late)
        far_early, far_late = cube_permute(early, 3), cube_permute(late, 3, LATE_ORDERS)
        twin_early, twin_late = bit_permute(early, 0), bit_permute(late, 0)
        mixture, log_totals = attend_forward(where, lengths, qkv, (early, late))
        far_early, far_late, twin_late, mixture = lax.optimization_barrier(
            (far_early, far_late, twin_late, mixture)
        )
        last_early, last_late = bit_permute(far_early, 0), bit_permute(far_late, 0)
        middle, hidden_in, hidden_t, unit, inverse = attend_out(mixture, wide, tokens, layer_vectors)
        feed_halves = (early, far_early, twin_early, last_early, late, far_late, twin_late, last_late)
    else:

        def planes(shard):
            full = lax.all_gather(lax.all_gather(shard, "dp", axis=0, tiled=True), "mp", axis=0)
            full = full.reshape(2, 2, 8, depth // 8, shard.shape[1]).transpose(1, 0, 2, 3, 4)
            return tuple(full.reshape(4, 8, depth // 8, shard.shape[1]))

        normed, normed_t, upstream_t = prepare(tokens, cotangent, layer_vectors, ())
        bias_full = lax.psum(bias_full, "mp")
        qkv, wide = project(where, spots, normed, planes(attend_shard), bias_full, ())
        mixture, log_totals = attend_forward(where, lengths, qkv, ())
        middle, hidden_in, hidden_t, unit, inverse = attend_out(mixture, wide, tokens, layer_vectors)
        split = depth // 8 * 2 // 3
        feed_planes = planes(feed_shard)
        feed_halves = tuple(array[:, :split] for array in feed_planes) + tuple(
            array[:, split:] for array in feed_planes
        )
    block_out, back, keep_early, send_early, keep_late, send_late, bias_grad = feed(
        where,
        spots,
        hidden_in,
        hidden_t,
        cotangent,
        upstream_t,
        feed_halves,
        bias_full,
        middle,
        layer_vectors,
    )
    middle_grad, mixture_grad, output_grad, middle_sums = middle_back(
        where, lengths, back, unit, inverse, cotangent, mixture, wide, layer_vectors
    )
    if cube:
        early = [keep_early, bit_permute(send_early, 0)]
        late = [keep_late, bit_permute(send_late, 0)]
        early[0], late[0], mixture_grad = lax.optimization_barrier((early[0], late[0], mixture_grad))
        away, far_away_late = leaving(early, 3), leaving(late, 3)
        packed_grad = attend_backward(
            where, lengths, qkv, mixture_grad, log_totals, (away, far_away_late)
        )
        early = staying(early, 3) + [cube_permute(away, 3)]
        late = staying(late, 3) + [cube_permute(far_away_late, 3, LATE_ORDERS)]
        early[0], late[0], packed_grad = lax.optimization_barrier((early[0], late[0], packed_grad))
        away, far_away_late = leaving(early, 2), leaving(late, 2)
        sums = (middle_sums, bias_grad)
        keep_attend, send_attend, rider = input_grad(
            where, spots, normed_t, packed_grad, output_grad, sums, 16, depth // 8, (away, far_away_late)
        )
        early = staying(early, 2) + [cube_permute(away, 2)]
        late = staying(late, 2) + [cube_permute(far_away_late, 2, LATE_ORDERS)]
        early[-1], late[-1], send_attend = lax.optimization_barrier((early[-1], late[-1], send_attend))
        twin_b, rider = with_rider(send_attend[8:], rider, lambda values: bit_permute(values, 0))
        twin_a = bit_permute(send_attend[:8], 0)
        away = (keep_attend[8:].astype(f32) + twin_b.astype(f32)).astype(low)
        arrived, rider = with_rider(away, rider, lambda values: cube_permute(values, 3))
        attend_parts = [keep_attend[:8], twin_a, arrived]
        feed_away = leaving(early, 1)
        token_grad, token_sums = token_back(
            packed_grad, wide, tokens, middle_grad, layer_vectors, (away, feed_away)
        )
        early = staying(early, 1) + [cube_permute(feed_away, 1)]
        attend_parts[0], late[0], token_sums = lax.optimization_barrier(
            (attend_parts[0], late[0], token_sums)
        )
        away = leaving(attend_parts, 2)
        arrived, rider = with_rider(away, rider, lambda values: cube_permute(values, 2))
        attend_parts = staying(attend_parts, 2) + [arrived]
        away, early[0] = lax.optimization_barrier((away, early[0]))
        feed_away = leaving(early, 0)
        early = staying(early, 0) + [cube_permute(feed_away, 0)]
        feed_away = leaving(late, 1)
        away = leaving(attend_parts, 1)
        arrived, rider = with_rider(away, rider, lambda values: cube_permute(values, 1))
        late = staying(late, 1) + [cube_permute(feed_away, 1, LATE_ORDERS)]
        attend_parts = staying(attend_parts, 1) + [arrived]
        away, early[0] = lax.optimization_barrier((away, early[0]))
        early_total = summed(early)
        feed_away = leaving(late, 0)
        away = leaving(attend_parts, 0)
        away, early_total = lax.optimization_barrier((away, early_total))
        arrived, vector_total = with_rider(away, rider, lambda values: cube_permute(values, 0))
        late = staying(late, 0) + [cube_permute(feed_away, 0, LATE_ORDERS)]
        attend_parts = staying(attend_parts, 0) + [arrived]
        late_total, attend_total = summed(late), summed(attend_parts)
        feed_totals = (early_total, late_total)
    else:
        packed_grad = attend_backward(where, lengths, qkv, mixture_grad, log_totals, ())
        sums = (middle_sums, bias_grad)
        keep_attend, send_attend, vector_total = input_grad(
            where, spots, normed_t, packed_grad, output_grad, sums, 16, depth // 8, ()
        )
        token_grad, token_sums = token_back(packed_grad, wide, tokens, middle_grad, layer_vectors, ())
        vector_total = lax.psum(vector_total, ("dp", "mp"))

    if not cube:

        def own_block(keep, send):
            full = jnp.stack([keep, send]).reshape(2, 2, 8, keep.shape[1], keep.shape[2])
            full = full.transpose(1, 0, 2, 3, 4).reshape(4, 8 * keep.shape[1], keep.shape[2])
            full = lax.psum_scatter(full, "mp", scatter_dimension=0, tiled=False)
            return lax.psum(full, "dp")

        def own_rows(*blocks):
            full = jnp.concatenate([block.reshape(8, -1, block.shape[1]) for block in blocks], axis=1)
            full = full.reshape(depth, full.shape[2]).astype(f32)
            return lax.dynamic_slice_in_dim(full, lax.axis_index("dp") * rows, rows, 0)

        attend_total = own_rows(own_block(keep_attend, send_attend))
        feed_total = own_rows(own_block(keep_early, send_early), own_block(keep_late, send_late))
        feed_totals = feed_total[: rows * 2 // 3], feed_total[rows * 2 // 3 :]
    owned = sum(jnp.sum(total * total) for total in (attend_total, *feed_totals))
    row = lax.broadcasted_iota(jnp.int32, (3, depth), 0)
    owned = jnp.where(row == 2, owned, jnp.pad(token_sums, ((0, 1), (0, 0))))
    owned = cube_sum(owned) if cube else lax.psum(owned, ("dp", "mp"))
    def turned(array):
        return array.transpose(1, 0, 2)

    state = (
        (turned(input_weight), turned(first_input), turned(second_input)),
        (output_weight, first_output, second_output),
        (expand_weight, first_expand, second_expand),
        (shrink_weight.T, first_shrink.T, second_shrink.T),
        (layer_vectors, first_vectors, second_vectors),
        (head_bias, first_head, second_head),
        tuple(array.reshape(hidden // 128, 128) for array in (expand_bias, first_bias, second_bias)),
    )
    grad_norm, *updates = optimize(where, owned, vector_total, attend_total, feed_totals, state)
    grad_norm = grad_norm[0, 0]
    moment_input, square_input, updated_input = (turned(array) for array in updates[:3])
    moment_output, square_output, updated_output = updates[3:6]
    moment_expand, square_expand, updated_expand = updates[6:9]
    moment_shrink, square_shrink, updated_shrink = (array.T for array in updates[9:12])
    moment_vectors, square_vectors, updated_vectors = updates[12:15]
    moment_head, square_head, updated_head = updates[15:18]
    moment_bias, square_bias, updated_bias = (array.reshape(hidden) for array in updates[18:])
    return (
        block_out,
        token_grad,
        grad_norm,
        moment_input,
        square_input,
        updated_input,
        moment_output,
        square_output,
        updated_output,
        moment_expand,
        square_expand,
        updated_expand,
        moment_shrink,
        square_shrink,
        updated_shrink,
        moment_vectors,
        square_vectors,
        updated_vectors,
        moment_head,
        square_head,
        updated_head,
        moment_bias,
        square_bias,
        updated_bias,
    )


def solution(mesh):
    in_specs = (
        P(("dp", "mp"), None),
        P(("dp", "mp"), None),
        P("dp"),
        P("dp", None, "mp"),
        P("mp", "dp"),
        P("dp", "mp"),
        P("mp", "dp"),
        P(),
        P(None, "mp"),
        P("mp"),
        P("dp", None, "mp"),
        P("mp", "dp"),
        P("dp", "mp"),
        P("mp", "dp"),
        P(),
        P(None, "mp"),
        P("mp"),
        P("dp", None, "mp"),
        P("mp", "dp"),
        P("dp", "mp"),
        P("mp", "dp"),
        P(),
        P(None, "mp"),
        P("mp"),
    )
    out_specs = (
        P(("dp", "mp"), None),
        P(("dp", "mp"), None),
        P(),
        P("dp", None, "mp"),
        P("dp", None, "mp"),
        P("dp", None, "mp"),
        P("mp", "dp"),
        P("mp", "dp"),
        P("mp", "dp"),
        P("dp", "mp"),
        P("dp", "mp"),
        P("dp", "mp"),
        P("mp", "dp"),
        P("mp", "dp"),
        P("mp", "dp"),
        P(),
        P(),
        P(),
        P(None, "mp"),
        P(None, "mp"),
        P(None, "mp"),
        P("mp"),
        P("mp"),
        P("mp"),
    )
    return jax.shard_map(shards, mesh=mesh, in_specs=in_specs, out_specs=out_specs, check_vma=False)
```

```python
import functools
import jax
import jax.numpy as jnp
from jax import lax
from jax.experimental import pallas as pl
from jax.experimental.pallas import tpu as pltpu
from jax.sharding import PartitionSpec as P

HEAD_DIM = 64
TILE = 256
STEP = 10

eps_norm = 1e-05
clip_norm = 1.0
beta_one = 0.9
beta_two = 0.999
adam_eps = 1e-08
rate = 0.05
vector_rate = 0.5
decay = 0.01
excluded = -1e30
low = jnp.bfloat16
f32 = jnp.float32
GELU_A = 0.7978845608028654
GELU_B = GELU_A * 0.044715


def params(limit_mib, **kw):
    return pltpu.CompilerParams(vmem_limit_bytes=limit_mib * 1024 * 1024, **kw)


def cost(flops, moved, special=0):
    return pl.CostEstimate(flops=int(flops), bytes_accessed=int(moved), transcendentals=int(special))


def mm(a, b):
    return jnp.dot(a, b, preferred_element_type=f32)


def mm_nt(a, b):
    return lax.dot_general(a, b, (((1,), (1,)), ((), ())), preferred_element_type=f32)


def whole(shape):
    zeros = (0,) * len(shape)
    return pl.BlockSpec(shape, lambda *_: zeros)


def once(shape):
    zeros = (0,) * len(shape)
    return pl.BlockSpec(shape, lambda *_: zeros, pipeline_mode=pl.Buffered(1))


def held_back(body, first, count):
    def run(*refs):
        return body(*refs[:first], *refs[first + count :])

    return run


LATER = pl.BlockSpec(memory_space=pl.ANY)


def far_away(shape, dtype):
    return pltpu.HBM(shape, dtype)


def from_far(*arrays):
    return [pltpu.with_memory_space_constraint(array, pltpu.HBM) for array in arrays]


def sds(shape, dtype):
    return jax.ShapeDtypeStruct(shape, dtype)


def live_blocks(length, count, body):
    for blocks in range(1, count + 1):
        low_end = (blocks - 1) * TILE
        high_end = blocks * TILE
        @pl.when((length > low_end) & (length <= high_end))
        def _(blocks=blocks):
            body(length, blocks)


PAIR = 2 * HEAD_DIM


def span(block):
    return slice(block * TILE, (block + 1) * TILE)


def both_heads(values):
    lane = lax.broadcasted_iota(jnp.int32, values.shape, 1)
    none = jnp.zeros_like(values)
    return jnp.concatenate(
        [jnp.where(lane < HEAD_DIM, values, none), jnp.where(lane >= HEAD_DIM, values, none)], axis=0
    )


def causal_mask():
    key_id = lax.broadcasted_iota(jnp.int32, (TILE, 2 * TILE), 0)
    query_id = lax.broadcasted_iota(jnp.int32, (TILE, 2 * TILE), 1) & (TILE - 1)
    return key_id <= query_id


def forward_body(where_ref, lengths_ref, q_ref, k_ref, v_ref, o_ref, lse_ref, vt_ref):
    seq = q_ref.shape[0]
    vt_ref[...] = v_ref[...].T
    causal = causal_mask()

    def run(length, blocks):
        def scores(b):
            q = q_ref[span(b), :] * jnp.asarray(HEAD_DIM**-0.5, low)
            return mm_nt(k_ref[: (b + 1) * TILE, :], both_heads(q))

        now = scores(0)
        for b in range(blocks):
            start, stop = b * TILE, (b + 1) * TILE
            later = scores(b + 1) if b + 1 < blocks else None
            last = jnp.where(causal, now[start:, :], excluded)
            top = jnp.max(last, axis=0, keepdims=True)
            if b:
                top = jnp.maximum(top, jnp.max(now[:start], axis=0, keepdims=True))
            p = jnp.exp(last - top)
            total = jnp.sum(p, axis=0, keepdims=True)
            pb = p.astype(low)
            if b:
                pf = jnp.exp(now[:start] - top)
                total = total + jnp.sum(pf, axis=0, keepdims=True)
                pb = jnp.concatenate([pf.astype(low), pb], axis=0)
            inverse = 1.0 / total
            lse = top + jnp.log(total)
            outs = []
            for h in range(2):
                at = slice(h * TILE, (h + 1) * TILE)
                out = mm(vt_ref[h * HEAD_DIM : (h + 1) * HEAD_DIM, :stop], pb[:, at])
                outs.append(out * inverse[:, at])
                lse_ref[0, h : h + 1, start:stop] = lse[:, at]
            both = jnp.concatenate(outs, axis=0).T
            row = start + lax.broadcasted_iota(jnp.int32, both.shape, 0)
            o_ref[start:stop, :] = jnp.where(row < length, both, 0.0).astype(low)
            now = later
        if blocks * TILE < seq:
            o_ref[blocks * TILE :, :] = jnp.zeros((seq - blocks * TILE, PAIR), low)
            lse_ref[0, :, blocks * TILE :] = jnp.zeros((2, seq - blocks * TILE), f32)

    live_blocks(lengths_ref[where_ref[2]], seq // TILE, run)


def attend_forward(where, lengths, qkv, after):
    seq, width = qkv.shape[0], qkv.shape[1] // 3
    pair = 2 * HEAD_DIM
    pairs = width // pair
    half = seq * seq * 5 // 8
    spec = lambda part: pl.BlockSpec((seq, pair), lambda i, *_: (0, part * pairs + i))
    return pl.pallas_call(
        held_back(forward_body, 5, len(after)),
        grid_spec=pltpu.PrefetchScalarGridSpec(
            num_scalar_prefetch=2,
            grid=(pairs,),
            in_specs=[spec(0), spec(1), spec(2)] + [LATER] * len(after),
            out_specs=[
                pl.BlockSpec((seq, pair), lambda i, *_: (0, i)),
                pl.BlockSpec((1, 2, seq), lambda i, *_: (i, 0, 0)),
            ],
            scratch_shapes=[pltpu.VMEM((pair, seq), low)],
        ),
        out_shape=[sds((seq, width), low), far_away((pairs, 2, seq), f32)],
        compiler_params=params(20),
        cost_estimate=cost(pairs * 2 * half * 2 * 2 * 256, seq * width * 8, pairs * 2 * half),
        name="attend_forward",
    )(where, lengths, *from_far(qkv, qkv, qkv), *after)


def backward_body(where_ref, lengths_ref, q_ref, k_ref, v_ref, do_ref, lse_ref, out_ref, kt_ref, ksum, vsum):
    seq = q_ref.shape[0]
    scale = HEAD_DIM**-0.5
    kt_ref[...] = k_ref[...].T
    causal = causal_mask()

    def run(length, blocks):
        def scores(b):
            qq = both_heads(q_ref[span(b), :] * jnp.asarray(scale, low))
            uu = both_heads(do_ref[span(b), :])
            stop = (b + 1) * TILE
            return qq, uu, mm_nt(k_ref[:stop, :], qq), mm_nt(v_ref[:stop, :], uu)

        now = scores(blocks - 1)
        for b in reversed(range(blocks)):
            start, stop = b * TILE, (b + 1) * TILE
            later = scores(b - 1) if b else None
            qq, uu, s, dp = now
            lse = jnp.concatenate([lse_ref[0, 0:1, start:stop], lse_ref[0, 1:2, start:stop]], axis=1)
            p = jnp.exp(jnp.where(causal, s[start:], excluded) - lse)
            inner = jnp.sum(p * dp[start:], axis=0, keepdims=True)
            if b:
                pf = jnp.exp(s[:start] - lse)
                inner = inner + jnp.sum(pf * dp[:start], axis=0, keepdims=True)
            ds = (p * (dp[start:] - inner)).astype(low)
            pb = p.astype(low)
            if b:
                ds = jnp.concatenate([(pf * (dp[:start] - inner)).astype(low), ds], axis=0)
                pb = jnp.concatenate([pf.astype(low), pb], axis=0)
            dk, dv = mm(ds, qq), mm(pb, uu)
            if b == blocks - 1:
                ksum[:stop, :] = dk
                vsum[:stop, :] = dv
            else:
                ksum[:stop, :] += dk
                vsum[:stop, :] += dv
            dq = jnp.concatenate(
                [
                    mm(
                        kt_ref[h * HEAD_DIM : (h + 1) * HEAD_DIM, :stop],
                        ds[:, h * TILE : (h + 1) * TILE],
                    )
                    for h in range(2)
                ],
                axis=0,
            )
            out_ref[1, start:stop, :] = ksum[start:stop, :].astype(low)
            out_ref[2, start:stop, :] = vsum[start:stop, :].astype(low)
            out_ref[0, start:stop, :] = (dq.T * scale).astype(low)
            now = later
        if blocks * TILE < seq:
            rest = jnp.zeros((seq - blocks * TILE, PAIR), low)
            for part in range(3):
                out_ref[part, blocks * TILE :, :] = rest

    live_blocks(lengths_ref[where_ref[2]], seq // TILE, run)


def attend_backward(where, lengths, qkv, upstream, lse, after):
    seq, width = upstream.shape
    pair = 2 * HEAD_DIM
    pairs = width // pair
    half = seq * seq * 5 // 8
    spec = lambda part: pl.BlockSpec((seq, pair), lambda i, *_: (0, part * pairs + i))
    own = pl.BlockSpec((seq, pair), lambda i, *_: (0, i))
    return pl.pallas_call(
        held_back(backward_body, 7, len(after)),
        grid_spec=pltpu.PrefetchScalarGridSpec(
            num_scalar_prefetch=2,
            grid=(pairs,),
            in_specs=[spec(0), spec(1), spec(2), own, pl.BlockSpec((1, 2, seq), lambda i, *_: (i, 0, 0))]
            + [LATER] * len(after),
            out_specs=pl.BlockSpec((3, seq, pair), lambda i, *_: (0, 0, i)),
            scratch_shapes=[
                pltpu.VMEM((pair, seq), low),
                pltpu.VMEM((seq, pair), f32),
                pltpu.VMEM((seq, pair), f32),
            ],
        ),
        out_shape=sds((3, seq, width), low),
        compiler_params=params(28),
        cost_estimate=cost(pairs * 2 * half * 5 * 2 * 256, seq * width * 14, pairs * 2 * half),
        name="attend_backward",
    )(where, lengths, *from_far(qkv, qkv, qkv), upstream, *from_far(lse), *after)


def normalize(values):
    average = jnp.mean(values, axis=-1, keepdims=True)
    centred = values - average
    inverse = lax.rsqrt(jnp.mean(centred * centred, axis=-1, keepdims=True) + eps_norm)
    return centred * inverse, inverse


def pull_norm(scaled, unit, inverse):
    first = jnp.mean(scaled, axis=-1, keepdims=True)
    second = jnp.mean(scaled * unit, axis=-1, keepdims=True)
    return inverse * (scaled - first - unit * second)


def columns_of(values):
    return jnp.sum(values, axis=0, keepdims=True)


def pack_body(
    input_ref, output_ref, expand_ref, shrink_ref, head_ref, hidden_ref, attend_ref, feed_ref, bias_ref
):
    width = input_ref.shape[2]
    part = expand_ref.shape[1] // 3
    for index in range(3):
        attend_ref[:, index * width : (index + 1) * width] = input_ref[index].astype(low)
        at = slice(index * part, (index + 1) * part)
        feed_ref[:, 2 * index * part : (2 * index + 1) * part] = expand_ref[:, at].astype(low)
        feed_ref[:, (2 * index + 1) * part : (2 * index + 2) * part] = shrink_ref[:, at].astype(low)
    attend_ref[:, 3 * width :] = output_ref[...].T.astype(low)
    pieces = [head_ref[0:1, :], head_ref[1:2, :]]
    pieces += [hidden_ref[row : row + 1, :] for row in range(hidden_ref.shape[0])]
    bias_ref[...] = jnp.zeros_like(bias_ref)
    bias_ref[pl.ds(lax.axis_index("mp"), 1), :] = jnp.concatenate(pieces, axis=1)


def pack(input_weight, output_weight, expand, shrink, head_bias, hidden_bias):
    rows, width = input_weight.shape[1:]
    hidden = expand.shape[1]
    return pl.pallas_call(
        pack_body,
        out_shape=[
            sds((rows, 4 * width), low),
            sds((rows, 2 * hidden), low),
            sds((4, 2 * width + hidden), f32),
        ],
        compiler_params=params(6),
        cost_estimate=cost(rows * hidden, rows * hidden * 18),
        name="pack",
    )(*from_far(input_weight, output_weight, expand, shrink, head_bias, hidden_bias))


def prepare_body(x_ref, up_ref, vec_ref, h_ref, ht_ref, upt_ref):
    unit, _ = normalize(x_ref[...].astype(f32))
    h = (unit * vec_ref[0:1, :] + vec_ref[1:2, :]).astype(low)
    h_ref[...] = h
    ht_ref[...] = h.T
    upt_ref[...] = up_ref[...].T


def prepare(x, up, vectors, after):
    seq, depth = x.shape
    rows = pl.BlockSpec((2 * TILE, depth), lambda i: (i, 0))
    turned = pl.BlockSpec((depth, 2 * TILE), lambda i: (0, i))
    return pl.pallas_call(
        held_back(prepare_body, 3, len(after)),
        grid=(seq // (2 * TILE),),
        in_specs=[rows, rows, once(vectors.shape)] + [LATER] * len(after),
        out_specs=[rows, turned, turned],
        out_shape=[sds((seq, depth), low), far_away((depth, seq), low), far_away((depth, seq), low)],
        compiler_params=params(16),
        cost_estimate=cost(seq * depth * 10, seq * depth * 10),
        name="prepare",
    )(*from_far(x, up), vectors, *after)


def slot(halves, spot, at):
    first, second = halves
    inner = spot & 7
    return jnp.where(spot < 8, first[inner, :, at], second[inner, :, at])


def project_body(
    where_ref, spots_ref, h_ref, mine_a, mine_b, twin_a, twin_b, bias_ref, qkv_ref, wide_ref, last_ref
):
    part = pl.program_id(0)
    rows = mine_a.shape[1]
    width = mine_a.shape[2] // 4
    groups = wide_ref.shape[1] // rows

    def collect(sources, index):
        columns = slice(index * width, (index + 1) * width)
        for group in range(groups):
            pieces = [slot(sources[model % 2], spots_ref[model, group], columns) for model in range(4)]
            at = slice(group * rows, (group + 1) * rows)
            if index < 3:
                wide_ref[0, at, :] = jnp.concatenate(pieces, axis=1)
            else:
                last_ref[at, :] = jnp.concatenate(pieces, axis=1)

    for index in range(4):
        for core in range(2):

            @pl.when((part == index) & (where_ref[0] == core))
            def _(index=index, core=core):
                mine, twin = (mine_a, mine_b), (twin_a, twin_b)
                collect((mine, twin) if core == 0 else (twin, mine), index)

    for index in range(3):

        @pl.when(part == index)
        def _(index=index):
            out = mm(h_ref[...], wide_ref[0])
            if index != 1:
                at = slice(index // 2 * width, (index // 2 + 1) * width)
                bias = jnp.concatenate([bias_ref[model : model + 1, at] for model in range(4)], axis=1)
                out = out + bias
            qkv_ref[...] = out.astype(low)


def project(where, spots, h, halves, bias, after):
    seq, depth = h.shape
    return pl.pallas_call(
        held_back(project_body, 8, len(after)),
        grid_spec=pltpu.PrefetchScalarGridSpec(
            num_scalar_prefetch=2,
            grid=(4,),
            in_specs=[
                once((seq, depth)),
                *[once(halves[0].shape)] * 4,
                once(bias.shape),
            ]
            + [LATER] * len(after),
            out_specs=[
                pl.BlockSpec((seq, depth), lambda i, *_: (0, jnp.minimum(i, 2))),
                pl.BlockSpec((1, depth, depth), lambda i, *_: (jnp.minimum(i, 2), 0, 0)),
                whole((depth, depth)),
            ],
        ),
        out_shape=[
            far_away((seq, 3 * depth), low),
            far_away((3, depth, depth), low),
            sds((depth, depth), low),
        ],
        compiler_params=params(24),
        cost_estimate=cost(2 * seq * depth * depth * 3, seq * depth * 16),
        name="project",
    )(where, spots, h, *halves, bias, *after)


NEAR = pl.BlockSpec(memory_space=pltpu.VMEM)
SCALARS = pl.BlockSpec(memory_space=pltpu.SMEM)


def attend_out_body(o_ref, w_ref, x_ref, vec_ref, middle_ref, h_ref, ht_ref, unit_ref, inverse_ref):
    for tile in range(o_ref.shape[0] // TILE):
        at = slice(tile * TILE, (tile + 1) * TILE)
        middle = x_ref[at, :].astype(f32) + mm_nt(o_ref[at, :], w_ref[...]) + vec_ref[4:5, :]
        middle_ref[at, :] = middle.astype(low)
        unit, inverse = normalize(middle)
        unit_ref[at, :] = unit.astype(low)
        inverse_ref[at, :] = jnp.broadcast_to(inverse, (TILE, inverse_ref.shape[1]))
        h = (unit * vec_ref[2:3, :] + vec_ref[3:4, :]).astype(low)
        h_ref[at, :] = h
        ht_ref[:, at] = h.T


def attend_out(o, wide_out, x, vectors):
    seq, depth = x.shape
    return pl.pallas_call(
        attend_out_body,
        in_specs=[NEAR] * 4,
        out_specs=[NEAR] * 5,
        out_shape=[
            sds((seq, depth), low),
            sds((seq, depth), low),
            sds((depth, seq), low),
            sds((seq, depth), low),
            sds((seq, 128), f32),
        ],
        compiler_params=params(10),
        cost_estimate=cost(2 * seq * depth * depth, seq * depth * 14),
        name="attend_out",
    )(o, wide_out, x, vectors)


def feed_body(
    where_ref,
    spots_ref,
    h2_ref,
    h2t_ref,
    up_ref,
    upt_ref,
    mine_a,
    mine_b,
    twin_a,
    twin_b,
    mine_c,
    mine_d,
    twin_c,
    twin_d,
    bias_ref,
    middle_ref,
    vec_ref,
    block_ref,
    back_ref,
    keep_a,
    send_a,
    keep_b,
    send_b,
    bias_grad_ref,
    out_ref,
    sum_ref,
    wide_ref,
    act_ref,
    pre_ref,
):
    part = mine_a.shape[2] // 6
    groups = spots_ref.shape[1]
    rows = wide_ref.shape[0] // groups
    split = mine_a.shape[1]
    skip = bias_ref.shape[1] - bias_grad_ref.shape[1]
    pieces = (
        ((mine_a, mine_b), (twin_a, twin_b), keep_a, send_a, 0, slice(0, split)),
        ((mine_c, mine_d), (twin_c, twin_d), keep_b, send_b, 4, slice(split, rows)),
    )
    out_ref[...] = middle_ref[...].astype(f32) + vec_ref[5:6, :]
    sum_ref[...] = jnp.zeros_like(sum_ref)

    def step(index, carry):
        side = lax.rem(index, 2)
        first = pl.multiple_of(index // 2 * part, 128)
        lanes = pl.ds(pl.multiple_of(2 * first, 128), part)
        next_lanes = pl.ds(pl.multiple_of(2 * first + part, 128), part)
        models = [where_ref[1] ^ (2 * side + core) for core in range(2)]
        for group in range(groups):
            for mine, twin, _, _, table, within in pieces:
                at = slice(group * rows + within.start, group * rows + within.stop)
                for core, halves in enumerate((mine, twin)):
                    spot = spots_ref[table + models[core], group]
                    wide_ref[at, core * part : (core + 1) * part] = slot(halves, spot, lanes)
                    wide_ref[at, (2 + core) * part : (3 + core) * part] = slot(halves, spot, next_lanes)

        expand = wide_ref[:, : 2 * part]
        shrink = wide_ref[:, 2 * part :]
        bias = jnp.concatenate(
            [bias_ref[pl.ds(model, 1), pl.ds(pl.multiple_of(skip + first, 128), part)] for model in models],
            axis=1,
        )
        sums = jnp.zeros((1, 2 * part), f32)
        for tile in range(h2_ref.shape[0] // TILE):
            at = slice(tile * TILE, (tile + 1) * TILE)
            u = mm(h2_ref[at, :], expand) + bias
            square = u * u
            th = jnp.tanh(u * (GELU_A + GELU_B * square))
            gate = 0.5 * th + 0.5
            slope = gate + (gate * (1.0 - gate)) * (u * (2.0 * GELU_A + (6.0 * GELU_B) * square))
            pre = (mm(up_ref[at, :], shrink) * slope).astype(low)
            act_ref[at, :] = (u * gate).astype(low)
            pre_ref[at, :] = pre
            sums = sums + columns_of(pre.astype(f32))
        for core, model in enumerate(models):
            bias_grad_ref[pl.ds(model, 1), pl.ds(first, part)] = sums[:, core * part : (core + 1) * part]
        out_ref[...] += mm_nt(act_ref[...], shrink)
        sum_ref[...] += mm_nt(pre_ref[...], expand)
        grad_expand = mm(h2t_ref[...], pre_ref[...]).astype(low)
        grad_shrink = mm(upt_ref[...], act_ref[...]).astype(low)
        for group in range(groups):
            for _, _, keep, send, table, within in pieces:
                at = slice(group * rows + within.start, group * rows + within.stop)
                for core, target in enumerate((keep, send)):
                    spot = spots_ref[table + models[core], group]
                    columns = slice(core * part, (core + 1) * part)
                    target[spot, :, lanes] = grad_expand[at, columns]
                    target[spot, :, next_lanes] = grad_shrink[at, columns]
        return carry

    lax.fori_loop(0, 6, step, 0)
    block_ref[...] = out_ref[...].astype(low)
    back_ref[...] = sum_ref[...].astype(low)


def feed(where, spots, h2, h2t, up, upt, halves, bias, middle, vectors):
    seq, depth = h2.shape
    half, _, columns = halves[0].shape
    part = columns // 6
    splits = [halves[0].shape[1], halves[4].shape[1]]
    return pl.pallas_call(
        feed_body,
        in_specs=[SCALARS] * 2 + [NEAR] * 15,
        out_specs=[NEAR] * 7,
        scratch_shapes=[
            pltpu.VMEM((seq, depth), f32),
            pltpu.VMEM((seq, depth), f32),
            pltpu.VMEM((depth, 4 * part), low),
            pltpu.VMEM((seq, 2 * part), low),
            pltpu.VMEM((seq, 2 * part), low),
        ],
        out_shape=[sds((seq, depth), low)] * 2
        + [sds((2 * half, rows, columns), low) for rows in splits for _ in range(2)]
        + [sds((4, 3 * part), f32)],
        compiler_params=params(22),
        cost_estimate=cost(12 * seq * depth * 12 * part, seq * depth * 40, seq * 6 * part),
        name="feed",
    )(where, spots, h2, h2t, up, upt, *halves, bias, middle, vectors)


def middle_back_body(
    where_ref,
    lengths_ref,
    back_ref,
    unit_ref,
    inverse_ref,
    up_ref,
    o_ref,
    w_ref,
    vec_ref,
    grad_ref,
    mixture_ref,
    weight_ref,
    sums_ref,
    turned_ref,
):
    length = lengths_ref[where_ref[2]]
    sums = jnp.zeros(sums_ref.shape, f32)
    for tile in range(back_ref.shape[0] // TILE):
        at = slice(tile * TILE, (tile + 1) * TILE)
        unit, inverse = unit_ref[at, :].astype(f32), inverse_ref[at, 0:1]
        back = back_ref[at, :].astype(f32)
        up = up_ref[at, :].astype(f32)
        grad = up + pull_norm(back * vec_ref[2:3, :], unit, inverse)
        rounded = grad.astype(low)
        grad_ref[at, :] = rounded
        turned_ref[:, at] = rounded.T
        row = tile * TILE + lax.broadcasted_iota(jnp.int32, grad.shape, 0)
        mixture_ref[at, :] = jnp.where(row < length, mm(rounded, w_ref[...]), 0.0).astype(low)
        sums = sums + jnp.concatenate(
            [columns_of(back * unit), columns_of(back), columns_of(grad), columns_of(up)], axis=0
        )
    sums_ref[...] = sums
    weight_ref[...] = mm(turned_ref[...], o_ref[...]).astype(low)


def middle_back(where, lengths, back, unit, inverse, up, o, wide_out, vectors):
    seq, depth = unit.shape
    return pl.pallas_call(
        middle_back_body,
        in_specs=[SCALARS] * 2 + [NEAR] * 7,
        out_specs=[NEAR] * 4,
        scratch_shapes=[pltpu.VMEM((depth, seq), low)],
        out_shape=[
            sds((seq, depth), low),
            sds((seq, depth), low),
            sds((depth, depth), low),
            sds((4, depth), f32),
        ],
        compiler_params=params(14),
        cost_estimate=cost(4 * seq * depth * depth, seq * depth * 28),
        name="middle_back",
    )(where, lengths, back, unit, inverse, up, o, wide_out, vectors)


def input_grad_body(
    where_ref,
    spots_ref,
    ht_ref,
    back_ref,
    out_grad_ref,
    middle_ref,
    bias_ref,
    keep_ref,
    send_ref,
    sums_ref,
):
    rows = keep_ref.shape[1]
    width = keep_ref.shape[2] // 4
    groups = ht_ref.shape[0] // rows

    def spread(targets, index, grad):
        at = slice(index * width, (index + 1) * width)
        for group in range(groups):
            for model in range(4):
                targets[model % 2][spots_ref[model, group], :, at] = grad[
                    group * rows : (group + 1) * rows, model * width : (model + 1) * width
                ]

    sums_ref[:2] = jnp.zeros((2, sums_ref.shape[1]), f32)
    sums_ref[2:6] = middle_ref[...]
    sums_ref[6:7] = columns_of(back_ref[0].astype(f32))
    sums_ref[7:8] = columns_of(back_ref[2].astype(f32))
    sums_ref[8:] = bias_ref[...]
    for index in range(4):
        grad = mm(ht_ref[...], back_ref[index]).astype(low) if index < 3 else out_grad_ref[...]
        for core in range(2):

            @pl.when(where_ref[0] == core)
            def _(core=core, index=index, grad=grad):
                spread((keep_ref, send_ref) if core == 0 else (send_ref, keep_ref), index, grad)


def input_grad(where, spots, ht, back, out_grad, sums, slots, rows, after):
    depth, seq = ht.shape
    shape = (slots, rows, depth)
    return pl.pallas_call(
        held_back(input_grad_body, 7, len(after)),
        in_specs=[SCALARS] * 2 + [NEAR] * 5 + [LATER] * len(after),
        out_specs=[NEAR] * 3,
        out_shape=[sds(shape, low), sds(shape, low), sds((12, depth), f32)],
        compiler_params=params(14),
        cost_estimate=cost(6 * seq * depth * depth, seq * depth * 14),
        name="input_grad",
    )(where, spots, ht, back, out_grad, *sums, *after)


def token_back_body(
    back_ref, w_ref, x_ref, grad_ref, vec_ref, token_ref, sums_ref
):
    step = pl.program_id(0)
    back = mm_nt(back_ref[0], w_ref[0]) + mm_nt(back_ref[1], w_ref[1]) + mm_nt(back_ref[2], w_ref[2])
    unit, inverse = normalize(x_ref[...].astype(f32))
    grad = grad_ref[...].astype(f32)
    token_ref[...] = (grad + pull_norm(back * vec_ref[0:1, :], unit, inverse)).astype(low)
    sums = jnp.concatenate([columns_of(back * unit), columns_of(back)], axis=0)

    @pl.when(step == 0)
    def _():
        sums_ref[...] = sums

    @pl.when(step > 0)
    def _():
        sums_ref[...] += sums


def token_back(back, wide, x, grad, vectors, after):
    seq, depth = x.shape
    rows = pl.BlockSpec((TILE, depth), lambda i: (i, 0))
    return pl.pallas_call(
        held_back(token_back_body, 5, len(after)),
        grid=(seq // TILE,),
        in_specs=[
            pl.BlockSpec((3, TILE, depth), lambda i: (0, i, 0)),
            pl.BlockSpec((3, depth, depth), lambda i: (0, 0, 0)),
            rows,
            rows,
            once(vectors.shape),
        ]
        + [LATER] * len(after),
        out_specs=[rows, whole((2, depth))],
        out_shape=[sds((seq, depth), low), sds((2, depth), f32)],
        compiler_params=params(24),
        cost_estimate=cost(0, 0),
        name="token_back",
    )(back, *from_far(wide, x), grad, vectors, *after)


CORE_ORDERS = ((4, 3, 2, 1), (3, 4, 1, 2))
LATE_ORDERS = ((2, 1, 4, 3), (1, 2, 3, 4))
STAGES = 4


def cube_permute(values, stage, orders=CORE_ORDERS):
    pairs = [(device, device ^ (1 << orders[device & 1][stage])) for device in range(32)]
    return lax.ppermute(values, ("dp", "mp"), pairs)


def bit_permute(values, bit):
    return lax.ppermute(values, ("dp", "mp"), [(device, device ^ (1 << bit)) for device in range(32)])


def place(distance, core, orders):
    spots = [
        sum(((distance >> bit) & 1) << step for step, bit in enumerate(order)) for order in orders
    ]
    return jnp.where(core == 0, spots[0], spots[1])


def joined(held, arrived):
    return jnp.concatenate([held, arrived], axis=0)


def leaving(parts, stage):
    half = 1 << stage
    return sum(part[half:].astype(f32) for part in parts).astype(low)


def staying(parts, stage):
    return [part[: 1 << stage] for part in parts]


def summed(parts):
    return sum(part[0].astype(f32) for part in parts)


def two_parts(values):
    high = lax.reduce_precision(values, 8, 7)
    rest = lax.reduce_precision(values - high, 8, 7)
    return jnp.concatenate([high, rest], axis=0).astype(low)


def one_part(parts):
    half = parts.shape[0] // 2
    return parts[:half].astype(f32) + parts[half:].astype(f32)


def with_rider(blocks, rider, send):
    count, rows, columns = blocks.shape
    parts = two_parts(rider)
    arrived = send(jnp.concatenate([blocks.reshape(count * rows, columns), parts], axis=0))
    total = one_part(parts) + one_part(arrived[count * rows :])
    return arrived[: count * rows].reshape(count, rows, columns), total


def cube_sum(values, bits=range(5)):
    for bit in bits:
        values = values + bit_permute(values, bit)
    return values


def adam_parts(weight, gradient, first_old, second_old, factor, step_rate):
    scaled = gradient * factor
    moment = beta_one * first_old + (1.0 - beta_one) * scaled
    square = beta_two * second_old + (1.0 - beta_two) * scaled * scaled
    spread = jnp.sqrt(square * (1.0 / (1.0 - beta_two**STEP)))
    ratio = moment * (1.0 / (1.0 - beta_one**STEP)) / (spread + adam_eps)
    return moment, square, weight - step_rate * (ratio + decay * weight)


def optimize_body(where_ref, owned_ref, vector_ref, attend_ref, feed_a, feed_b, *refs):
    state, outs = refs[:21], refs[21:]
    vectors = jnp.concatenate([owned_ref[:2], vector_ref[2:]], axis=0)
    total = owned_ref[2:3, 0:1] + jnp.sum(vectors * vectors)
    norm = jnp.sqrt(total)
    factor = clip_norm / jnp.maximum(norm, clip_norm)
    outs[0][...] = norm
    width = state[0].shape[2]
    part = state[6].shape[1] // 3

    def update(param, at, gradient, step_rate):
        weight, first, second = (ref[at] for ref in state[3 * param : 3 * param + 3])
        results = adam_parts(weight, gradient, first, second, factor, step_rate)
        for ref, result in zip(outs[1 + 3 * param : 4 + 3 * param], results):
            ref[at] = result

    for index in range(3):
        update(0, (index,), attend_ref[:, index * width : (index + 1) * width], rate)
    update(1, (...,), attend_ref[:, 3 * width :].T, rate)
    split, rows = feed_a.shape[0], state[6].shape[0]
    for feed_ref, within in ((feed_a, slice(0, split)), (feed_b, slice(split, rows))):
        for index in range(3):
            at = (within, slice(index * part, (index + 1) * part))
            first = 2 * index * part
            update(2, at, feed_ref[:, first : first + part], rate)
            update(3, at, feed_ref[:, first + part : first + 2 * part], rate)
    update(4, (...,), vectors[:6], vector_rate)
    model = where_ref[2]
    head = jnp.zeros((2, width), f32)
    for index in range(4):
        head = head + jnp.where(model == index, vectors[6:8, index * width : (index + 1) * width], 0.0)
    update(5, (...,), head, vector_rate)
    bias = vector_ref[pl.ds(8 + model, 1), :]
    bias = jnp.concatenate([bias[:, at : at + 128] for at in range(0, bias.shape[1], 128)], axis=0)
    update(6, (...,), bias, vector_rate)


def optimize(where, owned, vector_total, attend_total, feed_totals, state):
    shapes = [sds(group[0].shape, f32) for group in state for _ in range(3)]
    arrays = [array for group in state for array in group]
    return pl.pallas_call(
        optimize_body,
        in_specs=[pl.BlockSpec(memory_space=pltpu.SMEM)]
        + [pl.BlockSpec(memory_space=pltpu.VMEM)] * (5 + len(arrays)),
        out_shape=[sds((1, 1), f32)] + shapes,
        compiler_params=params(20),
        cost_estimate=cost(4e6, 8e6),
        name="optimize",
    )(where, owned, vector_total, attend_total, *feed_totals, *from_far(*arrays))


def shards(
    tokens,
    cotangent,
    lengths,
    input_weight,
    output_weight,
    expand_weight,
    shrink_weight,
    layer_vectors,
    head_bias,
    expand_bias,
    first_input,
    first_output,
    first_expand,
    first_shrink,
    first_vectors,
    first_head,
    first_bias,
    second_input,
    second_output,
    second_expand,
    second_shrink,
    second_vectors,
    second_head,
    second_bias,
):
    dp_count = lax.axis_size("dp")
    mp_count = lax.axis_size("mp")
    cube = dp_count == 8 and mp_count == 4
    rows = input_weight.shape[0]
    width = input_weight.shape[2]
    hidden = expand_weight.shape[1]
    seq, depth = tokens.shape
    part = hidden // 3
    model_index = lax.axis_index("mp")
    me = lax.axis_index("dp") * mp_count + model_index

    attend_shard, feed_shard, bias_full = pack(
        input_weight.transpose(1, 0, 2),
        output_weight,
        expand_weight,
        shrink_weight.T,
        head_bias,
        expand_bias.reshape(hidden // 128, 128),
    )
    if cube:
        core, near = me & 1, model_index
        devices = jnp.arange(32).reshape(8, 4).T
        spots = jnp.concatenate(
            [place(devices ^ me, devices & 1, orders) for orders in (CORE_ORDERS, LATE_ORDERS)]
        ).astype(jnp.int32)
    else:
        core = near = jnp.zeros((), jnp.int32)
        spots = (jnp.arange(8)[:, None] % 4 // 2 * 8 + jnp.arange(8)[None]).astype(jnp.int32)
    where = jnp.stack([core, near, model_index]).astype(jnp.int32)

    if cube:
        split = rows * 2 // 3
        held, early, late = attend_shard[None], feed_shard[None, :split], feed_shard[None, split:]
        arrived, far_late = cube_permute(held, 0), cube_permute(late, 0, LATE_ORDERS)
        held, bias_full = lax.optimization_barrier((joined(held, arrived), bias_full))
        arrived = cube_permute(held, 1)
        bias_full = bias_full + bit_permute(bias_full, 0)
        normed, normed_t, upstream_t = prepare(tokens, cotangent, layer_vectors, (held,))
        late = joined(late, far_late)
        held, early, late, normed, bias_full, spots, where = lax.optimization_barrier(
            (held, early, late, normed, bias_full, spots, where)
        )
        held = joined(held, arrived)
        arrived, far_early = cube_permute(held, 2), cube_permute(early, 0)
        far_late = cube_permute(late, 1, LATE_ORDERS)
        bias_full = bias_full + bit_permute(bias_full, 1)
        held, early, late = joined(held, arrived), joined(early, far_early), joined(late, far_late)
        held, early, late, bias_full = lax.optimization_barrier((held, early, late, bias_full))
        far, far_early = cube_permute(held, 3), cube_permute(early, 1)
        twin = bit_permute(held, 0)
        early = joined(early, far_early)
        far, early, late = lax.optimization_barrier((far, early, late))
        attend_halves = (held, far, twin, bit_permute(far, 0))
        far_early, far_late = cube_permute(early, 2), cube_permute(late, 2, LATE_ORDERS)
        qkv, wide, wide_out = project(where, spots, normed, attend_halves, bias_full, ())
        far_early, far_late, qkv = lax.optimization_barrier((far_early, far_late, qkv))
        early, late = joined(early, far_early), joined(late, far_late)
        far_early, far_late = cube_permute(early, 3), cube_permute(late, 3, LATE_ORDERS)
        twin_early, twin_late = bit_permute(early, 0), bit_permute(late, 0)
        mixture, log_totals = attend_forward(where, lengths, qkv, (early, late))
        far_early, far_late, twin_late, mixture = lax.optimization_barrier(
            (far_early, far_late, twin_late, mixture)
        )
        last_early, last_late = bit_permute(far_early, 0), bit_permute(far_late, 0)
        middle, hidden_in, hidden_t, unit, inverse = attend_out(mixture, wide_out, tokens, layer_vectors)
        feed_halves = (early, far_early, twin_early, last_early, late, far_late, twin_late, last_late)
    else:

        def planes(shard):
            full = lax.all_gather(lax.all_gather(shard, "dp", axis=0, tiled=True), "mp", axis=0)
            full = full.reshape(2, 2, 8, depth // 8, shard.shape[1]).transpose(1, 0, 2, 3, 4)
            return tuple(full.reshape(4, 8, depth // 8, shard.shape[1]))

        normed, normed_t, upstream_t = prepare(tokens, cotangent, layer_vectors, ())
        bias_full = lax.psum(bias_full, "mp")
        qkv, wide, wide_out = project(where, spots, normed, planes(attend_shard), bias_full, ())
        mixture, log_totals = attend_forward(where, lengths, qkv, ())
        middle, hidden_in, hidden_t, unit, inverse = attend_out(mixture, wide_out, tokens, layer_vectors)
        split = depth // 8 * 2 // 3
        feed_planes = planes(feed_shard)
        feed_halves = tuple(array[:, :split] for array in feed_planes) + tuple(
            array[:, split:] for array in feed_planes
        )
    block_out, back, keep_early, send_early, keep_late, send_late, bias_grad = feed(
        where,
        spots,
        hidden_in,
        hidden_t,
        cotangent,
        upstream_t,
        feed_halves,
        bias_full,
        middle,
        layer_vectors,
    )
    middle_grad, mixture_grad, output_grad, middle_sums = middle_back(
        where, lengths, back, unit, inverse, cotangent, mixture, wide_out, layer_vectors
    )
    if cube:
        early = [keep_early, bit_permute(send_early, 0)]
        late = [keep_late, bit_permute(send_late, 0)]
        early[0], late[0], mixture_grad = lax.optimization_barrier((early[0], late[0], mixture_grad))
        away, far_away_late = leaving(early, 3), leaving(late, 3)
        packed_grad = attend_backward(
            where, lengths, qkv, mixture_grad, log_totals, (away, far_away_late)
        )
        early = staying(early, 3) + [cube_permute(away, 3)]
        late = staying(late, 3) + [cube_permute(far_away_late, 3, LATE_ORDERS)]
        early[0], late[0], packed_grad = lax.optimization_barrier((early[0], late[0], packed_grad))
        away, far_away_late = leaving(early, 2), leaving(late, 2)
        sums = (middle_sums, bias_grad)
        keep_attend, send_attend, rider = input_grad(
            where, spots, normed_t, packed_grad, output_grad, sums, 16, depth // 8, (away, far_away_late)
        )
        early = staying(early, 2) + [cube_permute(away, 2)]
        late = staying(late, 2) + [cube_permute(far_away_late, 2, LATE_ORDERS)]
        early[-1], late[-1], send_attend = lax.optimization_barrier((early[-1], late[-1], send_attend))
        twin_b, rider = with_rider(send_attend[8:], rider, lambda values: bit_permute(values, 0))
        twin_a = bit_permute(send_attend[:8], 0)
        away = (keep_attend[8:].astype(f32) + twin_b.astype(f32)).astype(low)
        arrived, rider = with_rider(away, rider, lambda values: cube_permute(values, 3))
        attend_parts = [keep_attend[:8], twin_a, arrived]
        feed_away = leaving(early, 1)
        token_grad, token_sums = token_back(
            packed_grad, wide, tokens, middle_grad, layer_vectors, (away, feed_away)
        )
        early = staying(early, 1) + [cube_permute(feed_away, 1)]
        attend_parts[0], late[0], token_sums = lax.optimization_barrier(
            (attend_parts[0], late[0], token_sums)
        )
        away = leaving(attend_parts, 2)
        arrived, rider = with_rider(away, rider, lambda values: cube_permute(values, 2))
        attend_parts = staying(attend_parts, 2) + [arrived]
        away, early[0] = lax.optimization_barrier((away, early[0]))
        feed_away = leaving(early, 0)
        early = staying(early, 0) + [cube_permute(feed_away, 0)]
        feed_away = leaving(late, 1)
        away = leaving(attend_parts, 1)
        arrived, rider = with_rider(away, rider, lambda values: cube_permute(values, 1))
        late = staying(late, 1) + [cube_permute(feed_away, 1, LATE_ORDERS)]
        attend_parts = staying(attend_parts, 1) + [arrived]
        away, early[0] = lax.optimization_barrier((away, early[0]))
        early_total = summed(early)
        feed_away = leaving(late, 0)
        away = leaving(attend_parts, 0)
        away, early_total = lax.optimization_barrier((away, early_total))
        arrived, vector_total = with_rider(away, rider, lambda values: cube_permute(values, 0))
        late = staying(late, 0) + [cube_permute(feed_away, 0, LATE_ORDERS)]
        attend_parts = staying(attend_parts, 0) + [arrived]
        late_total, attend_total = summed(late), summed(attend_parts)
        feed_totals = (early_total, late_total)
    else:
        packed_grad = attend_backward(where, lengths, qkv, mixture_grad, log_totals, ())
        sums = (middle_sums, bias_grad)
        keep_attend, send_attend, vector_total = input_grad(
            where, spots, normed_t, packed_grad, output_grad, sums, 16, depth // 8, ()
        )
        token_grad, token_sums = token_back(packed_grad, wide, tokens, middle_grad, layer_vectors, ())
        vector_total = lax.psum(vector_total, ("dp", "mp"))

    if not cube:

        def own_block(keep, send):
            full = jnp.stack([keep, send]).reshape(2, 2, 8, keep.shape[1], keep.shape[2])
            full = full.transpose(1, 0, 2, 3, 4).reshape(4, 8 * keep.shape[1], keep.shape[2])
            full = lax.psum_scatter(full, "mp", scatter_dimension=0, tiled=False)
            return lax.psum(full, "dp")

        def own_rows(*blocks):
            full = jnp.concatenate([block.reshape(8, -1, block.shape[1]) for block in blocks], axis=1)
            full = full.reshape(depth, full.shape[2]).astype(f32)
            return lax.dynamic_slice_in_dim(full, lax.axis_index("dp") * rows, rows, 0)

        attend_total = own_rows(own_block(keep_attend, send_attend))
        feed_total = own_rows(own_block(keep_early, send_early), own_block(keep_late, send_late))
        feed_totals = feed_total[: rows * 2 // 3], feed_total[rows * 2 // 3 :]
    owned = sum(jnp.sum(total * total) for total in (attend_total, *feed_totals))
    row = lax.broadcasted_iota(jnp.int32, (3, depth), 0)
    owned = jnp.where(row == 2, owned, jnp.pad(token_sums, ((0, 1), (0, 0))))
    owned = cube_sum(owned) if cube else lax.psum(owned, ("dp", "mp"))
    def turned(array):
        return array.transpose(1, 0, 2)

    state = (
        (turned(input_weight), turned(first_input), turned(second_input)),
        (output_weight, first_output, second_output),
        (expand_weight, first_expand, second_expand),
        (shrink_weight.T, first_shrink.T, second_shrink.T),
        (layer_vectors, first_vectors, second_vectors),
        (head_bias, first_head, second_head),
        tuple(array.reshape(hidden // 128, 128) for array in (expand_bias, first_bias, second_bias)),
    )
    grad_norm, *updates = optimize(where, owned, vector_total, attend_total, feed_totals, state)
    grad_norm = grad_norm[0, 0]
    moment_input, square_input, updated_input = (turned(array) for array in updates[:3])
    moment_output, square_output, updated_output = updates[3:6]
    moment_expand, square_expand, updated_expand = updates[6:9]
    moment_shrink, square_shrink, updated_shrink = (array.T for array in updates[9:12])
    moment_vectors, square_vectors, updated_vectors = updates[12:15]
    moment_head, square_head, updated_head = updates[15:18]
    moment_bias, square_bias, updated_bias = (array.reshape(hidden) for array in updates[18:])
    return (
        block_out,
        token_grad,
        grad_norm,
        moment_input,
        square_input,
        updated_input,
        moment_output,
        square_output,
        updated_output,
        moment_expand,
        square_expand,
        updated_expand,
        moment_shrink,
        square_shrink,
        updated_shrink,
        moment_vectors,
        square_vectors,
        updated_vectors,
        moment_head,
        square_head,
        updated_head,
        moment_bias,
        square_bias,
        updated_bias,
    )


def solution(mesh):
    in_specs = (
        P(("dp", "mp"), None),
        P(("dp", "mp"), None),
        P("dp"),
        P("dp", None, "mp"),
        P("mp", "dp"),
        P("dp", "mp"),
        P("mp", "dp"),
        P(),
        P(None, "mp"),
        P("mp"),
        P("dp", None, "mp"),
        P("mp", "dp"),
        P("dp", "mp"),
        P("mp", "dp"),
        P(),
        P(None, "mp"),
        P("mp"),
        P("dp", None, "mp"),
        P("mp", "dp"),
        P("dp", "mp"),
        P("mp", "dp"),
        P(),
        P(None, "mp"),
        P("mp"),
    )
    out_specs = (
        P(("dp", "mp"), None),
        P(("dp", "mp"), None),
        P(),
        P("dp", None, "mp"),
        P("dp", None, "mp"),
        P("dp", None, "mp"),
        P("mp", "dp"),
        P("mp", "dp"),
        P("mp", "dp"),
        P("dp", "mp"),
        P("dp", "mp"),
        P("dp", "mp"),
        P("mp", "dp"),
        P("mp", "dp"),
        P("mp", "dp"),
        P(),
        P(),
        P(),
        P(None, "mp"),
        P(None, "mp"),
        P(None, "mp"),
        P("mp"),
        P("mp"),
        P("mp"),
    )
    return jax.shard_map(shards, mesh=mesh, in_specs=in_specs, out_specs=out_specs, check_vma=False)
```

```python
import functools
import jax
import jax.numpy as jnp
from jax import lax
from jax.experimental import pallas as pl
from jax.experimental.pallas import tpu as pltpu
from jax.sharding import PartitionSpec as P

HEAD_DIM = 64
TILE = 256
STEP = 10

eps_norm = 1e-05
clip_norm = 1.0
beta_one = 0.9
beta_two = 0.999
adam_eps = 1e-08
rate = 0.05
vector_rate = 0.5
decay = 0.01
excluded = -1e30
low = jnp.bfloat16
f32 = jnp.float32
GELU_A = 0.7978845608028654
GELU_B = GELU_A * 0.044715


def params(limit_mib, **kw):
    return pltpu.CompilerParams(vmem_limit_bytes=limit_mib * 1024 * 1024, **kw)


def cost(flops, moved, special=0):
    return pl.CostEstimate(flops=int(flops), bytes_accessed=int(moved), transcendentals=int(special))


def mm(a, b):
    return jnp.dot(a, b, preferred_element_type=f32)


def mm_nt(a, b):
    return lax.dot_general(a, b, (((1,), (1,)), ((), ())), preferred_element_type=f32)


def whole(shape):
    zeros = (0,) * len(shape)
    return pl.BlockSpec(shape, lambda *_: zeros)


def once(shape):
    zeros = (0,) * len(shape)
    return pl.BlockSpec(shape, lambda *_: zeros, pipeline_mode=pl.Buffered(1))


def held_back(body, first, count):
    def run(*refs):
        return body(*refs[:first], *refs[first + count :])

    return run


LATER = pl.BlockSpec(memory_space=pl.ANY)


def far_away(shape, dtype):
    return pltpu.HBM(shape, dtype)


def from_far(*arrays):
    return [pltpu.with_memory_space_constraint(array, pltpu.HBM) for array in arrays]


def sds(shape, dtype):
    return jax.ShapeDtypeStruct(shape, dtype)


def live_blocks(length, count, body):
    for blocks in range(1, count + 1):
        low_end = (blocks - 1) * TILE
        high_end = blocks * TILE
        @pl.when((length > low_end) & (length <= high_end))
        def _(blocks=blocks):
            body(length, blocks)


PAIR = 2 * HEAD_DIM


def span(block):
    return slice(block * TILE, (block + 1) * TILE)


def both_heads(values):
    lane = lax.broadcasted_iota(jnp.int32, values.shape, 1)
    none = jnp.zeros_like(values)
    return jnp.concatenate(
        [jnp.where(lane < HEAD_DIM, values, none), jnp.where(lane >= HEAD_DIM, values, none)], axis=0
    )


def causal_mask():
    key_id = lax.broadcasted_iota(jnp.int32, (TILE, 2 * TILE), 0)
    query_id = lax.broadcasted_iota(jnp.int32, (TILE, 2 * TILE), 1) & (TILE - 1)
    return key_id <= query_id


def forward_body(where_ref, lengths_ref, q_ref, k_ref, v_ref, o_ref, lse_ref, vt_ref):
    seq = q_ref.shape[0]
    vt_ref[...] = v_ref[...].T
    causal = causal_mask()

    def run(length, blocks):
        def scores(b):
            q = q_ref[span(b), :] * jnp.asarray(HEAD_DIM**-0.5, low)
            return mm_nt(k_ref[: (b + 1) * TILE, :], both_heads(q))

        now = scores(0)
        for b in range(blocks):
            start, stop = b * TILE, (b + 1) * TILE
            later = scores(b + 1) if b + 1 < blocks else None
            last = jnp.where(causal, now[start:, :], excluded)
            top = jnp.max(last, axis=0, keepdims=True)
            if b:
                top = jnp.maximum(top, jnp.max(now[:start], axis=0, keepdims=True))
            p = jnp.exp(last - top)
            total = jnp.sum(p, axis=0, keepdims=True)
            pb = p.astype(low)
            if b:
                pf = jnp.exp(now[:start] - top)
                total = total + jnp.sum(pf, axis=0, keepdims=True)
                pb = jnp.concatenate([pf.astype(low), pb], axis=0)
            inverse = 1.0 / total
            lse = top + jnp.log(total)
            outs = []
            for h in range(2):
                at = slice(h * TILE, (h + 1) * TILE)
                out = mm(vt_ref[h * HEAD_DIM : (h + 1) * HEAD_DIM, :stop], pb[:, at])
                outs.append(out * inverse[:, at])
                lse_ref[0, h : h + 1, start:stop] = lse[:, at]
            both = jnp.concatenate(outs, axis=0).T
            row = start + lax.broadcasted_iota(jnp.int32, both.shape, 0)
            o_ref[start:stop, :] = jnp.where(row < length, both, 0.0).astype(low)
            now = later
        if blocks * TILE < seq:
            o_ref[blocks * TILE :, :] = jnp.zeros((seq - blocks * TILE, PAIR), low)
            lse_ref[0, :, blocks * TILE :] = jnp.zeros((2, seq - blocks * TILE), f32)

    live_blocks(lengths_ref[where_ref[2]], seq // TILE, run)


def attend_forward(where, lengths, qkv, after):
    seq, width = qkv.shape[0], qkv.shape[1] // 3
    pair = 2 * HEAD_DIM
    pairs = width // pair
    half = seq * seq * 5 // 8
    spec = lambda part: pl.BlockSpec((seq, pair), lambda i, *_: (0, part * pairs + i))
    return pl.pallas_call(
        held_back(forward_body, 5, len(after)),
        grid_spec=pltpu.PrefetchScalarGridSpec(
            num_scalar_prefetch=2,
            grid=(pairs,),
            in_specs=[spec(0), spec(1), spec(2)] + [LATER] * len(after),
            out_specs=[
                pl.BlockSpec((seq, pair), lambda i, *_: (0, i)),
                pl.BlockSpec((1, 2, seq), lambda i, *_: (i, 0, 0)),
            ],
            scratch_shapes=[pltpu.VMEM((pair, seq), low)],
        ),
        out_shape=[sds((seq, width), low), far_away((pairs, 2, seq), f32)],
        compiler_params=params(20),
        cost_estimate=cost(pairs * 2 * half * 2 * 2 * 256, seq * width * 8, pairs * 2 * half),
        name="attend_forward",
    )(where, lengths, *from_far(qkv, qkv, qkv), *after)


def backward_body(where_ref, lengths_ref, q_ref, k_ref, v_ref, do_ref, lse_ref, out_ref, kt_ref, ksum, vsum):
    seq = q_ref.shape[0]
    scale = HEAD_DIM**-0.5
    kt_ref[...] = k_ref[...].T
    causal = causal_mask()

    def run(length, blocks):
        def scores(b):
            qq = both_heads(q_ref[span(b), :] * jnp.asarray(scale, low))
            uu = both_heads(do_ref[span(b), :])
            stop = (b + 1) * TILE
            return qq, uu, mm_nt(k_ref[:stop, :], qq), mm_nt(v_ref[:stop, :], uu)

        now = scores(blocks - 1)
        for b in reversed(range(blocks)):
            start, stop = b * TILE, (b + 1) * TILE
            later = scores(b - 1) if b else None
            qq, uu, s, dp = now
            lse = jnp.concatenate([lse_ref[0, 0:1, start:stop], lse_ref[0, 1:2, start:stop]], axis=1)
            p = jnp.exp(jnp.where(causal, s[start:], excluded) - lse)
            inner = jnp.sum(p * dp[start:], axis=0, keepdims=True)
            if b:
                pf = jnp.exp(s[:start] - lse)
                inner = inner + jnp.sum(pf * dp[:start], axis=0, keepdims=True)
            ds = (p * (dp[start:] - inner)).astype(low)
            pb = p.astype(low)
            if b:
                ds = jnp.concatenate([(pf * (dp[:start] - inner)).astype(low), ds], axis=0)
                pb = jnp.concatenate([pf.astype(low), pb], axis=0)
            dk, dv = mm(ds, qq), mm(pb, uu)
            if b == blocks - 1:
                ksum[:stop, :] = dk
                vsum[:stop, :] = dv
            else:
                ksum[:stop, :] += dk
                vsum[:stop, :] += dv
            dq = jnp.concatenate(
                [
                    mm(
                        kt_ref[h * HEAD_DIM : (h + 1) * HEAD_DIM, :stop],
                        ds[:, h * TILE : (h + 1) * TILE],
                    )
                    for h in range(2)
                ],
                axis=0,
            )
            out_ref[1, start:stop, :] = ksum[start:stop, :].astype(low)
            out_ref[2, start:stop, :] = vsum[start:stop, :].astype(low)
            out_ref[0, start:stop, :] = (dq.T * scale).astype(low)
            now = later
        if blocks * TILE < seq:
            rest = jnp.zeros((seq - blocks * TILE, PAIR), low)
            for part in range(3):
                out_ref[part, blocks * TILE :, :] = rest

    live_blocks(lengths_ref[where_ref[2]], seq // TILE, run)


def attend_backward(where, lengths, qkv, upstream, lse, after):
    seq, width = upstream.shape
    pair = 2 * HEAD_DIM
    pairs = width // pair
    half = seq * seq * 5 // 8
    spec = lambda part: pl.BlockSpec((seq, pair), lambda i, *_: (0, part * pairs + i))
    own = pl.BlockSpec((seq, pair), lambda i, *_: (0, i))
    return pl.pallas_call(
        held_back(backward_body, 7, len(after)),
        grid_spec=pltpu.PrefetchScalarGridSpec(
            num_scalar_prefetch=2,
            grid=(pairs,),
            in_specs=[spec(0), spec(1), spec(2), own, pl.BlockSpec((1, 2, seq), lambda i, *_: (i, 0, 0))]
            + [LATER] * len(after),
            out_specs=pl.BlockSpec((3, seq, pair), lambda i, *_: (0, 0, i)),
            scratch_shapes=[
                pltpu.VMEM((pair, seq), low),
                pltpu.VMEM((seq, pair), f32),
                pltpu.VMEM((seq, pair), f32),
            ],
        ),
        out_shape=sds((3, seq, width), low),
        compiler_params=params(28),
        cost_estimate=cost(pairs * 2 * half * 5 * 2 * 256, seq * width * 14, pairs * 2 * half),
        name="attend_backward",
    )(where, lengths, *from_far(qkv, qkv, qkv), upstream, *from_far(lse), *after)


def normalize(values):
    average = jnp.mean(values, axis=-1, keepdims=True)
    centred = values - average
    inverse = lax.rsqrt(jnp.mean(centred * centred, axis=-1, keepdims=True) + eps_norm)
    return centred * inverse, inverse


def pull_norm(scaled, unit, inverse):
    first = jnp.mean(scaled, axis=-1, keepdims=True)
    second = jnp.mean(scaled * unit, axis=-1, keepdims=True)
    return inverse * (scaled - first - unit * second)


def columns_of(values):
    return jnp.sum(values, axis=0, keepdims=True)


def pack_body(
    input_ref, output_ref, expand_ref, shrink_ref, head_ref, hidden_ref, attend_ref, feed_ref, bias_ref
):
    width = input_ref.shape[2]
    part = expand_ref.shape[1] // 3
    for index in range(3):
        attend_ref[:, index * width : (index + 1) * width] = input_ref[index].astype(low)
        at = slice(index * part, (index + 1) * part)
        feed_ref[:, 2 * index * part : (2 * index + 1) * part] = expand_ref[:, at].astype(low)
        feed_ref[:, (2 * index + 1) * part : (2 * index + 2) * part] = shrink_ref[:, at].astype(low)
    attend_ref[:, 3 * width :] = output_ref[...].T.astype(low)
    pieces = [head_ref[0:1, :], head_ref[1:2, :]]
    pieces += [hidden_ref[row : row + 1, :] for row in range(hidden_ref.shape[0])]
    bias_ref[...] = jnp.zeros_like(bias_ref)
    bias_ref[pl.ds(lax.axis_index("mp"), 1), :] = jnp.concatenate(pieces, axis=1)


def pack(input_weight, output_weight, expand, shrink, head_bias, hidden_bias):
    rows, width = input_weight.shape[1:]
    hidden = expand.shape[1]
    return pl.pallas_call(
        pack_body,
        out_shape=[
            sds((rows, 4 * width), low),
            sds((rows, 2 * hidden), low),
            sds((4, 2 * width + hidden), f32),
        ],
        compiler_params=params(6),
        cost_estimate=cost(rows * hidden, rows * hidden * 18),
        name="pack",
    )(*from_far(input_weight, output_weight, expand, shrink, head_bias, hidden_bias))


def prepare_body(x_ref, up_ref, vec_ref, h_ref, ht_ref, upt_ref):
    unit, _ = normalize(x_ref[...].astype(f32))
    h = (unit * vec_ref[0:1, :] + vec_ref[1:2, :]).astype(low)
    h_ref[...] = h
    ht_ref[...] = h.T
    upt_ref[...] = up_ref[...].T


def prepare(x, up, vectors, after):
    seq, depth = x.shape
    rows = pl.BlockSpec((2 * TILE, depth), lambda i: (i, 0))
    turned = pl.BlockSpec((depth, 2 * TILE), lambda i: (0, i))
    return pl.pallas_call(
        held_back(prepare_body, 3, len(after)),
        grid=(seq // (2 * TILE),),
        in_specs=[rows, rows, once(vectors.shape)] + [LATER] * len(after),
        out_specs=[rows, turned, turned],
        out_shape=[sds((seq, depth), low), sds((depth, seq), low), far_away((depth, seq), low)],
        compiler_params=params(16),
        cost_estimate=cost(seq * depth * 10, seq * depth * 10),
        name="prepare",
    )(*from_far(x, up), vectors, *after)


def slot(halves, spot, at):
    first, second = halves
    inner = spot & 7
    return jnp.where(spot < 8, first[inner, :, at], second[inner, :, at])


def project_body(
    where_ref, spots_ref, h_ref, mine_a, mine_b, twin_a, twin_b, bias_ref, qkv_ref, wide_ref, last_ref
):
    part = pl.program_id(0)
    rows = mine_a.shape[1]
    width = mine_a.shape[2] // 4
    groups = wide_ref.shape[1] // rows

    def collect(sources, index):
        columns = slice(index * width, (index + 1) * width)
        for group in range(groups):
            pieces = [slot(sources[model % 2], spots_ref[model, group], columns) for model in range(4)]
            at = slice(group * rows, (group + 1) * rows)
            if index < 3:
                wide_ref[0, at, :] = jnp.concatenate(pieces, axis=1)
            else:
                last_ref[at, :] = jnp.concatenate(pieces, axis=1)

    for index in range(4):
        for core in range(2):

            @pl.when((part == index) & (where_ref[0] == core))
            def _(index=index, core=core):
                mine, twin = (mine_a, mine_b), (twin_a, twin_b)
                collect((mine, twin) if core == 0 else (twin, mine), index)

    for index in range(3):

        @pl.when(part == index)
        def _(index=index):
            out = mm(h_ref[...], wide_ref[0])
            if index != 1:
                at = slice(index // 2 * width, (index // 2 + 1) * width)
                bias = jnp.concatenate([bias_ref[model : model + 1, at] for model in range(4)], axis=1)
                out = out + bias
            qkv_ref[...] = out.astype(low)


def project(where, spots, h, halves, bias, after):
    seq, depth = h.shape
    return pl.pallas_call(
        held_back(project_body, 8, len(after)),
        grid_spec=pltpu.PrefetchScalarGridSpec(
            num_scalar_prefetch=2,
            grid=(4,),
            in_specs=[
                once((seq, depth)),
                *[once(halves[0].shape)] * 4,
                once(bias.shape),
            ]
            + [LATER] * len(after),
            out_specs=[
                pl.BlockSpec((seq, depth), lambda i, *_: (0, jnp.minimum(i, 2))),
                pl.BlockSpec((1, depth, depth), lambda i, *_: (jnp.minimum(i, 2), 0, 0)),
                whole((depth, depth)),
            ],
        ),
        out_shape=[
            far_away((seq, 3 * depth), low),
            far_away((3, depth, depth), low),
            sds((depth, depth), low),
        ],
        compiler_params=params(24),
        cost_estimate=cost(2 * seq * depth * depth * 3, seq * depth * 16),
        name="project",
    )(where, spots, h, *halves, bias, *after)


NEAR = pl.BlockSpec(memory_space=pltpu.VMEM)
SCALARS = pl.BlockSpec(memory_space=pltpu.SMEM)


def attend_out_body(o_ref, w_ref, x_ref, vec_ref, middle_ref, h_ref, ht_ref, unit_ref, inverse_ref):
    for tile in range(o_ref.shape[0] // TILE):
        at = slice(tile * TILE, (tile + 1) * TILE)
        middle = x_ref[at, :].astype(f32) + mm_nt(o_ref[at, :], w_ref[...]) + vec_ref[4:5, :]
        middle_ref[at, :] = middle.astype(low)
        unit, inverse = normalize(middle)
        unit_ref[at, :] = unit.astype(low)
        inverse_ref[at, :] = jnp.broadcast_to(inverse, (TILE, inverse_ref.shape[1]))
        h = (unit * vec_ref[2:3, :] + vec_ref[3:4, :]).astype(low)
        h_ref[at, :] = h
        ht_ref[:, at] = h.T


def attend_out(o, wide_out, x, vectors):
    seq, depth = x.shape
    return pl.pallas_call(
        attend_out_body,
        in_specs=[NEAR] * 4,
        out_specs=[NEAR] * 5,
        out_shape=[
            sds((seq, depth), low),
            sds((seq, depth), low),
            sds((depth, seq), low),
            sds((seq, depth), low),
            sds((seq, 128), f32),
        ],
        compiler_params=params(10),
        cost_estimate=cost(2 * seq * depth * depth, seq * depth * 14),
        name="attend_out",
    )(o, wide_out, x, vectors)


def feed_body(
    where_ref,
    spots_ref,
    h2_ref,
    h2t_ref,
    up_ref,
    upt_ref,
    mine_a,
    mine_b,
    twin_a,
    twin_b,
    mine_c,
    mine_d,
    twin_c,
    twin_d,
    bias_ref,
    middle_ref,
    vec_ref,
    block_ref,
    back_ref,
    keep_a,
    send_a,
    keep_b,
    send_b,
    bias_grad_ref,
    out_ref,
    sum_ref,
    wide_ref,
    act_ref,
    pre_ref,
):
    part = mine_a.shape[2] // 6
    groups = spots_ref.shape[1]
    rows = wide_ref.shape[0] // groups
    split = mine_a.shape[1]
    skip = bias_ref.shape[1] - bias_grad_ref.shape[1]
    pieces = (
        ((mine_a, mine_b), (twin_a, twin_b), keep_a, send_a, 0, slice(0, split)),
        ((mine_c, mine_d), (twin_c, twin_d), keep_b, send_b, 4, slice(split, rows)),
    )
    out_ref[...] = middle_ref[...].astype(f32) + vec_ref[5:6, :]
    sum_ref[...] = jnp.zeros_like(sum_ref)

    def step(index, carry):
        side = lax.rem(index, 2)
        first = pl.multiple_of(index // 2 * part, 128)
        lanes = pl.ds(pl.multiple_of(2 * first, 128), part)
        next_lanes = pl.ds(pl.multiple_of(2 * first + part, 128), part)
        models = [where_ref[1] ^ (2 * side + core) for core in range(2)]
        for group in range(groups):
            for mine, twin, _, _, table, within in pieces:
                at = slice(group * rows + within.start, group * rows + within.stop)
                for core, halves in enumerate((mine, twin)):
                    spot = spots_ref[table + models[core], group]
                    wide_ref[at, core * part : (core + 1) * part] = slot(halves, spot, lanes)
                    wide_ref[at, (2 + core) * part : (3 + core) * part] = slot(halves, spot, next_lanes)

        expand = wide_ref[:, : 2 * part]
        shrink = wide_ref[:, 2 * part :]
        bias = jnp.concatenate(
            [bias_ref[pl.ds(model, 1), pl.ds(pl.multiple_of(skip + first, 128), part)] for model in models],
            axis=1,
        )
        sums = jnp.zeros((1, 2 * part), f32)
        for tile in range(h2_ref.shape[0] // TILE):
            at = slice(tile * TILE, (tile + 1) * TILE)
            u = mm(h2_ref[at, :], expand) + bias
            square = u * u
            th = jnp.tanh(u * (GELU_A + GELU_B * square))
            gate = 0.5 * th + 0.5
            slope = gate + (gate * (1.0 - gate)) * (u * (2.0 * GELU_A + (6.0 * GELU_B) * square))
            pre = (mm(up_ref[at, :], shrink) * slope).astype(low)
            act_ref[at, :] = (u * gate).astype(low)
            pre_ref[at, :] = pre
            sums = sums + columns_of(pre.astype(f32))
        for core, model in enumerate(models):
            bias_grad_ref[pl.ds(model, 1), pl.ds(first, part)] = sums[:, core * part : (core + 1) * part]
        out_ref[...] += mm_nt(act_ref[...], shrink)
        sum_ref[...] += mm_nt(pre_ref[...], expand)
        grad_expand = mm(h2t_ref[...], pre_ref[...]).astype(low)
        grad_shrink = mm(upt_ref[...], act_ref[...]).astype(low)
        for group in range(groups):
            for _, _, keep, send, table, within in pieces:
                at = slice(group * rows + within.start, group * rows + within.stop)
                for core, target in enumerate((keep, send)):
                    spot = spots_ref[table + models[core], group]
                    columns = slice(core * part, (core + 1) * part)
                    target[spot, :, lanes] = grad_expand[at, columns]
                    target[spot, :, next_lanes] = grad_shrink[at, columns]
        return carry

    lax.fori_loop(0, 6, step, 0)
    block_ref[...] = out_ref[...].astype(low)
    back_ref[...] = sum_ref[...].astype(low)


def feed(where, spots, h2, h2t, up, upt, halves, bias, middle, vectors):
    seq, depth = h2.shape
    half, _, columns = halves[0].shape
    part = columns // 6
    splits = [halves[0].shape[1], halves[4].shape[1]]
    return pl.pallas_call(
        feed_body,
        in_specs=[SCALARS] * 2 + [NEAR] * 15,
        out_specs=[NEAR] * 7,
        scratch_shapes=[
            pltpu.VMEM((seq, depth), f32),
            pltpu.VMEM((seq, depth), f32),
            pltpu.VMEM((depth, 4 * part), low),
            pltpu.VMEM((seq, 2 * part), low),
            pltpu.VMEM((seq, 2 * part), low),
        ],
        out_shape=[sds((seq, depth), low)] * 2
        + [sds((2 * half, rows, columns), low) for rows in splits for _ in range(2)]
        + [sds((4, 3 * part), f32)],
        compiler_params=params(22),
        cost_estimate=cost(12 * seq * depth * 12 * part, seq * depth * 40, seq * 6 * part),
        name="feed",
    )(where, spots, h2, h2t, up, upt, *halves, bias, middle, vectors)


def middle_back_body(
    where_ref,
    lengths_ref,
    back_ref,
    unit_ref,
    inverse_ref,
    up_ref,
    o_ref,
    w_ref,
    vec_ref,
    grad_ref,
    mixture_ref,
    weight_ref,
    sums_ref,
    turned_ref,
):
    length = lengths_ref[where_ref[2]]
    sums = jnp.zeros(sums_ref.shape, f32)
    for tile in range(back_ref.shape[0] // TILE):
        at = slice(tile * TILE, (tile + 1) * TILE)
        unit, inverse = unit_ref[at, :].astype(f32), inverse_ref[at, 0:1]
        back = back_ref[at, :].astype(f32)
        up = up_ref[at, :].astype(f32)
        grad = up + pull_norm(back * vec_ref[2:3, :], unit, inverse)
        rounded = grad.astype(low)
        grad_ref[at, :] = rounded
        turned_ref[:, at] = rounded.T
        row = tile * TILE + lax.broadcasted_iota(jnp.int32, grad.shape, 0)
        mixture_ref[at, :] = jnp.where(row < length, mm(rounded, w_ref[...]), 0.0).astype(low)
        sums = sums + jnp.concatenate(
            [columns_of(back * unit), columns_of(back), columns_of(grad), columns_of(up)], axis=0
        )
    sums_ref[...] = sums
    weight_ref[...] = mm(turned_ref[...], o_ref[...]).astype(low)


def middle_back(where, lengths, back, unit, inverse, up, o, wide_out, vectors):
    seq, depth = unit.shape
    return pl.pallas_call(
        middle_back_body,
        in_specs=[SCALARS] * 2 + [NEAR] * 7,
        out_specs=[NEAR] * 4,
        scratch_shapes=[pltpu.VMEM((depth, seq), low)],
        out_shape=[
            sds((seq, depth), low),
            sds((seq, depth), low),
            sds((depth, depth), low),
            sds((4, depth), f32),
        ],
        compiler_params=params(14),
        cost_estimate=cost(4 * seq * depth * depth, seq * depth * 28),
        name="middle_back",
    )(where, lengths, back, unit, inverse, up, o, wide_out, vectors)


def input_grad_body(
    where_ref,
    spots_ref,
    ht_ref,
    back_ref,
    out_grad_ref,
    middle_ref,
    bias_ref,
    keep_ref,
    send_ref,
    sums_ref,
):
    rows = keep_ref.shape[1]
    width = keep_ref.shape[2] // 4
    groups = ht_ref.shape[0] // rows

    def spread(targets, index, grad):
        at = slice(index * width, (index + 1) * width)
        for group in range(groups):
            for model in range(4):
                targets[model % 2][spots_ref[model, group], :, at] = grad[
                    group * rows : (group + 1) * rows, model * width : (model + 1) * width
                ]

    sums_ref[:2] = jnp.zeros((2, sums_ref.shape[1]), f32)
    sums_ref[2:6] = middle_ref[...]
    sums_ref[6:7] = columns_of(back_ref[0].astype(f32))
    sums_ref[7:8] = columns_of(back_ref[2].astype(f32))
    sums_ref[8:] = bias_ref[...]
    for index in range(4):
        grad = mm(ht_ref[...], back_ref[index]).astype(low) if index < 3 else out_grad_ref[...]
        for core in range(2):

            @pl.when(where_ref[0] == core)
            def _(core=core, index=index, grad=grad):
                spread((keep_ref, send_ref) if core == 0 else (send_ref, keep_ref), index, grad)


def input_grad(where, spots, ht, back, out_grad, sums, slots, rows, after):
    depth, seq = ht.shape
    shape = (slots, rows, depth)
    return pl.pallas_call(
        held_back(input_grad_body, 7, len(after)),
        in_specs=[SCALARS] * 2 + [NEAR] * 5 + [LATER] * len(after),
        out_specs=[NEAR] * 3,
        out_shape=[sds(shape, low), sds(shape, low), sds((12, depth), f32)],
        compiler_params=params(14),
        cost_estimate=cost(6 * seq * depth * depth, seq * depth * 14),
        name="input_grad",
    )(where, spots, ht, back, out_grad, *sums, *after)


def token_back_body(
    back_ref, w_ref, x_ref, grad_ref, vec_ref, token_ref, sums_ref
):
    step = pl.program_id(0)
    back = mm_nt(back_ref[0], w_ref[0]) + mm_nt(back_ref[1], w_ref[1]) + mm_nt(back_ref[2], w_ref[2])
    unit, inverse = normalize(x_ref[...].astype(f32))
    grad = grad_ref[...].astype(f32)
    token_ref[...] = (grad + pull_norm(back * vec_ref[0:1, :], unit, inverse)).astype(low)
    sums = jnp.concatenate([columns_of(back * unit), columns_of(back)], axis=0)

    @pl.when(step == 0)
    def _():
        sums_ref[...] = sums

    @pl.when(step > 0)
    def _():
        sums_ref[...] += sums


def token_back(back, wide, x, grad, vectors, after):
    seq, depth = x.shape
    rows = pl.BlockSpec((TILE, depth), lambda i: (i, 0))
    return pl.pallas_call(
        held_back(token_back_body, 5, len(after)),
        grid=(seq // TILE,),
        in_specs=[
            pl.BlockSpec((3, TILE, depth), lambda i: (0, i, 0)),
            pl.BlockSpec((3, depth, depth), lambda i: (0, 0, 0)),
            rows,
            rows,
            once(vectors.shape),
        ]
        + [LATER] * len(after),
        out_specs=[rows, whole((2, depth))],
        out_shape=[sds((seq, depth), low), sds((2, depth), f32)],
        compiler_params=params(24),
        cost_estimate=cost(6 * seq * depth * depth, seq * depth * 16),
        name="token_back",
    )(back, *from_far(wide, x), grad, vectors, *after)


CORE_ORDERS = ((4, 3, 2, 1), (3, 4, 1, 2))
LATE_ORDERS = ((2, 1, 4, 3), (1, 2, 3, 4))
STAGES = 4


def cube_permute(values, stage, orders=CORE_ORDERS):
    pairs = [(device, device ^ (1 << orders[device & 1][stage])) for device in range(32)]
    return lax.ppermute(values, ("dp", "mp"), pairs)


def bit_permute(values, bit):
    return lax.ppermute(values, ("dp", "mp"), [(device, device ^ (1 << bit)) for device in range(32)])


def place(distance, core, orders):
    spots = [
        sum(((distance >> bit) & 1) << step for step, bit in enumerate(order)) for order in orders
    ]
    return jnp.where(core == 0, spots[0], spots[1])


def joined(held, arrived):
    return jnp.concatenate([held, arrived], axis=0)


def leaving(parts, stage):
    half = 1 << stage
    return sum(part[half:].astype(f32) for part in parts).astype(low)


def staying(parts, stage):
    return [part[: 1 << stage] for part in parts]


def summed(parts):
    return sum(part[0].astype(f32) for part in parts)


def two_parts(values):
    high = lax.reduce_precision(values, 8, 7)
    rest = lax.reduce_precision(values - high, 8, 7)
    return jnp.concatenate([high, rest], axis=0).astype(low)


def one_part(parts):
    half = parts.shape[0] // 2
    return parts[:half].astype(f32) + parts[half:].astype(f32)


def with_rider(blocks, rider, send):
    count, rows, columns = blocks.shape
    parts = two_parts(rider)
    message = jnp.concatenate([blocks.reshape(count * rows, columns), parts], axis=0)
    arrived = send(message)
    total = one_part(parts) + one_part(arrived[count * rows :])
    return arrived[: count * rows].reshape(count, rows, columns), total, message


def cube_sum(values, bits=range(5)):
    for bit in bits:
        values = values + bit_permute(values, bit)
    return values


def adam_parts(weight, gradient, first_old, second_old, factor, step_rate):
    scaled = gradient * factor
    moment = beta_one * first_old + (1.0 - beta_one) * scaled
    square = beta_two * second_old + (1.0 - beta_two) * scaled * scaled
    spread = jnp.sqrt(square * (1.0 / (1.0 - beta_two**STEP)))
    ratio = moment * (1.0 / (1.0 - beta_one**STEP)) / (spread + adam_eps)
    return moment, square, weight - step_rate * (ratio + decay * weight)


def optimize_body(where_ref, owned_ref, vector_ref, attend_ref, feed_a, feed_b, *refs):
    state, outs = refs[:21], refs[21:]
    vectors = jnp.concatenate([owned_ref[:2], vector_ref[2:]], axis=0)
    total = owned_ref[2:3, 0:1] + jnp.sum(vectors * vectors)
    norm = jnp.sqrt(total)
    factor = clip_norm / jnp.maximum(norm, clip_norm)
    outs[0][...] = norm
    width = state[0].shape[2]
    part = state[6].shape[1] // 3

    def update(param, at, gradient, step_rate):
        weight, first, second = (ref[at] for ref in state[3 * param : 3 * param + 3])
        results = adam_parts(weight, gradient, first, second, factor, step_rate)
        for ref, result in zip(outs[1 + 3 * param : 4 + 3 * param], results):
            ref[at] = result

    for index in range(3):
        update(0, (index,), attend_ref[:, index * width : (index + 1) * width], rate)
    update(1, (...,), attend_ref[:, 3 * width :].T, rate)
    split, rows = feed_a.shape[0], state[6].shape[0]
    for feed_ref, within in ((feed_a, slice(0, split)), (feed_b, slice(split, rows))):
        for index in range(3):
            at = (within, slice(index * part, (index + 1) * part))
            first = 2 * index * part
            update(2, at, feed_ref[:, first : first + part], rate)
            update(3, at, feed_ref[:, first + part : first + 2 * part], rate)
    update(4, (...,), vectors[:6], vector_rate)
    model = where_ref[2]
    head = jnp.zeros((2, width), f32)
    for index in range(4):
        head = head + jnp.where(model == index, vectors[6:8, index * width : (index + 1) * width], 0.0)
    update(5, (...,), head, vector_rate)
    bias = vector_ref[pl.ds(8 + model, 1), :]
    bias = jnp.concatenate([bias[:, at : at + 128] for at in range(0, bias.shape[1], 128)], axis=0)
    update(6, (...,), bias, vector_rate)


def bring_body(*refs):
    half = len(refs) // 2
    for source, target in zip(refs[:half], refs[half:]):
        target[...] = source[...]


def bring(arrays, after):
    return pl.pallas_call(
        lambda *refs: bring_body(*refs[: len(arrays)], *refs[len(arrays) + len(after) :]),
        in_specs=[NEAR] * len(arrays) + [LATER] * len(after),
        out_specs=[NEAR] * len(arrays),
        out_shape=[sds(array.shape, f32) for array in arrays],
        compiler_params=params(8),
        cost_estimate=cost(4e6, 6e6),
        name="bring",
    )(*from_far(*arrays), *after)


def last_sum_body(*refs):
    parts, (early_ref, late_ref, token_ref, total_ref, owned_ref) = refs[:-5], refs[-5:]
    total = sum(part[0].astype(f32) for part in parts)
    total_ref[...] = total
    squares = sum(jnp.sum(values * values) for values in (total, early_ref[...], late_ref[...]))
    owned_ref[:2, :] = token_ref[...]
    owned_ref[2:, :] = jnp.full((1, owned_ref.shape[1]), squares, f32)


def last_sum(parts, early_total, late_total, token_sums):
    _, rows, columns = parts[0].shape
    return pl.pallas_call(
        last_sum_body,
        in_specs=[NEAR] * (len(parts) + 3),
        out_specs=[NEAR] * 2,
        out_shape=[sds((rows, columns), f32), sds((3, columns), f32)],
        compiler_params=params(8),
        cost_estimate=cost(0, 0),
        name="last_sum",
    )(*parts, early_total, late_total, token_sums)


def optimize(where, owned, vector_total, attend_total, feed_totals, arrays):
    shapes = [sds(array.shape, f32) for array in arrays]
    return pl.pallas_call(
        optimize_body,
        in_specs=[pl.BlockSpec(memory_space=pltpu.SMEM)]
        + [pl.BlockSpec(memory_space=pltpu.VMEM)] * (5 + len(arrays)),
        out_shape=[sds((1, 1), f32)] + shapes,
        compiler_params=params(20),
        cost_estimate=cost(4e6, 8e6),
        name="optimize",
    )(where, owned, vector_total, attend_total, *feed_totals, *arrays)


def shards(
    tokens,
    cotangent,
    lengths,
    input_weight,
    output_weight,
    expand_weight,
    shrink_weight,
    layer_vectors,
    head_bias,
    expand_bias,
    first_input,
    first_output,
    first_expand,
    first_shrink,
    first_vectors,
    first_head,
    first_bias,
    second_input,
    second_output,
    second_expand,
    second_shrink,
    second_vectors,
    second_head,
    second_bias,
):
    dp_count = lax.axis_size("dp")
    mp_count = lax.axis_size("mp")
    cube = dp_count == 8 and mp_count == 4
    rows = input_weight.shape[0]
    width = input_weight.shape[2]
    hidden = expand_weight.shape[1]
    seq, depth = tokens.shape
    part = hidden // 3
    model_index = lax.axis_index("mp")
    me = lax.axis_index("dp") * mp_count + model_index

    attend_shard, feed_shard, bias_full = pack(
        input_weight.transpose(1, 0, 2),
        output_weight,
        expand_weight,
        shrink_weight.T,
        head_bias,
        expand_bias.reshape(hidden // 128, 128),
    )
    if cube:
        core, near = me & 1, model_index
        devices = jnp.arange(32).reshape(8, 4).T
        spots = jnp.concatenate(
            [place(devices ^ me, devices & 1, orders) for orders in (CORE_ORDERS, LATE_ORDERS)]
        ).astype(jnp.int32)
    else:
        core = near = jnp.zeros((), jnp.int32)
        spots = (jnp.arange(8)[:, None] % 4 // 2 * 8 + jnp.arange(8)[None]).astype(jnp.int32)
    where = jnp.stack([core, near, model_index]).astype(jnp.int32)

    def turned(array):
        return array.transpose(1, 0, 2)

    state = (
        (turned(input_weight), turned(first_input), turned(second_input)),
        (output_weight, first_output, second_output),
        (expand_weight, first_expand, second_expand),
        (shrink_weight.T, first_shrink.T, second_shrink.T),
        (layer_vectors, first_vectors, second_vectors),
        (head_bias, first_head, second_head),
        tuple(array.reshape(hidden // 128, 128) for array in (expand_bias, first_bias, second_bias)),
    )
    arrays = [array for group in state for array in group]

    if cube:
        split = rows * 2 // 3
        held, early, late = attend_shard[None], feed_shard[None, :split], feed_shard[None, split:]
        arrived, far_late = cube_permute(held, 0), cube_permute(late, 0, LATE_ORDERS)
        held, bias_full = lax.optimization_barrier((joined(held, arrived), bias_full))
        arrived = cube_permute(held, 1)
        bias_full = bias_full + bit_permute(bias_full, 0)
        normed, normed_t, upstream_t = prepare(tokens, cotangent, layer_vectors, (held,))
        late = joined(late, far_late)
        held, early, late, normed, bias_full, spots, where = lax.optimization_barrier(
            (held, early, late, normed, bias_full, spots, where)
        )
        held = joined(held, arrived)
        arrived, far_early = cube_permute(held, 2), cube_permute(early, 0)
        far_late = cube_permute(late, 1, LATE_ORDERS)
        bias_full = bias_full + bit_permute(bias_full, 1)
        held, early, late = joined(held, arrived), joined(early, far_early), joined(late, far_late)
        held, early, late, bias_full = lax.optimization_barrier((held, early, late, bias_full))
        far, far_early = cube_permute(held, 3), cube_permute(early, 1)
        twin = bit_permute(held, 0)
        early = joined(early, far_early)
        far, early, late = lax.optimization_barrier((far, early, late))
        attend_halves = (held, far, twin, bit_permute(far, 0))
        far_early, far_late = cube_permute(early, 2), cube_permute(late, 2, LATE_ORDERS)
        qkv, wide, wide_out = project(where, spots, normed, attend_halves, bias_full, ())
        far_early, far_late, qkv = lax.optimization_barrier((far_early, far_late, qkv))
        early, late = joined(early, far_early), joined(late, far_late)
        far_early, far_late = cube_permute(early, 3), cube_permute(late, 3, LATE_ORDERS)
        twin_early, twin_late = bit_permute(early, 0), bit_permute(late, 0)
        mixture, log_totals = attend_forward(where, lengths, qkv, (early, late))
        far_early, far_late, twin_late, mixture = lax.optimization_barrier(
            (far_early, far_late, twin_late, mixture)
        )
        last_early, last_late = bit_permute(far_early, 0), bit_permute(far_late, 0)
        middle, hidden_in, hidden_t, unit, inverse = attend_out(mixture, wide_out, tokens, layer_vectors)
        feed_halves = (early, far_early, twin_early, last_early, late, far_late, twin_late, last_late)
    else:

        def planes(shard):
            full = lax.all_gather(lax.all_gather(shard, "dp", axis=0, tiled=True), "mp", axis=0)
            full = full.reshape(2, 2, 8, depth // 8, shard.shape[1]).transpose(1, 0, 2, 3, 4)
            return tuple(full.reshape(4, 8, depth // 8, shard.shape[1]))

        normed, normed_t, upstream_t = prepare(tokens, cotangent, layer_vectors, ())
        bias_full = lax.psum(bias_full, "mp")
        qkv, wide, wide_out = project(where, spots, normed, planes(attend_shard), bias_full, ())
        mixture, log_totals = attend_forward(where, lengths, qkv, ())
        middle, hidden_in, hidden_t, unit, inverse = attend_out(mixture, wide_out, tokens, layer_vectors)
        split = depth // 8 * 2 // 3
        feed_planes = planes(feed_shard)
        feed_halves = tuple(array[:, :split] for array in feed_planes) + tuple(
            array[:, split:] for array in feed_planes
        )
    block_out, back, keep_early, send_early, keep_late, send_late, bias_grad = feed(
        where,
        spots,
        hidden_in,
        hidden_t,
        cotangent,
        upstream_t,
        feed_halves,
        bias_full,
        middle,
        layer_vectors,
    )
    middle_grad, mixture_grad, output_grad, middle_sums = middle_back(
        where, lengths, back, unit, inverse, cotangent, mixture, wide_out, layer_vectors
    )
    if cube:
        early = [keep_early, bit_permute(send_early, 0)]
        late = [keep_late, bit_permute(send_late, 0)]
        early[0], late[0], mixture_grad = lax.optimization_barrier((early[0], late[0], mixture_grad))
        away, far_away_late = leaving(early, 3), leaving(late, 3)
        packed_grad = attend_backward(
            where, lengths, qkv, mixture_grad, log_totals, (away, far_away_late)
        )
        early = staying(early, 3) + [cube_permute(away, 3)]
        late = staying(late, 3) + [cube_permute(far_away_late, 3, LATE_ORDERS)]
        early[0], late[0], packed_grad = lax.optimization_barrier((early[0], late[0], packed_grad))
        away, far_away_late = leaving(early, 2), leaving(late, 2)
        sums = (middle_sums, bias_grad)
        keep_attend, send_attend, rider = input_grad(
            where, spots, normed_t, packed_grad, output_grad, sums, 16, depth // 8, (away, far_away_late)
        )
        early = staying(early, 2) + [cube_permute(away, 2)]
        late = staying(late, 2) + [cube_permute(far_away_late, 2, LATE_ORDERS)]
        early[-1], late[-1], send_attend = lax.optimization_barrier((early[-1], late[-1], send_attend))
        twin_b, rider, _ = with_rider(send_attend[8:], rider, lambda values: bit_permute(values, 0))
        twin_a = bit_permute(send_attend[:8], 0)
        away = (keep_attend[8:].astype(f32) + twin_b.astype(f32)).astype(low)
        arrived, rider, message = with_rider(away, rider, lambda values: cube_permute(values, 3))
        attend_parts = [keep_attend[:8], twin_a, arrived]
        feed_away = leaving(early, 1)
        token_grad, token_sums = token_back(
            packed_grad, wide, tokens, middle_grad, layer_vectors, (message, feed_away)
        )
        early = staying(early, 1) + [cube_permute(feed_away, 1)]
        attend_parts[0], token_sums = lax.optimization_barrier((attend_parts[0], token_sums))
        away = leaving(attend_parts, 2)
        arrived, rider, message = with_rider(away, rider, lambda values: cube_permute(values, 2))
        attend_parts = staying(attend_parts, 2) + [arrived]
        message, early[0], late[0] = lax.optimization_barrier((message, early[0], late[0]))
        feed_away = leaving(early, 0)
        early = staying(early, 0) + [cube_permute(feed_away, 0)]
        feed_away = leaving(late, 1)
        away = leaving(attend_parts, 1)
        arrived, rider, message = with_rider(away, rider, lambda values: cube_permute(values, 1))
        late = staying(late, 1) + [cube_permute(feed_away, 1, LATE_ORDERS)]
        attend_parts = staying(attend_parts, 1) + [arrived]
        message, early[0] = lax.optimization_barrier((message, early[0]))
        early_total = summed(early)
        arrays = list(bring(arrays, (message,)))
        attend_parts[0], arrays[0] = lax.optimization_barrier((attend_parts[0], arrays[0]))
        feed_away = leaving(late, 0)
        away = leaving(attend_parts, 0)
        away, early_total = lax.optimization_barrier((away, early_total))
        arrived, vector_total, _ = with_rider(away, rider, lambda values: cube_permute(values, 0))
        late = staying(late, 0) + [cube_permute(feed_away, 0, LATE_ORDERS)]
        attend_parts = staying(attend_parts, 0) + [arrived]
        late_total = summed(late)
        feed_totals = (early_total, late_total)
        attend_total, owned = last_sum(attend_parts, early_total, late_total, token_sums)
        owned = cube_sum(owned)
    else:
        packed_grad = attend_backward(where, lengths, qkv, mixture_grad, log_totals, ())
        sums = (middle_sums, bias_grad)
        keep_attend, send_attend, vector_total = input_grad(
            where, spots, normed_t, packed_grad, output_grad, sums, 16, depth // 8, ()
        )
        token_grad, token_sums = token_back(packed_grad, wide, tokens, middle_grad, layer_vectors, ())
        vector_total = lax.psum(vector_total, ("dp", "mp"))

    if not cube:

        def own_block(keep, send):
            full = jnp.stack([keep, send]).reshape(2, 2, 8, keep.shape[1], keep.shape[2])
            full = full.transpose(1, 0, 2, 3, 4).reshape(4, 8 * keep.shape[1], keep.shape[2])
            full = lax.psum_scatter(full, "mp", scatter_dimension=0, tiled=False)
            return lax.psum(full, "dp")

        def own_rows(*blocks):
            full = jnp.concatenate([block.reshape(8, -1, block.shape[1]) for block in blocks], axis=1)
            full = full.reshape(depth, full.shape[2]).astype(f32)
            return lax.dynamic_slice_in_dim(full, lax.axis_index("dp") * rows, rows, 0)

        attend_total = own_rows(own_block(keep_attend, send_attend))
        feed_total = own_rows(own_block(keep_early, send_early), own_block(keep_late, send_late))
        feed_totals = feed_total[: rows * 2 // 3], feed_total[rows * 2 // 3 :]
        attend_total, owned = last_sum((attend_total[None],), *feed_totals, token_sums)
        owned = lax.psum(owned, ("dp", "mp"))
    grad_norm, *updates = optimize(where, owned, vector_total, attend_total, feed_totals, arrays)
    grad_norm = grad_norm[0, 0]
    moment_input, square_input, updated_input = (turned(array) for array in updates[:3])
    moment_output, square_output, updated_output = updates[3:6]
    moment_expand, square_expand, updated_expand = updates[6:9]
    moment_shrink, square_shrink, updated_shrink = (array.T for array in updates[9:12])
    moment_vectors, square_vectors, updated_vectors = updates[12:15]
    moment_head, square_head, updated_head = updates[15:18]
    moment_bias, square_bias, updated_bias = (array.reshape(hidden) for array in updates[18:])
    return (
        block_out,
        token_grad,
        grad_norm,
        moment_input,
        square_input,
        updated_input,
        moment_output,
        square_output,
        updated_output,
        moment_expand,
        square_expand,
        updated_expand,
        moment_shrink,
        square_shrink,
        updated_shrink,
        moment_vectors,
        square_vectors,
        updated_vectors,
        moment_head,
        square_head,
        updated_head,
        moment_bias,
        square_bias,
        updated_bias,
    )


def solution(mesh):
    in_specs = (
        P(("dp", "mp"), None),
        P(("dp", "mp"), None),
        P("dp"),
        P("dp", None, "mp"),
        P("mp", "dp"),
        P("dp", "mp"),
        P("mp", "dp"),
        P(),
        P(None, "mp"),
        P("mp"),
        P("dp", None, "mp"),
        P("mp", "dp"),
        P("dp", "mp"),
        P("mp", "dp"),
        P(),
        P(None, "mp"),
        P("mp"),
        P("dp", None, "mp"),
        P("mp", "dp"),
        P("dp", "mp"),
        P("mp", "dp"),
        P(),
        P(None, "mp"),
        P("mp"),
    )
    out_specs = (
        P(("dp", "mp"), None),
        P(("dp", "mp"), None),
        P(),
        P("dp", None, "mp"),
        P("dp", None, "mp"),
        P("dp", None, "mp"),
        P("mp", "dp"),
        P("mp", "dp"),
        P("mp", "dp"),
        P("dp", "mp"),
        P("dp", "mp"),
        P("dp", "mp"),
        P("mp", "dp"),
        P("mp", "dp"),
        P("mp", "dp"),
        P(),
        P(),
        P(),
        P(None, "mp"),
        P(None, "mp"),
        P(None, "mp"),
        P("mp"),
        P("mp"),
        P("mp"),
    )
    return jax.shard_map(shards, mesh=mesh, in_specs=in_specs, out_specs=out_specs, check_vma=False)
```

```python
import functools
import jax
import jax.numpy as jnp
from jax import lax
from jax.experimental import pallas as pl
from jax.experimental.pallas import tpu as pltpu
from jax.sharding import PartitionSpec as P

HEAD_DIM = 64
TILE = 256
STEP = 10

eps_norm = 1e-05
clip_norm = 1.0
beta_one = 0.9
beta_two = 0.999
adam_eps = 1e-08
rate = 0.05
vector_rate = 0.5
decay = 0.01
excluded = -1e30
low = jnp.bfloat16
f32 = jnp.float32
GELU_A = 0.7978845608028654
GELU_B = GELU_A * 0.044715


def params(limit_mib, **kw):
    return pltpu.CompilerParams(vmem_limit_bytes=limit_mib * 1024 * 1024, **kw)


def cost(flops, moved, special=0):
    return pl.CostEstimate(flops=int(flops), bytes_accessed=int(moved), transcendentals=int(special))


def mm(a, b):
    return jnp.dot(a, b, preferred_element_type=f32)


def mm_nt(a, b):
    return lax.dot_general(a, b, (((1,), (1,)), ((), ())), preferred_element_type=f32)


def whole(shape):
    zeros = (0,) * len(shape)
    return pl.BlockSpec(shape, lambda *_: zeros)


def once(shape):
    zeros = (0,) * len(shape)
    return pl.BlockSpec(shape, lambda *_: zeros, pipeline_mode=pl.Buffered(1))


def held_back(body, first, count):
    def run(*refs):
        return body(*refs[:first], *refs[first + count :])

    return run


LATER = pl.BlockSpec(memory_space=pl.ANY)


def far_away(shape, dtype):
    return pltpu.HBM(shape, dtype)


def from_far(*arrays):
    return [pltpu.with_memory_space_constraint(array, pltpu.HBM) for array in arrays]


def sds(shape, dtype):
    return jax.ShapeDtypeStruct(shape, dtype)


def live_blocks(length, count, body):
    for blocks in range(1, count + 1):
        low_end = (blocks - 1) * TILE
        high_end = blocks * TILE
        @pl.when((length > low_end) & (length <= high_end))
        def _(blocks=blocks):
            body(length, blocks)


PAIR = 2 * HEAD_DIM


def span(block):
    return slice(block * TILE, (block + 1) * TILE)


def both_heads(values):
    lane = lax.broadcasted_iota(jnp.int32, values.shape, 1)
    none = jnp.zeros_like(values)
    return jnp.concatenate(
        [jnp.where(lane < HEAD_DIM, values, none), jnp.where(lane >= HEAD_DIM, values, none)], axis=0
    )


def causal_mask():
    key_id = lax.broadcasted_iota(jnp.int32, (TILE, 2 * TILE), 0)
    query_id = lax.broadcasted_iota(jnp.int32, (TILE, 2 * TILE), 1) & (TILE - 1)
    return key_id <= query_id


def forward_body(where_ref, lengths_ref, q_ref, k_ref, v_ref, o_ref, lse_ref, vt_ref):
    seq = q_ref.shape[0]
    vt_ref[...] = v_ref[...].T
    causal = causal_mask()

    def run(length, blocks):
        def scores(b):
            q = q_ref[span(b), :] * jnp.asarray(HEAD_DIM**-0.5, low)
            return mm_nt(k_ref[: (b + 1) * TILE, :], both_heads(q))

        now = scores(0)
        for b in range(blocks):
            start, stop = b * TILE, (b + 1) * TILE
            later = scores(b + 1) if b + 1 < blocks else None
            last = jnp.where(causal, now[start:, :], excluded)
            top = jnp.max(last, axis=0, keepdims=True)
            if b:
                top = jnp.maximum(top, jnp.max(now[:start], axis=0, keepdims=True))
            p = jnp.exp(last - top)
            total = jnp.sum(p, axis=0, keepdims=True)
            pb = p.astype(low)
            if b:
                pf = jnp.exp(now[:start] - top)
                total = total + jnp.sum(pf, axis=0, keepdims=True)
                pb = jnp.concatenate([pf.astype(low), pb], axis=0)
            inverse = 1.0 / total
            lse = top + jnp.log(total)
            outs = []
            for h in range(2):
                at = slice(h * TILE, (h + 1) * TILE)
                out = mm(vt_ref[h * HEAD_DIM : (h + 1) * HEAD_DIM, :stop], pb[:, at])
                outs.append(out * inverse[:, at])
                lse_ref[0, h : h + 1, start:stop] = lse[:, at]
            both = jnp.concatenate(outs, axis=0).T
            row = start + lax.broadcasted_iota(jnp.int32, both.shape, 0)
            o_ref[start:stop, :] = jnp.where(row < length, both, 0.0).astype(low)
            now = later
        if blocks * TILE < seq:
            o_ref[blocks * TILE :, :] = jnp.zeros((seq - blocks * TILE, PAIR), low)
            lse_ref[0, :, blocks * TILE :] = jnp.zeros((2, seq - blocks * TILE), f32)

    live_blocks(lengths_ref[where_ref[2]], seq // TILE, run)


def attend_forward(where, lengths, qkv, after):
    seq, width = qkv.shape[0], qkv.shape[1] // 3
    pair = 2 * HEAD_DIM
    pairs = width // pair
    half = seq * seq * 5 // 8
    spec = lambda part: pl.BlockSpec((seq, pair), lambda i, *_: (0, part * pairs + i))
    return pl.pallas_call(
        held_back(forward_body, 5, len(after)),
        grid_spec=pltpu.PrefetchScalarGridSpec(
            num_scalar_prefetch=2,
            grid=(pairs,),
            in_specs=[spec(0), spec(1), spec(2)] + [LATER] * len(after),
            out_specs=[
                pl.BlockSpec((seq, pair), lambda i, *_: (0, i)),
                pl.BlockSpec((1, 2, seq), lambda i, *_: (i, 0, 0)),
            ],
            scratch_shapes=[pltpu.VMEM((pair, seq), low)],
        ),
        out_shape=[sds((seq, width), low), far_away((pairs, 2, seq), f32)],
        compiler_params=params(20),
        cost_estimate=cost(pairs * 2 * half * 2 * 2 * 256, seq * width * 8, pairs * 2 * half),
        name="attend_forward",
    )(where, lengths, *from_far(qkv, qkv, qkv), *after)


def backward_body(where_ref, lengths_ref, q_ref, k_ref, v_ref, do_ref, lse_ref, out_ref, kt_ref, ksum, vsum):
    seq = q_ref.shape[0]
    scale = HEAD_DIM**-0.5
    kt_ref[...] = k_ref[...].T
    causal = causal_mask()

    def run(length, blocks):
        def scores(b):
            qq = both_heads(q_ref[span(b), :] * jnp.asarray(scale, low))
            uu = both_heads(do_ref[span(b), :])
            stop = (b + 1) * TILE
            return qq, uu, mm_nt(k_ref[:stop, :], qq), mm_nt(v_ref[:stop, :], uu)

        now = scores(blocks - 1)
        for b in reversed(range(blocks)):
            start, stop = b * TILE, (b + 1) * TILE
            later = scores(b - 1) if b else None
            qq, uu, s, dp = now
            lse = jnp.concatenate([lse_ref[0, 0:1, start:stop], lse_ref[0, 1:2, start:stop]], axis=1)
            p = jnp.exp(jnp.where(causal, s[start:], excluded) - lse)
            inner = jnp.sum(p * dp[start:], axis=0, keepdims=True)
            if b:
                pf = jnp.exp(s[:start] - lse)
                inner = inner + jnp.sum(pf * dp[:start], axis=0, keepdims=True)
            ds = (p * (dp[start:] - inner)).astype(low)
            pb = p.astype(low)
            if b:
                ds = jnp.concatenate([(pf * (dp[:start] - inner)).astype(low), ds], axis=0)
                pb = jnp.concatenate([pf.astype(low), pb], axis=0)
            dk, dv = mm(ds, qq), mm(pb, uu)
            if b == blocks - 1:
                ksum[:stop, :] = dk
                vsum[:stop, :] = dv
            else:
                ksum[:stop, :] += dk
                vsum[:stop, :] += dv
            dq = jnp.concatenate(
                [
                    mm(
                        kt_ref[h * HEAD_DIM : (h + 1) * HEAD_DIM, :stop],
                        ds[:, h * TILE : (h + 1) * TILE],
                    )
                    for h in range(2)
                ],
                axis=0,
            )
            out_ref[1, start:stop, :] = ksum[start:stop, :].astype(low)
            out_ref[2, start:stop, :] = vsum[start:stop, :].astype(low)
            out_ref[0, start:stop, :] = (dq.T * scale).astype(low)
            now = later
        if blocks * TILE < seq:
            rest = jnp.zeros((seq - blocks * TILE, PAIR), low)
            for part in range(3):
                out_ref[part, blocks * TILE :, :] = rest

    live_blocks(lengths_ref[where_ref[2]], seq // TILE, run)


def attend_backward(where, lengths, qkv, upstream, lse, after):
    seq, width = upstream.shape
    pair = 2 * HEAD_DIM
    pairs = width // pair
    half = seq * seq * 5 // 8
    spec = lambda part: pl.BlockSpec((seq, pair), lambda i, *_: (0, part * pairs + i))
    own = pl.BlockSpec((seq, pair), lambda i, *_: (0, i))
    return pl.pallas_call(
        held_back(backward_body, 7, len(after)),
        grid_spec=pltpu.PrefetchScalarGridSpec(
            num_scalar_prefetch=2,
            grid=(pairs,),
            in_specs=[spec(0), spec(1), spec(2), own, pl.BlockSpec((1, 2, seq), lambda i, *_: (i, 0, 0))]
            + [LATER] * len(after),
            out_specs=pl.BlockSpec((3, seq, pair), lambda i, *_: (0, 0, i)),
            scratch_shapes=[
                pltpu.VMEM((pair, seq), low),
                pltpu.VMEM((seq, pair), f32),
                pltpu.VMEM((seq, pair), f32),
            ],
        ),
        out_shape=sds((3, seq, width), low),
        compiler_params=params(28),
        cost_estimate=cost(pairs * 2 * half * 5 * 2 * 256, seq * width * 14, pairs * 2 * half),
        name="attend_backward",
    )(where, lengths, *from_far(qkv, qkv, qkv), upstream, *from_far(lse), *after)


def normalize(values):
    average = jnp.mean(values, axis=-1, keepdims=True)
    centred = values - average
    inverse = lax.rsqrt(jnp.mean(centred * centred, axis=-1, keepdims=True) + eps_norm)
    return centred * inverse, inverse


def pull_norm(scaled, unit, inverse):
    first = jnp.mean(scaled, axis=-1, keepdims=True)
    second = jnp.mean(scaled * unit, axis=-1, keepdims=True)
    return inverse * (scaled - first - unit * second)


def columns_of(values):
    return jnp.sum(values, axis=0, keepdims=True)


def pack_body(
    input_ref, output_ref, expand_ref, shrink_ref, head_ref, hidden_ref, attend_ref, feed_ref, bias_ref
):
    width = input_ref.shape[2]
    part = expand_ref.shape[1] // 3
    for index in range(3):
        attend_ref[:, index * width : (index + 1) * width] = input_ref[index].astype(low)
        at = slice(index * part, (index + 1) * part)
        feed_ref[:, 2 * index * part : (2 * index + 1) * part] = expand_ref[:, at].astype(low)
        feed_ref[:, (2 * index + 1) * part : (2 * index + 2) * part] = shrink_ref[:, at].astype(low)
    attend_ref[:, 3 * width :] = output_ref[...].T.astype(low)
    pieces = [head_ref[0:1, :], head_ref[1:2, :]]
    pieces += [hidden_ref[row : row + 1, :] for row in range(hidden_ref.shape[0])]
    bias_ref[...] = jnp.zeros_like(bias_ref)
    bias_ref[pl.ds(lax.axis_index("mp"), 1), :] = jnp.concatenate(pieces, axis=1)


def pack(input_weight, output_weight, expand, shrink, head_bias, hidden_bias):
    rows, width = input_weight.shape[1:]
    hidden = expand.shape[1]
    return pl.pallas_call(
        pack_body,
        out_shape=[
            sds((rows, 4 * width), low),
            sds((rows, 2 * hidden), low),
            sds((4, 2 * width + hidden), f32),
        ],
        compiler_params=params(6),
        cost_estimate=cost(rows * hidden, rows * hidden * 18),
        name="pack",
    )(*from_far(input_weight, output_weight, expand, shrink, head_bias, hidden_bias))


def prepare_body(x_ref, up_ref, vec_ref, h_ref, ht_ref, upt_ref):
    unit, _ = normalize(x_ref[...].astype(f32))
    h = (unit * vec_ref[0:1, :] + vec_ref[1:2, :]).astype(low)
    h_ref[...] = h
    ht_ref[...] = h.T
    upt_ref[...] = up_ref[...].T


def prepare(x, up, vectors, after):
    seq, depth = x.shape
    rows = pl.BlockSpec((2 * TILE, depth), lambda i: (i, 0))
    turned = pl.BlockSpec((depth, 2 * TILE), lambda i: (0, i))
    return pl.pallas_call(
        held_back(prepare_body, 3, len(after)),
        grid=(seq // (2 * TILE),),
        in_specs=[rows, rows, once(vectors.shape)] + [LATER] * len(after),
        out_specs=[rows, turned, turned],
        out_shape=[sds((seq, depth), low), far_away((depth, seq), low), far_away((depth, seq), low)],
        compiler_params=params(16),
        cost_estimate=cost(seq * depth * 10, seq * depth * 10),
        name="prepare",
    )(*from_far(x, up), vectors, *after)


def slot(halves, spot, at):
    first, second = halves
    inner = spot & 7
    return jnp.where(spot < 8, first[inner, :, at], second[inner, :, at])


def project_body(
    where_ref, spots_ref, h_ref, mine_a, mine_b, twin_a, twin_b, bias_ref, qkv_ref, wide_ref, last_ref
):
    part = pl.program_id(0)
    rows = mine_a.shape[1]
    width = mine_a.shape[2] // 4
    groups = wide_ref.shape[1] // rows

    def collect(sources, index):
        columns = slice(index * width, (index + 1) * width)
        for group in range(groups):
            pieces = [slot(sources[model % 2], spots_ref[model, group], columns) for model in range(4)]
            at = slice(group * rows, (group + 1) * rows)
            if index < 3:
                wide_ref[0, at, :] = jnp.concatenate(pieces, axis=1)
            else:
                last_ref[at, :] = jnp.concatenate(pieces, axis=1)

    for index in range(4):
        for core in range(2):

            @pl.when((part == index) & (where_ref[0] == core))
            def _(index=index, core=core):
                mine, twin = (mine_a, mine_b), (twin_a, twin_b)
                collect((mine, twin) if core == 0 else (twin, mine), index)

    for index in range(3):

        @pl.when(part == index)
        def _(index=index):
            out = mm(h_ref[...], wide_ref[0])
            if index != 1:
                at = slice(index // 2 * width, (index // 2 + 1) * width)
                bias = jnp.concatenate([bias_ref[model : model + 1, at] for model in range(4)], axis=1)
                out = out + bias
            qkv_ref[...] = out.astype(low)


def project(where, spots, h, halves, bias, after):
    seq, depth = h.shape
    return pl.pallas_call(
        held_back(project_body, 8, len(after)),
        grid_spec=pltpu.PrefetchScalarGridSpec(
            num_scalar_prefetch=2,
            grid=(4,),
            in_specs=[
                once((seq, depth)),
                *[once(halves[0].shape)] * 4,
                once(bias.shape),
            ]
            + [LATER] * len(after),
            out_specs=[
                pl.BlockSpec((seq, depth), lambda i, *_: (0, jnp.minimum(i, 2))),
                pl.BlockSpec((1, depth, depth), lambda i, *_: (jnp.minimum(i, 2), 0, 0)),
                whole((depth, depth)),
            ],
        ),
        out_shape=[
            far_away((seq, 3 * depth), low),
            far_away((3, depth, depth), low),
            sds((depth, depth), low),
        ],
        compiler_params=params(24),
        cost_estimate=cost(2 * seq * depth * depth * 3, seq * depth * 16),
        name="project",
    )(where, spots, h, *halves, bias, *after)


NEAR = pl.BlockSpec(memory_space=pltpu.VMEM)
SCALARS = pl.BlockSpec(memory_space=pltpu.SMEM)


def attend_out_body(o_ref, w_ref, x_ref, vec_ref, middle_ref, h_ref, ht_ref, unit_ref, inverse_ref):
    for tile in range(o_ref.shape[0] // TILE):
        at = slice(tile * TILE, (tile + 1) * TILE)
        middle = x_ref[at, :].astype(f32) + mm_nt(o_ref[at, :], w_ref[...]) + vec_ref[4:5, :]
        middle_ref[at, :] = middle.astype(low)
        unit, inverse = normalize(middle)
        unit_ref[at, :] = unit.astype(low)
        inverse_ref[at, :] = jnp.broadcast_to(inverse, (TILE, inverse_ref.shape[1]))
        h = (unit * vec_ref[2:3, :] + vec_ref[3:4, :]).astype(low)
        h_ref[at, :] = h
        ht_ref[:, at] = h.T


def attend_out(o, wide_out, x, vectors):
    seq, depth = x.shape
    return pl.pallas_call(
        attend_out_body,
        in_specs=[NEAR] * 4,
        out_specs=[NEAR] * 5,
        out_shape=[
            sds((seq, depth), low),
            sds((seq, depth), low),
            sds((depth, seq), low),
            sds((seq, depth), low),
            sds((seq, 128), f32),
        ],
        compiler_params=params(10),
        cost_estimate=cost(2 * seq * depth * depth, seq * depth * 14),
        name="attend_out",
    )(o, wide_out, x, vectors)


def feed_body(
    where_ref,
    spots_ref,
    h2_ref,
    h2t_ref,
    up_ref,
    upt_ref,
    mine_a,
    mine_b,
    twin_a,
    twin_b,
    mine_c,
    mine_d,
    twin_c,
    twin_d,
    bias_ref,
    middle_ref,
    vec_ref,
    block_ref,
    back_ref,
    keep_a,
    send_a,
    keep_b,
    send_b,
    bias_grad_ref,
    out_ref,
    sum_ref,
    wide_ref,
    act_ref,
    pre_ref,
):
    part = mine_a.shape[2] // 6
    groups = spots_ref.shape[1]
    rows = wide_ref.shape[0] // groups
    split = mine_a.shape[1]
    skip = bias_ref.shape[1] - bias_grad_ref.shape[1]
    pieces = (
        ((mine_a, mine_b), (twin_a, twin_b), keep_a, send_a, 0, slice(0, split)),
        ((mine_c, mine_d), (twin_c, twin_d), keep_b, send_b, 4, slice(split, rows)),
    )
    out_ref[...] = middle_ref[...].astype(f32) + vec_ref[5:6, :]
    sum_ref[...] = jnp.zeros_like(sum_ref)

    def step(index, carry):
        side = lax.rem(index, 2)
        first = pl.multiple_of(index // 2 * part, 128)
        lanes = pl.ds(pl.multiple_of(2 * first, 128), part)
        next_lanes = pl.ds(pl.multiple_of(2 * first + part, 128), part)
        models = [where_ref[1] ^ (2 * side + core) for core in range(2)]
        for group in range(groups):
            for mine, twin, _, _, table, within in pieces:
                at = slice(group * rows + within.start, group * rows + within.stop)
                for core, halves in enumerate((mine, twin)):
                    spot = spots_ref[table + models[core], group]
                    wide_ref[at, core * part : (core + 1) * part] = slot(halves, spot, lanes)
                    wide_ref[at, (2 + core) * part : (3 + core) * part] = slot(halves, spot, next_lanes)

        expand = wide_ref[:, : 2 * part]
        shrink = wide_ref[:, 2 * part :]
        bias = jnp.concatenate(
            [bias_ref[pl.ds(model, 1), pl.ds(pl.multiple_of(skip + first, 128), part)] for model in models],
            axis=1,
        )
        sums = jnp.zeros((1, 2 * part), f32)
        for tile in range(h2_ref.shape[0] // TILE):
            at = slice(tile * TILE, (tile + 1) * TILE)
            u = mm(h2_ref[at, :], expand) + bias
            square = u * u
            th = jnp.tanh(u * (GELU_A + GELU_B * square))
            gate = 0.5 * th + 0.5
            slope = gate + (gate * (1.0 - gate)) * (u * (2.0 * GELU_A + (6.0 * GELU_B) * square))
            pre = (mm(up_ref[at, :], shrink) * slope).astype(low)
            act_ref[at, :] = (u * gate).astype(low)
            pre_ref[at, :] = pre
            sums = sums + columns_of(pre.astype(f32))
        for core, model in enumerate(models):
            bias_grad_ref[pl.ds(model, 1), pl.ds(first, part)] = sums[:, core * part : (core + 1) * part]
        out_ref[...] += mm_nt(act_ref[...], shrink)
        sum_ref[...] += mm_nt(pre_ref[...], expand)
        grad_expand = mm(h2t_ref[...], pre_ref[...]).astype(low)
        grad_shrink = mm(upt_ref[...], act_ref[...]).astype(low)
        for group in range(groups):
            for _, _, keep, send, table, within in pieces:
                at = slice(group * rows + within.start, group * rows + within.stop)
                for core, target in enumerate((keep, send)):
                    spot = spots_ref[table + models[core], group]
                    columns = slice(core * part, (core + 1) * part)
                    target[spot, :, lanes] = grad_expand[at, columns]
                    target[spot, :, next_lanes] = grad_shrink[at, columns]
        return carry

    lax.fori_loop(0, 6, step, 0)
    block_ref[...] = out_ref[...].astype(low)
    back_ref[...] = sum_ref[...].astype(low)


def feed(where, spots, h2, h2t, up, upt, halves, bias, middle, vectors):
    seq, depth = h2.shape
    half, _, columns = halves[0].shape
    part = columns // 6
    splits = [halves[0].shape[1], halves[4].shape[1]]
    return pl.pallas_call(
        feed_body,
        in_specs=[SCALARS] * 2 + [NEAR] * 15,
        out_specs=[NEAR] * 7,
        scratch_shapes=[
            pltpu.VMEM((seq, depth), f32),
            pltpu.VMEM((seq, depth), f32),
            pltpu.VMEM((depth, 4 * part), low),
            pltpu.VMEM((seq, 2 * part), low),
            pltpu.VMEM((seq, 2 * part), low),
        ],
        out_shape=[sds((seq, depth), low)] * 2
        + [sds((2 * half, rows, columns), low) for rows in splits for _ in range(2)]
        + [sds((4, 3 * part), f32)],
        compiler_params=params(22),
        cost_estimate=cost(12 * seq * depth * 12 * part, seq * depth * 40, seq * 6 * part),
        name="feed",
    )(where, spots, h2, h2t, up, upt, *halves, bias, middle, vectors)


def middle_back_body(
    where_ref,
    lengths_ref,
    back_ref,
    unit_ref,
    inverse_ref,
    up_ref,
    o_ref,
    w_ref,
    vec_ref,
    grad_ref,
    mixture_ref,
    weight_ref,
    sums_ref,
    turned_ref,
):
    length = lengths_ref[where_ref[2]]
    sums = jnp.zeros(sums_ref.shape, f32)
    for tile in range(back_ref.shape[0] // TILE):
        at = slice(tile * TILE, (tile + 1) * TILE)
        unit, inverse = unit_ref[at, :].astype(f32), inverse_ref[at, 0:1]
        back = back_ref[at, :].astype(f32)
        up = up_ref[at, :].astype(f32)
        grad = up + pull_norm(back * vec_ref[2:3, :], unit, inverse)
        rounded = grad.astype(low)
        grad_ref[at, :] = rounded
        turned_ref[:, at] = rounded.T
        row = tile * TILE + lax.broadcasted_iota(jnp.int32, grad.shape, 0)
        mixture_ref[at, :] = jnp.where(row < length, mm(rounded, w_ref[...]), 0.0).astype(low)
        sums = sums + jnp.concatenate(
            [columns_of(back * unit), columns_of(back), columns_of(grad), columns_of(up)], axis=0
        )
    sums_ref[...] = sums
    weight_ref[...] = mm(turned_ref[...], o_ref[...]).astype(low)


def middle_back(where, lengths, back, unit, inverse, up, o, wide_out, vectors):
    seq, depth = unit.shape
    return pl.pallas_call(
        middle_back_body,
        in_specs=[SCALARS] * 2 + [NEAR] * 7,
        out_specs=[NEAR] * 4,
        scratch_shapes=[pltpu.VMEM((depth, seq), low)],
        out_shape=[
            sds((seq, depth), low),
            sds((seq, depth), low),
            sds((depth, depth), low),
            sds((4, depth), f32),
        ],
        compiler_params=params(14),
        cost_estimate=cost(4 * seq * depth * depth, seq * depth * 28),
        name="middle_back",
    )(where, lengths, back, unit, inverse, up, o, wide_out, vectors)


def input_grad_body(
    where_ref,
    spots_ref,
    ht_ref,
    back_ref,
    out_grad_ref,
    middle_ref,
    bias_ref,
    keep_ref,
    send_ref,
    sums_ref,
):
    rows = keep_ref.shape[1]
    width = keep_ref.shape[2] // 4
    groups = ht_ref.shape[0] // rows

    def spread(targets, index, grad):
        at = slice(index * width, (index + 1) * width)
        for group in range(groups):
            for model in range(4):
                targets[model % 2][spots_ref[model, group], :, at] = grad[
                    group * rows : (group + 1) * rows, model * width : (model + 1) * width
                ]

    sums_ref[:2] = jnp.zeros((2, sums_ref.shape[1]), f32)
    sums_ref[2:6] = middle_ref[...]
    sums_ref[6:7] = columns_of(back_ref[0].astype(f32))
    sums_ref[7:8] = columns_of(back_ref[2].astype(f32))
    sums_ref[8:] = bias_ref[...]
    for index in range(4):
        grad = mm(ht_ref[...], back_ref[index]).astype(low) if index < 3 else out_grad_ref[...]
        for core in range(2):

            @pl.when(where_ref[0] == core)
            def _(core=core, index=index, grad=grad):
                spread((keep_ref, send_ref) if core == 0 else (send_ref, keep_ref), index, grad)


def input_grad(where, spots, ht, back, out_grad, sums, slots, rows, after):
    depth, seq = ht.shape
    shape = (slots, rows, depth)
    return pl.pallas_call(
        held_back(input_grad_body, 7, len(after)),
        in_specs=[SCALARS] * 2 + [NEAR] * 5 + [LATER] * len(after),
        out_specs=[NEAR] * 3,
        out_shape=[sds(shape, low), sds(shape, low), sds((12, depth), f32)],
        compiler_params=params(14),
        cost_estimate=cost(6 * seq * depth * depth, seq * depth * 14),
        name="input_grad",
    )(where, spots, ht, back, out_grad, *sums, *after)


def token_back_body(
    back_ref, w_ref, x_ref, grad_ref, vec_ref, token_ref, sums_ref
):
    step = pl.program_id(0)
    back = mm_nt(back_ref[0], w_ref[0]) + mm_nt(back_ref[1], w_ref[1]) + mm_nt(back_ref[2], w_ref[2])
    unit, inverse = normalize(x_ref[...].astype(f32))
    grad = grad_ref[...].astype(f32)
    token_ref[...] = (grad + pull_norm(back * vec_ref[0:1, :], unit, inverse)).astype(low)
    sums = jnp.concatenate([columns_of(back * unit), columns_of(back)], axis=0)

    @pl.when(step == 0)
    def _():
        sums_ref[...] = sums

    @pl.when(step > 0)
    def _():
        sums_ref[...] += sums


def token_back(back, wide, x, grad, vectors, after):
    seq, depth = x.shape
    rows = pl.BlockSpec((TILE, depth), lambda i: (i, 0))
    return pl.pallas_call(
        held_back(token_back_body, 5, len(after)),
        grid=(seq // TILE,),
        in_specs=[
            pl.BlockSpec((3, TILE, depth), lambda i: (0, i, 0)),
            pl.BlockSpec((3, depth, depth), lambda i: (0, 0, 0)),
            rows,
            rows,
            once(vectors.shape),
        ]
        + [LATER] * len(after),
        out_specs=[rows, whole((2, depth))],
        out_shape=[sds((seq, depth), low), sds((2, depth), f32)],
        compiler_params=params(24),
        cost_estimate=cost(6 * seq * depth * depth, seq * depth * 16),
        name="token_back",
    )(back, *from_far(wide, x), grad, vectors, *after)


CORE_ORDERS = ((4, 3, 2, 1), (3, 4, 1, 2))
LATE_ORDERS = ((2, 1, 4, 3), (1, 2, 3, 4))
STAGES = 4


def cube_permute(values, stage, orders=CORE_ORDERS):
    pairs = [(device, device ^ (1 << orders[device & 1][stage])) for device in range(32)]
    return lax.ppermute(values, ("dp", "mp"), pairs)


def bit_permute(values, bit):
    return lax.ppermute(values, ("dp", "mp"), [(device, device ^ (1 << bit)) for device in range(32)])


def place(distance, core, orders):
    spots = [
        sum(((distance >> bit) & 1) << step for step, bit in enumerate(order)) for order in orders
    ]
    return jnp.where(core == 0, spots[0], spots[1])


def joined(held, arrived):
    return jnp.concatenate([held, arrived], axis=0)


def leaving(parts, stage):
    half = 1 << stage
    return sum(part[half:].astype(f32) for part in parts).astype(low)


def staying(parts, stage):
    return [part[: 1 << stage] for part in parts]


def summed(parts):
    return sum(part[0].astype(f32) for part in parts)


def two_parts(values):
    high = lax.reduce_precision(values, 8, 7)
    rest = lax.reduce_precision(values - high, 8, 7)
    return jnp.concatenate([high, rest], axis=0).astype(low)


def one_part(parts):
    half = parts.shape[0] // 2
    return parts[:half].astype(f32) + parts[half:].astype(f32)


def with_rider(blocks, rider, send):
    count, rows, columns = blocks.shape
    parts = two_parts(rider)
    message = jnp.concatenate([blocks.reshape(count * rows, columns), parts], axis=0)
    arrived = send(message)
    total = one_part(parts) + one_part(arrived[count * rows :])
    return arrived[: count * rows].reshape(count, rows, columns), total, message


def cube_sum(values, bits=range(5)):
    for bit in bits:
        values = values + bit_permute(values, bit)
    return values


def adam_parts(weight, gradient, first_old, second_old, factor, step_rate):
    scaled = gradient * factor
    moment = beta_one * first_old + (1.0 - beta_one) * scaled
    square = beta_two * second_old + (1.0 - beta_two) * scaled * scaled
    spread = jnp.sqrt(square * (1.0 / (1.0 - beta_two**STEP)))
    ratio = moment * (1.0 / (1.0 - beta_one**STEP)) / (spread + adam_eps)
    return moment, square, weight - step_rate * (ratio + decay * weight)


def optimize_body(where_ref, owned_ref, vector_ref, attend_ref, feed_a, feed_b, *refs):
    state, outs = refs[:21], refs[21:]
    vectors = jnp.concatenate([owned_ref[:2], vector_ref[2:]], axis=0)
    total = owned_ref[2:3, 0:1] + jnp.sum(vectors * vectors)
    norm = jnp.sqrt(total)
    factor = clip_norm / jnp.maximum(norm, clip_norm)
    outs[0][...] = norm
    width = state[0].shape[2]
    part = state[6].shape[1] // 3

    def update(param, at, gradient, step_rate):
        weight, first, second = (ref[at] for ref in state[3 * param : 3 * param + 3])
        results = adam_parts(weight, gradient, first, second, factor, step_rate)
        for ref, result in zip(outs[1 + 3 * param : 4 + 3 * param], results):
            ref[at] = result

    for index in range(3):
        update(0, (index,), attend_ref[:, index * width : (index + 1) * width], rate)
    update(1, (...,), attend_ref[:, 3 * width :].T, rate)
    split, rows = feed_a.shape[0], state[6].shape[0]
    for feed_ref, within in ((feed_a, slice(0, split)), (feed_b, slice(split, rows))):
        for index in range(3):
            at = (within, slice(index * part, (index + 1) * part))
            first = 2 * index * part
            update(2, at, feed_ref[:, first : first + part], rate)
            update(3, at, feed_ref[:, first + part : first + 2 * part], rate)
    update(4, (...,), vectors[:6], vector_rate)
    model = where_ref[2]
    head = jnp.zeros((2, width), f32)
    for index in range(4):
        head = head + jnp.where(model == index, vectors[6:8, index * width : (index + 1) * width], 0.0)
    update(5, (...,), head, vector_rate)
    bias = vector_ref[pl.ds(8 + model, 1), :]
    bias = jnp.concatenate([bias[:, at : at + 128] for at in range(0, bias.shape[1], 128)], axis=0)
    update(6, (...,), bias, vector_rate)


def bring_body(*refs):
    half = len(refs) // 2
    for source, target in zip(refs[:half], refs[half:]):
        target[...] = source[...]


def bring(arrays, after):
    return pl.pallas_call(
        lambda *refs: bring_body(*refs[: len(arrays)], *refs[len(arrays) + len(after) :]),
        in_specs=[NEAR] * len(arrays) + [LATER] * len(after),
        out_specs=[NEAR] * len(arrays),
        out_shape=[sds(array.shape, f32) for array in arrays],
        compiler_params=params(8),
        cost_estimate=cost(4e6, 6e6),
        name="bring",
    )(*from_far(*arrays), *after)


def last_sum_body(*refs):
    parts, (early_ref, late_ref, token_ref, total_ref, owned_ref) = refs[:-5], refs[-5:]
    total = sum(part[0].astype(f32) for part in parts)
    total_ref[...] = total
    squares = sum(jnp.sum(values * values) for values in (total, early_ref[...], late_ref[...]))
    owned_ref[:2, :] = token_ref[...]
    owned_ref[2:, :] = jnp.full((1, owned_ref.shape[1]), squares, f32)


def last_sum(parts, early_total, late_total, token_sums):
    _, rows, columns = parts[0].shape
    return pl.pallas_call(
        last_sum_body,
        in_specs=[NEAR] * (len(parts) + 3),
        out_specs=[NEAR] * 2,
        out_shape=[sds((rows, columns), f32), sds((3, columns), f32)],
        compiler_params=params(8),
        cost_estimate=cost(0, 0),
        name="last_sum",
    )(*parts, early_total, late_total, token_sums)


def optimize(where, owned, vector_total, attend_total, feed_totals, arrays):
    shapes = [sds(array.shape, f32) for array in arrays]
    return pl.pallas_call(
        optimize_body,
        in_specs=[pl.BlockSpec(memory_space=pltpu.SMEM)]
        + [pl.BlockSpec(memory_space=pltpu.VMEM)] * (5 + len(arrays)),
        out_shape=[sds((1, 1), f32)] + shapes,
        compiler_params=params(20),
        cost_estimate=cost(4e6, 8e6),
        name="optimize",
    )(where, owned, vector_total, attend_total, *feed_totals, *arrays)


def shards(
    tokens,
    cotangent,
    lengths,
    input_weight,
    output_weight,
    expand_weight,
    shrink_weight,
    layer_vectors,
    head_bias,
    expand_bias,
    first_input,
    first_output,
    first_expand,
    first_shrink,
    first_vectors,
    first_head,
    first_bias,
    second_input,
    second_output,
    second_expand,
    second_shrink,
    second_vectors,
    second_head,
    second_bias,
):
    dp_count = lax.axis_size("dp")
    mp_count = lax.axis_size("mp")
    cube = dp_count == 8 and mp_count == 4
    rows = input_weight.shape[0]
    width = input_weight.shape[2]
    hidden = expand_weight.shape[1]
    seq, depth = tokens.shape
    part = hidden // 3
    model_index = lax.axis_index("mp")
    me = lax.axis_index("dp") * mp_count + model_index

    attend_shard, feed_shard, bias_full = pack(
        input_weight.transpose(1, 0, 2),
        output_weight,
        expand_weight,
        shrink_weight.T,
        head_bias,
        expand_bias.reshape(hidden // 128, 128),
    )
    if cube:
        core, near = me & 1, model_index
        devices = jnp.arange(32).reshape(8, 4).T
        spots = jnp.concatenate(
            [place(devices ^ me, devices & 1, orders) for orders in (CORE_ORDERS, LATE_ORDERS)]
        ).astype(jnp.int32)
    else:
        core = near = jnp.zeros((), jnp.int32)
        spots = (jnp.arange(8)[:, None] % 4 // 2 * 8 + jnp.arange(8)[None]).astype(jnp.int32)
    where = jnp.stack([core, near, model_index]).astype(jnp.int32)

    def turned(array):
        return array.transpose(1, 0, 2)

    state = (
        (turned(input_weight), turned(first_input), turned(second_input)),
        (output_weight, first_output, second_output),
        (expand_weight, first_expand, second_expand),
        (shrink_weight.T, first_shrink.T, second_shrink.T),
        (layer_vectors, first_vectors, second_vectors),
        (head_bias, first_head, second_head),
        tuple(array.reshape(hidden // 128, 128) for array in (expand_bias, first_bias, second_bias)),
    )
    arrays = [array for group in state for array in group]

    if cube:
        split = rows * 2 // 3
        held, early, late = attend_shard[None], feed_shard[None, :split], feed_shard[None, split:]
        arrived, far_late = cube_permute(held, 0), cube_permute(late, 0, LATE_ORDERS)
        held, bias_full = lax.optimization_barrier((joined(held, arrived), bias_full))
        arrived = cube_permute(held, 1)
        bias_full = bias_full + bit_permute(bias_full, 0)
        late = joined(late, far_late)
        normed, normed_t, upstream_t = prepare(tokens, cotangent, layer_vectors, (held, late))
        late = joined(late, cube_permute(late, 1, LATE_ORDERS))
        held, early, late, normed, bias_full, spots, where = lax.optimization_barrier(
            (held, early, late, normed, bias_full, spots, where)
        )
        held, early = lax.optimization_barrier((joined(held, arrived), early))
        arrived, far_early = cube_permute(held, 2), cube_permute(early, 0)
        bias_full = bias_full + bit_permute(bias_full, 1)
        held, early = joined(held, arrived), joined(early, far_early)
        held, early, bias_full = lax.optimization_barrier((held, early, bias_full))
        far, far_early = cube_permute(held, 3), cube_permute(early, 1)
        twin = bit_permute(held, 0)
        early = joined(early, far_early)
        far, early, late = lax.optimization_barrier((far, early, late))
        attend_halves = (held, far, twin, bit_permute(far, 0))
        far_early, far_late = cube_permute(early, 2), cube_permute(late, 2, LATE_ORDERS)
        qkv, wide, wide_out = project(where, spots, normed, attend_halves, bias_full, ())
        far_early, far_late, qkv = lax.optimization_barrier((far_early, far_late, qkv))
        early, late = joined(early, far_early), joined(late, far_late)
        far_early, far_late = cube_permute(early, 3), cube_permute(late, 3, LATE_ORDERS)
        twin_early, twin_late = bit_permute(early, 0), bit_permute(late, 0)
        mixture, log_totals = attend_forward(where, lengths, qkv, (early, late))
        far_early, far_late, twin_late, mixture = lax.optimization_barrier(
            (far_early, far_late, twin_late, mixture)
        )
        last_early, last_late = bit_permute(far_early, 0), bit_permute(far_late, 0)
        middle, hidden_in, hidden_t, unit, inverse = attend_out(mixture, wide_out, tokens, layer_vectors)
        feed_halves = (early, far_early, twin_early, last_early, late, far_late, twin_late, last_late)
    else:

        def planes(shard):
            full = lax.all_gather(lax.all_gather(shard, "dp", axis=0, tiled=True), "mp", axis=0)
            full = full.reshape(2, 2, 8, depth // 8, shard.shape[1]).transpose(1, 0, 2, 3, 4)
            return tuple(full.reshape(4, 8, depth // 8, shard.shape[1]))

        normed, normed_t, upstream_t = prepare(tokens, cotangent, layer_vectors, ())
        bias_full = lax.psum(bias_full, "mp")
        qkv, wide, wide_out = project(where, spots, normed, planes(attend_shard), bias_full, ())
        mixture, log_totals = attend_forward(where, lengths, qkv, ())
        middle, hidden_in, hidden_t, unit, inverse = attend_out(mixture, wide_out, tokens, layer_vectors)
        split = depth // 8 * 2 // 3
        feed_planes = planes(feed_shard)
        feed_halves = tuple(array[:, :split] for array in feed_planes) + tuple(
            array[:, split:] for array in feed_planes
        )
    block_out, back, keep_early, send_early, keep_late, send_late, bias_grad = feed(
        where,
        spots,
        hidden_in,
        hidden_t,
        cotangent,
        upstream_t,
        feed_halves,
        bias_full,
        middle,
        layer_vectors,
    )
    middle_grad, mixture_grad, output_grad, middle_sums = middle_back(
        where, lengths, back, unit, inverse, cotangent, mixture, wide_out, layer_vectors
    )
    if cube:
        early = [keep_early, bit_permute(send_early, 0)]
        late = [keep_late, bit_permute(send_late, 0)]
        early[0], late[0], mixture_grad = lax.optimization_barrier((early[0], late[0], mixture_grad))
        away, far_away_late = leaving(early, 3), leaving(late, 3)
        packed_grad = attend_backward(
            where, lengths, qkv, mixture_grad, log_totals, (away, far_away_late)
        )
        early = staying(early, 3) + [cube_permute(away, 3)]
        late = staying(late, 3) + [cube_permute(far_away_late, 3, LATE_ORDERS)]
        early[0], late[0], packed_grad = lax.optimization_barrier((early[0], late[0], packed_grad))
        away, far_away_late = leaving(early, 2), leaving(late, 2)
        sums = (middle_sums, bias_grad)
        keep_attend, send_attend, rider = input_grad(
            where, spots, normed_t, packed_grad, output_grad, sums, 16, depth // 8, (away, far_away_late)
        )
        early = staying(early, 2) + [cube_permute(away, 2)]
        late = staying(late, 2) + [cube_permute(far_away_late, 2, LATE_ORDERS)]
        early[-1], late[-1], send_attend = lax.optimization_barrier((early[-1], late[-1], send_attend))
        twin_b, rider, _ = with_rider(send_attend[8:], rider, lambda values: bit_permute(values, 0))
        twin_a = bit_permute(send_attend[:8], 0)
        away = (keep_attend[8:].astype(f32) + twin_b.astype(f32)).astype(low)
        arrived, rider, message = with_rider(away, rider, lambda values: cube_permute(values, 3))
        attend_parts = [keep_attend[:8], twin_a, arrived]
        feed_away = leaving(early, 1)
        token_grad, token_sums = token_back(
            packed_grad, wide, tokens, middle_grad, layer_vectors, (message, feed_away)
        )
        early = staying(early, 1) + [cube_permute(feed_away, 1)]
        attend_parts[0], late[0], token_sums = lax.optimization_barrier(
            (attend_parts[0], late[0], token_sums)
        )
        feed_away = leaving(late, 1)
        late = staying(late, 1) + [cube_permute(feed_away, 1, LATE_ORDERS)]
        away = leaving(attend_parts, 2)
        arrived, rider, message = with_rider(away, rider, lambda values: cube_permute(values, 2))
        attend_parts = staying(attend_parts, 2) + [arrived]
        message, early[0], late[0] = lax.optimization_barrier((message, early[0], late[0]))
        feed_away = leaving(early, 0)
        early = staying(early, 0) + [cube_permute(feed_away, 0)]
        away = leaving(attend_parts, 1)
        arrived, rider, message = with_rider(away, rider, lambda values: cube_permute(values, 1))
        attend_parts = staying(attend_parts, 1) + [arrived]
        message, early[0], late[0] = lax.optimization_barrier((message, early[0], late[0]))
        early_total = summed(early)
        feed_away = leaving(late, 0)
        late = staying(late, 0) + [cube_permute(feed_away, 0, LATE_ORDERS)]
        arrays = list(bring(arrays, (message,)))
        attend_parts[0], arrays[0] = lax.optimization_barrier((attend_parts[0], arrays[0]))
        away = leaving(attend_parts, 0)
        away, early_total = lax.optimization_barrier((away, early_total))
        arrived, vector_total, _ = with_rider(away, rider, lambda values: cube_permute(values, 0))
        attend_parts = staying(attend_parts, 0) + [arrived]
        late_total = summed(late)
        feed_totals = (early_total, late_total)
        attend_total, owned = last_sum(attend_parts, early_total, late_total, token_sums)
        owned = cube_sum(owned)
    else:
        packed_grad = attend_backward(where, lengths, qkv, mixture_grad, log_totals, ())
        sums = (middle_sums, bias_grad)
        keep_attend, send_attend, vector_total = input_grad(
            where, spots, normed_t, packed_grad, output_grad, sums, 16, depth // 8, ()
        )
        token_grad, token_sums = token_back(packed_grad, wide, tokens, middle_grad, layer_vectors, ())
        vector_total = lax.psum(vector_total, ("dp", "mp"))

    if not cube:

        def own_block(keep, send):
            full = jnp.stack([keep, send]).reshape(2, 2, 8, keep.shape[1], keep.shape[2])
            full = full.transpose(1, 0, 2, 3, 4).reshape(4, 8 * keep.shape[1], keep.shape[2])
            full = lax.psum_scatter(full, "mp", scatter_dimension=0, tiled=False)
            return lax.psum(full, "dp")

        def own_rows(*blocks):
            full = jnp.concatenate([block.reshape(8, -1, block.shape[1]) for block in blocks], axis=1)
            full = full.reshape(depth, full.shape[2]).astype(f32)
            return lax.dynamic_slice_in_dim(full, lax.axis_index("dp") * rows, rows, 0)

        attend_total = own_rows(own_block(keep_attend, send_attend))
        feed_total = own_rows(own_block(keep_early, send_early), own_block(keep_late, send_late))
        feed_totals = feed_total[: rows * 2 // 3], feed_total[rows * 2 // 3 :]
        attend_total, owned = last_sum((attend_total[None],), *feed_totals, token_sums)
        owned = lax.psum(owned, ("dp", "mp"))
    grad_norm, *updates = optimize(where, owned, vector_total, attend_total, feed_totals, arrays)
    grad_norm = grad_norm[0, 0]
    moment_input, square_input, updated_input = (turned(array) for array in updates[:3])
    moment_output, square_output, updated_output = updates[3:6]
    moment_expand, square_expand, updated_expand = updates[6:9]
    moment_shrink, square_shrink, updated_shrink = (array.T for array in updates[9:12])
    moment_vectors, square_vectors, updated_vectors = updates[12:15]
    moment_head, square_head, updated_head = updates[15:18]
    moment_bias, square_bias, updated_bias = (array.reshape(hidden) for array in updates[18:])
    return (
        block_out,
        token_grad,
        grad_norm,
        moment_input,
        square_input,
        updated_input,
        moment_output,
        square_output,
        updated_output,
        moment_expand,
        square_expand,
        updated_expand,
        moment_shrink,
        square_shrink,
        updated_shrink,
        moment_vectors,
        square_vectors,
        updated_vectors,
        moment_head,
        square_head,
        updated_head,
        moment_bias,
        square_bias,
        updated_bias,
    )


def solution(mesh):
    in_specs = (
        P(("dp", "mp"), None),
        P(("dp", "mp"), None),
        P("dp"),
        P("dp", None, "mp"),
        P("mp", "dp"),
        P("dp", "mp"),
        P("mp", "dp"),
        P(),
        P(None, "mp"),
        P("mp"),
        P("dp", None, "mp"),
        P("mp", "dp"),
        P("dp", "mp"),
        P("mp", "dp"),
        P(),
        P(None, "mp"),
        P("mp"),
        P("dp", None, "mp"),
        P("mp", "dp"),
        P("dp", "mp"),
        P("mp", "dp"),
        P(),
        P(None, "mp"),
        P("mp"),
    )
    out_specs = (
        P(("dp", "mp"), None),
        P(("dp", "mp"), None),
        P(),
        P("dp", None, "mp"),
        P("dp", None, "mp"),
        P("dp", None, "mp"),
        P("mp", "dp"),
        P("mp", "dp"),
        P("mp", "dp"),
        P("dp", "mp"),
        P("dp", "mp"),
        P("dp", "mp"),
        P("mp", "dp"),
        P("mp", "dp"),
        P("mp", "dp"),
        P(),
        P(),
        P(),
        P(None, "mp"),
        P(None, "mp"),
        P(None, "mp"),
        P("mp"),
        P("mp"),
        P("mp"),
    )
    return jax.shard_map(shards, mesh=mesh, in_specs=in_specs, out_specs=out_specs, check_vma=False)
```

```python
import functools
import jax
import jax.numpy as jnp
from jax import lax
from jax.experimental import pallas as pl
from jax.experimental.pallas import tpu as pltpu
from jax.sharding import PartitionSpec as P

HEAD_DIM = 64
TILE = 256
STEP = 10

eps_norm = 1e-05
clip_norm = 1.0
beta_one = 0.9
beta_two = 0.999
adam_eps = 1e-08
rate = 0.05
vector_rate = 0.5
decay = 0.01
excluded = -1e30
low = jnp.bfloat16
f32 = jnp.float32
GELU_A = 0.7978845608028654
GELU_B = GELU_A * 0.044715


def params(limit_mib, **kw):
    return pltpu.CompilerParams(vmem_limit_bytes=limit_mib * 1024 * 1024, **kw)


def cost(flops, moved, special=0):
    return pl.CostEstimate(flops=int(flops), bytes_accessed=int(moved), transcendentals=int(special))


def mm(a, b):
    return jnp.dot(a, b, preferred_element_type=f32)


def mm_nt(a, b):
    return lax.dot_general(a, b, (((1,), (1,)), ((), ())), preferred_element_type=f32)


def whole(shape):
    zeros = (0,) * len(shape)
    return pl.BlockSpec(shape, lambda *_: zeros)


def once(shape):
    zeros = (0,) * len(shape)
    return pl.BlockSpec(shape, lambda *_: zeros, pipeline_mode=pl.Buffered(1))


def held_back(body, first, count):
    def run(*refs):
        return body(*refs[:first], *refs[first + count :])

    return run


LATER = pl.BlockSpec(memory_space=pl.ANY)


def far_away(shape, dtype):
    return pltpu.HBM(shape, dtype)


def from_far(*arrays):
    return [pltpu.with_memory_space_constraint(array, pltpu.HBM) for array in arrays]


def sds(shape, dtype):
    return jax.ShapeDtypeStruct(shape, dtype)


def live_blocks(length, count, body):
    for blocks in range(1, count + 1):
        low_end = (blocks - 1) * TILE
        high_end = blocks * TILE
        @pl.when((length > low_end) & (length <= high_end))
        def _(blocks=blocks):
            body(length, blocks)


PAIR = 2 * HEAD_DIM


def span(block):
    return slice(block * TILE, (block + 1) * TILE)


def both_heads(values):
    lane = lax.broadcasted_iota(jnp.int32, values.shape, 1)
    none = jnp.zeros_like(values)
    return jnp.concatenate(
        [jnp.where(lane < HEAD_DIM, values, none), jnp.where(lane >= HEAD_DIM, values, none)], axis=0
    )


def causal_mask():
    key_id = lax.broadcasted_iota(jnp.int32, (TILE, 2 * TILE), 0)
    query_id = lax.broadcasted_iota(jnp.int32, (TILE, 2 * TILE), 1) & (TILE - 1)
    return key_id <= query_id


def forward_body(where_ref, lengths_ref, q_ref, k_ref, v_ref, o_ref, lse_ref, vt_ref):
    seq = q_ref.shape[0]
    vt_ref[...] = v_ref[...].T
    causal = causal_mask()

    def run(length, blocks):
        def scores(b):
            q = q_ref[span(b), :] * jnp.asarray(HEAD_DIM**-0.5, low)
            return mm_nt(k_ref[: (b + 1) * TILE, :], both_heads(q))

        now = scores(0)
        for b in range(blocks):
            start, stop = b * TILE, (b + 1) * TILE
            later = scores(b + 1) if b + 1 < blocks else None
            last = jnp.where(causal, now[start:, :], excluded)
            top = jnp.max(last, axis=0, keepdims=True)
            if b:
                top = jnp.maximum(top, jnp.max(now[:start], axis=0, keepdims=True))
            p = jnp.exp(last - top)
            total = jnp.sum(p, axis=0, keepdims=True)
            pb = p.astype(low)
            if b:
                pf = jnp.exp(now[:start] - top)
                total = total + jnp.sum(pf, axis=0, keepdims=True)
                pb = jnp.concatenate([pf.astype(low), pb], axis=0)
            inverse = 1.0 / total
            lse = top + jnp.log(total)
            outs = []
            for h in range(2):
                at = slice(h * TILE, (h + 1) * TILE)
                out = mm(vt_ref[h * HEAD_DIM : (h + 1) * HEAD_DIM, :stop], pb[:, at])
                outs.append(out * inverse[:, at])
                lse_ref[0, h : h + 1, start:stop] = lse[:, at]
            both = jnp.concatenate(outs, axis=0).T
            row = start + lax.broadcasted_iota(jnp.int32, both.shape, 0)
            o_ref[start:stop, :] = jnp.where(row < length, both, 0.0).astype(low)
            now = later
        if blocks * TILE < seq:
            o_ref[blocks * TILE :, :] = jnp.zeros((seq - blocks * TILE, PAIR), low)
            lse_ref[0, :, blocks * TILE :] = jnp.zeros((2, seq - blocks * TILE), f32)

    live_blocks(lengths_ref[where_ref[2]], seq // TILE, run)


def attend_forward(where, lengths, qkv, after):
    seq, width = qkv.shape[0], qkv.shape[1] // 3
    pair = 2 * HEAD_DIM
    pairs = width // pair
    half = seq * seq * 5 // 8
    spec = lambda part: pl.BlockSpec((seq, pair), lambda i, *_: (0, part * pairs + i))
    return pl.pallas_call(
        held_back(forward_body, 5, len(after)),
        grid_spec=pltpu.PrefetchScalarGridSpec(
            num_scalar_prefetch=2,
            grid=(pairs,),
            in_specs=[spec(0), spec(1), spec(2)] + [LATER] * len(after),
            out_specs=[
                pl.BlockSpec((seq, pair), lambda i, *_: (0, i)),
                pl.BlockSpec((1, 2, seq), lambda i, *_: (i, 0, 0)),
            ],
            scratch_shapes=[pltpu.VMEM((pair, seq), low)],
        ),
        out_shape=[sds((seq, width), low), far_away((pairs, 2, seq), f32)],
        compiler_params=params(20),
        cost_estimate=cost(pairs * 2 * half * 2 * 2 * 256, seq * width * 8, pairs * 2 * half),
        name="attend_forward",
    )(where, lengths, *from_far(qkv, qkv, qkv), *after)


def backward_body(where_ref, lengths_ref, q_ref, k_ref, v_ref, do_ref, lse_ref, out_ref, kt_ref, ksum, vsum):
    seq = q_ref.shape[0]
    scale = HEAD_DIM**-0.5
    kt_ref[...] = k_ref[...].T
    causal = causal_mask()

    def run(length, blocks):
        def scores(b):
            qq = both_heads(q_ref[span(b), :] * jnp.asarray(scale, low))
            uu = both_heads(do_ref[span(b), :])
            stop = (b + 1) * TILE
            return qq, uu, mm_nt(k_ref[:stop, :], qq), mm_nt(v_ref[:stop, :], uu)

        now = scores(blocks - 1)
        for b in reversed(range(blocks)):
            start, stop = b * TILE, (b + 1) * TILE
            later = scores(b - 1) if b else None
            qq, uu, s, dp = now
            lse = jnp.concatenate([lse_ref[0, 0:1, start:stop], lse_ref[0, 1:2, start:stop]], axis=1)
            p = jnp.exp(jnp.where(causal, s[start:], excluded) - lse)
            inner = jnp.sum(p * dp[start:], axis=0, keepdims=True)
            if b:
                pf = jnp.exp(s[:start] - lse)
                inner = inner + jnp.sum(pf * dp[:start], axis=0, keepdims=True)
            ds = (p * (dp[start:] - inner)).astype(low)
            pb = p.astype(low)
            if b:
                ds = jnp.concatenate([(pf * (dp[:start] - inner)).astype(low), ds], axis=0)
                pb = jnp.concatenate([pf.astype(low), pb], axis=0)
            dk, dv = mm(ds, qq), mm(pb, uu)
            if b == blocks - 1:
                ksum[:stop, :] = dk
                vsum[:stop, :] = dv
            else:
                ksum[:stop, :] += dk
                vsum[:stop, :] += dv
            dq = jnp.concatenate(
                [
                    mm(
                        kt_ref[h * HEAD_DIM : (h + 1) * HEAD_DIM, :stop],
                        ds[:, h * TILE : (h + 1) * TILE],
                    )
                    for h in range(2)
                ],
                axis=0,
            )
            out_ref[1, start:stop, :] = ksum[start:stop, :].astype(low)
            out_ref[2, start:stop, :] = vsum[start:stop, :].astype(low)
            out_ref[0, start:stop, :] = (dq.T * scale).astype(low)
            now = later
        if blocks * TILE < seq:
            rest = jnp.zeros((seq - blocks * TILE, PAIR), low)
            for part in range(3):
                out_ref[part, blocks * TILE :, :] = rest

    live_blocks(lengths_ref[where_ref[2]], seq // TILE, run)


def attend_backward(where, lengths, qkv, upstream, lse, after):
    seq, width = upstream.shape
    pair = 2 * HEAD_DIM
    pairs = width // pair
    half = seq * seq * 5 // 8
    spec = lambda part: pl.BlockSpec((seq, pair), lambda i, *_: (0, part * pairs + i))
    own = pl.BlockSpec((seq, pair), lambda i, *_: (0, i))
    return pl.pallas_call(
        held_back(backward_body, 7, len(after)),
        grid_spec=pltpu.PrefetchScalarGridSpec(
            num_scalar_prefetch=2,
            grid=(pairs,),
            in_specs=[spec(0), spec(1), spec(2), own, pl.BlockSpec((1, 2, seq), lambda i, *_: (i, 0, 0))]
            + [LATER] * len(after),
            out_specs=pl.BlockSpec((3, seq, pair), lambda i, *_: (0, 0, i)),
            scratch_shapes=[
                pltpu.VMEM((pair, seq), low),
                pltpu.VMEM((seq, pair), f32),
                pltpu.VMEM((seq, pair), f32),
            ],
        ),
        out_shape=sds((3, seq, width), low),
        compiler_params=params(28),
        cost_estimate=cost(pairs * 2 * half * 5 * 2 * 256, seq * width * 14, pairs * 2 * half),
        name="attend_backward",
    )(where, lengths, *from_far(qkv, qkv, qkv), upstream, *from_far(lse), *after)


def normalize(values):
    average = jnp.mean(values, axis=-1, keepdims=True)
    centred = values - average
    inverse = lax.rsqrt(jnp.mean(centred * centred, axis=-1, keepdims=True) + eps_norm)
    return centred * inverse, inverse


def pull_norm(scaled, unit, inverse):
    first = jnp.mean(scaled, axis=-1, keepdims=True)
    second = jnp.mean(scaled * unit, axis=-1, keepdims=True)
    return inverse * (scaled - first - unit * second)


def columns_of(values):
    return jnp.sum(values, axis=0, keepdims=True)


def pack_body(
    input_ref, output_ref, expand_ref, shrink_ref, head_ref, hidden_ref, attend_ref, feed_ref, bias_ref
):
    width = input_ref.shape[2]
    part = expand_ref.shape[1] // 3
    for index in range(3):
        attend_ref[:, index * width : (index + 1) * width] = input_ref[index].astype(low)
        at = slice(index * part, (index + 1) * part)
        feed_ref[:, 2 * index * part : (2 * index + 1) * part] = expand_ref[:, at].astype(low)
        feed_ref[:, (2 * index + 1) * part : (2 * index + 2) * part] = shrink_ref[:, at].astype(low)
    attend_ref[:, 3 * width :] = output_ref[...].T.astype(low)
    pieces = [head_ref[0:1, :], head_ref[1:2, :]]
    pieces += [hidden_ref[row : row + 1, :] for row in range(hidden_ref.shape[0])]
    bias_ref[...] = jnp.zeros_like(bias_ref)
    bias_ref[pl.ds(lax.axis_index("mp"), 1), :] = jnp.concatenate(pieces, axis=1)


def pack(input_weight, output_weight, expand, shrink, head_bias, hidden_bias):
    rows, width = input_weight.shape[1:]
    hidden = expand.shape[1]
    return pl.pallas_call(
        pack_body,
        out_shape=[
            sds((rows, 4 * width), low),
            sds((rows, 2 * hidden), low),
            sds((4, 2 * width + hidden), f32),
        ],
        compiler_params=params(6),
        cost_estimate=cost(rows * hidden, rows * hidden * 18),
        name="pack",
    )(*from_far(input_weight, output_weight, expand, shrink, head_bias, hidden_bias))


def prepare_body(x_ref, up_ref, vec_ref, h_ref, ht_ref, upt_ref):
    unit, _ = normalize(x_ref[...].astype(f32))
    h = (unit * vec_ref[0:1, :] + vec_ref[1:2, :]).astype(low)
    h_ref[...] = h
    ht_ref[...] = h.T
    upt_ref[...] = up_ref[...].T


def prepare(x, up, vectors, after):
    seq, depth = x.shape
    rows = pl.BlockSpec((2 * TILE, depth), lambda i: (i, 0))
    turned = pl.BlockSpec((depth, 2 * TILE), lambda i: (0, i))
    return pl.pallas_call(
        held_back(prepare_body, 3, len(after)),
        grid=(seq // (2 * TILE),),
        in_specs=[rows, rows, once(vectors.shape)] + [LATER] * len(after),
        out_specs=[rows, turned, turned],
        out_shape=[sds((seq, depth), low), sds((depth, seq), low), far_away((depth, seq), low)],
        compiler_params=params(16),
        cost_estimate=cost(seq * depth * 10, seq * depth * 10),
        name="prepare",
    )(*from_far(x, up), vectors, *after)


def slot(halves, spot, at):
    first, second = halves
    inner = spot & 7
    return jnp.where(spot < 8, first[inner, :, at], second[inner, :, at])


def project_body(
    where_ref, spots_ref, h_ref, mine_a, mine_b, twin_a, twin_b, bias_ref, qkv_ref, wide_ref, last_ref
):
    part = pl.program_id(0)
    rows = mine_a.shape[1]
    width = mine_a.shape[2] // 4
    groups = wide_ref.shape[1] // rows

    def collect(sources, index):
        columns = slice(index * width, (index + 1) * width)
        for group in range(groups):
            pieces = [slot(sources[model % 2], spots_ref[model, group], columns) for model in range(4)]
            at = slice(group * rows, (group + 1) * rows)
            if index < 3:
                wide_ref[0, at, :] = jnp.concatenate(pieces, axis=1)
            else:
                last_ref[at, :] = jnp.concatenate(pieces, axis=1)

    for index in range(4):
        for core in range(2):

            @pl.when((part == index) & (where_ref[0] == core))
            def _(index=index, core=core):
                mine, twin = (mine_a, mine_b), (twin_a, twin_b)
                collect((mine, twin) if core == 0 else (twin, mine), index)

    for index in range(3):

        @pl.when(part == index)
        def _(index=index):
            out = mm(h_ref[...], wide_ref[0])
            if index != 1:
                at = slice(index // 2 * width, (index // 2 + 1) * width)
                bias = jnp.concatenate([bias_ref[model : model + 1, at] for model in range(4)], axis=1)
                out = out + bias
            qkv_ref[...] = out.astype(low)


def project(where, spots, h, halves, bias, after):
    seq, depth = h.shape
    return pl.pallas_call(
        held_back(project_body, 8, len(after)),
        grid_spec=pltpu.PrefetchScalarGridSpec(
            num_scalar_prefetch=2,
            grid=(4,),
            in_specs=[
                once((seq, depth)),
                *[once(halves[0].shape)] * 4,
                once(bias.shape),
            ]
            + [LATER] * len(after),
            out_specs=[
                pl.BlockSpec((seq, depth), lambda i, *_: (0, jnp.minimum(i, 2))),
                pl.BlockSpec((1, depth, depth), lambda i, *_: (jnp.minimum(i, 2), 0, 0)),
                whole((depth, depth)),
            ],
        ),
        out_shape=[
            far_away((seq, 3 * depth), low),
            far_away((3, depth, depth), low),
            sds((depth, depth), low),
        ],
        compiler_params=params(24),
        cost_estimate=cost(2 * seq * depth * depth * 3, seq * depth * 16),
        name="project",
    )(where, spots, h, *halves, bias, *after)


NEAR = pl.BlockSpec(memory_space=pltpu.VMEM)
SCALARS = pl.BlockSpec(memory_space=pltpu.SMEM)


def attend_out_body(o_ref, w_ref, x_ref, vec_ref, middle_ref, h_ref, ht_ref, unit_ref, inverse_ref):
    for tile in range(o_ref.shape[0] // TILE):
        at = slice(tile * TILE, (tile + 1) * TILE)
        middle = x_ref[at, :].astype(f32) + mm_nt(o_ref[at, :], w_ref[...]) + vec_ref[4:5, :]
        middle_ref[at, :] = middle.astype(low)
        unit, inverse = normalize(middle)
        unit_ref[at, :] = unit.astype(low)
        inverse_ref[at, :] = jnp.broadcast_to(inverse, (TILE, inverse_ref.shape[1]))
        h = (unit * vec_ref[2:3, :] + vec_ref[3:4, :]).astype(low)
        h_ref[at, :] = h
        ht_ref[:, at] = h.T


def attend_out(o, wide_out, x, vectors):
    seq, depth = x.shape
    return pl.pallas_call(
        attend_out_body,
        in_specs=[NEAR] * 4,
        out_specs=[NEAR] * 5,
        out_shape=[
            sds((seq, depth), low),
            sds((seq, depth), low),
            sds((depth, seq), low),
            sds((seq, depth), low),
            sds((seq, 128), f32),
        ],
        compiler_params=params(10),
        cost_estimate=cost(2 * seq * depth * depth, seq * depth * 14),
        name="attend_out",
    )(o, wide_out, x, vectors)


def feed_body(
    where_ref,
    spots_ref,
    h2_ref,
    h2t_ref,
    up_ref,
    upt_ref,
    mine_a,
    mine_b,
    twin_a,
    twin_b,
    mine_c,
    mine_d,
    twin_c,
    twin_d,
    bias_ref,
    middle_ref,
    vec_ref,
    block_ref,
    back_ref,
    keep_a,
    send_a,
    keep_b,
    send_b,
    bias_grad_ref,
    out_ref,
    sum_ref,
    wide_ref,
    act_ref,
    pre_ref,
):
    part = mine_a.shape[2] // 6
    groups = spots_ref.shape[1]
    rows = wide_ref.shape[0] // groups
    split = mine_a.shape[1]
    skip = bias_ref.shape[1] - bias_grad_ref.shape[1]
    pieces = (
        ((mine_a, mine_b), (twin_a, twin_b), 0, slice(0, split)),
        ((mine_c, mine_d), (twin_c, twin_d), 4, slice(split, rows)),
    )
    half = keep_a.shape[1]
    results = ((keep_a, send_a, 0, slice(0, half)), (keep_b, send_b, 4, slice(half, rows)))
    out_ref[...] = middle_ref[...].astype(f32) + vec_ref[5:6, :]
    sum_ref[...] = jnp.zeros_like(sum_ref)

    def step(index, carry):
        side = lax.rem(index, 2)
        first = pl.multiple_of(index // 2 * part, 128)
        lanes = pl.ds(pl.multiple_of(2 * first, 128), part)
        next_lanes = pl.ds(pl.multiple_of(2 * first + part, 128), part)
        models = [where_ref[1] ^ (2 * side + core) for core in range(2)]
        for group in range(groups):
            for mine, twin, table, within in pieces:
                at = slice(group * rows + within.start, group * rows + within.stop)
                for core, halves in enumerate((mine, twin)):
                    spot = spots_ref[table + models[core], group]
                    wide_ref[at, core * part : (core + 1) * part] = slot(halves, spot, lanes)
                    wide_ref[at, (2 + core) * part : (3 + core) * part] = slot(halves, spot, next_lanes)

        expand = wide_ref[:, : 2 * part]
        shrink = wide_ref[:, 2 * part :]
        bias = jnp.concatenate(
            [bias_ref[pl.ds(model, 1), pl.ds(pl.multiple_of(skip + first, 128), part)] for model in models],
            axis=1,
        )
        sums = jnp.zeros((1, 2 * part), f32)
        for tile in range(h2_ref.shape[0] // TILE):
            at = slice(tile * TILE, (tile + 1) * TILE)
            u = mm(h2_ref[at, :], expand) + bias
            square = u * u
            th = jnp.tanh(u * (GELU_A + GELU_B * square))
            gate = 0.5 * th + 0.5
            slope = gate + (gate * (1.0 - gate)) * (u * (2.0 * GELU_A + (6.0 * GELU_B) * square))
            pre = (mm(up_ref[at, :], shrink) * slope).astype(low)
            act_ref[at, :] = (u * gate).astype(low)
            pre_ref[at, :] = pre
            sums = sums + columns_of(pre.astype(f32))
        for core, model in enumerate(models):
            bias_grad_ref[pl.ds(model, 1), pl.ds(first, part)] = sums[:, core * part : (core + 1) * part]
        out_ref[...] += mm_nt(act_ref[...], shrink)
        sum_ref[...] += mm_nt(pre_ref[...], expand)
        grad_expand = mm(h2t_ref[...], pre_ref[...]).astype(low)
        grad_shrink = mm(upt_ref[...], act_ref[...]).astype(low)
        for group in range(groups):
            for keep, send, table, within in results:
                at = slice(group * rows + within.start, group * rows + within.stop)
                for core, target in enumerate((keep, send)):
                    spot = spots_ref[table + models[core], group]
                    columns = slice(core * part, (core + 1) * part)
                    target[spot, :, lanes] = grad_expand[at, columns]
                    target[spot, :, next_lanes] = grad_shrink[at, columns]
        return carry

    lax.fori_loop(0, 6, step, 0)
    block_ref[...] = out_ref[...].astype(low)
    back_ref[...] = sum_ref[...].astype(low)


def feed(where, spots, h2, h2t, up, upt, halves, bias, middle, vectors):
    seq, depth = h2.shape
    half, _, columns = halves[0].shape
    part = columns // 6
    splits = [halves[0].shape[1], halves[4].shape[1]]
    return pl.pallas_call(
        feed_body,
        in_specs=[SCALARS] * 2 + [NEAR] * 15,
        out_specs=[NEAR] * 7,
        scratch_shapes=[
            pltpu.VMEM((seq, depth), f32),
            pltpu.VMEM((seq, depth), f32),
            pltpu.VMEM((depth, 4 * part), low),
            pltpu.VMEM((seq, 2 * part), low),
            pltpu.VMEM((seq, 2 * part), low),
        ],
        out_shape=[sds((seq, depth), low)] * 2
        + [sds((2 * half, rows, columns), low) for rows in splits for _ in range(2)]
        + [sds((4, 3 * part), f32)],
        compiler_params=params(22),
        cost_estimate=cost(12 * seq * depth * 12 * part, seq * depth * 40, seq * 6 * part),
        name="feed",
    )(where, spots, h2, h2t, up, upt, *halves, bias, middle, vectors)


def middle_back_body(
    where_ref,
    lengths_ref,
    back_ref,
    unit_ref,
    inverse_ref,
    up_ref,
    o_ref,
    w_ref,
    vec_ref,
    grad_ref,
    mixture_ref,
    weight_ref,
    sums_ref,
    turned_ref,
):
    length = lengths_ref[where_ref[2]]
    sums = jnp.zeros(sums_ref.shape, f32)
    for tile in range(back_ref.shape[0] // TILE):
        at = slice(tile * TILE, (tile + 1) * TILE)
        unit, inverse = unit_ref[at, :].astype(f32), inverse_ref[at, 0:1]
        back = back_ref[at, :].astype(f32)
        up = up_ref[at, :].astype(f32)
        grad = up + pull_norm(back * vec_ref[2:3, :], unit, inverse)
        rounded = grad.astype(low)
        grad_ref[at, :] = rounded
        turned_ref[:, at] = rounded.T
        row = tile * TILE + lax.broadcasted_iota(jnp.int32, grad.shape, 0)
        mixture_ref[at, :] = jnp.where(row < length, mm(rounded, w_ref[...]), 0.0).astype(low)
        sums = sums + jnp.concatenate(
            [columns_of(back * unit), columns_of(back), columns_of(grad), columns_of(up)], axis=0
        )
    sums_ref[...] = sums
    weight_ref[...] = mm(turned_ref[...], o_ref[...]).astype(low)


def middle_back(where, lengths, back, unit, inverse, up, o, wide_out, vectors):
    seq, depth = unit.shape
    return pl.pallas_call(
        middle_back_body,
        in_specs=[SCALARS] * 2 + [NEAR] * 7,
        out_specs=[NEAR] * 4,
        scratch_shapes=[pltpu.VMEM((depth, seq), low)],
        out_shape=[
            sds((seq, depth), low),
            sds((seq, depth), low),
            sds((depth, depth), low),
            sds((4, depth), f32),
        ],
        compiler_params=params(14),
        cost_estimate=cost(4 * seq * depth * depth, seq * depth * 28),
        name="middle_back",
    )(where, lengths, back, unit, inverse, up, o, wide_out, vectors)


def input_grad_body(
    where_ref,
    spots_ref,
    ht_ref,
    back_ref,
    out_grad_ref,
    middle_ref,
    bias_ref,
    keep_ref,
    send_ref,
    sums_ref,
):
    rows = keep_ref.shape[1]
    width = keep_ref.shape[2] // 4
    groups = ht_ref.shape[0] // rows

    def spread(targets, index, grad):
        at = slice(index * width, (index + 1) * width)
        for group in range(groups):
            for model in range(4):
                targets[model % 2][spots_ref[model, group], :, at] = grad[
                    group * rows : (group + 1) * rows, model * width : (model + 1) * width
                ]

    sums_ref[:2] = jnp.zeros((2, sums_ref.shape[1]), f32)
    sums_ref[2:6] = middle_ref[...]
    sums_ref[6:7] = columns_of(back_ref[0].astype(f32))
    sums_ref[7:8] = columns_of(back_ref[2].astype(f32))
    sums_ref[8:] = bias_ref[...]
    for index in range(4):
        grad = mm(ht_ref[...], back_ref[index]).astype(low) if index < 3 else out_grad_ref[...]
        for core in range(2):

            @pl.when(where_ref[0] == core)
            def _(core=core, index=index, grad=grad):
                spread((keep_ref, send_ref) if core == 0 else (send_ref, keep_ref), index, grad)


def input_grad(where, spots, ht, back, out_grad, sums, slots, rows, after):
    depth, seq = ht.shape
    shape = (slots, rows, depth)
    return pl.pallas_call(
        held_back(input_grad_body, 7, len(after)),
        in_specs=[SCALARS] * 2 + [NEAR] * 5 + [LATER] * len(after),
        out_specs=[NEAR] * 3,
        out_shape=[sds(shape, low), sds(shape, low), sds((12, depth), f32)],
        compiler_params=params(14),
        cost_estimate=cost(6 * seq * depth * depth, seq * depth * 14),
        name="input_grad",
    )(where, spots, ht, back, out_grad, *sums, *after)


def token_back_body(
    back_ref, w_ref, x_ref, grad_ref, vec_ref, token_ref, sums_ref
):
    step = pl.program_id(0)
    back = mm_nt(back_ref[0], w_ref[0]) + mm_nt(back_ref[1], w_ref[1]) + mm_nt(back_ref[2], w_ref[2])
    unit, inverse = normalize(x_ref[...].astype(f32))
    grad = grad_ref[...].astype(f32)
    token_ref[...] = (grad + pull_norm(back * vec_ref[0:1, :], unit, inverse)).astype(low)
    sums = jnp.concatenate([columns_of(back * unit), columns_of(back)], axis=0)

    @pl.when(step == 0)
    def _():
        sums_ref[...] = sums

    @pl.when(step > 0)
    def _():
        sums_ref[...] += sums


def token_back(back, wide, x, grad, vectors, after):
    seq, depth = x.shape
    rows = pl.BlockSpec((TILE, depth), lambda i: (i, 0))
    return pl.pallas_call(
        held_back(token_back_body, 5, len(after)),
        grid=(seq // TILE,),
        in_specs=[
            pl.BlockSpec((3, TILE, depth), lambda i: (0, i, 0)),
            pl.BlockSpec((3, depth, depth), lambda i: (0, 0, 0)),
            rows,
            rows,
            once(vectors.shape),
        ]
        + [LATER] * len(after),
        out_specs=[rows, whole((2, depth))],
        out_shape=[sds((seq, depth), low), sds((2, depth), f32)],
        compiler_params=params(24),
        cost_estimate=cost(6 * seq * depth * depth, seq * depth * 16),
        name="token_back",
    )(back, *from_far(wide, x), grad, vectors, *after)


CORE_ORDERS = ((4, 3, 2, 1), (3, 4, 1, 2))
LATE_ORDERS = ((2, 1, 4, 3), (1, 2, 3, 4))
STAGES = 4


def cube_permute(values, stage, orders=CORE_ORDERS):
    pairs = [(device, device ^ (1 << orders[device & 1][stage])) for device in range(32)]
    return lax.ppermute(values, ("dp", "mp"), pairs)


def bit_permute(values, bit):
    return lax.ppermute(values, ("dp", "mp"), [(device, device ^ (1 << bit)) for device in range(32)])


def place(distance, core, orders):
    spots = [
        sum(((distance >> bit) & 1) << step for step, bit in enumerate(order)) for order in orders
    ]
    return jnp.where(core == 0, spots[0], spots[1])


def joined(held, arrived):
    return jnp.concatenate([held, arrived], axis=0)


def leaving(parts, stage):
    half = 1 << stage
    return sum(part[half:].astype(f32) for part in parts).astype(low)


def staying(parts, stage):
    return [part[: 1 << stage] for part in parts]


def summed(parts):
    return sum(part[0].astype(f32) for part in parts)


def two_parts(values):
    high = lax.reduce_precision(values, 8, 7)
    rest = lax.reduce_precision(values - high, 8, 7)
    return jnp.concatenate([high, rest], axis=0).astype(low)


def one_part(parts):
    half = parts.shape[0] // 2
    return parts[:half].astype(f32) + parts[half:].astype(f32)


def with_rider(blocks, rider, send):
    count, rows, columns = blocks.shape
    parts = two_parts(rider)
    message = jnp.concatenate([blocks.reshape(count * rows, columns), parts], axis=0)
    arrived = send(message)
    total = one_part(parts) + one_part(arrived[count * rows :])
    return arrived[: count * rows].reshape(count, rows, columns), total, message


def cube_sum(values, bits=range(5)):
    for bit in bits:
        values = values + bit_permute(values, bit)
    return values


def adam_parts(weight, gradient, first_old, second_old, factor, step_rate):
    scaled = gradient * factor
    moment = beta_one * first_old + (1.0 - beta_one) * scaled
    square = beta_two * second_old + (1.0 - beta_two) * scaled * scaled
    spread = jnp.sqrt(square * (1.0 / (1.0 - beta_two**STEP)))
    ratio = moment * (1.0 / (1.0 - beta_one**STEP)) / (spread + adam_eps)
    return moment, square, weight - step_rate * (ratio + decay * weight)


def optimize_body(where_ref, owned_ref, vector_ref, attend_ref, feed_a, feed_b, *refs):
    state, outs = refs[:21], refs[21:]
    vectors = jnp.concatenate([owned_ref[:2], vector_ref[2:]], axis=0)
    total = owned_ref[2:3, 0:1] + jnp.sum(vectors * vectors)
    norm = jnp.sqrt(total)
    factor = clip_norm / jnp.maximum(norm, clip_norm)
    outs[0][...] = norm
    width = state[0].shape[2]
    part = state[6].shape[1] // 3

    def update(param, at, gradient, step_rate):
        weight, first, second = (ref[at] for ref in state[3 * param : 3 * param + 3])
        results = adam_parts(weight, gradient, first, second, factor, step_rate)
        for ref, result in zip(outs[1 + 3 * param : 4 + 3 * param], results):
            ref[at] = result

    for index in range(3):
        update(0, (index,), attend_ref[:, index * width : (index + 1) * width], rate)
    update(1, (...,), attend_ref[:, 3 * width :].T, rate)
    split, rows = feed_a.shape[0], state[6].shape[0]
    for feed_ref, within in ((feed_a, slice(0, split)), (feed_b, slice(split, rows))):
        for index in range(3):
            at = (within, slice(index * part, (index + 1) * part))
            first = 2 * index * part
            update(2, at, feed_ref[:, first : first + part], rate)
            update(3, at, feed_ref[:, first + part : first + 2 * part], rate)
    update(4, (...,), vectors[:6], vector_rate)
    model = where_ref[2]
    head = jnp.zeros((2, width), f32)
    for index in range(4):
        head = head + jnp.where(model == index, vectors[6:8, index * width : (index + 1) * width], 0.0)
    update(5, (...,), head, vector_rate)
    bias = vector_ref[pl.ds(8 + model, 1), :]
    bias = jnp.concatenate([bias[:, at : at + 128] for at in range(0, bias.shape[1], 128)], axis=0)
    update(6, (...,), bias, vector_rate)


def bring_body(*refs):
    half = len(refs) // 2
    for source, target in zip(refs[:half], refs[half:]):
        target[...] = source[...]


def bring(arrays, after):
    return pl.pallas_call(
        lambda *refs: bring_body(*refs[: len(arrays)], *refs[len(arrays) + len(after) :]),
        in_specs=[NEAR] * len(arrays) + [LATER] * len(after),
        out_specs=[NEAR] * len(arrays),
        out_shape=[sds(array.shape, f32) for array in arrays],
        compiler_params=params(8),
        cost_estimate=cost(4e6, 6e6),
        name="bring",
    )(*from_far(*arrays), *after)


def last_sum_body(*refs):
    parts, (early_ref, late_ref, token_ref, total_ref, owned_ref) = refs[:-5], refs[-5:]
    total = sum(part[0].astype(f32) for part in parts)
    total_ref[...] = total
    squares = sum(jnp.sum(values * values) for values in (total, early_ref[...], late_ref[...]))
    owned_ref[:2, :] = token_ref[...]
    owned_ref[2:, :] = jnp.full((1, owned_ref.shape[1]), squares, f32)


def last_sum(parts, early_total, late_total, token_sums):
    _, rows, columns = parts[0].shape
    return pl.pallas_call(
        last_sum_body,
        in_specs=[NEAR] * (len(parts) + 3),
        out_specs=[NEAR] * 2,
        out_shape=[sds((rows, columns), f32), sds((3, columns), f32)],
        compiler_params=params(8),
        cost_estimate=cost(0, 0),
        name="last_sum",
    )(*parts, early_total, late_total, token_sums)


def optimize(where, owned, vector_total, attend_total, feed_totals, arrays):
    shapes = [sds(array.shape, f32) for array in arrays]
    return pl.pallas_call(
        optimize_body,
        in_specs=[pl.BlockSpec(memory_space=pltpu.SMEM)]
        + [pl.BlockSpec(memory_space=pltpu.VMEM)] * (5 + len(arrays)),
        out_shape=[sds((1, 1), f32)] + shapes,
        compiler_params=params(20),
        cost_estimate=cost(4e6, 8e6),
        name="optimize",
    )(where, owned, vector_total, attend_total, *feed_totals, *arrays)


def shards(
    tokens,
    cotangent,
    lengths,
    input_weight,
    output_weight,
    expand_weight,
    shrink_weight,
    layer_vectors,
    head_bias,
    expand_bias,
    first_input,
    first_output,
    first_expand,
    first_shrink,
    first_vectors,
    first_head,
    first_bias,
    second_input,
    second_output,
    second_expand,
    second_shrink,
    second_vectors,
    second_head,
    second_bias,
):
    dp_count = lax.axis_size("dp")
    mp_count = lax.axis_size("mp")
    cube = dp_count == 8 and mp_count == 4
    rows = input_weight.shape[0]
    width = input_weight.shape[2]
    hidden = expand_weight.shape[1]
    seq, depth = tokens.shape
    part = hidden // 3
    model_index = lax.axis_index("mp")
    me = lax.axis_index("dp") * mp_count + model_index

    attend_shard, feed_shard, bias_full = pack(
        input_weight.transpose(1, 0, 2),
        output_weight,
        expand_weight,
        shrink_weight.T,
        head_bias,
        expand_bias.reshape(hidden // 128, 128),
    )
    if cube:
        core, near = me & 1, model_index
        devices = jnp.arange(32).reshape(8, 4).T
        spots = jnp.concatenate(
            [place(devices ^ me, devices & 1, orders) for orders in (CORE_ORDERS, LATE_ORDERS)]
        ).astype(jnp.int32)
    else:
        core = near = jnp.zeros((), jnp.int32)
        spots = (jnp.arange(8)[:, None] % 4 // 2 * 8 + jnp.arange(8)[None]).astype(jnp.int32)
    where = jnp.stack([core, near, model_index]).astype(jnp.int32)

    def turned(array):
        return array.transpose(1, 0, 2)

    state = (
        (turned(input_weight), turned(first_input), turned(second_input)),
        (output_weight, first_output, second_output),
        (expand_weight, first_expand, second_expand),
        (shrink_weight.T, first_shrink.T, second_shrink.T),
        (layer_vectors, first_vectors, second_vectors),
        (head_bias, first_head, second_head),
        tuple(array.reshape(hidden // 128, 128) for array in (expand_bias, first_bias, second_bias)),
    )
    arrays = [array for group in state for array in group]

    if cube:
        split = rows * 2 // 3
        held, early, late = attend_shard[None], feed_shard[None, :split], feed_shard[None, split:]
        arrived, far_late = cube_permute(held, 0), cube_permute(late, 0, LATE_ORDERS)
        held, bias_full = lax.optimization_barrier((joined(held, arrived), bias_full))
        arrived = cube_permute(held, 1)
        bias_full = bias_full + bit_permute(bias_full, 0)
        late = joined(late, far_late)
        normed, normed_t, upstream_t = prepare(tokens, cotangent, layer_vectors, (held, late))
        late = joined(late, cube_permute(late, 1, LATE_ORDERS))
        held, early, late, normed, bias_full, spots, where = lax.optimization_barrier(
            (held, early, late, normed, bias_full, spots, where)
        )
        held, early = lax.optimization_barrier((joined(held, arrived), early))
        arrived, far_early = cube_permute(held, 2), cube_permute(early, 0)
        bias_full = bias_full + bit_permute(bias_full, 1)
        held, early = joined(held, arrived), joined(early, far_early)
        held, early, bias_full = lax.optimization_barrier((held, early, bias_full))
        far, far_early = cube_permute(held, 3), cube_permute(early, 1)
        twin = bit_permute(held, 0)
        early = joined(early, far_early)
        far, early, late = lax.optimization_barrier((far, early, late))
        attend_halves = (held, far, twin, bit_permute(far, 0))
        far_early, far_late = cube_permute(early, 2), cube_permute(late, 2, LATE_ORDERS)
        qkv, wide, wide_out = project(where, spots, normed, attend_halves, bias_full, ())
        far_early, far_late, qkv = lax.optimization_barrier((far_early, far_late, qkv))
        early, late = joined(early, far_early), joined(late, far_late)
        far_early, far_late = cube_permute(early, 3), cube_permute(late, 3, LATE_ORDERS)
        twin_early, twin_late = bit_permute(early, 0), bit_permute(late, 0)
        mixture, log_totals = attend_forward(where, lengths, qkv, (early, late))
        far_early, far_late, twin_late, mixture = lax.optimization_barrier(
            (far_early, far_late, twin_late, mixture)
        )
        last_early, last_late = bit_permute(far_early, 0), bit_permute(far_late, 0)
        middle, hidden_in, hidden_t, unit, inverse = attend_out(mixture, wide_out, tokens, layer_vectors)
        feed_halves = (early, far_early, twin_early, last_early, late, far_late, twin_late, last_late)
    else:

        def planes(shard):
            full = lax.all_gather(lax.all_gather(shard, "dp", axis=0, tiled=True), "mp", axis=0)
            full = full.reshape(2, 2, 8, depth // 8, shard.shape[1]).transpose(1, 0, 2, 3, 4)
            return tuple(full.reshape(4, 8, depth // 8, shard.shape[1]))

        normed, normed_t, upstream_t = prepare(tokens, cotangent, layer_vectors, ())
        bias_full = lax.psum(bias_full, "mp")
        qkv, wide, wide_out = project(where, spots, normed, planes(attend_shard), bias_full, ())
        mixture, log_totals = attend_forward(where, lengths, qkv, ())
        middle, hidden_in, hidden_t, unit, inverse = attend_out(mixture, wide_out, tokens, layer_vectors)
        split = depth // 8 * 2 // 3
        feed_planes = planes(feed_shard)
        feed_halves = tuple(array[:, :split] for array in feed_planes) + tuple(
            array[:, split:] for array in feed_planes
        )
    block_out, back, keep_early, send_early, keep_late, send_late, bias_grad = feed(
        where,
        spots,
        hidden_in,
        hidden_t,
        cotangent,
        upstream_t,
        feed_halves,
        bias_full,
        middle,
        layer_vectors,
    )
    middle_grad, mixture_grad, output_grad, middle_sums = middle_back(
        where, lengths, back, unit, inverse, cotangent, mixture, wide_out, layer_vectors
    )
    if cube:
        twin_early, twin_late = bit_permute(send_early[8:], 0), bit_permute(send_late[8:], 0)
        twin_early, twin_late, mixture_grad, send_early, send_late = lax.optimization_barrier(
            (twin_early, twin_late, mixture_grad, send_early, send_late)
        )
        away = (keep_early[8:].astype(f32) + twin_early.astype(f32)).astype(low)
        far_away_late = (keep_late[8:].astype(f32) + twin_late.astype(f32)).astype(low)
        early = [keep_early[:8], bit_permute(send_early[:8], 0)]
        late = [keep_late[:8], bit_permute(send_late[:8], 0)]
        packed_grad = attend_backward(
            where, lengths, qkv, mixture_grad, log_totals, (away, far_away_late)
        )
        early = early + [cube_permute(away, 3)]
        late = late + [cube_permute(far_away_late, 3, LATE_ORDERS)]
        early[0], late[0], packed_grad = lax.optimization_barrier((early[0], late[0], packed_grad))
        away, far_away_late = leaving(early, 2), leaving(late, 2)
        sums = (middle_sums, bias_grad)
        keep_attend, send_attend, rider = input_grad(
            where, spots, normed_t, packed_grad, output_grad, sums, 16, depth // 8, (away, far_away_late)
        )
        early = staying(early, 2) + [cube_permute(away, 2)]
        late = staying(late, 2) + [cube_permute(far_away_late, 2, LATE_ORDERS)]
        early[-1], late[-1], send_attend = lax.optimization_barrier((early[-1], late[-1], send_attend))
        twin_b, rider, _ = with_rider(send_attend[8:], rider, lambda values: bit_permute(values, 0))
        twin_a = bit_permute(send_attend[:8], 0)
        away = (keep_attend[8:].astype(f32) + twin_b.astype(f32)).astype(low)
        arrived, rider, message = with_rider(away, rider, lambda values: cube_permute(values, 3))
        attend_parts = [keep_attend[:8], twin_a, arrived]
        feed_away = leaving(early, 1)
        token_grad, token_sums = token_back(
            packed_grad, wide, tokens, middle_grad, layer_vectors, (message, feed_away)
        )
        early = staying(early, 1) + [cube_permute(feed_away, 1)]
        attend_parts[0], late[0], token_sums = lax.optimization_barrier(
            (attend_parts[0], late[0], token_sums)
        )
        feed_away = leaving(late, 1)
        late = staying(late, 1) + [cube_permute(feed_away, 1, LATE_ORDERS)]
        away = leaving(attend_parts, 2)
        arrived, rider, message = with_rider(away, rider, lambda values: cube_permute(values, 2))
        attend_parts = staying(attend_parts, 2) + [arrived]
        message, early[0], late[0] = lax.optimization_barrier((message, early[0], late[0]))
        feed_away = leaving(early, 0)
        early = staying(early, 0) + [cube_permute(feed_away, 0)]
        away = leaving(attend_parts, 1)
        arrived, rider, message = with_rider(away, rider, lambda values: cube_permute(values, 1))
        attend_parts = staying(attend_parts, 1) + [arrived]
        message, early[0], late[0] = lax.optimization_barrier((message, early[0], late[0]))
        early_total = summed(early)
        feed_away = leaving(late, 0)
        late = staying(late, 0) + [cube_permute(feed_away, 0, LATE_ORDERS)]
        arrays = list(bring(arrays, (message,)))
        attend_parts[0], arrays[0] = lax.optimization_barrier((attend_parts[0], arrays[0]))
        away = leaving(attend_parts, 0)
        away, early_total = lax.optimization_barrier((away, early_total))
        arrived, vector_total, _ = with_rider(away, rider, lambda values: cube_permute(values, 0))
        attend_parts = staying(attend_parts, 0) + [arrived]
        late_total = summed(late)
        feed_totals = (early_total, late_total)
        attend_total, owned = last_sum(attend_parts, early_total, late_total, token_sums)
        owned = cube_sum(owned)
    else:
        packed_grad = attend_backward(where, lengths, qkv, mixture_grad, log_totals, ())
        sums = (middle_sums, bias_grad)
        keep_attend, send_attend, vector_total = input_grad(
            where, spots, normed_t, packed_grad, output_grad, sums, 16, depth // 8, ()
        )
        token_grad, token_sums = token_back(packed_grad, wide, tokens, middle_grad, layer_vectors, ())
        vector_total = lax.psum(vector_total, ("dp", "mp"))

    if not cube:

        def own_block(keep, send):
            full = jnp.stack([keep, send]).reshape(2, 2, 8, keep.shape[1], keep.shape[2])
            full = full.transpose(1, 0, 2, 3, 4).reshape(4, 8 * keep.shape[1], keep.shape[2])
            full = lax.psum_scatter(full, "mp", scatter_dimension=0, tiled=False)
            return lax.psum(full, "dp")

        def own_rows(*blocks):
            full = jnp.concatenate([block.reshape(8, -1, block.shape[1]) for block in blocks], axis=1)
            full = full.reshape(depth, full.shape[2]).astype(f32)
            return lax.dynamic_slice_in_dim(full, lax.axis_index("dp") * rows, rows, 0)

        attend_total = own_rows(own_block(keep_attend, send_attend))
        feed_total = own_rows(own_block(keep_early, send_early), own_block(keep_late, send_late))
        feed_totals = feed_total[: rows * 2 // 3], feed_total[rows * 2 // 3 :]
        attend_total, owned = last_sum((attend_total[None],), *feed_totals, token_sums)
        owned = lax.psum(owned, ("dp", "mp"))
    grad_norm, *updates = optimize(where, owned, vector_total, attend_total, feed_totals, arrays)
    grad_norm = grad_norm[0, 0]
    moment_input, square_input, updated_input = (turned(array) for array in updates[:3])
    moment_output, square_output, updated_output = updates[3:6]
    moment_expand, square_expand, updated_expand = updates[6:9]
    moment_shrink, square_shrink, updated_shrink = (array.T for array in updates[9:12])
    moment_vectors, square_vectors, updated_vectors = updates[12:15]
    moment_head, square_head, updated_head = updates[15:18]
    moment_bias, square_bias, updated_bias = (array.reshape(hidden) for array in updates[18:])
    return (
        block_out,
        token_grad,
        grad_norm,
        moment_input,
        square_input,
        updated_input,
        moment_output,
        square_output,
        updated_output,
        moment_expand,
        square_expand,
        updated_expand,
        moment_shrink,
        square_shrink,
        updated_shrink,
        moment_vectors,
        square_vectors,
        updated_vectors,
        moment_head,
        square_head,
        updated_head,
        moment_bias,
        square_bias,
        updated_bias,
    )


def solution(mesh):
    in_specs = (
        P(("dp", "mp"), None),
        P(("dp", "mp"), None),
        P("dp"),
        P("dp", None, "mp"),
        P("mp", "dp"),
        P("dp", "mp"),
        P("mp", "dp"),
        P(),
        P(None, "mp"),
        P("mp"),
        P("dp", None, "mp"),
        P("mp", "dp"),
        P("dp", "mp"),
        P("mp", "dp"),
        P(),
        P(None, "mp"),
        P("mp"),
        P("dp", None, "mp"),
        P("mp", "dp"),
        P("dp", "mp"),
        P("mp", "dp"),
        P(),
        P(None, "mp"),
        P("mp"),
    )
    out_specs = (
        P(("dp", "mp"), None),
        P(("dp", "mp"), None),
        P(),
        P("dp", None, "mp"),
        P("dp", None, "mp"),
        P("dp", None, "mp"),
        P("mp", "dp"),
        P("mp", "dp"),
        P("mp", "dp"),
        P("dp", "mp"),
        P("dp", "mp"),
        P("dp", "mp"),
        P("mp", "dp"),
        P("mp", "dp"),
        P("mp", "dp"),
        P(),
        P(),
        P(),
        P(None, "mp"),
        P(None, "mp"),
        P(None, "mp"),
        P("mp"),
        P("mp"),
        P("mp"),
    )
    return jax.shard_map(shards, mesh=mesh, in_specs=in_specs, out_specs=out_specs, check_vma=False)
```

```python
import functools
import jax
import jax.numpy as jnp
from jax import lax
from jax.experimental import pallas as pl
from jax.experimental.pallas import tpu as pltpu
from jax.sharding import PartitionSpec as P

HEAD_DIM = 64
TILE = 256
STEP = 10

eps_norm = 1e-05
clip_norm = 1.0
beta_one = 0.9
beta_two = 0.999
adam_eps = 1e-08
rate = 0.05
vector_rate = 0.5
decay = 0.01
excluded = -1e30
low = jnp.bfloat16
f32 = jnp.float32
GELU_A = 0.7978845608028654
GELU_B = GELU_A * 0.044715


def params(limit_mib, **kw):
    return pltpu.CompilerParams(vmem_limit_bytes=limit_mib * 1024 * 1024, **kw)


def cost(flops, moved, special=0):
    return pl.CostEstimate(flops=int(flops), bytes_accessed=int(moved), transcendentals=int(special))


def mm(a, b):
    return jnp.dot(a, b, preferred_element_type=f32)


def mm_nt(a, b):
    return lax.dot_general(a, b, (((1,), (1,)), ((), ())), preferred_element_type=f32)


def whole(shape):
    zeros = (0,) * len(shape)
    return pl.BlockSpec(shape, lambda *_: zeros)


def once(shape):
    zeros = (0,) * len(shape)
    return pl.BlockSpec(shape, lambda *_: zeros, pipeline_mode=pl.Buffered(1))


def held_back(body, first, count):
    def run(*refs):
        return body(*refs[:first], *refs[first + count :])

    return run


LATER = pl.BlockSpec(memory_space=pl.ANY)


def far_away(shape, dtype):
    return pltpu.HBM(shape, dtype)


def from_far(*arrays):
    return [pltpu.with_memory_space_constraint(array, pltpu.HBM) for array in arrays]


def sds(shape, dtype):
    return jax.ShapeDtypeStruct(shape, dtype)


def live_blocks(length, count, body):
    for blocks in range(1, count + 1):
        low_end = (blocks - 1) * TILE
        high_end = blocks * TILE
        @pl.when((length > low_end) & (length <= high_end))
        def _(blocks=blocks):
            body(length, blocks)


PAIR = 2 * HEAD_DIM


def span(block):
    return slice(block * TILE, (block + 1) * TILE)


def both_heads(values):
    lane = lax.broadcasted_iota(jnp.int32, values.shape, 1)
    none = jnp.zeros_like(values)
    return jnp.concatenate(
        [jnp.where(lane < HEAD_DIM, values, none), jnp.where(lane >= HEAD_DIM, values, none)], axis=0
    )


def causal_mask():
    key_id = lax.broadcasted_iota(jnp.int32, (TILE, 2 * TILE), 0)
    query_id = lax.broadcasted_iota(jnp.int32, (TILE, 2 * TILE), 1) & (TILE - 1)
    return key_id <= query_id


def forward_body(where_ref, lengths_ref, q_ref, k_ref, v_ref, o_ref, lse_ref, vt_ref):
    seq = q_ref.shape[0]
    vt_ref[...] = v_ref[...].T
    causal = causal_mask()

    def run(length, blocks):
        def scores(b):
            q = q_ref[span(b), :] * jnp.asarray(HEAD_DIM**-0.5, low)
            return mm_nt(k_ref[: (b + 1) * TILE, :], both_heads(q))

        now = scores(0)
        for b in range(blocks):
            start, stop = b * TILE, (b + 1) * TILE
            later = scores(b + 1) if b + 1 < blocks else None
            last = jnp.where(causal, now[start:, :], excluded)
            top = jnp.max(last, axis=0, keepdims=True)
            if b:
                top = jnp.maximum(top, jnp.max(now[:start], axis=0, keepdims=True))
            p = jnp.exp(last - top)
            total = jnp.sum(p, axis=0, keepdims=True)
            pb = p.astype(low)
            if b:
                pf = jnp.exp(now[:start] - top)
                total = total + jnp.sum(pf, axis=0, keepdims=True)
                pb = jnp.concatenate([pf.astype(low), pb], axis=0)
            inverse = 1.0 / total
            lse = top + jnp.log(total)
            outs = []
            for h in range(2):
                at = slice(h * TILE, (h + 1) * TILE)
                out = mm(vt_ref[h * HEAD_DIM : (h + 1) * HEAD_DIM, :stop], pb[:, at])
                outs.append(out * inverse[:, at])
                lse_ref[0, h : h + 1, start:stop] = lse[:, at]
            both = jnp.concatenate(outs, axis=0).T
            row = start + lax.broadcasted_iota(jnp.int32, both.shape, 0)
            o_ref[start:stop, :] = jnp.where(row < length, both, 0.0).astype(low)
            now = later
        if blocks * TILE < seq:
            o_ref[blocks * TILE :, :] = jnp.zeros((seq - blocks * TILE, PAIR), low)
            lse_ref[0, :, blocks * TILE :] = jnp.zeros((2, seq - blocks * TILE), f32)

    live_blocks(lengths_ref[where_ref[2]], seq // TILE, run)


def attend_forward(where, lengths, qkv, after):
    seq, width = qkv.shape[0], qkv.shape[1] // 3
    pair = 2 * HEAD_DIM
    pairs = width // pair
    half = seq * seq * 5 // 8
    spec = lambda part: pl.BlockSpec((seq, pair), lambda i, *_: (0, part * pairs + i))
    return pl.pallas_call(
        held_back(forward_body, 5, len(after)),
        grid_spec=pltpu.PrefetchScalarGridSpec(
            num_scalar_prefetch=2,
            grid=(pairs,),
            in_specs=[spec(0), spec(1), spec(2)] + [LATER] * len(after),
            out_specs=[
                pl.BlockSpec((seq, pair), lambda i, *_: (0, i)),
                pl.BlockSpec((1, 2, seq), lambda i, *_: (i, 0, 0)),
            ],
            scratch_shapes=[pltpu.VMEM((pair, seq), low)],
        ),
        out_shape=[sds((seq, width), low), far_away((pairs, 2, seq), f32)],
        compiler_params=params(20),
        cost_estimate=cost(pairs * 2 * half * 2 * 2 * 256, seq * width * 8, pairs * 2 * half),
        name="attend_forward",
    )(where, lengths, *from_far(qkv, qkv, qkv), *after)


def backward_body(where_ref, lengths_ref, q_ref, k_ref, v_ref, do_ref, lse_ref, out_ref, kt_ref, ksum, vsum):
    seq = q_ref.shape[0]
    scale = HEAD_DIM**-0.5
    kt_ref[...] = k_ref[...].T
    causal = causal_mask()

    def run(length, blocks):
        def scores(b):
            qq = both_heads(q_ref[span(b), :] * jnp.asarray(scale, low))
            uu = both_heads(do_ref[span(b), :])
            stop = (b + 1) * TILE
            return qq, uu, mm_nt(k_ref[:stop, :], qq), mm_nt(v_ref[:stop, :], uu)

        now = scores(blocks - 1)
        for b in reversed(range(blocks)):
            start, stop = b * TILE, (b + 1) * TILE
            later = scores(b - 1) if b else None
            qq, uu, s, dp = now
            lse = jnp.concatenate([lse_ref[0, 0:1, start:stop], lse_ref[0, 1:2, start:stop]], axis=1)
            p = jnp.exp(jnp.where(causal, s[start:], excluded) - lse)
            inner = jnp.sum(p * dp[start:], axis=0, keepdims=True)
            if b:
                pf = jnp.exp(s[:start] - lse)
                inner = inner + jnp.sum(pf * dp[:start], axis=0, keepdims=True)
            ds = (p * (dp[start:] - inner)).astype(low)
            pb = p.astype(low)
            if b:
                ds = jnp.concatenate([(pf * (dp[:start] - inner)).astype(low), ds], axis=0)
                pb = jnp.concatenate([pf.astype(low), pb], axis=0)
            dk, dv = mm(ds, qq), mm(pb, uu)
            if b == blocks - 1:
                ksum[:stop, :] = dk
                vsum[:stop, :] = dv
            else:
                ksum[:stop, :] += dk
                vsum[:stop, :] += dv
            dq = jnp.concatenate(
                [
                    mm(
                        kt_ref[h * HEAD_DIM : (h + 1) * HEAD_DIM, :stop],
                        ds[:, h * TILE : (h + 1) * TILE],
                    )
                    for h in range(2)
                ],
                axis=0,
            )
            out_ref[1, start:stop, :] = ksum[start:stop, :].astype(low)
            out_ref[2, start:stop, :] = vsum[start:stop, :].astype(low)
            out_ref[0, start:stop, :] = (dq.T * scale).astype(low)
            now = later
        if blocks * TILE < seq:
            rest = jnp.zeros((seq - blocks * TILE, PAIR), low)
            for part in range(3):
                out_ref[part, blocks * TILE :, :] = rest

    live_blocks(lengths_ref[where_ref[2]], seq // TILE, run)


def attend_backward(where, lengths, qkv, upstream, lse, after):
    seq, width = upstream.shape
    pair = 2 * HEAD_DIM
    pairs = width // pair
    half = seq * seq * 5 // 8
    spec = lambda part: pl.BlockSpec((seq, pair), lambda i, *_: (0, part * pairs + i))
    own = pl.BlockSpec((seq, pair), lambda i, *_: (0, i))
    return pl.pallas_call(
        held_back(backward_body, 7, len(after)),
        grid_spec=pltpu.PrefetchScalarGridSpec(
            num_scalar_prefetch=2,
            grid=(pairs,),
            in_specs=[spec(0), spec(1), spec(2), own, pl.BlockSpec((1, 2, seq), lambda i, *_: (i, 0, 0))]
            + [LATER] * len(after),
            out_specs=pl.BlockSpec((3, seq, pair), lambda i, *_: (0, 0, i)),
            scratch_shapes=[
                pltpu.VMEM((pair, seq), low),
                pltpu.VMEM((seq, pair), f32),
                pltpu.VMEM((seq, pair), f32),
            ],
        ),
        out_shape=sds((3, seq, width), low),
        compiler_params=params(28),
        cost_estimate=cost(pairs * 2 * half * 5 * 2 * 256, seq * width * 14, pairs * 2 * half),
        name="attend_backward",
    )(where, lengths, *from_far(qkv, qkv, qkv), upstream, *from_far(lse), *after)


def normalize(values):
    average = jnp.mean(values, axis=-1, keepdims=True)
    centred = values - average
    inverse = lax.rsqrt(jnp.mean(centred * centred, axis=-1, keepdims=True) + eps_norm)
    return centred * inverse, inverse


def pull_norm(scaled, unit, inverse):
    first = jnp.mean(scaled, axis=-1, keepdims=True)
    second = jnp.mean(scaled * unit, axis=-1, keepdims=True)
    return inverse * (scaled - first - unit * second)


def columns_of(values):
    return jnp.sum(values, axis=0, keepdims=True)


def pack_body(
    input_ref, output_ref, expand_ref, shrink_ref, head_ref, hidden_ref, attend_ref, feed_ref, bias_ref
):
    width = input_ref.shape[2]
    part = expand_ref.shape[1] // 3
    for index in range(3):
        attend_ref[:, index * width : (index + 1) * width] = input_ref[index].astype(low)
        at = slice(index * part, (index + 1) * part)
        feed_ref[:, 2 * index * part : (2 * index + 1) * part] = expand_ref[:, at].astype(low)
        feed_ref[:, (2 * index + 1) * part : (2 * index + 2) * part] = shrink_ref[:, at].astype(low)
    attend_ref[:, 3 * width :] = output_ref[...].T.astype(low)
    pieces = [head_ref[0:1, :], head_ref[1:2, :]]
    pieces += [hidden_ref[row : row + 1, :] for row in range(hidden_ref.shape[0])]
    bias_ref[...] = jnp.zeros_like(bias_ref)
    bias_ref[pl.ds(lax.axis_index("mp"), 1), :] = jnp.concatenate(pieces, axis=1)


def pack(input_weight, output_weight, expand, shrink, head_bias, hidden_bias):
    rows, width = input_weight.shape[1:]
    hidden = expand.shape[1]
    return pl.pallas_call(
        pack_body,
        out_shape=[
            sds((rows, 4 * width), low),
            sds((rows, 2 * hidden), low),
            sds((4, 2 * width + hidden), f32),
        ],
        compiler_params=params(6),
        cost_estimate=cost(rows * hidden, rows * hidden * 18),
        name="pack",
    )(*from_far(input_weight, output_weight, expand, shrink, head_bias, hidden_bias))


def prepare_body(x_ref, up_ref, vec_ref, h_ref, ht_ref, upt_ref):
    unit, _ = normalize(x_ref[...].astype(f32))
    h = (unit * vec_ref[0:1, :] + vec_ref[1:2, :]).astype(low)
    h_ref[...] = h
    ht_ref[...] = h.T
    upt_ref[...] = up_ref[...].T


def prepare(x, up, vectors, after):
    seq, depth = x.shape
    rows = pl.BlockSpec((2 * TILE, depth), lambda i: (i, 0))
    turned = pl.BlockSpec((depth, 2 * TILE), lambda i: (0, i))
    return pl.pallas_call(
        held_back(prepare_body, 3, len(after)),
        grid=(seq // (2 * TILE),),
        in_specs=[rows, rows, once(vectors.shape)] + [LATER] * len(after),
        out_specs=[rows, turned, turned],
        out_shape=[sds((seq, depth), low), sds((depth, seq), low), far_away((depth, seq), low)],
        compiler_params=params(16),
        cost_estimate=cost(seq * depth * 10, seq * depth * 10),
        name="prepare",
    )(*from_far(x, up), vectors, *after)


def slot(halves, spot, at):
    first, second = halves
    inner = spot & 7
    return jnp.where(spot < 8, first[inner, :, at], second[inner, :, at])


def project_body(
    where_ref, spots_ref, h_ref, mine_a, mine_b, twin_a, twin_b, bias_ref, qkv_ref, wide_ref, last_ref
):
    part = pl.program_id(0)
    rows = mine_a.shape[1]
    width = mine_a.shape[2] // 4
    groups = wide_ref.shape[1] // rows

    def collect(sources, index):
        columns = slice(index * width, (index + 1) * width)
        for group in range(groups):
            pieces = [slot(sources[model % 2], spots_ref[model, group], columns) for model in range(4)]
            at = slice(group * rows, (group + 1) * rows)
            if index < 3:
                wide_ref[0, at, :] = jnp.concatenate(pieces, axis=1)
            else:
                last_ref[at, :] = jnp.concatenate(pieces, axis=1)

    for index in range(4):
        for core in range(2):

            @pl.when((part == index) & (where_ref[0] == core))
            def _(index=index, core=core):
                mine, twin = (mine_a, mine_b), (twin_a, twin_b)
                collect((mine, twin) if core == 0 else (twin, mine), index)

    for index in range(3):

        @pl.when(part == index)
        def _(index=index):
            out = mm(h_ref[...], wide_ref[0])
            if index != 1:
                at = slice(index // 2 * width, (index // 2 + 1) * width)
                bias = jnp.concatenate([bias_ref[model : model + 1, at] for model in range(4)], axis=1)
                out = out + bias
            qkv_ref[...] = out.astype(low)


def project(where, spots, h, halves, bias, after):
    seq, depth = h.shape
    return pl.pallas_call(
        held_back(project_body, 8, len(after)),
        grid_spec=pltpu.PrefetchScalarGridSpec(
            num_scalar_prefetch=2,
            grid=(4,),
            in_specs=[
                once((seq, depth)),
                *[once(halves[0].shape)] * 4,
                once(bias.shape),
            ]
            + [LATER] * len(after),
            out_specs=[
                pl.BlockSpec((seq, depth), lambda i, *_: (0, jnp.minimum(i, 2))),
                pl.BlockSpec((1, depth, depth), lambda i, *_: (jnp.minimum(i, 2), 0, 0)),
                whole((depth, depth)),
            ],
        ),
        out_shape=[
            far_away((seq, 3 * depth), low),
            far_away((3, depth, depth), low),
            sds((depth, depth), low),
        ],
        compiler_params=params(24),
        cost_estimate=cost(2 * seq * depth * depth * 3, seq * depth * 16),
        name="project",
    )(where, spots, h, *halves, bias, *after)


NEAR = pl.BlockSpec(memory_space=pltpu.VMEM)
SCALARS = pl.BlockSpec(memory_space=pltpu.SMEM)


def attend_out_body(o_ref, w_ref, x_ref, vec_ref, middle_ref, h_ref, ht_ref, unit_ref, inverse_ref):
    for tile in range(o_ref.shape[0] // TILE):
        at = slice(tile * TILE, (tile + 1) * TILE)
        middle = x_ref[at, :].astype(f32) + mm_nt(o_ref[at, :], w_ref[...]) + vec_ref[4:5, :]
        middle_ref[at, :] = middle.astype(low)
        unit, inverse = normalize(middle)
        unit_ref[at, :] = unit.astype(low)
        inverse_ref[at, :] = jnp.broadcast_to(inverse, (TILE, inverse_ref.shape[1]))
        h = (unit * vec_ref[2:3, :] + vec_ref[3:4, :]).astype(low)
        h_ref[at, :] = h
        ht_ref[:, at] = h.T


def attend_out(o, wide_out, x, vectors):
    seq, depth = x.shape
    return pl.pallas_call(
        attend_out_body,
        in_specs=[NEAR] * 4,
        out_specs=[NEAR] * 5,
        out_shape=[
            sds((seq, depth), low),
            sds((seq, depth), low),
            sds((depth, seq), low),
            sds((seq, depth), low),
            sds((seq, 128), f32),
        ],
        compiler_params=params(10),
        cost_estimate=cost(2 * seq * depth * depth, seq * depth * 14),
        name="attend_out",
    )(o, wide_out, x, vectors)


def feed_body(
    where_ref,
    spots_ref,
    h2_ref,
    h2t_ref,
    up_ref,
    upt_ref,
    mine_a,
    mine_b,
    twin_a,
    twin_b,
    mine_c,
    mine_d,
    twin_c,
    twin_d,
    bias_ref,
    middle_ref,
    vec_ref,
    block_ref,
    back_ref,
    keep_a,
    send_a,
    keep_b,
    send_b,
    bias_grad_ref,
    out_ref,
    sum_ref,
    wide_ref,
    act_ref,
    pre_ref,
):
    part = mine_a.shape[2] // 6
    groups = spots_ref.shape[1]
    rows = wide_ref.shape[0] // groups
    split = mine_a.shape[1]
    skip = bias_ref.shape[1] - bias_grad_ref.shape[1]
    pieces = (
        ((mine_a, mine_b), (twin_a, twin_b), 0, slice(0, split)),
        ((mine_c, mine_d), (twin_c, twin_d), 4, slice(split, rows)),
    )
    half = keep_a.shape[1]
    results = ((keep_a, send_a, 0, slice(0, half)), (keep_b, send_b, 4, slice(half, rows)))
    out_ref[...] = middle_ref[...].astype(f32) + vec_ref[5:6, :]
    sum_ref[...] = jnp.zeros_like(sum_ref)

    def step(index, carry):
        side = lax.rem(index, 2)
        first = pl.multiple_of(index // 2 * part, 128)
        lanes = pl.ds(pl.multiple_of(2 * first, 128), part)
        next_lanes = pl.ds(pl.multiple_of(2 * first + part, 128), part)
        models = [where_ref[1] ^ (2 * side + core) for core in range(2)]
        for group in range(groups):
            for mine, twin, table, within in pieces:
                at = slice(group * rows + within.start, group * rows + within.stop)
                for core, halves in enumerate((mine, twin)):
                    spot = spots_ref[table + models[core], group]
                    wide_ref[at, core * part : (core + 1) * part] = slot(halves, spot, lanes)
                    wide_ref[at, (2 + core) * part : (3 + core) * part] = slot(halves, spot, next_lanes)

        expand = wide_ref[:, : 2 * part]
        shrink = wide_ref[:, 2 * part :]
        bias = jnp.concatenate(
            [bias_ref[pl.ds(model, 1), pl.ds(pl.multiple_of(skip + first, 128), part)] for model in models],
            axis=1,
        )
        sums = jnp.zeros((1, 2 * part), f32)
        for tile in range(h2_ref.shape[0] // TILE):
            at = slice(tile * TILE, (tile + 1) * TILE)
            u = mm(h2_ref[at, :], expand) + bias
            square = u * u
            th = jnp.tanh(u * (GELU_A + GELU_B * square))
            gate = 0.5 * th + 0.5
            slope = gate + (gate * (1.0 - gate)) * (u * (2.0 * GELU_A + (6.0 * GELU_B) * square))
            pre = (mm(up_ref[at, :], shrink) * slope).astype(low)
            act_ref[at, :] = (u * gate).astype(low)
            pre_ref[at, :] = pre
            sums = sums + columns_of(pre.astype(f32))
        for core, model in enumerate(models):
            bias_grad_ref[pl.ds(model, 1), pl.ds(first, part)] = sums[:, core * part : (core + 1) * part]
        out_ref[...] += mm_nt(act_ref[...], shrink)
        sum_ref[...] += mm_nt(pre_ref[...], expand)
        grad_expand = mm(h2t_ref[...], pre_ref[...]).astype(low)
        grad_shrink = mm(upt_ref[...], act_ref[...]).astype(low)
        for group in range(groups):
            for keep, send, table, within in results:
                at = slice(group * rows + within.start, group * rows + within.stop)
                for core, target in enumerate((keep, send)):
                    spot = spots_ref[table + models[core], group]
                    columns = slice(core * part, (core + 1) * part)
                    target[spot, :, lanes] = grad_expand[at, columns]
                    target[spot, :, next_lanes] = grad_shrink[at, columns]
        return carry

    lax.fori_loop(0, 6, step, 0)
    block_ref[...] = out_ref[...].astype(low)
    back_ref[...] = sum_ref[...].astype(low)


def feed(where, spots, h2, h2t, up, upt, halves, bias, middle, vectors):
    seq, depth = h2.shape
    half, _, columns = halves[0].shape
    part = columns // 6
    splits = [halves[0].shape[1], halves[4].shape[1]]
    return pl.pallas_call(
        feed_body,
        in_specs=[SCALARS] * 2 + [NEAR] * 15,
        out_specs=[NEAR] * 7,
        scratch_shapes=[
            pltpu.VMEM((seq, depth), f32),
            pltpu.VMEM((seq, depth), f32),
            pltpu.VMEM((depth, 4 * part), low),
            pltpu.VMEM((seq, 2 * part), low),
            pltpu.VMEM((seq, 2 * part), low),
        ],
        out_shape=[sds((seq, depth), low)] * 2
        + [sds((2 * half, rows, columns), low) for rows in splits for _ in range(2)]
        + [sds((4, 3 * part), f32)],
        compiler_params=params(22),
        cost_estimate=cost(12 * seq * depth * 12 * part, seq * depth * 40, seq * 6 * part),
        name="feed",
    )(where, spots, h2, h2t, up, upt, *halves, bias, middle, vectors)


def middle_back_body(
    where_ref,
    lengths_ref,
    back_ref,
    unit_ref,
    inverse_ref,
    up_ref,
    o_ref,
    w_ref,
    vec_ref,
    grad_ref,
    mixture_ref,
    weight_ref,
    sums_ref,
    turned_ref,
):
    length = lengths_ref[where_ref[2]]
    sums = jnp.zeros(sums_ref.shape, f32)
    for tile in range(back_ref.shape[0] // TILE):
        at = slice(tile * TILE, (tile + 1) * TILE)
        unit, inverse = unit_ref[at, :].astype(f32), inverse_ref[at, 0:1]
        back = back_ref[at, :].astype(f32)
        up = up_ref[at, :].astype(f32)
        grad = up + pull_norm(back * vec_ref[2:3, :], unit, inverse)
        rounded = grad.astype(low)
        grad_ref[at, :] = rounded
        turned_ref[:, at] = rounded.T
        row = tile * TILE + lax.broadcasted_iota(jnp.int32, grad.shape, 0)
        mixture_ref[at, :] = jnp.where(row < length, mm(rounded, w_ref[...]), 0.0).astype(low)
        sums = sums + jnp.concatenate(
            [columns_of(back * unit), columns_of(back), columns_of(grad), columns_of(up)], axis=0
        )
    sums_ref[...] = sums
    weight_ref[...] = mm(turned_ref[...], o_ref[...]).astype(low)


def middle_back(where, lengths, back, unit, inverse, up, o, wide_out, vectors):
    seq, depth = unit.shape
    return pl.pallas_call(
        middle_back_body,
        in_specs=[SCALARS] * 2 + [NEAR] * 7,
        out_specs=[NEAR] * 4,
        scratch_shapes=[pltpu.VMEM((depth, seq), low)],
        out_shape=[
            sds((seq, depth), low),
            sds((seq, depth), low),
            sds((depth, depth), low),
            sds((4, depth), f32),
        ],
        compiler_params=params(14),
        cost_estimate=cost(4 * seq * depth * depth, seq * depth * 28),
        name="middle_back",
    )(where, lengths, back, unit, inverse, up, o, wide_out, vectors)


def input_grad_body(
    where_ref,
    spots_ref,
    ht_ref,
    back_ref,
    out_grad_ref,
    middle_ref,
    bias_ref,
    keep_ref,
    send_ref,
    sums_ref,
):
    rows = keep_ref.shape[1]
    width = keep_ref.shape[2] // 4
    groups = ht_ref.shape[0] // rows

    def spread(targets, index, grad):
        at = slice(index * width, (index + 1) * width)
        for group in range(groups):
            for model in range(4):
                targets[model % 2][spots_ref[model, group], :, at] = grad[
                    group * rows : (group + 1) * rows, model * width : (model + 1) * width
                ]

    sums_ref[:2] = jnp.zeros((2, sums_ref.shape[1]), f32)
    sums_ref[2:6] = middle_ref[...]
    sums_ref[6:7] = columns_of(back_ref[0].astype(f32))
    sums_ref[7:8] = columns_of(back_ref[2].astype(f32))
    sums_ref[8:] = bias_ref[...]
    for index in range(4):
        grad = mm(ht_ref[...], back_ref[index]).astype(low) if index < 3 else out_grad_ref[...]
        for core in range(2):

            @pl.when(where_ref[0] == core)
            def _(core=core, index=index, grad=grad):
                spread((keep_ref, send_ref) if core == 0 else (send_ref, keep_ref), index, grad)


def input_grad(where, spots, ht, back, out_grad, sums, slots, rows, after):
    depth, seq = ht.shape
    shape = (slots, rows, depth)
    return pl.pallas_call(
        held_back(input_grad_body, 7, len(after)),
        in_specs=[SCALARS] * 2 + [NEAR] * 5 + [LATER] * len(after),
        out_specs=[NEAR] * 3,
        out_shape=[sds(shape, low), sds(shape, low), sds((12, depth), f32)],
        compiler_params=params(14),
        cost_estimate=cost(6 * seq * depth * depth, seq * depth * 14),
        name="input_grad",
    )(where, spots, ht, back, out_grad, *sums, *after)


def token_back_body(
    back_ref, w_ref, x_ref, grad_ref, vec_ref, token_ref, sums_ref
):
    step = pl.program_id(0)
    back = mm_nt(back_ref[0], w_ref[0]) + mm_nt(back_ref[1], w_ref[1]) + mm_nt(back_ref[2], w_ref[2])
    unit, inverse = normalize(x_ref[...].astype(f32))
    grad = grad_ref[...].astype(f32)
    token_ref[...] = (grad + pull_norm(back * vec_ref[0:1, :], unit, inverse)).astype(low)
    sums = jnp.concatenate([columns_of(back * unit), columns_of(back)], axis=0)

    @pl.when(step == 0)
    def _():
        sums_ref[...] = sums

    @pl.when(step > 0)
    def _():
        sums_ref[...] += sums


def token_back(back, wide, x, grad, vectors, after):
    seq, depth = x.shape
    rows = pl.BlockSpec((TILE, depth), lambda i: (i, 0))
    return pl.pallas_call(
        held_back(token_back_body, 5, len(after)),
        grid=(seq // TILE,),
        in_specs=[
            pl.BlockSpec((3, TILE, depth), lambda i: (0, i, 0)),
            pl.BlockSpec((3, depth, depth), lambda i: (0, 0, 0)),
            rows,
            rows,
            once(vectors.shape),
        ]
        + [LATER] * len(after),
        out_specs=[rows, whole((2, depth))],
        out_shape=[sds((seq, depth), low), sds((2, depth), f32)],
        compiler_params=params(24),
        cost_estimate=cost(6 * seq * depth * depth, seq * depth * 16),
        name="token_back",
    )(back, *from_far(wide, x), grad, vectors, *after)


CORE_ORDERS = ((4, 3, 2, 1), (3, 4, 1, 2))
LATE_ORDERS = ((2, 1, 4, 3), (1, 2, 3, 4))
STAGES = 4


def cube_permute(values, stage, orders=CORE_ORDERS):
    pairs = [(device, device ^ (1 << orders[device & 1][stage])) for device in range(32)]
    return lax.ppermute(values, ("dp", "mp"), pairs)


def bit_permute(values, bit):
    return lax.ppermute(values, ("dp", "mp"), [(device, device ^ (1 << bit)) for device in range(32)])


def place(distance, core, orders):
    spots = [
        sum(((distance >> bit) & 1) << step for step, bit in enumerate(order)) for order in orders
    ]
    return jnp.where(core == 0, spots[0], spots[1])


def joined(held, arrived):
    return jnp.concatenate([held, arrived], axis=0)


def leaving(parts, stage):
    half = 1 << stage
    return sum(part[half:].astype(f32) for part in parts).astype(low)


def staying(parts, stage):
    return [part[: 1 << stage] for part in parts]


def summed(parts):
    return sum(part[0].astype(f32) for part in parts)


def two_parts(values):
    high = lax.reduce_precision(values, 8, 7)
    rest = lax.reduce_precision(values - high, 8, 7)
    return jnp.concatenate([high, rest], axis=0).astype(low)


def one_part(parts):
    half = parts.shape[0] // 2
    return parts[:half].astype(f32) + parts[half:].astype(f32)


def with_rider(blocks, rider, send):
    count, rows, columns = blocks.shape
    parts = two_parts(rider)
    message = jnp.concatenate([blocks.reshape(count * rows, columns), parts], axis=0)
    arrived = send(message)
    total = one_part(parts) + one_part(arrived[count * rows :])
    return arrived[: count * rows].reshape(count, rows, columns), total, message


def cube_sum(values, bits=range(5)):
    for bit in bits:
        values = values + bit_permute(values, bit)
    return values


def adam_parts(weight, gradient, first_old, second_old, factor, step_rate):
    scaled = gradient * factor
    moment = beta_one * first_old + (1.0 - beta_one) * scaled
    square = beta_two * second_old + (1.0 - beta_two) * scaled * scaled
    spread = jnp.sqrt(square * (1.0 / (1.0 - beta_two**STEP)))
    ratio = moment * (1.0 / (1.0 - beta_one**STEP)) / (spread + adam_eps)
    return moment, square, weight - step_rate * (ratio + decay * weight)


def optimize_body(where_ref, owned_ref, vector_ref, attend_ref, feed_a, feed_b, *refs):
    state, outs = refs[:21], refs[21:]
    vectors = jnp.concatenate([owned_ref[:2], vector_ref[2:]], axis=0)
    total = owned_ref[2:3, 0:1] + jnp.sum(vectors * vectors)
    norm = jnp.sqrt(total)
    factor = clip_norm / jnp.maximum(norm, clip_norm)
    outs[0][...] = norm
    width = state[0].shape[2]
    part = state[6].shape[1] // 3

    def update(param, at, gradient, step_rate):
        weight, first, second = (ref[at] for ref in state[3 * param : 3 * param + 3])
        results = adam_parts(weight, gradient, first, second, factor, step_rate)
        for ref, result in zip(outs[1 + 3 * param : 4 + 3 * param], results):
            ref[at] = result

    for index in range(3):
        update(0, (index,), attend_ref[:, index * width : (index + 1) * width], rate)
    update(1, (...,), attend_ref[:, 3 * width :].T, rate)
    split, rows = feed_a.shape[0], state[6].shape[0]
    for feed_ref, within in ((feed_a, slice(0, split)), (feed_b, slice(split, rows))):
        for index in range(3):
            at = (within, slice(index * part, (index + 1) * part))
            first = 2 * index * part
            update(2, at, feed_ref[:, first : first + part], rate)
            update(3, at, feed_ref[:, first + part : first + 2 * part], rate)
    update(4, (...,), vectors[:6], vector_rate)
    model = where_ref[2]
    head = jnp.zeros((2, width), f32)
    for index in range(4):
        head = head + jnp.where(model == index, vectors[6:8, index * width : (index + 1) * width], 0.0)
    update(5, (...,), head, vector_rate)
    bias = vector_ref[pl.ds(8 + model, 1), :]
    bias = jnp.concatenate([bias[:, at : at + 128] for at in range(0, bias.shape[1], 128)], axis=0)
    update(6, (...,), bias, vector_rate)


def bring_body(*refs):
    half = len(refs) // 2
    for source, target in zip(refs[:half], refs[half:]):
        target[...] = source[...]


def bring(arrays, after):
    return pl.pallas_call(
        lambda *refs: bring_body(*refs[: len(arrays)], *refs[len(arrays) + len(after) :]),
        in_specs=[NEAR] * len(arrays) + [LATER] * len(after),
        out_specs=[NEAR] * len(arrays),
        out_shape=[sds(array.shape, f32) for array in arrays],
        compiler_params=params(8),
        cost_estimate=cost(4e6, 6e6),
        name="bring",
    )(*from_far(*arrays), *after)


def last_sum_body(*refs):
    parts, (early_ref, late_ref, token_ref, total_ref, owned_ref) = refs[:-5], refs[-5:]
    total = sum(part[0].astype(f32) for part in parts)
    total_ref[...] = total
    squares = sum(jnp.sum(values * values) for values in (total, early_ref[...], late_ref[...]))
    owned_ref[:2, :] = token_ref[...]
    owned_ref[2:, :] = jnp.full((1, owned_ref.shape[1]), squares, f32)


def last_sum(parts, early_total, late_total, token_sums):
    _, rows, columns = parts[0].shape
    return pl.pallas_call(
        last_sum_body,
        in_specs=[NEAR] * (len(parts) + 3),
        out_specs=[NEAR] * 2,
        out_shape=[sds((rows, columns), f32), sds((3, columns), f32)],
        compiler_params=params(8),
        cost_estimate=cost(0, 0),
        name="last_sum",
    )(*parts, early_total, late_total, token_sums)


def optimize(where, owned, vector_total, attend_total, feed_totals, arrays):
    shapes = [sds(array.shape, f32) for array in arrays]
    return pl.pallas_call(
        optimize_body,
        in_specs=[pl.BlockSpec(memory_space=pltpu.SMEM)]
        + [pl.BlockSpec(memory_space=pltpu.VMEM)] * (5 + len(arrays)),
        out_shape=[sds((1, 1), f32)] + shapes,
        compiler_params=params(20),
        cost_estimate=cost(4e6, 8e6),
        name="optimize",
    )(where, owned, vector_total, attend_total, *feed_totals, *arrays)


def shards(
    tokens,
    cotangent,
    lengths,
    input_weight,
    output_weight,
    expand_weight,
    shrink_weight,
    layer_vectors,
    head_bias,
    expand_bias,
    first_input,
    first_output,
    first_expand,
    first_shrink,
    first_vectors,
    first_head,
    first_bias,
    second_input,
    second_output,
    second_expand,
    second_shrink,
    second_vectors,
    second_head,
    second_bias,
):
    dp_count = lax.axis_size("dp")
    mp_count = lax.axis_size("mp")
    cube = dp_count == 8 and mp_count == 4
    rows = input_weight.shape[0]
    width = input_weight.shape[2]
    hidden = expand_weight.shape[1]
    seq, depth = tokens.shape
    part = hidden // 3
    model_index = lax.axis_index("mp")
    me = lax.axis_index("dp") * mp_count + model_index

    attend_shard, feed_shard, bias_full = pack(
        input_weight.transpose(1, 0, 2),
        output_weight,
        expand_weight,
        shrink_weight.T,
        head_bias,
        expand_bias.reshape(hidden // 128, 128),
    )
    if cube:
        core, near = me & 1, model_index
        devices = jnp.arange(32).reshape(8, 4).T
        spots = jnp.concatenate(
            [place(devices ^ me, devices & 1, orders) for orders in (CORE_ORDERS, LATE_ORDERS)]
        ).astype(jnp.int32)
    else:
        core = near = jnp.zeros((), jnp.int32)
        spots = (jnp.arange(8)[:, None] % 4 // 2 * 8 + jnp.arange(8)[None]).astype(jnp.int32)
    where = jnp.stack([core, near, model_index]).astype(jnp.int32)

    def turned(array):
        return array.transpose(1, 0, 2)

    state = (
        (turned(input_weight), turned(first_input), turned(second_input)),
        (output_weight, first_output, second_output),
        (expand_weight, first_expand, second_expand),
        (shrink_weight.T, first_shrink.T, second_shrink.T),
        (layer_vectors, first_vectors, second_vectors),
        (head_bias, first_head, second_head),
        tuple(array.reshape(hidden // 128, 128) for array in (expand_bias, first_bias, second_bias)),
    )
    arrays = [array for group in state for array in group]

    if cube:
        split = rows * 2 // 3
        held, early, late = attend_shard[None], feed_shard[None, :split], feed_shard[None, split:]
        arrived, far_late = cube_permute(held, 0), cube_permute(late, 0, LATE_ORDERS)
        held, bias_full = lax.optimization_barrier((joined(held, arrived), bias_full))
        arrived = cube_permute(held, 1)
        bias_full = bias_full + bit_permute(bias_full, 0)
        normed, normed_t, upstream_t = prepare(tokens, cotangent, layer_vectors, (held,))
        late = joined(late, far_late)
        held, early, late, normed, bias_full, spots, where = lax.optimization_barrier(
            (held, early, late, normed, bias_full, spots, where)
        )
        held, early = lax.optimization_barrier((joined(held, arrived), early))
        arrived, far_early = cube_permute(held, 2), cube_permute(early, 0)
        far_late = cube_permute(late, 1, LATE_ORDERS)
        held, early, late = joined(held, arrived), joined(early, far_early), joined(late, far_late)
        held, early, late, bias_full = lax.optimization_barrier((held, early, late, bias_full))
        bias_full = bias_full + bit_permute(bias_full, 1)
        far, far_early = cube_permute(held, 3), cube_permute(early, 1)
        twin = bit_permute(held, 0)
        early = joined(early, far_early)
        far, early, late, bias_full = lax.optimization_barrier((far, early, late, bias_full))
        attend_halves = (held, far, twin, bit_permute(far, 0))
        far_early, far_late = cube_permute(early, 2), cube_permute(late, 2, LATE_ORDERS)
        qkv, wide, wide_out = project(where, spots, normed, attend_halves, bias_full, ())
        far_early, far_late, qkv = lax.optimization_barrier((far_early, far_late, qkv))
        early, late = joined(early, far_early), joined(late, far_late)
        far_early, far_late = cube_permute(early, 3), cube_permute(late, 3, LATE_ORDERS)
        twin_early, twin_late = bit_permute(early, 0), bit_permute(late, 0)
        mixture, log_totals = attend_forward(where, lengths, qkv, (early, late))
        far_early, far_late, twin_late, mixture = lax.optimization_barrier(
            (far_early, far_late, twin_late, mixture)
        )
        last_early, last_late = bit_permute(far_early, 0), bit_permute(far_late, 0)
        middle, hidden_in, hidden_t, unit, inverse = attend_out(mixture, wide_out, tokens, layer_vectors)
        feed_halves = (early, far_early, twin_early, last_early, late, far_late, twin_late, last_late)
    else:

        def planes(shard):
            full = lax.all_gather(lax.all_gather(shard, "dp", axis=0, tiled=True), "mp", axis=0)
            full = full.reshape(2, 2, 8, depth // 8, shard.shape[1]).transpose(1, 0, 2, 3, 4)
            return tuple(full.reshape(4, 8, depth // 8, shard.shape[1]))

        normed, normed_t, upstream_t = prepare(tokens, cotangent, layer_vectors, ())
        bias_full = lax.psum(bias_full, "mp")
        qkv, wide, wide_out = project(where, spots, normed, planes(attend_shard), bias_full, ())
        mixture, log_totals = attend_forward(where, lengths, qkv, ())
        middle, hidden_in, hidden_t, unit, inverse = attend_out(mixture, wide_out, tokens, layer_vectors)
        split = depth // 8 * 2 // 3
        feed_planes = planes(feed_shard)
        feed_halves = tuple(array[:, :split] for array in feed_planes) + tuple(
            array[:, split:] for array in feed_planes
        )
    block_out, back, keep_early, send_early, keep_late, send_late, bias_grad = feed(
        where,
        spots,
        hidden_in,
        hidden_t,
        cotangent,
        upstream_t,
        feed_halves,
        bias_full,
        middle,
        layer_vectors,
    )
    middle_grad, mixture_grad, output_grad, middle_sums = middle_back(
        where, lengths, back, unit, inverse, cotangent, mixture, wide_out, layer_vectors
    )
    if cube:
        twin_early, twin_late = bit_permute(send_early[8:], 0), bit_permute(send_late[8:], 0)
        twin_early, twin_late, mixture_grad, send_early, send_late = lax.optimization_barrier(
            (twin_early, twin_late, mixture_grad, send_early, send_late)
        )
        away = (keep_early[8:].astype(f32) + twin_early.astype(f32)).astype(low)
        far_away_late = (keep_late[8:].astype(f32) + twin_late.astype(f32)).astype(low)
        early = [keep_early[:8], bit_permute(send_early[:8], 0)]
        late = [keep_late[:8], bit_permute(send_late[:8], 0)]
        packed_grad = attend_backward(
            where, lengths, qkv, mixture_grad, log_totals, (away, far_away_late)
        )
        early = early + [cube_permute(away, 3)]
        late = late + [cube_permute(far_away_late, 3, LATE_ORDERS)]
        early[0], late[0], packed_grad = lax.optimization_barrier((early[0], late[0], packed_grad))
        away, far_away_late = leaving(early, 2), leaving(late, 2)
        sums = (middle_sums, bias_grad)
        keep_attend, send_attend, rider = input_grad(
            where, spots, normed_t, packed_grad, output_grad, sums, 16, depth // 8, (away, far_away_late)
        )
        early = staying(early, 2) + [cube_permute(away, 2)]
        late = staying(late, 2) + [cube_permute(far_away_late, 2, LATE_ORDERS)]
        early[-1], late[-1], send_attend = lax.optimization_barrier((early[-1], late[-1], send_attend))
        twin_b, rider, _ = with_rider(send_attend[8:], rider, lambda values: bit_permute(values, 0))
        twin_a = bit_permute(send_attend[:8], 0)
        away = (keep_attend[8:].astype(f32) + twin_b.astype(f32)).astype(low)
        arrived, rider, message = with_rider(away, rider, lambda values: cube_permute(values, 3))
        attend_parts = [keep_attend[:8], twin_a, arrived]
        feed_away = leaving(early, 1)
        token_grad, token_sums = token_back(
            packed_grad, wide, tokens, middle_grad, layer_vectors, (message, feed_away)
        )
        early = staying(early, 1) + [cube_permute(feed_away, 1)]
        attend_parts[0], late[0], token_sums = lax.optimization_barrier(
            (attend_parts[0], late[0], token_sums)
        )
        feed_away = leaving(late, 1)
        late = staying(late, 1) + [cube_permute(feed_away, 1, LATE_ORDERS)]
        away = leaving(attend_parts, 2)
        arrived, rider, message = with_rider(away, rider, lambda values: cube_permute(values, 2))
        attend_parts = staying(attend_parts, 2) + [arrived]
        message, early[0], late[0] = lax.optimization_barrier((message, early[0], late[0]))
        feed_away = leaving(early, 0)
        early = staying(early, 0) + [cube_permute(feed_away, 0)]
        away = leaving(attend_parts, 1)
        arrived, rider, message = with_rider(away, rider, lambda values: cube_permute(values, 1))
        attend_parts = staying(attend_parts, 1) + [arrived]
        message, early[0], late[0] = lax.optimization_barrier((message, early[0], late[0]))
        early_total = summed(early)
        feed_away = leaving(late, 0)
        late = staying(late, 0) + [cube_permute(feed_away, 0, LATE_ORDERS)]
        arrays = list(bring(arrays, (message,)))
        attend_parts[0], arrays[0] = lax.optimization_barrier((attend_parts[0], arrays[0]))
        away = leaving(attend_parts, 0)
        away, early_total = lax.optimization_barrier((away, early_total))
        arrived, vector_total, _ = with_rider(away, rider, lambda values: cube_permute(values, 0))
        attend_parts = staying(attend_parts, 0) + [arrived]
        late_total = summed(late)
        feed_totals = (early_total, late_total)
        attend_total, owned = last_sum(attend_parts, early_total, late_total, token_sums)
        owned = cube_sum(owned)
    else:
        packed_grad = attend_backward(where, lengths, qkv, mixture_grad, log_totals, ())
        sums = (middle_sums, bias_grad)
        keep_attend, send_attend, vector_total = input_grad(
            where, spots, normed_t, packed_grad, output_grad, sums, 16, depth // 8, ()
        )
        token_grad, token_sums = token_back(packed_grad, wide, tokens, middle_grad, layer_vectors, ())
        vector_total = lax.psum(vector_total, ("dp", "mp"))

    if not cube:

        def own_block(keep, send):
            full = jnp.stack([keep, send]).reshape(2, 2, 8, keep.shape[1], keep.shape[2])
            full = full.transpose(1, 0, 2, 3, 4).reshape(4, 8 * keep.shape[1], keep.shape[2])
            full = lax.psum_scatter(full, "mp", scatter_dimension=0, tiled=False)
            return lax.psum(full, "dp")

        def own_rows(*blocks):
            full = jnp.concatenate([block.reshape(8, -1, block.shape[1]) for block in blocks], axis=1)
            full = full.reshape(depth, full.shape[2]).astype(f32)
            return lax.dynamic_slice_in_dim(full, lax.axis_index("dp") * rows, rows, 0)

        attend_total = own_rows(own_block(keep_attend, send_attend))
        feed_total = own_rows(own_block(keep_early, send_early), own_block(keep_late, send_late))
        feed_totals = feed_total[: rows * 2 // 3], feed_total[rows * 2 // 3 :]
        attend_total, owned = last_sum((attend_total[None],), *feed_totals, token_sums)
        owned = lax.psum(owned, ("dp", "mp"))
    grad_norm, *updates = optimize(where, owned, vector_total, attend_total, feed_totals, arrays)
    grad_norm = grad_norm[0, 0]
    moment_input, square_input, updated_input = (turned(array) for array in updates[:3])
    moment_output, square_output, updated_output = updates[3:6]
    moment_expand, square_expand, updated_expand = updates[6:9]
    moment_shrink, square_shrink, updated_shrink = (array.T for array in updates[9:12])
    moment_vectors, square_vectors, updated_vectors = updates[12:15]
    moment_head, square_head, updated_head = updates[15:18]
    moment_bias, square_bias, updated_bias = (array.reshape(hidden) for array in updates[18:])
    return (
        block_out,
        token_grad,
        grad_norm,
        moment_input,
        square_input,
        updated_input,
        moment_output,
        square_output,
        updated_output,
        moment_expand,
        square_expand,
        updated_expand,
        moment_shrink,
        square_shrink,
        updated_shrink,
        moment_vectors,
        square_vectors,
        updated_vectors,
        moment_head,
        square_head,
        updated_head,
        moment_bias,
        square_bias,
        updated_bias,
    )


def solution(mesh):
    in_specs = (
        P(("dp", "mp"), None),
        P(("dp", "mp"), None),
        P("dp"),
        P("dp", None, "mp"),
        P("mp", "dp"),
        P("dp", "mp"),
        P("mp", "dp"),
        P(),
        P(None, "mp"),
        P("mp"),
        P("dp", None, "mp"),
        P("mp", "dp"),
        P("dp", "mp"),
        P("mp", "dp"),
        P(),
        P(None, "mp"),
        P("mp"),
        P("dp", None, "mp"),
        P("mp", "dp"),
        P("dp", "mp"),
        P("mp", "dp"),
        P(),
        P(None, "mp"),
        P("mp"),
    )
    out_specs = (
        P(("dp", "mp"), None),
        P(("dp", "mp"), None),
        P(),
        P("dp", None, "mp"),
        P("dp", None, "mp"),
        P("dp", None, "mp"),
        P("mp", "dp"),
        P("mp", "dp"),
        P("mp", "dp"),
        P("dp", "mp"),
        P("dp", "mp"),
        P("dp", "mp"),
        P("mp", "dp"),
        P("mp", "dp"),
        P("mp", "dp"),
        P(),
        P(),
        P(),
        P(None, "mp"),
        P(None, "mp"),
        P(None, "mp"),
        P("mp"),
        P("mp"),
        P("mp"),
    )
    return jax.shard_map(shards, mesh=mesh, in_specs=in_specs, out_specs=out_specs, check_vma=False)
```

```python
import functools
import jax
import jax.numpy as jnp
from jax import lax
from jax.experimental import pallas as pl
from jax.experimental.pallas import tpu as pltpu
from jax.sharding import PartitionSpec as P

HEAD_DIM = 64
TILE = 256
STEP = 10

eps_norm = 1e-05
clip_norm = 1.0
beta_one = 0.9
beta_two = 0.999
adam_eps = 1e-08
rate = 0.05
vector_rate = 0.5
decay = 0.01
excluded = -1e30
low = jnp.bfloat16
f32 = jnp.float32
GELU_A = 0.7978845608028654
GELU_B = GELU_A * 0.044715


def params(limit_mib, **kw):
    return pltpu.CompilerParams(vmem_limit_bytes=limit_mib * 1024 * 1024, **kw)


def cost(flops, moved, special=0):
    return pl.CostEstimate(flops=int(flops), bytes_accessed=int(moved), transcendentals=int(special))


def mm(a, b):
    return jnp.dot(a, b, preferred_element_type=f32)


def mm_nt(a, b):
    return lax.dot_general(a, b, (((1,), (1,)), ((), ())), preferred_element_type=f32)


def whole(shape):
    zeros = (0,) * len(shape)
    return pl.BlockSpec(shape, lambda *_: zeros)


def once(shape):
    zeros = (0,) * len(shape)
    return pl.BlockSpec(shape, lambda *_: zeros, pipeline_mode=pl.Buffered(1))


def held_back(body, first, count):
    def run(*refs):
        return body(*refs[:first], *refs[first + count :])

    return run


LATER = pl.BlockSpec(memory_space=pl.ANY)


def far_away(shape, dtype):
    return pltpu.HBM(shape, dtype)


def from_far(*arrays):
    return [pltpu.with_memory_space_constraint(array, pltpu.HBM) for array in arrays]


def sds(shape, dtype):
    return jax.ShapeDtypeStruct(shape, dtype)


def live_blocks(length, count, body):
    for blocks in range(1, count + 1):
        low_end = (blocks - 1) * TILE
        high_end = blocks * TILE
        @pl.when((length > low_end) & (length <= high_end))
        def _(blocks=blocks):
            body(length, blocks)


PAIR = 2 * HEAD_DIM


def span(block):
    return slice(block * TILE, (block + 1) * TILE)


def both_heads(values):
    lane = lax.broadcasted_iota(jnp.int32, values.shape, 1)
    none = jnp.zeros_like(values)
    return jnp.concatenate(
        [jnp.where(lane < HEAD_DIM, values, none), jnp.where(lane >= HEAD_DIM, values, none)], axis=0
    )


def causal_mask():
    key_id = lax.broadcasted_iota(jnp.int32, (TILE, 2 * TILE), 0)
    query_id = lax.broadcasted_iota(jnp.int32, (TILE, 2 * TILE), 1) & (TILE - 1)
    return key_id <= query_id


def forward_body(where_ref, lengths_ref, q_ref, k_ref, v_ref, o_ref, lse_ref, vt_ref):
    seq = q_ref.shape[0]
    vt_ref[...] = v_ref[...].T
    causal = causal_mask()

    def run(length, blocks):
        def scores(b):
            q = q_ref[span(b), :] * jnp.asarray(HEAD_DIM**-0.5, low)
            return mm_nt(k_ref[: (b + 1) * TILE, :], both_heads(q))

        now = scores(0)
        for b in range(blocks):
            start, stop = b * TILE, (b + 1) * TILE
            later = scores(b + 1) if b + 1 < blocks else None
            last = jnp.where(causal, now[start:, :], excluded)
            top = jnp.max(last, axis=0, keepdims=True)
            if b:
                top = jnp.maximum(top, jnp.max(now[:start], axis=0, keepdims=True))
            p = jnp.exp(last - top)
            total = jnp.sum(p, axis=0, keepdims=True)
            pb = p.astype(low)
            if b:
                pf = jnp.exp(now[:start] - top)
                total = total + jnp.sum(pf, axis=0, keepdims=True)
                pb = jnp.concatenate([pf.astype(low), pb], axis=0)
            inverse = 1.0 / total
            lse = top + jnp.log(total)
            outs = []
            for h in range(2):
                at = slice(h * TILE, (h + 1) * TILE)
                out = mm(vt_ref[h * HEAD_DIM : (h + 1) * HEAD_DIM, :stop], pb[:, at])
                outs.append(out * inverse[:, at])
                lse_ref[0, h : h + 1, start:stop] = lse[:, at]
            both = jnp.concatenate(outs, axis=0).T
            row = start + lax.broadcasted_iota(jnp.int32, both.shape, 0)
            o_ref[start:stop, :] = jnp.where(row < length, both, 0.0).astype(low)
            now = later
        if blocks * TILE < seq:
            o_ref[blocks * TILE :, :] = jnp.zeros((seq - blocks * TILE, PAIR), low)
            lse_ref[0, :, blocks * TILE :] = jnp.zeros((2, seq - blocks * TILE), f32)

    live_blocks(lengths_ref[where_ref[2]], seq // TILE, run)


def attend_forward(where, lengths, qkv, after):
    seq, width = qkv.shape[0], qkv.shape[1] // 3
    pair = 2 * HEAD_DIM
    pairs = width // pair
    half = seq * seq * 5 // 8
    spec = lambda part: pl.BlockSpec((seq, pair), lambda i, *_: (0, part * pairs + i))
    return pl.pallas_call(
        held_back(forward_body, 5, len(after)),
        grid_spec=pltpu.PrefetchScalarGridSpec(
            num_scalar_prefetch=2,
            grid=(pairs,),
            in_specs=[spec(0), spec(1), spec(2)] + [LATER] * len(after),
            out_specs=[
                pl.BlockSpec((seq, pair), lambda i, *_: (0, i)),
                pl.BlockSpec((1, 2, seq), lambda i, *_: (i, 0, 0)),
            ],
            scratch_shapes=[pltpu.VMEM((pair, seq), low)],
        ),
        out_shape=[sds((seq, width), low), far_away((pairs, 2, seq), f32)],
        compiler_params=params(20),
        cost_estimate=cost(pairs * 2 * half * 2 * 2 * 256, seq * width * 8, pairs * 2 * half),
        name="attend_forward",
    )(where, lengths, *from_far(qkv, qkv, qkv), *after)


def backward_body(where_ref, lengths_ref, q_ref, k_ref, v_ref, do_ref, lse_ref, out_ref, kt_ref, ksum, vsum):
    seq = q_ref.shape[0]
    scale = HEAD_DIM**-0.5
    kt_ref[...] = k_ref[...].T
    causal = causal_mask()

    def run(length, blocks):
        def scores(b):
            qq = both_heads(q_ref[span(b), :] * jnp.asarray(scale, low))
            uu = both_heads(do_ref[span(b), :])
            stop = (b + 1) * TILE
            return qq, uu, mm_nt(k_ref[:stop, :], qq), mm_nt(v_ref[:stop, :], uu)

        now = scores(blocks - 1)
        for b in reversed(range(blocks)):
            start, stop = b * TILE, (b + 1) * TILE
            later = scores(b - 1) if b else None
            qq, uu, s, dp = now
            lse = jnp.concatenate([lse_ref[0, 0:1, start:stop], lse_ref[0, 1:2, start:stop]], axis=1)
            p = jnp.exp(jnp.where(causal, s[start:], excluded) - lse)
            inner = jnp.sum(p * dp[start:], axis=0, keepdims=True)
            if b:
                pf = jnp.exp(s[:start] - lse)
                inner = inner + jnp.sum(pf * dp[:start], axis=0, keepdims=True)
            ds = (p * (dp[start:] - inner)).astype(low)
            pb = p.astype(low)
            if b:
                ds = jnp.concatenate([(pf * (dp[:start] - inner)).astype(low), ds], axis=0)
                pb = jnp.concatenate([pf.astype(low), pb], axis=0)
            dq = jnp.concatenate(
                [
                    mm(
                        kt_ref[h * HEAD_DIM : (h + 1) * HEAD_DIM, :stop],
                        ds[:, h * TILE : (h + 1) * TILE],
                    )
                    for h in range(2)
                ],
                axis=0,
            )
            dk, dv = mm(ds, qq), mm(pb, uu)
            if b == blocks - 1:
                ksum[:stop, :] = dk
                vsum[:stop, :] = dv
            else:
                ksum[:stop, :] += dk
                vsum[:stop, :] += dv
            out_ref[1, start:stop, :] = ksum[start:stop, :].astype(low)
            out_ref[2, start:stop, :] = vsum[start:stop, :].astype(low)
            out_ref[0, start:stop, :] = (dq.T * scale).astype(low)
            now = later
        if blocks * TILE < seq:
            rest = jnp.zeros((seq - blocks * TILE, PAIR), low)
            for part in range(3):
                out_ref[part, blocks * TILE :, :] = rest

    live_blocks(lengths_ref[where_ref[2]], seq // TILE, run)


def attend_backward(where, lengths, qkv, upstream, lse, after):
    seq, width = upstream.shape
    pair = 2 * HEAD_DIM
    pairs = width // pair
    half = seq * seq * 5 // 8
    spec = lambda part: pl.BlockSpec((seq, pair), lambda i, *_: (0, part * pairs + i))
    own = pl.BlockSpec((seq, pair), lambda i, *_: (0, i))
    return pl.pallas_call(
        held_back(backward_body, 7, len(after)),
        grid_spec=pltpu.PrefetchScalarGridSpec(
            num_scalar_prefetch=2,
            grid=(pairs,),
            in_specs=[spec(0), spec(1), spec(2), own, pl.BlockSpec((1, 2, seq), lambda i, *_: (i, 0, 0))]
            + [LATER] * len(after),
            out_specs=pl.BlockSpec((3, seq, pair), lambda i, *_: (0, 0, i)),
            scratch_shapes=[
                pltpu.VMEM((pair, seq), low),
                pltpu.VMEM((seq, pair), f32),
                pltpu.VMEM((seq, pair), f32),
            ],
        ),
        out_shape=sds((3, seq, width), low),
        compiler_params=params(28),
        cost_estimate=cost(pairs * 2 * half * 5 * 2 * 256, seq * width * 14, pairs * 2 * half),
        name="attend_backward",
    )(where, lengths, *from_far(qkv, qkv, qkv), upstream, *from_far(lse), *after)


def normalize(values):
    average = jnp.mean(values, axis=-1, keepdims=True)
    centred = values - average
    inverse = lax.rsqrt(jnp.mean(centred * centred, axis=-1, keepdims=True) + eps_norm)
    return centred * inverse, inverse


def pull_norm(scaled, unit, inverse):
    first = jnp.mean(scaled, axis=-1, keepdims=True)
    second = jnp.mean(scaled * unit, axis=-1, keepdims=True)
    return inverse * (scaled - first - unit * second)


def columns_of(values):
    return jnp.sum(values, axis=0, keepdims=True)


def pack_body(
    input_ref, output_ref, expand_ref, shrink_ref, head_ref, hidden_ref, attend_ref, feed_ref, bias_ref
):
    width = input_ref.shape[2]
    part = expand_ref.shape[1] // 3
    for index in range(3):
        attend_ref[:, index * width : (index + 1) * width] = input_ref[index].astype(low)
        at = slice(index * part, (index + 1) * part)
        feed_ref[:, 2 * index * part : (2 * index + 1) * part] = expand_ref[:, at].astype(low)
        feed_ref[:, (2 * index + 1) * part : (2 * index + 2) * part] = shrink_ref[:, at].astype(low)
    attend_ref[:, 3 * width :] = output_ref[...].T.astype(low)
    pieces = [head_ref[0:1, :], head_ref[1:2, :]]
    pieces += [hidden_ref[row : row + 1, :] for row in range(hidden_ref.shape[0])]
    bias_ref[...] = jnp.zeros_like(bias_ref)
    bias_ref[pl.ds(lax.axis_index("mp"), 1), :] = jnp.concatenate(pieces, axis=1)


def pack(input_weight, output_weight, expand, shrink, head_bias, hidden_bias):
    rows, width = input_weight.shape[1:]
    hidden = expand.shape[1]
    return pl.pallas_call(
        pack_body,
        out_shape=[
            sds((rows, 4 * width), low),
            sds((rows, 2 * hidden), low),
            sds((4, 2 * width + hidden), f32),
        ],
        compiler_params=params(6),
        cost_estimate=cost(rows * hidden, rows * hidden * 18),
        name="pack",
    )(*from_far(input_weight, output_weight, expand, shrink, head_bias, hidden_bias))


def prepare_body(x_ref, up_ref, vec_ref, h_ref, ht_ref, upt_ref):
    unit, _ = normalize(x_ref[...].astype(f32))
    h = (unit * vec_ref[0:1, :] + vec_ref[1:2, :]).astype(low)
    h_ref[...] = h
    ht_ref[...] = h.T
    upt_ref[...] = up_ref[...].T


def prepare(x, up, vectors, after):
    seq, depth = x.shape
    rows = pl.BlockSpec((2 * TILE, depth), lambda i: (i, 0))
    turned = pl.BlockSpec((depth, 2 * TILE), lambda i: (0, i))
    return pl.pallas_call(
        held_back(prepare_body, 3, len(after)),
        grid=(seq // (2 * TILE),),
        in_specs=[rows, rows, once(vectors.shape)] + [LATER] * len(after),
        out_specs=[rows, turned, turned],
        out_shape=[sds((seq, depth), low), sds((depth, seq), low), far_away((depth, seq), low)],
        compiler_params=params(16),
        cost_estimate=cost(seq * depth * 10, seq * depth * 10),
        name="prepare",
    )(*from_far(x, up), vectors, *after)


def slot(halves, spot, at):
    first, second = halves
    inner = spot & 7
    return jnp.where(spot < 8, first[inner, :, at], second[inner, :, at])


def project_body(
    where_ref, spots_ref, h_ref, mine_a, mine_b, twin_a, twin_b, bias_ref, qkv_ref, wide_ref, last_ref
):
    part = pl.program_id(0)
    rows = mine_a.shape[1]
    width = mine_a.shape[2] // 4
    groups = wide_ref.shape[1] // rows

    def collect(sources, index):
        columns = slice(index * width, (index + 1) * width)
        for group in range(groups):
            pieces = [slot(sources[model % 2], spots_ref[model, group], columns) for model in range(4)]
            at = slice(group * rows, (group + 1) * rows)
            if index < 3:
                wide_ref[0, at, :] = jnp.concatenate(pieces, axis=1)
            else:
                last_ref[at, :] = jnp.concatenate(pieces, axis=1)

    for index in range(4):
        for core in range(2):

            @pl.when((part == index) & (where_ref[0] == core))
            def _(index=index, core=core):
                mine, twin = (mine_a, mine_b), (twin_a, twin_b)
                collect((mine, twin) if core == 0 else (twin, mine), index)

    for index in range(3):

        @pl.when(part == index)
        def _(index=index):
            out = mm(h_ref[...], wide_ref[0])
            if index != 1:
                at = slice(index // 2 * width, (index // 2 + 1) * width)
                bias = jnp.concatenate([bias_ref[model : model + 1, at] for model in range(4)], axis=1)
                out = out + bias
            qkv_ref[...] = out.astype(low)


def project(where, spots, h, halves, bias, after):
    seq, depth = h.shape
    return pl.pallas_call(
        held_back(project_body, 8, len(after)),
        grid_spec=pltpu.PrefetchScalarGridSpec(
            num_scalar_prefetch=2,
            grid=(4,),
            in_specs=[
                once((seq, depth)),
                *[once(halves[0].shape)] * 4,
                once(bias.shape),
            ]
            + [LATER] * len(after),
            out_specs=[
                pl.BlockSpec((seq, depth), lambda i, *_: (0, jnp.minimum(i, 2))),
                pl.BlockSpec((1, depth, depth), lambda i, *_: (jnp.minimum(i, 2), 0, 0)),
                whole((depth, depth)),
            ],
        ),
        out_shape=[
            far_away((seq, 3 * depth), low),
            far_away((3, depth, depth), low),
            sds((depth, depth), low),
        ],
        compiler_params=params(24),
        cost_estimate=cost(2 * seq * depth * depth * 3, seq * depth * 16),
        name="project",
    )(where, spots, h, *halves, bias, *after)


NEAR = pl.BlockSpec(memory_space=pltpu.VMEM)
SCALARS = pl.BlockSpec(memory_space=pltpu.SMEM)


def attend_out_body(o_ref, w_ref, x_ref, vec_ref, middle_ref, h_ref, ht_ref, unit_ref, inverse_ref):
    for tile in range(o_ref.shape[0] // TILE):
        at = slice(tile * TILE, (tile + 1) * TILE)
        middle = x_ref[at, :].astype(f32) + mm_nt(o_ref[at, :], w_ref[...]) + vec_ref[4:5, :]
        middle_ref[at, :] = middle.astype(low)
        unit, inverse = normalize(middle)
        unit_ref[at, :] = unit.astype(low)
        inverse_ref[at, :] = jnp.broadcast_to(inverse, (TILE, inverse_ref.shape[1]))
        h = (unit * vec_ref[2:3, :] + vec_ref[3:4, :]).astype(low)
        h_ref[at, :] = h
        ht_ref[:, at] = h.T


def attend_out(o, wide_out, x, vectors):
    seq, depth = x.shape
    return pl.pallas_call(
        attend_out_body,
        in_specs=[NEAR] * 4,
        out_specs=[NEAR] * 5,
        out_shape=[
            sds((seq, depth), low),
            sds((seq, depth), low),
            sds((depth, seq), low),
            sds((seq, depth), low),
            sds((seq, 128), f32),
        ],
        compiler_params=params(10),
        cost_estimate=cost(2 * seq * depth * depth, seq * depth * 14),
        name="attend_out",
    )(o, wide_out, x, vectors)


def feed_body(
    where_ref,
    spots_ref,
    h2_ref,
    h2t_ref,
    up_ref,
    upt_ref,
    mine_a,
    mine_b,
    twin_a,
    twin_b,
    mine_c,
    mine_d,
    twin_c,
    twin_d,
    bias_ref,
    middle_ref,
    vec_ref,
    block_ref,
    back_ref,
    keep_a,
    send_a,
    keep_b,
    send_b,
    bias_grad_ref,
    out_ref,
    sum_ref,
    wide_ref,
    act_ref,
    pre_ref,
):
    part = mine_a.shape[2] // 6
    groups = spots_ref.shape[1]
    rows = wide_ref.shape[0] // groups
    split = mine_a.shape[1]
    skip = bias_ref.shape[1] - bias_grad_ref.shape[1]
    pieces = (
        ((mine_a, mine_b), (twin_a, twin_b), 0, slice(0, split)),
        ((mine_c, mine_d), (twin_c, twin_d), 4, slice(split, rows)),
    )
    half = keep_a.shape[1]
    results = ((keep_a, send_a, 0, slice(0, half)), (keep_b, send_b, 4, slice(half, rows)))
    out_ref[...] = middle_ref[...].astype(f32) + vec_ref[5:6, :]
    sum_ref[...] = jnp.zeros_like(sum_ref)

    def step(index, carry):
        side = lax.rem(index, 2)
        first = pl.multiple_of(index // 2 * part, 128)
        lanes = pl.ds(pl.multiple_of(2 * first, 128), part)
        next_lanes = pl.ds(pl.multiple_of(2 * first + part, 128), part)
        models = [where_ref[1] ^ (2 * side + core) for core in range(2)]
        for group in range(groups):
            for mine, twin, table, within in pieces:
                at = slice(group * rows + within.start, group * rows + within.stop)
                for core, halves in enumerate((mine, twin)):
                    spot = spots_ref[table + models[core], group]
                    wide_ref[at, core * part : (core + 1) * part] = slot(halves, spot, lanes)
                    wide_ref[at, (2 + core) * part : (3 + core) * part] = slot(halves, spot, next_lanes)

        expand = wide_ref[:, : 2 * part]
        shrink = wide_ref[:, 2 * part :]
        bias = jnp.concatenate(
            [bias_ref[pl.ds(model, 1), pl.ds(pl.multiple_of(skip + first, 128), part)] for model in models],
            axis=1,
        )
        sums = jnp.zeros((1, 2 * part), f32)
        for tile in range(h2_ref.shape[0] // TILE):
            at = slice(tile * TILE, (tile + 1) * TILE)
            u = mm(h2_ref[at, :], expand) + bias
            square = u * u
            th = jnp.tanh(u * (GELU_A + GELU_B * square))
            gate = 0.5 * th + 0.5
            slope = gate + (gate * (1.0 - gate)) * (u * (2.0 * GELU_A + (6.0 * GELU_B) * square))
            pre = (mm(up_ref[at, :], shrink) * slope).astype(low)
            act_ref[at, :] = (u * gate).astype(low)
            pre_ref[at, :] = pre
            sums = sums + columns_of(pre.astype(f32))
        for core, model in enumerate(models):
            bias_grad_ref[pl.ds(model, 1), pl.ds(first, part)] = sums[:, core * part : (core + 1) * part]
        grad_expand = mm(h2t_ref[...], pre_ref[...]).astype(low)
        grad_shrink = mm(upt_ref[...], act_ref[...]).astype(low)
        out_ref[...] += mm_nt(act_ref[...], shrink)
        sum_ref[...] += mm_nt(pre_ref[...], expand)
        for group in range(groups):
            for keep, send, table, within in results:
                at = slice(group * rows + within.start, group * rows + within.stop)
                for core, target in enumerate((keep, send)):
                    spot = spots_ref[table + models[core], group]
                    columns = slice(core * part, (core + 1) * part)
                    target[spot, :, lanes] = grad_expand[at, columns]
                    target[spot, :, next_lanes] = grad_shrink[at, columns]
        return carry

    lax.fori_loop(0, 6, step, 0)
    block_ref[...] = out_ref[...].astype(low)
    back_ref[...] = sum_ref[...].astype(low)


def feed(where, spots, h2, h2t, up, upt, halves, bias, middle, vectors):
    seq, depth = h2.shape
    half, _, columns = halves[0].shape
    part = columns // 6
    splits = [halves[0].shape[1], halves[4].shape[1]]
    return pl.pallas_call(
        feed_body,
        in_specs=[SCALARS] * 2 + [NEAR] * 15,
        out_specs=[NEAR] * 7,
        scratch_shapes=[
            pltpu.VMEM((seq, depth), f32),
            pltpu.VMEM((seq, depth), f32),
            pltpu.VMEM((depth, 4 * part), low),
            pltpu.VMEM((seq, 2 * part), low),
            pltpu.VMEM((seq, 2 * part), low),
        ],
        out_shape=[sds((seq, depth), low)] * 2
        + [sds((2 * half, rows, columns), low) for rows in splits for _ in range(2)]
        + [sds((4, 3 * part), f32)],
        compiler_params=params(22),
        cost_estimate=cost(12 * seq * depth * 12 * part, seq * depth * 40, seq * 6 * part),
        name="feed",
    )(where, spots, h2, h2t, up, upt, *halves, bias, middle, vectors)


def middle_back_body(
    where_ref,
    lengths_ref,
    back_ref,
    unit_ref,
    inverse_ref,
    up_ref,
    o_ref,
    w_ref,
    vec_ref,
    grad_ref,
    mixture_ref,
    weight_ref,
    sums_ref,
    turned_ref,
):
    length = lengths_ref[where_ref[2]]
    sums = jnp.zeros(sums_ref.shape, f32)
    for tile in range(back_ref.shape[0] // TILE):
        at = slice(tile * TILE, (tile + 1) * TILE)
        unit, inverse = unit_ref[at, :].astype(f32), inverse_ref[at, 0:1]
        back = back_ref[at, :].astype(f32)
        up = up_ref[at, :].astype(f32)
        grad = up + pull_norm(back * vec_ref[2:3, :], unit, inverse)
        rounded = grad.astype(low)
        grad_ref[at, :] = rounded
        turned_ref[:, at] = rounded.T
        row = tile * TILE + lax.broadcasted_iota(jnp.int32, grad.shape, 0)
        mixture_ref[at, :] = jnp.where(row < length, mm(rounded, w_ref[...]), 0.0).astype(low)
        sums = sums + jnp.concatenate(
            [columns_of(back * unit), columns_of(back), columns_of(grad), columns_of(up)], axis=0
        )
    sums_ref[...] = sums
    weight_ref[...] = mm(turned_ref[...], o_ref[...]).astype(low)


def middle_back(where, lengths, back, unit, inverse, up, o, wide_out, vectors):
    seq, depth = unit.shape
    return pl.pallas_call(
        middle_back_body,
        in_specs=[SCALARS] * 2 + [NEAR] * 7,
        out_specs=[NEAR] * 4,
        scratch_shapes=[pltpu.VMEM((depth, seq), low)],
        out_shape=[
            sds((seq, depth), low),
            sds((seq, depth), low),
            sds((depth, depth), low),
            sds((4, depth), f32),
        ],
        compiler_params=params(14),
        cost_estimate=cost(4 * seq * depth * depth, seq * depth * 28),
        name="middle_back",
    )(where, lengths, back, unit, inverse, up, o, wide_out, vectors)


def input_grad_body(
    where_ref,
    spots_ref,
    ht_ref,
    back_ref,
    out_grad_ref,
    middle_ref,
    bias_ref,
    keep_ref,
    send_ref,
    sums_ref,
):
    rows = keep_ref.shape[1]
    width = keep_ref.shape[2] // 4
    groups = ht_ref.shape[0] // rows

    def spread(targets, index, grad):
        at = slice(index * width, (index + 1) * width)
        for group in range(groups):
            for model in range(4):
                targets[model % 2][spots_ref[model, group], :, at] = grad[
                    group * rows : (group + 1) * rows, model * width : (model + 1) * width
                ]

    sums_ref[:2] = jnp.zeros((2, sums_ref.shape[1]), f32)
    sums_ref[2:6] = middle_ref[...]
    sums_ref[6:7] = columns_of(back_ref[0].astype(f32))
    sums_ref[7:8] = columns_of(back_ref[2].astype(f32))
    sums_ref[8:] = bias_ref[...]
    for index in range(4):
        grad = mm(ht_ref[...], back_ref[index]).astype(low) if index < 3 else out_grad_ref[...]
        for core in range(2):

            @pl.when(where_ref[0] == core)
            def _(core=core, index=index, grad=grad):
                spread((keep_ref, send_ref) if core == 0 else (send_ref, keep_ref), index, grad)


def input_grad(where, spots, ht, back, out_grad, sums, slots, rows, after):
    depth, seq = ht.shape
    shape = (slots, rows, depth)
    return pl.pallas_call(
        held_back(input_grad_body, 7, len(after)),
        in_specs=[SCALARS] * 2 + [NEAR] * 5 + [LATER] * len(after),
        out_specs=[NEAR] * 3,
        out_shape=[sds(shape, low), sds(shape, low), sds((12, depth), f32)],
        compiler_params=params(14),
        cost_estimate=cost(6 * seq * depth * depth, seq * depth * 14),
        name="input_grad",
    )(where, spots, ht, back, out_grad, *sums, *after)


def token_back_body(
    back_ref, w_ref, x_ref, grad_ref, vec_ref, token_ref, sums_ref
):
    step = pl.program_id(0)
    back = mm_nt(back_ref[0], w_ref[0]) + mm_nt(back_ref[1], w_ref[1]) + mm_nt(back_ref[2], w_ref[2])
    unit, inverse = normalize(x_ref[...].astype(f32))
    grad = grad_ref[...].astype(f32)
    token_ref[...] = (grad + pull_norm(back * vec_ref[0:1, :], unit, inverse)).astype(low)
    sums = jnp.concatenate([columns_of(back * unit), columns_of(back)], axis=0)

    @pl.when(step == 0)
    def _():
        sums_ref[...] = sums

    @pl.when(step > 0)
    def _():
        sums_ref[...] += sums


def token_back(back, wide, x, grad, vectors, after):
    seq, depth = x.shape
    rows = pl.BlockSpec((TILE, depth), lambda i: (i, 0))
    return pl.pallas_call(
        held_back(token_back_body, 5, len(after)),
        grid=(seq // TILE,),
        in_specs=[
            pl.BlockSpec((3, TILE, depth), lambda i: (0, i, 0)),
            pl.BlockSpec((3, depth, depth), lambda i: (0, 0, 0)),
            rows,
            rows,
            once(vectors.shape),
        ]
        + [LATER] * len(after),
        out_specs=[rows, whole((2, depth))],
        out_shape=[sds((seq, depth), low), sds((2, depth), f32)],
        compiler_params=params(24),
        cost_estimate=cost(6 * seq * depth * depth, seq * depth * 16),
        name="token_back",
    )(back, *from_far(wide, x), grad, vectors, *after)


CORE_ORDERS = ((4, 3, 2, 1), (3, 4, 1, 2))
LATE_ORDERS = ((2, 1, 4, 3), (1, 2, 3, 4))
STAGES = 4


def cube_permute(values, stage, orders=CORE_ORDERS):
    pairs = [(device, device ^ (1 << orders[device & 1][stage])) for device in range(32)]
    return lax.ppermute(values, ("dp", "mp"), pairs)


def bit_permute(values, bit):
    return lax.ppermute(values, ("dp", "mp"), [(device, device ^ (1 << bit)) for device in range(32)])


def place(distance, core, orders):
    spots = [
        sum(((distance >> bit) & 1) << step for step, bit in enumerate(order)) for order in orders
    ]
    return jnp.where(core == 0, spots[0], spots[1])


def joined(held, arrived):
    return jnp.concatenate([held, arrived], axis=0)


def leaving(parts, stage):
    half = 1 << stage
    return sum(part[half:].astype(f32) for part in parts).astype(low)


def staying(parts, stage):
    return [part[: 1 << stage] for part in parts]


def summed(parts):
    return sum(part[0].astype(f32) for part in parts)


def two_parts(values):
    high = lax.reduce_precision(values, 8, 7)
    rest = lax.reduce_precision(values - high, 8, 7)
    return jnp.concatenate([high, rest], axis=0).astype(low)


def one_part(parts):
    half = parts.shape[0] // 2
    return parts[:half].astype(f32) + parts[half:].astype(f32)


def with_rider(blocks, rider, send):
    count, rows, columns = blocks.shape
    parts = two_parts(rider)
    message = jnp.concatenate([blocks.reshape(count * rows, columns), parts], axis=0)
    arrived = send(message)
    total = one_part(parts) + one_part(arrived[count * rows :])
    return arrived[: count * rows].reshape(count, rows, columns), total, message


def cube_sum(values, bits=range(5)):
    for bit in bits:
        values = values + bit_permute(values, bit)
    return values


def adam_parts(weight, gradient, first_old, second_old, factor, step_rate):
    scaled = gradient * factor
    moment = beta_one * first_old + (1.0 - beta_one) * scaled
    square = beta_two * second_old + (1.0 - beta_two) * scaled * scaled
    spread = jnp.sqrt(square * (1.0 / (1.0 - beta_two**STEP)))
    ratio = moment * (1.0 / (1.0 - beta_one**STEP)) / (spread + adam_eps)
    return moment, square, weight - step_rate * (ratio + decay * weight)


def optimize_body(where_ref, owned_ref, vector_ref, attend_ref, feed_a, feed_b, *refs):
    state, outs = refs[:21], refs[21:]
    vectors = jnp.concatenate([owned_ref[:2], vector_ref[2:]], axis=0)
    total = owned_ref[2:3, 0:1] + jnp.sum(vectors * vectors)
    norm = jnp.sqrt(total)
    factor = clip_norm / jnp.maximum(norm, clip_norm)
    outs[0][...] = norm
    width = state[0].shape[2]
    part = state[6].shape[1] // 3

    def update(param, at, gradient, step_rate):
        weight, first, second = (ref[at] for ref in state[3 * param : 3 * param + 3])
        results = adam_parts(weight, gradient, first, second, factor, step_rate)
        for ref, result in zip(outs[1 + 3 * param : 4 + 3 * param], results):
            ref[at] = result

    for index in range(3):
        update(0, (index,), attend_ref[:, index * width : (index + 1) * width], rate)
    update(1, (...,), attend_ref[:, 3 * width :].T, rate)
    split, rows = feed_a.shape[0], state[6].shape[0]
    for feed_ref, within in ((feed_a, slice(0, split)), (feed_b, slice(split, rows))):
        for index in range(3):
            at = (within, slice(index * part, (index + 1) * part))
            first = 2 * index * part
            update(2, at, feed_ref[:, first : first + part], rate)
            update(3, at, feed_ref[:, first + part : first + 2 * part], rate)
    update(4, (...,), vectors[:6], vector_rate)
    model = where_ref[2]
    head = jnp.zeros((2, width), f32)
    for index in range(4):
        head = head + jnp.where(model == index, vectors[6:8, index * width : (index + 1) * width], 0.0)
    update(5, (...,), head, vector_rate)
    bias = vector_ref[pl.ds(8 + model, 1), :]
    bias = jnp.concatenate([bias[:, at : at + 128] for at in range(0, bias.shape[1], 128)], axis=0)
    update(6, (...,), bias, vector_rate)


def bring_body(*refs):
    half = len(refs) // 2
    for source, target in zip(refs[:half], refs[half:]):
        target[...] = source[...]


def bring(arrays, after):
    return pl.pallas_call(
        lambda *refs: bring_body(*refs[: len(arrays)], *refs[len(arrays) + len(after) :]),
        in_specs=[NEAR] * len(arrays) + [LATER] * len(after),
        out_specs=[NEAR] * len(arrays),
        out_shape=[sds(array.shape, f32) for array in arrays],
        compiler_params=params(8),
        cost_estimate=cost(4e6, 6e6),
        name="bring",
    )(*from_far(*arrays), *after)


def last_sum_body(*refs):
    parts, (early_ref, late_ref, token_ref, total_ref, owned_ref) = refs[:-5], refs[-5:]
    total = sum(part[0].astype(f32) for part in parts)
    total_ref[...] = total
    squares = sum(jnp.sum(values * values) for values in (total, early_ref[...], late_ref[...]))
    owned_ref[:2, :] = token_ref[...]
    owned_ref[2:, :] = jnp.full((1, owned_ref.shape[1]), squares, f32)


def last_sum(parts, early_total, late_total, token_sums):
    _, rows, columns = parts[0].shape
    return pl.pallas_call(
        last_sum_body,
        in_specs=[NEAR] * (len(parts) + 3),
        out_specs=[NEAR] * 2,
        out_shape=[sds((rows, columns), f32), sds((3, columns), f32)],
        compiler_params=params(8),
        cost_estimate=cost(0, 0),
        name="last_sum",
    )(*parts, early_total, late_total, token_sums)


def optimize(where, owned, vector_total, attend_total, feed_totals, arrays):
    shapes = [sds(array.shape, f32) for array in arrays]
    return pl.pallas_call(
        optimize_body,
        in_specs=[pl.BlockSpec(memory_space=pltpu.SMEM)]
        + [pl.BlockSpec(memory_space=pltpu.VMEM)] * (5 + len(arrays)),
        out_shape=[sds((1, 1), f32)] + shapes,
        compiler_params=params(20),
        cost_estimate=cost(4e6, 8e6),
        name="optimize",
    )(where, owned, vector_total, attend_total, *feed_totals, *arrays)


def shards(
    tokens,
    cotangent,
    lengths,
    input_weight,
    output_weight,
    expand_weight,
    shrink_weight,
    layer_vectors,
    head_bias,
    expand_bias,
    first_input,
    first_output,
    first_expand,
    first_shrink,
    first_vectors,
    first_head,
    first_bias,
    second_input,
    second_output,
    second_expand,
    second_shrink,
    second_vectors,
    second_head,
    second_bias,
):
    dp_count = lax.axis_size("dp")
    mp_count = lax.axis_size("mp")
    cube = dp_count == 8 and mp_count == 4
    rows = input_weight.shape[0]
    width = input_weight.shape[2]
    hidden = expand_weight.shape[1]
    seq, depth = tokens.shape
    part = hidden // 3
    model_index = lax.axis_index("mp")
    me = lax.axis_index("dp") * mp_count + model_index

    attend_shard, feed_shard, bias_full = pack(
        input_weight.transpose(1, 0, 2),
        output_weight,
        expand_weight,
        shrink_weight.T,
        head_bias,
        expand_bias.reshape(hidden // 128, 128),
    )
    if cube:
        core, near = me & 1, model_index
        devices = jnp.arange(32).reshape(8, 4).T
        spots = jnp.concatenate(
            [place(devices ^ me, devices & 1, orders) for orders in (CORE_ORDERS, LATE_ORDERS)]
        ).astype(jnp.int32)
    else:
        core = near = jnp.zeros((), jnp.int32)
        spots = (jnp.arange(8)[:, None] % 4 // 2 * 8 + jnp.arange(8)[None]).astype(jnp.int32)
    where = jnp.stack([core, near, model_index]).astype(jnp.int32)

    def turned(array):
        return array.transpose(1, 0, 2)

    state = (
        (turned(input_weight), turned(first_input), turned(second_input)),
        (output_weight, first_output, second_output),
        (expand_weight, first_expand, second_expand),
        (shrink_weight.T, first_shrink.T, second_shrink.T),
        (layer_vectors, first_vectors, second_vectors),
        (head_bias, first_head, second_head),
        tuple(array.reshape(hidden // 128, 128) for array in (expand_bias, first_bias, second_bias)),
    )
    arrays = [array for group in state for array in group]

    if cube:
        split = rows * 2 // 3
        held, early, late = attend_shard[None], feed_shard[None, :split], feed_shard[None, split:]
        arrived, far_late = cube_permute(held, 0), cube_permute(late, 0, LATE_ORDERS)
        held, bias_full = lax.optimization_barrier((joined(held, arrived), bias_full))
        arrived = cube_permute(held, 1)
        bias_full = bias_full + bit_permute(bias_full, 0)
        normed, normed_t, upstream_t = prepare(tokens, cotangent, layer_vectors, (held,))
        late = joined(late, far_late)
        held, early, late, normed, bias_full, spots, where = lax.optimization_barrier(
            (held, early, late, normed, bias_full, spots, where)
        )
        held, early = lax.optimization_barrier((joined(held, arrived), early))
        arrived, far_early = cube_permute(held, 2), cube_permute(early, 0)
        far_late = cube_permute(late, 1, LATE_ORDERS)
        held, early, late = joined(held, arrived), joined(early, far_early), joined(late, far_late)
        held, early, late, bias_full = lax.optimization_barrier((held, early, late, bias_full))
        bias_full = bias_full + bit_permute(bias_full, 1)
        far, far_early = cube_permute(held, 3), cube_permute(early, 1)
        twin = bit_permute(held, 0)
        early = joined(early, far_early)
        far, early, late, bias_full = lax.optimization_barrier((far, early, late, bias_full))
        attend_halves = (held, far, twin, bit_permute(far, 0))
        far_early, far_late = cube_permute(early, 2), cube_permute(late, 2, LATE_ORDERS)
        qkv, wide, wide_out = project(where, spots, normed, attend_halves, bias_full, ())
        far_early, far_late, qkv = lax.optimization_barrier((far_early, far_late, qkv))
        early, late = joined(early, far_early), joined(late, far_late)
        far_early, far_late = cube_permute(early, 3), cube_permute(late, 3, LATE_ORDERS)
        twin_early, twin_late = bit_permute(early, 0), bit_permute(late, 0)
        mixture, log_totals = attend_forward(where, lengths, qkv, (early, late))
        far_early, far_late, twin_late, mixture = lax.optimization_barrier(
            (far_early, far_late, twin_late, mixture)
        )
        last_early, last_late = bit_permute(far_early, 0), bit_permute(far_late, 0)
        middle, hidden_in, hidden_t, unit, inverse = attend_out(mixture, wide_out, tokens, layer_vectors)
        feed_halves = (early, far_early, twin_early, last_early, late, far_late, twin_late, last_late)
    else:

        def planes(shard):
            full = lax.all_gather(lax.all_gather(shard, "dp", axis=0, tiled=True), "mp", axis=0)
            full = full.reshape(2, 2, 8, depth // 8, shard.shape[1]).transpose(1, 0, 2, 3, 4)
            return tuple(full.reshape(4, 8, depth // 8, shard.shape[1]))

        normed, normed_t, upstream_t = prepare(tokens, cotangent, layer_vectors, ())
        bias_full = lax.psum(bias_full, "mp")
        qkv, wide, wide_out = project(where, spots, normed, planes(attend_shard), bias_full, ())
        mixture, log_totals = attend_forward(where, lengths, qkv, ())
        middle, hidden_in, hidden_t, unit, inverse = attend_out(mixture, wide_out, tokens, layer_vectors)
        split = depth // 8 * 2 // 3
        feed_planes = planes(feed_shard)
        feed_halves = tuple(array[:, :split] for array in feed_planes) + tuple(
            array[:, split:] for array in feed_planes
        )
    block_out, back, keep_early, send_early, keep_late, send_late, bias_grad = feed(
        where,
        spots,
        hidden_in,
        hidden_t,
        cotangent,
        upstream_t,
        feed_halves,
        bias_full,
        middle,
        layer_vectors,
    )
    middle_grad, mixture_grad, output_grad, middle_sums = middle_back(
        where, lengths, back, unit, inverse, cotangent, mixture, wide_out, layer_vectors
    )
    if cube:
        twin_early, twin_late = bit_permute(send_early[8:], 0), bit_permute(send_late[8:], 0)
        twin_early, twin_late, mixture_grad, send_early, send_late = lax.optimization_barrier(
            (twin_early, twin_late, mixture_grad, send_early, send_late)
        )
        away = (keep_early[8:].astype(f32) + twin_early.astype(f32)).astype(low)
        far_away_late = (keep_late[8:].astype(f32) + twin_late.astype(f32)).astype(low)
        early = [keep_early[:8], bit_permute(send_early[:8], 0)]
        late = [keep_late[:8], bit_permute(send_late[:8], 0)]
        packed_grad = attend_backward(
            where, lengths, qkv, mixture_grad, log_totals, (away, far_away_late)
        )
        early = early + [cube_permute(away, 3)]
        late = late + [cube_permute(far_away_late, 3, LATE_ORDERS)]
        early[0], late[0], packed_grad = lax.optimization_barrier((early[0], late[0], packed_grad))
        away, far_away_late = leaving(early, 2), leaving(late, 2)
        sums = (middle_sums, bias_grad)
        keep_attend, send_attend, rider = input_grad(
            where, spots, normed_t, packed_grad, output_grad, sums, 16, depth // 8, (away, far_away_late)
        )
        early = staying(early, 2) + [cube_permute(away, 2)]
        late = staying(late, 2) + [cube_permute(far_away_late, 2, LATE_ORDERS)]
        early[-1], late[-1], send_attend = lax.optimization_barrier((early[-1], late[-1], send_attend))
        twin_b, rider, _ = with_rider(send_attend[8:], rider, lambda values: bit_permute(values, 0))
        twin_a = bit_permute(send_attend[:8], 0)
        away = (keep_attend[8:].astype(f32) + twin_b.astype(f32)).astype(low)
        arrived, rider, message = with_rider(away, rider, lambda values: cube_permute(values, 3))
        attend_parts = [keep_attend[:8], twin_a, arrived]
        feed_away = leaving(early, 1)
        token_grad, token_sums = token_back(
            packed_grad, wide, tokens, middle_grad, layer_vectors, (message, feed_away)
        )
        early = staying(early, 1) + [cube_permute(feed_away, 1)]
        attend_parts[0], late[0], token_sums = lax.optimization_barrier(
            (attend_parts[0], late[0], token_sums)
        )
        feed_away = leaving(late, 1)
        late = staying(late, 1) + [cube_permute(feed_away, 1, LATE_ORDERS)]
        away = leaving(attend_parts, 2)
        arrived, rider, message = with_rider(away, rider, lambda values: cube_permute(values, 2))
        attend_parts = staying(attend_parts, 2) + [arrived]
        message, early[0], late[0] = lax.optimization_barrier((message, early[0], late[0]))
        feed_away = leaving(early, 0)
        early = staying(early, 0) + [cube_permute(feed_away, 0)]
        away = leaving(attend_parts, 1)
        arrived, rider, message = with_rider(away, rider, lambda values: cube_permute(values, 1))
        attend_parts = staying(attend_parts, 1) + [arrived]
        message, early[0], late[0] = lax.optimization_barrier((message, early[0], late[0]))
        early_total = summed(early)
        feed_away = leaving(late, 0)
        late = staying(late, 0) + [cube_permute(feed_away, 0, LATE_ORDERS)]
        arrays = list(bring(arrays, (message,)))
        attend_parts[0], arrays[0] = lax.optimization_barrier((attend_parts[0], arrays[0]))
        away = leaving(attend_parts, 0)
        away, early_total = lax.optimization_barrier((away, early_total))
        arrived, vector_total, _ = with_rider(away, rider, lambda values: cube_permute(values, 0))
        attend_parts = staying(attend_parts, 0) + [arrived]
        late_total = summed(late)
        feed_totals = (early_total, late_total)
        attend_total, owned = last_sum(attend_parts, early_total, late_total, token_sums)
        owned = cube_sum(owned)
    else:
        packed_grad = attend_backward(where, lengths, qkv, mixture_grad, log_totals, ())
        sums = (middle_sums, bias_grad)
        keep_attend, send_attend, vector_total = input_grad(
            where, spots, normed_t, packed_grad, output_grad, sums, 16, depth // 8, ()
        )
        token_grad, token_sums = token_back(packed_grad, wide, tokens, middle_grad, layer_vectors, ())
        vector_total = lax.psum(vector_total, ("dp", "mp"))

    if not cube:

        def own_block(keep, send):
            full = jnp.stack([keep, send]).reshape(2, 2, 8, keep.shape[1], keep.shape[2])
            full = full.transpose(1, 0, 2, 3, 4).reshape(4, 8 * keep.shape[1], keep.shape[2])
            full = lax.psum_scatter(full, "mp", scatter_dimension=0, tiled=False)
            return lax.psum(full, "dp")

        def own_rows(*blocks):
            full = jnp.concatenate([block.reshape(8, -1, block.shape[1]) for block in blocks], axis=1)
            full = full.reshape(depth, full.shape[2]).astype(f32)
            return lax.dynamic_slice_in_dim(full, lax.axis_index("dp") * rows, rows, 0)

        attend_total = own_rows(own_block(keep_attend, send_attend))
        feed_total = own_rows(own_block(keep_early, send_early), own_block(keep_late, send_late))
        feed_totals = feed_total[: rows * 2 // 3], feed_total[rows * 2 // 3 :]
        attend_total, owned = last_sum((attend_total[None],), *feed_totals, token_sums)
        owned = lax.psum(owned, ("dp", "mp"))
    grad_norm, *updates = optimize(where, owned, vector_total, attend_total, feed_totals, arrays)
    grad_norm = grad_norm[0, 0]
    moment_input, square_input, updated_input = (turned(array) for array in updates[:3])
    moment_output, square_output, updated_output = updates[3:6]
    moment_expand, square_expand, updated_expand = updates[6:9]
    moment_shrink, square_shrink, updated_shrink = (array.T for array in updates[9:12])
    moment_vectors, square_vectors, updated_vectors = updates[12:15]
    moment_head, square_head, updated_head = updates[15:18]
    moment_bias, square_bias, updated_bias = (array.reshape(hidden) for array in updates[18:])
    return (
        block_out,
        token_grad,
        grad_norm,
        moment_input,
        square_input,
        updated_input,
        moment_output,
        square_output,
        updated_output,
        moment_expand,
        square_expand,
        updated_expand,
        moment_shrink,
        square_shrink,
        updated_shrink,
        moment_vectors,
        square_vectors,
        updated_vectors,
        moment_head,
        square_head,
        updated_head,
        moment_bias,
        square_bias,
        updated_bias,
    )


def solution(mesh):
    in_specs = (
        P(("dp", "mp"), None),
        P(("dp", "mp"), None),
        P("dp"),
        P("dp", None, "mp"),
        P("mp", "dp"),
        P("dp", "mp"),
        P("mp", "dp"),
        P(),
        P(None, "mp"),
        P("mp"),
        P("dp", None, "mp"),
        P("mp", "dp"),
        P("dp", "mp"),
        P("mp", "dp"),
        P(),
        P(None, "mp"),
        P("mp"),
        P("dp", None, "mp"),
        P("mp", "dp"),
        P("dp", "mp"),
        P("mp", "dp"),
        P(),
        P(None, "mp"),
        P("mp"),
    )
    out_specs = (
        P(("dp", "mp"), None),
        P(("dp", "mp"), None),
        P(),
        P("dp", None, "mp"),
        P("dp", None, "mp"),
        P("dp", None, "mp"),
        P("mp", "dp"),
        P("mp", "dp"),
        P("mp", "dp"),
        P("dp", "mp"),
        P("dp", "mp"),
        P("dp", "mp"),
        P("mp", "dp"),
        P("mp", "dp"),
        P("mp", "dp"),
        P(),
        P(),
        P(),
        P(None, "mp"),
        P(None, "mp"),
        P(None, "mp"),
        P("mp"),
        P("mp"),
        P("mp"),
    )
    return jax.shard_map(shards, mesh=mesh, in_specs=in_specs, out_specs=out_specs, check_vma=False)
```

```python
import functools
import jax
import jax.numpy as jnp
from jax import lax
from jax.experimental import pallas as pl
from jax.experimental.pallas import tpu as pltpu
from jax.sharding import PartitionSpec as P

HEAD_DIM = 64
TILE = 256
STEP = 10

eps_norm = 1e-05
clip_norm = 1.0
beta_one = 0.9
beta_two = 0.999
adam_eps = 1e-08
rate = 0.05
vector_rate = 0.5
decay = 0.01
excluded = -1e30
low = jnp.bfloat16
f32 = jnp.float32
GELU_A = 0.7978845608028654
GELU_B = GELU_A * 0.044715


def params(limit_mib, **kw):
    return pltpu.CompilerParams(vmem_limit_bytes=limit_mib * 1024 * 1024, **kw)


def cost(flops, moved, special=0):
    return pl.CostEstimate(flops=int(flops), bytes_accessed=int(moved), transcendentals=int(special))


def mm(a, b):
    return jnp.dot(a, b, preferred_element_type=f32)


def mm_nt(a, b):
    return lax.dot_general(a, b, (((1,), (1,)), ((), ())), preferred_element_type=f32)


def whole(shape):
    zeros = (0,) * len(shape)
    return pl.BlockSpec(shape, lambda *_: zeros)


def once(shape):
    zeros = (0,) * len(shape)
    return pl.BlockSpec(shape, lambda *_: zeros, pipeline_mode=pl.Buffered(1))


def held_back(body, first, count):
    def run(*refs):
        return body(*refs[:first], *refs[first + count :])

    return run


LATER = pl.BlockSpec(memory_space=pl.ANY)


def far_away(shape, dtype):
    return pltpu.HBM(shape, dtype)


def from_far(*arrays):
    return [pltpu.with_memory_space_constraint(array, pltpu.HBM) for array in arrays]


def sds(shape, dtype):
    return jax.ShapeDtypeStruct(shape, dtype)


def live_blocks(length, count, body):
    for blocks in range(1, count + 1):
        low_end = (blocks - 1) * TILE
        high_end = blocks * TILE
        @pl.when((length > low_end) & (length <= high_end))
        def _(blocks=blocks):
            body(length, blocks)


PAIR = 2 * HEAD_DIM


def span(block):
    return slice(block * TILE, (block + 1) * TILE)


def both_heads(values):
    lane = lax.broadcasted_iota(jnp.int32, values.shape, 1)
    none = jnp.zeros_like(values)
    return jnp.concatenate(
        [jnp.where(lane < HEAD_DIM, values, none), jnp.where(lane >= HEAD_DIM, values, none)], axis=0
    )


def causal_mask():
    key_id = lax.broadcasted_iota(jnp.int32, (TILE, 2 * TILE), 0)
    query_id = lax.broadcasted_iota(jnp.int32, (TILE, 2 * TILE), 1) & (TILE - 1)
    return key_id <= query_id


def forward_body(where_ref, lengths_ref, q_ref, k_ref, v_ref, o_ref, lse_ref, vt_ref):
    seq = q_ref.shape[0]
    vt_ref[...] = v_ref[...].T
    causal = causal_mask()

    def run(length, blocks):
        def scores(b):
            q = q_ref[span(b), :] * jnp.asarray(HEAD_DIM**-0.5, low)
            return mm_nt(k_ref[: (b + 1) * TILE, :], both_heads(q))

        now = scores(0)
        for b in range(blocks):
            start, stop = b * TILE, (b + 1) * TILE
            later = scores(b + 1) if b + 1 < blocks else None
            last = jnp.where(causal, now[start:, :], excluded)
            top = jnp.max(last, axis=0, keepdims=True)
            if b:
                top = jnp.maximum(top, jnp.max(now[:start], axis=0, keepdims=True))
            p = jnp.exp(last - top)
            total = jnp.sum(p, axis=0, keepdims=True)
            pb = p.astype(low)
            if b:
                pf = jnp.exp(now[:start] - top)
                total = total + jnp.sum(pf, axis=0, keepdims=True)
                pb = jnp.concatenate([pf.astype(low), pb], axis=0)
            inverse = 1.0 / total
            lse = top + jnp.log(total)
            outs = []
            for h in range(2):
                at = slice(h * TILE, (h + 1) * TILE)
                out = mm(vt_ref[h * HEAD_DIM : (h + 1) * HEAD_DIM, :stop], pb[:, at])
                outs.append(out * inverse[:, at])
                lse_ref[0, h : h + 1, start:stop] = lse[:, at]
            both = jnp.concatenate(outs, axis=0).T
            row = start + lax.broadcasted_iota(jnp.int32, both.shape, 0)
            o_ref[start:stop, :] = jnp.where(row < length, both, 0.0).astype(low)
            now = later
        if blocks * TILE < seq:
            o_ref[blocks * TILE :, :] = jnp.zeros((seq - blocks * TILE, PAIR), low)
            lse_ref[0, :, blocks * TILE :] = jnp.zeros((2, seq - blocks * TILE), f32)

    live_blocks(lengths_ref[where_ref[2]], seq // TILE, run)


def attend_forward(where, lengths, qkv, after):
    seq, width = qkv.shape[0], qkv.shape[1] // 3
    pair = 2 * HEAD_DIM
    pairs = width // pair
    half = seq * seq * 5 // 8
    spec = lambda part: pl.BlockSpec((seq, pair), lambda i, *_: (0, part * pairs + i))
    return pl.pallas_call(
        held_back(forward_body, 5, len(after)),
        grid_spec=pltpu.PrefetchScalarGridSpec(
            num_scalar_prefetch=2,
            grid=(pairs,),
            in_specs=[spec(0), spec(1), spec(2)] + [LATER] * len(after),
            out_specs=[
                pl.BlockSpec((seq, pair), lambda i, *_: (0, i)),
                pl.BlockSpec((1, 2, seq), lambda i, *_: (i, 0, 0)),
            ],
            scratch_shapes=[pltpu.VMEM((pair, seq), low)],
        ),
        out_shape=[sds((seq, width), low), far_away((pairs, 2, seq), f32)],
        compiler_params=params(20),
        cost_estimate=cost(pairs * 2 * half * 2 * 2 * 256, seq * width * 8, pairs * 2 * half),
        name="attend_forward",
    )(where, lengths, *from_far(qkv, qkv, qkv), *after)


def backward_body(where_ref, lengths_ref, q_ref, k_ref, v_ref, do_ref, lse_ref, out_ref, kt_ref, ksum, vsum):
    seq = q_ref.shape[0]
    scale = HEAD_DIM**-0.5
    kt_ref[...] = k_ref[...].T
    causal = causal_mask()

    def run(length, blocks):
        def scores(b):
            qq = both_heads(q_ref[span(b), :] * jnp.asarray(scale, low))
            uu = both_heads(do_ref[span(b), :])
            stop = (b + 1) * TILE
            return qq, uu, mm_nt(k_ref[:stop, :], qq), mm_nt(v_ref[:stop, :], uu)

        now = scores(blocks - 1)
        for b in reversed(range(blocks)):
            start, stop = b * TILE, (b + 1) * TILE
            later = scores(b - 1) if b else None
            qq, uu, s, dp = now
            lse = jnp.concatenate([lse_ref[0, 0:1, start:stop], lse_ref[0, 1:2, start:stop]], axis=1)
            p = jnp.exp(jnp.where(causal, s[start:], excluded) - lse)
            inner = jnp.sum(p * dp[start:], axis=0, keepdims=True)
            if b:
                pf = jnp.exp(s[:start] - lse)
                inner = inner + jnp.sum(pf * dp[:start], axis=0, keepdims=True)
            ds = (p * (dp[start:] - inner)).astype(low)
            pb = p.astype(low)
            if b:
                ds = jnp.concatenate([(pf * (dp[:start] - inner)).astype(low), ds], axis=0)
                pb = jnp.concatenate([pf.astype(low), pb], axis=0)
            dq = jnp.concatenate(
                [
                    mm(
                        kt_ref[h * HEAD_DIM : (h + 1) * HEAD_DIM, :stop],
                        ds[:, h * TILE : (h + 1) * TILE],
                    )
                    for h in range(2)
                ],
                axis=0,
            )
            dk, dv = mm(ds, qq), mm(pb, uu)
            if b == blocks - 1:
                ksum[:stop, :] = dk
                vsum[:stop, :] = dv
            else:
                ksum[:stop, :] += dk
                vsum[:stop, :] += dv
            out_ref[1, start:stop, :] = ksum[start:stop, :].astype(low)
            out_ref[2, start:stop, :] = vsum[start:stop, :].astype(low)
            out_ref[0, start:stop, :] = (dq.T * scale).astype(low)
            now = later
        if blocks * TILE < seq:
            rest = jnp.zeros((seq - blocks * TILE, PAIR), low)
            for part in range(3):
                out_ref[part, blocks * TILE :, :] = rest

    live_blocks(lengths_ref[where_ref[2]], seq // TILE, run)


def attend_backward(where, lengths, qkv, upstream, lse, after):
    seq, width = upstream.shape
    pair = 2 * HEAD_DIM
    pairs = width // pair
    half = seq * seq * 5 // 8
    spec = lambda part: pl.BlockSpec((seq, pair), lambda i, *_: (0, part * pairs + i))
    own = pl.BlockSpec((seq, pair), lambda i, *_: (0, i))
    return pl.pallas_call(
        held_back(backward_body, 7, len(after)),
        grid_spec=pltpu.PrefetchScalarGridSpec(
            num_scalar_prefetch=2,
            grid=(pairs,),
            in_specs=[spec(0), spec(1), spec(2), own, pl.BlockSpec((1, 2, seq), lambda i, *_: (i, 0, 0))]
            + [LATER] * len(after),
            out_specs=pl.BlockSpec((3, seq, pair), lambda i, *_: (0, 0, i)),
            scratch_shapes=[
                pltpu.VMEM((pair, seq), low),
                pltpu.VMEM((seq, pair), f32),
                pltpu.VMEM((seq, pair), f32),
            ],
        ),
        out_shape=sds((3, seq, width), low),
        compiler_params=params(28),
        cost_estimate=cost(pairs * 2 * half * 5 * 2 * 256, seq * width * 14, pairs * 2 * half),
        name="attend_backward",
    )(where, lengths, *from_far(qkv, qkv, qkv), upstream, *from_far(lse), *after)


def normalize(values):
    average = jnp.mean(values, axis=-1, keepdims=True)
    centred = values - average
    inverse = lax.rsqrt(jnp.mean(centred * centred, axis=-1, keepdims=True) + eps_norm)
    return centred * inverse, inverse


def pull_norm(scaled, unit, inverse):
    first = jnp.mean(scaled, axis=-1, keepdims=True)
    second = jnp.mean(scaled * unit, axis=-1, keepdims=True)
    return inverse * (scaled - first - unit * second)


def columns_of(values):
    return jnp.sum(values, axis=0, keepdims=True)


def pack_body(
    input_ref, output_ref, expand_ref, shrink_ref, head_ref, hidden_ref, attend_ref, feed_ref, bias_ref
):
    width = input_ref.shape[2]
    part = expand_ref.shape[1] // 3
    for index in range(3):
        attend_ref[:, index * width : (index + 1) * width] = input_ref[index].astype(low)
        at = slice(index * part, (index + 1) * part)
        feed_ref[:, 2 * index * part : (2 * index + 1) * part] = expand_ref[:, at].astype(low)
        feed_ref[:, (2 * index + 1) * part : (2 * index + 2) * part] = shrink_ref[:, at].astype(low)
    attend_ref[:, 3 * width :] = output_ref[...].T.astype(low)
    pieces = [head_ref[0:1, :], head_ref[1:2, :]]
    pieces += [hidden_ref[row : row + 1, :] for row in range(hidden_ref.shape[0])]
    bias_ref[...] = jnp.zeros_like(bias_ref)
    bias_ref[pl.ds(lax.axis_index("mp"), 1), :] = jnp.concatenate(pieces, axis=1)


def pack(input_weight, output_weight, expand, shrink, head_bias, hidden_bias):
    rows, width = input_weight.shape[1:]
    hidden = expand.shape[1]
    return pl.pallas_call(
        pack_body,
        out_shape=[
            sds((rows, 4 * width), low),
            sds((rows, 2 * hidden), low),
            sds((4, 2 * width + hidden), f32),
        ],
        compiler_params=params(6),
        cost_estimate=cost(rows * hidden, rows * hidden * 18),
        name="pack",
    )(*from_far(input_weight, output_weight, expand, shrink, head_bias, hidden_bias))


def prepare_body(x_ref, up_ref, vec_ref, h_ref, ht_ref, upt_ref):
    unit, _ = normalize(x_ref[...].astype(f32))
    h = (unit * vec_ref[0:1, :] + vec_ref[1:2, :]).astype(low)
    h_ref[...] = h
    ht_ref[...] = h.T
    upt_ref[...] = up_ref[...].T


def prepare(x, up, vectors, after):
    seq, depth = x.shape
    rows = pl.BlockSpec((2 * TILE, depth), lambda i: (i, 0))
    turned = pl.BlockSpec((depth, 2 * TILE), lambda i: (0, i))
    return pl.pallas_call(
        held_back(prepare_body, 3, len(after)),
        grid=(seq // (2 * TILE),),
        in_specs=[rows, rows, once(vectors.shape)] + [LATER] * len(after),
        out_specs=[rows, turned, turned],
        out_shape=[sds((seq, depth), low), sds((depth, seq), low), far_away((depth, seq), low)],
        compiler_params=params(16),
        cost_estimate=cost(seq * depth * 10, seq * depth * 10),
        name="prepare",
    )(*from_far(x, up), vectors, *after)


def slot(halves, spot, at):
    first, second = halves
    inner = spot & 7
    return jnp.where(spot < 8, first[inner, :, at], second[inner, :, at])


def project_body(
    where_ref, spots_ref, h_ref, mine_a, mine_b, twin_a, twin_b, bias_ref, qkv_ref, wide_ref, last_ref
):
    part = pl.program_id(0)
    rows = mine_a.shape[1]
    width = mine_a.shape[2] // 4
    groups = wide_ref.shape[1] // rows

    def collect(sources, index):
        columns = slice(index * width, (index + 1) * width)
        for group in range(groups):
            pieces = [slot(sources[model % 2], spots_ref[model, group], columns) for model in range(4)]
            at = slice(group * rows, (group + 1) * rows)
            if index < 3:
                wide_ref[0, at, :] = jnp.concatenate(pieces, axis=1)
            else:
                last_ref[at, :] = jnp.concatenate(pieces, axis=1)

    for index in range(4):
        for core in range(2):

            @pl.when((part == index) & (where_ref[0] == core))
            def _(index=index, core=core):
                mine, twin = (mine_a, mine_b), (twin_a, twin_b)
                collect((mine, twin) if core == 0 else (twin, mine), index)

    for index in range(3):

        @pl.when(part == index)
        def _(index=index):
            out = mm(h_ref[...], wide_ref[0])
            if index != 1:
                at = slice(index // 2 * width, (index // 2 + 1) * width)
                bias = jnp.concatenate([bias_ref[model : model + 1, at] for model in range(4)], axis=1)
                out = out + bias
            qkv_ref[...] = out.astype(low)


def project(where, spots, h, halves, bias, after):
    seq, depth = h.shape
    return pl.pallas_call(
        held_back(project_body, 8, len(after)),
        grid_spec=pltpu.PrefetchScalarGridSpec(
            num_scalar_prefetch=2,
            grid=(4,),
            in_specs=[
                once((seq, depth)),
                *[once(halves[0].shape)] * 4,
                once(bias.shape),
            ]
            + [LATER] * len(after),
            out_specs=[
                pl.BlockSpec((seq, depth), lambda i, *_: (0, jnp.minimum(i, 2))),
                pl.BlockSpec((1, depth, depth), lambda i, *_: (jnp.minimum(i, 2), 0, 0)),
                whole((depth, depth)),
            ],
        ),
        out_shape=[
            far_away((seq, 3 * depth), low),
            far_away((3, depth, depth), low),
            sds((depth, depth), low),
        ],
        compiler_params=params(24),
        cost_estimate=cost(2 * seq * depth * depth * 3, seq * depth * 16),
        name="project",
    )(where, spots, h, *halves, bias, *after)


NEAR = pl.BlockSpec(memory_space=pltpu.VMEM)
SCALARS = pl.BlockSpec(memory_space=pltpu.SMEM)


def attend_out_body(o_ref, w_ref, x_ref, vec_ref, middle_ref, h_ref, ht_ref, unit_ref, inverse_ref):
    for tile in range(o_ref.shape[0] // TILE):
        at = slice(tile * TILE, (tile + 1) * TILE)
        middle = x_ref[at, :].astype(f32) + mm_nt(o_ref[at, :], w_ref[...]) + vec_ref[4:5, :]
        middle_ref[at, :] = middle.astype(low)
        unit, inverse = normalize(middle)
        unit_ref[at, :] = unit.astype(low)
        inverse_ref[at, :] = jnp.broadcast_to(inverse, (TILE, inverse_ref.shape[1]))
        h = (unit * vec_ref[2:3, :] + vec_ref[3:4, :]).astype(low)
        h_ref[at, :] = h
        ht_ref[:, at] = h.T


def attend_out(o, wide_out, x, vectors):
    seq, depth = x.shape
    return pl.pallas_call(
        attend_out_body,
        in_specs=[NEAR] * 4,
        out_specs=[NEAR] * 5,
        out_shape=[
            sds((seq, depth), low),
            sds((seq, depth), low),
            sds((depth, seq), low),
            sds((seq, depth), low),
            sds((seq, 128), f32),
        ],
        compiler_params=params(10),
        cost_estimate=cost(2 * seq * depth * depth, seq * depth * 14),
        name="attend_out",
    )(o, wide_out, x, vectors)


def feed_body(
    where_ref,
    spots_ref,
    h2_ref,
    h2t_ref,
    up_ref,
    upt_ref,
    mine_a,
    mine_b,
    twin_a,
    twin_b,
    mine_c,
    mine_d,
    twin_c,
    twin_d,
    bias_ref,
    middle_ref,
    vec_ref,
    block_ref,
    back_ref,
    keep_a,
    send_a,
    keep_b,
    send_b,
    bias_grad_ref,
    out_ref,
    sum_ref,
    wide_ref,
    act_ref,
    pre_ref,
):
    part = mine_a.shape[2] // 6
    groups = spots_ref.shape[1]
    rows = wide_ref.shape[0] // groups
    split = mine_a.shape[1]
    skip = bias_ref.shape[1] - bias_grad_ref.shape[1]
    pieces = (
        ((mine_a, mine_b), (twin_a, twin_b), 0, slice(0, split)),
        ((mine_c, mine_d), (twin_c, twin_d), 4, slice(split, rows)),
    )
    half = keep_a.shape[1]
    results = ((keep_a, send_a, 0, slice(0, half)), (keep_b, send_b, 4, slice(half, rows)))
    out_ref[...] = middle_ref[...].astype(f32) + vec_ref[5:6, :]
    sum_ref[...] = jnp.zeros_like(sum_ref)

    def step(index, carry):
        side = lax.rem(index, 2)
        first = pl.multiple_of(index // 2 * part, 128)
        lanes = pl.ds(pl.multiple_of(2 * first, 128), part)
        next_lanes = pl.ds(pl.multiple_of(2 * first + part, 128), part)
        models = [where_ref[1] ^ (2 * side + core) for core in range(2)]
        for group in range(groups):
            for mine, twin, table, within in pieces:
                at = slice(group * rows + within.start, group * rows + within.stop)
                for core, halves in enumerate((mine, twin)):
                    spot = spots_ref[table + models[core], group]
                    wide_ref[at, core * part : (core + 1) * part] = slot(halves, spot, lanes)
                    wide_ref[at, (2 + core) * part : (3 + core) * part] = slot(halves, spot, next_lanes)

        expand = wide_ref[:, : 2 * part]
        shrink = wide_ref[:, 2 * part :]
        bias = jnp.concatenate(
            [bias_ref[pl.ds(model, 1), pl.ds(pl.multiple_of(skip + first, 128), part)] for model in models],
            axis=1,
        )
        sums = jnp.zeros((1, 2 * part), f32)
        for tile in range(h2_ref.shape[0] // TILE):
            at = slice(tile * TILE, (tile + 1) * TILE)
            u = mm(h2_ref[at, :], expand) + bias
            square = u * u
            th = jnp.tanh(u * (GELU_A + GELU_B * square))
            gate = 0.5 * th + 0.5
            slope = gate + (gate * (1.0 - gate)) * (u * (2.0 * GELU_A + (6.0 * GELU_B) * square))
            pre = (mm(up_ref[at, :], shrink) * slope).astype(low)
            act_ref[at, :] = (u * gate).astype(low)
            pre_ref[at, :] = pre
            sums = sums + columns_of(pre.astype(f32))
        for core, model in enumerate(models):
            bias_grad_ref[pl.ds(model, 1), pl.ds(first, part)] = sums[:, core * part : (core + 1) * part]
        out_ref[...] += mm_nt(act_ref[...], shrink)
        sum_ref[...] += mm_nt(pre_ref[...], expand)
        grad_expand = mm(h2t_ref[...], pre_ref[...]).astype(low)
        grad_shrink = mm(upt_ref[...], act_ref[...]).astype(low)
        for group in range(groups):
            for keep, send, table, within in results:
                at = slice(group * rows + within.start, group * rows + within.stop)
                for core, target in enumerate((keep, send)):
                    spot = spots_ref[table + models[core], group]
                    columns = slice(core * part, (core + 1) * part)
                    target[spot, :, lanes] = grad_expand[at, columns]
                    target[spot, :, next_lanes] = grad_shrink[at, columns]
        return carry

    lax.fori_loop(0, 6, step, 0)
    block_ref[...] = out_ref[...].astype(low)
    back_ref[...] = sum_ref[...].astype(low)


def feed(where, spots, h2, h2t, up, upt, halves, bias, middle, vectors):
    seq, depth = h2.shape
    half, _, columns = halves[0].shape
    part = columns // 6
    splits = [halves[0].shape[1], halves[4].shape[1]]
    return pl.pallas_call(
        feed_body,
        in_specs=[SCALARS] * 2 + [NEAR] * 15,
        out_specs=[NEAR] * 7,
        scratch_shapes=[
            pltpu.VMEM((seq, depth), f32),
            pltpu.VMEM((seq, depth), f32),
            pltpu.VMEM((depth, 4 * part), low),
            pltpu.VMEM((seq, 2 * part), low),
            pltpu.VMEM((seq, 2 * part), low),
        ],
        out_shape=[sds((seq, depth), low)] * 2
        + [sds((2 * half, rows, columns), low) for rows in splits for _ in range(2)]
        + [sds((4, 3 * part), f32)],
        compiler_params=params(22),
        cost_estimate=cost(12 * seq * depth * 12 * part, seq * depth * 40, seq * 6 * part),
        name="feed",
    )(where, spots, h2, h2t, up, upt, *halves, bias, middle, vectors)


def middle_back_body(
    where_ref,
    lengths_ref,
    back_ref,
    unit_ref,
    inverse_ref,
    up_ref,
    o_ref,
    w_ref,
    vec_ref,
    grad_ref,
    mixture_ref,
    weight_ref,
    sums_ref,
    turned_ref,
):
    length = lengths_ref[where_ref[2]]
    sums = jnp.zeros(sums_ref.shape, f32)
    for tile in range(back_ref.shape[0] // TILE):
        at = slice(tile * TILE, (tile + 1) * TILE)
        unit, inverse = unit_ref[at, :].astype(f32), inverse_ref[at, 0:1]
        back = back_ref[at, :].astype(f32)
        up = up_ref[at, :].astype(f32)
        grad = up + pull_norm(back * vec_ref[2:3, :], unit, inverse)
        rounded = grad.astype(low)
        grad_ref[at, :] = rounded
        turned_ref[:, at] = rounded.T
        row = tile * TILE + lax.broadcasted_iota(jnp.int32, grad.shape, 0)
        mixture_ref[at, :] = jnp.where(row < length, mm(rounded, w_ref[...]), 0.0).astype(low)
        sums = sums + jnp.concatenate(
            [columns_of(back * unit), columns_of(back), columns_of(grad), columns_of(up)], axis=0
        )
    sums_ref[...] = sums
    weight_ref[...] = mm(turned_ref[...], o_ref[...]).astype(low)


def middle_back(where, lengths, back, unit, inverse, up, o, wide_out, vectors):
    seq, depth = unit.shape
    return pl.pallas_call(
        middle_back_body,
        in_specs=[SCALARS] * 2 + [NEAR] * 7,
        out_specs=[NEAR] * 4,
        scratch_shapes=[pltpu.VMEM((depth, seq), low)],
        out_shape=[
            sds((seq, depth), low),
            sds((seq, depth), low),
            sds((depth, depth), low),
            sds((4, depth), f32),
        ],
        compiler_params=params(14),
        cost_estimate=cost(4 * seq * depth * depth, seq * depth * 28),
        name="middle_back",
    )(where, lengths, back, unit, inverse, up, o, wide_out, vectors)


def input_grad_body(
    where_ref,
    spots_ref,
    ht_ref,
    back_ref,
    out_grad_ref,
    middle_ref,
    bias_ref,
    keep_ref,
    send_ref,
    sums_ref,
):
    rows = keep_ref.shape[1]
    width = keep_ref.shape[2] // 4
    groups = ht_ref.shape[0] // rows

    def spread(targets, index, grad):
        at = slice(index * width, (index + 1) * width)
        for group in range(groups):
            for model in range(4):
                targets[model % 2][spots_ref[model, group], :, at] = grad[
                    group * rows : (group + 1) * rows, model * width : (model + 1) * width
                ]

    sums_ref[:2] = jnp.zeros((2, sums_ref.shape[1]), f32)
    sums_ref[2:6] = middle_ref[...]
    sums_ref[6:7] = columns_of(back_ref[0].astype(f32))
    sums_ref[7:8] = columns_of(back_ref[2].astype(f32))
    sums_ref[8:] = bias_ref[...]
    for index in range(4):
        grad = mm(ht_ref[...], back_ref[index]).astype(low) if index < 3 else out_grad_ref[...]
        for core in range(2):

            @pl.when(where_ref[0] == core)
            def _(core=core, index=index, grad=grad):
                spread((keep_ref, send_ref) if core == 0 else (send_ref, keep_ref), index, grad)


def input_grad(where, spots, ht, back, out_grad, sums, slots, rows, after):
    depth, seq = ht.shape
    shape = (slots, rows, depth)
    return pl.pallas_call(
        held_back(input_grad_body, 7, len(after)),
        in_specs=[SCALARS] * 2 + [NEAR] * 5 + [LATER] * len(after),
        out_specs=[NEAR] * 3,
        out_shape=[sds(shape, low), sds(shape, low), sds((12, depth), f32)],
        compiler_params=params(14),
        cost_estimate=cost(6 * seq * depth * depth, seq * depth * 14),
        name="input_grad",
    )(where, spots, ht, back, out_grad, *sums, *after)


def token_back_body(
    back_ref, w_ref, x_ref, grad_ref, vec_ref, token_ref, sums_ref
):
    step = pl.program_id(0)
    back = mm_nt(back_ref[0], w_ref[0]) + mm_nt(back_ref[1], w_ref[1]) + mm_nt(back_ref[2], w_ref[2])
    unit, inverse = normalize(x_ref[...].astype(f32))
    grad = grad_ref[...].astype(f32)
    token_ref[...] = (grad + pull_norm(back * vec_ref[0:1, :], unit, inverse)).astype(low)
    sums = jnp.concatenate([columns_of(back * unit), columns_of(back)], axis=0)

    @pl.when(step == 0)
    def _():
        sums_ref[...] = sums

    @pl.when(step > 0)
    def _():
        sums_ref[...] += sums


def token_back(back, wide, x, grad, vectors, after):
    seq, depth = x.shape
    rows = pl.BlockSpec((TILE, depth), lambda i: (i, 0))
    return pl.pallas_call(
        held_back(token_back_body, 5, len(after)),
        grid=(seq // TILE,),
        in_specs=[
            pl.BlockSpec((3, TILE, depth), lambda i: (0, i, 0)),
            pl.BlockSpec((3, depth, depth), lambda i: (0, 0, 0)),
            rows,
            rows,
            once(vectors.shape),
        ]
        + [LATER] * len(after),
        out_specs=[rows, whole((2, depth))],
        out_shape=[sds((seq, depth), low), sds((2, depth), f32)],
        compiler_params=params(24),
        cost_estimate=cost(6 * seq * depth * depth, seq * depth * 16),
        name="token_back",
    )(back, *from_far(wide, x), grad, vectors, *after)


CORE_ORDERS = ((4, 3, 2, 1), (3, 4, 1, 2))
LATE_ORDERS = ((2, 1, 4, 3), (1, 2, 3, 4))
STAGES = 4


def cube_permute(values, stage, orders=CORE_ORDERS):
    pairs = [(device, device ^ (1 << orders[device & 1][stage])) for device in range(32)]
    return lax.ppermute(values, ("dp", "mp"), pairs)


def bit_permute(values, bit):
    return lax.ppermute(values, ("dp", "mp"), [(device, device ^ (1 << bit)) for device in range(32)])


def place(distance, core, orders):
    spots = [
        sum(((distance >> bit) & 1) << step for step, bit in enumerate(order)) for order in orders
    ]
    return jnp.where(core == 0, spots[0], spots[1])


def joined(held, arrived):
    return jnp.concatenate([held, arrived], axis=0)


def leaving(parts, stage):
    half = 1 << stage
    return sum(part[half:].astype(f32) for part in parts).astype(low)


def staying(parts, stage):
    return [part[: 1 << stage] for part in parts]


def summed(parts):
    return sum(part[0].astype(f32) for part in parts)


def two_parts(values):
    high = lax.reduce_precision(values, 8, 7)
    rest = lax.reduce_precision(values - high, 8, 7)
    return jnp.concatenate([high, rest], axis=0).astype(low)


def one_part(parts):
    half = parts.shape[0] // 2
    return parts[:half].astype(f32) + parts[half:].astype(f32)


def with_rider(blocks, rider, send):
    count, rows, columns = blocks.shape
    parts = two_parts(rider)
    message = jnp.concatenate([blocks.reshape(count * rows, columns), parts], axis=0)
    arrived = send(message)
    total = one_part(parts) + one_part(arrived[count * rows :])
    return arrived[: count * rows].reshape(count, rows, columns), total, message


def cube_sum(values, bits=range(5)):
    for bit in bits:
        values = values + bit_permute(values, bit)
    return values


def adam_parts(weight, gradient, first_old, second_old, factor, step_rate):
    scaled = gradient * factor
    moment = beta_one * first_old + (1.0 - beta_one) * scaled
    square = beta_two * second_old + (1.0 - beta_two) * scaled * scaled
    spread = jnp.sqrt(square * (1.0 / (1.0 - beta_two**STEP)))
    ratio = moment * (1.0 / (1.0 - beta_one**STEP)) / (spread + adam_eps)
    return moment, square, weight - step_rate * (ratio + decay * weight)


def optimize_body(where_ref, owned_ref, vector_ref, attend_ref, feed_a, feed_b, *refs):
    state, outs = refs[:21], refs[21:]
    vectors = jnp.concatenate([owned_ref[:2], vector_ref[2:]], axis=0)
    total = owned_ref[2:3, 0:1] + jnp.sum(vectors * vectors)
    norm = jnp.sqrt(total)
    factor = clip_norm / jnp.maximum(norm, clip_norm)
    outs[0][...] = norm
    width = state[0].shape[2]
    part = state[6].shape[1] // 3

    def update(param, at, gradient, step_rate):
        weight, first, second = (ref[at] for ref in state[3 * param : 3 * param + 3])
        results = adam_parts(weight, gradient, first, second, factor, step_rate)
        for ref, result in zip(outs[1 + 3 * param : 4 + 3 * param], results):
            ref[at] = result

    for index in range(3):
        update(0, (index,), attend_ref[:, index * width : (index + 1) * width], rate)
    update(1, (...,), attend_ref[:, 3 * width :].T, rate)
    split, rows = feed_a.shape[0], state[6].shape[0]
    for feed_ref, within in ((feed_a, slice(0, split)), (feed_b, slice(split, rows))):
        for index in range(3):
            at = (within, slice(index * part, (index + 1) * part))
            first = 2 * index * part
            update(2, at, feed_ref[:, first : first + part], rate)
            update(3, at, feed_ref[:, first + part : first + 2 * part], rate)
    update(4, (...,), vectors[:6], vector_rate)
    model = where_ref[2]
    head = jnp.zeros((2, width), f32)
    for index in range(4):
        head = head + jnp.where(model == index, vectors[6:8, index * width : (index + 1) * width], 0.0)
    update(5, (...,), head, vector_rate)
    bias = vector_ref[pl.ds(8 + model, 1), :]
    bias = jnp.concatenate([bias[:, at : at + 128] for at in range(0, bias.shape[1], 128)], axis=0)
    update(6, (...,), bias, vector_rate)


def bring_body(*refs):
    half = len(refs) // 2
    for source, target in zip(refs[:half], refs[half:]):
        target[...] = source[...]


def bring(arrays, after):
    return pl.pallas_call(
        lambda *refs: bring_body(*refs[: len(arrays)], *refs[len(arrays) + len(after) :]),
        in_specs=[NEAR] * len(arrays) + [LATER] * len(after),
        out_specs=[NEAR] * len(arrays),
        out_shape=[sds(array.shape, f32) for array in arrays],
        compiler_params=params(8),
        cost_estimate=cost(4e6, 6e6),
        name="bring",
    )(*from_far(*arrays), *after)


def last_sum_body(*refs):
    parts, (early_ref, late_ref, token_ref, total_ref, owned_ref) = refs[:-5], refs[-5:]
    total = sum(part[0].astype(f32) for part in parts)
    total_ref[...] = total
    squares = sum(jnp.sum(values * values) for values in (total, early_ref[...], late_ref[...]))
    owned_ref[:2, :] = token_ref[...]
    owned_ref[2:, :] = jnp.full((1, owned_ref.shape[1]), squares, f32)


def last_sum(parts, early_total, late_total, token_sums):
    _, rows, columns = parts[0].shape
    return pl.pallas_call(
        last_sum_body,
        in_specs=[NEAR] * (len(parts) + 3),
        out_specs=[NEAR] * 2,
        out_shape=[sds((rows, columns), f32), sds((3, columns), f32)],
        compiler_params=params(8),
        cost_estimate=cost(0, 0),
        name="last_sum",
    )(*parts, early_total, late_total, token_sums)


def optimize(where, owned, vector_total, attend_total, feed_totals, arrays):
    shapes = [sds(array.shape, f32) for array in arrays]
    return pl.pallas_call(
        optimize_body,
        in_specs=[pl.BlockSpec(memory_space=pltpu.SMEM)]
        + [pl.BlockSpec(memory_space=pltpu.VMEM)] * (5 + len(arrays)),
        out_shape=[sds((1, 1), f32)] + shapes,
        compiler_params=params(20),
        cost_estimate=cost(4e6, 8e6),
        name="optimize",
    )(where, owned, vector_total, attend_total, *feed_totals, *arrays)


def shards(
    tokens,
    cotangent,
    lengths,
    input_weight,
    output_weight,
    expand_weight,
    shrink_weight,
    layer_vectors,
    head_bias,
    expand_bias,
    first_input,
    first_output,
    first_expand,
    first_shrink,
    first_vectors,
    first_head,
    first_bias,
    second_input,
    second_output,
    second_expand,
    second_shrink,
    second_vectors,
    second_head,
    second_bias,
):
    dp_count = lax.axis_size("dp")
    mp_count = lax.axis_size("mp")
    cube = dp_count == 8 and mp_count == 4
    rows = input_weight.shape[0]
    width = input_weight.shape[2]
    hidden = expand_weight.shape[1]
    seq, depth = tokens.shape
    part = hidden // 3
    model_index = lax.axis_index("mp")
    me = lax.axis_index("dp") * mp_count + model_index

    attend_shard, feed_shard, bias_full = pack(
        input_weight.transpose(1, 0, 2),
        output_weight,
        expand_weight,
        shrink_weight.T,
        head_bias,
        expand_bias.reshape(hidden // 128, 128),
    )
    if cube:
        core, near = me & 1, model_index
        devices = jnp.arange(32).reshape(8, 4).T
        spots = jnp.concatenate(
            [place(devices ^ me, devices & 1, orders) for orders in (CORE_ORDERS, LATE_ORDERS)]
        ).astype(jnp.int32)
    else:
        core = near = jnp.zeros((), jnp.int32)
        spots = (jnp.arange(8)[:, None] % 4 // 2 * 8 + jnp.arange(8)[None]).astype(jnp.int32)
    where = jnp.stack([core, near, model_index]).astype(jnp.int32)

    def turned(array):
        return array.transpose(1, 0, 2)

    state = (
        (turned(input_weight), turned(first_input), turned(second_input)),
        (output_weight, first_output, second_output),
        (expand_weight, first_expand, second_expand),
        (shrink_weight.T, first_shrink.T, second_shrink.T),
        (layer_vectors, first_vectors, second_vectors),
        (head_bias, first_head, second_head),
        tuple(array.reshape(hidden // 128, 128) for array in (expand_bias, first_bias, second_bias)),
    )
    arrays = [array for group in state for array in group]

    if cube:
        split = rows * 2 // 3
        held, early, late = attend_shard[None], feed_shard[None, :split], feed_shard[None, split:]
        arrived, far_late = cube_permute(held, 0), cube_permute(late, 0, LATE_ORDERS)
        held, bias_full = lax.optimization_barrier((joined(held, arrived), bias_full))
        arrived = cube_permute(held, 1)
        bias_full = bias_full + bit_permute(bias_full, 0)
        normed, normed_t, upstream_t = prepare(tokens, cotangent, layer_vectors, (held,))
        late = joined(late, far_late)
        held, early, late, normed, bias_full, spots, where = lax.optimization_barrier(
            (held, early, late, normed, bias_full, spots, where)
        )
        held, early = lax.optimization_barrier((joined(held, arrived), early))
        arrived, far_early = cube_permute(held, 2), cube_permute(early, 0)
        far_late = cube_permute(late, 1, LATE_ORDERS)
        held, early, late = joined(held, arrived), joined(early, far_early), joined(late, far_late)
        held, early, late, bias_full = lax.optimization_barrier((held, early, late, bias_full))
        bias_full = bias_full + bit_permute(bias_full, 1)
        far, far_early = cube_permute(held, 3), cube_permute(early, 1)
        twin = bit_permute(held, 0)
        early = joined(early, far_early)
        far, early, late, bias_full = lax.optimization_barrier((far, early, late, bias_full))
        attend_halves = (held, far, twin, bit_permute(far, 0))
        far_early, far_late = cube_permute(early, 2), cube_permute(late, 2, LATE_ORDERS)
        qkv, wide, wide_out = project(where, spots, normed, attend_halves, bias_full, ())
        far_early, far_late, qkv = lax.optimization_barrier((far_early, far_late, qkv))
        early, late = joined(early, far_early), joined(late, far_late)
        far_early, far_late = cube_permute(early, 3), cube_permute(late, 3, LATE_ORDERS)
        twin_early, twin_late = bit_permute(early, 0), bit_permute(late, 0)
        mixture, log_totals = attend_forward(where, lengths, qkv, (early, late))
        far_early, far_late, twin_late, mixture = lax.optimization_barrier(
            (far_early, far_late, twin_late, mixture)
        )
        last_early, last_late = bit_permute(far_early, 0), bit_permute(far_late, 0)
        middle, hidden_in, hidden_t, unit, inverse = attend_out(mixture, wide_out, tokens, layer_vectors)
        feed_halves = (early, far_early, twin_early, last_early, late, far_late, twin_late, last_late)
    else:

        def planes(shard):
            full = lax.all_gather(lax.all_gather(shard, "dp", axis=0, tiled=True), "mp", axis=0)
            full = full.reshape(2, 2, 8, depth // 8, shard.shape[1]).transpose(1, 0, 2, 3, 4)
            return tuple(full.reshape(4, 8, depth // 8, shard.shape[1]))

        normed, normed_t, upstream_t = prepare(tokens, cotangent, layer_vectors, ())
        bias_full = lax.psum(bias_full, "mp")
        qkv, wide, wide_out = project(where, spots, normed, planes(attend_shard), bias_full, ())
        mixture, log_totals = attend_forward(where, lengths, qkv, ())
        middle, hidden_in, hidden_t, unit, inverse = attend_out(mixture, wide_out, tokens, layer_vectors)
        split = depth // 8 * 2 // 3
        feed_planes = planes(feed_shard)
        feed_halves = tuple(array[:, :split] for array in feed_planes) + tuple(
            array[:, split:] for array in feed_planes
        )
    block_out, back, keep_early, send_early, keep_late, send_late, bias_grad = feed(
        where,
        spots,
        hidden_in,
        hidden_t,
        cotangent,
        upstream_t,
        feed_halves,
        bias_full,
        middle,
        layer_vectors,
    )
    middle_grad, mixture_grad, output_grad, middle_sums = middle_back(
        where, lengths, back, unit, inverse, cotangent, mixture, wide_out, layer_vectors
    )
    if cube:
        twin_early, twin_late = bit_permute(send_early[8:], 0), bit_permute(send_late[8:], 0)
        twin_early, twin_late, mixture_grad, send_early, send_late = lax.optimization_barrier(
            (twin_early, twin_late, mixture_grad, send_early, send_late)
        )
        away = (keep_early[8:].astype(f32) + twin_early.astype(f32)).astype(low)
        far_away_late = (keep_late[8:].astype(f32) + twin_late.astype(f32)).astype(low)
        early = [keep_early[:8], bit_permute(send_early[:8], 0)]
        late = [keep_late[:8], bit_permute(send_late[:8], 0)]
        packed_grad = attend_backward(
            where, lengths, qkv, mixture_grad, log_totals, (away, far_away_late)
        )
        early = early + [cube_permute(away, 3)]
        late = late + [cube_permute(far_away_late, 3, LATE_ORDERS)]
        early[0], late[0], packed_grad = lax.optimization_barrier((early[0], late[0], packed_grad))
        away, far_away_late = leaving(early, 2), leaving(late, 2)
        sums = (middle_sums, bias_grad)
        keep_attend, send_attend, rider = input_grad(
            where, spots, normed_t, packed_grad, output_grad, sums, 16, depth // 8, (away, far_away_late)
        )
        early = staying(early, 2) + [cube_permute(away, 2)]
        late = staying(late, 2) + [cube_permute(far_away_late, 2, LATE_ORDERS)]
        early[-1], late[-1], send_attend = lax.optimization_barrier((early[-1], late[-1], send_attend))
        twin_b, rider, _ = with_rider(send_attend[8:], rider, lambda values: bit_permute(values, 0))
        twin_a = bit_permute(send_attend[:8], 0)
        away = (keep_attend[8:].astype(f32) + twin_b.astype(f32)).astype(low)
        arrived, rider, message = with_rider(away, rider, lambda values: cube_permute(values, 3))
        attend_parts = [keep_attend[:8], twin_a, arrived]
        feed_away = leaving(early, 1)
        token_grad, token_sums = token_back(
            packed_grad, wide, tokens, middle_grad, layer_vectors, (message, feed_away)
        )
        early = staying(early, 1) + [cube_permute(feed_away, 1)]
        attend_parts[0], late[0], token_sums = lax.optimization_barrier(
            (attend_parts[0], late[0], token_sums)
        )
        feed_away = leaving(late, 1)
        late = staying(late, 1) + [cube_permute(feed_away, 1, LATE_ORDERS)]
        away = leaving(attend_parts, 2)
        arrived, rider, message = with_rider(away, rider, lambda values: cube_permute(values, 2))
        attend_parts = staying(attend_parts, 2) + [arrived]
        message, early[0], late[0] = lax.optimization_barrier((message, early[0], late[0]))
        feed_away = leaving(early, 0)
        early = staying(early, 0) + [cube_permute(feed_away, 0)]
        away = leaving(attend_parts, 1)
        arrived, rider, message = with_rider(away, rider, lambda values: cube_permute(values, 1))
        attend_parts = staying(attend_parts, 1) + [arrived]
        message, early[0], late[0] = lax.optimization_barrier((message, early[0], late[0]))
        early_total = summed(early)
        feed_away = leaving(late, 0)
        late = staying(late, 0) + [cube_permute(feed_away, 0, LATE_ORDERS)]
        arrays = list(bring(arrays, (message,)))
        attend_parts[0], arrays[0] = lax.optimization_barrier((attend_parts[0], arrays[0]))
        away = leaving(attend_parts, 0)
        away, early_total = lax.optimization_barrier((away, early_total))
        arrived, vector_total, _ = with_rider(away, rider, lambda values: cube_permute(values, 0))
        attend_parts = staying(attend_parts, 0) + [arrived]
        late_total = summed(late)
        feed_totals = (early_total, late_total)
        attend_total, owned = last_sum(attend_parts, early_total, late_total, token_sums)
        owned = cube_sum(owned)
    else:
        packed_grad = attend_backward(where, lengths, qkv, mixture_grad, log_totals, ())
        sums = (middle_sums, bias_grad)
        keep_attend, send_attend, vector_total = input_grad(
            where, spots, normed_t, packed_grad, output_grad, sums, 16, depth // 8, ()
        )
        token_grad, token_sums = token_back(packed_grad, wide, tokens, middle_grad, layer_vectors, ())
        vector_total = lax.psum(vector_total, ("dp", "mp"))

    if not cube:

        def own_block(keep, send):
            full = jnp.stack([keep, send]).reshape(2, 2, 8, keep.shape[1], keep.shape[2])
            full = full.transpose(1, 0, 2, 3, 4).reshape(4, 8 * keep.shape[1], keep.shape[2])
            full = lax.psum_scatter(full, "mp", scatter_dimension=0, tiled=False)
            return lax.psum(full, "dp")

        def own_rows(*blocks):
            full = jnp.concatenate([block.reshape(8, -1, block.shape[1]) for block in blocks], axis=1)
            full = full.reshape(depth, full.shape[2]).astype(f32)
            return lax.dynamic_slice_in_dim(full, lax.axis_index("dp") * rows, rows, 0)

        attend_total = own_rows(own_block(keep_attend, send_attend))
        feed_total = own_rows(own_block(keep_early, send_early), own_block(keep_late, send_late))
        feed_totals = feed_total[: rows * 2 // 3], feed_total[rows * 2 // 3 :]
        attend_total, owned = last_sum((attend_total[None],), *feed_totals, token_sums)
        owned = lax.psum(owned, ("dp", "mp"))
    grad_norm, *updates = optimize(where, owned, vector_total, attend_total, feed_totals, arrays)
    grad_norm = grad_norm[0, 0]
    moment_input, square_input, updated_input = (turned(array) for array in updates[:3])
    moment_output, square_output, updated_output = updates[3:6]
    moment_expand, square_expand, updated_expand = updates[6:9]
    moment_shrink, square_shrink, updated_shrink = (array.T for array in updates[9:12])
    moment_vectors, square_vectors, updated_vectors = updates[12:15]
    moment_head, square_head, updated_head = updates[15:18]
    moment_bias, square_bias, updated_bias = (array.reshape(hidden) for array in updates[18:])
    return (
        block_out,
        token_grad,
        grad_norm,
        moment_input,
        square_input,
        updated_input,
        moment_output,
        square_output,
        updated_output,
        moment_expand,
        square_expand,
        updated_expand,
        moment_shrink,
        square_shrink,
        updated_shrink,
        moment_vectors,
        square_vectors,
        updated_vectors,
        moment_head,
        square_head,
        updated_head,
        moment_bias,
        square_bias,
        updated_bias,
    )


def solution(mesh):
    in_specs = (
        P(("dp", "mp"), None),
        P(("dp", "mp"), None),
        P("dp"),
        P("dp", None, "mp"),
        P("mp", "dp"),
        P("dp", "mp"),
        P("mp", "dp"),
        P(),
        P(None, "mp"),
        P("mp"),
        P("dp", None, "mp"),
        P("mp", "dp"),
        P("dp", "mp"),
        P("mp", "dp"),
        P(),
        P(None, "mp"),
        P("mp"),
        P("dp", None, "mp"),
        P("mp", "dp"),
        P("dp", "mp"),
        P("mp", "dp"),
        P(),
        P(None, "mp"),
        P("mp"),
    )
    out_specs = (
        P(("dp", "mp"), None),
        P(("dp", "mp"), None),
        P(),
        P("dp", None, "mp"),
        P("dp", None, "mp"),
        P("dp", None, "mp"),
        P("mp", "dp"),
        P("mp", "dp"),
        P("mp", "dp"),
        P("dp", "mp"),
        P("dp", "mp"),
        P("dp", "mp"),
        P("mp", "dp"),
        P("mp", "dp"),
        P("mp", "dp"),
        P(),
        P(),
        P(),
        P(None, "mp"),
        P(None, "mp"),
        P(None, "mp"),
        P("mp"),
        P("mp"),
        P("mp"),
    )
    return jax.shard_map(shards, mesh=mesh, in_specs=in_specs, out_specs=out_specs, check_vma=False)
```
